32 devices in a mesh: seq: 8 (over z, x), shard: 4 (over y, core).
Axes of the slice: x: 2, y: 2, z: 4, core: 2. Of those that a mesh axis runs over, the one named last changes fastest.
Arguments:
- tokens: bfloat16 [4, 1920, 1536], P('shard', 'seq'), may hold values from -6 to 6
- gains_taps: float32 [5, 1536], replicated, may hold values from 0.5 to 1.5
- weights: float32 [1536, 26880], P('seq', 'shard'), may hold values from -0.15625 to 0.15625
- cotangent: bfloat16 [4, 1920, 1536], P('shard', 'seq'), may hold values from -6 to 6
- weight_first: float32 [1536, 26880], P('seq', 'shard'), may hold values from -56 to 56
- weight_second: float32 [1536, 26880], P('seq', 'shard'), may hold values from 76.8 to 3840
- gains_first: float32 [5, 1536], replicated, may hold values from -56 to 56
- gains_second: float32 [5, 1536], replicated, may hold values from 76.8 to 3840
Outputs:
- block_out: bfloat16 [4, 1920, 1536], P('shard', 'seq')
- input_grad: bfloat16 [4, 1920, 1536], P('shard', 'seq')
- weight_grad: float32 [1536, 26880], P('seq', 'shard')
- weight_first_new: float32 [1536, 26880], P('seq', 'shard')
- weight_second_new: float32 [1536, 26880], P('seq', 'shard')
- weight_new: float32 [1536, 26880], P('seq', 'shard')
- gains_grad: float32 [5, 1536], replicated
- gains_first_new: float32 [5, 1536], replicated
- gains_second_new: float32 [5, 1536], replicated
- gains_new: float32 [5, 1536], replicated
The draws below stay inside these ranges and needn't reach their ends.
All inputs are finite; a program needn't handle non-finite values.
Results may differ from the reference program's by a relative error of at most 0.012.
The reference program's roundings to bfloat16 on the way count: a program that leaves them out, or rounds other values in their place, can miss the bound.
Values may be sent and summed in bfloat16 or wider, within the bound.
A program may use at most 640 MiB of HBM per device.

```python
import math
import jax
import jax.numpy as jnp
from jax import lax

D = 1536
FF = 6912
STEP = 10
SEQS = 4
LENGTH = 1920
TOKENS = 7680
COLS = 26880


def levels(own_key, dims, shards, low, top_value):
    loudness = 1.0
    for dim, blocks in shards:
        draws = jax.random.uniform(jax.random.fold_in(jax.random.fold_in(own_key, 6), dim), (blocks,), jnp.float32, low / len(shards), top_value / len(shards))
        loudness = loudness * jnp.repeat(jnp.exp(draws), dims[dim] // blocks).reshape((-1,) + (1,) * (len(dims) - 1 - dim))
    return loudness


def gaussian(key, extent, deviation, bound, pieces=(), dtype=jnp.bfloat16):
    values = deviation * jax.random.normal(key, extent, jnp.float32)
    if pieces:
        values = values * levels(key, extent, pieces, -0.22, 0.18)
    return jnp.clip(values, -bound, bound).astype(dtype)


def setup_inputs(seed: int = 0) -> dict:
    arg_keys = jax.random.split(jax.random.key(seed), 9)
    tokens = gaussian(arg_keys[0], (SEQS, LENGTH, D), 1.0, 6.0, ((0, 4), (1, 8)))
    gains_taps = jnp.clip(1.0 + 0.1 * jax.random.normal(arg_keys[1], (5, D), jnp.float32), 0.5, 1.5)
    weights = gaussian(arg_keys[2], (D, COLS), D ** -0.5, 0.15625, ((0, 8), (1, 4)), jnp.float32)
    cotangent = gaussian(arg_keys[3], (SEQS, LENGTH, D), 1.0, 6.0, ((0, 4), (1, 8)))
    weight_first = gaussian(arg_keys[4], (D, COLS), (0.1 * TOKENS ** 0.5), 56.0, ((0, 8), (1, 4)), jnp.float32)
    weight_second = jnp.clip(jnp.exp(math.log(3840.0) - 3.912023 * jax.random.uniform(arg_keys[5], (D, COLS), jnp.float32) ** levels(arg_keys[5], (D, COLS), ((0, 8), (1, 4)), -0.2, 0.2)), 76.8, 3840.0)
    gains_first = gaussian(arg_keys[6], (5, D), (0.1 * TOKENS ** 0.5), 56.0, (), jnp.float32)
    gains_second = jnp.clip(jnp.exp(jax.random.uniform(arg_keys[7], (5, D), jnp.float32, math.log(76.8), math.log(3840.0))), 76.8, 3840.0)
    return {"tokens": tokens, "gains_taps": gains_taps, "weights": weights, "cotangent": cotangent, "weight_first": weight_first, "weight_second": weight_second, "gains_first": gains_first, "gains_second": gains_second}


MOMENT_DECAY = 0.9
SQUARE_DECAY = 0.95
ADAM_EPSILON = 1e-08
NORM_EPSILON = 1e-05
WEIGHT_RATE = 0.02
GAIN_RATE = 0.2
WEIGHT_DECAY = 0.1

@jax.custom_vjp
def low(v):
    return lax.optimization_barrier(v.astype(jnp.bfloat16)).astype(jnp.float32)

@jax.custom_vjp
def low_back(v):
    return v

def low_keep(v):
    return (low(v), None)

def low_pass(kept, grad):
    return (grad,)

def back_keep(v):
    return (v, None)

def back_low(kept, grad):
    return (low(grad),)
low.defvjp(low_keep, low_pass)
low_back.defvjp(back_keep, back_low)

def matmul(left, right):
    return jnp.dot(left, right, precision=lax.Precision.HIGHEST, preferred_element_type=jnp.float32)

def root_norm(values, gain):
    scale = lax.rsqrt(lax.optimization_barrier(jnp.mean(values * values, axis=-1, keepdims=True)) + NORM_EPSILON)
    return values * scale * gain

def pick_block(rounded, low_col, width):
    grouped = rounded.reshape(D, 4, COLS // 4)
    return grouped[:, :, low_col:low_col + width].reshape(D, 4 * width)

def forward(inputs, gains_taps, weights):
    quarter = D // 4
    unit_quarter = FF // 4
    rounded = low(weights)
    w_b = pick_block(rounded, 0, quarter)
    w_c = pick_block(rounded, quarter, quarter)
    w_x = pick_block(rounded, 2 * quarter, quarter)
    w_out_t = pick_block(rounded, 3 * quarter, quarter)
    w_gate = pick_block(rounded, 4 * quarter, unit_quarter)
    w_up = pick_block(rounded, 4 * quarter + unit_quarter, unit_quarter)
    w_down = pick_block(rounded, 4 * quarter + 2 * unit_quarter, unit_quarter)
    normed = low(root_norm(inputs, gains_taps[0]))
    project = low_back(jnp.concatenate([matmul(normed, w_b), matmul(normed, w_c), matmul(normed, w_x)], axis=1))
    b_part = project[:, :D]
    c_part = project[:, D:2 * D]
    x_part = project[:, 2 * D:]
    gated = low(b_part * x_part)
    padded = jnp.concatenate([jnp.zeros((2, D), jnp.float32), gated], axis=0)
    conv = gains_taps[2] * padded[:-2] + gains_taps[3] * padded[1:-1] + gains_taps[4] * padded[2:]
    mixed = low(c_part * conv)
    branch = low_back(matmul(mixed, w_out_t.T))
    resid = inputs + branch
    normed_two = low(root_norm(resid, gains_taps[1]))
    gate_up = low_back(jnp.concatenate([matmul(normed_two, w_gate), matmul(normed_two, w_up)], axis=1))
    gate_pre = gate_up[:, :FF]
    up_value = gate_up[:, FF:]
    active = low(jax.nn.silu(gate_pre) * up_value)
    ffn_out = low_back(matmul(active, w_down.T))
    return resid + ffn_out

def adam_update(param, grad, first, second, rate, decay):
    first_new = MOMENT_DECAY * first + (1.0 - MOMENT_DECAY) * grad
    second_new = SQUARE_DECAY * second + (1.0 - SQUARE_DECAY) * grad * grad
    first_hat = first_new / (1.0 - MOMENT_DECAY ** STEP)
    second_hat = second_new / (1.0 - SQUARE_DECAY ** STEP)
    param_new = param - rate * (first_hat / (jnp.sqrt(second_hat) + ADAM_EPSILON) + decay * param)
    return (first_new, second_new, param_new)

def reference(tokens, gains_taps, weights, cotangent, weight_first, weight_second, gains_first, gains_second):
    inputs = tokens.astype(jnp.float32)
    upstream = cotangent.astype(jnp.float32)

    def one_sequence(carry, pair):
        seq_in, seq_up = pair
        result, pullback = jax.vjp(forward, seq_in, gains_taps, weights)
        grad_in, grad_gains, grad_weights = pullback(seq_up)
        return ((carry[0] + grad_gains, carry[1] + grad_weights), (result.astype(jnp.bfloat16), grad_in.astype(jnp.bfloat16)))
    start = (jnp.zeros((5, D), jnp.float32), jnp.zeros((D, COLS), jnp.float32))
    (gains_grad, weight_grad), (block_out, input_grad) = lax.scan(one_sequence, start, (inputs, upstream))
    weight_first_new, weight_second_new, weight_new = adam_update(weights, weight_grad, weight_first, weight_second, WEIGHT_RATE, WEIGHT_DECAY)
    gains_first_new, gains_second_new, gains_new = adam_update(gains_taps, gains_grad, gains_first, gains_second, GAIN_RATE, 0.0)
    return (block_out, input_grad, weight_grad, weight_first_new, weight_second_new, weight_new, gains_grad, gains_first_new, gains_second_new, gains_new)
```

```python
import functools

import jax
import jax.numpy as jnp
from jax import lax
from jax.experimental import pallas as pl
from jax.experimental.pallas import tpu as pltpu
from jax.sharding import PartitionSpec as P

D = 1536
FF = 6912
STEP = 10
GROUPS = 4
QUARTER = D // GROUPS
UNITS = FF // GROUPS
HALF_Q = QUARTER // 2
HALF_F = UNITS // 2
LANES = 128
PAD_F = -(-HALF_F // LANES) * LANES
CONV_COLS = 4 * HALF_Q
WIDTHS = (CONV_COLS, PAD_F, PAD_F, PAD_F)
STARTS = (0, CONV_COLS, CONV_COLS + PAD_F, CONV_COLS + 2 * PAD_F)
SPLIT = 128

MOMENT_DECAY = 0.9
SQUARE_DECAY = 0.95
ADAM_EPSILON = 1e-08
NORM_EPSILON = 1e-05
WEIGHT_RATE = 0.02
GAIN_RATE = 0.2
WEIGHT_DECAY = 0.1

BF16 = jnp.bfloat16
F32 = jnp.float32
MESH = pl.DeviceIdType.MESH
VMEM_BYTES = 56 * 1024 * 1024


def place():
    seq, shard = lax.axis_index("seq"), lax.axis_index("shard")
    inner, core = lax.rem(seq, 2), lax.rem(shard, 2)
    return seq, shard, inner, core


def partners():
    seq, shard, inner, core = place()
    across = {"seq": seq + 1 - 2 * inner, "shard": shard}
    beside = {"seq": seq, "shard": lax.rem(shard + 2, 4)}
    twin = {"seq": seq, "shard": shard + 1 - 2 * core}
    return across, beside, twin


def greet(*devices):
    barrier = pltpu.get_barrier_semaphore()
    for device in devices:
        pl.semaphore_signal(barrier, inc=1, device_id=device, device_id_type=MESH)
    pl.semaphore_wait(barrier, len(devices))


def remote(src, dst, send, recv, device):
    return pltpu.make_async_remote_copy(
        src_ref=src, dst_ref=dst, send_sem=send, recv_sem=recv, device_id=device, device_id_type=MESH
    )


def spread_kernel(own_ref, all_ref, local, send, recv):
    _, shard, inner, core = place()
    across, beside, twin = partners()
    greet(across, beside, twin)
    rows = own_ref.shape[0]
    low, high = pl.ds(0, SPLIT), pl.ds(SPLIT, rows - SPLIT)
    other_in, other_row = 1 - inner, lax.rem(shard + 2, 4)

    def block(s, i):
        return all_ref.at[s, i]

    mine = pltpu.make_async_copy(own_ref, block(shard, inner), local)
    mine.start()
    to_across = remote(own_ref, block(shard, inner), send.at[0], recv.at[0], across)
    to_beside = remote(own_ref, block(shard, inner), send.at[1], recv.at[1], beside)
    to_twin = remote(own_ref, block(shard, inner), send.at[2], recv.at[2], twin)
    to_across.start()
    to_beside.start()
    to_twin.start()

    def passed(s, i, part, slot, device):
        ref = block(s, i).at[part]
        copy = remote(ref, ref, send.at[slot], recv.at[slot], device)
        copy.start()
        return copy

    whole = pl.ds(0, rows)
    to_across.wait_recv()
    low_on = passed(shard, other_in, low, 3, beside)
    twin_a = passed(shard, other_in, whole, 4, twin)
    to_beside.wait_recv()
    high_on = passed(other_row, inner, high, 5, across)
    twin_b = passed(other_row, inner, whole, 6, twin)
    low_on.wait_recv()
    twin_c = passed(other_row, other_in, low, 7, twin)
    high_on.wait_recv()
    twin_d = passed(other_row, other_in, high, 8, twin)
    for copy in (to_twin, twin_a, twin_b, twin_c, twin_d):
        copy.wait_recv()
    for copy in (to_across, to_beside, to_twin, low_on, twin_a, high_on, twin_b, twin_c, twin_d):
        copy.wait_send()
    mine.wait()


def spread(own, ident):
    rows, width = own.shape
    return pl.pallas_call(
        spread_kernel,
        out_shape=jax.ShapeDtypeStruct((4, 2, rows, width), own.dtype),
        in_specs=[pl.BlockSpec(memory_space=pl.ANY)],
        out_specs=pl.BlockSpec(memory_space=pl.ANY),
        scratch_shapes=[
            pltpu.SemaphoreType.DMA,
            pltpu.SemaphoreType.DMA((9,)),
            pltpu.SemaphoreType.DMA((9,)),
        ],
        compiler_params=pltpu.CompilerParams(collective_id=ident, has_side_effects=True),
        name="spread",
    )(own)


def collect_kernel(part_ref, sum_ref, from_twin, pair, near, joined, send, recv):
    _, shard, inner, core = place()
    across, beside, twin = partners()
    rows = sum_ref.shape[0]
    low, high = pl.ds(0, SPLIT), pl.ds(SPLIT, rows - SPLIT)
    other_in, other_row = 1 - inner, lax.rem(shard + 2, 4)
    twin_shard = shard + 1 - 2 * core
    twin_row = lax.rem(twin_shard + 2, 4)
    greet(across, beside, twin)
    theirs = ((twin_row, other_in), (twin_shard, other_in), (twin_row, inner), (twin_shard, inner))
    ours = ((other_row, other_in), (shard, other_in), (other_row, inner), (shard, inner))
    to_twin = []
    for k, (s, i) in enumerate(theirs):
        copy = remote(part_ref.at[s, i], from_twin.at[k], send.at[k], recv.at[k], twin)
        copy.start()
        to_twin.append(copy)

    def add_pair(k):
        to_twin[k].wait_recv()
        s, i = ours[k]
        pair[k] = (part_ref[s, i].astype(F32) + from_twin[k].astype(F32)).astype(BF16)

    add_pair(0)
    far_low = remote(pair.at[0, low], joined.at[low], send.at[4], recv.at[4], across)
    far_high = remote(pair.at[0, high], joined.at[high], send.at[5], recv.at[5], beside)
    far_low.start()
    far_high.start()
    add_pair(1)
    near_low = remote(pair.at[1, low], near.at[0, low], send.at[6], recv.at[6], across)
    near_low.start()
    add_pair(2)
    near_high = remote(pair.at[2, high], near.at[1, high], send.at[7], recv.at[7], beside)
    near_high.start()
    far_low.wait_recv()
    pair[2, low] = (pair[2, low].astype(F32) + joined[low].astype(F32)).astype(BF16)
    last_low = remote(pair.at[2, low], near.at[1, low], send.at[8], recv.at[8], beside)
    last_low.start()
    far_high.wait_recv()
    pair[1, high] = (pair[1, high].astype(F32) + joined[high].astype(F32)).astype(BF16)
    last_high = remote(pair.at[1, high], near.at[0, high], send.at[9], recv.at[9], across)
    last_high.start()
    to_twin[3].wait_recv()
    sum_ref[...] = part_ref[shard, inner].astype(F32) + from_twin[3].astype(F32)
    near_low.wait_recv()
    last_low.wait_recv()
    sum_ref[low] = sum_ref[low] + near[0, low].astype(F32) + near[1, low].astype(F32)
    near_high.wait_recv()
    last_high.wait_recv()
    sum_ref[high] = sum_ref[high] + near[0, high].astype(F32) + near[1, high].astype(F32)
    for copy in (*to_twin, far_low, far_high, near_low, near_high, last_low, last_high):
        copy.wait_send()


def collect(part, ident):
    _, _, rows, width = part.shape
    return pl.pallas_call(
        collect_kernel,
        out_shape=jax.ShapeDtypeStruct((rows, width), F32),
        in_specs=[pl.BlockSpec(memory_space=pltpu.VMEM)],
        out_specs=pl.BlockSpec(memory_space=pltpu.VMEM),
        scratch_shapes=[
            pltpu.VMEM((4, rows, width), BF16),
            pltpu.VMEM((4, rows, width), BF16),
            pltpu.VMEM((2, rows, width), BF16),
            pltpu.VMEM((rows, width), BF16),
            pltpu.SemaphoreType.DMA((10,)),
            pltpu.SemaphoreType.DMA((10,)),
        ],
        compiler_params=pltpu.CompilerParams(
            collective_id=ident, has_side_effects=True, vmem_limit_bytes=VMEM_BYTES
        ),
        name="collect",
    )(part)


def line():
    seq, shard, inner, _ = place()
    outer = seq // 2
    return outer, {"seq": seq - 2, "shard": shard}, {"seq": seq + 2, "shard": shard}


def greet_line(layers, across):
    outer, left, right = line()
    barrier = pltpu.get_barrier_semaphore()
    pl.semaphore_signal(barrier, inc=1, device_id=across, device_id_type=MESH)

    @pl.when(outer > 0)
    def _():
        pl.semaphore_signal(barrier, inc=1, device_id=left, device_id_type=MESH)

    @pl.when(outer < layers - 1)
    def _():
        pl.semaphore_signal(barrier, inc=1, device_id=right, device_id_type=MESH)

    ends = jnp.int32(outer > 0) + jnp.int32(outer < layers - 1)
    pl.semaphore_wait(barrier, 1 + ends)


def gather_weights_kernel(layers, rows, own_ref, oth_ref, *refs):
    count = len(WIDTHS)
    outs = refs[:count]
    local, send_x, recv_x, send_z, recv_z = refs[count:]
    seq, _, inner, _ = place()
    outer, left, right = line()
    across, _, _ = partners()
    other_seq = seq + 1 - 2 * inner
    greet_line(layers, across)
    x_copies, l_copies = [], []
    has_next = (outer < layers - 1, outer > 0)
    nexts = (right, left)

    def has_come(direction, step):
        return outer >= step if direction == 0 else outer + step <= layers - 1

    def layer_rows(direction, step):
        origin = outer - step if direction == 0 else outer + step
        return pl.ds(origin * 2 * rows, 2 * rows)

    def z_copy(k, src, ref, direction, slot):
        return remote(
            src, ref, send_z.at[k, direction, slot], recv_z.at[k, direction, slot], nexts[direction]
        )

    def own_copy(k, direction):
        here = outs[k].at[pl.ds(seq * rows, rows)]
        return z_copy(k, own_ref.at[:, pl.ds(STARTS[k], WIDTHS[k])], here, direction, 0)

    def other_copy(k, direction):
        there = outs[k].at[pl.ds(other_seq * rows, rows)]
        return z_copy(k, there, there, direction, 1)

    def pass_copy(k, direction, step):
        ref = outs[k].at[layer_rows(direction, step - 1)]
        return z_copy(k, ref, ref, direction, step)

    def issue(k):
        cols = pl.ds(STARTS[k], WIDTHS[k])
        here = outs[k].at[pl.ds(seq * rows, rows)]
        copy = remote(oth_ref.at[:, cols], here, send_x.at[k], recv_x.at[k], across)
        copy.start()
        x_copies.append(copy)
        copy = pltpu.make_async_copy(own_ref.at[:, cols], here, local.at[k])
        copy.start()
        l_copies.append(copy)
        for direction in (0, 1):

            @pl.when(has_next[direction])
            def _():
                own_copy(k, direction).start()

    def advance(k):
        x_copies[k].wait_recv()
        for direction in (0, 1):

            @pl.when(has_next[direction])
            def _():
                other_copy(k, direction).start()

        for step in range(1, layers):
            for direction in (0, 1):

                @pl.when(has_come(direction, step))
                def _():
                    if step == 1:
                        for slot in (0, 1):
                            origin = outer - 1 if direction == 0 else outer + 1
                            part = outs[k].at[
                                pl.ds((2 * origin + (inner if slot == 0 else 1 - inner)) * rows, rows)
                            ]
                            z_copy(k, part, part, direction, slot).wait_recv()
                    else:
                        ref = outs[k].at[layer_rows(direction, step)]
                        z_copy(k, ref, ref, direction, step).wait_recv()
                    if step < layers - 1:

                        @pl.when(has_next[direction])
                        def _():
                            pass_copy(k, direction, step + 1).start()

    issue(0)
    for k in range(count):
        if k + 1 < count:
            issue(k + 1)
        advance(k)
    for k in range(count):
        x_copies[k].wait_send()
        l_copies[k].wait()
        for direction in (0, 1):

            @pl.when(has_next[direction])
            def _():
                own_copy(k, direction).wait_send()
                other_copy(k, direction).wait_send()
                for step in range(2, layers):

                    @pl.when(has_come(direction, step - 1))
                    def _():
                        pass_copy(k, direction, step).wait_send()


def gather_weights(own, oth, layers, ident):
    rows = own.shape[0]
    count = len(WIDTHS)
    return pl.pallas_call(
        functools.partial(gather_weights_kernel, layers, rows),
        out_shape=[jax.ShapeDtypeStruct((D, width), BF16) for width in WIDTHS],
        in_specs=[pl.BlockSpec(memory_space=pl.ANY)] * 2,
        out_specs=[pl.BlockSpec(memory_space=pl.ANY)] * count,
        scratch_shapes=[
            pltpu.SemaphoreType.DMA((count,)),
            pltpu.SemaphoreType.DMA((count,)),
            pltpu.SemaphoreType.DMA((count,)),
            pltpu.SemaphoreType.DMA((count, 2, max(layers, 2))),
            pltpu.SemaphoreType.DMA((count, 2, max(layers, 2))),
        ],
        compiler_params=pltpu.CompilerParams(collective_id=ident, has_side_effects=True),
        name="gather_weights",
    )(own, oth)


def reduce_weights_kernel(layers, rows, *refs):
    count = len(WIDTHS)
    grads, mine, theirs = refs[:count], refs[count : 2 * count], refs[2 * count : 3 * count]
    refs = refs[3 * count :]
    slots, refs = refs[:count], refs[count:]
    final, outgoing = refs[:count], refs[count : 2 * count]
    send_z, recv_z, send_x, recv_x = refs[2 * count :]
    seq, _, inner, _ = place()
    outer, left, right = line()
    across, _, _ = partners()
    greet_line(layers, across)
    nexts = (right, left)

    def z_copy(k, src, direction, owner):
        index = owner - 1 if direction == 0 else owner
        return remote(
            src,
            slots[k].at[direction, index],
            send_z.at[k, direction, index],
            recv_z.at[k, direction, index],
            nexts[direction],
        )

    def slot(k, direction, owner):
        return slots[k].at[direction, owner - 1 if direction == 0 else owner]

    def owner_rows(owner):
        return pl.ds(owner * 2 * rows, 2 * rows)

    def came(direction):
        return outer > 0 if direction == 0 else outer < layers - 1

    def goes(direction, owner):
        return owner > outer if direction == 0 else owner < outer

    def travel(k):
        for step in range(layers - 1):
            for direction in (0, 1):
                owner = layers - 1 - step if direction == 0 else step

                @pl.when(goes(direction, owner) & came(direction))
                def _():
                    ref = slot(k, direction, owner)
                    z_copy(k, ref, direction, owner).wait_recv()
                    ref[...] = (
                        ref[...].astype(F32) + grads[k][owner_rows(owner)].astype(F32)
                    ).astype(BF16)
                    z_copy(k, ref, direction, owner).start()

                @pl.when(goes(direction, owner) & jnp.logical_not(came(direction)))
                def _():
                    z_copy(k, grads[k].at[owner_rows(owner)], direction, owner).start()

    x_copies = []

    def finish(k):
        total = final[k]
        total[...] = grads[k][pl.ds(pl.multiple_of(outer * 2 * rows, 16), 2 * rows)].astype(F32)
        for direction in (0, 1):
            for owner in range(1, layers) if direction == 0 else range(layers - 1):

                @pl.when((outer == owner) & came(direction))
                def _():
                    ref = slot(k, direction, owner)
                    z_copy(k, ref, direction, owner).wait_recv()
                    total[...] += ref[...].astype(F32)

        mine[k][...] = total[pl.ds(pl.multiple_of(inner * rows, 16), rows)]
        outgoing[k][...] = total[pl.ds(pl.multiple_of((1 - inner) * rows, 16), rows)].astype(BF16)
        copy = remote(outgoing[k], theirs[k], send_x.at[k], recv_x.at[k], across)
        copy.start()
        x_copies.append(copy)

    travel(0)
    for k in range(count):
        if k + 1 < count:
            travel(k + 1)
        finish(k)
    for k in range(count):
        x_copies[k].wait()
        for direction in (0, 1):
            for owner in range(1, layers) if direction == 0 else range(layers - 1):

                @pl.when(goes(direction, owner))
                def _():
                    z_copy(k, slot(k, direction, owner), direction, owner).wait_send()


def reduce_weights(grads, layers, rows, ident):
    count = len(WIDTHS)
    vmem = pl.BlockSpec(memory_space=pltpu.VMEM)
    hops = layers - 1
    results = pl.pallas_call(
        functools.partial(reduce_weights_kernel, layers, rows),
        out_shape=[jax.ShapeDtypeStruct((rows, width), F32) for width in WIDTHS]
        + [jax.ShapeDtypeStruct((rows, width), BF16) for width in WIDTHS],
        in_specs=[vmem] * count,
        out_specs=[vmem] * (2 * count),
        scratch_shapes=[pltpu.VMEM((2, hops, 2 * rows, width), BF16) for width in WIDTHS]
        + [pltpu.VMEM((2 * rows, width), F32) for width in WIDTHS]
        + [pltpu.VMEM((rows, width), BF16) for width in WIDTHS]
        + [
            pltpu.SemaphoreType.DMA((count, 2, hops)),
            pltpu.SemaphoreType.DMA((count, 2, hops)),
            pltpu.SemaphoreType.DMA((count,)),
            pltpu.SemaphoreType.DMA((count,)),
        ],
        compiler_params=pltpu.CompilerParams(
            collective_id=ident, has_side_effects=True, vmem_limit_bytes=VMEM_BYTES
        ),
        name="reduce_weights",
    )(*grads)
    return results[:count], results[count:]


def halves(local, inner):
    def half(h):
        convs = [local[:, m * QUARTER + h * HALF_Q : m * QUARTER + (h + 1) * HALF_Q] for m in range(4)]
        first = 4 * QUARTER
        units = [
            jnp.pad(
                local[:, first + m * UNITS + h * HALF_F : first + m * UNITS + (h + 1) * HALF_F],
                ((0, 0), (0, PAD_F - HALF_F)),
            )
            for m in range(3)
        ]
        return jnp.concatenate(convs + units, axis=1)

    low, high = half(0), half(1)
    is_low = inner == 0
    return jnp.where(is_low, low, high), jnp.where(is_low, high, low)


def joined_columns(mine, theirs, inner):
    is_low = inner == 0
    parts = []
    for m in range(4):
        a = mine[0][:, m * HALF_Q : (m + 1) * HALF_Q]
        b = theirs[0][:, m * HALF_Q : (m + 1) * HALF_Q].astype(F32)
        parts += [jnp.where(is_low, a, b), jnp.where(is_low, b, a)]
    for m in range(3):
        a = mine[1 + m][:, :HALF_F]
        b = theirs[1 + m][:, :HALF_F].astype(F32)
        parts += [jnp.where(is_low, a, b), jnp.where(is_low, b, a)]
    return jnp.concatenate(parts, axis=1)


def shifted(block, distance):
    devices = range(lax.axis_size("seq"))
    route = [(i - distance, i) for i in devices if i - distance in devices]
    return lax.ppermute(block, "seq", route)


def root_norm(values, gain):
    scale = lax.rsqrt(jnp.mean(values * values, axis=-1, keepdims=True) + NORM_EPSILON)
    return (values * scale * gain, scale)


def norm_back(values, scale, gain, upstream):
    scaled = gain * upstream
    inner = jnp.mean(scaled * values, axis=-1, keepdims=True)
    return (
        scale * scaled - values * scale * scale * scale * inner,
        jnp.sum(upstream * values * scale, axis=0),
    )


def times_rows(left, right):
    return lax.dot_general(left, right, (((1,), (1,)), ((), ())), preferred_element_type=F32)


def outer_sum(left, right):
    return lax.dot_general(left, right, (((0,), (0,)), ((), ())), preferred_element_type=F32)


def adam_update(param, grad, first, second, rate, decay):
    first_new = MOMENT_DECAY * first + (1.0 - MOMENT_DECAY) * grad
    second_new = SQUARE_DECAY * second + (1.0 - SQUARE_DECAY) * grad * grad
    first_hat = first_new / (1.0 - MOMENT_DECAY**STEP)
    second_hat = second_new / (1.0 - SQUARE_DECAY**STEP)
    param_new = param - rate * (first_hat / (jnp.sqrt(second_hat) + ADAM_EPSILON) + decay * param)
    return (first_new, second_new, param_new)


def conv_forward(gated, taps):
    before = shifted(gated[:, -2:], 2)
    padded = jnp.concatenate([before, gated], axis=1).astype(F32)
    conv = taps[0] * padded[:, :-2] + taps[1] * padded[:, 1:-1] + taps[2] * padded[:, 2:]
    return (padded, conv)


def conv_backward(dconv, padded, taps):
    dpadded = (
        jnp.pad(taps[0] * dconv, ((0, 0), (0, 2), (0, 0)))
        + jnp.pad(taps[1] * dconv, ((0, 0), (1, 1), (0, 0)))
        + jnp.pad(taps[2] * dconv, ((0, 0), (2, 0), (0, 0)))
    )
    dtaps = jnp.stack(
        [
            jnp.sum(dconv * padded[:, :-2], axis=(0, 1)),
            jnp.sum(dconv * padded[:, 1:-1], axis=(0, 1)),
            jnp.sum(dconv * padded[:, 2:], axis=(0, 1)),
        ]
    )
    from_next = shifted(dpadded[:, :2], -2)
    dgated = dpadded[:, 2:].at[:, -2:].add(from_next)
    return (dgated, dtaps)


def on_device(
    tokens, gains_taps, weights, cotangent, weight_first, weight_second, gains_first, gains_second
):
    seq, shard = lax.axis_index("seq"), lax.axis_index("shard")
    inner = seq % 2
    rows = weights.shape[0]
    layers = lax.axis_size("seq") // 2
    inputs = tokens[0].astype(F32)
    seg_len = inputs.shape[0]
    layer_tokens = GROUPS * 2 * seg_len

    own, oth = halves(weights.astype(BF16), inner)
    w_conv, w_gate, w_up, w_down = gather_weights(own, oth, layers, 0)
    w_bcx, w_out_t = w_conv[:, : 3 * HALF_Q], w_conv[:, 3 * HALF_Q :]

    def as_rows(blocks):
        return blocks.reshape(layer_tokens, D)

    def as_blocks(values):
        return values.astype(BF16).reshape(GROUPS, 2, seg_len, D)

    col = shard * QUARTER + inner * HALF_Q
    taps = lax.dynamic_slice(gains_taps, (2, col), (3, HALF_Q))

    normed_f, scale_one = root_norm(inputs, gains_taps[0])
    normed = as_rows(spread(normed_f.astype(BF16), 1))
    upstream = as_rows(spread(cotangent[0], 2))

    parts = jnp.dot(normed, w_bcx, preferred_element_type=F32)
    b_part, c_part, x_part = (parts[:, m * HALF_Q : (m + 1) * HALF_Q] for m in range(3))
    gated = (b_part * x_part).astype(BF16).reshape(GROUPS, 2 * seg_len, HALF_Q)
    padded, conv = conv_forward(gated, taps)
    conv_rows = conv.reshape(layer_tokens, HALF_Q)
    mixed = (c_part * conv_rows).astype(BF16)
    branch = collect(as_blocks(times_rows(mixed, w_out_t)), 3)
    resid = inputs + branch
    normed_two_f, scale_two = root_norm(resid, gains_taps[1])
    normed_two = as_rows(spread(normed_two_f.astype(BF16), 4))

    gate_pre = jnp.dot(normed_two, w_gate, preferred_element_type=F32)
    up_value = jnp.dot(normed_two, w_up, preferred_element_type=F32)
    dactive = jnp.dot(upstream, w_down, preferred_element_type=F32)
    sigma = jax.nn.sigmoid(gate_pre)
    silu_val = gate_pre * sigma
    active = (silu_val * up_value).astype(BF16)
    dgate = (dactive * up_value * sigma * (1.0 + gate_pre * (1.0 - sigma))).astype(BF16)
    dup = (dactive * silu_val).astype(BF16)

    dnormed_two = collect(as_blocks(times_rows(dgate, w_gate) + times_rows(dup, w_up)), 5)
    ffn_out = collect(as_blocks(times_rows(active, w_down)), 6)
    block_out = (resid + ffn_out).astype(BF16)
    dresid_part, grad_gain_two = norm_back(resid, scale_two, gains_taps[1], dnormed_two)
    dresid = cotangent[0].astype(F32) + dresid_part
    dbranch = as_rows(spread(dresid.astype(BF16), 7))
    dmixed = jnp.dot(dbranch, w_out_t, preferred_element_type=F32)
    dc_part = (dmixed * conv_rows).astype(BF16)
    dconv = (dmixed * c_part).reshape(GROUPS, 2 * seg_len, HALF_Q)
    dgated, dtaps = conv_backward(dconv, padded, taps)
    dgated_rows = dgated.reshape(layer_tokens, HALF_Q)
    db_part = (dgated_rows * x_part).astype(BF16)
    dx_part = (dgated_rows * b_part).astype(BF16)
    dparts = jnp.concatenate([db_part, dc_part, dx_part], axis=1)
    dnormed = collect(as_blocks(times_rows(dparts, w_bcx)), 8)
    dinput_part, grad_gain_one = norm_back(inputs, scale_one, gains_taps[0], dnormed)
    input_grad = (dresid + dinput_part).astype(BF16)

    grads = [
        jnp.concatenate([outer_sum(normed, dparts), outer_sum(dbranch, mixed)], axis=1).astype(BF16),
        outer_sum(normed_two, dgate).astype(BF16),
        outer_sum(normed_two, dup).astype(BF16),
        outer_sum(upstream, active).astype(BF16),
    ]
    mine, theirs = reduce_weights(grads, layers, rows, 9)
    weight_grad = joined_columns(mine, theirs, inner)

    dtaps_wide = lax.dynamic_update_slice(jnp.zeros((3, D), F32), dtaps, (0, col))
    local_gains = jnp.concatenate([grad_gain_one[None], grad_gain_two[None], dtaps_wide], axis=0)
    gains_grad = lax.psum(local_gains, ("seq", "shard"))
    weight_first_new, weight_second_new, weight_new = adam_update(
        weights, weight_grad, weight_first, weight_second, WEIGHT_RATE, WEIGHT_DECAY
    )
    gains_first_new, gains_second_new, gains_new = adam_update(
        gains_taps, gains_grad, gains_first, gains_second, GAIN_RATE, 0.0
    )
    return (
        block_out[None],
        input_grad[None],
        weight_grad,
        weight_first_new,
        weight_second_new,
        weight_new,
        gains_grad,
        gains_first_new,
        gains_second_new,
        gains_new,
    )


def solution(mesh):
    tokens, rows, whole = P("shard", "seq", None), P("seq", "shard"), P()
    return jax.shard_map(
        on_device,
        mesh=mesh,
        in_specs=(tokens, whole, rows, tokens, rows, rows, whole, whole),
        out_specs=(tokens, tokens, rows, rows, rows, rows, whole, whole, whole, whole),
        check_vma=False,
    )
```

```python
import functools

import jax
import jax.numpy as jnp
from jax import lax
from jax.experimental import pallas as pl
from jax.experimental.pallas import tpu as pltpu
from jax.sharding import PartitionSpec as P

D = 1536
FF = 6912
STEP = 10
GROUPS = 4
QUARTER = D // GROUPS
UNITS = FF // GROUPS
HALF_Q = QUARTER // 2
HALF_F = UNITS // 2
LANES = 128
PAD_F = -(-HALF_F // LANES) * LANES
WIDE = 256
CONV_COLS = 4 * HALF_Q
UNIT_CHUNKS = (384, 256, PAD_F - 640)
UNIT_STARTS = (0, 384, 640)
WIDTHS = (CONV_COLS,) + tuple(3 * units for units in UNIT_CHUNKS)
STARTS = tuple(sum(WIDTHS[:k]) for k in range(len(WIDTHS)))
SPLIT = 128

MOMENT_DECAY = 0.9
SQUARE_DECAY = 0.95
ADAM_EPSILON = 1e-08
NORM_EPSILON = 1e-05
WEIGHT_RATE = 0.02
GAIN_RATE = 0.2
WEIGHT_DECAY = 0.1

BF16 = jnp.bfloat16
F32 = jnp.float32
MESH = pl.DeviceIdType.MESH
VMEM_BYTES = 60 * 1024 * 1024


def place():
    seq, shard = lax.axis_index("seq"), lax.axis_index("shard")
    inner, core = lax.rem(seq, 2), lax.rem(shard, 2)
    return seq, shard, inner, core


def partners():
    seq, shard, inner, core = place()
    across = {"seq": seq + 1 - 2 * inner, "shard": shard}
    beside = {"seq": seq, "shard": lax.rem(shard + 2, 4)}
    twin = {"seq": seq, "shard": shard + 1 - 2 * core}
    return across, beside, twin


def greet(*devices):
    barrier = pltpu.get_barrier_semaphore()
    for device in devices:
        pl.semaphore_signal(barrier, inc=1, device_id=device, device_id_type=MESH)
    pl.semaphore_wait(barrier, len(devices))


def remote(src, dst, send, recv, device):
    return pltpu.make_async_remote_copy(
        src_ref=src, dst_ref=dst, send_sem=send, recv_sem=recv, device_id=device, device_id_type=MESH
    )


def spread_kernel(own_ref, all_ref, local, send, recv):
    _, shard, inner, core = place()
    across, beside, twin = partners()
    greet(across, beside, twin)
    rows = own_ref.shape[0]
    low, high = pl.ds(0, SPLIT), pl.ds(SPLIT, rows - SPLIT)
    other_in, other_row = 1 - inner, lax.rem(shard + 2, 4)

    def block(s, i):
        return all_ref.at[s, i]

    mine = pltpu.make_async_copy(own_ref, block(shard, inner), local)
    mine.start()
    to_across = remote(own_ref, block(shard, inner), send.at[0], recv.at[0], across)
    to_beside = remote(own_ref, block(shard, inner), send.at[1], recv.at[1], beside)
    to_twin = remote(own_ref, block(shard, inner), send.at[2], recv.at[2], twin)
    to_across.start()
    to_beside.start()
    to_twin.start()

    def passed(s, i, part, slot, device):
        ref = block(s, i).at[part]
        copy = remote(ref, ref, send.at[slot], recv.at[slot], device)
        copy.start()
        return copy

    whole = pl.ds(0, rows)
    to_across.wait_recv()
    low_on = passed(shard, other_in, low, 3, beside)
    twin_a = passed(shard, other_in, whole, 4, twin)
    to_beside.wait_recv()
    high_on = passed(other_row, inner, high, 5, across)
    twin_b = passed(other_row, inner, whole, 6, twin)
    low_on.wait_recv()
    twin_c = passed(other_row, other_in, low, 7, twin)
    high_on.wait_recv()
    twin_d = passed(other_row, other_in, high, 8, twin)
    for copy in (to_twin, twin_a, twin_b, twin_c, twin_d):
        copy.wait_recv()
    for copy in (to_across, to_beside, to_twin, low_on, twin_a, high_on, twin_b, twin_c, twin_d):
        copy.wait_send()
    mine.wait()


def spread(own, ident):
    rows, width = own.shape
    return pl.pallas_call(
        spread_kernel,
        out_shape=jax.ShapeDtypeStruct((4, 2, rows, width), own.dtype),
        in_specs=[pl.BlockSpec(memory_space=pl.ANY)],
        out_specs=pl.BlockSpec(memory_space=pl.ANY),
        scratch_shapes=[
            pltpu.SemaphoreType.DMA,
            pltpu.SemaphoreType.DMA((9,)),
            pltpu.SemaphoreType.DMA((9,)),
        ],
        compiler_params=pltpu.CompilerParams(collective_id=ident, has_side_effects=True),
        name="spread",
    )(own)


def collect_kernel(part_ref, sum_ref, from_twin, pair, near, joined, send, recv):
    _, shard, inner, core = place()
    across, beside, twin = partners()
    rows = sum_ref.shape[0]
    low, high = pl.ds(0, SPLIT), pl.ds(SPLIT, rows - SPLIT)
    other_in, other_row = 1 - inner, lax.rem(shard + 2, 4)
    twin_shard = shard + 1 - 2 * core
    twin_row = lax.rem(twin_shard + 2, 4)
    greet(across, beside, twin)
    theirs = ((twin_row, other_in), (twin_shard, other_in), (twin_row, inner), (twin_shard, inner))
    ours = ((other_row, other_in), (shard, other_in), (other_row, inner), (shard, inner))
    to_twin = []
    for k, (s, i) in enumerate(theirs):
        copy = remote(part_ref.at[s, i], from_twin.at[k], send.at[k], recv.at[k], twin)
        copy.start()
        to_twin.append(copy)

    def add_pair(k):
        to_twin[k].wait_recv()
        s, i = ours[k]
        pair[k] = (part_ref[s, i].astype(F32) + from_twin[k].astype(F32)).astype(BF16)

    add_pair(0)
    far_low = remote(pair.at[0, low], joined.at[low], send.at[4], recv.at[4], across)
    far_high = remote(pair.at[0, high], joined.at[high], send.at[5], recv.at[5], beside)
    far_low.start()
    far_high.start()
    add_pair(1)
    near_low = remote(pair.at[1, low], near.at[0, low], send.at[6], recv.at[6], across)
    near_low.start()
    add_pair(2)
    near_high = remote(pair.at[2, high], near.at[1, high], send.at[7], recv.at[7], beside)
    near_high.start()
    far_low.wait_recv()
    pair[2, low] = (pair[2, low].astype(F32) + joined[low].astype(F32)).astype(BF16)
    last_low = remote(pair.at[2, low], near.at[1, low], send.at[8], recv.at[8], beside)
    last_low.start()
    far_high.wait_recv()
    pair[1, high] = (pair[1, high].astype(F32) + joined[high].astype(F32)).astype(BF16)
    last_high = remote(pair.at[1, high], near.at[0, high], send.at[9], recv.at[9], across)
    last_high.start()
    to_twin[3].wait_recv()
    sum_ref[...] = part_ref[shard, inner].astype(F32) + from_twin[3].astype(F32)
    near_low.wait_recv()
    last_low.wait_recv()
    sum_ref[low] = sum_ref[low] + near[0, low].astype(F32) + near[1, low].astype(F32)
    near_high.wait_recv()
    last_high.wait_recv()
    sum_ref[high] = sum_ref[high] + near[0, high].astype(F32) + near[1, high].astype(F32)
    for copy in (*to_twin, far_low, far_high, near_low, near_high, last_low, last_high):
        copy.wait_send()


def collect(part, ident):
    _, _, rows, width = part.shape
    return pl.pallas_call(
        collect_kernel,
        out_shape=jax.ShapeDtypeStruct((rows, width), F32),
        in_specs=[pl.BlockSpec(memory_space=pltpu.VMEM)],
        out_specs=pl.BlockSpec(memory_space=pltpu.VMEM),
        scratch_shapes=[
            pltpu.VMEM((4, rows, width), BF16),
            pltpu.VMEM((4, rows, width), BF16),
            pltpu.VMEM((2, rows, width), BF16),
            pltpu.VMEM((rows, width), BF16),
            pltpu.SemaphoreType.DMA((10,)),
            pltpu.SemaphoreType.DMA((10,)),
        ],
        compiler_params=pltpu.CompilerParams(
            collective_id=ident, has_side_effects=True, vmem_limit_bytes=VMEM_BYTES
        ),
        name="collect",
    )(part)


def line():
    seq, shard, inner, _ = place()
    outer = seq // 2
    return outer, {"seq": seq - 2, "shard": shard}, {"seq": seq + 2, "shard": shard}


def greet_layer_and_line(layers):
    outer, left, right = line()
    barrier = pltpu.get_barrier_semaphore()
    for device in partners():
        pl.semaphore_signal(barrier, inc=1, device_id=device, device_id_type=MESH)

    @pl.when(outer > 0)
    def _():
        pl.semaphore_signal(barrier, inc=1, device_id=left, device_id_type=MESH)

    @pl.when(outer < layers - 1)
    def _():
        pl.semaphore_signal(barrier, inc=1, device_id=right, device_id_type=MESH)

    ends = jnp.int32(outer > 0) + jnp.int32(outer < layers - 1)
    pl.semaphore_wait(barrier, 3 + ends)


def greet_line(layers, across):
    outer, left, right = line()
    barrier = pltpu.get_barrier_semaphore()
    pl.semaphore_signal(barrier, inc=1, device_id=across, device_id_type=MESH)

    @pl.when(outer > 0)
    def _():
        pl.semaphore_signal(barrier, inc=1, device_id=left, device_id_type=MESH)

    @pl.when(outer < layers - 1)
    def _():
        pl.semaphore_signal(barrier, inc=1, device_id=right, device_id_type=MESH)

    ends = jnp.int32(outer > 0) + jnp.int32(outer < layers - 1)
    pl.semaphore_wait(barrier, 1 + ends)


class Behind:
    def __init__(self):
        self.steps = []

    def add(self, name, step):
        self.steps.append((name, step))

    def upto(self, name):
        assert any(own == name for own, _ in self.steps) or name in self.done, name
        while any(own == name for own, _ in self.steps):
            self.done.add(self.steps[0][0])
            self.steps.pop(0)[1]()

    done = None


def weights_behind(layers, rows, own_ref, oth_ref, outs, send_x, recv_x, send_z, recv_z, local):
    seq, _, inner, _ = place()
    outer, left, right = line()
    across, _, _ = partners()
    other_seq = seq + 1 - 2 * inner
    count = len(outs)
    has_next = (outer < layers - 1, outer > 0)
    nexts = (right, left)
    x_copies, l_copies = {}, {}

    def has_come(direction, step):
        return outer >= step if direction == 0 else outer + step <= layers - 1

    def layer_rows(direction, step):
        origin = outer - step if direction == 0 else outer + step
        return pl.ds(pl.multiple_of(origin * 2 * rows, 16), 2 * rows)

    def seq_rows(index):
        return pl.ds(pl.multiple_of(index * rows, 16), rows)

    def z_copy(k, src, ref, direction, slot):
        return remote(
            src, ref, send_z.at[k, direction, slot], recv_z.at[k, direction, slot], nexts[direction]
        )

    def own_copy(k, direction):
        src = own_ref.at[:, pl.ds(STARTS[k], WIDTHS[k])]
        return z_copy(k, src, outs[k].at[seq_rows(seq)], direction, 0)

    def other_copy(k, direction):
        there = outs[k].at[seq_rows(other_seq)]
        return z_copy(k, there, there, direction, 1)

    def pass_copy(k, direction, step):
        ref = outs[k].at[layer_rows(direction, step - 1)]
        return z_copy(k, ref, ref, direction, step)

    def issue(k):
        cols = pl.ds(STARTS[k], WIDTHS[k])
        here = outs[k].at[seq_rows(seq)]
        x_copies[k] = remote(oth_ref.at[:, cols], here, send_x.at[k], recv_x.at[k], across)
        x_copies[k].start()
        l_copies[k] = pltpu.make_async_copy(own_ref.at[:, cols], here, local.at[k])
        l_copies[k].start()
        for direction in (0, 1):

            @pl.when(has_next[direction])
            def _():
                own_copy(k, direction).start()

    def first(k):
        x_copies[k].wait_recv()
        for direction in (0, 1):

            @pl.when(has_next[direction])
            def _():
                other_copy(k, direction).start()

    def advance(k, step):
        for direction in (0, 1):

            @pl.when(has_come(direction, step))
            def _():
                if step == 1:
                    origin = outer - 1 if direction == 0 else outer + 1
                    for slot in (0, 1):
                        part = outs[k].at[seq_rows(2 * origin + (inner if slot == 0 else 1 - inner))]
                        z_copy(k, part, part, direction, slot).wait_recv()
                else:
                    ref = outs[k].at[layer_rows(direction, step)]
                    z_copy(k, ref, ref, direction, step).wait_recv()
                if step < layers - 1:

                    @pl.when(has_next[direction])
                    def _():
                        pass_copy(k, direction, step + 1).start()

        if step == layers - 1:
            l_copies[k].wait()

    def finish():
        for k in range(count):
            x_copies[k].wait_send()
            for direction in (0, 1):

                @pl.when(has_next[direction])
                def _():
                    own_copy(k, direction).wait_send()
                    other_copy(k, direction).wait_send()
                    for step in range(2, layers):

                        @pl.when(has_come(direction, step - 1))
                        def _():
                            pass_copy(k, direction, step).wait_send()

    behind = Behind()
    behind.done = set()
    behind.add(("issue", 0), lambda: issue(0))
    behind.add(("first", 0), lambda: first(0))
    for k in range(count):
        for step in range(1, layers):
            behind.add((k, step), functools.partial(advance, k, step))
            if step == 1 and k + 1 < count:
                behind.add(("issue", k + 1), functools.partial(issue, k + 1))
            if step == min(2, layers - 1) and k + 1 < count:
                behind.add(("first", k + 1), functools.partial(first, k + 1))
    behind.add("sent", finish)
    return behind


def spread_steps(buf, send, recv):
    _, shard, inner, _ = place()
    across, beside, twin = partners()
    rows = buf.shape[1]
    low, high, whole = pl.ds(0, SPLIT), pl.ds(SPLIT, rows - SPLIT), pl.ds(0, rows)
    other_row = lax.rem(shard + 2, 4)
    me, at_across = 2 * shard + inner, 2 * shard + 1 - inner
    at_beside, far = 2 * other_row + inner, 2 * other_row + 1 - inner
    sent = []

    def push(block, part, slot, device):
        ref = buf.at[block, part]
        copy = remote(ref, ref, send.at[slot], recv.at[slot], device)
        copy.start()
        sent.append(copy)
        return copy

    from_across = push(me, whole, 0, across)
    from_beside = push(me, whole, 1, beside)
    push(me, whole, 2, twin)
    yield
    from_across.wait_recv()
    far_low = push(at_across, low, 3, beside)
    push(at_across, whole, 4, twin)
    yield
    from_beside.wait_recv()
    far_high = push(at_beside, high, 5, across)
    push(at_beside, whole, 6, twin)
    yield
    far_low.wait_recv()
    push(far, low, 7, twin)
    far_high.wait_recv()
    push(far, high, 8, twin)
    yield
    for slot in (2, 4, 6, 7, 8):
        sent[slot].wait_recv()
    for copy in sent:
        copy.wait_send()


def collect_steps(part, total, pair, near, joined, send, recv):
    _, shard, inner, core = place()
    across, beside, twin = partners()
    rows = total.shape[0]
    low, high = pl.ds(0, SPLIT), pl.ds(SPLIT, rows - SPLIT)

    def blocks(s):
        row = lax.rem(s + 2, 4)
        return (2 * row + 1 - inner, 2 * s + 1 - inner, 2 * row + inner, 2 * s + inner)

    theirs, ours = blocks(shard + 1 - 2 * core), blocks(shard)
    copies = {}

    def push(slot, src, dst, device):
        copies[slot] = remote(src, dst, send.at[slot], recv.at[slot], device)
        copies[slot].start()

    for k in range(4):
        push(k, part.at[theirs[k]], pair.at[k], twin)
    yield

    def add_pair(k):
        copies[k].wait_recv()
        pair[k] = (part[ours[k]].astype(F32) + pair[k].astype(F32)).astype(BF16)

    add_pair(0)
    push(4, pair.at[0, low], joined.at[low], across)
    push(5, pair.at[0, high], joined.at[high], beside)
    add_pair(1)
    push(6, pair.at[1, low], near.at[0, low], across)
    add_pair(2)
    push(7, pair.at[2, high], near.at[1, high], beside)
    copies[3].wait_recv()
    total[...] = part[ours[3]].astype(F32) + pair[3].astype(F32)
    yield
    copies[4].wait_recv()
    pair[2, low] = (pair[2, low].astype(F32) + joined[low].astype(F32)).astype(BF16)
    push(8, pair.at[2, low], near.at[1, low], beside)
    copies[5].wait_recv()
    pair[1, high] = (pair[1, high].astype(F32) + joined[high].astype(F32)).astype(BF16)
    push(9, pair.at[1, high], near.at[0, high], across)
    yield
    copies[6].wait_recv()
    copies[8].wait_recv()
    total[low] = total[low] + near[0, low].astype(F32) + near[1, low].astype(F32)
    copies[7].wait_recv()
    copies[9].wait_recv()
    total[high] = total[high] + near[0, high].astype(F32) + near[1, high].astype(F32)
    for slot in range(10):
        copies[slot].wait_send()


def dot(left, right):
    return jnp.dot(left, right, preferred_element_type=F32)


def dot_rows(left, right):
    return lax.dot_general(left, right, (((1,), (1,)), ((), ())), preferred_element_type=F32)


FRONT_REFS = (
    "tok",
    "cot",
    "gains",
    "taps",
    "own",
    "oth",
    "w0",
    "w1",
    "w2",
    "w3",
    "n1_out",
    "dout",
    "normed",
    "b_all",
    "c_all",
    "x_all",
    "gated",
    "mixed",
    "act",
    "dgate",
    "dup",
    "resid",
    "part",
    "pair",
    "near",
    "joined",
    "spill",
    "halo_send",
    "halo_recv",
    "local",
    "send_x",
    "recv_x",
    "send_z",
    "recv_z",
    "send_s",
    "recv_s",
    "send_c",
    "recv_c",
)


def front_kernel(layers, rows, *all_refs):
    r = dict(zip(FRONT_REFS, all_refs, strict=True))
    tok, cot, gains, taps = r["tok"], r["cot"], r["gains"], r["taps"]
    normed, dout, gated, part = r["normed"], r["dout"], r["gated"], r["part"]
    weights = (r["w0"], r["w1"], r["w2"], r["w3"])
    seg = tok.shape[0]
    _, shard, inner, _ = place()
    outer, left, right = line()
    me = 2 * shard + inner
    greet_layer_and_line(layers)
    behind = weights_behind(
        layers, rows, r["own"], r["oth"], weights,
        r["send_x"], r["recv_x"], r["send_z"], r["recv_z"], r["local"],
    )
    last = layers - 1
    behind.upto(("issue", 0))

    values = tok[...].astype(F32)
    scale = lax.rsqrt(jnp.mean(values * values, axis=-1, keepdims=True) + NORM_EPSILON)
    normed[me] = (values * scale * gains[0:1, :]).astype(BF16)
    one = spread_steps(normed, r["send_s"].at[0], r["recv_s"].at[0])
    next(one)
    dout[me] = cot[...]
    behind.upto(("first", 0))
    next(one)
    next(one)
    behind.upto((0, 1))
    next(one)
    up = spread_steps(dout, r["send_s"].at[1], r["recv_s"].at[1])
    next(up)
    for _ in one:
        pass
    spilled = pltpu.make_async_copy(normed, r["n1_out"], r["spill"])
    spilled.start()
    next(up)
    next(up)
    behind.upto((0, last))

    lanes = lax.broadcasted_iota(jnp.int32, (seg, WIDE), 1) < HALF_Q

    def project(s, _):
        for i in (0, 1):
            t = 2 * s + i
            parts = dot(normed[t], weights[0][...])
            b = jnp.where(lanes, parts[:, :WIDE], 0.0)
            middle = pltpu.roll(parts[:, 128 : 128 + 384], 384 - 64, 1)[:, :WIDE]
            x = parts[:, 384 : 384 + WIDE]
            r["b_all"][t] = b
            r["c_all"][t] = jnp.where(lanes, middle, 0.0)
            r["x_all"][t] = x
            gated[s, pl.ds(8 + i * seg, seg)] = (b * x).astype(BF16).astype(F32)
        return 0

    lax.fori_loop(0, GROUPS, project, 0)
    halo = remote(
        gated.at[:, pl.ds(2 * seg, 8)], gated.at[:, pl.ds(0, 8)], r["halo_send"], r["halo_recv"], right
    )

    @pl.when(outer < layers - 1)
    def _():
        halo.start()

    @pl.when(outer == 0)
    def _():
        gated[:, pl.ds(0, 8)] = jnp.zeros((GROUPS, 8, WIDE), F32)

    next(up)
    behind.upto((1, 1))

    @pl.when(outer > 0)
    def _():
        halo.wait_recv()

    def convolve(s, _):
        for i in (0, 1):
            t = 2 * s + i
            conv = (
                taps[0:1, :] * gated[s, pl.ds(6 + i * seg, seg)]
                + taps[1:2, :] * gated[s, pl.ds(7 + i * seg, seg)]
                + taps[2:3, :] * gated[s, pl.ds(8 + i * seg, seg)]
            )
            mixed = pltpu.roll(r["c_all"][t] * conv, 64, 1).astype(BF16)
            r["mixed"][t] = mixed
            part[t] = dot_rows(mixed, weights[0][:, pl.ds(512, WIDE)]).astype(BF16)
        return 0

    lax.fori_loop(0, GROUPS, convolve, 0)
    spilled.wait()
    for _ in up:
        pass

    branch = collect_steps(
        part, r["resid"], r["pair"], r["near"], r["joined"], r["send_c"].at[0], r["recv_c"].at[0]
    )
    next(branch)
    next(branch)
    next(branch)
    behind.upto((1, min(2, last)))
    for _ in branch:
        pass
    values = tok[...].astype(F32) + r["resid"][...]
    r["resid"][...] = values
    scale = lax.rsqrt(jnp.mean(values * values, axis=-1, keepdims=True) + NORM_EPSILON)
    normed[me] = (values * scale * gains[1:2, :]).astype(BF16)
    two = spread_steps(normed, r["send_s"].at[2], r["recv_s"].at[2])
    next(two)
    next(two)
    next(two)
    behind.upto((1, last))
    for _ in two:
        pass

    for chunk, (start, units) in enumerate(zip(UNIT_STARTS, UNIT_CHUNKS)):
        behind.upto((chunk + 1, last))
        held = weights[chunk + 1]
        cols = pl.ds(start, units)

        def hidden(t, _):
            gate = dot(normed[t], held[:, pl.ds(0, units)])
            upval = dot(normed[t], held[:, pl.ds(units, units)])
            dact = dot(dout[t], held[:, pl.ds(2 * units, units)])
            sigma = jax.nn.sigmoid(gate)
            silu = gate * sigma
            r["act"][t, :, cols] = (silu * upval).astype(BF16)
            r["dgate"][t, :, cols] = (dact * upval * sigma * (1.0 + gate * (1.0 - sigma))).astype(BF16)
            r["dup"][t, :, cols] = (dact * silu).astype(BF16)
            return 0

        lax.fori_loop(0, 2 * GROUPS, hidden, 0)
    behind.upto("sent")

    @pl.when(outer < layers - 1)
    def _():
        halo.wait_send()


def front(tok, cot, gains, taps, own, oth, layers, ident):
    rows, seg = own.shape[0], tok.shape[0]
    count = len(WIDTHS)
    blocks = 2 * GROUPS
    vmem, anywhere = pl.BlockSpec(memory_space=pltpu.VMEM), pl.BlockSpec(memory_space=pl.ANY)
    shape = jax.ShapeDtypeStruct
    out_shape = (
        [shape((D, width), BF16) for width in WIDTHS]
        + [shape((blocks, seg, D), BF16)] * 3
        + [shape((blocks, seg, WIDE), F32)] * 3
        + [shape((GROUPS, 8 + 2 * seg, WIDE), F32), shape((blocks, seg, WIDE), BF16)]
        + [shape((blocks, seg, PAD_F), BF16)] * 3
        + [shape((seg, D), F32)]
    )
    out_specs = [vmem] * len(out_shape)
    out_specs[count] = anywhere
    dma = pltpu.SemaphoreType.DMA
    slots = max(layers, 2)
    return pl.pallas_call(
        functools.partial(front_kernel, layers, rows),
        out_shape=out_shape,
        in_specs=[vmem] * 4 + [anywhere] * 2,
        out_specs=out_specs,
        scratch_shapes=[
            pltpu.VMEM((blocks, seg, D), BF16),
            pltpu.VMEM((4, seg, D), BF16),
            pltpu.VMEM((2, seg, D), BF16),
            pltpu.VMEM((seg, D), BF16),
            dma,
            dma,
            dma,
            dma((count,)),
            dma((count,)),
            dma((count,)),
            dma((count, 2, slots)),
            dma((count, 2, slots)),
            dma((3, 9)),
            dma((3, 9)),
            dma((1, 10)),
            dma((1, 10)),
        ],
        compiler_params=pltpu.CompilerParams(
            collective_id=ident, has_side_effects=True, vmem_limit_bytes=VMEM_BYTES
        ),
        name="front",
    )(tok, cot, gains, taps, own, oth)


def reduce_weights_kernel(layers, rows, *refs):
    count = len(WIDTHS)
    grads, mine, theirs = refs[:count], refs[count : 2 * count], refs[2 * count : 3 * count]
    refs = refs[3 * count :]
    slots, refs = refs[:count], refs[count:]
    final, outgoing = refs[:count], refs[count : 2 * count]
    send_z, recv_z, send_x, recv_x = refs[2 * count :]
    seq, _, inner, _ = place()
    outer, left, right = line()
    across, _, _ = partners()
    greet_line(layers, across)
    nexts = (right, left)

    def z_copy(k, src, direction, owner):
        index = owner - 1 if direction == 0 else owner
        return remote(
            src,
            slots[k].at[direction, index],
            send_z.at[k, direction, index],
            recv_z.at[k, direction, index],
            nexts[direction],
        )

    def slot(k, direction, owner):
        return slots[k].at[direction, owner - 1 if direction == 0 else owner]

    def owner_rows(owner):
        return pl.ds(owner * 2 * rows, 2 * rows)

    def came(direction):
        return outer > 0 if direction == 0 else outer < layers - 1

    def goes(direction, owner):
        return owner > outer if direction == 0 else owner < outer

    def travel(k):
        for step in range(layers - 1):
            for direction in (0, 1):
                owner = layers - 1 - step if direction == 0 else step

                @pl.when(goes(direction, owner) & came(direction))
                def _():
                    ref = slot(k, direction, owner)
                    z_copy(k, ref, direction, owner).wait_recv()
                    ref[...] = (
                        ref[...].astype(F32) + grads[k][owner_rows(owner)].astype(F32)
                    ).astype(BF16)
                    z_copy(k, ref, direction, owner).start()

                @pl.when(goes(direction, owner) & jnp.logical_not(came(direction)))
                def _():
                    z_copy(k, grads[k].at[owner_rows(owner)], direction, owner).start()

    x_copies = []

    def finish(k):
        total = final[k]
        total[...] = grads[k][pl.ds(pl.multiple_of(outer * 2 * rows, 16), 2 * rows)].astype(F32)
        for direction in (0, 1):
            for owner in range(1, layers) if direction == 0 else range(layers - 1):

                @pl.when((outer == owner) & came(direction))
                def _():
                    ref = slot(k, direction, owner)
                    z_copy(k, ref, direction, owner).wait_recv()
                    total[...] += ref[...].astype(F32)

        mine[k][...] = total[pl.ds(pl.multiple_of(inner * rows, 16), rows)]
        outgoing[k][...] = total[pl.ds(pl.multiple_of((1 - inner) * rows, 16), rows)].astype(BF16)
        copy = remote(outgoing[k], theirs[k], send_x.at[k], recv_x.at[k], across)
        copy.start()
        x_copies.append(copy)

    travel(0)
    for k in range(count):
        if k + 1 < count:
            travel(k + 1)
        finish(k)
    for k in range(count):
        x_copies[k].wait()
        for direction in (0, 1):
            for owner in range(1, layers) if direction == 0 else range(layers - 1):

                @pl.when(goes(direction, owner))
                def _():
                    z_copy(k, slot(k, direction, owner), direction, owner).wait_send()


def reduce_weights(grads, layers, rows, ident):
    count = len(WIDTHS)
    vmem = pl.BlockSpec(memory_space=pltpu.VMEM)
    hops = layers - 1
    results = pl.pallas_call(
        functools.partial(reduce_weights_kernel, layers, rows),
        out_shape=[jax.ShapeDtypeStruct((rows, width), F32) for width in WIDTHS]
        + [jax.ShapeDtypeStruct((rows, width), BF16) for width in WIDTHS],
        in_specs=[vmem] * count,
        out_specs=[vmem] * (2 * count),
        scratch_shapes=[pltpu.VMEM((2, hops, 2 * rows, width), BF16) for width in WIDTHS]
        + [pltpu.VMEM((2 * rows, width), F32) for width in WIDTHS]
        + [pltpu.VMEM((rows, width), BF16) for width in WIDTHS]
        + [
            pltpu.SemaphoreType.DMA((count, 2, hops)),
            pltpu.SemaphoreType.DMA((count, 2, hops)),
            pltpu.SemaphoreType.DMA((count,)),
            pltpu.SemaphoreType.DMA((count,)),
        ],
        compiler_params=pltpu.CompilerParams(
            collective_id=ident, has_side_effects=True, vmem_limit_bytes=VMEM_BYTES
        ),
        name="reduce_weights",
    )(*grads)
    return results[:count], results[count:]


def unit_pieces(half):
    pieces = []
    for start, units in zip(UNIT_STARTS, UNIT_CHUNKS):
        real = min(units, HALF_F - start)
        for m in range(3):
            first = 4 * QUARTER + m * UNITS + half * HALF_F + start
            pieces.append((m, first, real, units - real))
    return pieces


def halves(local, inner):
    def half(h):
        parts = [local[:, m * QUARTER + h * HALF_Q : m * QUARTER + (h + 1) * HALF_Q] for m in range(4)]
        for _, first, real, padding in unit_pieces(h):
            parts.append(jnp.pad(local[:, first : first + real], ((0, 0), (0, padding))))
        return jnp.concatenate(parts, axis=1)

    low, high = half(0), half(1)
    is_low = inner == 0
    return jnp.where(is_low, low, high), jnp.where(is_low, high, low)


def joined_columns(mine, theirs, inner):
    is_low = inner == 0
    parts = []
    for m in range(4):
        a = mine[0][:, m * HALF_Q : (m + 1) * HALF_Q]
        b = theirs[0][:, m * HALF_Q : (m + 1) * HALF_Q].astype(F32)
        parts += [jnp.where(is_low, a, b), jnp.where(is_low, b, a)]
    for m in range(3):
        for swap in (False, True):
            for chunk, (start, units) in enumerate(zip(UNIT_STARTS, UNIT_CHUNKS)):
                real = min(units, HALF_F - start)
                a = mine[1 + chunk][:, m * units : m * units + real]
                b = theirs[1 + chunk][:, m * units : m * units + real].astype(F32)
                parts.append(jnp.where(is_low, b, a) if swap else jnp.where(is_low, a, b))
    return jnp.concatenate(parts, axis=1)


def shifted(block, distance):
    devices = range(lax.axis_size("seq"))
    route = [(i - distance, i) for i in devices if i - distance in devices]
    return lax.ppermute(block, "seq", route)


def root_norm(values, gain):
    scale = lax.rsqrt(jnp.mean(values * values, axis=-1, keepdims=True) + NORM_EPSILON)
    return (values * scale * gain, scale)


def norm_back(values, scale, gain, upstream):
    scaled = gain * upstream
    inner = jnp.mean(scaled * values, axis=-1, keepdims=True)
    return (
        scale * scaled - values * scale * scale * scale * inner,
        jnp.sum(upstream * values * scale, axis=0),
    )


def times_rows(left, right):
    return lax.dot_general(left, right, (((1,), (1,)), ((), ())), preferred_element_type=F32)


def outer_sum(left, right):
    return lax.dot_general(left, right, (((0,), (0,)), ((), ())), preferred_element_type=F32)


def adam_update(param, grad, first, second, rate, decay):
    first_new = MOMENT_DECAY * first + (1.0 - MOMENT_DECAY) * grad
    second_new = SQUARE_DECAY * second + (1.0 - SQUARE_DECAY) * grad * grad
    first_hat = first_new / (1.0 - MOMENT_DECAY**STEP)
    second_hat = second_new / (1.0 - SQUARE_DECAY**STEP)
    param_new = param - rate * (first_hat / (jnp.sqrt(second_hat) + ADAM_EPSILON) + decay * param)
    return (first_new, second_new, param_new)


def conv_backward(dconv, gated, taps):
    length = dconv.shape[1]
    after = shifted(dconv[:, :2], -2)
    padded = jnp.concatenate([dconv, after], axis=1)
    dgated = taps[2] * dconv + taps[1] * padded[:, 1 : 1 + length] + taps[0] * padded[:, 2 : 2 + length]
    dtaps = jnp.stack([jnp.sum(dconv * gated[:, 6 + k : 6 + k + length], axis=(0, 1)) for k in range(3)])
    return (dgated, dtaps)


def on_device(
    tokens, gains_taps, weights, cotangent, weight_first, weight_second, gains_first, gains_second
):
    seq, shard = lax.axis_index("seq"), lax.axis_index("shard")
    inner = seq % 2
    rows = weights.shape[0]
    layers = lax.axis_size("seq") // 2
    inputs = tokens[0].astype(F32)
    seg_len = inputs.shape[0]
    layer_tokens = GROUPS * 2 * seg_len

    own, oth = halves(weights.astype(BF16), inner)

    def as_rows(blocks):
        return blocks.reshape(layer_tokens, blocks.shape[-1])

    def as_blocks(values):
        return values.astype(BF16).reshape(GROUPS, 2, seg_len, D)

    col = shard * QUARTER + inner * HALF_Q
    taps = lax.dynamic_slice(gains_taps, (2, col), (3, HALF_Q))
    taps_wide = jnp.pad(taps, ((0, 0), (0, WIDE - HALF_Q)))
    (
        w_conv, w_one, w_two, w_three, n1, dout, n2, b_all, c_all, x_all, gated, mixed, act, dgate, dup, resid,
    ) = front(tokens[0], cotangent[0], gains_taps, taps_wide, own, oth, layers, 0)
    w_units = (w_one, w_two, w_three)
    w_bcx, w_out_t = w_conv[:, : 3 * HALF_Q], w_conv[:, 3 * HALF_Q :]
    normed, upstream, normed_two = as_rows(n1), as_rows(dout), as_rows(n2)
    b_part, c_part, x_part = (as_rows(v)[:, :HALF_Q] for v in (b_all, c_all, x_all))
    mixed = as_rows(mixed)[:, WIDE - HALF_Q :]
    gated = gated[:, :, :HALF_Q]
    length = 2 * seg_len
    conv_rows = sum(taps[k] * gated[:, 6 + k : 6 + k + length] for k in range(3)).reshape(layer_tokens, HALF_Q)
    active, dgate, dup = as_rows(act), as_rows(dgate), as_rows(dup)
    _, scale_one = root_norm(inputs, gains_taps[0])
    _, scale_two = root_norm(resid, gains_taps[1])

    def over_units(values, m):
        return sum(
            times_rows(values[:, start : start + units], w[:, m * units : (m + 1) * units])
            for start, units, w in zip(UNIT_STARTS, UNIT_CHUNKS, w_units)
        )

    dnormed_two = collect(as_blocks(over_units(dgate, 0) + over_units(dup, 1)), 5)
    ffn_out = collect(as_blocks(over_units(active, 2)), 6)
    block_out = (resid + ffn_out).astype(BF16)
    dresid_part, grad_gain_two = norm_back(resid, scale_two, gains_taps[1], dnormed_two)
    dresid = cotangent[0].astype(F32) + dresid_part
    dbranch = as_rows(spread(dresid.astype(BF16), 7))
    dmixed = jnp.dot(dbranch, w_out_t, preferred_element_type=F32)
    dc_part = (dmixed * conv_rows).astype(BF16)
    dconv = (dmixed * c_part).reshape(GROUPS, 2 * seg_len, HALF_Q)
    dgated, dtaps = conv_backward(dconv, gated, taps)
    dgated_rows = dgated.reshape(layer_tokens, HALF_Q)
    db_part = (dgated_rows * x_part).astype(BF16)
    dx_part = (dgated_rows * b_part).astype(BF16)
    dparts = jnp.concatenate([db_part, dc_part, dx_part], axis=1)
    dnormed = collect(as_blocks(times_rows(dparts, w_bcx)), 8)
    dinput_part, grad_gain_one = norm_back(inputs, scale_one, gains_taps[0], dnormed)
    input_grad = (dresid + dinput_part).astype(BF16)

    grads = [jnp.concatenate([outer_sum(normed, dparts), outer_sum(dbranch, mixed)], axis=1).astype(BF16)]
    for start, units in zip(UNIT_STARTS, UNIT_CHUNKS):
        part = slice(start, start + units)
        grads.append(
            jnp.concatenate(
                [
                    outer_sum(normed_two, dgate[:, part]),
                    outer_sum(normed_two, dup[:, part]),
                    outer_sum(upstream, active[:, part]),
                ],
                axis=1,
            ).astype(BF16)
        )
    mine, theirs = reduce_weights(grads, layers, rows, 9)
    weight_grad = joined_columns(mine, theirs, inner)

    dtaps_wide = lax.dynamic_update_slice(jnp.zeros((3, D), F32), dtaps, (0, col))
    local_gains = jnp.concatenate([grad_gain_one[None], grad_gain_two[None], dtaps_wide], axis=0)
    gains_grad = lax.psum(local_gains, ("seq", "shard"))
    weight_first_new, weight_second_new, weight_new = adam_update(
        weights, weight_grad, weight_first, weight_second, WEIGHT_RATE, WEIGHT_DECAY
    )
    gains_first_new, gains_second_new, gains_new = adam_update(
        gains_taps, gains_grad, gains_first, gains_second, GAIN_RATE, 0.0
    )
    return (
        block_out[None],
        input_grad[None],
        weight_grad,
        weight_first_new,
        weight_second_new,
        weight_new,
        gains_grad,
        gains_first_new,
        gains_second_new,
        gains_new,
    )


def solution(mesh):
    tokens, rows, whole = P("shard", "seq", None), P("seq", "shard"), P()
    return jax.shard_map(
        on_device,
        mesh=mesh,
        in_specs=(tokens, whole, rows, tokens, rows, rows, whole, whole),
        out_specs=(tokens, tokens, rows, rows, rows, rows, whole, whole, whole, whole),
        check_vma=False,
    )
```

```python
import functools

import jax
import jax.numpy as jnp
from jax import lax
from jax.experimental import pallas as pl
from jax.experimental.pallas import tpu as pltpu
from jax.sharding import PartitionSpec as P

D = 1536
FF = 6912
STEP = 10
GROUPS = 4
QUARTER = D // GROUPS
UNITS = FF // GROUPS
HALF_Q = QUARTER // 2
HALF_F = UNITS // 2
LANES = 128
PAD_F = -(-HALF_F // LANES) * LANES
WIDE = 256
CONV_COLS = 4 * HALF_Q
UNIT_CHUNKS = (384, 256, PAD_F - 640)
UNIT_STARTS = (0, 384, 640)
WIDTHS = (CONV_COLS,) + tuple(3 * units for units in UNIT_CHUNKS)
STARTS = tuple(sum(WIDTHS[:k]) for k in range(len(WIDTHS)))
SPLIT = 128
REACH = (1, 2, 2, 2)
SLICE = 384
TILE = 32
ROWS = 48

MOMENT_DECAY = 0.9
SQUARE_DECAY = 0.95
ADAM_EPSILON = 1e-08
NORM_EPSILON = 1e-05
WEIGHT_RATE = 0.02
GAIN_RATE = 0.2
WEIGHT_DECAY = 0.1

BF16 = jnp.bfloat16
F32 = jnp.float32
MESH = pl.DeviceIdType.MESH
VMEM_BYTES = 63 * 1024 * 1024


def place():
    seq, shard = lax.axis_index("seq"), lax.axis_index("shard")
    inner, core = lax.rem(seq, 2), lax.rem(shard, 2)
    return seq, shard, inner, core


def partners():
    seq, shard, inner, core = place()
    across = {"seq": seq + 1 - 2 * inner, "shard": shard}
    beside = {"seq": seq, "shard": lax.rem(shard + 2, 4)}
    twin = {"seq": seq, "shard": shard + 1 - 2 * core}
    return across, beside, twin


def remote(src, dst, send, recv, device):
    return pltpu.make_async_remote_copy(
        src_ref=src, dst_ref=dst, send_sem=send, recv_sem=recv, device_id=device, device_id_type=MESH
    )


def line():
    seq, shard, _, _ = place()
    return seq // 2, lambda steps: {"seq": seq + 2 * steps, "shard": shard}


def greet(layers):
    outer, at = line()
    barrier = pltpu.get_barrier_semaphore()
    for device in partners():
        pl.semaphore_signal(barrier, inc=1, device_id=device, device_id_type=MESH)
    for steps in range(1, layers):
        for sign in (1, -1):

            @pl.when(in_line(outer + sign * steps, layers))
            def _():
                pl.semaphore_signal(barrier, inc=1, device_id=at(sign * steps), device_id_type=MESH)

    pl.semaphore_wait(barrier, 3 + layers - 1)


def in_line(index, layers):
    return (index >= 0) & (index < layers)


def allow(credit):
    for device in partners():
        pl.semaphore_signal(credit, inc=1, device_id=device, device_id_type=MESH)


def dot(left, right):
    return jnp.dot(left, right, preferred_element_type=F32)


def dot_rows(left, right):
    return lax.dot_general(left, right, (((1,), (1,)), ((), ())), preferred_element_type=F32)


def dot_columns(left, right):
    return lax.dot_general(left, right, (((0,), (0,)), ((), ())), preferred_element_type=F32)


def aligned(start, size, multiple=16):
    return pl.ds(pl.multiple_of(start, multiple), size)


class Gather:
    def __init__(self, layers, rows, own, oth, outs, send_x, recv_x, send_z, recv_z, local):
        self.layers, self.rows, self.own, self.oth, self.outs = layers, rows, own, oth, outs
        self.send_x, self.recv_x, self.send_z, self.recv_z, self.local = send_x, recv_x, send_z, recv_z, local
        self.seq, _, self.inner, _ = place()
        self.outer, self.at = line()
        self.across = partners()[0]
        self.x_copies, self.l_copies = {}, {}
        self.reached = {k: 0 for k in range(len(outs))}

    def seq_rows(self, index):
        return aligned(index * self.rows, self.rows)

    def layer_rows(self, direction, distance):
        origin = self.outer - distance if direction == 0 else self.outer + distance
        return aligned(origin * 2 * self.rows, 2 * self.rows)

    def copy(self, k, src, dst, direction, distance, hop, piece):
        slot = (k, direction, distance + hop - 1, piece)
        return remote(
            src, dst, self.send_z.at[slot], self.recv_z.at[slot], self.at(hop if direction == 0 else -hop)
        )

    def goes(self, direction, hop):
        return in_line(self.outer + (hop if direction == 0 else -hop), self.layers)

    def has_come(self, direction, distance):
        return in_line(self.outer + (-distance if direction == 0 else distance), self.layers)

    def hops(self, k, distance):
        return range(1, min(REACH[k], self.layers - 1 - distance) + 1)

    def own_copy(self, k, direction, hop):
        src = self.own.at[:, pl.ds(STARTS[k], WIDTHS[k])]
        return self.copy(k, src, self.outs[k].at[self.seq_rows(self.seq)], direction, 0, hop, 0)

    def other_copy(self, k, direction, hop):
        there = self.outs[k].at[self.seq_rows(self.seq + 1 - 2 * self.inner)]
        return self.copy(k, there, there, direction, 0, hop, 1)

    def pass_copy(self, k, direction, distance, hop):
        ref = self.outs[k].at[self.layer_rows(direction, distance)]
        return self.copy(k, ref, ref, direction, distance, hop, 0)

    def exchange(self, k):
        cols = pl.ds(STARTS[k], WIDTHS[k])
        here = self.outs[k].at[self.seq_rows(self.seq)]
        self.x_copies[k] = remote(
            self.oth.at[:, cols], here, self.send_x.at[k], self.recv_x.at[k], self.across
        )
        self.x_copies[k].start()
        self.l_copies[k] = pltpu.make_async_copy(self.own.at[:, cols], here, self.local.at[k])
        self.l_copies[k].start()

    def send_own(self, k):
        for hop in self.hops(k, 0):
            for direction in (0, 1):

                @pl.when(self.goes(direction, hop))
                def _():
                    self.own_copy(k, direction, hop).start()

    def send_other(self, k):
        self.x_copies[k].wait_recv()
        for hop in self.hops(k, 0):
            for direction in (0, 1):

                @pl.when(self.goes(direction, hop))
                def _():
                    self.other_copy(k, direction, hop).start()

    def step(self, k, distance):
        for direction in (0, 1):

            @pl.when(self.has_come(direction, distance))
            def _():
                if distance <= REACH[k]:
                    origin = self.outer - distance if direction == 0 else self.outer + distance
                    for piece in (0, 1):
                        index = 2 * origin + (self.inner if piece == 0 else 1 - self.inner)
                        ref = self.outs[k].at[self.seq_rows(index)]
                        self.copy(k, ref, ref, direction, distance - 1, 1, piece).wait_recv()
                else:
                    ref = self.outs[k].at[self.layer_rows(direction, distance)]
                    self.copy(k, ref, ref, direction, distance - 1, 1, 0).wait_recv()
                if distance % REACH[k] == 0:
                    for hop in self.hops(k, distance):

                        @pl.when(self.goes(direction, hop))
                        def _():
                            self.pass_copy(k, direction, distance, hop).start()

        if distance == self.layers - 1:
            self.l_copies[k].wait()

    def upto(self, k, distance=None):
        limit = self.layers - 1 if distance is None else min(distance, self.layers - 1)
        while self.reached[k] < limit:
            self.reached[k] += 1
            self.step(k, self.reached[k])

    def finish(self):
        for k in range(len(self.outs)):
            self.x_copies[k].wait_send()
            for distance in range(0, self.layers - 1, REACH[k]):
                for hop in self.hops(k, distance):
                    for direction in (0, 1):

                        @pl.when(self.goes(direction, hop) & self.has_come(direction, distance))
                        def _():
                            if distance == 0:
                                self.own_copy(k, direction, hop).wait_send()
                                self.other_copy(k, direction, hop).wait_send()
                            else:
                                self.pass_copy(k, direction, distance, hop).wait_send()


class Reduce:
    def __init__(self, layers, rows, grads, slots, stage, total, outgoing, mine, theirs, sems):
        self.layers, self.rows, self.grads, self.slots = layers, rows, grads, slots
        self.stage, self.total, self.outgoing, self.mine, self.theirs = stage, total, outgoing, mine, theirs
        self.send_g, self.recv_g, self.fetched, self.stored, self.send_o, self.recv_o = sems
        _, _, self.inner, _ = place()
        self.outer, self.at = line()
        self.across = partners()[0]
        self.stores, self.o_copies = [], []

    def owner(self, direction, distance):
        return self.outer + distance if direction == 0 else self.outer - distance

    def upstream(self, direction, steps):
        return in_line(self.outer - steps if direction == 0 else self.outer + steps, self.layers)

    def block(self, k, owner):
        return self.grads[k].at[aligned(owner * 2 * self.rows, 2 * self.rows), pl.ds(0, WIDTHS[k])]

    def copy(self, k, src, direction, distance):
        hop = 1 if distance % 2 else 2
        slot = (direction, distance - 1)
        return remote(
            src,
            self.slots[k].at[slot],
            self.send_g.at[(k,) + slot],
            self.recv_g.at[(k,) + slot],
            self.at(hop if direction == 0 else -hop),
        )

    def send(self, k, direction, distance):
        self.copy(k, self.block(k, self.owner(direction, distance)), direction, distance).start()

    def direct(self, k, part):
        for distance in range(self.layers - 1, 0, -1):
            for direction in (0, 1):
                owner = self.owner(direction, distance)
                here = in_line(owner, self.layers) & (owner * 2 * self.rows // SLICE == part)
                if distance % 2 == 0:
                    here = here & jnp.logical_not(self.upstream(direction, 1))

                @pl.when(here)
                def _():
                    self.send(k, direction, distance)

    def fetch(self, k, direction, distance):
        slot = self.slots[k].at[direction, distance - 1]
        self.copy(k, slot, direction, distance).wait_recv()
        held = self.stage.at[:, pl.ds(0, WIDTHS[k])]
        copy = pltpu.make_async_copy(slot, held, self.fetched)
        copy.start()
        copy.wait()

    def tiles(self, body):
        def step(n, _):
            body(aligned(n * TILE, TILE))
            return 0

        lax.fori_loop(0, 2 * self.rows // TILE, step, 0)

    def join(self, k):
        cols = pl.ds(0, WIDTHS[k])
        for distance in range((self.layers - 1) // 2 * 2, 0, -2):
            for direction in (0, 1):
                owner = self.owner(direction, distance)

                @pl.when(in_line(owner, self.layers) & self.upstream(direction, 1))
                def _():
                    def add(tile):
                        base = self.owner(direction, distance) * 2 * self.rows
                        rows = pl.ds(pl.multiple_of(base + tile.start, 16), TILE)
                        ref = self.grads[k]
                        ref[rows, cols] = (
                            ref[rows, cols].astype(F32) + self.stage[tile, cols].astype(F32)
                        ).astype(BF16)

                    self.fetch(k, direction, distance + 1)
                    self.tiles(add)
                    if distance + 2 < self.layers:

                        @pl.when(self.upstream(direction, 2))
                        def _():
                            self.fetch(k, direction, distance + 2)
                            self.tiles(add)

                    self.send(k, direction, distance)

    def final(self, k):
        cols = pl.ds(0, WIDTHS[k])
        if self.stores:
            self.stores[-1].wait()

        def begin(tile):
            rows = pl.ds(pl.multiple_of(self.outer * 2 * self.rows + tile.start, 16), TILE)
            self.total[tile, cols] = self.grads[k][rows, cols].astype(F32)

        def add(tile):
            self.total[tile, cols] = self.total[tile, cols] + self.stage[tile, cols].astype(F32)

        self.tiles(begin)
        for distance in range(1, min(2, self.layers - 1) + 1):
            for direction in (0, 1):

                @pl.when(self.upstream(direction, distance))
                def _():
                    self.fetch(k, direction, distance)
                    self.tiles(add)

        wide = pl.ds(STARTS[k], WIDTHS[k])
        here, there = aligned(self.inner * self.rows, self.rows), aligned((1 - self.inner) * self.rows, self.rows)
        self.outgoing[:, wide] = self.total[there, cols].astype(BF16)
        copy = remote(
            self.outgoing.at[:, wide], self.theirs.at[:, wide], self.send_o.at[k], self.recv_o.at[k], self.across
        )
        copy.start()
        self.o_copies.append(copy)
        store = pltpu.make_async_copy(self.total.at[here, cols], self.mine.at[:, wide], self.stored.at[k])
        store.start()
        self.stores.append(store)

    def wait_sent(self, k):
        for distance in range(1, self.layers):
            for direction in (0, 1):
                owner = self.owner(direction, distance)

                @pl.when(in_line(owner, self.layers))
                def _():
                    self.copy(k, self.block(k, owner), direction, distance).wait_send()

    def finish(self):
        self.stores[-1].wait()
        for copy in self.o_copies:
            copy.wait()


def spread_steps(buf, seg, send, recv):
    _, shard, inner, _ = place()
    across, beside, twin = partners()
    low, high, whole = (0, SPLIT), (SPLIT, seg - SPLIT), (0, seg)
    other_row = lax.rem(shard + 2, 4)
    me, at_across = 2 * shard + inner, 2 * shard + 1 - inner
    at_beside, far = 2 * other_row + inner, 2 * other_row + 1 - inner
    sent = []

    def push(block, part, slot, device):
        ref = buf.at[aligned(block * seg + part[0], part[1])]
        copy = remote(ref, ref, send.at[slot], recv.at[slot], device)
        copy.start()
        sent.append(copy)
        return copy

    from_across = push(me, whole, 0, across)
    from_beside = push(me, whole, 1, beside)
    push(me, whole, 2, twin)
    yield
    from_across.wait_recv()
    far_low = push(at_across, low, 3, beside)
    push(at_across, whole, 4, twin)
    yield
    from_beside.wait_recv()
    far_high = push(at_beside, high, 5, across)
    push(at_beside, whole, 6, twin)
    yield
    far_low.wait_recv()
    push(far, low, 7, twin)
    far_high.wait_recv()
    push(far, high, 8, twin)
    yield
    for slot in (2, 4, 6, 7, 8):
        sent[slot].wait_recv()
    for copy in sent:
        copy.wait_send()


def collect_steps(part, seg, total, pair, near, joined, send, recv):
    _, shard, inner, core = place()
    across, beside, twin = partners()
    low, high = pl.ds(0, SPLIT), pl.ds(SPLIT, seg - SPLIT)

    def blocks(s):
        row = lax.rem(s + 2, 4)
        indices = (2 * row + 1 - inner, 2 * s + 1 - inner, 2 * row + inner, 2 * s + inner)
        return [aligned(index * seg, seg) for index in indices]

    theirs, ours = blocks(shard + 1 - 2 * core), blocks(shard)
    cols = pl.ds(0, D)
    copies = {}

    def push(slot, src, dst, device):
        copies[slot] = remote(src, dst, send.at[slot], recv.at[slot], device)
        copies[slot].start()

    for k in range(4):
        push(k, part.at[theirs[k], cols], pair.at[k], twin)
    yield

    def add_pair(k):
        copies[k].wait_recv()
        pair[k] = (part[ours[k], cols].astype(F32) + pair[k].astype(F32)).astype(BF16)

    add_pair(0)
    push(4, pair.at[0, low], joined.at[low], across)
    push(5, pair.at[0, high], joined.at[high], beside)
    add_pair(1)
    push(6, pair.at[1, low], near.at[0, low], across)
    add_pair(2)
    push(7, pair.at[2, high], near.at[1, high], beside)
    copies[3].wait_recv()
    total[...] = part[ours[3], cols].astype(F32) + pair[3].astype(F32)
    yield
    copies[4].wait_recv()
    pair[2, low] = (pair[2, low].astype(F32) + joined[low].astype(F32)).astype(BF16)
    push(8, pair.at[2, low], near.at[1, low], beside)
    copies[5].wait_recv()
    pair[1, high] = (pair[1, high].astype(F32) + joined[high].astype(F32)).astype(BF16)
    push(9, pair.at[1, high], near.at[0, high], across)
    yield
    copies[6].wait_recv()
    copies[8].wait_recv()
    total[low] = total[low] + near[0, low].astype(F32) + near[1, low].astype(F32)
    copies[7].wait_recv()
    copies[9].wait_recv()
    total[high] = total[high] + near[0, high].astype(F32) + near[1, high].astype(F32)
    for slot in range(10):
        copies[slot].wait_send()


def drain(steps):
    for _ in steps:
        pass


def norm_scale(values):
    return lax.rsqrt(jnp.mean(values * values, axis=-1, keepdims=True) + NORM_EPSILON)


def by_rows(rows, body, carry=0):
    def step(n, carry):
        return body(aligned(n * ROWS, ROWS), carry)

    return lax.fori_loop(0, rows // ROWS, step, carry)


def norm_back(values, gain, upstream):
    scale = norm_scale(values)
    scaled = gain * upstream
    inner = jnp.mean(scaled * values, axis=-1, keepdims=True)
    return (
        scale * scaled - values * scale * scale * scale * inner,
        jnp.sum(upstream * values * scale, axis=0, keepdims=True),
    )


REFS = (
    "tok", "cot", "gains", "taps", "own", "oth",
    "block_out", "input_grad", "gain_sums", "mine", "theirs", "n1_held", "slot0", "slot1", "slot2", "slot3",
    "w0", "w1", "w2", "w3", "seq_a", "seq_b", "du", "act", "c_all", "gated", "mixed", "resid", "dresid", "total",
    "pair", "near", "joined", "g1", "g2", "g3", "stage", "sum", "outgoing", "gain_in", "gain_line",
    "held", "local", "send_x", "recv_x", "send_z", "recv_z", "send_s", "recv_s", "send_c", "recv_c", "credit",
    "halo_send", "halo_recv", "send_g", "recv_g", "fetched", "stored", "send_o", "recv_o",
    "send_a", "recv_a", "send_l", "recv_l",
)


def block_kernel(layers, rows, *all_refs):
    r = dict(zip(REFS, all_refs, strict=True))
    tok, cot, gains, taps = r["tok"], r["cot"], r["gains"], r["taps"]
    seq_a, seq_b, du, act = r["seq_a"], r["seq_b"], r["du"], r["act"]
    c_all, gated, mixed, total = r["c_all"], r["gated"], r["mixed"], r["total"]
    weights = (r["w0"], r["w1"], r["w2"], r["w3"])
    seg = tok.shape[0]
    _, shard, inner, _ = place()
    outer, at = line()
    me = 2 * shard + inner
    my_rows = aligned(me * seg, seg)
    chunks = list(zip(range(1, 1 + len(UNIT_CHUNKS)), UNIT_STARTS, UNIT_CHUNKS))
    last = len(chunks)
    gather = Gather(
        layers, rows, r["own"], r["oth"], weights,
        r["send_x"], r["recv_x"], r["send_z"], r["recv_z"], r["local"],
    )
    reduce = Reduce(
        layers, rows, (r["w2"], r["g1"], r["g2"], r["g3"]), (r["slot0"], r["slot1"], r["slot2"], r["slot3"]),
        r["stage"], r["sum"], r["outgoing"], r["mine"], r["theirs"],
        (r["send_g"], r["recv_g"], r["fetched"], r["stored"], r["send_o"], r["recv_o"]),
    )

    def spread(buf, n):
        return spread_steps(buf, seg, r["send_s"].at[n], r["recv_s"].at[n])

    def collect(part, n):
        return collect_steps(
            part, seg, total, r["pair"], r["near"], r["joined"], r["send_c"].at[n], r["recv_c"].at[n]
        )

    def block(t):
        return aligned(t * seg, seg)

    lanes = lax.broadcasted_iota(jnp.int32, (seg, WIDE), 1) < HALF_Q

    greet(layers)
    gather.exchange(0)
    gather.send_own(0)

    def mine(part):
        return pl.ds(pl.multiple_of(me * seg + part.start, 16), part.size)

    def first_norm(part, _):
        values = tok[part].astype(F32)
        seq_a[mine(part)] = (values * norm_scale(values) * gains[0:1, :]).astype(BF16)
        return 0

    by_rows(seg, first_norm)
    one = spread(seq_a, 0)
    next(one)
    seq_b[my_rows] = cot[...]
    gather.send_other(0)
    gather.exchange(1)
    gather.upto(0, 1)
    gather.send_own(1)
    next(one)
    next(one)
    gather.upto(0, 2)
    gather.send_other(1)
    next(one)
    drain(one)
    held = pltpu.make_async_copy(seq_a, r["n1_held"], r["held"])
    held.start()
    up = spread(seq_b, 1)
    next(up)
    gather.upto(0)

    def project(s, _):
        for i in (0, 1):
            parts = dot(seq_a[block(2 * s + i)], weights[0][...])
            b = jnp.where(lanes, parts[:, :WIDE], 0.0)
            c = pltpu.roll(parts[:, 128 : 128 + 384], 384 - 64, 1)[:, :WIDE]
            x = parts[:, 384 : 384 + WIDE]
            c_all[s, pl.ds(i * seg, seg)] = jnp.where(lanes, c, 0.0)
            gated[s, pl.ds(8 + i * seg, seg)] = (b * x).astype(BF16).astype(F32)
        return 0

    lax.fori_loop(0, GROUPS, project, 0)
    ahead = remote(
        gated.at[:, pl.ds(2 * seg, 8)], gated.at[:, pl.ds(0, 8)], r["halo_send"].at[0], r["halo_recv"].at[0], at(1)
    )

    @pl.when(outer < layers - 1)
    def _():
        ahead.start()

    @pl.when(outer == 0)
    def _():
        gated[:, pl.ds(0, 8)] = jnp.zeros((GROUPS, 8, WIDE), F32)

    gather.exchange(2)
    next(up)
    next(up)
    gather.send_own(2)
    held.wait()

    @pl.when(outer > 0)
    def _():
        ahead.wait_recv()

    def convolved(s, i):
        return (
            taps[0:1, :] * gated[s, pl.ds(6 + i * seg, seg)]
            + taps[1:2, :] * gated[s, pl.ds(7 + i * seg, seg)]
            + taps[2:3, :] * gated[s, pl.ds(8 + i * seg, seg)]
        )

    def convolve(s, _):
        for i in (0, 1):
            t = block(2 * s + i)
            mixed[t] = pltpu.roll(c_all[s, pl.ds(i * seg, seg)] * convolved(s, i), 64, 1).astype(BF16)
            seq_a[t] = dot_rows(mixed[t], weights[0][:, pl.ds(512, WIDE)]).astype(BF16)
        return 0

    lax.fori_loop(0, GROUPS, convolve, 0)

    branch = collect(seq_a, 0)
    next(branch)
    gather.send_other(2)
    drain(up)
    next(branch)
    next(branch)
    gather.exchange(3)
    drain(branch)
    allow(r["credit"].at[0])

    def second_norm(part, _):
        values = tok[part].astype(F32) + total[part]
        r["resid"][part] = values
        seq_a[mine(part)] = (values * norm_scale(values) * gains[1:2, :]).astype(BF16)
        return 0

    by_rows(seg, second_norm)
    pl.semaphore_wait(r["credit"].at[0], 3)
    two = spread(seq_a, 2)
    next(two)
    gather.upto(1, 2)
    gather.send_own(3)
    next(two)
    next(two)
    gather.send_other(3)
    next(two)
    drain(two)

    def hidden(k, start, units):
        ref = weights[k]

        def step(t, _):
            here = block(t)
            gate = dot(seq_a[here], ref[:, pl.ds(0, units)])
            upval = dot(seq_a[here], ref[:, pl.ds(units, units)])
            dact = dot(seq_b[here], ref[:, pl.ds(2 * units, units)])
            sigma = jax.nn.sigmoid(gate)
            silu = gate * sigma
            act[here, pl.ds(start, units)] = (silu * upval).astype(BF16)
            dgate = dact * upval * sigma * (1.0 + gate * (1.0 - sigma))
            du[here, pl.ds(2 * start, units)] = dgate.astype(BF16)
            du[here, pl.ds(2 * start + units, units)] = (dact * silu).astype(BF16)
            return 0

        lax.fori_loop(0, 2 * GROUPS, step, 0)

    def slices(body):
        def step(n, _):
            body(jnp.where(outer < layers // 2, D // SLICE - 1 - n, n))
            return 0

        lax.fori_loop(0, D // SLICE, step, 0)

    def gate_up_grads(k, start, units, part):
        held_rows = aligned(part * SLICE, SLICE)
        left = seq_a[:, aligned(part * SLICE, SLICE, 128)]
        for m in (0, 1):
            reduce.grads[k][held_rows, pl.ds(m * units, units)] = dot_columns(
                left, du[:, pl.ds(2 * start + m * units, units)]
            ).astype(BF16)

    def down_grads(k, start, units, part):
        held_rows = aligned(part * SLICE, SLICE)
        left = seq_b[:, aligned(part * SLICE, SLICE, 128)]
        reduce.grads[k][held_rows, pl.ds(2 * units, units)] = dot_columns(
            left, act[:, pl.ds(start, units)]
        ).astype(BF16)

    for k, start, units in chunks[:-1]:
        gather.upto(k)
        hidden(k, start, units)
        gather.upto(k + 1, 2)

        def grads(part):
            gate_up_grads(k, start, units, part)
            down_grads(k, start, units, part)
            reduce.direct(k, part)

        slices(grads)
    gather.upto(last)
    hidden(*chunks[-1])
    slices(functools.partial(down_grads, *chunks[-1]))

    def second(t, _):
        here = block(t)
        seq_b[here] = sum(
            dot_rows(du[here, pl.ds(2 * start, 2 * units)], weights[k][:, pl.ds(0, 2 * units)])
            for k, start, units in chunks
        ).astype(BF16)
        return 0

    lax.fori_loop(0, 2 * GROUPS, second, 0)
    down = collect(seq_b, 1)
    next(down)
    reduce.join(1)

    def grads(part):
        gate_up_grads(*chunks[-1], part)
        reduce.direct(last, part)

    next(down)
    slices(grads)
    next(down)

    def forward(t, _):
        here = block(t)
        du[here, pl.ds(0, D)] = sum(
            dot_rows(act[here, pl.ds(start, units)], weights[k][:, pl.ds(2 * units, units)])
            for k, start, units in chunks
        ).astype(BF16)
        return 0

    drain(down)
    reload = pltpu.make_async_copy(r["n1_held"], seq_b, r["held"])
    reload.start()
    allow(r["credit"].at[1])

    def second_back(part, gain):
        dpart, dgain = norm_back(r["resid"][part], gains[1:2, :], total[part])
        dresid = cot[part].astype(F32) + dpart
        r["dresid"][part] = dresid
        seq_a[mine(part)] = dresid.astype(BF16)
        return gain + dgain

    gain_two = by_rows(seg, second_back, jnp.zeros((1, D), F32))
    pl.semaphore_wait(r["credit"].at[1], 3)
    three = spread(seq_a, 3)
    next(three)
    reduce.join(2)
    next(three)
    next(three)
    lax.fori_loop(0, 2 * GROUPS, forward, 0)
    next(three)
    drain(three)
    gather.finish()

    kept = pl.ds(D, WIDE)

    def mix_back(s, _):
        for i in (0, 1):
            t = block(2 * s + i)
            dmixed = pltpu.roll(dot(seq_a[t], weights[0][:, pl.ds(512, WIDE)]), WIDE - 64, 1)
            dmixed = jnp.where(lanes, dmixed, 0.0)
            du[t, kept] = (dmixed * convolved(s, i)).astype(BF16)
            c_all[s, pl.ds(i * seg, seg)] = dmixed * c_all[s, pl.ds(i * seg, seg)]
        return 0

    lax.fori_loop(0, GROUPS, mix_back, 0)
    after = remote(
        c_all.at[:, pl.ds(0, 8)], c_all.at[:, pl.ds(2 * seg, 8)], r["halo_send"].at[1], r["halo_recv"].at[1], at(-1)
    )

    @pl.when(outer > 0)
    def _():
        after.start()

    @pl.when(outer == layers - 1)
    def _():
        c_all[:, pl.ds(2 * seg, 8)] = jnp.zeros((GROUPS, 8, WIDE), F32)

    feed = collect(du, 2)
    next(feed)
    reload.wait()

    @pl.when(outer < layers - 1)
    def _():
        after.wait_recv()

    def conv_back(s, sums):
        for i in (0, 1):
            t = block(2 * s + i)
            dconv = c_all[s, pl.ds(i * seg, seg)]
            dgated = (
                taps[2:3, :] * dconv
                + taps[1:2, :] * c_all[s, pl.ds(1 + i * seg, seg)]
                + taps[0:1, :] * c_all[s, pl.ds(2 + i * seg, seg)]
            )
            parts = dot(seq_b[t], weights[0][:, pl.ds(0, 640)])
            db = dgated * parts[:, 384:640]
            dx = dgated * parts[:, :WIDE]
            dc = jnp.concatenate([du[t, kept].astype(F32), jnp.zeros((seg, 128), F32)], axis=1)
            dc = pltpu.roll(dc, 64, 1)
            act[t, pl.ds(0, 128)] = db[:, :128].astype(BF16)
            act[t, pl.ds(128, 128)] = (db[:, 128:] + dc[:, :128]).astype(BF16)
            act[t, pl.ds(256, 128)] = dc[:, 128:256].astype(BF16)
            act[t, pl.ds(384, WIDE)] = dx.astype(BF16)
            act[t, pl.ds(640, 128)] = jnp.zeros((seg, 128), BF16)
            sums = sums + jnp.concatenate(
                [
                    jnp.sum(dconv * gated[s, pl.ds(6 + k + i * seg, seg)], axis=0, keepdims=True)
                    for k in range(3)
                ]
                + [jnp.zeros((5, WIDE), F32)],
                axis=0,
            )
        return sums

    tap_sums = lax.fori_loop(0, GROUPS, conv_back, jnp.zeros((8, WIDE), F32))

    def conv_grads(part):
        held_rows, cols = aligned(part * SLICE, SLICE), aligned(part * SLICE, SLICE, 128)
        ref = reduce.grads[0]
        ref[held_rows, pl.ds(0, 512)] = dot_columns(seq_b[:, cols], act[:, pl.ds(0, 512)]).astype(BF16)
        ref[held_rows, pl.ds(512, WIDE)] = (
            dot_columns(seq_b[:, cols], act[:, pl.ds(512, WIDE)]) + dot_columns(seq_a[:, cols], mixed[...])
        ).astype(BF16)
        reduce.direct(0, part)

    slices(conv_grads)
    reduce.join(last)
    next(feed)

    def first(t, _):
        here = block(t)
        seq_a[here] = dot_rows(act[here, pl.ds(0, 640)], weights[0][:, pl.ds(0, 640)]).astype(BF16)
        return 0

    lax.fori_loop(0, 2 * GROUPS, first, 0)
    next(feed)
    reduce.join(0)
    drain(feed)
    allow(r["credit"].at[2])
    r["block_out"][...] = (r["resid"][...] + total[...]).astype(BF16)
    reduce.final(1)
    pl.semaphore_wait(r["credit"].at[2], 3)
    inputs = collect(seq_a, 3)
    next(inputs)
    next(inputs)
    next(inputs)
    reduce.final(2)
    drain(inputs)

    def first_back(part, gain):
        dpart, dgain = norm_back(tok[part].astype(F32), gains[0:1, :], total[part])
        r["input_grad"][part] = (r["dresid"][part] + dpart).astype(BF16)
        return gain + dgain

    gain_one = by_rows(seg, first_back, jnp.zeros((1, D), F32))

    sums = r["gain_sums"]
    sums[...] = jnp.zeros(sums.shape, F32)
    sums[0:1, pl.ds(0, D)] = gain_one
    sums[1:2, pl.ds(0, D)] = gain_two
    sums[2:5, aligned(me * WIDE, WIDE, 128)] = tap_sums[0:3]
    for n, device in enumerate(partners()):
        copy = remote(sums, r["gain_in"].at[n], r["send_a"].at[n], r["recv_a"].at[n], device)
        copy.start()
        if n == 1:
            reduce.final(3)
        copy.wait()
        sums[...] = sums[...] + r["gain_in"][n]

    def line_copy(sign, steps):
        slot = (0 if sign > 0 else 1, steps - 1)
        return remote(
            sums, r["gain_line"].at[slot], r["send_l"].at[slot], r["recv_l"].at[slot], at(sign * steps)
        )

    for steps in range(1, layers):
        for sign in (1, -1):

            @pl.when(in_line(outer + sign * steps, layers))
            def _():
                line_copy(sign, steps).start()

    reduce.final(0)
    for steps in range(1, layers):
        for sign in (1, -1):

            @pl.when(in_line(outer + sign * steps, layers))
            def _():
                line_copy(sign, steps).wait_send()

            @pl.when(in_line(outer - sign * steps, layers))
            def _():
                line_copy(sign, steps).wait_recv()

    own_sums = sums[...]
    for origin in range(layers):
        for steps in range(1, layers):
            for sign in (1, -1):

                @pl.when((outer - sign * steps == origin))
                def _():
                    came = r["gain_line"][0 if sign > 0 else 1, steps - 1]
                    sums[...] = came if origin == 0 else sums[...] + came

        if origin > 0:

            @pl.when(outer == origin)
            def _():
                sums[...] = sums[...] + own_sums

    reduce.finish()
    for k in range(len(WIDTHS)):
        reduce.wait_sent(k)

    @pl.when(outer < layers - 1)
    def _():
        ahead.wait_send()

    @pl.when(outer > 0)
    def _():
        after.wait_send()


def block_step(tok, cot, gains, taps, own, oth, layers):
    rows, seg = own.shape[0], tok.shape[0]
    count = len(WIDTHS)
    tokens = 2 * GROUPS * seg
    vmem, anywhere = pl.BlockSpec(memory_space=pltpu.VMEM), pl.BlockSpec(memory_space=pl.ANY)
    shape, scratch = jax.ShapeDtypeStruct, pltpu.VMEM
    dma, regular = pltpu.SemaphoreType.DMA, pltpu.SemaphoreType.REGULAR
    hops = layers - 1
    wide, biggest = sum(WIDTHS), max(WIDTHS)
    out_shape = [
        shape((seg, D), BF16),
        shape((seg, D), BF16),
        shape((8, 2 * GROUPS * WIDE), F32),
        shape((rows, wide), F32),
        shape((rows, wide), BF16),
        shape((tokens, D), BF16),
    ] + [shape((2, hops, 2 * rows, width), BF16) for width in WIDTHS]
    scratch_shapes = (
        [scratch((D, width), BF16) for width in WIDTHS]
        + [
            scratch((tokens, D), BF16),
            scratch((tokens, D), BF16),
            scratch((tokens, 2 * PAD_F), BF16),
            scratch((tokens, PAD_F), BF16),
            scratch((GROUPS, 8 + 2 * seg, WIDE), F32),
            scratch((GROUPS, 8 + 2 * seg, WIDE), F32),
            scratch((tokens, WIDE), BF16),
            scratch((seg, D), F32),
            scratch((seg, D), F32),
            scratch((seg, D), F32),
            scratch((4, seg, D), BF16),
            scratch((2, seg, D), BF16),
            scratch((seg, D), BF16),
        ]
        + [scratch((D, width), BF16) for width in WIDTHS[1:]]
        + [
            scratch((2 * rows, biggest), BF16),
            scratch((2 * rows, biggest), F32),
            scratch((rows, wide), BF16),
            scratch((3, 8, 2 * GROUPS * WIDE), F32),
            scratch((2, hops, 8, 2 * GROUPS * WIDE), F32),
            dma,
            dma((count,)),
            dma((count,)),
            dma((count,)),
            dma((count, 2, hops, 2)),
            dma((count, 2, hops, 2)),
            dma((4, 9)),
            dma((4, 9)),
            dma((4, 10)),
            dma((4, 10)),
            regular((3,)),
            dma((2,)),
            dma((2,)),
            dma((count, 2, hops)),
            dma((count, 2, hops)),
            dma,
            dma((count,)),
            dma((count,)),
            dma((count,)),
            dma((3,)),
            dma((3,)),
            dma((2, hops)),
            dma((2, hops)),
        ]
    )
    return pl.pallas_call(
        functools.partial(block_kernel, layers, rows),
        out_shape=out_shape,
        in_specs=[vmem] * 4 + [anywhere] * 2,
        out_specs=[vmem] * 3 + [anywhere] * (3 + count),
        scratch_shapes=scratch_shapes,
        compiler_params=pltpu.CompilerParams(
            collective_id=0, has_side_effects=True, vmem_limit_bytes=VMEM_BYTES
        ),
        name="block_step",
    )(tok, cot, gains, taps, own, oth)[:5]


def unit_pieces(half):
    pieces = []
    for start, units in zip(UNIT_STARTS, UNIT_CHUNKS):
        real = min(units, HALF_F - start)
        for m in range(3):
            first = 4 * QUARTER + m * UNITS + half * HALF_F + start
            pieces.append((m, first, real, units - real))
    return pieces


def halves(local, inner):
    def half(h):
        parts = [local[:, m * QUARTER + h * HALF_Q : m * QUARTER + (h + 1) * HALF_Q] for m in range(4)]
        for _, first, real, padding in unit_pieces(h):
            parts.append(jnp.pad(local[:, first : first + real], ((0, 0), (0, padding))))
        return jnp.concatenate(parts, axis=1)

    low, high = half(0), half(1)
    is_low = inner == 0
    return jnp.where(is_low, low, high), jnp.where(is_low, high, low)


def joined_columns(mine, theirs, inner):
    is_low = inner == 0
    theirs = theirs.astype(F32)

    def pieces(values):
        convs = [values[:, m * HALF_Q : (m + 1) * HALF_Q] for m in range(4)]
        units = []
        for m in range(3):
            parts = []
            for k, (start, width) in enumerate(zip(UNIT_STARTS, UNIT_CHUNKS), 1):
                first = STARTS[k] + m * width
                parts.append(values[:, first : first + min(width, HALF_F - start)])
            units.append(jnp.concatenate(parts, axis=1))
        return convs + units

    parts = []
    for a, b in zip(pieces(mine), pieces(theirs)):
        parts += [jnp.where(is_low, a, b), jnp.where(is_low, b, a)]
    return jnp.concatenate(parts, axis=1)


def adam_update(param, grad, first, second, rate, decay):
    first_new = MOMENT_DECAY * first + (1.0 - MOMENT_DECAY) * grad
    second_new = SQUARE_DECAY * second + (1.0 - SQUARE_DECAY) * grad * grad
    first_hat = first_new / (1.0 - MOMENT_DECAY**STEP)
    second_hat = second_new / (1.0 - SQUARE_DECAY**STEP)
    param_new = param - rate * (first_hat / (jnp.sqrt(second_hat) + ADAM_EPSILON) + decay * param)
    return (first_new, second_new, param_new)


def on_device(
    tokens, gains_taps, weights, cotangent, weight_first, weight_second, gains_first, gains_second
):
    seq, shard = lax.axis_index("seq"), lax.axis_index("shard")
    inner = seq % 2
    layers = lax.axis_size("seq") // 2
    own, oth = halves(weights.astype(BF16), inner)
    taps = lax.dynamic_slice(gains_taps, (2, shard * QUARTER + inner * HALF_Q), (3, HALF_Q))
    taps = jnp.pad(taps, ((0, 0), (0, WIDE - HALF_Q)))
    block_out, input_grad, gain_sums, mine, theirs = block_step(
        tokens[0], cotangent[0], gains_taps, taps, own, oth, layers
    )
    weight_grad = joined_columns(mine, theirs, inner)
    dtaps = gain_sums[2:5].reshape(3, 2 * GROUPS, WIDE)[:, :, :HALF_Q].reshape(3, D)
    gains_grad = jnp.concatenate([gain_sums[0:2, :D], dtaps], axis=0)
    weight_first_new, weight_second_new, weight_new = adam_update(
        weights, weight_grad, weight_first, weight_second, WEIGHT_RATE, WEIGHT_DECAY
    )
    gains_first_new, gains_second_new, gains_new = adam_update(
        gains_taps, gains_grad, gains_first, gains_second, GAIN_RATE, 0.0
    )
    return (
        block_out[None],
        input_grad[None],
        weight_grad,
        weight_first_new,
        weight_second_new,
        weight_new,
        gains_grad,
        gains_first_new,
        gains_second_new,
        gains_new,
    )


def solution(mesh):
    tokens, rows, whole = P("shard", "seq", None), P("seq", "shard"), P()
    return jax.shard_map(
        on_device,
        mesh=mesh,
        in_specs=(tokens, whole, rows, tokens, rows, rows, whole, whole),
        out_specs=(tokens, tokens, rows, rows, rows, rows, whole, whole, whole, whole),
        check_vma=False,
    )
```

```python
import functools

import jax
import jax.numpy as jnp
from jax import lax
from jax.experimental import pallas as pl
from jax.experimental.pallas import tpu as pltpu
from jax.sharding import PartitionSpec as P

D = 1536
FF = 6912
STEP = 10
GROUPS = 4
QUARTER = D // GROUPS
UNITS = FF // GROUPS
HALF_Q = QUARTER // 2
HALF_F = UNITS // 2
LANES = 128
PAD_F = -(-HALF_F // LANES) * LANES
WIDE = 256
CONV_COLS = 4 * HALF_Q
UNIT_CHUNKS = (384, 256, PAD_F - 640)
UNIT_STARTS = (0, 384, 640)
WIDTHS = (CONV_COLS,) + tuple(3 * units for units in UNIT_CHUNKS)
STARTS = tuple(sum(WIDTHS[:k]) for k in range(len(WIDTHS)))
SPLIT = 128
REACH = (1, 2, 2, 3)
SLICE = 384
TILE = 32
ROWS = 48

MOMENT_DECAY = 0.9
SQUARE_DECAY = 0.95
ADAM_EPSILON = 1e-08
NORM_EPSILON = 1e-05
WEIGHT_RATE = 0.02
GAIN_RATE = 0.2
WEIGHT_DECAY = 0.1

BF16 = jnp.bfloat16
F32 = jnp.float32
MESH = pl.DeviceIdType.MESH
VMEM_BYTES = 63 * 1024 * 1024


def place():
    seq, shard = lax.axis_index("seq"), lax.axis_index("shard")
    inner, core = lax.rem(seq, 2), lax.rem(shard, 2)
    return seq, shard, inner, core


def partners():
    seq, shard, inner, core = place()
    across = {"seq": seq + 1 - 2 * inner, "shard": shard}
    beside = {"seq": seq, "shard": lax.rem(shard + 2, 4)}
    twin = {"seq": seq, "shard": shard + 1 - 2 * core}
    return across, beside, twin


def remote(src, dst, send, recv, device):
    return pltpu.make_async_remote_copy(
        src_ref=src, dst_ref=dst, send_sem=send, recv_sem=recv, device_id=device, device_id_type=MESH
    )


def line():
    seq, shard, _, _ = place()
    return seq // 2, lambda steps: {"seq": seq + 2 * steps, "shard": shard}


def greet(layers):
    outer, at = line()
    barrier = pltpu.get_barrier_semaphore()
    for device in partners():
        pl.semaphore_signal(barrier, inc=1, device_id=device, device_id_type=MESH)
    for steps in range(1, layers):
        for sign in (1, -1):

            @pl.when(in_line(outer + sign * steps, layers))
            def _():
                pl.semaphore_signal(barrier, inc=1, device_id=at(sign * steps), device_id_type=MESH)

    pl.semaphore_wait(barrier, 3 + layers - 1)


def in_line(index, layers):
    return (index >= 0) & (index < layers)


def allow(credit):
    for device in partners():
        pl.semaphore_signal(credit, inc=1, device_id=device, device_id_type=MESH)


def dot(left, right):
    return jnp.dot(left, right, preferred_element_type=F32)


def dot_rows(left, right):
    return lax.dot_general(left, right, (((1,), (1,)), ((), ())), preferred_element_type=F32)


def dot_columns(left, right):
    return lax.dot_general(left, right, (((0,), (0,)), ((), ())), preferred_element_type=F32)


def aligned(start, size, multiple=16):
    return pl.ds(pl.multiple_of(start, multiple), size)


class Gather:
    def __init__(self, layers, rows, own, oth, outs, send_x, recv_x, send_z, recv_z, local):
        self.layers, self.rows, self.own, self.oth, self.outs = layers, rows, own, oth, outs
        self.send_x, self.recv_x, self.send_z, self.recv_z, self.local = send_x, recv_x, send_z, recv_z, local
        self.seq, _, self.inner, _ = place()
        self.outer, self.at = line()
        self.across = partners()[0]

    def seq_rows(self, index):
        return aligned(index * self.rows, self.rows)

    def layer_rows(self, direction, distance):
        origin = self.outer - distance if direction == 0 else self.outer + distance
        return aligned(origin * 2 * self.rows, 2 * self.rows)

    def copy(self, k, src, dst, direction, distance, hop, piece):
        slot = (k, direction, distance + hop - 1, piece)
        return remote(
            src, dst, self.send_z.at[slot], self.recv_z.at[slot], self.at(hop if direction == 0 else -hop)
        )

    def goes(self, direction, hop):
        return in_line(self.outer + (hop if direction == 0 else -hop), self.layers)

    def has_come(self, direction, distance):
        return in_line(self.outer + (-distance if direction == 0 else distance), self.layers)

    def hops(self, k, distance):
        return range(1, min(REACH[k], self.layers - 1 - distance) + 1)

    def own_copy(self, k, direction, hop):
        src = self.own.at[:, pl.ds(STARTS[k], WIDTHS[k])]
        return self.copy(k, src, self.outs[k].at[self.seq_rows(self.seq)], direction, 0, hop, 0)

    def other_copy(self, k, direction, hop):
        there = self.outs[k].at[self.seq_rows(self.seq + 1 - 2 * self.inner)]
        return self.copy(k, there, there, direction, 0, hop, 1)

    def pass_copy(self, k, direction, distance, hop):
        ref = self.outs[k].at[self.layer_rows(direction, distance)]
        return self.copy(k, ref, ref, direction, distance, hop, 0)

    def x_copy(self, k):
        return remote(
            self.oth.at[:, pl.ds(STARTS[k], WIDTHS[k])],
            self.outs[k].at[self.seq_rows(self.seq)],
            self.send_x.at[k],
            self.recv_x.at[k],
            self.across,
        )

    def l_copy(self, k):
        return pltpu.make_async_copy(
            self.own.at[:, pl.ds(STARTS[k], WIDTHS[k])], self.outs[k].at[self.seq_rows(self.seq)], self.local.at[k]
        )

    def exchange(self, k):
        self.x_copy(k).start()
        self.l_copy(k).start()

    def send_own(self, k):
        for hop in self.hops(k, 0):
            for direction in (0, 1):

                @pl.when(self.goes(direction, hop))
                def _():
                    self.own_copy(k, direction, hop).start()

    def send_other(self, k):
        self.x_copy(k).wait_recv()
        for hop in self.hops(k, 0):
            for direction in (0, 1):

                @pl.when(self.goes(direction, hop))
                def _():
                    self.other_copy(k, direction, hop).start()

    def step(self, k, distance):
        for direction in (0, 1):

            @pl.when(self.has_come(direction, distance))
            def _():
                if distance <= REACH[k]:
                    origin = self.outer - distance if direction == 0 else self.outer + distance
                    for piece in (0, 1):
                        index = 2 * origin + (self.inner if piece == 0 else 1 - self.inner)
                        ref = self.outs[k].at[self.seq_rows(index)]
                        self.copy(k, ref, ref, direction, distance - 1, 1, piece).wait_recv()
                else:
                    ref = self.outs[k].at[self.layer_rows(direction, distance)]
                    self.copy(k, ref, ref, direction, distance - 1, 1, 0).wait_recv()
                if distance % REACH[k] == 0:
                    for hop in self.hops(k, distance):

                        @pl.when(self.goes(direction, hop))
                        def _():
                            self.pass_copy(k, direction, distance, hop).start()

        if distance == self.layers - 1:
            self.l_copy(k).wait()

    def steps(self, k, first, last=None):
        last = self.layers - 1 if last is None else min(last, self.layers - 1)
        for distance in range(first, last + 1):
            self.step(k, distance)

    def finish(self):
        for k in range(len(self.outs)):
            self.x_copy(k).wait_send()
            for distance in range(0, self.layers - 1, REACH[k]):
                for hop in self.hops(k, distance):
                    for direction in (0, 1):

                        @pl.when(self.goes(direction, hop) & self.has_come(direction, distance))
                        def _():
                            if distance == 0:
                                self.own_copy(k, direction, hop).wait_send()
                                self.other_copy(k, direction, hop).wait_send()
                            else:
                                self.pass_copy(k, direction, distance, hop).wait_send()


class Reduce:
    def __init__(self, layers, rows, grads, slots, stage, total, outgoing, mine, theirs, sems):
        self.layers, self.rows, self.grads, self.slots = layers, rows, grads, slots
        self.stage, self.total, self.outgoing, self.mine, self.theirs = stage, total, outgoing, mine, theirs
        self.send_g, self.recv_g, self.fetched, self.stored, self.send_o, self.recv_o = sems
        _, _, self.inner, _ = place()
        self.outer, self.at = line()
        self.across = partners()[0]

    def owner(self, direction, distance):
        return self.outer + distance if direction == 0 else self.outer - distance

    def upstream(self, direction, steps):
        return in_line(self.outer - steps if direction == 0 else self.outer + steps, self.layers)

    def block(self, k, owner):
        return self.grads[k].at[aligned(owner * 2 * self.rows, 2 * self.rows), pl.ds(0, WIDTHS[k])]

    def copy(self, k, src, direction, distance):
        hop = 1 if distance % 2 else 2
        slot = (direction, distance - 1)
        return remote(
            src,
            self.slots[k].at[slot],
            self.send_g.at[(k,) + slot],
            self.recv_g.at[(k,) + slot],
            self.at(hop if direction == 0 else -hop),
        )

    def send(self, k, direction, distance):
        self.copy(k, self.block(k, self.owner(direction, distance)), direction, distance).start()

    def direct(self, k, part):
        for distance in range(self.layers - 1, 0, -1):
            for direction in (0, 1):
                owner = self.owner(direction, distance)
                here = in_line(owner, self.layers) & (owner * 2 * self.rows // SLICE == part)
                if distance % 2 == 0:
                    here = here & jnp.logical_not(self.upstream(direction, 1))

                @pl.when(here)
                def _():
                    self.send(k, direction, distance)

    def fetch(self, k, direction, distance):
        slot = self.slots[k].at[direction, distance - 1]
        self.copy(k, slot, direction, distance).wait_recv()
        held = self.stage.at[:, pl.ds(0, WIDTHS[k])]
        copy = pltpu.make_async_copy(slot, held, self.fetched)
        copy.start()
        copy.wait()

    def tiles(self, body):
        def step(n, _):
            body(aligned(n * TILE, TILE))
            return 0

        lax.fori_loop(0, 2 * self.rows // TILE, step, 0)

    def join(self, k):
        cols = pl.ds(0, WIDTHS[k])
        for distance in range((self.layers - 1) // 2 * 2, 0, -2):
            for direction in (0, 1):
                owner = self.owner(direction, distance)

                @pl.when(in_line(owner, self.layers) & self.upstream(direction, 1))
                def _():
                    def add(tile):
                        base = self.owner(direction, distance) * 2 * self.rows
                        rows = pl.ds(pl.multiple_of(base + tile.start, 16), TILE)
                        ref = self.grads[k]
                        ref[rows, cols] = (
                            ref[rows, cols].astype(F32) + self.stage[tile, cols].astype(F32)
                        ).astype(BF16)

                    self.fetch(k, direction, distance + 1)
                    self.tiles(add)
                    if distance + 2 < self.layers:

                        @pl.when(self.upstream(direction, 2))
                        def _():
                            self.fetch(k, direction, distance + 2)
                            self.tiles(add)

                    self.send(k, direction, distance)

    def final(self, k, before=None):
        cols = pl.ds(0, WIDTHS[k])
        if before is not None:
            self.store(before).wait()

        def begin(tile):
            rows = pl.ds(pl.multiple_of(self.outer * 2 * self.rows + tile.start, 16), TILE)
            self.total[tile, cols] = self.grads[k][rows, cols].astype(F32)

        def add(tile):
            self.total[tile, cols] = self.total[tile, cols] + self.stage[tile, cols].astype(F32)

        self.tiles(begin)
        for distance in range(1, min(2, self.layers - 1) + 1):
            for direction in (0, 1):

                @pl.when(self.upstream(direction, distance))
                def _():
                    self.fetch(k, direction, distance)
                    self.tiles(add)

        there = aligned((1 - self.inner) * self.rows, self.rows)
        self.outgoing[:, pl.ds(STARTS[k], WIDTHS[k])] = self.total[there, cols].astype(BF16)
        self.over(k).start()
        self.store(k).start()

    def over(self, k):
        wide = pl.ds(STARTS[k], WIDTHS[k])
        return remote(
            self.outgoing.at[:, wide], self.theirs.at[:, wide], self.send_o.at[k], self.recv_o.at[k], self.across
        )

    def store(self, k):
        here = aligned(self.inner * self.rows, self.rows)
        return pltpu.make_async_copy(
            self.total.at[here, pl.ds(0, WIDTHS[k])], self.mine.at[:, pl.ds(STARTS[k], WIDTHS[k])], self.stored.at[k]
        )

    def wait_sent(self, k):
        for distance in range(1, self.layers):
            for direction in (0, 1):
                owner = self.owner(direction, distance)

                @pl.when(in_line(owner, self.layers))
                def _():
                    self.copy(k, self.block(k, owner), direction, distance).wait_send()

    def finish(self, before):
        self.store(before).wait()
        for k in range(len(self.grads)):
            self.over(k).wait()


class Spread:
    def __init__(self, buf, seg, split, send, recv):
        self.buf, self.seg, self.split, self.send, self.recv = buf, seg, split, send, recv
        self.both = split < seg

    def index(self, n):
        _, shard, inner, core = place()
        row, flip, other = (n // 2) % 2, n // 4, n % 2
        return 2 * (lax.rem(shard + 2 * row, 4) + other * (1 - 2 * core)) + inner + flip * (1 - 2 * inner)

    def copy(self, slot):
        across, beside, twin = partners()
        low, high, whole = (0, self.split), (self.split, self.seg - self.split), (0, self.seg)
        n, (first, size), device = {
            0: (0, whole, across),
            1: (0, whole, beside),
            2: (0, whole, twin),
            3: (4, low, beside),
            4: (4, whole, twin),
            5: (2, high, across),
            6: (2, whole, twin),
            7: (6, low, twin),
            8: (6, high, twin),
        }[slot]
        ref = self.buf.at[aligned(self.index(n) * self.seg + first, size)]
        return remote(ref, ref, self.send.at[slot], self.recv.at[slot], device)

    def push(self, *slots):
        for slot in slots:
            if self.both or slot not in (5, 8):
                self.copy(slot).start()

    def came(self, *slots):
        for slot in slots:
            if self.both or slot not in (5, 8):
                self.copy(slot).wait_recv()

    def start(self):
        self.push(0, 1, 2)

    def near(self):
        self.came(1)
        self.push(5, 6)
        self.came(0)
        self.push(3, 4)

    def far(self):
        self.came(3)
        self.push(7)
        self.came(5)
        self.push(8)

    def end(self, *came):
        self.came(*came)
        for slot in range(9):
            if self.both or slot not in (5, 8):
                self.copy(slot).wait_send()

    def run(self, body, hooks):
        waits = {
            1: lambda: self.came(2),
            2: self.near,
            3: lambda: self.came(6),
            5: lambda: self.came(4),
            6: self.far,
            7: lambda: self.came(7, 8),
        }

        def step(n, _):
            for m in range(8):
                acts = [a[m] for a in (hooks, waits) if m in a]
                if acts:

                    @pl.when(n == m)
                    def _():
                        for act in acts:
                            act()

            body(self.index(n))
            return 0

        lax.fori_loop(0, 8, step, 0)
        self.end()


def collect_steps(part, seg, total, pair, near, joined, send, recv, produce=None):
    _, shard, inner, core = place()
    across, beside, twin = partners()
    low, high, whole = (0, SPLIT), (SPLIT, seg - SPLIT), (0, seg)
    twin_shard = shard + 1 - 2 * core
    cols = pl.ds(0, D)

    def index(s, k):
        row, flip = 1 - k % 2, 1 - k // 2
        return 2 * lax.rem(s + 2 * row, 4) + inner + flip * (1 - 2 * inner)

    def pair_copy(k):
        src = part.at[aligned(index(twin_shard, k) * seg, seg), cols]
        return remote(src, pair.at[k], send.at[k], recv.at[k], twin)

    def copy(slot):
        src, dst, (first, size), device = {
            4: (pair.at[0], joined, low, across),
            5: (pair.at[0], joined, high, beside),
            6: (pair.at[1], near.at[0], low, across),
            7: (pair.at[2], near.at[1], high, beside),
            8: (pair.at[2], near.at[1], low, beside),
            9: (pair.at[1], near.at[0], high, across),
        }[slot]
        rows = pl.ds(first, size)
        return remote(src.at[rows], dst.at[rows], send.at[slot], recv.at[slot], device)

    def over(span, body):
        def step(n, _):
            body(aligned(span[0] + n * 16, 16))
            return 0

        lax.fori_loop(0, span[1] // 16, step, 0)

    def add_pair(k):
        def add(rows):
            mine = part[aligned(index(shard, k) * seg + rows.start, 16), cols].astype(F32)
            pair[k, rows] = (mine + pair[k, rows].astype(F32)).astype(BF16)

        pair_copy(k).wait_recv()
        over(whole, add)

    def add_own():
        def add(rows):
            mine = part[aligned(index(shard, 3) * seg + rows.start, 16), cols].astype(F32)
            total[rows] = mine + pair[3, rows].astype(F32)

        pair_copy(3).wait_recv()
        over(whole, add)

    def pass_on(slot, k, span, after):
        def add(rows):
            pair[k, rows] = (pair[k, rows].astype(F32) + joined[rows].astype(F32)).astype(BF16)

        copy(slot).wait_recv()
        over(span, add)
        copy(after).start()

    def after_pair(k):
        add_pair(k)
        if k == 0:
            copy(4).start()
            copy(5).start()
        elif k == 1:
            copy(6).start()
        else:
            copy(7).start()
            pass_on(4, 2, low, 8)
            pass_on(5, 1, high, 9)

    def half(base):
        def step(n, _):
            k, own = base + n // 2, n % 2
            produce(index(jnp.where(own == 1, shard, twin_shard), k))

            @pl.when(own == 0)
            def _():
                pair_copy(k).start()

            for m in (base, base + 1):

                @pl.when((own == 1) & (k == m))
                def _():
                    if m < 3:
                        after_pair(m)
                    else:
                        add_own()

            return 0

        lax.fori_loop(0, 4, step, 0)

    if produce is None:
        for k in range(4):
            pair_copy(k).start()
        yield
        after_pair(0)
        after_pair(1)
        yield
        after_pair(2)
        add_own()
    else:
        half(0)
        yield
        half(2)
    yield

    def add_near(span):
        def add(rows):
            total[rows] = total[rows] + near[0, rows].astype(F32) + near[1, rows].astype(F32)

        over(span, add)

    copy(6).wait_recv()
    copy(8).wait_recv()
    add_near(low)
    copy(7).wait_recv()
    copy(9).wait_recv()
    add_near(high)
    for k in range(4):
        pair_copy(k).wait_send()
    for slot in range(4, 10):
        copy(slot).wait_send()


def drain(steps):
    for _ in steps:
        pass


def norm_scale(values):
    return lax.rsqrt(jnp.mean(values * values, axis=-1, keepdims=True) + NORM_EPSILON)


def by_rows(rows, body, carry=0):
    def step(n, carry):
        return body(aligned(n * ROWS, ROWS), carry)

    return lax.fori_loop(0, rows // ROWS, step, carry)


def norm_back(values, gain, upstream):
    scale = norm_scale(values)
    scaled = gain * upstream
    inner = jnp.mean(scaled * values, axis=-1, keepdims=True)
    return (
        scale * scaled - values * scale * scale * scale * inner,
        jnp.sum(upstream * values * scale, axis=0, keepdims=True),
    )


REFS = (
    "tok", "cot", "gains", "taps", "own", "oth",
    "block_out", "input_grad", "gain_sums", "mine", "theirs", "n1_held", "slot0", "slot1", "slot2", "slot3",
    "w0", "w1", "w2", "w3", "seq_a", "seq_b", "du", "act", "c_all", "gated", "mixed", "resid", "dresid", "total",
    "pair", "near", "joined", "g1", "g2", "g3", "stage", "sum", "outgoing", "gain_in", "gain_line",
    "held", "local", "send_x", "recv_x", "send_z", "recv_z", "send_s", "recv_s", "send_c", "recv_c", "credit",
    "halo_send", "halo_recv", "send_g", "recv_g", "fetched", "stored", "send_o", "recv_o",
    "send_a", "recv_a", "send_l", "recv_l",
)


def block_kernel(layers, rows, *all_refs):
    r = dict(zip(REFS, all_refs, strict=True))
    tok, cot, gains, taps = r["tok"], r["cot"], r["gains"], r["taps"]
    seq_a, seq_b, du, act = r["seq_a"], r["seq_b"], r["du"], r["act"]
    c_all, gated, mixed, total = r["c_all"], r["gated"], r["mixed"], r["total"]
    weights = (r["w0"], r["w1"], r["w2"], r["w3"])
    seg = tok.shape[0]
    _, shard, inner, _ = place()
    outer, at = line()
    me = 2 * shard + inner
    my_rows = aligned(me * seg, seg)
    chunks = list(zip(range(1, 1 + len(UNIT_CHUNKS)), UNIT_STARTS, UNIT_CHUNKS))
    last = len(chunks)
    gather = Gather(
        layers, rows, r["own"], r["oth"], weights,
        r["send_x"], r["recv_x"], r["send_z"], r["recv_z"], r["local"],
    )
    reduce = Reduce(
        layers, rows, (r["w2"], r["g1"], r["g2"], r["g3"]), (r["slot0"], r["slot1"], r["slot2"], r["slot3"]),
        r["stage"], r["sum"], r["outgoing"], r["mine"], r["theirs"],
        (r["send_g"], r["recv_g"], r["fetched"], r["stored"], r["send_o"], r["recv_o"]),
    )

    def spread(buf, n, split=SPLIT):
        return Spread(buf, seg, split, r["send_s"].at[n], r["recv_s"].at[n])

    def collect(part, n, produce=None):
        return collect_steps(
            part, seg, total, r["pair"], r["near"], r["joined"], r["send_c"].at[n], r["recv_c"].at[n], produce
        )

    def block(t):
        return aligned(t * seg, seg)

    lanes = lax.broadcasted_iota(jnp.int32, (seg, WIDE), 1) < HALF_Q

    greet(layers)
    gather.exchange(0)
    gather.send_own(0)

    def mine(part):
        return pl.ds(pl.multiple_of(me * seg + part.start, 16), part.size)

    def first_norm(part, _):
        values = tok[part].astype(F32)
        seq_a[mine(part)] = (values * norm_scale(values) * gains[0:1, :]).astype(BF16)
        return 0

    by_rows(seg, first_norm)
    one = spread(seq_a, 0)
    one.start()
    seq_b[my_rows] = cot[...]
    gather.send_other(0)
    gather.steps(0, 1, 1)
    one.near()
    gather.exchange(1)
    gather.steps(0, 2, 2)
    gather.send_own(1)
    one.far()
    one.end(2, 4, 6, 7, 8)
    held = pltpu.make_async_copy(seq_a, r["n1_held"], r["held"])
    held.start()
    up = spread(seq_b, 1, seg)
    up.start()
    gather.steps(0, 3)

    def project(s, _):
        for i in (0, 1):
            parts = dot(seq_a[block(2 * s + i)], weights[0][...])
            b = jnp.where(lanes, parts[:, :WIDE], 0.0)
            c = pltpu.roll(parts[:, 128 : 128 + 384], 384 - 64, 1)[:, :WIDE]
            x = parts[:, 384 : 384 + WIDE]
            c_all[s, pl.ds(i * seg, seg)] = jnp.where(lanes, c, 0.0)
            gated[s, pl.ds(8 + i * seg, seg)] = (b * x).astype(BF16).astype(F32)
        return 0

    lax.fori_loop(0, GROUPS, project, 0)
    ahead = remote(
        gated.at[:, pl.ds(2 * seg, 8)], gated.at[:, pl.ds(0, 8)], r["halo_send"].at[0], r["halo_recv"].at[0], at(1)
    )

    @pl.when(outer < layers - 1)
    def _():
        ahead.start()

    @pl.when(outer == 0)
    def _():
        gated[:, pl.ds(0, 8)] = jnp.zeros((GROUPS, 8, WIDE), F32)

    gather.send_other(1)
    up.near()
    gather.exchange(2)
    gather.send_own(2)
    held.wait()

    @pl.when(outer > 0)
    def _():
        ahead.wait_recv()

    def convolved(s, i):
        return (
            taps[0:1, :] * gated[s, pl.ds(6 + i * seg, seg)]
            + taps[1:2, :] * gated[s, pl.ds(7 + i * seg, seg)]
            + taps[2:3, :] * gated[s, pl.ds(8 + i * seg, seg)]
        )

    def convolve(t):
        for i in (0, 1):

            @pl.when(t % 2 == i)
            def _():
                s = t // 2
                mixed[block(t)] = pltpu.roll(c_all[s, pl.ds(i * seg, seg)] * convolved(s, i), 64, 1).astype(BF16)

        seq_a[block(t)] = dot_rows(mixed[block(t)], weights[0][:, pl.ds(512, WIDE)]).astype(BF16)

    branch = collect(seq_a, 0, convolve)
    next(branch)
    gather.send_other(2)
    next(branch)
    up.far()
    gather.exchange(3)
    gather.steps(1, 1, 2)
    drain(branch)
    allow(r["credit"].at[0])

    def second_norm(part, _):
        values = tok[part].astype(F32) + total[part]
        r["resid"][part] = values
        seq_a[mine(part)] = (values * norm_scale(values) * gains[1:2, :]).astype(BF16)
        return 0

    by_rows(seg, second_norm)
    gather.send_own(3)
    pl.semaphore_wait(r["credit"].at[0], 3)
    two = spread(seq_a, 2)
    two.start()
    up.end(2, 4, 6, 7, 8)

    def hidden(k, start, units, t):
        ref, here = weights[k], block(t)
        gate = dot(seq_a[here], ref[:, pl.ds(0, units)])
        upval = dot(seq_a[here], ref[:, pl.ds(units, units)])
        dact = dot(seq_b[here], ref[:, pl.ds(2 * units, units)])
        sigma = jax.nn.sigmoid(gate)
        silu = gate * sigma
        act[here, pl.ds(start, units)] = (silu * upval).astype(BF16)
        dgate = dact * upval * sigma * (1.0 + gate * (1.0 - sigma))
        du[here, pl.ds(2 * start, units)] = dgate.astype(BF16)
        du[here, pl.ds(2 * start + units, units)] = (dact * silu).astype(BF16)

    def each_block(body):
        def step(t, _):
            body(t)
            return 0

        lax.fori_loop(0, 2 * GROUPS, step, 0)

    def slices(body):
        def step(n, _):
            body(jnp.where(outer < layers // 2, D // SLICE - 1 - n, n))
            return 0

        lax.fori_loop(0, D // SLICE, step, 0)

    def gate_up_grads(k, start, units, part):
        held_rows = aligned(part * SLICE, SLICE)
        left = seq_a[:, aligned(part * SLICE, SLICE, 128)]
        for m in (0, 1):
            reduce.grads[k][held_rows, pl.ds(m * units, units)] = dot_columns(
                left, du[:, pl.ds(2 * start + m * units, units)]
            ).astype(BF16)

    def down_grads(k, start, units, part):
        held_rows = aligned(part * SLICE, SLICE)
        left = seq_b[:, aligned(part * SLICE, SLICE, 128)]
        reduce.grads[k][held_rows, pl.ds(2 * units, units)] = dot_columns(
            left, act[:, pl.ds(start, units)]
        ).astype(BF16)

    two.run(
        functools.partial(hidden, *chunks[0]),
        {0: lambda: gather.steps(1, 3), 4: lambda: gather.send_other(3)},
    )
    gather.steps(2, 1, 2)
    for k, start, units in chunks[:-1]:
        if k > 1:
            each_block(functools.partial(hidden, k, start, units))

        def grads(part):
            gate_up_grads(k, start, units, part)
            down_grads(k, start, units, part)
            reduce.direct(k, part)

        slices(grads)
        gather.steps(k + 1, 3 if k + 1 < last else 1)
    each_block(functools.partial(hidden, *chunks[-1]))
    slices(functools.partial(down_grads, *chunks[-1]))

    def second(t):
        here = block(t)
        seq_b[here] = sum(
            dot_rows(du[here, pl.ds(2 * start, 2 * units)], weights[k][:, pl.ds(0, 2 * units)])
            for k, start, units in chunks
        ).astype(BF16)

    down = collect(seq_b, 1, second)
    next(down)
    next(down)
    reduce.join(1)

    def grads(part):
        gate_up_grads(*chunks[-1], part)
        reduce.direct(last, part)

    slices(grads)

    def forward(t):
        here = block(t)
        du[here, pl.ds(0, D)] = sum(
            dot_rows(act[here, pl.ds(start, units)], weights[k][:, pl.ds(2 * units, units)])
            for k, start, units in chunks
        ).astype(BF16)

    drain(down)
    reload = pltpu.make_async_copy(r["n1_held"], seq_b, r["held"])
    reload.start()
    allow(r["credit"].at[1])

    def second_back(part, gain):
        dpart, dgain = norm_back(r["resid"][part], gains[1:2, :], total[part])
        dresid = cot[part].astype(F32) + dpart
        r["dresid"][part] = dresid
        seq_a[mine(part)] = dresid.astype(BF16)
        return gain + dgain

    gain_two = by_rows(seg, second_back, jnp.zeros((1, D), F32))
    pl.semaphore_wait(r["credit"].at[1], 3)
    three = spread(seq_a, 3)
    three.start()

    kept = pl.ds(D, WIDE)

    def mix_back(t):
        s, here = t // 2, block(t)
        dmixed = pltpu.roll(dot(seq_a[here], weights[0][:, pl.ds(512, WIDE)]), WIDE - 64, 1)
        dmixed = jnp.where(lanes, dmixed, 0.0)
        for i in (0, 1):

            @pl.when(t % 2 == i)
            def _():
                du[here, kept] = (dmixed * convolved(s, i)).astype(BF16)
                c_all[s, pl.ds(i * seg, seg)] = dmixed * c_all[s, pl.ds(i * seg, seg)]

    three.run(mix_back, {1: lambda: each_block(forward), 6: lambda: reduce.join(2)})
    gather.finish()
    after = remote(
        c_all.at[:, pl.ds(0, 8)], c_all.at[:, pl.ds(2 * seg, 8)], r["halo_send"].at[1], r["halo_recv"].at[1], at(-1)
    )

    @pl.when(outer > 0)
    def _():
        after.start()

    @pl.when(outer == layers - 1)
    def _():
        c_all[:, pl.ds(2 * seg, 8)] = jnp.zeros((GROUPS, 8, WIDE), F32)

    feed = collect(du, 2)
    next(feed)
    next(feed)
    reload.wait()

    @pl.when(outer < layers - 1)
    def _():
        after.wait_recv()

    def conv_back(s, sums):
        for i in (0, 1):
            t = block(2 * s + i)
            dconv = c_all[s, pl.ds(i * seg, seg)]
            dgated = (
                taps[2:3, :] * dconv
                + taps[1:2, :] * c_all[s, pl.ds(1 + i * seg, seg)]
                + taps[0:1, :] * c_all[s, pl.ds(2 + i * seg, seg)]
            )
            parts = dot(seq_b[t], weights[0][:, pl.ds(0, 640)])
            db = dgated * parts[:, 384:640]
            dx = dgated * parts[:, :WIDE]
            dc = jnp.concatenate([du[t, kept].astype(F32), jnp.zeros((seg, 128), F32)], axis=1)
            dc = pltpu.roll(dc, 64, 1)
            act[t, pl.ds(0, 128)] = db[:, :128].astype(BF16)
            act[t, pl.ds(128, 128)] = (db[:, 128:] + dc[:, :128]).astype(BF16)
            act[t, pl.ds(256, 128)] = dc[:, 128:256].astype(BF16)
            act[t, pl.ds(384, WIDE)] = dx.astype(BF16)
            act[t, pl.ds(640, 128)] = jnp.zeros((seg, 128), BF16)
            sums = sums + jnp.concatenate(
                [
                    jnp.sum(dconv * gated[s, pl.ds(6 + k + i * seg, seg)], axis=0, keepdims=True)
                    for k in range(3)
                ]
                + [jnp.zeros((5, WIDE), F32)],
                axis=0,
            )
        return sums

    tap_sums = lax.fori_loop(0, GROUPS, conv_back, jnp.zeros((8, WIDE), F32))

    def conv_grads(part):
        held_rows, cols = aligned(part * SLICE, SLICE), aligned(part * SLICE, SLICE, 128)
        ref = reduce.grads[0]
        ref[held_rows, pl.ds(0, 512)] = dot_columns(seq_b[:, cols], act[:, pl.ds(0, 512)]).astype(BF16)
        ref[held_rows, pl.ds(512, WIDE)] = (
            dot_columns(seq_b[:, cols], act[:, pl.ds(512, WIDE)]) + dot_columns(seq_a[:, cols], mixed[...])
        ).astype(BF16)
        reduce.direct(0, part)

    slices(conv_grads)
    next(feed)
    reduce.join(last)
    drain(feed)
    allow(r["credit"].at[2])
    r["block_out"][...] = (r["resid"][...] + total[...]).astype(BF16)
    pl.semaphore_wait(r["credit"].at[2], 3)

    def first(t):
        here = block(t)
        seq_a[here] = dot_rows(act[here, pl.ds(0, 640)], weights[0][:, pl.ds(0, 640)]).astype(BF16)

    inputs = collect(seq_a, 3, first)
    next(inputs)
    next(inputs)
    reduce.join(0)
    reduce.final(1)
    reduce.final(2, 1)
    drain(inputs)

    def first_back(part, gain):
        dpart, dgain = norm_back(tok[part].astype(F32), gains[0:1, :], total[part])
        r["input_grad"][part] = (r["dresid"][part] + dpart).astype(BF16)
        return gain + dgain

    gain_one = by_rows(seg, first_back, jnp.zeros((1, D), F32))

    sums = r["gain_sums"]
    sums[...] = jnp.zeros(sums.shape, F32)
    sums[0:1, pl.ds(0, D)] = gain_one
    sums[1:2, pl.ds(0, D)] = gain_two
    sums[2:5, aligned(me * WIDE, WIDE, 128)] = tap_sums[0:3]
    for n, device in enumerate(partners()):
        copy = remote(sums, r["gain_in"].at[n], r["send_a"].at[n], r["recv_a"].at[n], device)
        copy.start()
        if n == 1:
            reduce.final(3, 2)
        copy.wait()
        sums[...] = sums[...] + r["gain_in"][n]

    def line_copy(sign, steps):
        slot = (0 if sign > 0 else 1, steps - 1)
        return remote(
            sums, r["gain_line"].at[slot], r["send_l"].at[slot], r["recv_l"].at[slot], at(sign * steps)
        )

    for steps in range(1, layers):
        for sign in (1, -1):

            @pl.when(in_line(outer + sign * steps, layers))
            def _():
                line_copy(sign, steps).start()

    reduce.final(0, 3)
    for steps in range(1, layers):
        for sign in (1, -1):

            @pl.when(in_line(outer + sign * steps, layers))
            def _():
                line_copy(sign, steps).wait_send()

            @pl.when(in_line(outer - sign * steps, layers))
            def _():
                line_copy(sign, steps).wait_recv()

    own_sums = sums[...]
    for origin in range(layers):
        for steps in range(1, layers):
            for sign in (1, -1):

                @pl.when((outer - sign * steps == origin))
                def _():
                    came = r["gain_line"][0 if sign > 0 else 1, steps - 1]
                    sums[...] = came if origin == 0 else sums[...] + came

        if origin > 0:

            @pl.when(outer == origin)
            def _():
                sums[...] = sums[...] + own_sums

    reduce.finish(0)
    for k in range(len(WIDTHS)):
        reduce.wait_sent(k)

    @pl.when(outer < layers - 1)
    def _():
        ahead.wait_send()

    @pl.when(outer > 0)
    def _():
        after.wait_send()


def block_step(tok, cot, gains, taps, own, oth, layers):
    rows, seg = own.shape[0], tok.shape[0]
    count = len(WIDTHS)
    tokens = 2 * GROUPS * seg
    vmem, anywhere = pl.BlockSpec(memory_space=pltpu.VMEM), pl.BlockSpec(memory_space=pl.ANY)
    shape, scratch = jax.ShapeDtypeStruct, pltpu.VMEM
    dma, regular = pltpu.SemaphoreType.DMA, pltpu.SemaphoreType.REGULAR
    hops = layers - 1
    wide, biggest = sum(WIDTHS), max(WIDTHS)
    out_shape = [
        shape((seg, D), BF16),
        shape((seg, D), BF16),
        shape((8, 2 * GROUPS * WIDE), F32),
        shape((rows, wide), F32),
        shape((rows, wide), BF16),
        shape((tokens, D), BF16),
    ] + [shape((2, hops, 2 * rows, width), BF16) for width in WIDTHS]
    scratch_shapes = (
        [scratch((D, width), BF16) for width in WIDTHS]
        + [
            scratch((tokens, D), BF16),
            scratch((tokens, D), BF16),
            scratch((tokens, 2 * PAD_F), BF16),
            scratch((tokens, PAD_F), BF16),
            scratch((GROUPS, 8 + 2 * seg, WIDE), F32),
            scratch((GROUPS, 8 + 2 * seg, WIDE), F32),
            scratch((tokens, WIDE), BF16),
            scratch((seg, D), F32),
            scratch((seg, D), F32),
            scratch((seg, D), F32),
            scratch((4, seg, D), BF16),
            scratch((2, seg, D), BF16),
            scratch((seg, D), BF16),
        ]
        + [scratch((D, width), BF16) for width in WIDTHS[1:]]
        + [
            scratch((2 * rows, biggest), BF16),
            scratch((2 * rows, biggest), F32),
            scratch((rows, wide), BF16),
            scratch((3, 8, 2 * GROUPS * WIDE), F32),
            scratch((2, hops, 8, 2 * GROUPS * WIDE), F32),
            dma,
            dma((count,)),
            dma((count,)),
            dma((count,)),
            dma((count, 2, hops, 2)),
            dma((count, 2, hops, 2)),
            dma((4, 9)),
            dma((4, 9)),
            dma((4, 10)),
            dma((4, 10)),
            regular((3,)),
            dma((2,)),
            dma((2,)),
            dma((count, 2, hops)),
            dma((count, 2, hops)),
            dma,
            dma((count,)),
            dma((count,)),
            dma((count,)),
            dma((3,)),
            dma((3,)),
            dma((2, hops)),
            dma((2, hops)),
        ]
    )
    return pl.pallas_call(
        functools.partial(block_kernel, layers, rows),
        out_shape=out_shape,
        in_specs=[vmem] * 4 + [anywhere] * 2,
        out_specs=[vmem] * 3 + [anywhere] * (3 + count),
        scratch_shapes=scratch_shapes,
        compiler_params=pltpu.CompilerParams(
            collective_id=0, has_side_effects=True, vmem_limit_bytes=VMEM_BYTES
        ),
        name="block_step",
    )(tok, cot, gains, taps, own, oth)[:5]


def unit_pieces(half):
    pieces = []
    for start, units in zip(UNIT_STARTS, UNIT_CHUNKS):
        real = min(units, HALF_F - start)
        for m in range(3):
            first = 4 * QUARTER + m * UNITS + half * HALF_F + start
            pieces.append((m, first, real, units - real))
    return pieces


def halves(local, inner):
    def half(h):
        parts = [local[:, m * QUARTER + h * HALF_Q : m * QUARTER + (h + 1) * HALF_Q] for m in range(4)]
        for _, first, real, padding in unit_pieces(h):
            parts.append(jnp.pad(local[:, first : first + real], ((0, 0), (0, padding))))
        return jnp.concatenate(parts, axis=1)

    low, high = half(0), half(1)
    is_low = inner == 0
    return jnp.where(is_low, low, high), jnp.where(is_low, high, low)


def joined_columns(mine, theirs, inner):
    is_low = inner == 0
    theirs = theirs.astype(F32)

    def pieces(values):
        convs = [values[:, m * HALF_Q : (m + 1) * HALF_Q] for m in range(4)]
        units = []
        for m in range(3):
            parts = []
            for k, (start, width) in enumerate(zip(UNIT_STARTS, UNIT_CHUNKS), 1):
                first = STARTS[k] + m * width
                parts.append(values[:, first : first + min(width, HALF_F - start)])
            units.append(jnp.concatenate(parts, axis=1))
        return convs + units

    parts = []
    for a, b in zip(pieces(mine), pieces(theirs)):
        parts += [jnp.where(is_low, a, b), jnp.where(is_low, b, a)]
    return jnp.concatenate(parts, axis=1)


def adam_update(param, grad, first, second, rate, decay):
    first_new = MOMENT_DECAY * first + (1.0 - MOMENT_DECAY) * grad
    second_new = SQUARE_DECAY * second + (1.0 - SQUARE_DECAY) * grad * grad
    first_hat = first_new / (1.0 - MOMENT_DECAY**STEP)
    second_hat = second_new / (1.0 - SQUARE_DECAY**STEP)
    param_new = param - rate * (first_hat / (jnp.sqrt(second_hat) + ADAM_EPSILON) + decay * param)
    return (first_new, second_new, param_new)


def on_device(
    tokens, gains_taps, weights, cotangent, weight_first, weight_second, gains_first, gains_second
):
    seq, shard = lax.axis_index("seq"), lax.axis_index("shard")
    inner = seq % 2
    layers = lax.axis_size("seq") // 2
    own, oth = halves(weights.astype(BF16), inner)
    taps = lax.dynamic_slice(gains_taps, (2, shard * QUARTER + inner * HALF_Q), (3, HALF_Q))
    taps = jnp.pad(taps, ((0, 0), (0, WIDE - HALF_Q)))
    block_out, input_grad, gain_sums, mine, theirs = block_step(
        tokens[0], cotangent[0], gains_taps, taps, own, oth, layers
    )
    weight_grad = joined_columns(mine, theirs, inner)
    dtaps = gain_sums[2:5].reshape(3, 2 * GROUPS, WIDE)[:, :, :HALF_Q].reshape(3, D)
    gains_grad = jnp.concatenate([gain_sums[0:2, :D], dtaps], axis=0)
    weight_first_new, weight_second_new, weight_new = adam_update(
        weights, weight_grad, weight_first, weight_second, WEIGHT_RATE, WEIGHT_DECAY
    )
    gains_first_new, gains_second_new, gains_new = adam_update(
        gains_taps, gains_grad, gains_first, gains_second, GAIN_RATE, 0.0
    )
    return (
        block_out[None],
        input_grad[None],
        weight_grad,
        weight_first_new,
        weight_second_new,
        weight_new,
        gains_grad,
        gains_first_new,
        gains_second_new,
        gains_new,
    )


def solution(mesh):
    tokens, rows, whole = P("shard", "seq", None), P("seq", "shard"), P()
    return jax.shard_map(
        on_device,
        mesh=mesh,
        in_specs=(tokens, whole, rows, tokens, rows, rows, whole, whole),
        out_specs=(tokens, tokens, rows, rows, rows, rows, whole, whole, whole, whole),
        check_vma=False,
    )
```

```python
import functools

import jax
import jax.numpy as jnp
from jax import lax
from jax.experimental import pallas as pl
from jax.experimental.pallas import tpu as pltpu
from jax.sharding import PartitionSpec as P

D = 1536
FF = 6912
STEP = 10
GROUPS = 4
QUARTER = D // GROUPS
UNITS = FF // GROUPS
HALF_Q = QUARTER // 2
HALF_F = UNITS // 2
LANES = 128
PAD_F = -(-HALF_F // LANES) * LANES
WIDE = 256
CONV_COLS = 4 * HALF_Q
UNIT_CHUNKS = (384, 256, PAD_F - 640)
UNIT_STARTS = (0, 384, 640)
WIDTHS = (CONV_COLS,) + tuple(3 * units for units in UNIT_CHUNKS)
STARTS = tuple(sum(WIDTHS[:k]) for k in range(len(WIDTHS)))
SPLIT = 128
REACH = (1, 1, 1, 1)
SLICE = 384
TILE = 32
ROWS = 48

MOMENT_DECAY = 0.9
SQUARE_DECAY = 0.95
ADAM_EPSILON = 1e-08
NORM_EPSILON = 1e-05
WEIGHT_RATE = 0.02
GAIN_RATE = 0.2
WEIGHT_DECAY = 0.1

BF16 = jnp.bfloat16
F32 = jnp.float32
MESH = pl.DeviceIdType.MESH
VMEM_BYTES = 63 * 1024 * 1024


def place():
    seq, shard = lax.axis_index("seq"), lax.axis_index("shard")
    inner, core = lax.rem(seq, 2), lax.rem(shard, 2)
    return seq, shard, inner, core


def partners():
    seq, shard, inner, core = place()
    across = {"seq": seq + 1 - 2 * inner, "shard": shard}
    beside = {"seq": seq, "shard": lax.rem(shard + 2, 4)}
    twin = {"seq": seq, "shard": shard + 1 - 2 * core}
    return across, beside, twin


def remote(src, dst, send, recv, device):
    return pltpu.make_async_remote_copy(
        src_ref=src, dst_ref=dst, send_sem=send, recv_sem=recv, device_id=device, device_id_type=MESH
    )


def line():
    seq, shard, _, _ = place()
    return seq // 2, lambda steps: {"seq": seq + 2 * steps, "shard": shard}


def greet(layers):
    outer, at = line()
    barrier = pltpu.get_barrier_semaphore()
    for device in partners():
        pl.semaphore_signal(barrier, inc=1, device_id=device, device_id_type=MESH)
    for steps in range(1, layers):
        for sign in (1, -1):

            @pl.when(in_line(outer + sign * steps, layers))
            def _():
                pl.semaphore_signal(barrier, inc=1, device_id=at(sign * steps), device_id_type=MESH)

    pl.semaphore_wait(barrier, 3 + layers - 1)


def in_line(index, layers):
    return (index >= 0) & (index < layers)


def allow(credit):
    for device in partners():
        pl.semaphore_signal(credit, inc=1, device_id=device, device_id_type=MESH)


def dot(left, right):
    return jnp.dot(left, right, preferred_element_type=F32)


def dot_rows(left, right):
    return lax.dot_general(left, right, (((1,), (1,)), ((), ())), preferred_element_type=F32)


def dot_columns(left, right):
    return lax.dot_general(left, right, (((0,), (0,)), ((), ())), preferred_element_type=F32)


def aligned(start, size, multiple=16):
    return pl.ds(pl.multiple_of(start, multiple), size)


class Gather:
    def __init__(self, layers, rows, own, oth, outs, send_x, recv_x, send_z, recv_z, local):
        self.layers, self.rows, self.own, self.oth, self.outs = layers, rows, own, oth, outs
        self.send_x, self.recv_x, self.send_z, self.recv_z, self.local = send_x, recv_x, send_z, recv_z, local
        self.seq, _, self.inner, _ = place()
        self.outer, self.at = line()
        self.across = partners()[0]

    def seq_rows(self, index):
        return aligned(index * self.rows, self.rows)

    def layer_rows(self, direction, distance):
        origin = self.outer - distance if direction == 0 else self.outer + distance
        return aligned(origin * 2 * self.rows, 2 * self.rows)

    def copy(self, k, src, dst, direction, distance, hop, piece):
        slot = (k, direction, distance + hop - 1, piece)
        return remote(
            src, dst, self.send_z.at[slot], self.recv_z.at[slot], self.at(hop if direction == 0 else -hop)
        )

    def goes(self, direction, hop):
        return in_line(self.outer + (hop if direction == 0 else -hop), self.layers)

    def has_come(self, direction, distance):
        return in_line(self.outer + (-distance if direction == 0 else distance), self.layers)

    def hops(self, k, distance):
        return range(1, min(REACH[k], self.layers - 1 - distance) + 1)

    def own_copy(self, k, direction, hop):
        src = self.own.at[:, pl.ds(STARTS[k], WIDTHS[k])]
        return self.copy(k, src, self.outs[k].at[self.seq_rows(self.seq)], direction, 0, hop, 0)

    def other_copy(self, k, direction, hop):
        there = self.outs[k].at[self.seq_rows(self.seq + 1 - 2 * self.inner)]
        return self.copy(k, there, there, direction, 0, hop, 1)

    def pass_copy(self, k, direction, distance, hop):
        ref = self.outs[k].at[self.layer_rows(direction, distance)]
        return self.copy(k, ref, ref, direction, distance, hop, 0)

    def x_copy(self, k):
        return remote(
            self.oth.at[:, pl.ds(STARTS[k], WIDTHS[k])],
            self.outs[k].at[self.seq_rows(self.seq)],
            self.send_x.at[k],
            self.recv_x.at[k],
            self.across,
        )

    def l_copy(self, k):
        return pltpu.make_async_copy(
            self.own.at[:, pl.ds(STARTS[k], WIDTHS[k])], self.outs[k].at[self.seq_rows(self.seq)], self.local.at[k]
        )

    def exchange(self, k):
        self.x_copy(k).start()
        self.l_copy(k).start()

    def send_own(self, k):
        for hop in self.hops(k, 0):
            for direction in (0, 1):

                @pl.when(self.goes(direction, hop))
                def _():
                    self.own_copy(k, direction, hop).start()

    def send_other(self, k):
        self.x_copy(k).wait_recv()
        for hop in self.hops(k, 0):
            for direction in (0, 1):

                @pl.when(self.goes(direction, hop))
                def _():
                    self.other_copy(k, direction, hop).start()

    def step(self, k, distance):
        for direction in (0, 1):

            @pl.when(self.has_come(direction, distance))
            def _():
                if distance <= REACH[k]:
                    origin = self.outer - distance if direction == 0 else self.outer + distance
                    for piece in (0, 1):
                        index = 2 * origin + (self.inner if piece == 0 else 1 - self.inner)
                        ref = self.outs[k].at[self.seq_rows(index)]
                        self.copy(k, ref, ref, direction, distance - 1, 1, piece).wait_recv()
                else:
                    ref = self.outs[k].at[self.layer_rows(direction, distance)]
                    self.copy(k, ref, ref, direction, distance - 1, 1, 0).wait_recv()
                if distance % REACH[k] == 0:
                    for hop in self.hops(k, distance):

                        @pl.when(self.goes(direction, hop))
                        def _():
                            self.pass_copy(k, direction, distance, hop).start()

        if distance == self.layers - 1:
            self.l_copy(k).wait()

    def steps(self, k, first, last=None):
        last = self.layers - 1 if last is None else min(last, self.layers - 1)
        for distance in range(first, last + 1):
            self.step(k, distance)

    def finish(self):
        for k in range(len(self.outs)):
            self.x_copy(k).wait_send()
            for distance in range(0, self.layers - 1, REACH[k]):
                for hop in self.hops(k, distance):
                    for direction in (0, 1):

                        @pl.when(self.goes(direction, hop) & self.has_come(direction, distance))
                        def _():
                            if distance == 0:
                                self.own_copy(k, direction, hop).wait_send()
                                self.other_copy(k, direction, hop).wait_send()
                            else:
                                self.pass_copy(k, direction, distance, hop).wait_send()


class Reduce:
    def __init__(self, layers, rows, grads, slots, stage, spare, total, outgoing, mine, theirs, sems):
        self.layers, self.rows, self.grads, self.slots = layers, rows, grads, slots
        self.stage, self.spare, self.total, self.outgoing = stage, spare, total, outgoing
        self.mine, self.theirs = mine, theirs
        self.send_g, self.recv_g, self.fetched, self.fetches, self.stored, self.send_o, self.recv_o = sems
        _, _, self.inner, _ = place()
        self.outer, self.at = line()
        self.across = partners()[0]

    def owner(self, direction, distance):
        return self.outer + distance if direction == 0 else self.outer - distance

    def upstream(self, direction, steps):
        return in_line(self.outer - steps if direction == 0 else self.outer + steps, self.layers)

    def block(self, k, owner):
        return self.grads[k].at[aligned(owner * 2 * self.rows, 2 * self.rows), pl.ds(0, WIDTHS[k])]

    def copy(self, k, src, direction, distance):
        hop = 1 if distance % 2 else 2
        slot = (direction, distance - 1)
        return remote(
            src,
            self.slots[k].at[slot],
            self.send_g.at[(k,) + slot],
            self.recv_g.at[(k,) + slot],
            self.at(hop if direction == 0 else -hop),
        )

    def send(self, k, direction, distance):
        self.copy(k, self.block(k, self.owner(direction, distance)), direction, distance).start()

    def direct(self, k, part=None, ends=None):
        at_end = (self.outer == 0) | (self.outer == self.layers - 1)
        for distance in range(self.layers - 1, 0, -1):
            for direction in (0, 1):
                owner = self.owner(direction, distance)
                here = in_line(owner, self.layers)
                if part is not None:
                    here = here & (owner * 2 * self.rows // SLICE == part)
                if ends is not None:
                    here = here & (at_end if ends else jnp.logical_not(at_end))
                if distance % 2 == 0:
                    here = here & jnp.logical_not(self.upstream(direction, 1))

                @pl.when(here)
                def _():
                    self.send(k, direction, distance)

    def fetch(self, k, direction, distance):
        slot = self.slots[k].at[direction, distance - 1]
        self.copy(k, slot, direction, distance).wait_recv()
        held = self.stage.at[:, pl.ds(0, WIDTHS[k])]
        copy = pltpu.make_async_copy(slot, held, self.fetched)
        copy.start()
        copy.wait()

    def tiles(self, body):
        def step(n, _):
            body(aligned(n * TILE, TILE))
            return 0

        lax.fori_loop(0, 2 * self.rows // TILE, step, 0)

    def join(self, k):
        cols = pl.ds(0, WIDTHS[k])
        for distance in range((self.layers - 1) // 2 * 2, 0, -2):
            for direction in (0, 1):
                owner = self.owner(direction, distance)

                @pl.when(in_line(owner, self.layers) & self.upstream(direction, 1))
                def _():
                    def add(tile):
                        base = self.owner(direction, distance) * 2 * self.rows
                        rows = pl.ds(pl.multiple_of(base + tile.start, 16), TILE)
                        ref = self.grads[k]
                        ref[rows, cols] = (
                            ref[rows, cols].astype(F32) + self.stage[tile, cols].astype(F32)
                        ).astype(BF16)

                    self.fetch(k, direction, distance + 1)
                    self.tiles(add)
                    if distance + 2 < self.layers:

                        @pl.when(self.upstream(direction, 2))
                        def _():
                            self.fetch(k, direction, distance + 2)
                            self.tiles(add)

                    self.send(k, direction, distance)

    def final(self, k, before=None):
        cols = pl.ds(0, WIDTHS[k])
        came = [(distance, direction) for distance in (1, 2) for direction in (0, 1) if distance < self.layers]

        def held(n, tile):
            return pl.ds(pl.multiple_of(n * 2 * self.rows + tile.start, 16), tile.size)

        def fetch(n, distance, direction):
            return pltpu.make_async_copy(
                self.slots[k].at[direction, distance - 1],
                self.spare.at[pl.ds(n * 2 * self.rows, 2 * self.rows), cols],
                self.fetches.at[n],
            )

        for n, (distance, direction) in enumerate(came):

            @pl.when(self.upstream(direction, distance))
            def _():
                self.copy(k, self.slots[k].at[direction, distance - 1], direction, distance).wait_recv()
                fetch(n, distance, direction).start()

        if before is not None:
            self.store(before).wait()

        def begin(tile):
            rows = pl.ds(pl.multiple_of(self.outer * 2 * self.rows + tile.start, 16), TILE)
            self.total[tile, cols] = self.grads[k][rows, cols].astype(F32)

        self.tiles(begin)
        for n, (distance, direction) in enumerate(came):

            @pl.when(self.upstream(direction, distance))
            def _():
                def add(tile):
                    self.total[tile, cols] = self.total[tile, cols] + self.spare[held(n, tile), cols].astype(F32)

                fetch(n, distance, direction).wait()
                self.tiles(add)

        there = aligned((1 - self.inner) * self.rows, self.rows)
        self.outgoing[:, pl.ds(STARTS[k], WIDTHS[k])] = self.total[there, cols].astype(BF16)
        self.over(k).start()
        self.store(k).start()

    def over(self, k):
        wide = pl.ds(STARTS[k], WIDTHS[k])
        return remote(
            self.outgoing.at[:, wide], self.theirs.at[:, wide], self.send_o.at[k], self.recv_o.at[k], self.across
        )

    def store(self, k):
        here = aligned(self.inner * self.rows, self.rows)
        return pltpu.make_async_copy(
            self.total.at[here, pl.ds(0, WIDTHS[k])], self.mine.at[:, pl.ds(STARTS[k], WIDTHS[k])], self.stored.at[k]
        )

    def wait_sent(self, k):
        for distance in range(1, self.layers):
            for direction in (0, 1):
                owner = self.owner(direction, distance)

                @pl.when(in_line(owner, self.layers))
                def _():
                    self.copy(k, self.block(k, owner), direction, distance).wait_send()

    def finish(self, before):
        self.store(before).wait()
        for k in range(len(self.grads)):
            self.over(k).wait()


class Spread:
    def __init__(self, buf, seg, split, send, recv):
        self.buf, self.seg, self.split, self.send, self.recv = buf, seg, split, send, recv
        self.both = split < seg

    def index(self, n):
        _, shard, inner, core = place()
        row, flip, other = (n // 2) % 2, n // 4, n % 2
        return 2 * (lax.rem(shard + 2 * row, 4) + other * (1 - 2 * core)) + inner + flip * (1 - 2 * inner)

    def copy(self, slot):
        across, beside, twin = partners()
        low, high, whole = (0, self.split), (self.split, self.seg - self.split), (0, self.seg)
        n, (first, size), device = {
            0: (0, whole, across),
            1: (0, whole, beside),
            2: (0, whole, twin),
            3: (4, low, beside),
            4: (4, whole, twin),
            5: (2, high, across),
            6: (2, whole, twin),
            7: (6, low, twin),
            8: (6, high, twin),
        }[slot]
        ref = self.buf.at[aligned(self.index(n) * self.seg + first, size)]
        return remote(ref, ref, self.send.at[slot], self.recv.at[slot], device)

    def push(self, *slots):
        for slot in slots:
            if self.both or slot not in (5, 8):
                self.copy(slot).start()

    def came(self, *slots):
        for slot in slots:
            if self.both or slot not in (5, 8):
                self.copy(slot).wait_recv()

    def start(self):
        self.push(0, 1, 2)

    def near(self):
        self.came(1)
        self.push(5, 6)
        self.came(0)
        self.push(3, 4)

    def far(self):
        self.came(3)
        self.push(7)
        self.came(5)
        self.push(8)

    def end(self, *came):
        self.came(*came)
        for slot in range(9):
            if self.both or slot not in (5, 8):
                self.copy(slot).wait_send()

    def run(self, body, hooks):
        waits = {
            1: lambda: self.came(2),
            2: self.near,
            3: lambda: self.came(6),
            5: lambda: self.came(4),
            6: self.far,
            7: lambda: self.came(7, 8),
        }

        def step(n, _):
            for m in range(8):
                acts = [a[m] for a in (hooks, waits) if m in a]
                if acts:

                    @pl.when(n == m)
                    def _():
                        for act in acts:
                            act()

            body(self.index(n))
            return 0

        lax.fori_loop(0, 8, step, 0)
        self.end()


def collect_steps(part, seg, total, pair, near, joined, send, recv, produce=None):
    _, shard, inner, core = place()
    across, beside, twin = partners()
    low, high, whole = (0, SPLIT), (SPLIT, seg - SPLIT), (0, seg)
    twin_shard = shard + 1 - 2 * core
    cols = pl.ds(0, D)

    def index(s, k):
        row, flip = 1 - k % 2, 1 - k // 2
        return 2 * lax.rem(s + 2 * row, 4) + inner + flip * (1 - 2 * inner)

    def pair_copy(k):
        src = part.at[aligned(index(twin_shard, k) * seg, seg), cols]
        return remote(src, pair.at[k], send.at[k], recv.at[k], twin)

    def copy(slot):
        src, dst, (first, size), device = {
            4: (pair.at[0], joined, low, across),
            5: (pair.at[0], joined, high, beside),
            6: (pair.at[1], near.at[0], low, across),
            7: (pair.at[2], near.at[1], high, beside),
            8: (pair.at[2], near.at[1], low, beside),
            9: (pair.at[1], near.at[0], high, across),
        }[slot]
        rows = pl.ds(first, size)
        return remote(src.at[rows], dst.at[rows], send.at[slot], recv.at[slot], device)

    def over(span, body):
        def step(n, _):
            body(aligned(span[0] + n * 16, 16))
            return 0

        lax.fori_loop(0, span[1] // 16, step, 0)

    def add_pair(k):
        def add(rows):
            mine = part[aligned(index(shard, k) * seg + rows.start, 16), cols].astype(F32)
            pair[k, rows] = (mine + pair[k, rows].astype(F32)).astype(BF16)

        pair_copy(k).wait_recv()
        over(whole, add)

    def add_own():
        def add(rows):
            mine = part[aligned(index(shard, 3) * seg + rows.start, 16), cols].astype(F32)
            total[rows] = mine + pair[3, rows].astype(F32)

        pair_copy(3).wait_recv()
        over(whole, add)

    def pass_on(slot, k, span, after):
        def add(rows):
            pair[k, rows] = (pair[k, rows].astype(F32) + joined[rows].astype(F32)).astype(BF16)

        copy(slot).wait_recv()
        over(span, add)
        copy(after).start()

    def after_pair(k):
        add_pair(k)
        if k == 0:
            copy(4).start()
            copy(5).start()
        elif k == 1:
            copy(6).start()
        else:
            copy(7).start()
            pass_on(4, 2, low, 8)
            pass_on(5, 1, high, 9)

    def half(base):
        def step(n, _):
            k, own = base + n // 2, n % 2
            produce(index(jnp.where(own == 1, shard, twin_shard), k))

            @pl.when(own == 0)
            def _():
                pair_copy(k).start()

            for m in (base, base + 1):

                @pl.when((own == 1) & (k == m))
                def _():
                    if m < 3:
                        after_pair(m)
                    else:
                        add_own()

            return 0

        lax.fori_loop(0, 4, step, 0)

    if produce is None:
        for k in range(4):
            pair_copy(k).start()
        yield
        after_pair(0)
        after_pair(1)
        yield
        after_pair(2)
        add_own()
    else:
        half(0)
        yield
        half(2)
    yield

    def add_near(span):
        def add(rows):
            total[rows] = total[rows] + near[0, rows].astype(F32) + near[1, rows].astype(F32)

        over(span, add)

    copy(6).wait_recv()
    copy(8).wait_recv()
    add_near(low)
    copy(7).wait_recv()
    copy(9).wait_recv()
    add_near(high)
    for k in range(4):
        pair_copy(k).wait_send()
    for slot in range(4, 10):
        copy(slot).wait_send()


def drain(steps):
    for _ in steps:
        pass


def norm_scale(values):
    return lax.rsqrt(jnp.mean(values * values, axis=-1, keepdims=True) + NORM_EPSILON)


def by_rows(rows, body, carry=0):
    def step(n, carry):
        return body(aligned(n * ROWS, ROWS), carry)

    return lax.fori_loop(0, rows // ROWS, step, carry)


def norm_back(values, gain, upstream):
    scale = norm_scale(values)
    scaled = gain * upstream
    inner = jnp.mean(scaled * values, axis=-1, keepdims=True)
    return (
        scale * scaled - values * scale * scale * scale * inner,
        jnp.sum(upstream * values * scale, axis=0, keepdims=True),
    )


REFS = (
    "tok", "cot", "gains", "taps", "own", "oth",
    "block_out", "input_grad", "gain_sums", "mine", "theirs", "n1_held", "slot0", "slot1", "slot2", "slot3",
    "w0", "w1", "w2", "w3", "seq_a", "seq_b", "du", "act", "c_all", "gated", "mixed", "resid", "dresid", "total",
    "pair", "near", "joined", "g1", "g2", "g3", "stage", "sum", "outgoing", "gain_in", "gain_line",
    "held", "local", "send_x", "recv_x", "send_z", "recv_z", "send_s", "recv_s", "send_c", "recv_c", "credit",
    "halo_send", "halo_recv", "send_g", "recv_g", "fetched", "fetches", "stored", "send_o", "recv_o",
    "send_a", "recv_a", "send_l", "recv_l",
)


def block_kernel(layers, rows, *all_refs):
    r = dict(zip(REFS, all_refs, strict=True))
    tok, cot, gains, taps = r["tok"], r["cot"], r["gains"], r["taps"]
    seq_a, seq_b, du, act = r["seq_a"], r["seq_b"], r["du"], r["act"]
    c_all, gated, mixed, total = r["c_all"], r["gated"], r["mixed"], r["total"]
    weights = (r["w0"], r["w1"], r["w2"], r["w3"])
    seg = tok.shape[0]
    _, shard, inner, _ = place()
    outer, at = line()
    me = 2 * shard + inner
    my_rows = aligned(me * seg, seg)
    chunks = list(zip(range(1, 1 + len(UNIT_CHUNKS)), UNIT_STARTS, UNIT_CHUNKS))
    gather = Gather(
        layers, rows, r["own"], r["oth"], weights,
        r["send_x"], r["recv_x"], r["send_z"], r["recv_z"], r["local"],
    )
    reduce = Reduce(
        layers, rows, (r["w2"], r["g1"], r["g2"], r["g3"]), (r["slot0"], r["slot1"], r["slot2"], r["slot3"]),
        r["stage"], r["w1"], r["sum"], r["outgoing"], r["mine"], r["theirs"],
        (r["send_g"], r["recv_g"], r["fetched"], r["fetches"], r["stored"], r["send_o"], r["recv_o"]),
    )

    def spread(buf, n, split=SPLIT):
        return Spread(buf, seg, split, r["send_s"].at[n], r["recv_s"].at[n])

    def collect(part, n, produce=None):
        return collect_steps(
            part, seg, total, r["pair"], r["near"], r["joined"], r["send_c"].at[n], r["recv_c"].at[n], produce
        )

    def block(t):
        return aligned(t * seg, seg)

    lanes = lax.broadcasted_iota(jnp.int32, (seg, WIDE), 1) < HALF_Q

    greet(layers)
    gather.exchange(0)
    gather.send_own(0)

    def mine(part):
        return pl.ds(pl.multiple_of(me * seg + part.start, 16), part.size)

    def first_norm(part, _):
        values = tok[part].astype(F32)
        seq_a[mine(part)] = (values * norm_scale(values) * gains[0:1, :]).astype(BF16)
        return 0

    by_rows(seg, first_norm)
    one = spread(seq_a, 0)
    one.start()
    seq_b[my_rows] = cot[...]
    gather.send_other(0)
    gather.steps(0, 1, 1)
    one.near()
    gather.exchange(1)
    gather.steps(0, 2, 2)
    gather.send_own(1)
    one.far()
    one.end(2, 4, 6, 7, 8)
    held = pltpu.make_async_copy(seq_a, r["n1_held"], r["held"])
    held.start()
    up = spread(seq_b, 1, seg)
    up.start()
    gather.steps(0, 3)

    def project(s, _):
        for i in (0, 1):
            parts = dot(seq_a[block(2 * s + i)], weights[0][...])
            b = jnp.where(lanes, parts[:, :WIDE], 0.0)
            c = pltpu.roll(parts[:, 128 : 128 + 384], 384 - 64, 1)[:, :WIDE]
            x = parts[:, 384 : 384 + WIDE]
            c_all[s, pl.ds(i * seg, seg)] = jnp.where(lanes, c, 0.0)
            gated[s, pl.ds(8 + i * seg, seg)] = (b * x).astype(BF16).astype(F32)
        return 0

    lax.fori_loop(0, GROUPS, project, 0)
    ahead = remote(
        gated.at[:, pl.ds(2 * seg, 8)], gated.at[:, pl.ds(0, 8)], r["halo_send"].at[0], r["halo_recv"].at[0], at(1)
    )

    @pl.when(outer < layers - 1)
    def _():
        ahead.start()

    @pl.when(outer == 0)
    def _():
        gated[:, pl.ds(0, 8)] = jnp.zeros((GROUPS, 8, WIDE), F32)

    gather.send_other(1)
    up.near()
    gather.exchange(2)
    gather.send_own(2)
    held.wait()

    @pl.when(outer > 0)
    def _():
        ahead.wait_recv()

    def convolved(s, i):
        return (
            taps[0:1, :] * gated[s, pl.ds(6 + i * seg, seg)]
            + taps[1:2, :] * gated[s, pl.ds(7 + i * seg, seg)]
            + taps[2:3, :] * gated[s, pl.ds(8 + i * seg, seg)]
        )

    def convolve(t):
        for i in (0, 1):

            @pl.when(t % 2 == i)
            def _():
                s = t // 2
                mixed[block(t)] = pltpu.roll(c_all[s, pl.ds(i * seg, seg)] * convolved(s, i), 64, 1).astype(BF16)

        seq_a[block(t)] = dot_rows(mixed[block(t)], weights[0][:, pl.ds(512, WIDE)]).astype(BF16)

    branch = collect(seq_a, 0, convolve)
    next(branch)
    gather.exchange(3)
    gather.steps(1, 1, 1)
    gather.send_other(2)
    next(branch)
    up.far()
    gather.steps(1, 2, 2)
    drain(branch)
    allow(r["credit"].at[0])

    def second_norm(part, _):
        values = tok[part].astype(F32) + total[part]
        r["resid"][part] = values
        seq_a[mine(part)] = (values * norm_scale(values) * gains[1:2, :]).astype(BF16)
        return 0

    by_rows(seg, second_norm)
    gather.send_own(3)
    gather.send_other(3)
    pl.semaphore_wait(r["credit"].at[0], 3)
    two = spread(seq_a, 2)
    two.start()
    up.end(2, 4, 6, 7, 8)

    def hidden(k, start, units, t):
        ref, here = weights[k], block(t)
        gate = dot(seq_a[here], ref[:, pl.ds(0, units)])
        upval = dot(seq_a[here], ref[:, pl.ds(units, units)])
        dact = dot(seq_b[here], ref[:, pl.ds(2 * units, units)])
        sigma = jax.nn.sigmoid(gate)
        silu = gate * sigma
        act[here, pl.ds(start, units)] = (silu * upval).astype(BF16)
        dgate = dact * upval * sigma * (1.0 + gate * (1.0 - sigma))
        du[here, pl.ds(2 * start, units)] = dgate.astype(BF16)
        du[here, pl.ds(2 * start + units, units)] = (dact * silu).astype(BF16)

    def each_block(body):
        def step(t, _):
            body(t)
            return 0

        lax.fori_loop(0, 2 * GROUPS, step, 0)

    def slices(body):
        def step(n, _):
            body(jnp.where(outer < layers // 2, D // SLICE - 1 - n, n))
            return 0

        lax.fori_loop(0, D // SLICE, step, 0)

    def gate_up_grads(k, start, units, part):
        held_rows = aligned(part * SLICE, SLICE)
        left = seq_a[:, aligned(part * SLICE, SLICE, 128)]
        for m in (0, 1):
            reduce.grads[k][held_rows, pl.ds(m * units, units)] = dot_columns(
                left, du[:, pl.ds(2 * start + m * units, units)]
            ).astype(BF16)

    def down_grads(k, start, units, part):
        held_rows = aligned(part * SLICE, SLICE)
        left = seq_b[:, aligned(part * SLICE, SLICE, 128)]
        reduce.grads[k][held_rows, pl.ds(2 * units, units)] = dot_columns(
            left, act[:, pl.ds(start, units)]
        ).astype(BF16)

    two.run(
        functools.partial(hidden, *chunks[0]),
        {0: lambda: gather.steps(1, 3), 3: lambda: gather.steps(2, 1, 1), 7: lambda: gather.steps(2, 2, 2)},
    )
    gather.steps(3, 1, 1)
    def grads(k, start, units, part):
        gate_up_grads(k, start, units, part)
        down_grads(k, start, units, part)
        reduce.direct(k, part, ends=True)

    slices(functools.partial(grads, *chunks[0]))
    gather.steps(2, 3)
    each_block(functools.partial(hidden, *chunks[1]))
    gather.steps(3, 2, 2)
    slices(functools.partial(grads, *chunks[1]))
    gather.steps(3, 3)
    reduce.direct(1, ends=False)
    reduce.direct(2, ends=False)
    each_block(functools.partial(hidden, *chunks[2]))
    slices(functools.partial(down_grads, *chunks[2]))
    gather.finish()

    def second(t):
        here = block(t)
        seq_b[here] = sum(
            dot_rows(du[here, pl.ds(2 * start, 2 * units)], weights[k][:, pl.ds(0, 2 * units)])
            for k, start, units in chunks
        ).astype(BF16)

    down = collect(seq_b, 1, second)
    next(down)
    next(down)
    reduce.join(1)

    slices(functools.partial(gate_up_grads, *chunks[2]))

    def forward(t):
        here = block(t)
        du[here, pl.ds(0, D)] = sum(
            dot_rows(act[here, pl.ds(start, units)], weights[k][:, pl.ds(2 * units, units)])
            for k, start, units in chunks
        ).astype(BF16)

    drain(down)
    reload = pltpu.make_async_copy(r["n1_held"], seq_b, r["held"])
    reload.start()
    allow(r["credit"].at[1])

    def second_back(part, gain):
        dpart, dgain = norm_back(r["resid"][part], gains[1:2, :], total[part])
        dresid = cot[part].astype(F32) + dpart
        r["dresid"][part] = dresid
        seq_a[mine(part)] = dresid.astype(BF16)
        return gain + dgain

    gain_two = by_rows(seg, second_back, jnp.zeros((1, D), F32))
    pl.semaphore_wait(r["credit"].at[1], 3)
    three = spread(seq_a, 3)
    three.start()

    kept = pl.ds(D, WIDE)

    def mix_back(t):
        s, here = t // 2, block(t)
        dmixed = pltpu.roll(dot(seq_a[here], weights[0][:, pl.ds(512, WIDE)]), WIDE - 64, 1)
        dmixed = jnp.where(lanes, dmixed, 0.0)
        for i in (0, 1):

            @pl.when(t % 2 == i)
            def _():
                du[here, kept] = (dmixed * convolved(s, i)).astype(BF16)
                c_all[s, pl.ds(i * seg, seg)] = dmixed * c_all[s, pl.ds(i * seg, seg)]

    three.run(
        mix_back, {1: lambda: each_block(forward), 3: lambda: reduce.final(1), 6: lambda: reduce.join(2)}
    )
    after = remote(
        c_all.at[:, pl.ds(0, 8)], c_all.at[:, pl.ds(2 * seg, 8)], r["halo_send"].at[1], r["halo_recv"].at[1], at(-1)
    )

    @pl.when(outer > 0)
    def _():
        after.start()

    @pl.when(outer == layers - 1)
    def _():
        c_all[:, pl.ds(2 * seg, 8)] = jnp.zeros((GROUPS, 8, WIDE), F32)

    reduce.direct(3)
    feed = collect(du, 2)
    next(feed)
    next(feed)
    reload.wait()

    @pl.when(outer < layers - 1)
    def _():
        after.wait_recv()

    def conv_back(s, sums):
        for i in (0, 1):
            t = block(2 * s + i)
            dconv = c_all[s, pl.ds(i * seg, seg)]
            dgated = (
                taps[2:3, :] * dconv
                + taps[1:2, :] * c_all[s, pl.ds(1 + i * seg, seg)]
                + taps[0:1, :] * c_all[s, pl.ds(2 + i * seg, seg)]
            )
            parts = dot(seq_b[t], weights[0][:, pl.ds(0, 640)])
            db = dgated * parts[:, 384:640]
            dx = dgated * parts[:, :WIDE]
            dc = jnp.concatenate([du[t, kept].astype(F32), jnp.zeros((seg, 128), F32)], axis=1)
            dc = pltpu.roll(dc, 64, 1)
            act[t, pl.ds(0, 128)] = db[:, :128].astype(BF16)
            act[t, pl.ds(128, 128)] = (db[:, 128:] + dc[:, :128]).astype(BF16)
            act[t, pl.ds(256, 128)] = dc[:, 128:256].astype(BF16)
            act[t, pl.ds(384, WIDE)] = dx.astype(BF16)
            act[t, pl.ds(640, 128)] = jnp.zeros((seg, 128), BF16)
            sums = sums + jnp.concatenate(
                [
                    jnp.sum(dconv * gated[s, pl.ds(6 + k + i * seg, seg)], axis=0, keepdims=True)
                    for k in range(3)
                ]
                + [jnp.zeros((5, WIDE), F32)],
                axis=0,
            )
        return sums

    tap_sums = lax.fori_loop(0, GROUPS, conv_back, jnp.zeros((8, WIDE), F32))
    next(feed)

    def conv_grads(part):
        held_rows, cols = aligned(part * SLICE, SLICE), aligned(part * SLICE, SLICE, 128)
        ref = reduce.grads[0]
        ref[held_rows, pl.ds(0, 512)] = dot_columns(seq_b[:, cols], act[:, pl.ds(0, 512)]).astype(BF16)
        ref[held_rows, pl.ds(512, WIDE)] = (
            dot_columns(seq_b[:, cols], act[:, pl.ds(512, WIDE)]) + dot_columns(seq_a[:, cols], mixed[...])
        ).astype(BF16)
        reduce.direct(0, part)

    slices(conv_grads)
    reduce.join(3)
    drain(feed)
    allow(r["credit"].at[2])
    r["block_out"][...] = (r["resid"][...] + total[...]).astype(BF16)
    pl.semaphore_wait(r["credit"].at[2], 3)

    def first(t):
        here = block(t)
        seq_a[here] = dot_rows(act[here, pl.ds(0, 640)], weights[0][:, pl.ds(0, 640)]).astype(BF16)

    inputs = collect(seq_a, 3, first)
    next(inputs)
    reduce.final(2, 1)
    next(inputs)
    reduce.join(0)
    reduce.final(3, 2)
    drain(inputs)

    def first_back(part, gain):
        dpart, dgain = norm_back(tok[part].astype(F32), gains[0:1, :], total[part])
        r["input_grad"][part] = (r["dresid"][part] + dpart).astype(BF16)
        return gain + dgain

    gain_one = by_rows(seg, first_back, jnp.zeros((1, D), F32))

    sums = r["gain_sums"]
    sums[...] = jnp.zeros(sums.shape, F32)
    sums[0:1, pl.ds(0, D)] = gain_one
    sums[1:2, pl.ds(0, D)] = gain_two
    sums[2:5, aligned(me * WIDE, WIDE, 128)] = tap_sums[0:3]
    for n, device in enumerate(partners()):
        copy = remote(sums, r["gain_in"].at[n], r["send_a"].at[n], r["recv_a"].at[n], device)
        copy.start()
        copy.wait()
        sums[...] = sums[...] + r["gain_in"][n]

    def line_copy(sign, steps):
        slot = (0 if sign > 0 else 1, steps - 1)
        return remote(
            sums, r["gain_line"].at[slot], r["send_l"].at[slot], r["recv_l"].at[slot], at(sign * steps)
        )

    for steps in range(1, layers):
        for sign in (1, -1):

            @pl.when(in_line(outer + sign * steps, layers))
            def _():
                line_copy(sign, steps).start()

    reduce.final(0, 3)
    for steps in range(1, layers):
        for sign in (1, -1):

            @pl.when(in_line(outer + sign * steps, layers))
            def _():
                line_copy(sign, steps).wait_send()

            @pl.when(in_line(outer - sign * steps, layers))
            def _():
                line_copy(sign, steps).wait_recv()

    own_sums = sums[...]
    for origin in range(layers):
        for steps in range(1, layers):
            for sign in (1, -1):

                @pl.when((outer - sign * steps == origin))
                def _():
                    came = r["gain_line"][0 if sign > 0 else 1, steps - 1]
                    sums[...] = came if origin == 0 else sums[...] + came

        if origin > 0:

            @pl.when(outer == origin)
            def _():
                sums[...] = sums[...] + own_sums

    reduce.finish(0)
    for k in range(len(WIDTHS)):
        reduce.wait_sent(k)

    @pl.when(outer < layers - 1)
    def _():
        ahead.wait_send()

    @pl.when(outer > 0)
    def _():
        after.wait_send()


def block_step(tok, cot, gains, taps, own, oth, layers):
    rows, seg = own.shape[0], tok.shape[0]
    count = len(WIDTHS)
    tokens = 2 * GROUPS * seg
    vmem, anywhere = pl.BlockSpec(memory_space=pltpu.VMEM), pl.BlockSpec(memory_space=pl.ANY)
    shape, scratch = jax.ShapeDtypeStruct, pltpu.VMEM
    dma, regular = pltpu.SemaphoreType.DMA, pltpu.SemaphoreType.REGULAR
    hops = layers - 1
    wide, biggest = sum(WIDTHS), max(WIDTHS)
    out_shape = [
        shape((seg, D), BF16),
        shape((seg, D), BF16),
        shape((8, 2 * GROUPS * WIDE), F32),
        shape((rows, wide), F32),
        shape((rows, wide), BF16),
        shape((tokens, D), BF16),
    ] + [shape((2, hops, 2 * rows, width), BF16) for width in WIDTHS]
    scratch_shapes = (
        [scratch((D, width), BF16) for width in WIDTHS]
        + [
            scratch((tokens, D), BF16),
            scratch((tokens, D), BF16),
            scratch((tokens, 2 * PAD_F), BF16),
            scratch((tokens, PAD_F), BF16),
            scratch((GROUPS, 8 + 2 * seg, WIDE), F32),
            scratch((GROUPS, 8 + 2 * seg, WIDE), F32),
            scratch((tokens, WIDE), BF16),
            scratch((seg, D), F32),
            scratch((seg, D), F32),
            scratch((seg, D), F32),
            scratch((4, seg, D), BF16),
            scratch((2, seg, D), BF16),
            scratch((seg, D), BF16),
        ]
        + [scratch((D, width), BF16) for width in WIDTHS[1:]]
        + [
            scratch((2 * rows, biggest), BF16),
            scratch((2 * rows, biggest), F32),
            scratch((rows, wide), BF16),
            scratch((3, 8, 2 * GROUPS * WIDE), F32),
            scratch((2, hops, 8, 2 * GROUPS * WIDE), F32),
            dma,
            dma((count,)),
            dma((count,)),
            dma((count,)),
            dma((count, 2, hops, 2)),
            dma((count, 2, hops, 2)),
            dma((4, 9)),
            dma((4, 9)),
            dma((4, 10)),
            dma((4, 10)),
            regular((3,)),
            dma((2,)),
            dma((2,)),
            dma((count, 2, hops)),
            dma((count, 2, hops)),
            dma,
            dma((4,)),
            dma((count,)),
            dma((count,)),
            dma((count,)),
            dma((3,)),
            dma((3,)),
            dma((2, hops)),
            dma((2, hops)),
        ]
    )
    return pl.pallas_call(
        functools.partial(block_kernel, layers, rows),
        out_shape=out_shape,
        in_specs=[vmem] * 4 + [anywhere] * 2,
        out_specs=[vmem] * 3 + [anywhere] * (3 + count),
        scratch_shapes=scratch_shapes,
        compiler_params=pltpu.CompilerParams(
            collective_id=0, has_side_effects=True, vmem_limit_bytes=VMEM_BYTES
        ),
        name="block_step",
    )(tok, cot, gains, taps, own, oth)[:5]


def unit_pieces(half):
    pieces = []
    for start, units in zip(UNIT_STARTS, UNIT_CHUNKS):
        real = min(units, HALF_F - start)
        for m in range(3):
            first = 4 * QUARTER + m * UNITS + half * HALF_F + start
            pieces.append((m, first, real, units - real))
    return pieces


def halves(local, inner):
    def half(h):
        parts = [local[:, m * QUARTER + h * HALF_Q : m * QUARTER + (h + 1) * HALF_Q] for m in range(4)]
        for _, first, real, padding in unit_pieces(h):
            parts.append(jnp.pad(local[:, first : first + real], ((0, 0), (0, padding))))
        return jnp.concatenate(parts, axis=1)

    low, high = half(0), half(1)
    is_low = inner == 0
    return jnp.where(is_low, low, high), jnp.where(is_low, high, low)


def joined_columns(mine, theirs, inner):
    is_low = inner == 0
    theirs = theirs.astype(F32)

    def pieces(values):
        convs = [values[:, m * HALF_Q : (m + 1) * HALF_Q] for m in range(4)]
        units = []
        for m in range(3):
            parts = []
            for k, (start, width) in enumerate(zip(UNIT_STARTS, UNIT_CHUNKS), 1):
                first = STARTS[k] + m * width
                parts.append(values[:, first : first + min(width, HALF_F - start)])
            units.append(jnp.concatenate(parts, axis=1))
        return convs + units

    parts = []
    for a, b in zip(pieces(mine), pieces(theirs)):
        parts += [jnp.where(is_low, a, b), jnp.where(is_low, b, a)]
    return jnp.concatenate(parts, axis=1)


def adam_update(param, grad, first, second, rate, decay):
    first_new = MOMENT_DECAY * first + (1.0 - MOMENT_DECAY) * grad
    second_new = SQUARE_DECAY * second + (1.0 - SQUARE_DECAY) * grad * grad
    first_hat = first_new / (1.0 - MOMENT_DECAY**STEP)
    second_hat = second_new / (1.0 - SQUARE_DECAY**STEP)
    param_new = param - rate * (first_hat / (jnp.sqrt(second_hat) + ADAM_EPSILON) + decay * param)
    return (first_new, second_new, param_new)


def on_device(
    tokens, gains_taps, weights, cotangent, weight_first, weight_second, gains_first, gains_second
):
    seq, shard = lax.axis_index("seq"), lax.axis_index("shard")
    inner = seq % 2
    layers = lax.axis_size("seq") // 2
    own, oth = halves(weights.astype(BF16), inner)
    taps = lax.dynamic_slice(gains_taps, (2, shard * QUARTER + inner * HALF_Q), (3, HALF_Q))
    taps = jnp.pad(taps, ((0, 0), (0, WIDE - HALF_Q)))
    block_out, input_grad, gain_sums, mine, theirs = block_step(
        tokens[0], cotangent[0], gains_taps, taps, own, oth, layers
    )
    weight_grad = joined_columns(mine, theirs, inner)
    dtaps = gain_sums[2:5].reshape(3, 2 * GROUPS, WIDE)[:, :, :HALF_Q].reshape(3, D)
    gains_grad = jnp.concatenate([gain_sums[0:2, :D], dtaps], axis=0)
    weight_first_new, weight_second_new, weight_new = adam_update(
        weights, weight_grad, weight_first, weight_second, WEIGHT_RATE, WEIGHT_DECAY
    )
    gains_first_new, gains_second_new, gains_new = adam_update(
        gains_taps, gains_grad, gains_first, gains_second, GAIN_RATE, 0.0
    )
    return (
        block_out[None],
        input_grad[None],
        weight_grad,
        weight_first_new,
        weight_second_new,
        weight_new,
        gains_grad,
        gains_first_new,
        gains_second_new,
        gains_new,
    )


def solution(mesh):
    tokens, rows, whole = P("shard", "seq", None), P("seq", "shard"), P()
    return jax.shard_map(
        on_device,
        mesh=mesh,
        in_specs=(tokens, whole, rows, tokens, rows, rows, whole, whole),
        out_specs=(tokens, tokens, rows, rows, rows, rows, whole, whole, whole, whole),
        check_vma=False,
    )
```

```python
import functools

import jax
import jax.numpy as jnp
from jax import lax
from jax.experimental import pallas as pl
from jax.experimental.pallas import tpu as pltpu
from jax.sharding import PartitionSpec as P

D = 1536
FF = 6912
STEP = 10
GROUPS = 4
QUARTER = D // GROUPS
UNITS = FF // GROUPS
HALF_Q = QUARTER // 2
HALF_F = UNITS // 2
LANES = 128
PAD_F = -(-HALF_F // LANES) * LANES
WIDE = 256
CONV_COLS = 4 * HALF_Q
UNIT_CHUNKS = (384, 256, PAD_F - 640)
UNIT_STARTS = (0, 384, 640)
WIDTHS = (CONV_COLS,) + tuple(3 * units for units in UNIT_CHUNKS)
STARTS = tuple(sum(WIDTHS[:k]) for k in range(len(WIDTHS)))
SPLIT = 128
REACH = (1, 1, 1, 1)
SLICE = 384
TILE = 32
ROWS = 48
BAND = 16

MOMENT_DECAY = 0.9
SQUARE_DECAY = 0.95
ADAM_EPSILON = 1e-08
NORM_EPSILON = 1e-05
WEIGHT_RATE = 0.02
GAIN_RATE = 0.2
WEIGHT_DECAY = 0.1

BF16 = jnp.bfloat16
F32 = jnp.float32
MESH = pl.DeviceIdType.MESH
VMEM_BYTES = 63 * 1024 * 1024


def place():
    seq, shard = lax.axis_index("seq"), lax.axis_index("shard")
    inner, core = lax.rem(seq, 2), lax.rem(shard, 2)
    return seq, shard, inner, core


def partners():
    seq, shard, inner, core = place()
    across = {"seq": seq + 1 - 2 * inner, "shard": shard}
    beside = {"seq": seq, "shard": lax.rem(shard + 2, 4)}
    twin = {"seq": seq, "shard": shard + 1 - 2 * core}
    return across, beside, twin


def remote(src, dst, send, recv, device):
    return pltpu.make_async_remote_copy(
        src_ref=src, dst_ref=dst, send_sem=send, recv_sem=recv, device_id=device, device_id_type=MESH
    )


def line():
    seq, shard, _, _ = place()
    return seq // 2, lambda steps: {"seq": seq + 2 * steps, "shard": shard}


def greet(layers):
    outer, at = line()
    barrier = pltpu.get_barrier_semaphore()
    for device in partners():
        pl.semaphore_signal(barrier, inc=1, device_id=device, device_id_type=MESH)
    for steps in range(1, layers):
        for sign in (1, -1):

            @pl.when(in_line(outer + sign * steps, layers))
            def _():
                pl.semaphore_signal(barrier, inc=1, device_id=at(sign * steps), device_id_type=MESH)

    pl.semaphore_wait(barrier, 3 + layers - 1)


def in_line(index, layers):
    return (index >= 0) & (index < layers)


def allow(credit):
    for device in partners():
        pl.semaphore_signal(credit, inc=1, device_id=device, device_id_type=MESH)


def dot(left, right):
    return jnp.dot(left, right, preferred_element_type=F32)


def dot_rows(left, right):
    return lax.dot_general(left, right, (((1,), (1,)), ((), ())), preferred_element_type=F32)


def dot_columns(left, right):
    return lax.dot_general(left, right, (((0,), (0,)), ((), ())), preferred_element_type=F32)


def aligned(start, size, multiple=16):
    return pl.ds(pl.multiple_of(start, multiple), size)


class Gather:
    def __init__(self, layers, rows, own, oth, outs, send_x, recv_x, send_z, recv_z, local):
        self.layers, self.rows, self.own, self.oth, self.outs = layers, rows, own, oth, outs
        self.send_x, self.recv_x, self.send_z, self.recv_z, self.local = send_x, recv_x, send_z, recv_z, local
        self.seq, _, self.inner, _ = place()
        self.outer, self.at = line()
        self.across = partners()[0]

    def seq_rows(self, index):
        return aligned(index * self.rows, self.rows)

    def layer_rows(self, direction, distance):
        origin = self.outer - distance if direction == 0 else self.outer + distance
        return aligned(origin * 2 * self.rows, 2 * self.rows)

    def copy(self, k, src, dst, direction, distance, hop, piece):
        slot = (k, direction, distance + hop - 1, piece)
        return remote(
            src, dst, self.send_z.at[slot], self.recv_z.at[slot], self.at(hop if direction == 0 else -hop)
        )

    def goes(self, direction, hop):
        return in_line(self.outer + (hop if direction == 0 else -hop), self.layers)

    def has_come(self, direction, distance):
        return in_line(self.outer + (-distance if direction == 0 else distance), self.layers)

    def hops(self, k, distance):
        return range(1, min(REACH[k], self.layers - 1 - distance) + 1)

    def own_copy(self, k, direction, hop):
        src = self.own.at[:, pl.ds(STARTS[k], WIDTHS[k])]
        return self.copy(k, src, self.outs[k].at[self.seq_rows(self.seq)], direction, 0, hop, 0)

    def other_copy(self, k, direction, hop):
        there = self.outs[k].at[self.seq_rows(self.seq + 1 - 2 * self.inner)]
        return self.copy(k, there, there, direction, 0, hop, 1)

    def pass_copy(self, k, direction, distance, hop):
        ref = self.outs[k].at[self.layer_rows(direction, distance)]
        return self.copy(k, ref, ref, direction, distance, hop, 0)

    def x_copy(self, k):
        return remote(
            self.oth.at[:, pl.ds(STARTS[k], WIDTHS[k])],
            self.outs[k].at[self.seq_rows(self.seq)],
            self.send_x.at[k],
            self.recv_x.at[k],
            self.across,
        )

    def l_copy(self, k):
        return pltpu.make_async_copy(
            self.own.at[:, pl.ds(STARTS[k], WIDTHS[k])], self.outs[k].at[self.seq_rows(self.seq)], self.local.at[k]
        )

    def exchange(self, k):
        self.x_copy(k).start()
        self.l_copy(k).start()

    def send_own(self, k):
        for hop in self.hops(k, 0):
            for direction in (0, 1):

                @pl.when(self.goes(direction, hop))
                def _():
                    self.own_copy(k, direction, hop).start()

    def send_other(self, k):
        self.x_copy(k).wait_recv()
        for hop in self.hops(k, 0):
            for direction in (0, 1):

                @pl.when(self.goes(direction, hop))
                def _():
                    self.other_copy(k, direction, hop).start()

    def step(self, k, distance):
        for direction in (0, 1):

            @pl.when(self.has_come(direction, distance))
            def _():
                if distance <= REACH[k]:
                    origin = self.outer - distance if direction == 0 else self.outer + distance
                    for piece in (0, 1):
                        index = 2 * origin + (self.inner if piece == 0 else 1 - self.inner)
                        ref = self.outs[k].at[self.seq_rows(index)]
                        self.copy(k, ref, ref, direction, distance - 1, 1, piece).wait_recv()
                else:
                    ref = self.outs[k].at[self.layer_rows(direction, distance)]
                    self.copy(k, ref, ref, direction, distance - 1, 1, 0).wait_recv()
                if distance % REACH[k] == 0:
                    for hop in self.hops(k, distance):

                        @pl.when(self.goes(direction, hop))
                        def _():
                            self.pass_copy(k, direction, distance, hop).start()

        if distance == self.layers - 1:
            self.l_copy(k).wait()

    def steps(self, k, first, last=None):
        last = self.layers - 1 if last is None else min(last, self.layers - 1)
        for distance in range(first, last + 1):
            self.step(k, distance)

    def finish(self):
        for k in range(len(self.outs)):
            self.x_copy(k).wait_send()
            for distance in range(0, self.layers - 1, REACH[k]):
                for hop in self.hops(k, distance):
                    for direction in (0, 1):

                        @pl.when(self.goes(direction, hop) & self.has_come(direction, distance))
                        def _():
                            if distance == 0:
                                self.own_copy(k, direction, hop).wait_send()
                                self.other_copy(k, direction, hop).wait_send()
                            else:
                                self.pass_copy(k, direction, distance, hop).wait_send()


class Reduce:
    def __init__(self, layers, rows, grads, slots, stage, spare, total, outgoing, mine, theirs, sems):
        self.layers, self.rows, self.grads, self.slots = layers, rows, grads, slots
        self.stage, self.spare, self.total, self.outgoing = stage, spare, total, outgoing
        self.mine, self.theirs = mine, theirs
        self.send_g, self.recv_g, self.fetched, self.fetches, self.stored, self.send_o, self.recv_o = sems
        _, _, self.inner, _ = place()
        self.outer, self.at = line()
        self.across = partners()[0]

    def owner(self, direction, distance):
        return self.outer + distance if direction == 0 else self.outer - distance

    def upstream(self, direction, steps):
        return in_line(self.outer - steps if direction == 0 else self.outer + steps, self.layers)

    def block(self, k, owner):
        return self.grads[k].at[aligned(owner * 2 * self.rows, 2 * self.rows), pl.ds(0, WIDTHS[k])]

    def copy(self, k, src, direction, distance):
        hop = 1 if distance % 2 else 2
        slot = (direction, distance - 1)
        return remote(
            src,
            self.slots[k].at[slot],
            self.send_g.at[(k,) + slot],
            self.recv_g.at[(k,) + slot],
            self.at(hop if direction == 0 else -hop),
        )

    def send(self, k, direction, distance):
        self.copy(k, self.block(k, self.owner(direction, distance)), direction, distance).start()

    def direct(self, k, part=None, ends=None):
        at_end = (self.outer == 0) | (self.outer == self.layers - 1)
        for distance in range(self.layers - 1, 0, -1):
            for direction in (0, 1):
                owner = self.owner(direction, distance)
                here = in_line(owner, self.layers)
                if part is not None:
                    here = here & (owner * 2 * self.rows // SLICE == part)
                if ends is not None:
                    here = here & (at_end if ends else jnp.logical_not(at_end))
                if distance % 2 == 0:
                    here = here & jnp.logical_not(self.upstream(direction, 1))

                @pl.when(here)
                def _():
                    self.send(k, direction, distance)

    def fetch(self, k, direction, distance):
        slot = self.slots[k].at[direction, distance - 1]
        self.copy(k, slot, direction, distance).wait_recv()
        held = self.stage.at[:, pl.ds(0, WIDTHS[k])]
        copy = pltpu.make_async_copy(slot, held, self.fetched)
        copy.start()
        copy.wait()

    def tiles(self, body):
        def step(n, _):
            body(aligned(n * TILE, TILE))
            return 0

        lax.fori_loop(0, 2 * self.rows // TILE, step, 0)

    def join(self, k):
        cols = pl.ds(0, WIDTHS[k])
        for distance in range((self.layers - 1) // 2 * 2, 0, -2):
            for direction in (0, 1):
                owner = self.owner(direction, distance)

                @pl.when(in_line(owner, self.layers) & self.upstream(direction, 1))
                def _():
                    def add(tile):
                        base = self.owner(direction, distance) * 2 * self.rows
                        rows = pl.ds(pl.multiple_of(base + tile.start, 16), TILE)
                        ref = self.grads[k]
                        ref[rows, cols] = (
                            ref[rows, cols].astype(F32) + self.stage[tile, cols].astype(F32)
                        ).astype(BF16)

                    self.fetch(k, direction, distance + 1)
                    self.tiles(add)
                    if distance + 2 < self.layers:

                        @pl.when(self.upstream(direction, 2))
                        def _():
                            self.fetch(k, direction, distance + 2)
                            self.tiles(add)

                    self.send(k, direction, distance)

    def final(self, k, before=None):
        cols = pl.ds(0, WIDTHS[k])
        came = [(distance, direction) for distance in (1, 2) for direction in (0, 1) if distance < self.layers]

        def held(n, tile):
            return pl.ds(pl.multiple_of(n * 2 * self.rows + tile.start, 16), tile.size)

        def fetch(n, distance, direction):
            return pltpu.make_async_copy(
                self.slots[k].at[direction, distance - 1],
                self.spare.at[pl.ds(n * 2 * self.rows, 2 * self.rows), cols],
                self.fetches.at[n],
            )

        for n, (distance, direction) in enumerate(came):

            @pl.when(self.upstream(direction, distance))
            def _():
                self.copy(k, self.slots[k].at[direction, distance - 1], direction, distance).wait_recv()
                fetch(n, distance, direction).start()

        if before is not None:
            self.store(before).wait()

        def begin(tile):
            rows = pl.ds(pl.multiple_of(self.outer * 2 * self.rows + tile.start, 16), TILE)
            self.total[tile, cols] = self.grads[k][rows, cols].astype(F32)

        self.tiles(begin)
        for n, (distance, direction) in enumerate(came):

            @pl.when(self.upstream(direction, distance))
            def _():
                def add(tile):
                    self.total[tile, cols] = self.total[tile, cols] + self.spare[held(n, tile), cols].astype(F32)

                fetch(n, distance, direction).wait()
                self.tiles(add)

        there = aligned((1 - self.inner) * self.rows, self.rows)
        self.outgoing[:, pl.ds(STARTS[k], WIDTHS[k])] = self.total[there, cols].astype(BF16)
        self.over(k).start()
        self.store(k).start()

    def over(self, k):
        wide = pl.ds(STARTS[k], WIDTHS[k])
        return remote(
            self.outgoing.at[:, wide], self.theirs.at[:, wide], self.send_o.at[k], self.recv_o.at[k], self.across
        )

    def store(self, k):
        here = aligned(self.inner * self.rows, self.rows)
        return pltpu.make_async_copy(
            self.total.at[here, pl.ds(0, WIDTHS[k])], self.mine.at[:, pl.ds(STARTS[k], WIDTHS[k])], self.stored.at[k]
        )

    def wait_sent(self, k):
        for distance in range(1, self.layers):
            for direction in (0, 1):
                owner = self.owner(direction, distance)

                @pl.when(in_line(owner, self.layers))
                def _():
                    self.copy(k, self.block(k, owner), direction, distance).wait_send()

    def finish(self, before):
        self.store(before).wait()
        for k in range(len(self.grads)):
            self.over(k).wait()


class Spread:
    def __init__(self, buf, seg, split, send, recv):
        self.buf, self.seg, self.split, self.send, self.recv = buf, seg, split, send, recv
        self.both = split < seg

    def index(self, n):
        _, shard, inner, core = place()
        row, flip, other = (n // 2) % 2, n // 4, n % 2
        return 2 * (lax.rem(shard + 2 * row, 4) + other * (1 - 2 * core)) + inner + flip * (1 - 2 * inner)

    def copy(self, slot):
        across, beside, twin = partners()
        low, high, whole = (0, self.split), (self.split, self.seg - self.split), (0, self.seg)
        n, (first, size), device = {
            0: (0, whole, across),
            1: (0, whole, beside),
            2: (0, whole, twin),
            3: (4, low, beside),
            4: (4, whole, twin),
            5: (2, high, across),
            6: (2, whole, twin),
            7: (6, low, twin),
            8: (6, high, twin),
        }[slot]
        ref = self.buf.at[aligned(self.index(n) * self.seg + first, size)]
        return remote(ref, ref, self.send.at[slot], self.recv.at[slot], device)

    def push(self, *slots):
        for slot in slots:
            if self.both or slot not in (5, 8):
                self.copy(slot).start()

    def came(self, *slots):
        for slot in slots:
            if self.both or slot not in (5, 8):
                self.copy(slot).wait_recv()

    def start(self):
        self.push(0, 1, 2)

    def near(self):
        self.came(1)
        self.push(5, 6)
        self.came(0)
        self.push(3, 4)

    def far(self):
        self.came(3)
        self.push(7)
        self.came(5)
        self.push(8)

    def end(self, *came):
        self.came(*came)
        for slot in range(9):
            if self.both or slot not in (5, 8):
                self.copy(slot).wait_send()

    def run(self, body, hooks):
        waits = {
            1: lambda: self.came(2),
            2: self.near,
            3: lambda: self.came(6),
            5: lambda: self.came(4),
            6: self.far,
            7: lambda: self.came(7, 8),
        }

        def step(n, _):
            for m in range(8):
                acts = [a[m] for a in (hooks, waits) if m in a]
                if acts:

                    @pl.when(n == m)
                    def _():
                        for act in acts:
                            act()

            body(self.index(n))
            return 0

        lax.fori_loop(0, 8, step, 0)
        self.end()


def collect_steps(part, seg, total, pair, near, joined, send, recv, produce=None):
    _, shard, inner, core = place()
    across, beside, twin = partners()
    low, high, whole = (0, SPLIT), (SPLIT, seg - SPLIT), (0, seg)
    twin_shard = shard + 1 - 2 * core
    cols = pl.ds(0, D)

    def index(s, k):
        row, flip = 1 - k % 2, 1 - k // 2
        return 2 * lax.rem(s + 2 * row, 4) + inner + flip * (1 - 2 * inner)

    def pair_copy(k):
        src = part.at[aligned(index(twin_shard, k) * seg, seg), cols]
        return remote(src, pair.at[k], send.at[k], recv.at[k], twin)

    def copy(slot):
        src, dst, (first, size), device = {
            4: (pair.at[0], joined, low, across),
            5: (pair.at[0], joined, high, beside),
            6: (pair.at[1], near.at[0], low, across),
            7: (pair.at[2], near.at[1], high, beside),
            8: (pair.at[2], near.at[1], low, beside),
            9: (pair.at[1], near.at[0], high, across),
        }[slot]
        rows = pl.ds(first, size)
        return remote(src.at[rows], dst.at[rows], send.at[slot], recv.at[slot], device)

    def over(span, body):
        def step(n, _):
            body(aligned(span[0] + n * 16, 16))
            return 0

        lax.fori_loop(0, span[1] // 16, step, 0)

    def add_pair(k):
        def add(rows):
            mine = part[aligned(index(shard, k) * seg + rows.start, 16), cols].astype(F32)
            pair[k, rows] = (mine + pair[k, rows].astype(F32)).astype(BF16)

        pair_copy(k).wait_recv()
        over(whole, add)

    def add_own():
        def add(rows):
            mine = part[aligned(index(shard, 3) * seg + rows.start, 16), cols].astype(F32)
            total[rows] = mine + pair[3, rows].astype(F32)

        pair_copy(3).wait_recv()
        over(whole, add)

    def pass_on(slot, k, span, after):
        def add(rows):
            pair[k, rows] = (pair[k, rows].astype(F32) + joined[rows].astype(F32)).astype(BF16)

        copy(slot).wait_recv()
        over(span, add)
        copy(after).start()

    def after_pair(k):
        add_pair(k)
        if k == 0:
            copy(4).start()
            copy(5).start()
        elif k == 1:
            copy(6).start()
        else:
            copy(7).start()
            pass_on(4, 2, low, 8)
            pass_on(5, 1, high, 9)

    def half(base):
        def step(n, _):
            k, own = base + n // 2, n % 2
            produce(index(jnp.where(own == 1, shard, twin_shard), k))

            @pl.when(own == 0)
            def _():
                pair_copy(k).start()

            for m in (base, base + 1):

                @pl.when((own == 1) & (k == m))
                def _():
                    if m < 3:
                        after_pair(m)
                    else:
                        add_own()

            return 0

        lax.fori_loop(0, 4, step, 0)

    if produce is None:
        for k in range(4):
            pair_copy(k).start()
        yield
        after_pair(0)
        after_pair(1)
        yield
        after_pair(2)
        add_own()
    else:
        half(0)
        yield
        half(2)
    yield

    def add_near(span):
        def add(rows):
            total[rows] = total[rows] + near[0, rows].astype(F32) + near[1, rows].astype(F32)

        over(span, add)

    copy(6).wait_recv()
    copy(8).wait_recv()
    add_near(low)
    copy(7).wait_recv()
    copy(9).wait_recv()
    add_near(high)
    for k in range(4):
        pair_copy(k).wait_send()
    for slot in range(4, 10):
        copy(slot).wait_send()


def drain(steps):
    for _ in steps:
        pass


def norm_scale(values):
    return lax.rsqrt(jnp.mean(values * values, axis=-1, keepdims=True) + NORM_EPSILON)


def by_rows(rows, body, carry=0):
    def step(n, carry):
        return body(aligned(n * ROWS, ROWS), carry)

    return lax.fori_loop(0, rows // ROWS, step, carry)


def norm_back(values, gain, upstream):
    scale = norm_scale(values)
    scaled = gain * upstream
    inner = jnp.mean(scaled * values, axis=-1, keepdims=True)
    return (
        scale * scaled - values * scale * scale * scale * inner,
        jnp.sum(upstream * values * scale, axis=0, keepdims=True),
    )


REFS = (
    "tok", "cot", "gains", "taps", "own", "oth",
    "block_out", "input_grad", "gain_sums", "mine", "theirs", "n1_held", "slot0", "slot1", "slot2", "slot3",
    "w0", "w1", "w2", "w3", "seq_a", "seq_b", "du", "act", "c_all", "gated", "mixed", "resid", "dresid", "total",
    "pair", "near", "joined", "g1", "g2", "g3", "stage", "sum", "outgoing", "gain_in", "gain_line",
    "held", "local", "send_x", "recv_x", "send_z", "recv_z", "send_s", "recv_s", "send_c", "recv_c", "credit",
    "halo_send", "halo_recv", "send_g", "recv_g", "fetched", "fetches", "stored", "send_o", "recv_o",
    "send_a", "recv_a", "send_l", "recv_l",
)


def block_kernel(layers, rows, *all_refs):
    r = dict(zip(REFS, all_refs, strict=True))
    tok, cot, gains, taps = r["tok"], r["cot"], r["gains"], r["taps"]
    seq_a, seq_b, du, act = r["seq_a"], r["seq_b"], r["du"], r["act"]
    c_all, gated, mixed, total = r["c_all"], r["gated"], r["mixed"], r["total"]
    weights = (r["w0"], r["w1"], r["w2"], r["w3"])
    seg = tok.shape[0]
    _, shard, inner, _ = place()
    outer, at = line()
    me = 2 * shard + inner
    my_rows = aligned(me * seg, seg)
    chunks = list(zip(range(1, 1 + len(UNIT_CHUNKS)), UNIT_STARTS, UNIT_CHUNKS))
    gather = Gather(
        layers, rows, r["own"], r["oth"], weights,
        r["send_x"], r["recv_x"], r["send_z"], r["recv_z"], r["local"],
    )
    reduce = Reduce(
        layers, rows, (r["w2"], r["g1"], r["g2"], r["g3"]), (r["slot0"], r["slot1"], r["slot2"], r["slot3"]),
        r["stage"], r["w1"], r["sum"], r["outgoing"], r["mine"], r["theirs"],
        (r["send_g"], r["recv_g"], r["fetched"], r["fetches"], r["stored"], r["send_o"], r["recv_o"]),
    )

    def spread(buf, n, split=SPLIT):
        return Spread(buf, seg, split, r["send_s"].at[n], r["recv_s"].at[n])

    def collect(part, n, produce=None):
        return collect_steps(
            part, seg, total, r["pair"], r["near"], r["joined"], r["send_c"].at[n], r["recv_c"].at[n], produce
        )

    def block(t):
        return aligned(t * seg, seg)

    lanes = lax.broadcasted_iota(jnp.int32, (seg, WIDE), 1) < HALF_Q

    greet(layers)
    gather.exchange(0)
    gather.send_own(0)

    def mine(part):
        return pl.ds(pl.multiple_of(me * seg + part.start, 16), part.size)

    def first_norm(part, _):
        values = tok[part].astype(F32)
        seq_a[mine(part)] = (values * norm_scale(values) * gains[0:1, :]).astype(BF16)
        return 0

    by_rows(seg, first_norm)
    one = spread(seq_a, 0)
    one.start()
    seq_b[my_rows] = cot[...]
    gather.send_other(0)
    gather.steps(0, 1, 1)
    one.near()
    gather.exchange(1)
    gather.steps(0, 2, 2)
    gather.send_own(1)
    one.far()
    one.end(2, 4, 6, 7, 8)
    held = pltpu.make_async_copy(seq_a, r["n1_held"], r["held"])
    held.start()
    up = spread(seq_b, 1, seg)
    up.start()
    gather.steps(0, 3)

    def project(s, _):
        for i in (0, 1):
            parts = dot(seq_a[block(2 * s + i)], weights[0][...])
            b = jnp.where(lanes, parts[:, :WIDE], 0.0)
            c = pltpu.roll(parts[:, 128 : 128 + 384], 384 - 64, 1)[:, :WIDE]
            x = parts[:, 384 : 384 + WIDE]
            c_all[s, pl.ds(i * seg, seg)] = jnp.where(lanes, c, 0.0)
            gated[s, pl.ds(8 + i * seg, seg)] = (b * x).astype(BF16).astype(F32)
        return 0

    lax.fori_loop(0, GROUPS, project, 0)
    ahead = remote(
        gated.at[:, pl.ds(2 * seg, 8)], gated.at[:, pl.ds(0, 8)], r["halo_send"].at[0], r["halo_recv"].at[0], at(1)
    )

    @pl.when(outer < layers - 1)
    def _():
        ahead.start()

    @pl.when(outer == 0)
    def _():
        gated[:, pl.ds(0, 8)] = jnp.zeros((GROUPS, 8, WIDE), F32)

    gather.send_other(1)
    up.near()
    gather.exchange(2)
    gather.send_own(2)
    held.wait()

    @pl.when(outer > 0)
    def _():
        ahead.wait_recv()

    def convolved(s, i):
        return (
            taps[0:1, :] * gated[s, pl.ds(6 + i * seg, seg)]
            + taps[1:2, :] * gated[s, pl.ds(7 + i * seg, seg)]
            + taps[2:3, :] * gated[s, pl.ds(8 + i * seg, seg)]
        )

    def convolve(t):
        for i in (0, 1):

            @pl.when(t % 2 == i)
            def _():
                s = t // 2
                mixed[block(t)] = pltpu.roll(c_all[s, pl.ds(i * seg, seg)] * convolved(s, i), 64, 1).astype(BF16)

        seq_a[block(t)] = dot_rows(mixed[block(t)], weights[0][:, pl.ds(512, WIDE)]).astype(BF16)

    branch = collect(seq_a, 0, convolve)
    next(branch)
    gather.exchange(3)
    gather.steps(1, 1, 1)
    gather.send_other(2)
    next(branch)
    up.far()
    gather.steps(1, 2, 2)
    drain(branch)
    allow(r["credit"].at[0])

    def second_norm(part, _):
        values = tok[part].astype(F32) + total[part]
        r["resid"][part] = values
        seq_a[mine(part)] = (values * norm_scale(values) * gains[1:2, :]).astype(BF16)
        return 0

    by_rows(seg, second_norm)
    gather.send_own(3)
    gather.send_other(3)
    pl.semaphore_wait(r["credit"].at[0], 3)
    two = spread(seq_a, 2)
    two.start()
    up.end(2, 4, 6, 7, 8)

    def hidden(k, start, units, t):
        ref, here = weights[k], block(t)
        gate = dot(seq_a[here], ref[:, pl.ds(0, units)])
        upval = dot(seq_a[here], ref[:, pl.ds(units, units)])
        dact = dot(seq_b[here], ref[:, pl.ds(2 * units, units)])
        sigma = jax.nn.sigmoid(gate)
        silu = gate * sigma
        act[here, pl.ds(start, units)] = (silu * upval).astype(BF16)
        dgate = dact * upval * sigma * (1.0 + gate * (1.0 - sigma))
        du[here, pl.ds(2 * start, units)] = dgate.astype(BF16)
        du[here, pl.ds(2 * start + units, units)] = (dact * silu).astype(BF16)

    def each_block(body):
        def step(t, _):
            body(t)
            return 0

        lax.fori_loop(0, 2 * GROUPS, step, 0)

    def slices(body):
        def step(n, _):
            body(jnp.where(outer < layers // 2, D // SLICE - 1 - n, n))
            return 0

        lax.fori_loop(0, D // SLICE, step, 0)

    def gate_up_grads(k, start, units, part):
        held_rows = aligned(part * SLICE, SLICE)
        left = seq_a[:, aligned(part * SLICE, SLICE, 128)]
        for m in (0, 1):
            reduce.grads[k][held_rows, pl.ds(m * units, units)] = dot_columns(
                left, du[:, pl.ds(2 * start + m * units, units)]
            ).astype(BF16)

    def down_grads(k, start, units, part):
        held_rows = aligned(part * SLICE, SLICE)
        left = seq_b[:, aligned(part * SLICE, SLICE, 128)]
        reduce.grads[k][held_rows, pl.ds(2 * units, units)] = dot_columns(
            left, act[:, pl.ds(start, units)]
        ).astype(BF16)

    two.run(
        functools.partial(hidden, *chunks[0]),
        {0: lambda: gather.steps(1, 3), 3: lambda: gather.steps(2, 1, 1), 7: lambda: gather.steps(2, 2, 2)},
    )
    gather.steps(3, 1, 1)
    def grads(k, start, units, part):
        gate_up_grads(k, start, units, part)
        down_grads(k, start, units, part)
        reduce.direct(k, part, ends=True)

    slices(functools.partial(grads, *chunks[0]))
    gather.steps(2, 3)
    each_block(functools.partial(hidden, *chunks[1]))
    gather.steps(3, 2, 2)
    slices(functools.partial(grads, *chunks[1]))
    gather.steps(3, 3)
    reduce.direct(1, ends=False)
    reduce.direct(2, ends=False)
    each_block(functools.partial(hidden, *chunks[2]))
    slices(functools.partial(down_grads, *chunks[2]))
    gather.finish()

    def second(t):
        here = block(t)
        seq_b[here] = sum(
            dot_rows(du[here, pl.ds(2 * start, 2 * units)], weights[k][:, pl.ds(0, 2 * units)])
            for k, start, units in chunks
        ).astype(BF16)

    down = collect(seq_b, 1, second)
    next(down)
    next(down)
    reduce.join(1)

    slices(functools.partial(gate_up_grads, *chunks[2]))

    def forward(t):
        here = block(t)
        du[here, pl.ds(0, D)] = sum(
            dot_rows(act[here, pl.ds(start, units)], weights[k][:, pl.ds(2 * units, units)])
            for k, start, units in chunks
        ).astype(BF16)

    drain(down)
    reload = pltpu.make_async_copy(r["n1_held"], seq_b, r["held"])
    reload.start()
    allow(r["credit"].at[1])

    def second_back(part, gain):
        dpart, dgain = norm_back(r["resid"][part], gains[1:2, :], total[part])
        dresid = cot[part].astype(F32) + dpart
        r["dresid"][part] = dresid
        seq_a[mine(part)] = dresid.astype(BF16)
        return gain + dgain

    gain_two = by_rows(seg, second_back, jnp.zeros((1, D), F32))
    pl.semaphore_wait(r["credit"].at[1], 3)
    three = spread(seq_a, 3)
    three.start()

    kept = pl.ds(D, WIDE)

    def mix_back(t):
        s, here = t // 2, block(t)
        dmixed = pltpu.roll(dot(seq_a[here], weights[0][:, pl.ds(512, WIDE)]), WIDE - 64, 1)
        dmixed = jnp.where(lanes, dmixed, 0.0)
        for i in (0, 1):

            @pl.when(t % 2 == i)
            def _():
                du[here, kept] = (dmixed * convolved(s, i)).astype(BF16)
                c_all[s, pl.ds(i * seg, seg)] = dmixed * c_all[s, pl.ds(i * seg, seg)]

    three.run(
        mix_back, {1: lambda: each_block(forward), 3: lambda: reduce.final(1), 6: lambda: reduce.join(2)}
    )
    after = remote(
        c_all.at[:, pl.ds(0, 8)], c_all.at[:, pl.ds(2 * seg, 8)], r["halo_send"].at[1], r["halo_recv"].at[1], at(-1)
    )

    @pl.when(outer > 0)
    def _():
        after.start()

    @pl.when(outer == layers - 1)
    def _():
        c_all[:, pl.ds(2 * seg, 8)] = jnp.zeros((GROUPS, 8, WIDE), F32)

    reduce.direct(3)
    feed = collect(du, 2)
    next(feed)
    next(feed)
    reload.wait()

    @pl.when(outer < layers - 1)
    def _():
        after.wait_recv()

    def conv_back(s, sums):
        for i in (0, 1):
            t = block(2 * s + i)
            dconv = c_all[s, pl.ds(i * seg, seg)]
            dgated = (
                taps[2:3, :] * dconv
                + taps[1:2, :] * c_all[s, pl.ds(1 + i * seg, seg)]
                + taps[0:1, :] * c_all[s, pl.ds(2 + i * seg, seg)]
            )
            parts = dot(seq_b[t], weights[0][:, pl.ds(0, 640)])
            db = dgated * parts[:, 384:640]
            dx = dgated * parts[:, :WIDE]
            dc = jnp.concatenate([du[t, kept].astype(F32), jnp.zeros((seg, 128), F32)], axis=1)
            dc = pltpu.roll(dc, 64, 1)
            act[t, pl.ds(0, 128)] = db[:, :128].astype(BF16)
            act[t, pl.ds(128, 128)] = (db[:, 128:] + dc[:, :128]).astype(BF16)
            act[t, pl.ds(256, 128)] = dc[:, 128:256].astype(BF16)
            act[t, pl.ds(384, WIDE)] = dx.astype(BF16)
            act[t, pl.ds(640, 128)] = jnp.zeros((seg, 128), BF16)
            sums = sums + jnp.concatenate(
                [
                    jnp.sum(dconv * gated[s, pl.ds(6 + k + i * seg, seg)], axis=0, keepdims=True)
                    for k in range(3)
                ]
                + [jnp.zeros((5, WIDE), F32)],
                axis=0,
            )
        return sums

    tap_sums = lax.fori_loop(0, GROUPS, conv_back, jnp.zeros((8, WIDE), F32))
    next(feed)

    def conv_grads(part):
        held_rows, cols = aligned(part * SLICE, SLICE), aligned(part * SLICE, SLICE, 128)
        ref = reduce.grads[0]
        ref[held_rows, pl.ds(0, 512)] = dot_columns(seq_b[:, cols], act[:, pl.ds(0, 512)]).astype(BF16)
        ref[held_rows, pl.ds(512, WIDE)] = (
            dot_columns(seq_b[:, cols], act[:, pl.ds(512, WIDE)]) + dot_columns(seq_a[:, cols], mixed[...])
        ).astype(BF16)
        reduce.direct(0, part)

    slices(conv_grads)
    reduce.join(3)
    drain(feed)
    allow(r["credit"].at[2])
    r["block_out"][...] = (r["resid"][...] + total[...]).astype(BF16)
    pl.semaphore_wait(r["credit"].at[2], 3)

    def first(t):
        here = block(t)
        seq_a[here] = dot_rows(act[here, pl.ds(0, 640)], weights[0][:, pl.ds(0, 640)]).astype(BF16)

    inputs = collect(seq_a, 3, first)
    next(inputs)
    reduce.final(2, 1)
    next(inputs)
    reduce.join(0)
    reduce.final(3, 2)
    drain(inputs)

    def first_back(part, gain):
        dpart, dgain = norm_back(tok[part].astype(F32), gains[0:1, :], total[part])
        r["input_grad"][part] = (r["dresid"][part] + dpart).astype(BF16)
        return gain + dgain

    gain_one = by_rows(seg, first_back, jnp.zeros((1, D), F32))

    sums = r["gain_sums"]
    sums[...] = jnp.zeros(sums.shape, F32)
    sums[0:1, pl.ds(0, D)] = gain_one
    sums[1:2, pl.ds(0, D)] = gain_two
    sums[2:5, aligned(me * WIDE, WIDE, 128)] = tap_sums[0:3]
    for n, device in enumerate(partners()):
        copy = remote(sums, r["gain_in"].at[n], r["send_a"].at[n], r["recv_a"].at[n], device)
        copy.start()
        copy.wait()
        sums[...] = sums[...] + r["gain_in"][n]

    def line_copy(sign, steps):
        slot = (0 if sign > 0 else 1, steps - 1)
        return remote(
            sums, r["gain_line"].at[slot], r["send_l"].at[slot], r["recv_l"].at[slot], at(sign * steps)
        )

    for steps in range(1, layers):
        for sign in (1, -1):

            @pl.when(in_line(outer + sign * steps, layers))
            def _():
                line_copy(sign, steps).start()

    reduce.final(0, 3)
    for steps in range(1, layers):
        for sign in (1, -1):

            @pl.when(in_line(outer + sign * steps, layers))
            def _():
                line_copy(sign, steps).wait_send()

            @pl.when(in_line(outer - sign * steps, layers))
            def _():
                line_copy(sign, steps).wait_recv()

    own_sums = sums[...]
    for origin in range(layers):
        for steps in range(1, layers):
            for sign in (1, -1):

                @pl.when((outer - sign * steps == origin))
                def _():
                    came = r["gain_line"][0 if sign > 0 else 1, steps - 1]
                    sums[...] = came if origin == 0 else sums[...] + came

        if origin > 0:

            @pl.when(outer == origin)
            def _():
                sums[...] = sums[...] + own_sums

    reduce.finish(0)
    for k in range(len(WIDTHS)):
        reduce.wait_sent(k)

    @pl.when(outer < layers - 1)
    def _():
        ahead.wait_send()

    @pl.when(outer > 0)
    def _():
        after.wait_send()


def block_step(tok, cot, gains, taps, own, oth, layers):
    rows, seg = own.shape[0], tok.shape[0]
    count = len(WIDTHS)
    tokens = 2 * GROUPS * seg
    vmem, anywhere = pl.BlockSpec(memory_space=pltpu.VMEM), pl.BlockSpec(memory_space=pl.ANY)
    shape, scratch = jax.ShapeDtypeStruct, pltpu.VMEM
    dma, regular = pltpu.SemaphoreType.DMA, pltpu.SemaphoreType.REGULAR
    hops = layers - 1
    wide, biggest = sum(WIDTHS), max(WIDTHS)
    out_shape = [
        shape((seg, D), BF16),
        shape((seg, D), BF16),
        shape((8, 2 * GROUPS * WIDE), F32),
        shape((rows, wide), F32),
        shape((rows, wide), BF16),
        shape((tokens, D), BF16),
    ] + [shape((2, hops, 2 * rows, width), BF16) for width in WIDTHS]
    scratch_shapes = (
        [scratch((D, width), BF16) for width in WIDTHS]
        + [
            scratch((tokens, D), BF16),
            scratch((tokens, D), BF16),
            scratch((tokens, 2 * PAD_F), BF16),
            scratch((tokens, PAD_F), BF16),
            scratch((GROUPS, 8 + 2 * seg, WIDE), F32),
            scratch((GROUPS, 8 + 2 * seg, WIDE), F32),
            scratch((tokens, WIDE), BF16),
            scratch((seg, D), F32),
            scratch((seg, D), F32),
            scratch((seg, D), F32),
            scratch((4, seg, D), BF16),
            scratch((2, seg, D), BF16),
            scratch((seg, D), BF16),
        ]
        + [scratch((D, width), BF16) for width in WIDTHS[1:]]
        + [
            scratch((2 * rows, biggest), BF16),
            scratch((2 * rows, biggest), F32),
            scratch((rows, wide), BF16),
            scratch((3, 8, 2 * GROUPS * WIDE), F32),
            scratch((2, hops, 8, 2 * GROUPS * WIDE), F32),
            dma,
            dma((count,)),
            dma((count,)),
            dma((count,)),
            dma((count, 2, hops, 2)),
            dma((count, 2, hops, 2)),
            dma((4, 9)),
            dma((4, 9)),
            dma((4, 10)),
            dma((4, 10)),
            regular((3,)),
            dma((2,)),
            dma((2,)),
            dma((count, 2, hops)),
            dma((count, 2, hops)),
            dma,
            dma((4,)),
            dma((count,)),
            dma((count,)),
            dma((count,)),
            dma((3,)),
            dma((3,)),
            dma((2, hops)),
            dma((2, hops)),
        ]
    )
    return pl.pallas_call(
        functools.partial(block_kernel, layers, rows),
        out_shape=out_shape,
        in_specs=[vmem] * 4 + [anywhere] * 2,
        out_specs=[vmem] * 3 + [anywhere] * (3 + count),
        scratch_shapes=scratch_shapes,
        compiler_params=pltpu.CompilerParams(
            collective_id=0, has_side_effects=True, vmem_limit_bytes=VMEM_BYTES
        ),
        name="block_step",
    )(tok, cot, gains, taps, own, oth)[:5]


def column_pieces(half):
    pieces = [(m * QUARTER + half * HALF_Q, m * HALF_Q, HALF_Q, 0) for m in range(4)]
    for k, (start, units) in enumerate(zip(UNIT_STARTS, UNIT_CHUNKS), 1):
        real = min(units, HALF_F - start)
        for m in range(3):
            first = 4 * QUARTER + m * UNITS + half * HALF_F + start
            pieces.append((first, STARTS[k] + m * units, real, units - real))
    return pieces


def halves_kernel(inner_ref, weights_ref, own_ref, oth_ref):
    is_low = inner_ref[0] == 0

    def half(h):
        parts = []
        for first, _, width, padding in column_pieces(h):
            parts.append(weights_ref[:, first : first + width])
            if padding:
                parts.append(jnp.zeros((parts[-1].shape[0], padding), F32))
        return jnp.concatenate(parts, axis=1)

    low, high = half(0), half(1)
    own_ref[...] = jnp.where(is_low, low, high).astype(BF16)
    oth_ref[...] = jnp.where(is_low, high, low).astype(BF16)


def halves(weights, inner):
    rows, cols = weights.shape
    wide = sum(WIDTHS)
    by_row = lambda width: pl.BlockSpec((BAND, width), lambda n: (n, 0))
    return pl.pallas_call(
        halves_kernel,
        grid=(rows // BAND,),
        out_shape=[jax.ShapeDtypeStruct((rows, wide), BF16)] * 2,
        in_specs=[pl.BlockSpec(memory_space=pltpu.SMEM), by_row(cols)],
        out_specs=[by_row(wide)] * 2,
        compiler_params=pltpu.CompilerParams(vmem_limit_bytes=VMEM_BYTES),
        name="halves",
    )(inner, weights)


def adam_update(param, grad, first, second, rate, decay):
    first_new = MOMENT_DECAY * first + (1.0 - MOMENT_DECAY) * grad
    second_new = SQUARE_DECAY * second + (1.0 - SQUARE_DECAY) * grad * grad
    first_hat = first_new / (1.0 - MOMENT_DECAY**STEP)
    second_hat = second_new / (1.0 - SQUARE_DECAY**STEP)
    param_new = param - rate * (first_hat / (jnp.sqrt(second_hat) + ADAM_EPSILON) + decay * param)
    return (first_new, second_new, param_new)


def update_kernel(
    inner_ref, mine_ref, theirs_ref, weights_ref, first_ref, second_ref, sums_ref, gains_ref, gains_first_ref,
    gains_second_ref, grad_out, first_out, second_out, weights_out, gains_grad_out, gains_first_out,
    gains_second_out, gains_out,
):
    is_low = inner_ref[0] == 0
    mine, theirs = mine_ref[...], theirs_ref[...].astype(F32)
    for half in (0, 1):
        chosen = jnp.where(is_low, mine, theirs) if half == 0 else jnp.where(is_low, theirs, mine)
        for first, own, width, _ in column_pieces(half):
            grad_out[:, first : first + width] = chosen[:, own : own + width]
    first_out[...], second_out[...], weights_out[...] = adam_update(
        weights_ref[...], grad_out[...], first_ref[...], second_ref[...], WEIGHT_RATE, WEIGHT_DECAY
    )

    @pl.when(pl.program_id(0) == 0)
    def _():
        gains_grad_out[0:2] = sums_ref[0:2, :D]
        for n in range(2 * GROUPS):
            gains_grad_out[2:5, n * HALF_Q : (n + 1) * HALF_Q] = sums_ref[2:5, n * WIDE : n * WIDE + HALF_Q]
        gains_first_out[...], gains_second_out[...], gains_out[...] = adam_update(
            gains_ref[...], gains_grad_out[...], gains_first_ref[...], gains_second_ref[...], GAIN_RATE, 0.0
        )


def update(inner, mine, theirs, weights, first, second, sums, gains, gains_first, gains_second):
    rows, cols = weights.shape
    wide = mine.shape[1]
    by_row = lambda width: pl.BlockSpec((BAND, width), lambda n: (n, 0))
    whole = lambda values: pl.BlockSpec(values.shape, lambda n: (0, 0))
    shape = jax.ShapeDtypeStruct
    return pl.pallas_call(
        update_kernel,
        grid=(rows // BAND,),
        out_shape=[shape((rows, cols), F32)] * 4 + [shape(gains.shape, F32)] * 4,
        in_specs=[pl.BlockSpec(memory_space=pltpu.SMEM)]
        + [by_row(wide)] * 2
        + [by_row(cols)] * 3
        + [whole(sums)]
        + [whole(gains)] * 3,
        out_specs=[by_row(cols)] * 4 + [whole(gains)] * 4,
        compiler_params=pltpu.CompilerParams(vmem_limit_bytes=VMEM_BYTES),
        name="update",
    )(inner, mine, theirs, weights, first, second, sums, gains, gains_first, gains_second)


def on_device(
    tokens, gains_taps, weights, cotangent, weight_first, weight_second, gains_first, gains_second
):
    seq, shard = lax.axis_index("seq"), lax.axis_index("shard")
    inner = seq % 2
    layers = lax.axis_size("seq") // 2
    inner_word = inner.astype(jnp.int32).reshape(1)
    own, oth = halves(weights, inner_word)
    taps = lax.dynamic_slice(gains_taps, (2, shard * QUARTER + inner * HALF_Q), (3, HALF_Q))
    taps = jnp.pad(taps, ((0, 0), (0, WIDE - HALF_Q)))
    block_out, input_grad, gain_sums, mine, theirs = block_step(
        tokens[0], cotangent[0], gains_taps, taps, own, oth, layers
    )
    (
        weight_grad, weight_first_new, weight_second_new, weight_new,
        gains_grad, gains_first_new, gains_second_new, gains_new,
    ) = update(
        inner_word, mine, theirs, weights, weight_first, weight_second, gain_sums, gains_taps, gains_first, gains_second
    )
    return (
        block_out[None],
        input_grad[None],
        weight_grad,
        weight_first_new,
        weight_second_new,
        weight_new,
        gains_grad,
        gains_first_new,
        gains_second_new,
        gains_new,
    )


def solution(mesh):
    tokens, rows, whole = P("shard", "seq", None), P("seq", "shard"), P()
    return jax.shard_map(
        on_device,
        mesh=mesh,
        in_specs=(tokens, whole, rows, tokens, rows, rows, whole, whole),
        out_specs=(tokens, tokens, rows, rows, rows, rows, whole, whole, whole, whole),
        check_vma=False,
    )
```

```python
import functools

import jax
import jax.numpy as jnp
from jax import lax
from jax.experimental import pallas as pl
from jax.experimental.pallas import tpu as pltpu
from jax.sharding import PartitionSpec as P

D = 1536
FF = 6912
STEP = 10
GROUPS = 4
QUARTER = D // GROUPS
UNITS = FF // GROUPS
HALF_Q = QUARTER // 2
HALF_F = UNITS // 2
LANES = 128
PAD_F = -(-HALF_F // LANES) * LANES
WIDE = 256
CONV_COLS = 4 * HALF_Q
UNIT_CHUNKS = (384, 256, PAD_F - 640)
UNIT_STARTS = (0, 384, 640)
WIDTHS = (CONV_COLS,) + tuple(3 * units for units in UNIT_CHUNKS)
STARTS = tuple(sum(WIDTHS[:k]) for k in range(len(WIDTHS)))
SPLIT = 128
REACH = (1, 1, 1, 1)
SLICE = 384
TILE = 16
ROWS = 48

MOMENT_DECAY = 0.9
SQUARE_DECAY = 0.95
ADAM_EPSILON = 1e-08
NORM_EPSILON = 1e-05
WEIGHT_RATE = 0.02
GAIN_RATE = 0.2
WEIGHT_DECAY = 0.1

BF16 = jnp.bfloat16
F32 = jnp.float32
MESH = pl.DeviceIdType.MESH
VMEM_BYTES = 63 * 1024 * 1024


def place():
    seq, shard = lax.axis_index("seq"), lax.axis_index("shard")
    inner, core = lax.rem(seq, 2), lax.rem(shard, 2)
    return seq, shard, inner, core


def partners():
    seq, shard, inner, core = place()
    across = {"seq": seq + 1 - 2 * inner, "shard": shard}
    beside = {"seq": seq, "shard": lax.rem(shard + 2, 4)}
    twin = {"seq": seq, "shard": shard + 1 - 2 * core}
    return across, beside, twin


def remote(src, dst, send, recv, device):
    return pltpu.make_async_remote_copy(
        src_ref=src, dst_ref=dst, send_sem=send, recv_sem=recv, device_id=device, device_id_type=MESH
    )


def line():
    seq, shard, _, _ = place()
    return seq // 2, lambda steps: {"seq": seq + 2 * steps, "shard": shard}


def greet(layers):
    outer, at = line()
    barrier = pltpu.get_barrier_semaphore()
    for device in partners():
        pl.semaphore_signal(barrier, inc=1, device_id=device, device_id_type=MESH)
    for steps in range(1, layers):
        for sign in (1, -1):

            @pl.when(in_line(outer + sign * steps, layers))
            def _():
                pl.semaphore_signal(barrier, inc=1, device_id=at(sign * steps), device_id_type=MESH)

    pl.semaphore_wait(barrier, 3 + layers - 1)


def in_line(index, layers):
    return (index >= 0) & (index < layers)


def allow(credit):
    for device in partners():
        pl.semaphore_signal(credit, inc=1, device_id=device, device_id_type=MESH)


def dot(left, right):
    return jnp.dot(left, right, preferred_element_type=F32)


def dot_rows(left, right):
    return lax.dot_general(left, right, (((1,), (1,)), ((), ())), preferred_element_type=F32)


def dot_columns(left, right):
    return lax.dot_general(left, right, (((0,), (0,)), ((), ())), preferred_element_type=F32)


def aligned(start, size, multiple=16):
    return pl.ds(pl.multiple_of(start, multiple), size)


class Gather:
    def __init__(self, layers, rows, own, oth, outs, send_x, recv_x, send_z, recv_z, local):
        self.layers, self.rows, self.own, self.oth, self.outs = layers, rows, own, oth, outs
        self.send_x, self.recv_x, self.send_z, self.recv_z, self.local = send_x, recv_x, send_z, recv_z, local
        self.seq, _, self.inner, _ = place()
        self.outer, self.at = line()
        self.across = partners()[0]

    def seq_rows(self, index):
        return aligned(index * self.rows, self.rows)

    def layer_rows(self, direction, distance):
        origin = self.outer - distance if direction == 0 else self.outer + distance
        return aligned(origin * 2 * self.rows, 2 * self.rows)

    def copy(self, k, src, dst, direction, distance, hop, piece):
        slot = (k, direction, distance + hop - 1, piece)
        return remote(
            src, dst, self.send_z.at[slot], self.recv_z.at[slot], self.at(hop if direction == 0 else -hop)
        )

    def goes(self, direction, hop):
        return in_line(self.outer + (hop if direction == 0 else -hop), self.layers)

    def has_come(self, direction, distance):
        return in_line(self.outer + (-distance if direction == 0 else distance), self.layers)

    def hops(self, k, distance):
        return range(1, min(REACH[k], self.layers - 1 - distance) + 1)

    def own_copy(self, k, direction, hop):
        src = self.own.at[:, pl.ds(STARTS[k], WIDTHS[k])]
        return self.copy(k, src, self.outs[k].at[self.seq_rows(self.seq)], direction, 0, hop, 0)

    def other_copy(self, k, direction, hop):
        there = self.outs[k].at[self.seq_rows(self.seq + 1 - 2 * self.inner)]
        return self.copy(k, there, there, direction, 0, hop, 1)

    def pass_copy(self, k, direction, distance, hop):
        ref = self.outs[k].at[self.layer_rows(direction, distance)]
        return self.copy(k, ref, ref, direction, distance, hop, 0)

    def x_copy(self, k):
        return remote(
            self.oth.at[:, pl.ds(STARTS[k], WIDTHS[k])],
            self.outs[k].at[self.seq_rows(self.seq)],
            self.send_x.at[k],
            self.recv_x.at[k],
            self.across,
        )

    def l_copy(self, k):
        return pltpu.make_async_copy(
            self.own.at[:, pl.ds(STARTS[k], WIDTHS[k])], self.outs[k].at[self.seq_rows(self.seq)], self.local.at[k]
        )

    def exchange(self, k):
        self.x_copy(k).start()
        self.l_copy(k).start()

    def send_own(self, k):
        for hop in self.hops(k, 0):
            for direction in (0, 1):

                @pl.when(self.goes(direction, hop))
                def _():
                    self.own_copy(k, direction, hop).start()

    def send_other(self, k):
        self.x_copy(k).wait_recv()
        for hop in self.hops(k, 0):
            for direction in (0, 1):

                @pl.when(self.goes(direction, hop))
                def _():
                    self.other_copy(k, direction, hop).start()

    def step(self, k, distance):
        for direction in (0, 1):

            @pl.when(self.has_come(direction, distance))
            def _():
                if distance <= REACH[k]:
                    origin = self.outer - distance if direction == 0 else self.outer + distance
                    for piece in (0, 1):
                        index = 2 * origin + (self.inner if piece == 0 else 1 - self.inner)
                        ref = self.outs[k].at[self.seq_rows(index)]
                        self.copy(k, ref, ref, direction, distance - 1, 1, piece).wait_recv()
                else:
                    ref = self.outs[k].at[self.layer_rows(direction, distance)]
                    self.copy(k, ref, ref, direction, distance - 1, 1, 0).wait_recv()
                if distance % REACH[k] == 0:
                    for hop in self.hops(k, distance):

                        @pl.when(self.goes(direction, hop))
                        def _():
                            self.pass_copy(k, direction, distance, hop).start()

        if distance == self.layers - 1:
            self.l_copy(k).wait()

    def steps(self, k, first, last=None):
        last = self.layers - 1 if last is None else min(last, self.layers - 1)
        for distance in range(first, last + 1):
            self.step(k, distance)

    def finish(self):
        for k in range(len(self.outs)):
            self.x_copy(k).wait_send()
            for distance in range(0, self.layers - 1, REACH[k]):
                for hop in self.hops(k, distance):
                    for direction in (0, 1):

                        @pl.when(self.goes(direction, hop) & self.has_come(direction, distance))
                        def _():
                            if distance == 0:
                                self.own_copy(k, direction, hop).wait_send()
                                self.other_copy(k, direction, hop).wait_send()
                            else:
                                self.pass_copy(k, direction, distance, hop).wait_send()


class Reduce:
    def __init__(self, layers, rows, grads, slots, stage, spare, total, outgoing, mine, theirs, sems):
        self.layers, self.rows, self.grads, self.slots = layers, rows, grads, slots
        self.stage, self.spare, self.total, self.outgoing = stage, spare, total, outgoing
        self.mine, self.theirs = mine, theirs
        self.send_g, self.recv_g, self.fetched, self.fetches, self.stored, self.send_o, self.recv_o = sems
        _, _, self.inner, _ = place()
        self.outer, self.at = line()
        self.across = partners()[0]

    def owner(self, direction, distance):
        return self.outer + distance if direction == 0 else self.outer - distance

    def upstream(self, direction, steps):
        return in_line(self.outer - steps if direction == 0 else self.outer + steps, self.layers)

    def block(self, k, owner):
        return self.grads[k].at[aligned(owner * 2 * self.rows, 2 * self.rows), pl.ds(0, WIDTHS[k])]

    def copy(self, k, src, direction, distance):
        hop = 1 if distance % 2 else 2
        slot = (direction, distance - 1)
        return remote(
            src,
            self.slots[k].at[slot],
            self.send_g.at[(k,) + slot],
            self.recv_g.at[(k,) + slot],
            self.at(hop if direction == 0 else -hop),
        )

    def send(self, k, direction, distance):
        self.copy(k, self.block(k, self.owner(direction, distance)), direction, distance).start()

    def direct(self, k, part=None, ends=None):
        at_end = (self.outer == 0) | (self.outer == self.layers - 1)
        for distance in range(self.layers - 1, 0, -1):
            for direction in (0, 1):
                owner = self.owner(direction, distance)
                here = in_line(owner, self.layers)
                if part is not None:
                    here = here & (owner * 2 * self.rows // SLICE == part)
                if ends is not None:
                    here = here & (at_end if ends else jnp.logical_not(at_end))
                if distance % 2 == 0:
                    here = here & jnp.logical_not(self.upstream(direction, 1))

                @pl.when(here)
                def _():
                    self.send(k, direction, distance)

    def fetch(self, k, direction, distance):
        slot = self.slots[k].at[direction, distance - 1]
        self.copy(k, slot, direction, distance).wait_recv()
        held = self.stage.at[:, pl.ds(0, WIDTHS[k])]
        copy = pltpu.make_async_copy(slot, held, self.fetched)
        copy.start()
        copy.wait()

    def tiles(self, body):
        def step(n, _):
            body(aligned(n * TILE, TILE))
            return 0

        lax.fori_loop(0, 2 * self.rows // TILE, step, 0)

    def join(self, k):
        cols = pl.ds(0, WIDTHS[k])
        for distance in range((self.layers - 1) // 2 * 2, 0, -2):
            for direction in (0, 1):
                owner = self.owner(direction, distance)

                @pl.when(in_line(owner, self.layers) & self.upstream(direction, 1))
                def _():
                    def add(tile):
                        base = self.owner(direction, distance) * 2 * self.rows
                        rows = pl.ds(pl.multiple_of(base + tile.start, 16), TILE)
                        ref = self.grads[k]
                        ref[rows, cols] = (
                            ref[rows, cols].astype(F32) + self.stage[tile, cols].astype(F32)
                        ).astype(BF16)

                    self.fetch(k, direction, distance + 1)
                    self.tiles(add)
                    if distance + 2 < self.layers:

                        @pl.when(self.upstream(direction, 2))
                        def _():
                            self.fetch(k, direction, distance + 2)
                            self.tiles(add)

                    self.send(k, direction, distance)

    def final(self, k, before=None):
        cols = pl.ds(0, WIDTHS[k])
        came = [(distance, direction) for distance in (1, 2) for direction in (0, 1) if distance < self.layers]

        def fetch(n, distance, direction):
            return pltpu.make_async_copy(
                self.slots[k].at[direction, distance - 1],
                self.spare.at[pl.ds(n * 2 * self.rows, 2 * self.rows), cols],
                self.fetches.at[n],
            )

        for n, (distance, direction) in enumerate(came):

            @pl.when(self.upstream(direction, distance))
            def _():
                self.copy(k, self.slots[k].at[direction, distance - 1], direction, distance).wait_recv()
                fetch(n, distance, direction).start()

        if before is not None:
            self.store(before).wait()

        here, there = self.inner * self.rows, (1 - self.inner) * self.rows

        def each(base, body):
            def step(n, _):
                body(base + n * TILE, n * TILE)
                return 0

            lax.fori_loop(0, self.rows // TILE, step, 0)

        for n, (distance, direction) in enumerate(came):

            @pl.when(self.upstream(direction, distance))
            def _():
                fetch(n, distance, direction).wait()

        def add_up(flags):
            def total(rows):
                value = self.grads[k][aligned(self.outer * 2 * self.rows + rows, TILE), cols].astype(F32)
                for n, flag in enumerate(flags):
                    if flag:
                        value = value + self.spare[aligned(n * 2 * self.rows + rows, TILE), cols].astype(F32)
                return value

            def send(rows, at):
                self.outgoing[aligned(at, TILE), pl.ds(STARTS[k], WIDTHS[k])] = total(rows).astype(BF16)

            def keep(rows, at):
                self.total[aligned(at, TILE), cols] = total(rows)

            each(there, send)
            self.over(k).start()
            each(here, keep)
            self.store(k).start()

        patterns = {}
        for place_in_line in range(self.layers):
            flags = tuple(
                0 <= (place_in_line - distance if direction == 0 else place_in_line + distance) < self.layers
                for distance, direction in came
            )
            patterns.setdefault(flags, []).append(place_in_line)
        for flags, places in patterns.items():
            here_now = functools.reduce(jnp.logical_or, [self.outer == p for p in places])

            @pl.when(here_now)
            def _():
                add_up(flags)

    def over(self, k):
        wide = pl.ds(STARTS[k], WIDTHS[k])
        return remote(
            self.outgoing.at[:, wide], self.theirs.at[:, wide], self.send_o.at[k], self.recv_o.at[k], self.across
        )

    def store(self, k):
        return pltpu.make_async_copy(
            self.total.at[:, pl.ds(0, WIDTHS[k])], self.mine.at[:, pl.ds(STARTS[k], WIDTHS[k])], self.stored.at[k]
        )

    def wait_sent(self, k):
        for distance in range(1, self.layers):
            for direction in (0, 1):
                owner = self.owner(direction, distance)

                @pl.when(in_line(owner, self.layers))
                def _():
                    self.copy(k, self.block(k, owner), direction, distance).wait_send()

    def finish(self, before):
        self.store(before).wait()
        for k in range(len(self.grads)):
            self.over(k).wait()


class Spread:
    def __init__(self, buf, seg, split, send, recv):
        self.buf, self.seg, self.split, self.send, self.recv = buf, seg, split, send, recv
        self.both = split < seg

    def index(self, n):
        _, shard, inner, core = place()
        row, flip, other = (n // 2) % 2, n // 4, n % 2
        return 2 * (lax.rem(shard + 2 * row, 4) + other * (1 - 2 * core)) + inner + flip * (1 - 2 * inner)

    def copy(self, slot):
        across, beside, twin = partners()
        low, high, whole = (0, self.split), (self.split, self.seg - self.split), (0, self.seg)
        n, (first, size), device = {
            0: (0, whole, across),
            1: (0, whole, beside),
            2: (0, whole, twin),
            3: (4, low, beside),
            4: (4, whole, twin),
            5: (2, high, across),
            6: (2, whole, twin),
            7: (6, low, twin),
            8: (6, high, twin),
        }[slot]
        ref = self.buf.at[aligned(self.index(n) * self.seg + first, size)]
        return remote(ref, ref, self.send.at[slot], self.recv.at[slot], device)

    def push(self, *slots):
        for slot in slots:
            if self.both or slot not in (5, 8):
                self.copy(slot).start()

    def came(self, *slots):
        for slot in slots:
            if self.both or slot not in (5, 8):
                self.copy(slot).wait_recv()

    def start(self):
        self.push(0, 1, 2)

    def near(self):
        self.came(1)
        self.push(5, 6)
        self.came(0)
        self.push(3, 4)

    def far(self):
        self.came(3)
        self.push(7)
        self.came(5)
        self.push(8)

    def end(self, *came):
        self.came(*came)
        for slot in range(9):
            if self.both or slot not in (5, 8):
                self.copy(slot).wait_send()

    def run(self, body, hooks):
        waits = {
            1: lambda: self.came(2),
            2: self.near,
            3: lambda: self.came(6),
            5: lambda: self.came(4),
            6: self.far,
            7: lambda: self.came(7, 8),
        }

        def step(n, _):
            for m in range(8):
                acts = [a[m] for a in (hooks, waits) if m in a]
                if acts:

                    @pl.when(n == m)
                    def _():
                        for act in acts:
                            act()

            body(self.index(n))
            return 0

        lax.fori_loop(0, 8, step, 0)
        self.end()


def collect_steps(part, seg, total, pair, near, joined, send, recv, produce=None):
    _, shard, inner, core = place()
    across, beside, twin = partners()
    low, high, whole = (0, SPLIT), (SPLIT, seg - SPLIT), (0, seg)
    twin_shard = shard + 1 - 2 * core
    cols = pl.ds(0, D)

    def index(s, k):
        row, flip = 1 - k % 2, 1 - k // 2
        return 2 * lax.rem(s + 2 * row, 4) + inner + flip * (1 - 2 * inner)

    def pair_copy(k):
        src = part.at[aligned(index(twin_shard, k) * seg, seg), cols]
        return remote(src, pair.at[k], send.at[k], recv.at[k], twin)

    def copy(slot):
        src, dst, (first, size), device = {
            4: (pair.at[0], joined, low, across),
            5: (pair.at[0], joined, high, beside),
            6: (pair.at[1], near.at[0], low, across),
            7: (pair.at[2], near.at[1], high, beside),
            8: (pair.at[2], near.at[1], low, beside),
            9: (pair.at[1], near.at[0], high, across),
        }[slot]
        rows = pl.ds(first, size)
        return remote(src.at[rows], dst.at[rows], send.at[slot], recv.at[slot], device)

    def over(span, body):
        def step(n, _):
            body(aligned(span[0] + n * 16, 16))
            return 0

        lax.fori_loop(0, span[1] // 16, step, 0)

    def add_pair(k):
        def add(rows):
            mine = part[aligned(index(shard, k) * seg + rows.start, 16), cols].astype(F32)
            pair[k, rows] = (mine + pair[k, rows].astype(F32)).astype(BF16)

        pair_copy(k).wait_recv()
        over(whole, add)

    def add_own():
        def add(rows):
            mine = part[aligned(index(shard, 3) * seg + rows.start, 16), cols].astype(F32)
            total[rows] = mine + pair[3, rows].astype(F32)

        pair_copy(3).wait_recv()
        over(whole, add)

    def pass_on(slot, k, span, after):
        def add(rows):
            pair[k, rows] = (pair[k, rows].astype(F32) + joined[rows].astype(F32)).astype(BF16)

        copy(slot).wait_recv()
        over(span, add)
        copy(after).start()

    def after_pair(k):
        add_pair(k)
        if k == 0:
            copy(4).start()
            copy(5).start()
        elif k == 1:
            copy(6).start()
        else:
            copy(7).start()
            pass_on(4, 2, low, 8)
            pass_on(5, 1, high, 9)

    def half(base):
        def step(n, _):
            k, own = base + n // 2, n % 2
            produce(index(jnp.where(own == 1, shard, twin_shard), k))

            @pl.when(own == 0)
            def _():
                pair_copy(k).start()

            for m in (base, base + 1):

                @pl.when((own == 1) & (k == m))
                def _():
                    if m < 3:
                        after_pair(m)
                    else:
                        add_own()

            return 0

        lax.fori_loop(0, 4, step, 0)

    if produce is None:
        for k in range(4):
            pair_copy(k).start()
        yield
        after_pair(0)
        after_pair(1)
        yield
        after_pair(2)
        add_own()
    else:
        half(0)
        yield
        half(2)
    yield

    def add_near(span):
        def add(rows):
            total[rows] = total[rows] + near[0, rows].astype(F32) + near[1, rows].astype(F32)

        over(span, add)

    copy(6).wait_recv()
    copy(8).wait_recv()
    add_near(low)
    copy(7).wait_recv()
    copy(9).wait_recv()
    add_near(high)
    for k in range(4):
        pair_copy(k).wait_send()
    for slot in range(4, 10):
        copy(slot).wait_send()


def drain(steps):
    for _ in steps:
        pass


def norm_scale(values):
    return lax.rsqrt(jnp.mean(values * values, axis=-1, keepdims=True) + NORM_EPSILON)


def by_rows(rows, body, carry=0):
    def step(n, carry):
        return body(aligned(n * ROWS, ROWS), carry)

    return lax.fori_loop(0, rows // ROWS, step, carry)


def norm_back(values, gain, upstream):
    scale = norm_scale(values)
    scaled = gain * upstream
    inner = jnp.mean(scaled * values, axis=-1, keepdims=True)
    return (
        scale * scaled - values * scale * scale * scale * inner,
        jnp.sum(upstream * values * scale, axis=0, keepdims=True),
    )


REFS = (
    "tok", "cot", "gains", "own", "oth",
    "block_out", "input_grad", "gain_sums", "mine", "theirs", "n1_held", "slot0", "slot1", "slot2", "slot3",
    "w0", "w1", "w2", "w3", "seq_a", "seq_b", "du", "act", "c_all", "gated", "mixed", "resid", "dresid", "total",
    "pair", "near", "joined", "g1", "g2", "g3", "stage", "sum", "outgoing", "gain_in", "gain_line",
    "held", "local", "send_x", "recv_x", "send_z", "recv_z", "send_s", "recv_s", "send_c", "recv_c", "credit",
    "halo_send", "halo_recv", "send_g", "recv_g", "fetched", "fetches", "stored", "send_o", "recv_o",
    "send_a", "recv_a", "send_l", "recv_l",
)


def block_kernel(layers, rows, *all_refs):
    r = dict(zip(REFS, all_refs, strict=True))
    tok, cot, gains = r["tok"], r["cot"], r["gains"]
    seq_a, seq_b, du, act = r["seq_a"], r["seq_b"], r["du"], r["act"]
    c_all, gated, mixed, total = r["c_all"], r["gated"], r["mixed"], r["total"]
    weights = (r["w0"], r["w1"], r["w2"], r["w3"])
    seg = tok.shape[0]
    _, shard, inner, _ = place()
    outer, at = line()
    me = 2 * shard + inner
    my_rows = aligned(me * seg, seg)
    chunks = list(zip(range(1, 1 + len(UNIT_CHUNKS)), UNIT_STARTS, UNIT_CHUNKS))
    gather = Gather(
        layers, rows, r["own"], r["oth"], weights,
        r["send_x"], r["recv_x"], r["send_z"], r["recv_z"], r["local"],
    )
    reduce = Reduce(
        layers, rows, (r["w2"], r["g1"], r["g2"], r["g3"]), (r["slot0"], r["slot1"], r["slot2"], r["slot3"]),
        r["stage"], r["w1"], r["sum"], r["outgoing"], r["mine"], r["theirs"],
        (r["send_g"], r["recv_g"], r["fetched"], r["fetches"], r["stored"], r["send_o"], r["recv_o"]),
    )

    def spread(buf, n, split=SPLIT):
        return Spread(buf, seg, split, r["send_s"].at[n], r["recv_s"].at[n])

    def collect(part, n, produce=None):
        return collect_steps(
            part, seg, total, r["pair"], r["near"], r["joined"], r["send_c"].at[n], r["recv_c"].at[n], produce
        )

    def block(t):
        return aligned(t * seg, seg)

    lanes = lax.broadcasted_iota(jnp.int32, (seg, WIDE), 1) < HALF_Q
    taps = pltpu.roll(gains[...], lax.rem(D - shard * QUARTER - inner * HALF_Q, D), 1)[2:5, :WIDE]

    greet(layers)
    gather.exchange(0)
    gather.send_own(0)

    def mine(part):
        return pl.ds(pl.multiple_of(me * seg + part.start, 16), part.size)

    def first_norm(part, _):
        values = tok[part].astype(F32)
        seq_a[mine(part)] = (values * norm_scale(values) * gains[0:1, :]).astype(BF16)
        return 0

    by_rows(seg, first_norm)
    one = spread(seq_a, 0)
    one.start()
    seq_b[my_rows] = cot[...]
    gather.send_other(0)
    gather.steps(0, 1, 1)
    one.near()
    gather.exchange(1)
    gather.steps(0, 2, 2)
    gather.send_own(1)
    one.far()
    one.end(2, 4, 6, 7, 8)
    held = pltpu.make_async_copy(seq_a, r["n1_held"], r["held"])
    held.start()
    up = spread(seq_b, 1, seg)
    up.start()
    gather.steps(0, 3)

    def project(s, _):
        for i in (0, 1):
            parts = dot(seq_a[block(2 * s + i)], weights[0][...])
            b = jnp.where(lanes, parts[:, :WIDE], 0.0)
            c = pltpu.roll(parts[:, 128 : 128 + 384], 384 - 64, 1)[:, :WIDE]
            x = parts[:, 384 : 384 + WIDE]
            c_all[s, pl.ds(i * seg, seg)] = jnp.where(lanes, c, 0.0)
            gated[s, pl.ds(8 + i * seg, seg)] = (b * x).astype(BF16).astype(F32)
        return 0

    lax.fori_loop(0, GROUPS, project, 0)
    ahead = remote(
        gated.at[:, pl.ds(2 * seg, 8)], gated.at[:, pl.ds(0, 8)], r["halo_send"].at[0], r["halo_recv"].at[0], at(1)
    )

    @pl.when(outer < layers - 1)
    def _():
        ahead.start()

    @pl.when(outer == 0)
    def _():
        gated[:, pl.ds(0, 8)] = jnp.zeros((GROUPS, 8, WIDE), F32)

    gather.send_other(1)
    up.near()
    gather.exchange(2)
    gather.send_own(2)
    held.wait()

    @pl.when(outer > 0)
    def _():
        ahead.wait_recv()

    def convolved(s, i):
        return (
            taps[0:1, :] * gated[s, pl.ds(6 + i * seg, seg)]
            + taps[1:2, :] * gated[s, pl.ds(7 + i * seg, seg)]
            + taps[2:3, :] * gated[s, pl.ds(8 + i * seg, seg)]
        )

    def convolve(t):
        for i in (0, 1):

            @pl.when(t % 2 == i)
            def _():
                s = t // 2
                mixed[block(t)] = pltpu.roll(c_all[s, pl.ds(i * seg, seg)] * convolved(s, i), 64, 1).astype(BF16)

        seq_a[block(t)] = dot_rows(mixed[block(t)], weights[0][:, pl.ds(512, WIDE)]).astype(BF16)

    branch = collect(seq_a, 0, convolve)
    next(branch)
    gather.exchange(3)
    gather.steps(1, 1, 1)
    gather.send_other(2)
    next(branch)
    up.far()
    gather.steps(1, 2, 2)
    drain(branch)
    allow(r["credit"].at[0])

    def second_norm(part, _):
        values = tok[part].astype(F32) + total[part]
        r["resid"][part] = values
        seq_a[mine(part)] = (values * norm_scale(values) * gains[1:2, :]).astype(BF16)
        return 0

    by_rows(seg, second_norm)
    gather.send_own(3)
    gather.send_other(3)
    pl.semaphore_wait(r["credit"].at[0], 3)
    two = spread(seq_a, 2)
    two.start()
    up.end(2, 4, 6, 7, 8)

    def hidden(k, start, units, t):
        ref, here = weights[k], block(t)
        gate = dot(seq_a[here], ref[:, pl.ds(0, units)])
        upval = dot(seq_a[here], ref[:, pl.ds(units, units)])
        dact = dot(seq_b[here], ref[:, pl.ds(2 * units, units)])
        sigma = jax.nn.sigmoid(gate)
        silu = gate * sigma
        act[here, pl.ds(start, units)] = (silu * upval).astype(BF16)
        dgate = dact * upval * sigma * (1.0 + gate * (1.0 - sigma))
        du[here, pl.ds(2 * start, units)] = dgate.astype(BF16)
        du[here, pl.ds(2 * start + units, units)] = (dact * silu).astype(BF16)

    def each_block(body):
        def step(t, _):
            body(t)
            return 0

        lax.fori_loop(0, 2 * GROUPS, step, 0)

    def slices(body):
        def step(n, _):
            body(jnp.where(outer < layers // 2, D // SLICE - 1 - n, n))
            return 0

        lax.fori_loop(0, D // SLICE, step, 0)

    def gate_up_grads(k, start, units, part):
        held_rows = aligned(part * SLICE, SLICE)
        left = seq_a[:, aligned(part * SLICE, SLICE, 128)]
        for m in (0, 1):
            reduce.grads[k][held_rows, pl.ds(m * units, units)] = dot_columns(
                left, du[:, pl.ds(2 * start + m * units, units)]
            ).astype(BF16)

    def down_grads(k, start, units, part):
        held_rows = aligned(part * SLICE, SLICE)
        left = seq_b[:, aligned(part * SLICE, SLICE, 128)]
        reduce.grads[k][held_rows, pl.ds(2 * units, units)] = dot_columns(
            left, act[:, pl.ds(start, units)]
        ).astype(BF16)

    two.run(
        functools.partial(hidden, *chunks[0]),
        {0: lambda: gather.steps(1, 3), 3: lambda: gather.steps(2, 1, 1), 7: lambda: gather.steps(2, 2, 2)},
    )
    gather.steps(3, 1, 1)
    def grads(k, start, units, part):
        gate_up_grads(k, start, units, part)
        down_grads(k, start, units, part)
        reduce.direct(k, part, ends=True)

    slices(functools.partial(grads, *chunks[0]))
    gather.steps(2, 3)
    each_block(functools.partial(hidden, *chunks[1]))
    gather.steps(3, 2, 2)
    slices(functools.partial(grads, *chunks[1]))
    gather.steps(3, 3)
    reduce.direct(1, ends=False)
    reduce.direct(2, ends=False)
    each_block(functools.partial(hidden, *chunks[2]))
    slices(functools.partial(down_grads, *chunks[2]))
    gather.finish()

    def second(t):
        here = block(t)
        seq_b[here] = sum(
            dot_rows(du[here, pl.ds(2 * start, 2 * units)], weights[k][:, pl.ds(0, 2 * units)])
            for k, start, units in chunks
        ).astype(BF16)

    down = collect(seq_b, 1, second)
    next(down)
    next(down)
    reduce.join(1)

    slices(functools.partial(gate_up_grads, *chunks[2]))

    def forward(t):
        here = block(t)
        du[here, pl.ds(0, D)] = sum(
            dot_rows(act[here, pl.ds(start, units)], weights[k][:, pl.ds(2 * units, units)])
            for k, start, units in chunks
        ).astype(BF16)

    drain(down)
    reload = pltpu.make_async_copy(r["n1_held"], seq_b, r["held"])
    reload.start()
    allow(r["credit"].at[1])

    def second_back(part, gain):
        dpart, dgain = norm_back(r["resid"][part], gains[1:2, :], total[part])
        dresid = cot[part].astype(F32) + dpart
        r["dresid"][part] = dresid
        seq_a[mine(part)] = dresid.astype(BF16)
        return gain + dgain

    gain_two = by_rows(seg, second_back, jnp.zeros((1, D), F32))
    pl.semaphore_wait(r["credit"].at[1], 3)
    three = spread(seq_a, 3)
    three.start()

    kept = pl.ds(D, WIDE)

    def mix_back(t):
        s, here = t // 2, block(t)
        dmixed = pltpu.roll(dot(seq_a[here], weights[0][:, pl.ds(512, WIDE)]), WIDE - 64, 1)
        dmixed = jnp.where(lanes, dmixed, 0.0)
        for i in (0, 1):

            @pl.when(t % 2 == i)
            def _():
                du[here, kept] = (dmixed * convolved(s, i)).astype(BF16)
                c_all[s, pl.ds(i * seg, seg)] = dmixed * c_all[s, pl.ds(i * seg, seg)]

    three.run(
        mix_back, {1: lambda: each_block(forward), 3: lambda: reduce.final(1), 6: lambda: reduce.join(2)}
    )
    after = remote(
        c_all.at[:, pl.ds(0, 8)], c_all.at[:, pl.ds(2 * seg, 8)], r["halo_send"].at[1], r["halo_recv"].at[1], at(-1)
    )

    @pl.when(outer > 0)
    def _():
        after.start()

    @pl.when(outer == layers - 1)
    def _():
        c_all[:, pl.ds(2 * seg, 8)] = jnp.zeros((GROUPS, 8, WIDE), F32)

    reduce.direct(3)
    feed = collect(du, 2)
    next(feed)
    next(feed)
    reload.wait()

    @pl.when(outer < layers - 1)
    def _():
        after.wait_recv()

    def conv_back(s, sums):
        for i in (0, 1):
            t = block(2 * s + i)
            dconv = c_all[s, pl.ds(i * seg, seg)]
            dgated = (
                taps[2:3, :] * dconv
                + taps[1:2, :] * c_all[s, pl.ds(1 + i * seg, seg)]
                + taps[0:1, :] * c_all[s, pl.ds(2 + i * seg, seg)]
            )
            parts = dot(seq_b[t], weights[0][:, pl.ds(0, 640)])
            db = dgated * parts[:, 384:640]
            dx = dgated * parts[:, :WIDE]
            dc = jnp.concatenate([du[t, kept].astype(F32), jnp.zeros((seg, 128), F32)], axis=1)
            dc = pltpu.roll(dc, 64, 1)
            act[t, pl.ds(0, 128)] = db[:, :128].astype(BF16)
            act[t, pl.ds(128, 128)] = (db[:, 128:] + dc[:, :128]).astype(BF16)
            act[t, pl.ds(256, 128)] = dc[:, 128:256].astype(BF16)
            act[t, pl.ds(384, WIDE)] = dx.astype(BF16)
            act[t, pl.ds(640, 128)] = jnp.zeros((seg, 128), BF16)
            sums = sums + jnp.concatenate(
                [
                    jnp.sum(dconv * gated[s, pl.ds(6 + k + i * seg, seg)], axis=0, keepdims=True)
                    for k in range(3)
                ]
                + [jnp.zeros((5, WIDE), F32)],
                axis=0,
            )
        return sums

    tap_sums = lax.fori_loop(0, GROUPS, conv_back, jnp.zeros((8, WIDE), F32))
    next(feed)

    def conv_grads(part):
        held_rows, cols = aligned(part * SLICE, SLICE), aligned(part * SLICE, SLICE, 128)
        ref = reduce.grads[0]
        ref[held_rows, pl.ds(0, 512)] = dot_columns(seq_b[:, cols], act[:, pl.ds(0, 512)]).astype(BF16)
        ref[held_rows, pl.ds(512, WIDE)] = (
            dot_columns(seq_b[:, cols], act[:, pl.ds(512, WIDE)]) + dot_columns(seq_a[:, cols], mixed[...])
        ).astype(BF16)
        reduce.direct(0, part)

    slices(conv_grads)
    reduce.join(3)
    drain(feed)
    allow(r["credit"].at[2])
    r["block_out"][...] = (r["resid"][...] + total[...]).astype(BF16)
    pl.semaphore_wait(r["credit"].at[2], 3)

    def first(t):
        here = block(t)
        seq_a[here] = dot_rows(act[here, pl.ds(0, 640)], weights[0][:, pl.ds(0, 640)]).astype(BF16)

    inputs = collect(seq_a, 3, first)
    next(inputs)
    reduce.final(2, 1)
    next(inputs)
    reduce.join(0)
    reduce.final(3, 2)
    drain(inputs)

    def first_back(part, gain):
        dpart, dgain = norm_back(tok[part].astype(F32), gains[0:1, :], total[part])
        r["input_grad"][part] = (r["dresid"][part] + dpart).astype(BF16)
        return gain + dgain

    gain_one = by_rows(seg, first_back, jnp.zeros((1, D), F32))

    sums = r["gain_sums"]
    sums[...] = jnp.zeros(sums.shape, F32)
    sums[0:1, pl.ds(0, D)] = gain_one
    sums[1:2, pl.ds(0, D)] = gain_two
    sums[2:5, aligned(me * WIDE, WIDE, 128)] = tap_sums[0:3]
    for n, device in enumerate(partners()):
        copy = remote(sums, r["gain_in"].at[n], r["send_a"].at[n], r["recv_a"].at[n], device)
        copy.start()
        copy.wait()
        sums[...] = sums[...] + r["gain_in"][n]

    def line_copy(sign, steps):
        slot = (0 if sign > 0 else 1, steps - 1)
        return remote(
            sums, r["gain_line"].at[slot], r["send_l"].at[slot], r["recv_l"].at[slot], at(sign * steps)
        )

    for steps in range(1, layers):
        for sign in (1, -1):

            @pl.when(in_line(outer + sign * steps, layers))
            def _():
                line_copy(sign, steps).start()

    reduce.final(0, 3)
    for steps in range(1, layers):
        for sign in (1, -1):

            @pl.when(in_line(outer + sign * steps, layers))
            def _():
                line_copy(sign, steps).wait_send()

            @pl.when(in_line(outer - sign * steps, layers))
            def _():
                line_copy(sign, steps).wait_recv()

    own_sums = sums[...]
    for origin in range(layers):
        for steps in range(1, layers):
            for sign in (1, -1):

                @pl.when((outer - sign * steps == origin))
                def _():
                    came = r["gain_line"][0 if sign > 0 else 1, steps - 1]
                    sums[...] = came if origin == 0 else sums[...] + came

        if origin > 0:

            @pl.when(outer == origin)
            def _():
                sums[...] = sums[...] + own_sums

    reduce.finish(0)
    for k in range(len(WIDTHS)):
        reduce.wait_sent(k)

    @pl.when(outer < layers - 1)
    def _():
        ahead.wait_send()

    @pl.when(outer > 0)
    def _():
        after.wait_send()


def block_step(tok, cot, gains, own, oth, layers):
    rows, seg = own.shape[0], tok.shape[0]
    count = len(WIDTHS)
    tokens = 2 * GROUPS * seg
    vmem, anywhere = pl.BlockSpec(memory_space=pltpu.VMEM), pl.BlockSpec(memory_space=pl.ANY)
    shape, scratch = jax.ShapeDtypeStruct, pltpu.VMEM
    dma, regular = pltpu.SemaphoreType.DMA, pltpu.SemaphoreType.REGULAR
    hops = layers - 1
    wide, biggest = sum(WIDTHS), max(WIDTHS)
    out_shape = [
        shape((seg, D), BF16),
        shape((seg, D), BF16),
        shape((8, 2 * GROUPS * WIDE), F32),
        shape((rows, wide), F32),
        shape((rows, wide), BF16),
        shape((tokens, D), BF16),
    ] + [shape((2, hops, 2 * rows, width), BF16) for width in WIDTHS]
    scratch_shapes = (
        [scratch((D, width), BF16) for width in WIDTHS]
        + [
            scratch((tokens, D), BF16),
            scratch((tokens, D), BF16),
            scratch((tokens, 2 * PAD_F), BF16),
            scratch((tokens, PAD_F), BF16),
            scratch((GROUPS, 8 + 2 * seg, WIDE), F32),
            scratch((GROUPS, 8 + 2 * seg, WIDE), F32),
            scratch((tokens, WIDE), BF16),
            scratch((seg, D), F32),
            scratch((seg, D), F32),
            scratch((seg, D), F32),
            scratch((4, seg, D), BF16),
            scratch((2, seg, D), BF16),
            scratch((seg, D), BF16),
        ]
        + [scratch((D, width), BF16) for width in WIDTHS[1:]]
        + [
            scratch((2 * rows, biggest), BF16),
            scratch((rows, biggest), F32),
            scratch((rows, wide), BF16),
            scratch((3, 8, 2 * GROUPS * WIDE), F32),
            scratch((2, hops, 8, 2 * GROUPS * WIDE), F32),
            dma,
            dma((count,)),
            dma((count,)),
            dma((count,)),
            dma((count, 2, hops, 2)),
            dma((count, 2, hops, 2)),
            dma((4, 9)),
            dma((4, 9)),
            dma((4, 10)),
            dma((4, 10)),
            regular((3,)),
            dma((2,)),
            dma((2,)),
            dma((count, 2, hops)),
            dma((count, 2, hops)),
            dma,
            dma((4,)),
            dma((count,)),
            dma((count,)),
            dma((count,)),
            dma((3,)),
            dma((3,)),
            dma((2, hops)),
            dma((2, hops)),
        ]
    )
    return pl.pallas_call(
        functools.partial(block_kernel, layers, rows),
        out_shape=out_shape,
        in_specs=[vmem] * 3 + [anywhere] * 2,
        out_specs=[vmem] * 3 + [anywhere] * (3 + count),
        scratch_shapes=scratch_shapes,
        compiler_params=pltpu.CompilerParams(
            collective_id=0, has_side_effects=True, vmem_limit_bytes=VMEM_BYTES
        ),
        name="block_step",
    )(tok, cot, gains, own, oth)[:5]


def column_pieces(half):
    pieces = [(m * QUARTER + half * HALF_Q, m * HALF_Q, HALF_Q, 0) for m in range(4)]
    for k, (start, units) in enumerate(zip(UNIT_STARTS, UNIT_CHUNKS), 1):
        real = min(units, HALF_F - start)
        for m in range(3):
            first = 4 * QUARTER + m * UNITS + half * HALF_F + start
            pieces.append((first, STARTS[k] + m * units, real, units - real))
    return pieces


def halves_kernel(inner_ref, weights_ref, own_ref, oth_ref):
    is_low = inner_ref[0] == 0

    def half(h):
        parts = []
        for first, _, width, padding in column_pieces(h):
            parts.append(weights_ref[:, first : first + width])
            if padding:
                parts.append(jnp.zeros((parts[-1].shape[0], padding), F32))
        return jnp.concatenate(parts, axis=1)

    low, high = half(0), half(1)
    own_ref[...] = jnp.where(is_low, low, high).astype(BF16)
    oth_ref[...] = jnp.where(is_low, high, low).astype(BF16)


def band(rows, most):
    return max(size for size in range(16, most + 1, 16) if rows % size == 0)


def halves(weights, inner):
    rows, cols = weights.shape
    wide = sum(WIDTHS)
    size = band(rows, 96)
    by_row = lambda width: pl.BlockSpec((size, width), lambda n: (n, 0))
    return pl.pallas_call(
        halves_kernel,
        grid=(rows // size,),
        out_shape=[jax.ShapeDtypeStruct((rows, wide), BF16)] * 2,
        in_specs=[pl.BlockSpec(memory_space=pltpu.SMEM), by_row(cols)],
        out_specs=[by_row(wide)] * 2,
        compiler_params=pltpu.CompilerParams(vmem_limit_bytes=VMEM_BYTES),
        name="halves",
    )(inner, weights)


def adam_update(param, grad, first, second, rate, decay):
    first_new = MOMENT_DECAY * first + (1.0 - MOMENT_DECAY) * grad
    second_new = SQUARE_DECAY * second + (1.0 - SQUARE_DECAY) * grad * grad
    first_hat = first_new / (1.0 - MOMENT_DECAY**STEP)
    second_hat = second_new / (1.0 - SQUARE_DECAY**STEP)
    param_new = param - rate * (first_hat / (jnp.sqrt(second_hat) + ADAM_EPSILON) + decay * param)
    return (first_new, second_new, param_new)


def update_kernel(
    inner_ref, mine_ref, theirs_ref, weights_ref, first_ref, second_ref, sums_ref, gains_ref, gains_first_ref,
    gains_second_ref, block_ref, input_ref, grad_out, first_out, second_out, weights_out, gains_grad_out,
    gains_first_out, gains_second_out, gains_out, block_out, input_out, copied,
):
    copies = (
        pltpu.make_async_copy(block_ref, block_out, copied.at[0]),
        pltpu.make_async_copy(input_ref, input_out, copied.at[1]),
    )

    @pl.when(pl.program_id(0) == 0)
    def _():
        for copy in copies:
            copy.start()

    is_low = inner_ref[0] == 0
    mine, theirs = mine_ref[...], theirs_ref[...].astype(F32)
    for half in (0, 1):
        chosen = jnp.where(is_low, mine, theirs) if half == 0 else jnp.where(is_low, theirs, mine)
        for first, own, width, _ in column_pieces(half):
            grad_out[:, first : first + width] = chosen[:, own : own + width]
    first_out[...], second_out[...], weights_out[...] = adam_update(
        weights_ref[...], grad_out[...], first_ref[...], second_ref[...], WEIGHT_RATE, WEIGHT_DECAY
    )

    @pl.when(pl.program_id(0) == 0)
    def _():
        gains_grad_out[0:2] = sums_ref[0:2, :D]
        for n in range(2 * GROUPS):
            gains_grad_out[2:5, n * HALF_Q : (n + 1) * HALF_Q] = sums_ref[2:5, n * WIDE : n * WIDE + HALF_Q]
        gains_first_out[...], gains_second_out[...], gains_out[...] = adam_update(
            gains_ref[...], gains_grad_out[...], gains_first_ref[...], gains_second_ref[...], GAIN_RATE, 0.0
        )

    @pl.when(pl.program_id(0) == pl.num_programs(0) - 1)
    def _():
        for copy in copies:
            copy.wait()


def update(inner, mine, theirs, weights, first, second, sums, gains, gains_first, gains_second, block, grad):
    rows, cols = weights.shape
    wide = mine.shape[1]
    size = band(rows, 32)
    by_row = lambda width: pl.BlockSpec((size, width), lambda n: (n, 0))
    whole = lambda values: pl.BlockSpec(values.shape, lambda n: (0, 0))
    anywhere = pl.BlockSpec(memory_space=pl.ANY)
    shape = jax.ShapeDtypeStruct
    return pl.pallas_call(
        update_kernel,
        grid=(rows // size,),
        out_shape=[shape((rows, cols), F32)] * 4 + [shape(gains.shape, F32)] * 4 + [shape(block.shape, BF16)] * 2,
        in_specs=[pl.BlockSpec(memory_space=pltpu.SMEM)]
        + [by_row(wide)] * 2
        + [by_row(cols)] * 3
        + [whole(sums)]
        + [whole(gains)] * 3
        + [anywhere] * 2,
        out_specs=[by_row(cols)] * 4 + [whole(gains)] * 4 + [anywhere] * 2,
        scratch_shapes=[pltpu.SemaphoreType.DMA((2,))],
        compiler_params=pltpu.CompilerParams(vmem_limit_bytes=VMEM_BYTES),
        name="update",
    )(inner, mine, theirs, weights, first, second, sums, gains, gains_first, gains_second, block, grad)


def on_device(
    tokens, gains_taps, weights, cotangent, weight_first, weight_second, gains_first, gains_second
):
    layers = lax.axis_size("seq") // 2
    inner_word = (lax.axis_index("seq") % 2).astype(jnp.int32).reshape(1)
    own, oth = halves(weights, inner_word)
    block_out, input_grad, gain_sums, mine, theirs = block_step(
        tokens[0], cotangent[0], gains_taps, own, oth, layers
    )
    (
        weight_grad, weight_first_new, weight_second_new, weight_new,
        gains_grad, gains_first_new, gains_second_new, gains_new, block_out, input_grad,
    ) = update(
        inner_word, mine, theirs, weights, weight_first, weight_second,
        gain_sums, gains_taps, gains_first, gains_second, block_out, input_grad,
    )
    return (
        block_out[None],
        input_grad[None],
        weight_grad,
        weight_first_new,
        weight_second_new,
        weight_new,
        gains_grad,
        gains_first_new,
        gains_second_new,
        gains_new,
    )


def solution(mesh):
    tokens, rows, whole = P("shard", "seq", None), P("seq", "shard"), P()
    return jax.shard_map(
        on_device,
        mesh=mesh,
        in_specs=(tokens, whole, rows, tokens, rows, rows, whole, whole),
        out_specs=(tokens, tokens, rows, rows, rows, rows, whole, whole, whole, whole),
        check_vma=False,
    )
```

```python
import functools

import jax
import jax.numpy as jnp
from jax import lax
from jax.experimental import pallas as pl
from jax.experimental.pallas import tpu as pltpu
from jax.sharding import PartitionSpec as P

D = 1536
FF = 6912
STEP = 10
GROUPS = 4
QUARTER = D // GROUPS
UNITS = FF // GROUPS
HALF_Q = QUARTER // 2
HALF_F = UNITS // 2
LANES = 128
PAD_F = -(-HALF_F // LANES) * LANES
WIDE = 256
CONV_COLS = 4 * HALF_Q
UNIT_CHUNKS = (384, 256, PAD_F - 640)
UNIT_STARTS = (0, 384, 640)
WIDTHS = (CONV_COLS,) + tuple(3 * units for units in UNIT_CHUNKS)
STARTS = tuple(sum(WIDTHS[:k]) for k in range(len(WIDTHS)))
SPLIT = 128
REACH = (1, 1, 1, 1)
SLICE = 384
TILE = 16
ROWS = 48

MOMENT_DECAY = 0.9
SQUARE_DECAY = 0.95
ADAM_EPSILON = 1e-08
NORM_EPSILON = 1e-05
WEIGHT_RATE = 0.02
GAIN_RATE = 0.2
WEIGHT_DECAY = 0.1

BF16 = jnp.bfloat16
F32 = jnp.float32
MESH = pl.DeviceIdType.MESH
VMEM_BYTES = 63 * 1024 * 1024


def place():
    seq, shard = lax.axis_index("seq"), lax.axis_index("shard")
    inner, core = lax.rem(seq, 2), lax.rem(shard, 2)
    return seq, shard, inner, core


def partners():
    seq, shard, inner, core = place()
    across = {"seq": seq + 1 - 2 * inner, "shard": shard}
    beside = {"seq": seq, "shard": lax.rem(shard + 2, 4)}
    twin = {"seq": seq, "shard": shard + 1 - 2 * core}
    return across, beside, twin


def remote(src, dst, send, recv, device):
    return pltpu.make_async_remote_copy(
        src_ref=src, dst_ref=dst, send_sem=send, recv_sem=recv, device_id=device, device_id_type=MESH
    )


def line():
    seq, shard, _, _ = place()
    return seq // 2, lambda steps: {"seq": seq + 2 * steps, "shard": shard}


def greet(layers):
    outer, at = line()
    barrier = pltpu.get_barrier_semaphore()
    for device in partners():
        pl.semaphore_signal(barrier, inc=1, device_id=device, device_id_type=MESH)
    for steps in range(1, layers):
        for sign in (1, -1):

            @pl.when(in_line(outer + sign * steps, layers))
            def _():
                pl.semaphore_signal(barrier, inc=1, device_id=at(sign * steps), device_id_type=MESH)

    pl.semaphore_wait(barrier, 3 + layers - 1)


def in_line(index, layers):
    return (index >= 0) & (index < layers)


def allow(credit):
    for device in partners():
        pl.semaphore_signal(credit, inc=1, device_id=device, device_id_type=MESH)


def dot(left, right):
    return jnp.dot(left, right, preferred_element_type=F32)


def dot_rows(left, right):
    return lax.dot_general(left, right, (((1,), (1,)), ((), ())), preferred_element_type=F32)


def dot_columns(left, right):
    return lax.dot_general(left, right, (((0,), (0,)), ((), ())), preferred_element_type=F32)


def aligned(start, size, multiple=16):
    return pl.ds(pl.multiple_of(start, multiple), size)


class Gather:
    def __init__(self, layers, rows, own, oth, outs, send_x, recv_x, send_z, recv_z, local):
        self.layers, self.rows, self.own, self.oth, self.outs = layers, rows, own, oth, outs
        self.send_x, self.recv_x, self.send_z, self.recv_z, self.local = send_x, recv_x, send_z, recv_z, local
        self.seq, _, self.inner, _ = place()
        self.outer, self.at = line()
        self.across = partners()[0]

    def seq_rows(self, index):
        return aligned(index * self.rows, self.rows)

    def layer_rows(self, direction, distance):
        origin = self.outer - distance if direction == 0 else self.outer + distance
        return aligned(origin * 2 * self.rows, 2 * self.rows)

    def copy(self, k, src, dst, direction, distance, hop, piece):
        slot = (k, direction, distance + hop - 1, piece)
        return remote(
            src, dst, self.send_z.at[slot], self.recv_z.at[slot], self.at(hop if direction == 0 else -hop)
        )

    def goes(self, direction, hop):
        return in_line(self.outer + (hop if direction == 0 else -hop), self.layers)

    def has_come(self, direction, distance):
        return in_line(self.outer + (-distance if direction == 0 else distance), self.layers)

    def hops(self, k, distance):
        return range(1, min(REACH[k], self.layers - 1 - distance) + 1)

    def own_copy(self, k, direction, hop):
        src = self.own.at[:, pl.ds(STARTS[k], WIDTHS[k])]
        return self.copy(k, src, self.outs[k].at[self.seq_rows(self.seq)], direction, 0, hop, 0)

    def other_copy(self, k, direction, hop):
        there = self.outs[k].at[self.seq_rows(self.seq + 1 - 2 * self.inner)]
        return self.copy(k, there, there, direction, 0, hop, 1)

    def pass_copy(self, k, direction, distance, hop):
        ref = self.outs[k].at[self.layer_rows(direction, distance)]
        return self.copy(k, ref, ref, direction, distance, hop, 0)

    def x_copy(self, k):
        return remote(
            self.oth.at[:, pl.ds(STARTS[k], WIDTHS[k])],
            self.outs[k].at[self.seq_rows(self.seq)],
            self.send_x.at[k],
            self.recv_x.at[k],
            self.across,
        )

    def l_copy(self, k):
        return pltpu.make_async_copy(
            self.own.at[:, pl.ds(STARTS[k], WIDTHS[k])], self.outs[k].at[self.seq_rows(self.seq)], self.local.at[k]
        )

    def exchange(self, k):
        self.x_copy(k).start()
        self.l_copy(k).start()

    def send_own(self, k):
        for hop in self.hops(k, 0):
            for direction in (0, 1):

                @pl.when(self.goes(direction, hop))
                def _():
                    self.own_copy(k, direction, hop).start()

    def send_other(self, k):
        self.x_copy(k).wait_recv()
        for hop in self.hops(k, 0):
            for direction in (0, 1):

                @pl.when(self.goes(direction, hop))
                def _():
                    self.other_copy(k, direction, hop).start()

    def step(self, k, distance):
        for direction in (0, 1):

            @pl.when(self.has_come(direction, distance))
            def _():
                if distance <= REACH[k]:
                    origin = self.outer - distance if direction == 0 else self.outer + distance
                    for piece in (0, 1):
                        index = 2 * origin + (self.inner if piece == 0 else 1 - self.inner)
                        ref = self.outs[k].at[self.seq_rows(index)]
                        self.copy(k, ref, ref, direction, distance - 1, 1, piece).wait_recv()
                else:
                    ref = self.outs[k].at[self.layer_rows(direction, distance)]
                    self.copy(k, ref, ref, direction, distance - 1, 1, 0).wait_recv()
                if distance % REACH[k] == 0:
                    for hop in self.hops(k, distance):

                        @pl.when(self.goes(direction, hop))
                        def _():
                            self.pass_copy(k, direction, distance, hop).start()

        if distance == self.layers - 1:
            self.l_copy(k).wait()

    def steps(self, k, first, last=None):
        last = self.layers - 1 if last is None else min(last, self.layers - 1)
        for distance in range(first, last + 1):
            self.step(k, distance)

    def finish(self):
        for k in range(len(self.outs)):
            self.x_copy(k).wait_send()
            for distance in range(0, self.layers - 1, REACH[k]):
                for hop in self.hops(k, distance):
                    for direction in (0, 1):

                        @pl.when(self.goes(direction, hop) & self.has_come(direction, distance))
                        def _():
                            if distance == 0:
                                self.own_copy(k, direction, hop).wait_send()
                                self.other_copy(k, direction, hop).wait_send()
                            else:
                                self.pass_copy(k, direction, distance, hop).wait_send()


class Reduce:
    def __init__(self, layers, rows, grads, slots, stage, spare, total, outgoing, mine, theirs, sems):
        self.layers, self.rows, self.grads, self.slots = layers, rows, grads, slots
        self.stage, self.spare, self.total, self.outgoing = stage, spare, total, outgoing
        self.mine, self.theirs = mine, theirs
        self.send_g, self.recv_g, self.fetched, self.fetches, self.stored, self.send_o, self.recv_o = sems
        _, _, self.inner, _ = place()
        self.outer, self.at = line()
        self.across = partners()[0]

    def owner(self, direction, distance):
        return self.outer + distance if direction == 0 else self.outer - distance

    def upstream(self, direction, steps):
        return in_line(self.outer - steps if direction == 0 else self.outer + steps, self.layers)

    def block(self, k, owner):
        return self.grads[k].at[aligned(owner * 2 * self.rows, 2 * self.rows), pl.ds(0, WIDTHS[k])]

    def copy(self, k, src, direction, distance):
        hop = 1 if distance % 2 else 2
        slot = (direction, distance - 1)
        return remote(
            src,
            self.slots[k].at[slot],
            self.send_g.at[(k,) + slot],
            self.recv_g.at[(k,) + slot],
            self.at(hop if direction == 0 else -hop),
        )

    def send(self, k, direction, distance):
        self.copy(k, self.block(k, self.owner(direction, distance)), direction, distance).start()

    def direct(self, k, part=None, ends=None):
        at_end = (self.outer == 0) | (self.outer == self.layers - 1)
        for distance in range(self.layers - 1, 0, -1):
            for direction in (0, 1):
                owner = self.owner(direction, distance)
                here = in_line(owner, self.layers)
                if part is not None:
                    here = here & (owner * 2 * self.rows // SLICE == part)
                if ends is not None:
                    here = here & (at_end if ends else jnp.logical_not(at_end))
                if distance % 2 == 0:
                    here = here & jnp.logical_not(self.upstream(direction, 1))

                @pl.when(here)
                def _():
                    self.send(k, direction, distance)

    def fetch(self, k, direction, distance):
        slot = self.slots[k].at[direction, distance - 1]
        self.copy(k, slot, direction, distance).wait_recv()
        held = self.stage.at[:, pl.ds(0, WIDTHS[k])]
        copy = pltpu.make_async_copy(slot, held, self.fetched)
        copy.start()
        copy.wait()

    def tiles(self, body):
        def step(n, _):
            body(aligned(n * TILE, TILE))
            return 0

        lax.fori_loop(0, 2 * self.rows // TILE, step, 0)

    def join(self, k):
        cols = pl.ds(0, WIDTHS[k])
        for distance in range((self.layers - 1) // 2 * 2, 0, -2):
            for direction in (0, 1):
                owner = self.owner(direction, distance)

                @pl.when(in_line(owner, self.layers) & self.upstream(direction, 1))
                def _():
                    def add(tile):
                        base = self.owner(direction, distance) * 2 * self.rows
                        rows = pl.ds(pl.multiple_of(base + tile.start, 16), TILE)
                        ref = self.grads[k]
                        ref[rows, cols] = (
                            ref[rows, cols].astype(F32) + self.stage[tile, cols].astype(F32)
                        ).astype(BF16)

                    self.fetch(k, direction, distance + 1)
                    self.tiles(add)
                    if distance + 2 < self.layers:

                        @pl.when(self.upstream(direction, 2))
                        def _():
                            self.fetch(k, direction, distance + 2)
                            self.tiles(add)

                    self.send(k, direction, distance)

    def final(self, k, before=None):
        cols = pl.ds(0, WIDTHS[k])
        came = [(distance, direction) for distance in (1, 2) for direction in (0, 1) if distance < self.layers]

        def fetch(n, distance, direction):
            return pltpu.make_async_copy(
                self.slots[k].at[direction, distance - 1],
                self.spare.at[pl.ds(n * 2 * self.rows, 2 * self.rows), cols],
                self.fetches.at[n],
            )

        for n, (distance, direction) in enumerate(came):

            @pl.when(self.upstream(direction, distance))
            def _():
                self.copy(k, self.slots[k].at[direction, distance - 1], direction, distance).wait_recv()
                fetch(n, distance, direction).start()

        if before is not None:
            self.store(before).wait()

        here, there = self.inner * self.rows, (1 - self.inner) * self.rows

        def each(base, body):
            def step(n, _):
                body(base + n * TILE, n * TILE)
                return 0

            lax.fori_loop(0, self.rows // TILE, step, 0)

        for n, (distance, direction) in enumerate(came):

            @pl.when(self.upstream(direction, distance))
            def _():
                fetch(n, distance, direction).wait()

        def add_up(flags):
            def total(rows):
                value = self.grads[k][aligned(self.outer * 2 * self.rows + rows, TILE), cols].astype(F32)
                for n, flag in enumerate(flags):
                    if flag:
                        value = value + self.spare[aligned(n * 2 * self.rows + rows, TILE), cols].astype(F32)
                return value

            def send(rows, at):
                self.outgoing[aligned(at, TILE), pl.ds(STARTS[k], WIDTHS[k])] = total(rows).astype(BF16)

            def keep(rows, at):
                self.total[aligned(at, TILE), cols] = total(rows)

            each(there, send)
            self.over(k).start()
            each(here, keep)
            self.store(k).start()

        patterns = {}
        for place_in_line in range(self.layers):
            flags = tuple(
                0 <= (place_in_line - distance if direction == 0 else place_in_line + distance) < self.layers
                for distance, direction in came
            )
            patterns.setdefault(flags, []).append(place_in_line)
        for flags, places in patterns.items():
            here_now = functools.reduce(jnp.logical_or, [self.outer == p for p in places])

            @pl.when(here_now)
            def _():
                add_up(flags)

    def over(self, k):
        wide = pl.ds(STARTS[k], WIDTHS[k])
        return remote(
            self.outgoing.at[:, wide], self.theirs.at[:, wide], self.send_o.at[k], self.recv_o.at[k], self.across
        )

    def store(self, k):
        return pltpu.make_async_copy(
            self.total.at[:, pl.ds(0, WIDTHS[k])], self.mine.at[:, pl.ds(STARTS[k], WIDTHS[k])], self.stored.at[k]
        )

    def wait_sent(self, k):
        for distance in range(1, self.layers):
            for direction in (0, 1):
                owner = self.owner(direction, distance)

                @pl.when(in_line(owner, self.layers))
                def _():
                    self.copy(k, self.block(k, owner), direction, distance).wait_send()

    def finish(self, before):
        self.store(before).wait()
        for k in range(len(self.grads)):
            self.over(k).wait()


class Spread:
    def __init__(self, buf, seg, split, send, recv):
        self.buf, self.seg, self.split, self.send, self.recv = buf, seg, split, send, recv
        self.both = split < seg

    def index(self, n):
        _, shard, inner, core = place()
        row, flip, other = (n // 2) % 2, n // 4, n % 2
        return 2 * (lax.rem(shard + 2 * row, 4) + other * (1 - 2 * core)) + inner + flip * (1 - 2 * inner)

    def copy(self, slot):
        across, beside, twin = partners()
        low, high, whole = (0, self.split), (self.split, self.seg - self.split), (0, self.seg)
        n, (first, size), device = {
            0: (0, whole, across),
            1: (0, whole, beside),
            2: (0, whole, twin),
            3: (4, low, beside),
            4: (4, whole, twin),
            5: (2, high, across),
            6: (2, whole, twin),
            7: (6, low, twin),
            8: (6, high, twin),
        }[slot]
        ref = self.buf.at[aligned(self.index(n) * self.seg + first, size)]
        return remote(ref, ref, self.send.at[slot], self.recv.at[slot], device)

    def push(self, *slots):
        for slot in slots:
            if self.both or slot not in (5, 8):
                self.copy(slot).start()

    def came(self, *slots):
        for slot in slots:
            if self.both or slot not in (5, 8):
                self.copy(slot).wait_recv()

    def start(self):
        self.push(0, 1, 2)

    def near(self):
        self.came(1)
        self.push(5, 6)
        self.came(0)
        self.push(3, 4)

    def far(self):
        self.came(3)
        self.push(7)
        self.came(5)
        self.push(8)

    def end(self, *came):
        self.came(*came)
        for slot in range(9):
            if self.both or slot not in (5, 8):
                self.copy(slot).wait_send()

    def run(self, body, hooks):
        waits = {
            1: lambda: self.came(2),
            2: self.near,
            3: lambda: self.came(6),
            5: lambda: self.came(4),
            6: self.far,
            7: lambda: self.came(7, 8),
        }

        def step(n, _):
            for m in range(8):
                acts = [a[m] for a in (hooks, waits) if m in a]
                if acts:

                    @pl.when(n == m)
                    def _():
                        for act in acts:
                            act()

            body(self.index(n))
            return 0

        lax.fori_loop(0, 8, step, 0)
        self.end()


def collect_steps(part, seg, total, pair, near, joined, send, recv, produce=None):
    _, shard, inner, core = place()
    across, beside, twin = partners()
    low, high, whole = (0, SPLIT), (SPLIT, seg - SPLIT), (0, seg)
    twin_shard = shard + 1 - 2 * core
    cols = pl.ds(0, D)

    def index(s, k):
        row, flip = 1 - k % 2, 1 - k // 2
        return 2 * lax.rem(s + 2 * row, 4) + inner + flip * (1 - 2 * inner)

    def pair_copy(k):
        src = part.at[aligned(index(twin_shard, k) * seg, seg), cols]
        return remote(src, pair.at[k], send.at[k], recv.at[k], twin)

    def copy(slot):
        src, dst, (first, size), device = {
            4: (pair.at[0], joined, low, across),
            5: (pair.at[0], joined, high, beside),
            6: (pair.at[1], near.at[0], low, across),
            7: (pair.at[2], near.at[1], high, beside),
            8: (pair.at[2], near.at[1], low, beside),
            9: (pair.at[1], near.at[0], high, across),
        }[slot]
        rows = pl.ds(first, size)
        return remote(src.at[rows], dst.at[rows], send.at[slot], recv.at[slot], device)

    def over(span, body):
        def step(n, _):
            body(aligned(span[0] + n * 16, 16))
            return 0

        lax.fori_loop(0, span[1] // 16, step, 0)

    def add_pair(k):
        def add(rows):
            mine = part[aligned(index(shard, k) * seg + rows.start, 16), cols].astype(F32)
            pair[k, rows] = (mine + pair[k, rows].astype(F32)).astype(BF16)

        pair_copy(k).wait_recv()
        over(whole, add)

    def add_own():
        def add(rows):
            mine = part[aligned(index(shard, 3) * seg + rows.start, 16), cols].astype(F32)
            total[rows] = mine + pair[3, rows].astype(F32)

        pair_copy(3).wait_recv()
        over(whole, add)

    def pass_on(slot, k, span, after):
        def add(rows):
            pair[k, rows] = (pair[k, rows].astype(F32) + joined[rows].astype(F32)).astype(BF16)

        copy(slot).wait_recv()
        over(span, add)
        copy(after).start()

    def after_pair(k):
        add_pair(k)
        if k == 0:
            copy(4).start()
            copy(5).start()
        elif k == 1:
            copy(6).start()
        else:
            copy(7).start()
            pass_on(4, 2, low, 8)
            pass_on(5, 1, high, 9)

    def half(base):
        def step(n, _):
            k, own = base + n // 2, n % 2
            produce(index(jnp.where(own == 1, shard, twin_shard), k))

            @pl.when(own == 0)
            def _():
                pair_copy(k).start()

            for m in (base, base + 1):

                @pl.when((own == 1) & (k == m))
                def _():
                    if m < 3:
                        after_pair(m)
                    else:
                        add_own()

            return 0

        lax.fori_loop(0, 4, step, 0)

    if produce is None:
        for k in range(4):
            pair_copy(k).start()
        yield
        after_pair(0)
        after_pair(1)
        yield
        after_pair(2)
        add_own()
    else:
        half(0)
        yield
        half(2)
    yield

    def add_near(span):
        def add(rows):
            total[rows] = total[rows] + near[0, rows].astype(F32) + near[1, rows].astype(F32)

        over(span, add)

    copy(6).wait_recv()
    copy(8).wait_recv()
    add_near(low)
    copy(7).wait_recv()
    copy(9).wait_recv()
    add_near(high)
    for k in range(4):
        pair_copy(k).wait_send()
    for slot in range(4, 10):
        copy(slot).wait_send()


def drain(steps):
    for _ in steps:
        pass


def norm_scale(values):
    return lax.rsqrt(jnp.mean(values * values, axis=-1, keepdims=True) + NORM_EPSILON)


def by_rows(rows, body, carry=0):
    def step(n, carry):
        return body(aligned(n * ROWS, ROWS), carry)

    return lax.fori_loop(0, rows // ROWS, step, carry)


def norm_back(values, gain, upstream):
    scale = norm_scale(values)
    scaled = gain * upstream
    inner = jnp.mean(scaled * values, axis=-1, keepdims=True)
    return (
        scale * scaled - values * scale * scale * scale * inner,
        jnp.sum(upstream * values * scale, axis=0, keepdims=True),
    )


REFS = (
    "tok", "cot", "gains", "own", "oth",
    "block_out", "input_grad", "gain_sums", "mine", "theirs", "n1_held", "slot0", "slot1", "slot2", "slot3",
    "w0", "w1", "w2", "w3", "seq_a", "seq_b", "du", "act", "c_all", "gated", "mixed", "resid", "dresid", "total",
    "pair", "near", "joined", "g1", "g2", "g3", "stage", "sum", "outgoing", "gain_in", "gain_line",
    "held", "local", "send_x", "recv_x", "send_z", "recv_z", "send_s", "recv_s", "send_c", "recv_c", "credit",
    "halo_send", "halo_recv", "send_g", "recv_g", "fetched", "fetches", "stored", "send_o", "recv_o",
    "send_a", "recv_a", "send_l", "recv_l",
)


def block_kernel(layers, rows, *all_refs):
    r = dict(zip(REFS, all_refs, strict=True))
    tok, cot, gains = r["tok"], r["cot"], r["gains"]
    seq_a, seq_b, du, act = r["seq_a"], r["seq_b"], r["du"], r["act"]
    c_all, gated, mixed, total = r["c_all"], r["gated"], r["mixed"], r["total"]
    weights = (r["w0"], r["w1"], r["w2"], r["w3"])
    seg = tok.shape[0]
    _, shard, inner, _ = place()
    outer, at = line()
    me = 2 * shard + inner
    my_rows = aligned(me * seg, seg)
    chunks = list(zip(range(1, 1 + len(UNIT_CHUNKS)), UNIT_STARTS, UNIT_CHUNKS))
    gather = Gather(
        layers, rows, r["own"], r["oth"], weights,
        r["send_x"], r["recv_x"], r["send_z"], r["recv_z"], r["local"],
    )
    reduce = Reduce(
        layers, rows, (r["w2"], r["g1"], r["g2"], r["g3"]), (r["slot0"], r["slot1"], r["slot2"], r["slot3"]),
        r["stage"], r["w1"], r["sum"], r["outgoing"], r["mine"], r["theirs"],
        (r["send_g"], r["recv_g"], r["fetched"], r["fetches"], r["stored"], r["send_o"], r["recv_o"]),
    )

    def spread(buf, n, split=SPLIT):
        return Spread(buf, seg, split, r["send_s"].at[n], r["recv_s"].at[n])

    def collect(part, n, produce=None):
        return collect_steps(
            part, seg, total, r["pair"], r["near"], r["joined"], r["send_c"].at[n], r["recv_c"].at[n], produce
        )

    def block(t):
        return aligned(t * seg, seg)

    lanes = lax.broadcasted_iota(jnp.int32, (seg, WIDE), 1) < HALF_Q
    taps = pltpu.roll(gains[...], lax.rem(D - shard * QUARTER - inner * HALF_Q, D), 1)[2:5, :WIDE]

    greet(layers)
    gather.exchange(0)
    gather.send_own(0)

    def mine(part):
        return pl.ds(pl.multiple_of(me * seg + part.start, 16), part.size)

    def first_norm(part, _):
        values = tok[part].astype(F32)
        seq_a[mine(part)] = (values * norm_scale(values) * gains[0:1, :]).astype(BF16)
        return 0

    by_rows(seg, first_norm)
    one = spread(seq_a, 0)
    one.start()
    seq_b[my_rows] = cot[...]
    gather.send_other(0)
    gather.steps(0, 1, 1)
    one.near()
    gather.exchange(1)
    gather.steps(0, 2, 2)
    gather.send_own(1)
    one.far()
    one.end(2, 4, 6, 7, 8)
    held = pltpu.make_async_copy(seq_a, r["n1_held"], r["held"])
    held.start()
    up = spread(seq_b, 1, seg)
    up.start()
    gather.steps(0, 3)

    def project(s, _):
        for i in (0, 1):
            parts = dot(seq_a[block(2 * s + i)], weights[0][...])
            b = jnp.where(lanes, parts[:, :WIDE], 0.0)
            c = pltpu.roll(parts[:, 128 : 128 + 384], 384 - 64, 1)[:, :WIDE]
            x = parts[:, 384 : 384 + WIDE]
            c_all[s, pl.ds(i * seg, seg)] = jnp.where(lanes, c, 0.0)
            gated[s, pl.ds(8 + i * seg, seg)] = (b * x).astype(BF16).astype(F32)
        return 0

    lax.fori_loop(0, GROUPS, project, 0)
    ahead = remote(
        gated.at[:, pl.ds(2 * seg, 8)], gated.at[:, pl.ds(0, 8)], r["halo_send"].at[0], r["halo_recv"].at[0], at(1)
    )

    @pl.when(outer < layers - 1)
    def _():
        ahead.start()

    @pl.when(outer == 0)
    def _():
        gated[:, pl.ds(0, 8)] = jnp.zeros((GROUPS, 8, WIDE), F32)

    gather.send_other(1)
    up.near()
    gather.exchange(2)
    gather.send_own(2)
    held.wait()

    @pl.when(outer > 0)
    def _():
        ahead.wait_recv()

    def convolved(s, i):
        return (
            taps[0:1, :] * gated[s, pl.ds(6 + i * seg, seg)]
            + taps[1:2, :] * gated[s, pl.ds(7 + i * seg, seg)]
            + taps[2:3, :] * gated[s, pl.ds(8 + i * seg, seg)]
        )

    def convolve(t):
        for i in (0, 1):

            @pl.when(t % 2 == i)
            def _():
                s = t // 2
                mixed[block(t)] = pltpu.roll(c_all[s, pl.ds(i * seg, seg)] * convolved(s, i), 64, 1).astype(BF16)

        seq_a[block(t)] = dot_rows(mixed[block(t)], weights[0][:, pl.ds(512, WIDE)]).astype(BF16)

    branch = collect(seq_a, 0, convolve)
    next(branch)
    gather.exchange(3)
    gather.steps(1, 1, 1)
    gather.send_other(2)
    next(branch)
    up.far()
    gather.steps(1, 2, 2)
    drain(branch)
    allow(r["credit"].at[0])

    def second_norm(part, _):
        values = tok[part].astype(F32) + total[part]
        r["resid"][part] = values
        seq_a[mine(part)] = (values * norm_scale(values) * gains[1:2, :]).astype(BF16)
        return 0

    by_rows(seg, second_norm)
    gather.send_own(3)
    gather.send_other(3)
    pl.semaphore_wait(r["credit"].at[0], 3)
    two = spread(seq_a, 2)
    two.start()
    up.end(2, 4, 6, 7, 8)

    def hidden(k, start, units, t):
        ref, here = weights[k], block(t)
        gate = dot(seq_a[here], ref[:, pl.ds(0, units)])
        upval = dot(seq_a[here], ref[:, pl.ds(units, units)])
        dact = dot(seq_b[here], ref[:, pl.ds(2 * units, units)])
        sigma = jax.nn.sigmoid(gate)
        silu = gate * sigma
        act[here, pl.ds(start, units)] = (silu * upval).astype(BF16)
        dgate = dact * upval * sigma * (1.0 + gate * (1.0 - sigma))
        du[here, pl.ds(2 * start, units)] = dgate.astype(BF16)
        du[here, pl.ds(2 * start + units, units)] = (dact * silu).astype(BF16)

    def each_block(body):
        def step(t, _):
            body(t)
            return 0

        lax.fori_loop(0, 2 * GROUPS, step, 0)

    def slices(body):
        def step(n, _):
            body(jnp.where(outer < layers // 2, D // SLICE - 1 - n, n))
            return 0

        lax.fori_loop(0, D // SLICE, step, 0)

    def gate_up_grads(k, start, units, part):
        held_rows = aligned(part * SLICE, SLICE)
        left = seq_a[:, aligned(part * SLICE, SLICE, 128)]
        for m in (0, 1):
            reduce.grads[k][held_rows, pl.ds(m * units, units)] = dot_columns(
                left, du[:, pl.ds(2 * start + m * units, units)]
            ).astype(BF16)

    def down_grads(k, start, units, part):
        held_rows = aligned(part * SLICE, SLICE)
        left = seq_b[:, aligned(part * SLICE, SLICE, 128)]
        reduce.grads[k][held_rows, pl.ds(2 * units, units)] = dot_columns(
            left, act[:, pl.ds(start, units)]
        ).astype(BF16)

    two.run(
        functools.partial(hidden, *chunks[0]),
        {0: lambda: gather.steps(1, 3), 3: lambda: gather.steps(2, 1, 1), 7: lambda: gather.steps(2, 2, 2)},
    )
    gather.steps(3, 1, 1)
    def grads(k, start, units, part):
        gate_up_grads(k, start, units, part)
        down_grads(k, start, units, part)
        reduce.direct(k, part, ends=True)

    slices(functools.partial(grads, *chunks[0]))
    gather.steps(2, 3)
    each_block(functools.partial(hidden, *chunks[1]))
    gather.steps(3, 2, 2)
    slices(functools.partial(grads, *chunks[1]))
    gather.steps(3, 3)
    reduce.direct(1, ends=False)
    reduce.direct(2, ends=False)
    each_block(functools.partial(hidden, *chunks[2]))
    slices(functools.partial(down_grads, *chunks[2]))
    gather.finish()

    def second(t):
        here = block(t)
        seq_b[here] = sum(
            dot_rows(du[here, pl.ds(2 * start, 2 * units)], weights[k][:, pl.ds(0, 2 * units)])
            for k, start, units in chunks
        ).astype(BF16)

    down = collect(seq_b, 1, second)
    next(down)
    next(down)
    reduce.join(1)

    slices(functools.partial(gate_up_grads, *chunks[2]))

    def forward(t):
        here = block(t)
        du[here, pl.ds(0, D)] = sum(
            dot_rows(act[here, pl.ds(start, units)], weights[k][:, pl.ds(2 * units, units)])
            for k, start, units in chunks
        ).astype(BF16)

    drain(down)
    reload = pltpu.make_async_copy(r["n1_held"], seq_b, r["held"])
    reload.start()
    allow(r["credit"].at[1])

    def second_back(part, gain):
        dpart, dgain = norm_back(r["resid"][part], gains[1:2, :], total[part])
        dresid = cot[part].astype(F32) + dpart
        r["dresid"][part] = dresid
        seq_a[mine(part)] = dresid.astype(BF16)
        return gain + dgain

    gain_two = by_rows(seg, second_back, jnp.zeros((1, D), F32))
    pl.semaphore_wait(r["credit"].at[1], 3)
    three = spread(seq_a, 3)
    three.start()

    kept = pl.ds(D, WIDE)

    def mix_back(t):
        s, here = t // 2, block(t)
        dmixed = pltpu.roll(dot(seq_a[here], weights[0][:, pl.ds(512, WIDE)]), WIDE - 64, 1)
        dmixed = jnp.where(lanes, dmixed, 0.0)
        for i in (0, 1):

            @pl.when(t % 2 == i)
            def _():
                du[here, kept] = (dmixed * convolved(s, i)).astype(BF16)
                c_all[s, pl.ds(i * seg, seg)] = dmixed * c_all[s, pl.ds(i * seg, seg)]

    three.run(
        mix_back, {1: lambda: each_block(forward), 3: lambda: reduce.final(1), 6: lambda: reduce.join(2)}
    )
    after = remote(
        c_all.at[:, pl.ds(0, 8)], c_all.at[:, pl.ds(2 * seg, 8)], r["halo_send"].at[1], r["halo_recv"].at[1], at(-1)
    )

    @pl.when(outer > 0)
    def _():
        after.start()

    @pl.when(outer == layers - 1)
    def _():
        c_all[:, pl.ds(2 * seg, 8)] = jnp.zeros((GROUPS, 8, WIDE), F32)

    reduce.direct(3)
    feed = collect(du, 2)
    next(feed)
    next(feed)
    reload.wait()

    @pl.when(outer < layers - 1)
    def _():
        after.wait_recv()

    def conv_back(s, sums):
        for i in (0, 1):
            t = block(2 * s + i)
            dconv = c_all[s, pl.ds(i * seg, seg)]
            dgated = (
                taps[2:3, :] * dconv
                + taps[1:2, :] * c_all[s, pl.ds(1 + i * seg, seg)]
                + taps[0:1, :] * c_all[s, pl.ds(2 + i * seg, seg)]
            )
            parts = dot(seq_b[t], weights[0][:, pl.ds(0, 640)])
            db = dgated * parts[:, 384:640]
            dx = dgated * parts[:, :WIDE]
            dc = jnp.concatenate([du[t, kept].astype(F32), jnp.zeros((seg, 128), F32)], axis=1)
            dc = pltpu.roll(dc, 64, 1)
            act[t, pl.ds(0, 128)] = db[:, :128].astype(BF16)
            act[t, pl.ds(128, 128)] = (db[:, 128:] + dc[:, :128]).astype(BF16)
            act[t, pl.ds(256, 128)] = dc[:, 128:256].astype(BF16)
            act[t, pl.ds(384, WIDE)] = dx.astype(BF16)
            act[t, pl.ds(640, 128)] = jnp.zeros((seg, 128), BF16)
            sums = sums + jnp.concatenate(
                [
                    jnp.sum(dconv * gated[s, pl.ds(6 + k + i * seg, seg)], axis=0, keepdims=True)
                    for k in range(3)
                ]
                + [jnp.zeros((5, WIDE), F32)],
                axis=0,
            )
        return sums

    tap_sums = lax.fori_loop(0, GROUPS, conv_back, jnp.zeros((8, WIDE), F32))
    next(feed)

    def conv_grads(part):
        held_rows, cols = aligned(part * SLICE, SLICE), aligned(part * SLICE, SLICE, 128)
        ref = reduce.grads[0]
        ref[held_rows, pl.ds(0, 512)] = dot_columns(seq_b[:, cols], act[:, pl.ds(0, 512)]).astype(BF16)
        ref[held_rows, pl.ds(512, WIDE)] = (
            dot_columns(seq_b[:, cols], act[:, pl.ds(512, WIDE)]) + dot_columns(seq_a[:, cols], mixed[...])
        ).astype(BF16)
        reduce.direct(0, part)

    slices(conv_grads)
    reduce.join(3)
    drain(feed)
    allow(r["credit"].at[2])
    r["block_out"][...] = (r["resid"][...] + total[...]).astype(BF16)
    pl.semaphore_wait(r["credit"].at[2], 3)

    def first(t):
        here = block(t)
        seq_a[here] = dot_rows(act[here, pl.ds(0, 640)], weights[0][:, pl.ds(0, 640)]).astype(BF16)

    inputs = collect(seq_a, 3, first)
    next(inputs)
    reduce.final(2, 1)
    next(inputs)
    reduce.join(0)
    reduce.final(3, 2)
    drain(inputs)

    def first_back(part, gain):
        dpart, dgain = norm_back(tok[part].astype(F32), gains[0:1, :], total[part])
        r["input_grad"][part] = (r["dresid"][part] + dpart).astype(BF16)
        return gain + dgain

    gain_one = by_rows(seg, first_back, jnp.zeros((1, D), F32))

    sums = r["gain_sums"]
    sums[...] = jnp.zeros(sums.shape, F32)
    sums[0:1, pl.ds(0, D)] = gain_one
    sums[1:2, pl.ds(0, D)] = gain_two
    sums[2:5, aligned(me * WIDE, WIDE, 128)] = tap_sums[0:3]
    for n, device in enumerate(partners()):
        copy = remote(sums, r["gain_in"].at[n], r["send_a"].at[n], r["recv_a"].at[n], device)
        copy.start()
        copy.wait()
        sums[...] = sums[...] + r["gain_in"][n]

    def line_copy(sign, steps):
        slot = (0 if sign > 0 else 1, steps - 1)
        return remote(
            sums, r["gain_line"].at[slot], r["send_l"].at[slot], r["recv_l"].at[slot], at(sign * steps)
        )

    for steps in range(1, layers):
        for sign in (1, -1):

            @pl.when(in_line(outer + sign * steps, layers))
            def _():
                line_copy(sign, steps).start()

    reduce.final(0, 3)
    for steps in range(1, layers):
        for sign in (1, -1):

            @pl.when(in_line(outer + sign * steps, layers))
            def _():
                line_copy(sign, steps).wait_send()

            @pl.when(in_line(outer - sign * steps, layers))
            def _():
                line_copy(sign, steps).wait_recv()

    own_sums = sums[...]
    for origin in range(layers):
        for steps in range(1, layers):
            for sign in (1, -1):

                @pl.when((outer - sign * steps == origin))
                def _():
                    came = r["gain_line"][0 if sign > 0 else 1, steps - 1]
                    sums[...] = came if origin == 0 else sums[...] + came

        if origin > 0:

            @pl.when(outer == origin)
            def _():
                sums[...] = sums[...] + own_sums

    reduce.finish(0)
    for k in range(len(WIDTHS)):
        reduce.wait_sent(k)

    @pl.when(outer < layers - 1)
    def _():
        ahead.wait_send()

    @pl.when(outer > 0)
    def _():
        after.wait_send()


def block_step(tok, cot, gains, own, oth, layers):
    rows, seg = own.shape[0], tok.shape[0]
    count = len(WIDTHS)
    tokens = 2 * GROUPS * seg
    vmem, anywhere = pl.BlockSpec(memory_space=pltpu.VMEM), pl.BlockSpec(memory_space=pl.ANY)
    shape, scratch = jax.ShapeDtypeStruct, pltpu.VMEM
    dma, regular = pltpu.SemaphoreType.DMA, pltpu.SemaphoreType.REGULAR
    hops = layers - 1
    wide, biggest = sum(WIDTHS), max(WIDTHS)
    out_shape = [
        shape((seg, D), BF16),
        shape((seg, D), BF16),
        shape((8, 2 * GROUPS * WIDE), F32),
        shape((rows, wide), F32),
        shape((rows, wide), BF16),
        shape((tokens, D), BF16),
    ] + [shape((2, hops, 2 * rows, width), BF16) for width in WIDTHS]
    scratch_shapes = (
        [scratch((D, width), BF16) for width in WIDTHS]
        + [
            scratch((tokens, D), BF16),
            scratch((tokens, D), BF16),
            scratch((tokens, 2 * PAD_F), BF16),
            scratch((tokens, PAD_F), BF16),
            scratch((GROUPS, 8 + 2 * seg, WIDE), F32),
            scratch((GROUPS, 8 + 2 * seg, WIDE), F32),
            scratch((tokens, WIDE), BF16),
            scratch((seg, D), F32),
            scratch((seg, D), F32),
            scratch((seg, D), F32),
            scratch((4, seg, D), BF16),
            scratch((2, seg, D), BF16),
            scratch((seg, D), BF16),
        ]
        + [scratch((D, width), BF16) for width in WIDTHS[1:]]
        + [
            scratch((2 * rows, biggest), BF16),
            scratch((rows, biggest), F32),
            scratch((rows, wide), BF16),
            scratch((3, 8, 2 * GROUPS * WIDE), F32),
            scratch((2, hops, 8, 2 * GROUPS * WIDE), F32),
            dma,
            dma((count,)),
            dma((count,)),
            dma((count,)),
            dma((count, 2, hops, 2)),
            dma((count, 2, hops, 2)),
            dma((4, 9)),
            dma((4, 9)),
            dma((4, 10)),
            dma((4, 10)),
            regular((3,)),
            dma((2,)),
            dma((2,)),
            dma((count, 2, hops)),
            dma((count, 2, hops)),
            dma,
            dma((4,)),
            dma((count,)),
            dma((count,)),
            dma((count,)),
            dma((3,)),
            dma((3,)),
            dma((2, hops)),
            dma((2, hops)),
        ]
    )
    return pl.pallas_call(
        functools.partial(block_kernel, layers, rows),
        out_shape=out_shape,
        in_specs=[vmem] * 3 + [anywhere] * 2,
        out_specs=[vmem] * 3 + [anywhere] * (3 + count),
        scratch_shapes=scratch_shapes,
        compiler_params=pltpu.CompilerParams(
            collective_id=0, has_side_effects=True, vmem_limit_bytes=VMEM_BYTES
        ),
        name="block_step",
    )(tok, cot, gains, own, oth)[:5]


def column_pieces(half):
    pieces = [(m * QUARTER + half * HALF_Q, m * HALF_Q, HALF_Q, 0) for m in range(4)]
    for k, (start, units) in enumerate(zip(UNIT_STARTS, UNIT_CHUNKS), 1):
        real = min(units, HALF_F - start)
        for m in range(3):
            first = 4 * QUARTER + m * UNITS + half * HALF_F + start
            pieces.append((first, STARTS[k] + m * units, real, units - real))
    return pieces


def halves_kernel(inner_ref, weights_ref, own_ref, oth_ref):
    is_low = inner_ref[0] == 0

    def half(h):
        parts = []
        for first, _, width, padding in column_pieces(h):
            parts.append(weights_ref[:, first : first + width])
            if padding:
                parts.append(jnp.zeros((parts[-1].shape[0], padding), F32))
        return jnp.concatenate(parts, axis=1)

    low, high = half(0), half(1)
    own_ref[...] = jnp.where(is_low, low, high).astype(BF16)
    oth_ref[...] = jnp.where(is_low, high, low).astype(BF16)


def band(rows, most):
    return max(size for size in range(16, most + 1, 16) if rows % size == 0)


def halves(weights, inner):
    rows, cols = weights.shape
    wide = sum(WIDTHS)
    size = band(rows, 96)
    by_row = lambda width: pl.BlockSpec((size, width), lambda n: (n, 0))
    return pl.pallas_call(
        halves_kernel,
        grid=(rows // size,),
        out_shape=[jax.ShapeDtypeStruct((rows, wide), BF16)] * 2,
        in_specs=[pl.BlockSpec(memory_space=pltpu.SMEM), by_row(cols)],
        out_specs=[by_row(wide)] * 2,
        compiler_params=pltpu.CompilerParams(vmem_limit_bytes=VMEM_BYTES),
        name="halves",
    )(inner, weights)


def adam_update(param, grad, first, second, rate, decay):
    first_new = MOMENT_DECAY * first + (1.0 - MOMENT_DECAY) * grad
    second_new = SQUARE_DECAY * second + (1.0 - SQUARE_DECAY) * grad * grad
    first_hat = first_new / (1.0 - MOMENT_DECAY**STEP)
    second_hat = second_new / (1.0 - SQUARE_DECAY**STEP)
    param_new = param - rate * (first_hat / (jnp.sqrt(second_hat) + ADAM_EPSILON) + decay * param)
    return (first_new, second_new, param_new)


def update_kernel(
    inner_ref, mine_ref, theirs_ref, weights_ref, first_ref, second_ref, sums_ref, gains_ref, gains_first_ref,
    gains_second_ref, block_ref, input_ref, grad_out, first_out, second_out, weights_out, gains_grad_out,
    gains_first_out, gains_second_out, gains_out, block_out, input_out,
):
    is_low = inner_ref[0] == 0
    mine, theirs = mine_ref[...], theirs_ref[...].astype(F32)
    for half in (0, 1):
        chosen = jnp.where(is_low, mine, theirs) if half == 0 else jnp.where(is_low, theirs, mine)
        for first, own, width, _ in column_pieces(half):
            grad_out[:, first : first + width] = chosen[:, own : own + width]
    first_out[...], second_out[...], weights_out[...] = adam_update(
        weights_ref[...], grad_out[...], first_ref[...], second_ref[...], WEIGHT_RATE, WEIGHT_DECAY
    )

    @pl.when(pl.program_id(0) == 0)
    def _():
        gains_grad_out[0:2] = sums_ref[0:2, :D]
        for n in range(2 * GROUPS):
            gains_grad_out[2:5, n * HALF_Q : (n + 1) * HALF_Q] = sums_ref[2:5, n * WIDE : n * WIDE + HALF_Q]
        gains_first_out[...], gains_second_out[...], gains_out[...] = adam_update(
            gains_ref[...], gains_grad_out[...], gains_first_ref[...], gains_second_ref[...], GAIN_RATE, 0.0
        )
        block_out[...] = block_ref[...]
        input_out[...] = input_ref[...]


def update(inner, mine, theirs, weights, first, second, sums, gains, gains_first, gains_second, block, grad):
    rows, cols = weights.shape
    wide = mine.shape[1]
    size = band(rows, 32)
    by_row = lambda width: pl.BlockSpec((size, width), lambda n: (n, 0))
    whole = lambda values: pl.BlockSpec(values.shape, lambda n: (0, 0))
    shape = jax.ShapeDtypeStruct
    return pl.pallas_call(
        update_kernel,
        grid=(rows // size,),
        out_shape=[shape((rows, cols), F32)] * 4 + [shape(gains.shape, F32)] * 4 + [shape(block.shape, BF16)] * 2,
        in_specs=[pl.BlockSpec(memory_space=pltpu.SMEM)]
        + [by_row(wide)] * 2
        + [by_row(cols)] * 3
        + [whole(sums)]
        + [whole(gains)] * 3
        + [whole(block)] * 2,
        out_specs=[by_row(cols)] * 4 + [whole(gains)] * 4 + [whole(block)] * 2,
        compiler_params=pltpu.CompilerParams(vmem_limit_bytes=VMEM_BYTES),
        name="update",
    )(inner, mine, theirs, weights, first, second, sums, gains, gains_first, gains_second, block, grad)


def on_device(
    tokens, gains_taps, weights, cotangent, weight_first, weight_second, gains_first, gains_second
):
    layers = lax.axis_size("seq") // 2
    inner_word = (lax.axis_index("seq") % 2).astype(jnp.int32).reshape(1)
    own, oth = halves(weights, inner_word)
    block_out, input_grad, gain_sums, mine, theirs = block_step(
        tokens[0], cotangent[0], gains_taps, own, oth, layers
    )
    (
        weight_grad, weight_first_new, weight_second_new, weight_new,
        gains_grad, gains_first_new, gains_second_new, gains_new, block_out, input_grad,
    ) = update(
        inner_word, mine, theirs, weights, weight_first, weight_second,
        gain_sums, gains_taps, gains_first, gains_second, block_out, input_grad,
    )
    return (
        block_out[None],
        input_grad[None],
        weight_grad,
        weight_first_new,
        weight_second_new,
        weight_new,
        gains_grad,
        gains_first_new,
        gains_second_new,
        gains_new,
    )


def solution(mesh):
    tokens, rows, whole = P("shard", "seq", None), P("seq", "shard"), P()
    return jax.shard_map(
        on_device,
        mesh=mesh,
        in_specs=(tokens, whole, rows, tokens, rows, rows, whole, whole),
        out_specs=(tokens, tokens, rows, rows, rows, rows, whole, whole, whole, whole),
        check_vma=False,
    )
```

```python
import functools

import jax
import jax.numpy as jnp
from jax import lax
from jax.experimental import pallas as pl
from jax.experimental.pallas import tpu as pltpu
from jax.sharding import PartitionSpec as P

D = 1536
FF = 6912
STEP = 10
GROUPS = 4
QUARTER = D // GROUPS
UNITS = FF // GROUPS
HALF_Q = QUARTER // 2
HALF_F = UNITS // 2
LANES = 128
PAD_F = -(-HALF_F // LANES) * LANES
WIDE = 256
CONV_COLS = 4 * HALF_Q
UNIT_CHUNKS = (384, 256, PAD_F - 640)
UNIT_STARTS = (0, 384, 640)
WIDTHS = (CONV_COLS,) + tuple(3 * units for units in UNIT_CHUNKS)
STARTS = tuple(sum(WIDTHS[:k]) for k in range(len(WIDTHS)))
SPLIT = 128
REACH = (1, 1, 1, 1)
SLICE = 384
TILE = 16
ROWS = 48

MOMENT_DECAY = 0.9
SQUARE_DECAY = 0.95
ADAM_EPSILON = 1e-08
NORM_EPSILON = 1e-05
WEIGHT_RATE = 0.02
GAIN_RATE = 0.2
WEIGHT_DECAY = 0.1

BF16 = jnp.bfloat16
F32 = jnp.float32
MESH = pl.DeviceIdType.MESH
VMEM_BYTES = 63 * 1024 * 1024


def place():
    seq, shard = lax.axis_index("seq"), lax.axis_index("shard")
    inner, core = lax.rem(seq, 2), lax.rem(shard, 2)
    return seq, shard, inner, core


def partners():
    seq, shard, inner, core = place()
    across = {"seq": seq + 1 - 2 * inner, "shard": shard}
    beside = {"seq": seq, "shard": lax.rem(shard + 2, 4)}
    twin = {"seq": seq, "shard": shard + 1 - 2 * core}
    return across, beside, twin


def remote(src, dst, send, recv, device):
    return pltpu.make_async_remote_copy(
        src_ref=src, dst_ref=dst, send_sem=send, recv_sem=recv, device_id=device, device_id_type=MESH
    )


def line():
    seq, shard, _, _ = place()
    return seq // 2, lambda steps: {"seq": seq + 2 * steps, "shard": shard}


def greet(layers):
    outer, at = line()
    barrier = pltpu.get_barrier_semaphore()
    for device in partners():
        pl.semaphore_signal(barrier, inc=1, device_id=device, device_id_type=MESH)
    for steps in range(1, layers):
        for sign in (1, -1):

            @pl.when(in_line(outer + sign * steps, layers))
            def _():
                pl.semaphore_signal(barrier, inc=1, device_id=at(sign * steps), device_id_type=MESH)

    pl.semaphore_wait(barrier, 3 + layers - 1)


def in_line(index, layers):
    return (index >= 0) & (index < layers)


def allow(credit):
    for device in partners():
        pl.semaphore_signal(credit, inc=1, device_id=device, device_id_type=MESH)


def dot(left, right):
    return jnp.dot(left, right, preferred_element_type=F32)


def dot_rows(left, right):
    return lax.dot_general(left, right, (((1,), (1,)), ((), ())), preferred_element_type=F32)


def dot_columns(left, right):
    return lax.dot_general(left, right, (((0,), (0,)), ((), ())), preferred_element_type=F32)


def aligned(start, size, multiple=16):
    return pl.ds(pl.multiple_of(start, multiple), size)


class Gather:
    def __init__(self, layers, rows, own, oth, outs, send_x, recv_x, send_z, recv_z, local):
        self.layers, self.rows, self.own, self.oth, self.outs = layers, rows, own, oth, outs
        self.send_x, self.recv_x, self.send_z, self.recv_z, self.local = send_x, recv_x, send_z, recv_z, local
        self.seq, _, self.inner, _ = place()
        self.outer, self.at = line()
        self.across = partners()[0]

    def seq_rows(self, index):
        return aligned(index * self.rows, self.rows)

    def layer_rows(self, direction, distance):
        origin = self.outer - distance if direction == 0 else self.outer + distance
        return aligned(origin * 2 * self.rows, 2 * self.rows)

    def copy(self, k, src, dst, direction, distance, hop, piece):
        slot = (k, direction, distance + hop - 1, piece)
        return remote(
            src, dst, self.send_z.at[slot], self.recv_z.at[slot], self.at(hop if direction == 0 else -hop)
        )

    def goes(self, direction, hop):
        return in_line(self.outer + (hop if direction == 0 else -hop), self.layers)

    def has_come(self, direction, distance):
        return in_line(self.outer + (-distance if direction == 0 else distance), self.layers)

    def hops(self, k, distance):
        return range(1, min(REACH[k], self.layers - 1 - distance) + 1)

    def own_copy(self, k, direction, hop):
        src = self.own.at[:, pl.ds(STARTS[k], WIDTHS[k])]
        return self.copy(k, src, self.outs[k].at[self.seq_rows(self.seq)], direction, 0, hop, 0)

    def other_copy(self, k, direction, hop):
        there = self.outs[k].at[self.seq_rows(self.seq + 1 - 2 * self.inner)]
        return self.copy(k, there, there, direction, 0, hop, 1)

    def pass_copy(self, k, direction, distance, hop):
        ref = self.outs[k].at[self.layer_rows(direction, distance)]
        return self.copy(k, ref, ref, direction, distance, hop, 0)

    def x_copy(self, k):
        return remote(
            self.oth.at[:, pl.ds(STARTS[k], WIDTHS[k])],
            self.outs[k].at[self.seq_rows(self.seq)],
            self.send_x.at[k],
            self.recv_x.at[k],
            self.across,
        )

    def l_copy(self, k):
        return pltpu.make_async_copy(
            self.own.at[:, pl.ds(STARTS[k], WIDTHS[k])], self.outs[k].at[self.seq_rows(self.seq)], self.local.at[k]
        )

    def exchange(self, k):
        self.x_copy(k).start()
        self.l_copy(k).start()

    def send_own(self, k):
        for hop in self.hops(k, 0):
            for direction in (0, 1):

                @pl.when(self.goes(direction, hop))
                def _():
                    self.own_copy(k, direction, hop).start()

    def send_other(self, k):
        self.x_copy(k).wait_recv()
        for hop in self.hops(k, 0):
            for direction in (0, 1):

                @pl.when(self.goes(direction, hop))
                def _():
                    self.other_copy(k, direction, hop).start()

    def step(self, k, distance):
        for direction in (0, 1):

            @pl.when(self.has_come(direction, distance))
            def _():
                if distance <= REACH[k]:
                    origin = self.outer - distance if direction == 0 else self.outer + distance
                    for piece in (0, 1):
                        index = 2 * origin + (self.inner if piece == 0 else 1 - self.inner)
                        ref = self.outs[k].at[self.seq_rows(index)]
                        self.copy(k, ref, ref, direction, distance - 1, 1, piece).wait_recv()
                else:
                    ref = self.outs[k].at[self.layer_rows(direction, distance)]
                    self.copy(k, ref, ref, direction, distance - 1, 1, 0).wait_recv()
                if distance % REACH[k] == 0:
                    for hop in self.hops(k, distance):

                        @pl.when(self.goes(direction, hop))
                        def _():
                            self.pass_copy(k, direction, distance, hop).start()

        if distance == self.layers - 1:
            self.l_copy(k).wait()

    def steps(self, k, first, last=None):
        last = self.layers - 1 if last is None else min(last, self.layers - 1)
        for distance in range(first, last + 1):
            self.step(k, distance)

    def finish(self):
        for k in range(len(self.outs)):
            self.x_copy(k).wait_send()
            for distance in range(0, self.layers - 1, REACH[k]):
                for hop in self.hops(k, distance):
                    for direction in (0, 1):

                        @pl.when(self.goes(direction, hop) & self.has_come(direction, distance))
                        def _():
                            if distance == 0:
                                self.own_copy(k, direction, hop).wait_send()
                                self.other_copy(k, direction, hop).wait_send()
                            else:
                                self.pass_copy(k, direction, distance, hop).wait_send()


class Reduce:
    def __init__(self, layers, rows, grads, slots, stage, spare, total, outgoing, mine, theirs, sems):
        self.layers, self.rows, self.grads, self.slots = layers, rows, grads, slots
        self.stage, self.spare, self.total, self.outgoing = stage, spare, total, outgoing
        self.mine, self.theirs = mine, theirs
        self.send_g, self.recv_g, self.fetched, self.fetches, self.stored, self.send_o, self.recv_o = sems
        _, _, self.inner, _ = place()
        self.outer, self.at = line()
        self.across = partners()[0]

    def owner(self, direction, distance):
        return self.outer + distance if direction == 0 else self.outer - distance

    def upstream(self, direction, steps):
        return in_line(self.outer - steps if direction == 0 else self.outer + steps, self.layers)

    def block(self, k, owner):
        return self.grads[k].at[aligned(owner * 2 * self.rows, 2 * self.rows), pl.ds(0, WIDTHS[k])]

    def copy(self, k, src, direction, distance):
        hop = 1 if distance % 2 else 2
        slot = (direction, distance - 1)
        return remote(
            src,
            self.slots[k].at[slot],
            self.send_g.at[(k,) + slot],
            self.recv_g.at[(k,) + slot],
            self.at(hop if direction == 0 else -hop),
        )

    def send(self, k, direction, distance):
        self.copy(k, self.block(k, self.owner(direction, distance)), direction, distance).start()

    def direct(self, k, part=None, ends=None, least=1, most=None):
        at_end = (self.outer == 0) | (self.outer == self.layers - 1)
        for distance in range(most or self.layers - 1, least - 1, -1):
            for direction in (0, 1):
                owner = self.owner(direction, distance)
                here = in_line(owner, self.layers)
                if part is not None:
                    here = here & (owner * 2 * self.rows // SLICE == part)
                if ends is not None:
                    here = here & (at_end if ends else jnp.logical_not(at_end))
                if distance % 2 == 0:
                    here = here & jnp.logical_not(self.upstream(direction, 1))

                @pl.when(here)
                def _():
                    self.send(k, direction, distance)

    def fetch(self, k, direction, distance):
        slot = self.slots[k].at[direction, distance - 1]
        self.copy(k, slot, direction, distance).wait_recv()
        held = self.stage.at[:, pl.ds(0, WIDTHS[k])]
        copy = pltpu.make_async_copy(slot, held, self.fetched)
        copy.start()
        copy.wait()

    def tiles(self, body):
        def step(n, _):
            body(aligned(n * TILE, TILE))
            return 0

        lax.fori_loop(0, 2 * self.rows // TILE, step, 0)

    def join(self, k):
        cols = pl.ds(0, WIDTHS[k])
        for distance in range((self.layers - 1) // 2 * 2, 0, -2):
            for direction in (0, 1):
                owner = self.owner(direction, distance)

                @pl.when(in_line(owner, self.layers) & self.upstream(direction, 1))
                def _():
                    def add(tile):
                        base = self.owner(direction, distance) * 2 * self.rows
                        rows = pl.ds(pl.multiple_of(base + tile.start, 16), TILE)
                        ref = self.grads[k]
                        ref[rows, cols] = (
                            ref[rows, cols].astype(F32) + self.stage[tile, cols].astype(F32)
                        ).astype(BF16)

                    self.fetch(k, direction, distance + 1)
                    self.tiles(add)
                    if distance + 2 < self.layers:

                        @pl.when(self.upstream(direction, 2))
                        def _():
                            self.fetch(k, direction, distance + 2)
                            self.tiles(add)

                    self.send(k, direction, distance)

    def final(self, k, before=None):
        cols = pl.ds(0, WIDTHS[k])
        came = [(distance, direction) for distance in (1, 2) for direction in (0, 1) if distance < self.layers]

        def fetch(n, distance, direction):
            return pltpu.make_async_copy(
                self.slots[k].at[direction, distance - 1],
                self.spare.at[pl.ds(n * 2 * self.rows, 2 * self.rows), cols],
                self.fetches.at[n],
            )

        for n, (distance, direction) in enumerate(came):

            @pl.when(self.upstream(direction, distance))
            def _():
                self.copy(k, self.slots[k].at[direction, distance - 1], direction, distance).wait_recv()
                fetch(n, distance, direction).start()

        if before is not None:
            self.store(before).wait()

        here, there = self.inner * self.rows, (1 - self.inner) * self.rows

        def each(base, body):
            def step(n, _):
                body(base + n * TILE, n * TILE)
                return 0

            lax.fori_loop(0, self.rows // TILE, step, 0)

        for n, (distance, direction) in enumerate(came):

            @pl.when(self.upstream(direction, distance))
            def _():
                fetch(n, distance, direction).wait()

        def add_up(flags):
            def total(rows):
                value = self.grads[k][aligned(self.outer * 2 * self.rows + rows, TILE), cols].astype(F32)
                for n, flag in enumerate(flags):
                    if flag:
                        value = value + self.spare[aligned(n * 2 * self.rows + rows, TILE), cols].astype(F32)
                return value

            def send(rows, at):
                self.outgoing[aligned(at, TILE), pl.ds(STARTS[k], WIDTHS[k])] = total(rows).astype(BF16)

            def keep(rows, at):
                self.total[aligned(at, TILE), cols] = total(rows)

            each(there, send)
            self.over(k).start()
            each(here, keep)
            self.store(k).start()

        patterns = {}
        for place_in_line in range(self.layers):
            flags = tuple(
                0 <= (place_in_line - distance if direction == 0 else place_in_line + distance) < self.layers
                for distance, direction in came
            )
            patterns.setdefault(flags, []).append(place_in_line)
        for flags, places in patterns.items():
            here_now = functools.reduce(jnp.logical_or, [self.outer == p for p in places])

            @pl.when(here_now)
            def _():
                add_up(flags)

    def over(self, k):
        wide = pl.ds(STARTS[k], WIDTHS[k])
        return remote(
            self.outgoing.at[:, wide], self.theirs.at[:, wide], self.send_o.at[k], self.recv_o.at[k], self.across
        )

    def store(self, k):
        return pltpu.make_async_copy(
            self.total.at[:, pl.ds(0, WIDTHS[k])], self.mine.at[:, pl.ds(STARTS[k], WIDTHS[k])], self.stored.at[k]
        )

    def wait_sent(self, k):
        for distance in range(1, self.layers):
            for direction in (0, 1):
                owner = self.owner(direction, distance)

                @pl.when(in_line(owner, self.layers))
                def _():
                    self.copy(k, self.block(k, owner), direction, distance).wait_send()

    def finish(self, before):
        self.store(before).wait()
        for k in range(len(self.grads)):
            self.over(k).wait()


class Spread:
    slots = range(11)

    def __init__(self, buf, seg, send, recv):
        self.buf, self.seg, self.send, self.recv = buf, seg, send, recv

    def index(self, n):
        _, shard, inner, core = place()
        row, flip, other = (n // 2) % 2, n // 4, n % 2
        return 2 * (lax.rem(shard + 2 * row, 4) + other * (1 - 2 * core)) + inner + flip * (1 - 2 * inner)

    def copy(self, slot):
        across, beside, twin = partners()
        low, high, whole = (0, SPLIT), (SPLIT, self.seg - SPLIT), (0, self.seg)
        n, (first, size), device = {
            0: (0, low, across),
            9: (0, high, across),
            1: (0, high, beside),
            10: (0, low, beside),
            2: (0, whole, twin),
            3: (4, low, beside),
            4: (4, whole, twin),
            5: (2, high, across),
            6: (2, whole, twin),
            7: (6, low, twin),
            8: (6, high, twin),
        }[slot]
        ref = self.buf.at[aligned(self.index(n) * self.seg + first, size)]
        return remote(ref, ref, self.send.at[slot], self.recv.at[slot], device)

    def push(self, *slots):
        for slot in slots:
            self.copy(slot).start()

    def came(self, *slots):
        for slot in slots:
            self.copy(slot).wait_recv()

    def start(self):
        self.push(0, 1, 9, 10, 2)

    def first(self):
        self.came(1)
        self.push(5)
        self.came(0)
        self.push(3)

    def near(self):
        self.came(10)
        self.push(6)
        self.came(9)
        self.push(4)

    def far(self):
        self.came(3)
        self.push(7)
        self.came(5)
        self.push(8)

    def sent(self):
        for slot in self.slots:
            self.copy(slot).wait_send()

    def end(self):
        self.came(2, 4, 6, 7, 8)
        self.sent()

    def before(self, n):
        return {
            1: (lambda: self.came(2),),
            2: (self.first, self.near),
            3: (lambda: self.came(6),),
            5: (lambda: self.came(4),),
            6: (self.far,),
            7: (lambda: self.came(7, 8),),
        }.get(n, ())


class Collect:
    def __init__(self, part, seg, total, pair, near, joined, send, recv):
        self.part, self.seg, self.total = part, seg, total
        self.pair, self.near, self.joined, self.send, self.recv = pair, near, joined, send, recv
        _, self.shard, self.inner, core = place()
        self.twin_shard = self.shard + 1 - 2 * core
        self.low, self.high, self.whole = (0, SPLIT), (SPLIT, seg - SPLIT), (0, seg)
        self.cols = pl.ds(0, D)

    def index(self, s, k):
        row, flip = 1 - k % 2, 1 - k // 2
        return 2 * lax.rem(s + 2 * row, 4) + self.inner + flip * (1 - 2 * self.inner)

    def pair_copy(self, k):
        src = self.part.at[aligned(self.index(self.twin_shard, k) * self.seg, self.seg), self.cols]
        return remote(src, self.pair.at[k], self.send.at[k], self.recv.at[k], partners()[2])

    def copy(self, slot):
        across, beside, _ = partners()
        src, dst, (first, size), device = {
            4: (self.pair.at[0], self.joined, self.low, across),
            5: (self.pair.at[0], self.joined, self.high, beside),
            6: (self.pair.at[1], self.near.at[0], self.low, across),
            7: (self.pair.at[2], self.near.at[1], self.high, beside),
            8: (self.pair.at[2], self.near.at[1], self.low, beside),
            9: (self.pair.at[1], self.near.at[0], self.high, across),
        }[slot]
        rows = pl.ds(first, size)
        return remote(src.at[rows], dst.at[rows], self.send.at[slot], self.recv.at[slot], device)

    def over(self, span, body):
        def step(n, _):
            body(aligned(span[0] + n * 16, 16))
            return 0

        lax.fori_loop(0, span[1] // 16, step, 0)

    def mine(self, k, rows):
        return self.part[aligned(self.index(self.shard, k) * self.seg + rows.start, 16), self.cols].astype(F32)

    def add_pair(self, k):
        def add(rows):
            self.pair[k, rows] = (self.mine(k, rows) + self.pair[k, rows].astype(F32)).astype(BF16)

        self.pair_copy(k).wait_recv()
        self.over(self.whole, add)
        for slot in ((4, 5), (6,), (7,))[k]:
            self.copy(slot).start()

    def add_own(self):
        def add(rows):
            self.total[rows] = self.mine(3, rows) + self.pair[3, rows].astype(F32)

        self.pair_copy(3).wait_recv()
        self.over(self.whole, add)

    def pass_on(self):
        for slot, k, span, after in ((4, 2, self.low, 8), (5, 1, self.high, 9)):

            def add(rows):
                self.pair[k, rows] = (self.pair[k, rows].astype(F32) + self.joined[rows].astype(F32)).astype(BF16)

            self.copy(slot).wait_recv()
            self.over(span, add)
            self.copy(after).start()

    def push(self):
        for k in range(4):
            self.pair_copy(k).start()

    def make(self, n, produce):
        k, own = n // 2, n % 2
        produce(self.index(jnp.where(own == 1, self.shard, self.twin_shard), k))

        @pl.when(own == 0)
        def _():
            self.pair_copy(k).start()

        for m in range(3):

            @pl.when(n == 2 * m + 1)
            def _():
                self.add_pair(m)
                if m == 2:
                    self.pass_on()

        pl.when(n == 7)(self.add_own)

    def end(self):
        def add(rows):
            near = self.near[0, rows].astype(F32) + self.near[1, rows].astype(F32)
            self.total[rows] = self.total[rows] + near

        for slots, span in (((6, 8), self.low), ((7, 9), self.high)):
            for slot in slots:
                self.copy(slot).wait_recv()
            self.over(span, add)
        for k in range(4):
            self.pair_copy(k).wait_send()
        for slot in range(4, 10):
            self.copy(slot).wait_send()


def norm_scale(values):
    return lax.rsqrt(jnp.mean(values * values, axis=-1, keepdims=True) + NORM_EPSILON)


def by_rows(rows, body, carry=0):
    def step(n, carry):
        return body(aligned(n * ROWS, ROWS), carry)

    return lax.fori_loop(0, rows // ROWS, step, carry)


def norm_back(values, gain, upstream):
    scale = norm_scale(values)
    scaled = gain * upstream
    inner = jnp.mean(scaled * values, axis=-1, keepdims=True)
    return (
        scale * scaled - values * scale * scale * scale * inner,
        jnp.sum(upstream * values * scale, axis=0, keepdims=True),
    )


REFS = (
    "tok", "cot", "gains", "own", "oth",
    "block_out", "input_grad", "gain_sums", "mine", "theirs", "n1_held", "slot0", "slot1", "slot2", "slot3",
    "w0", "w1", "w2", "w3", "seq_a", "seq_b", "du", "act", "c_all", "gated", "mixed", "resid", "dresid", "total",
    "pair", "near", "joined", "g1", "g2", "g3", "stage", "sum", "outgoing", "tap_sums", "gain_in", "gain_line",
    "held", "local", "send_x", "recv_x", "send_z", "recv_z", "send_s", "recv_s", "send_c", "recv_c", "credit",
    "halo_send", "halo_recv", "send_g", "recv_g", "fetched", "fetches", "stored", "send_o", "recv_o",
    "send_a", "recv_a", "send_l", "recv_l",
)


def block_kernel(layers, rows, *all_refs):
    r = dict(zip(REFS, all_refs, strict=True))
    tok, cot, gains = r["tok"], r["cot"], r["gains"]
    seq_a, seq_b, du, act = r["seq_a"], r["seq_b"], r["du"], r["act"]
    c_all, gated, mixed, total = r["c_all"], r["gated"], r["mixed"], r["total"]
    weights = (r["w0"], r["w1"], r["w2"], r["w3"])
    seg = tok.shape[0]
    _, shard, inner, _ = place()
    outer, at = line()
    me = 2 * shard + inner
    my_rows = aligned(me * seg, seg)
    chunks = list(zip(range(1, 1 + len(UNIT_CHUNKS)), UNIT_STARTS, UNIT_CHUNKS))
    gather = Gather(
        layers, rows, r["own"], r["oth"], weights,
        r["send_x"], r["recv_x"], r["send_z"], r["recv_z"], r["local"],
    )
    reduce = Reduce(
        layers, rows, (r["w2"], r["g1"], r["g2"], r["g3"]), (r["slot0"], r["slot1"], r["slot2"], r["slot3"]),
        r["stage"], r["w1"], r["sum"], r["outgoing"], r["mine"], r["theirs"],
        (r["send_g"], r["recv_g"], r["fetched"], r["fetches"], r["stored"], r["send_o"], r["recv_o"]),
    )

    def spread(buf, n):
        return Spread(buf, seg, r["send_s"].at[n], r["recv_s"].at[n])

    def collect(part, n):
        return Collect(part, seg, total, r["pair"], r["near"], r["joined"], r["send_c"].at[n], r["recv_c"].at[n])

    one, up, two, three = spread(seq_a, 0), spread(seq_b, 1), spread(seq_a, 2), spread(seq_a, 3)
    branch, down, feed, inputs = collect(seq_a, 0), collect(seq_b, 1), collect(du, 2), collect(seq_a, 3)
    lanes = lax.broadcasted_iota(jnp.int32, (seg, WIDE), 1) < HALF_Q
    taps = pltpu.roll(gains[...], lax.rem(D - shard * QUARTER - inner * HALF_Q, D), 1)[2:5, :WIDE]
    kept = pl.ds(D, WIDE)
    sums, tap_sums = r["gain_sums"], r["tap_sums"]

    def block(t):
        return aligned(t * seg, seg)

    def mine(part):
        return pl.ds(pl.multiple_of(me * seg + part.start, 16), part.size)

    def first_norm():
        def rows(part, _):
            values = tok[part].astype(F32)
            seq_a[mine(part)] = (values * norm_scale(values) * gains[0:1, :]).astype(BF16)
            return 0

        by_rows(seg, rows)

    def up_start():
        seq_b[my_rows] = cot[...]
        up.start()

    def held():
        return pltpu.make_async_copy(seq_a, r["n1_held"], r["held"])

    def reload():
        return pltpu.make_async_copy(r["n1_held"], seq_b, r["held"])

    def project(s):
        for i in (0, 1):
            parts = dot(seq_a[block(2 * s + i)], weights[0][...])
            b = jnp.where(lanes, parts[:, :WIDE], 0.0)
            c = pltpu.roll(parts[:, 128 : 128 + 384], 384 - 64, 1)[:, :WIDE]
            x = parts[:, 384 : 384 + WIDE]
            c_all[s, pl.ds(i * seg, seg)] = jnp.where(lanes, c, 0.0)
            gated[s, pl.ds(8 + i * seg, seg)] = (b * x).astype(BF16).astype(F32)

    def ahead():
        return remote(
            gated.at[:, pl.ds(2 * seg, 8)], gated.at[:, pl.ds(0, 8)], r["halo_send"].at[0], r["halo_recv"].at[0], at(1)
        )

    def halo():
        pl.when(outer < layers - 1)(lambda: ahead().start())

        @pl.when(outer == 0)
        def _():
            gated[:, pl.ds(0, 8)] = jnp.zeros((GROUPS, 8, WIDE), F32)

    def convolved(s, i):
        return (
            taps[0:1, :] * gated[s, pl.ds(6 + i * seg, seg)]
            + taps[1:2, :] * gated[s, pl.ds(7 + i * seg, seg)]
            + taps[2:3, :] * gated[s, pl.ds(8 + i * seg, seg)]
        )

    def convolve(t):
        for i in (0, 1):

            @pl.when(t % 2 == i)
            def _():
                s = t // 2
                mixed[block(t)] = pltpu.roll(c_all[s, pl.ds(i * seg, seg)] * convolved(s, i), 64, 1).astype(BF16)

        seq_a[block(t)] = dot_rows(mixed[block(t)], weights[0][:, pl.ds(512, WIDE)]).astype(BF16)

    def branch_end():
        branch.end()
        allow(r["credit"].at[0])

    def second_norm():
        def rows(part, _):
            values = tok[part].astype(F32) + total[part]
            r["resid"][part] = values
            seq_a[mine(part)] = (values * norm_scale(values) * gains[1:2, :]).astype(BF16)
            return 0

        by_rows(seg, rows)
        pl.semaphore_wait(r["credit"].at[0], 3)

    def hidden(k, start, units, t):
        ref, here = weights[k], block(t)
        gate = dot(seq_a[here], ref[:, pl.ds(0, units)])
        upval = dot(seq_a[here], ref[:, pl.ds(units, units)])
        dact = dot(seq_b[here], ref[:, pl.ds(2 * units, units)])
        sigma = jax.nn.sigmoid(gate)
        silu = gate * sigma
        act[here, pl.ds(start, units)] = (silu * upval).astype(BF16)
        dgate = dact * upval * sigma * (1.0 + gate * (1.0 - sigma))
        du[here, pl.ds(2 * start, units)] = dgate.astype(BF16)
        du[here, pl.ds(2 * start + units, units)] = (dact * silu).astype(BF16)

    def slice_of(n):
        return jnp.where(outer < layers // 2, D // SLICE - 1 - n, n)

    def gate_up_grads(k, start, units, n):
        part = slice_of(n)
        left = seq_a[:, aligned(part * SLICE, SLICE, 128)]
        for m in (0, 1):
            reduce.grads[k][aligned(part * SLICE, SLICE), pl.ds(m * units, units)] = dot_columns(
                left, du[:, pl.ds(2 * start + m * units, units)]
            ).astype(BF16)

    def down_grads(k, start, units, n):
        part = slice_of(n)
        left = seq_b[:, aligned(part * SLICE, SLICE, 128)]
        reduce.grads[k][aligned(part * SLICE, SLICE), pl.ds(2 * units, units)] = dot_columns(
            left, act[:, pl.ds(start, units)]
        ).astype(BF16)

    def grads(k, start, units, n):
        gate_up_grads(k, start, units, n)
        down_grads(k, start, units, n)
        reduce.direct(k, slice_of(n), ends=True)

    def second(t):
        here = block(t)
        seq_b[here] = sum(
            dot_rows(du[here, pl.ds(2 * start, 2 * units)], weights[k][:, pl.ds(0, 2 * units)])
            for k, start, units in chunks
        ).astype(BF16)

    def down_end():
        down.end()
        reload().start()
        allow(r["credit"].at[1])

    def forward(t):
        here = block(t)
        du[here, pl.ds(0, D)] = sum(
            dot_rows(act[here, pl.ds(start, units)], weights[k][:, pl.ds(2 * units, units)])
            for k, start, units in chunks
        ).astype(BF16)

    def second_back():
        def rows(part, gain):
            dpart, dgain = norm_back(r["resid"][part], gains[1:2, :], total[part])
            dresid = cot[part].astype(F32) + dpart
            r["dresid"][part] = dresid
            seq_a[mine(part)] = dresid.astype(BF16)
            return gain + dgain

        sums[...] = jnp.zeros(sums.shape, F32)
        tap_sums[...] = jnp.zeros(tap_sums.shape, F32)
        sums[1:2, pl.ds(0, D)] = by_rows(seg, rows, jnp.zeros((1, D), F32))
        pl.semaphore_wait(r["credit"].at[1], 3)

    def mix_back(t):
        s, here = t // 2, block(t)
        dmixed = pltpu.roll(dot(seq_a[here], weights[0][:, pl.ds(512, WIDE)]), WIDE - 64, 1)
        dmixed = jnp.where(lanes, dmixed, 0.0)
        for i in (0, 1):

            @pl.when(t % 2 == i)
            def _():
                du[here, kept] = (dmixed * convolved(s, i)).astype(BF16)
                c_all[s, pl.ds(i * seg, seg)] = dmixed * c_all[s, pl.ds(i * seg, seg)]

    def after():
        return remote(
            c_all.at[:, pl.ds(0, 8)], c_all.at[:, pl.ds(2 * seg, 8)], r["halo_send"].at[1], r["halo_recv"].at[1], at(-1)
        )

    def halo_back():
        pl.when(outer > 0)(lambda: after().start())

        @pl.when(outer == layers - 1)
        def _():
            c_all[:, pl.ds(2 * seg, 8)] = jnp.zeros((GROUPS, 8, WIDE), F32)

    def conv_back(n):
        for i in (0, 1):
            pl.when(n // GROUPS == i)(functools.partial(conv_back_half, n % GROUPS, i))

    def conv_back_half(s, i):
        t = block(2 * s + i)
        dconv = c_all[s, pl.ds(i * seg, seg)]
        dgated = (
            taps[2:3, :] * dconv
            + taps[1:2, :] * c_all[s, pl.ds(1 + i * seg, seg)]
            + taps[0:1, :] * c_all[s, pl.ds(2 + i * seg, seg)]
        )
        parts = dot(seq_b[t], weights[0][:, pl.ds(0, 640)])
        db = dgated * parts[:, 384:640]
        dx = dgated * parts[:, :WIDE]
        dc = jnp.concatenate([du[t, kept].astype(F32), jnp.zeros((seg, 128), F32)], axis=1)
        dc = pltpu.roll(dc, 64, 1)
        act[t, pl.ds(0, 128)] = db[:, :128].astype(BF16)
        act[t, pl.ds(128, 128)] = (db[:, 128:] + dc[:, :128]).astype(BF16)
        act[t, pl.ds(256, 128)] = dc[:, 128:256].astype(BF16)
        act[t, pl.ds(384, WIDE)] = dx.astype(BF16)
        act[t, pl.ds(640, 128)] = jnp.zeros((seg, 128), BF16)
        for k in range(3):
            moved = gated[s, pl.ds(6 + k + i * seg, seg)]
            tap_sums[k : k + 1] = tap_sums[k : k + 1] + jnp.sum(dconv * moved, axis=0, keepdims=True)

    def conv_grads(n):
        part = slice_of(n)
        held_rows, cols = aligned(part * SLICE, SLICE), aligned(part * SLICE, SLICE, 128)
        ref = reduce.grads[0]
        ref[held_rows, pl.ds(0, 512)] = dot_columns(seq_b[:, cols], act[:, pl.ds(0, 512)]).astype(BF16)
        ref[held_rows, pl.ds(512, WIDE)] = (
            dot_columns(seq_b[:, cols], act[:, pl.ds(512, WIDE)]) + dot_columns(seq_a[:, cols], mixed[...])
        ).astype(BF16)
        reduce.direct(0, part)

    def feed_end():
        feed.end()
        allow(r["credit"].at[2])
        r["block_out"][...] = (r["resid"][...] + total[...]).astype(BF16)

    def first(t):
        here = block(t)
        seq_a[here] = dot_rows(act[here, pl.ds(0, 640)], weights[0][:, pl.ds(0, 640)]).astype(BF16)

    def first_back():
        def rows(part, gain):
            dpart, dgain = norm_back(tok[part].astype(F32), gains[0:1, :], total[part])
            r["input_grad"][part] = (r["dresid"][part] + dpart).astype(BF16)
            return gain + dgain

        sums[0:1, pl.ds(0, D)] = by_rows(seg, rows, jnp.zeros((1, D), F32))
        sums[2:5, aligned(me * WIDE, WIDE, 128)] = tap_sums[0:3]

    def gains_across(n):
        return remote(sums, r["gain_in"].at[n], r["send_a"].at[n], r["recv_a"].at[n], partners()[n])

    def gains_add(n):
        gains_across(n).wait()
        sums[...] = sums[...] + r["gain_in"][n]

    def line_copy(sign, steps):
        slot = (0 if sign > 0 else 1, steps - 1)
        return remote(
            sums, r["gain_line"].at[slot], r["send_l"].at[slot], r["recv_l"].at[slot], at(sign * steps)
        )

    def gains_line():
        for steps in range(1, layers):
            for sign in (1, -1):
                pl.when(in_line(outer + sign * steps, layers))(line_copy(sign, steps).start)

    def gains_end():
        for steps in range(1, layers):
            for sign in (1, -1):
                pl.when(in_line(outer + sign * steps, layers))(line_copy(sign, steps).wait_send)
                pl.when(in_line(outer - sign * steps, layers))(line_copy(sign, steps).wait_recv)

        own_sums = sums[...]
        for origin in range(layers):
            for steps in range(1, layers):
                for sign in (1, -1):

                    @pl.when((outer - sign * steps == origin))
                    def _():
                        came = r["gain_line"][0 if sign > 0 else 1, steps - 1]
                        sums[...] = came if origin == 0 else sums[...] + came

            if origin > 0:

                @pl.when(outer == origin)
                def _():
                    sums[...] = sums[...] + own_sums

    def end():
        reduce.finish(0)
        for k in range(len(WIDTHS)):
            reduce.wait_sent(k)
        pl.when(outer < layers - 1)(lambda: ahead().wait_send())
        pl.when(outer > 0)(lambda: after().wait_send())

    def start():
        greet(layers)

    def hold():
        held().start()

    def hold_end():
        held().wait()

    def halo_end():
        pl.when(outer > 0)(lambda: ahead().wait_recv())

    def reload_end():
        reload().wait()

    def halo_back_end():
        pl.when(outer < layers - 1)(lambda: after().wait_recv())

    def feed_credit():
        pl.semaphore_wait(r["credit"].at[2], 3)

    def from_spread(moved, body):
        def step(n):
            for m in range(8):
                if moved.before(m):

                    @pl.when(n == m)
                    def _():
                        for act in moved.before(m):
                            act()

            body(moved.index(n))

        return step

    def each(body, *cases):
        return [functools.partial(body, *(case if isinstance(case, tuple) else (case,))) for case in cases]

    every = range(len(WIDTHS))
    exchange, send_own, send_other = (
        each(body, *every) for body in (gather.exchange, gather.send_own, gather.send_other)
    )
    step = [each(gather.steps, (k, 1, 1), (k, 2, 2), (k, 3)) for k in every]
    join = each(reduce.join, *every)
    final = each(reduce.final, (0, 3), 1, (2, 1), (3, 2))
    feed_pair = each(feed.add_pair, 0, 1, 2)
    gain_send = [lambda n=n: gains_across(n).start() for n in range(3)]
    gain_add = each(gains_add, 0, 1, 2)
    d1 = functools.partial(reduce.direct, 1, ends=False)
    d2 = functools.partial(reduce.direct, 2, ends=False)
    d3_far = functools.partial(reduce.direct, 3, least=2)
    d3_near = functools.partial(reduce.direct, 3, most=1)
    blocks, parts = 2 * GROUPS, D // SLICE
    proj = Loop(GROUPS, project)
    mix = Loop(blocks, lambda n: branch.make(n, convolve))
    hid1 = Loop(blocks, from_spread(two, functools.partial(hidden, *chunks[0])))
    hid2, hid3 = (Loop(blocks, functools.partial(hidden, *chunk)) for chunk in chunks[1:])
    grad1, grad2 = (Loop(parts, functools.partial(grads, *chunk)) for chunk in chunks[:2])
    down3 = Loop(parts, functools.partial(down_grads, *chunks[2]))
    back2 = Loop(blocks, lambda n: down.make(n, second))
    gate3 = Loop(parts, functools.partial(gate_up_grads, *chunks[2]))
    ffn = Loop(blocks, forward)
    back_mix = Loop(blocks, from_spread(three, mix_back))
    back_conv = Loop(blocks, conv_back)
    grad0 = Loop(parts, conv_grads)
    back1 = Loop(blocks, lambda n: inputs.make(n, first))
    play(
        [
            start, send_own[0], exchange[0], first_norm, send_own[3], one.start, send_other[0], exchange[1],
            step[0][0], one.first, up_start, step[0][1], send_other[1], exchange[2], one.near, one.far, send_own[1],
            step[0][2], one.end, proj[0], proj[1], hold, proj[2], up.first, proj[3], halo, halo_end, step[1][0],
            hold_end, mix[0], mix[1], mix[2], mix[3], send_own[2], mix[4], mix[5], mix[6], up.near, step[1][1],
            exchange[3], up.far, up.end, mix[7], branch_end, second_norm, send_other[2], two.start, step[1][2],
            hid1[0], send_other[3], hid1[1], hid1[2], step[2][0], hid1[3], hid1[4], hid1[5], step[3][0], hid1[6],
            hid1[7], two.sent, grad1[0], grad1[1], grad1[2], step[2][1], grad1[3], step[2][2], hid2[0], hid2[1],
            hid2[2], hid2[3], hid2[4], step[3][1], d1, hid2[5], hid2[6], hid2[7], grad2[0], grad2[1], grad2[2],
            step[3][2], grad2[3], hid3[0], hid3[1], hid3[2], hid3[3], hid3[4], hid3[5], hid3[6], hid3[7], down3[0],
            down3[1], down3[2], down3[3], d2, back2[0], back2[1], back2[2], join[1], back2[3], back2[4], back2[5],
            back2[6], back2[7], gate3[0], gate3[1], gate3[2], gate3[3], d3_far, down_end, second_back, join[2],
            three.start, back_mix[0], ffn[0], ffn[1], ffn[2], ffn[3], ffn[4], ffn[5], ffn[6], ffn[7], feed.push,
            reload_end, back_mix[1], back_mix[2], back_mix[3], feed_pair[0], back_mix[4], back_mix[5], feed_pair[1],
            gather.finish, back_mix[6], final[1], back_mix[7], three.sent, halo_back, back_conv[0], back_conv[1],
            back_conv[2], feed_pair[2], halo_back_end, d3_near, back_conv[3], back_conv[4], feed.pass_on, join[3],
            final[2], back_conv[5], back_conv[6], back_conv[7], grad0[0], feed.add_own, grad0[1], grad0[2],
            grad0[3], feed_end, feed_credit, back1[0], back1[1], back1[2], join[0], back1[3], back1[4], back1[5],
            back1[6], back1[7], final[3], inputs.end, first_back, gain_send[0], gain_add[0], gain_send[1], final[0],
            gain_add[1], gain_send[2], gain_add[2], gains_line, gains_end, end,
        ]
    )


class Loop:
    def __init__(self, count, body):
        self.count, self.body = count, body

    def __getitem__(self, n):
        return (self, n)


def play(order):
    order = list(order)
    while order:
        entry = order.pop(0)
        if not isinstance(entry, tuple):
            entry()
            continue
        loop, _ = entry
        between = {}
        for n in range(1, loop.count):
            between[n] = []
            while order[0] != (loop, n):
                between[n].append(order.pop(0))
            order.pop(0)

        def turn(n, _):
            for m, acts in between.items():
                if acts:

                    @pl.when(n == m)
                    def _():
                        play(acts)

            loop.body(n)
            return 0

        lax.fori_loop(0, loop.count, turn, 0)


def block_step(tok, cot, gains, own, oth, layers):
    rows, seg = own.shape[0], tok.shape[0]
    count = len(WIDTHS)
    tokens = 2 * GROUPS * seg
    vmem, anywhere = pl.BlockSpec(memory_space=pltpu.VMEM), pl.BlockSpec(memory_space=pl.ANY)
    shape, scratch = jax.ShapeDtypeStruct, pltpu.VMEM
    dma, regular = pltpu.SemaphoreType.DMA, pltpu.SemaphoreType.REGULAR
    hops = layers - 1
    wide, biggest = sum(WIDTHS), max(WIDTHS)
    out_shape = [
        shape((seg, D), BF16),
        shape((seg, D), BF16),
        shape((8, 2 * GROUPS * WIDE), F32),
        shape((rows, wide), F32),
        shape((rows, wide), BF16),
        shape((tokens, D), BF16),
    ] + [shape((2, hops, 2 * rows, width), BF16) for width in WIDTHS]
    scratch_shapes = (
        [scratch((D, width), BF16) for width in WIDTHS]
        + [
            scratch((tokens, D), BF16),
            scratch((tokens, D), BF16),
            scratch((tokens, 2 * PAD_F), BF16),
            scratch((tokens, PAD_F), BF16),
            scratch((GROUPS, 8 + 2 * seg, WIDE), F32),
            scratch((GROUPS, 8 + 2 * seg, WIDE), F32),
            scratch((tokens, WIDE), BF16),
            scratch((seg, D), F32),
            scratch((seg, D), F32),
            scratch((seg, D), F32),
            scratch((4, seg, D), BF16),
            scratch((2, seg, D), BF16),
            scratch((seg, D), BF16),
        ]
        + [scratch((D, width), BF16) for width in WIDTHS[1:]]
        + [
            scratch((2 * rows, biggest), BF16),
            scratch((rows, biggest), F32),
            scratch((rows, wide), BF16),
            scratch((8, WIDE), F32),
            scratch((3, 8, 2 * GROUPS * WIDE), F32),
            scratch((2, hops, 8, 2 * GROUPS * WIDE), F32),
            dma,
            dma((count,)),
            dma((count,)),
            dma((count,)),
            dma((count, 2, hops, 2)),
            dma((count, 2, hops, 2)),
            dma((4, 11)),
            dma((4, 11)),
            dma((4, 10)),
            dma((4, 10)),
            regular((3,)),
            dma((2,)),
            dma((2,)),
            dma((count, 2, hops)),
            dma((count, 2, hops)),
            dma,
            dma((4,)),
            dma((count,)),
            dma((count,)),
            dma((count,)),
            dma((3,)),
            dma((3,)),
            dma((2, hops)),
            dma((2, hops)),
        ]
    )
    return pl.pallas_call(
        functools.partial(block_kernel, layers, rows),
        out_shape=out_shape,
        in_specs=[vmem] * 3 + [anywhere] * 2,
        out_specs=[vmem] * 3 + [anywhere] * (3 + count),
        scratch_shapes=scratch_shapes,
        compiler_params=pltpu.CompilerParams(
            collective_id=0, has_side_effects=True, vmem_limit_bytes=VMEM_BYTES
        ),
        name="block_step",
    )(tok, cot, gains, own, oth)[:5]


def column_pieces(half):
    pieces = [(m * QUARTER + half * HALF_Q, m * HALF_Q, HALF_Q, 0) for m in range(4)]
    for k, (start, units) in enumerate(zip(UNIT_STARTS, UNIT_CHUNKS), 1):
        real = min(units, HALF_F - start)
        for m in range(3):
            first = 4 * QUARTER + m * UNITS + half * HALF_F + start
            pieces.append((first, STARTS[k] + m * units, real, units - real))
    return pieces


def halves_kernel(inner_ref, weights_ref, own_ref, oth_ref):
    is_low = inner_ref[0] == 0

    def half(h):
        parts = []
        for first, _, width, padding in column_pieces(h):
            parts.append(weights_ref[:, first : first + width])
            if padding:
                parts.append(jnp.zeros((parts[-1].shape[0], padding), F32))
        return jnp.concatenate(parts, axis=1)

    low, high = half(0), half(1)
    own_ref[...] = jnp.where(is_low, low, high).astype(BF16)
    oth_ref[...] = jnp.where(is_low, high, low).astype(BF16)


def band(rows, most):
    return max(size for size in range(16, most + 1, 16) if rows % size == 0)


def halves(weights, inner):
    rows, cols = weights.shape
    wide = sum(WIDTHS)
    size = band(rows, 96)
    by_row = lambda width: pl.BlockSpec((size, width), lambda n: (n, 0))
    return pl.pallas_call(
        halves_kernel,
        grid=(rows // size,),
        out_shape=[jax.ShapeDtypeStruct((rows, wide), BF16)] * 2,
        in_specs=[pl.BlockSpec(memory_space=pltpu.SMEM), by_row(cols)],
        out_specs=[by_row(wide)] * 2,
        compiler_params=pltpu.CompilerParams(vmem_limit_bytes=VMEM_BYTES),
        name="halves",
    )(inner, weights)


def adam_update(param, grad, first, second, rate, decay):
    first_new = MOMENT_DECAY * first + (1.0 - MOMENT_DECAY) * grad
    second_new = SQUARE_DECAY * second + (1.0 - SQUARE_DECAY) * grad * grad
    root = jnp.sqrt(second_new * (1.0 / (1.0 - SQUARE_DECAY**STEP))) + ADAM_EPSILON
    step = first_new * (rate / (1.0 - MOMENT_DECAY**STEP)) / root
    return (first_new, second_new, param * (1.0 - rate * decay) - step)


def update_kernel(
    inner_ref, mine_ref, theirs_ref, weights_ref, first_ref, second_ref, sums_ref, gains_ref, gains_first_ref,
    gains_second_ref, block_ref, input_ref, grad_out, first_out, second_out, weights_out, gains_grad_out,
    gains_first_out, gains_second_out, gains_out, block_out, input_out,
):
    is_low = inner_ref[0] == 0
    mine, theirs = mine_ref[...], theirs_ref[...].astype(F32)
    for half in (0, 1):
        chosen = jnp.where(is_low, mine, theirs) if half == 0 else jnp.where(is_low, theirs, mine)
        for first, own, width, _ in column_pieces(half):
            grad_out[:, first : first + width] = chosen[:, own : own + width]
    first_out[...], second_out[...], weights_out[...] = adam_update(
        weights_ref[...], grad_out[...], first_ref[...], second_ref[...], WEIGHT_RATE, WEIGHT_DECAY
    )

    @pl.when(pl.program_id(0) == 0)
    def _():
        gains_grad_out[0:2] = sums_ref[0:2, :D]
        for n in range(2 * GROUPS):
            gains_grad_out[2:5, n * HALF_Q : (n + 1) * HALF_Q] = sums_ref[2:5, n * WIDE : n * WIDE + HALF_Q]
        gains_first_out[...], gains_second_out[...], gains_out[...] = adam_update(
            gains_ref[...], gains_grad_out[...], gains_first_ref[...], gains_second_ref[...], GAIN_RATE, 0.0
        )
        block_out[...] = block_ref[...]
        input_out[...] = input_ref[...]


def update(inner, mine, theirs, weights, first, second, sums, gains, gains_first, gains_second, block, grad):
    rows, cols = weights.shape
    wide = mine.shape[1]
    size = band(rows, 32)
    by_row = lambda width: pl.BlockSpec((size, width), lambda n: (n, 0))
    whole = lambda values: pl.BlockSpec(values.shape, lambda n: (0, 0))
    shape = jax.ShapeDtypeStruct
    return pl.pallas_call(
        update_kernel,
        grid=(rows // size,),
        out_shape=[shape((rows, cols), F32)] * 4 + [shape(gains.shape, F32)] * 4 + [shape(block.shape, BF16)] * 2,
        in_specs=[pl.BlockSpec(memory_space=pltpu.SMEM)]
        + [by_row(wide)] * 2
        + [by_row(cols)] * 3
        + [whole(sums)]
        + [whole(gains)] * 3
        + [whole(block)] * 2,
        out_specs=[by_row(cols)] * 4 + [whole(gains)] * 4 + [whole(block)] * 2,
        compiler_params=pltpu.CompilerParams(vmem_limit_bytes=VMEM_BYTES),
        name="update",
    )(inner, mine, theirs, weights, first, second, sums, gains, gains_first, gains_second, block, grad)


def on_device(
    tokens, gains_taps, weights, cotangent, weight_first, weight_second, gains_first, gains_second
):
    layers = lax.axis_size("seq") // 2
    inner_word = (lax.axis_index("seq") % 2).astype(jnp.int32).reshape(1)
    own, oth = halves(weights, inner_word)
    block_out, input_grad, gain_sums, mine, theirs = block_step(
        tokens[0], cotangent[0], gains_taps, own, oth, layers
    )
    (
        weight_grad, weight_first_new, weight_second_new, weight_new,
        gains_grad, gains_first_new, gains_second_new, gains_new, block_out, input_grad,
    ) = update(
        inner_word, mine, theirs, weights, weight_first, weight_second,
        gain_sums, gains_taps, gains_first, gains_second, block_out, input_grad,
    )
    return (
        block_out[None],
        input_grad[None],
        weight_grad,
        weight_first_new,
        weight_second_new,
        weight_new,
        gains_grad,
        gains_first_new,
        gains_second_new,
        gains_new,
    )


def solution(mesh):
    tokens, rows, whole = P("shard", "seq", None), P("seq", "shard"), P()
    return jax.shard_map(
        on_device,
        mesh=mesh,
        in_specs=(tokens, whole, rows, tokens, rows, rows, whole, whole),
        out_specs=(tokens, tokens, rows, rows, rows, rows, whole, whole, whole, whole),
        check_vma=False,
    )
```

```python
import functools

import jax
import jax.numpy as jnp
from jax import lax
from jax.experimental import pallas as pl
from jax.experimental.pallas import tpu as pltpu
from jax.sharding import PartitionSpec as P

D = 1536
FF = 6912
STEP = 10
GROUPS = 4
QUARTER = D // GROUPS
UNITS = FF // GROUPS
HALF_Q = QUARTER // 2
HALF_F = UNITS // 2
LANES = 128
PAD_F = -(-HALF_F // LANES) * LANES
WIDE = 256
CONV_COLS = 4 * HALF_Q
UNIT_CHUNKS = (384, 256, PAD_F - 640)
UNIT_STARTS = (0, 384, 640)
WIDTHS = (CONV_COLS,) + tuple(3 * units for units in UNIT_CHUNKS)
STARTS = tuple(sum(WIDTHS[:k]) for k in range(len(WIDTHS)))
SPLIT = 128
REACH = (1, 1, 1, 1)
SLICE = 384
TILE = 16
ROWS = 48

MOMENT_DECAY = 0.9
SQUARE_DECAY = 0.95
ADAM_EPSILON = 1e-08
NORM_EPSILON = 1e-05
WEIGHT_RATE = 0.02
GAIN_RATE = 0.2
WEIGHT_DECAY = 0.1

BF16 = jnp.bfloat16
F32 = jnp.float32
MESH = pl.DeviceIdType.MESH
VMEM_BYTES = 63 * 1024 * 1024


def place():
    seq, shard = lax.axis_index("seq"), lax.axis_index("shard")
    inner, core = lax.rem(seq, 2), lax.rem(shard, 2)
    return seq, shard, inner, core


def partners():
    seq, shard, inner, core = place()
    across = {"seq": seq + 1 - 2 * inner, "shard": shard}
    beside = {"seq": seq, "shard": lax.rem(shard + 2, 4)}
    twin = {"seq": seq, "shard": shard + 1 - 2 * core}
    return across, beside, twin


def remote(src, dst, send, recv, device):
    return pltpu.make_async_remote_copy(
        src_ref=src, dst_ref=dst, send_sem=send, recv_sem=recv, device_id=device, device_id_type=MESH
    )


def line():
    seq, shard, _, _ = place()
    return seq // 2, lambda steps: {"seq": seq + 2 * steps, "shard": shard}


def greet(layers):
    outer, at = line()
    barrier = pltpu.get_barrier_semaphore()
    for device in partners():
        pl.semaphore_signal(barrier, inc=1, device_id=device, device_id_type=MESH)
    for steps in range(1, layers):
        for sign in (1, -1):

            @pl.when(in_line(outer + sign * steps, layers))
            def _():
                pl.semaphore_signal(barrier, inc=1, device_id=at(sign * steps), device_id_type=MESH)

    pl.semaphore_wait(barrier, 3 + layers - 1)


def in_line(index, layers):
    return (index >= 0) & (index < layers)


def allow(credit):
    for device in partners():
        pl.semaphore_signal(credit, inc=1, device_id=device, device_id_type=MESH)


def dot(left, right):
    return jnp.dot(left, right, preferred_element_type=F32)


def dot_rows(left, right):
    return lax.dot_general(left, right, (((1,), (1,)), ((), ())), preferred_element_type=F32)


def dot_columns(left, right):
    return lax.dot_general(left, right, (((0,), (0,)), ((), ())), preferred_element_type=F32)


def aligned(start, size, multiple=16):
    return pl.ds(pl.multiple_of(start, multiple), size)


class Gather:
    def __init__(self, layers, rows, own, oth, outs, send_x, recv_x, send_z, recv_z, local):
        self.layers, self.rows, self.own, self.oth, self.outs = layers, rows, own, oth, outs
        self.send_x, self.recv_x, self.send_z, self.recv_z, self.local = send_x, recv_x, send_z, recv_z, local
        self.seq, _, self.inner, _ = place()
        self.outer, self.at = line()
        self.across = partners()[0]

    def seq_rows(self, index):
        return aligned(index * self.rows, self.rows)

    def layer_rows(self, direction, distance):
        origin = self.outer - distance if direction == 0 else self.outer + distance
        return aligned(origin * 2 * self.rows, 2 * self.rows)

    def copy(self, k, src, dst, direction, distance, hop, piece):
        slot = (k, direction, distance + hop - 1, piece)
        return remote(
            src, dst, self.send_z.at[slot], self.recv_z.at[slot], self.at(hop if direction == 0 else -hop)
        )

    def goes(self, direction, hop):
        return in_line(self.outer + (hop if direction == 0 else -hop), self.layers)

    def has_come(self, direction, distance):
        return in_line(self.outer + (-distance if direction == 0 else distance), self.layers)

    def hops(self, k, distance):
        return range(1, min(REACH[k], self.layers - 1 - distance) + 1)

    def own_copy(self, k, direction, hop):
        src = self.own.at[:, pl.ds(STARTS[k], WIDTHS[k])]
        return self.copy(k, src, self.outs[k].at[self.seq_rows(self.seq)], direction, 0, hop, 0)

    def other_copy(self, k, direction, hop):
        there = self.outs[k].at[self.seq_rows(self.seq + 1 - 2 * self.inner)]
        return self.copy(k, there, there, direction, 0, hop, 1)

    def pass_copy(self, k, direction, distance, hop):
        ref = self.outs[k].at[self.layer_rows(direction, distance)]
        return self.copy(k, ref, ref, direction, distance, hop, 0)

    def x_copy(self, k):
        return remote(
            self.oth.at[:, pl.ds(STARTS[k], WIDTHS[k])],
            self.outs[k].at[self.seq_rows(self.seq)],
            self.send_x.at[k],
            self.recv_x.at[k],
            self.across,
        )

    def l_copy(self, k):
        return pltpu.make_async_copy(
            self.own.at[:, pl.ds(STARTS[k], WIDTHS[k])], self.outs[k].at[self.seq_rows(self.seq)], self.local.at[k]
        )

    def exchange(self, k):
        self.x_copy(k).start()
        self.l_copy(k).start()

    def send_own(self, k):
        for hop in self.hops(k, 0):
            for direction in (0, 1):

                @pl.when(self.goes(direction, hop))
                def _():
                    self.own_copy(k, direction, hop).start()

    def send_other(self, k):
        self.x_copy(k).wait_recv()
        for hop in self.hops(k, 0):
            for direction in (0, 1):

                @pl.when(self.goes(direction, hop))
                def _():
                    self.other_copy(k, direction, hop).start()

    def step(self, k, distance):
        for direction in (0, 1):

            @pl.when(self.has_come(direction, distance))
            def _():
                if distance <= REACH[k]:
                    origin = self.outer - distance if direction == 0 else self.outer + distance
                    for piece in (0, 1):
                        index = 2 * origin + (self.inner if piece == 0 else 1 - self.inner)
                        ref = self.outs[k].at[self.seq_rows(index)]
                        self.copy(k, ref, ref, direction, distance - 1, 1, piece).wait_recv()
                else:
                    ref = self.outs[k].at[self.layer_rows(direction, distance)]
                    self.copy(k, ref, ref, direction, distance - 1, 1, 0).wait_recv()
                if distance % REACH[k] == 0:
                    for hop in self.hops(k, distance):

                        @pl.when(self.goes(direction, hop))
                        def _():
                            self.pass_copy(k, direction, distance, hop).start()

        if distance == self.layers - 1:
            self.l_copy(k).wait()

    def steps(self, k, first, last=None):
        last = self.layers - 1 if last is None else min(last, self.layers - 1)
        for distance in range(first, last + 1):
            self.step(k, distance)

    def finish(self):
        for k in range(len(self.outs)):
            self.x_copy(k).wait_send()
            for distance in range(0, self.layers - 1, REACH[k]):
                for hop in self.hops(k, distance):
                    for direction in (0, 1):

                        @pl.when(self.goes(direction, hop) & self.has_come(direction, distance))
                        def _():
                            if distance == 0:
                                self.own_copy(k, direction, hop).wait_send()
                                self.other_copy(k, direction, hop).wait_send()
                            else:
                                self.pass_copy(k, direction, distance, hop).wait_send()


class Reduce:
    def __init__(self, layers, rows, grads, slots, stage, spare, total, outgoing, mine, theirs, sems):
        self.layers, self.rows, self.grads, self.slots = layers, rows, grads, slots
        self.stage, self.spare, self.total, self.outgoing = stage, spare, total, outgoing
        self.mine, self.theirs = mine, theirs
        self.send_g, self.recv_g, self.fetched, self.fetches, self.stored, self.send_o, self.recv_o = sems
        _, _, self.inner, _ = place()
        self.outer, self.at = line()
        self.across = partners()[0]

    def owner(self, direction, distance):
        return self.outer + distance if direction == 0 else self.outer - distance

    def upstream(self, direction, steps):
        return in_line(self.outer - steps if direction == 0 else self.outer + steps, self.layers)

    def block(self, k, owner):
        return self.grads[k].at[aligned(owner * 2 * self.rows, 2 * self.rows), pl.ds(0, WIDTHS[k])]

    def copy(self, k, src, direction, distance):
        hop = 1 if distance % 2 else 2
        slot = (direction, distance - 1)
        return remote(
            src,
            self.slots[k].at[slot],
            self.send_g.at[(k,) + slot],
            self.recv_g.at[(k,) + slot],
            self.at(hop if direction == 0 else -hop),
        )

    def send(self, k, direction, distance):
        self.copy(k, self.block(k, self.owner(direction, distance)), direction, distance).start()

    def direct(self, k, part=None, ends=None, least=1, most=None):
        at_end = (self.outer == 0) | (self.outer == self.layers - 1)
        for distance in range(most or self.layers - 1, least - 1, -1):
            for direction in (0, 1):
                owner = self.owner(direction, distance)
                here = in_line(owner, self.layers)
                if part is not None:
                    here = here & (owner * 2 * self.rows // SLICE == part)
                if ends is not None:
                    here = here & (at_end if ends else jnp.logical_not(at_end))
                if distance % 2 == 0:
                    here = here & jnp.logical_not(self.upstream(direction, 1))

                @pl.when(here)
                def _():
                    self.send(k, direction, distance)

    def fetch(self, k, direction, distance):
        slot = self.slots[k].at[direction, distance - 1]
        self.copy(k, slot, direction, distance).wait_recv()
        held = self.stage.at[:, pl.ds(0, WIDTHS[k])]
        copy = pltpu.make_async_copy(slot, held, self.fetched)
        copy.start()
        copy.wait()

    def tiles(self, body):
        def step(n, _):
            body(aligned(n * TILE, TILE))
            return 0

        lax.fori_loop(0, 2 * self.rows // TILE, step, 0)

    def join(self, k):
        cols = pl.ds(0, WIDTHS[k])
        for distance in range((self.layers - 1) // 2 * 2, 0, -2):
            for direction in (0, 1):
                owner = self.owner(direction, distance)

                @pl.when(in_line(owner, self.layers) & self.upstream(direction, 1))
                def _():
                    def add(tile):
                        base = self.owner(direction, distance) * 2 * self.rows
                        rows = pl.ds(pl.multiple_of(base + tile.start, 16), TILE)
                        ref = self.grads[k]
                        ref[rows, cols] = (
                            ref[rows, cols].astype(F32) + self.stage[tile, cols].astype(F32)
                        ).astype(BF16)

                    self.fetch(k, direction, distance + 1)
                    self.tiles(add)
                    if distance + 2 < self.layers:

                        @pl.when(self.upstream(direction, 2))
                        def _():
                            self.fetch(k, direction, distance + 2)
                            self.tiles(add)

                    self.send(k, direction, distance)

    def final(self, k, before=None):
        cols = pl.ds(0, WIDTHS[k])
        came = [(distance, direction) for distance in (1, 2) for direction in (0, 1) if distance < self.layers]

        def fetch(n, distance, direction):
            return pltpu.make_async_copy(
                self.slots[k].at[direction, distance - 1],
                self.spare.at[pl.ds(n * 2 * self.rows, 2 * self.rows), cols],
                self.fetches.at[n],
            )

        for n, (distance, direction) in enumerate(came):

            @pl.when(self.upstream(direction, distance))
            def _():
                self.copy(k, self.slots[k].at[direction, distance - 1], direction, distance).wait_recv()
                fetch(n, distance, direction).start()

        if before is not None:
            self.store(before).wait()

        here, there = self.inner * self.rows, (1 - self.inner) * self.rows

        def each(base, body):
            def step(n, _):
                body(base + n * TILE, n * TILE)
                return 0

            lax.fori_loop(0, self.rows // TILE, step, 0)

        for n, (distance, direction) in enumerate(came):

            @pl.when(self.upstream(direction, distance))
            def _():
                fetch(n, distance, direction).wait()

        def add_up(flags):
            def total(rows):
                value = self.grads[k][aligned(self.outer * 2 * self.rows + rows, TILE), cols].astype(F32)
                for n, flag in enumerate(flags):
                    if flag:
                        value = value + self.spare[aligned(n * 2 * self.rows + rows, TILE), cols].astype(F32)
                return value

            def send(rows, at):
                self.outgoing[aligned(at, TILE), pl.ds(STARTS[k], WIDTHS[k])] = total(rows).astype(BF16)

            def keep(rows, at):
                self.total[aligned(at, TILE), cols] = total(rows)

            each(there, send)
            self.over(k).start()
            each(here, keep)
            self.store(k).start()

        patterns = {}
        for place_in_line in range(self.layers):
            flags = tuple(
                0 <= (place_in_line - distance if direction == 0 else place_in_line + distance) < self.layers
                for distance, direction in came
            )
            patterns.setdefault(flags, []).append(place_in_line)
        for flags, places in patterns.items():
            here_now = functools.reduce(jnp.logical_or, [self.outer == p for p in places])

            @pl.when(here_now)
            def _():
                add_up(flags)

    def over(self, k):
        wide = pl.ds(STARTS[k], WIDTHS[k])
        return remote(
            self.outgoing.at[:, wide], self.theirs.at[:, wide], self.send_o.at[k], self.recv_o.at[k], self.across
        )

    def store(self, k):
        return pltpu.make_async_copy(
            self.total.at[:, pl.ds(0, WIDTHS[k])], self.mine.at[:, pl.ds(STARTS[k], WIDTHS[k])], self.stored.at[k]
        )

    def wait_sent(self, k):
        for distance in range(1, self.layers):
            for direction in (0, 1):
                owner = self.owner(direction, distance)

                @pl.when(in_line(owner, self.layers))
                def _():
                    self.copy(k, self.block(k, owner), direction, distance).wait_send()

    def finish(self, before):
        self.store(before).wait()
        for k in range(len(self.grads)):
            self.over(k).wait()


class Spread:
    slots = range(11)

    def __init__(self, buf, seg, send, recv):
        self.buf, self.seg, self.send, self.recv = buf, seg, send, recv

    def index(self, n):
        _, shard, inner, core = place()
        row, flip, other = (n // 2) % 2, n // 4, n % 2
        return 2 * (lax.rem(shard + 2 * row, 4) + other * (1 - 2 * core)) + inner + flip * (1 - 2 * inner)

    def copy(self, slot):
        across, beside, twin = partners()
        low, high, whole = (0, SPLIT), (SPLIT, self.seg - SPLIT), (0, self.seg)
        n, (first, size), device = {
            0: (0, low, across),
            9: (0, high, across),
            1: (0, high, beside),
            10: (0, low, beside),
            2: (0, whole, twin),
            3: (4, low, beside),
            4: (4, whole, twin),
            5: (2, high, across),
            6: (2, whole, twin),
            7: (6, low, twin),
            8: (6, high, twin),
        }[slot]
        ref = self.buf.at[aligned(self.index(n) * self.seg + first, size)]
        return remote(ref, ref, self.send.at[slot], self.recv.at[slot], device)

    def push(self, *slots):
        for slot in slots:
            self.copy(slot).start()

    def came(self, *slots):
        for slot in slots:
            self.copy(slot).wait_recv()

    def start(self):
        self.push(0, 1, 9, 10, 2)

    def first(self):
        self.came(1)
        self.push(5)
        self.came(0)
        self.push(3)

    def near(self):
        self.came(10)
        self.push(6)
        self.came(9)
        self.push(4)

    def far(self):
        self.came(3)
        self.push(7)
        self.came(5)
        self.push(8)

    def sent(self):
        for slot in self.slots:
            self.copy(slot).wait_send()

    def end(self):
        self.came(2, 4, 6, 7, 8)
        self.sent()

    def before(self, n):
        return {
            1: (lambda: self.came(2),),
            2: (self.first, self.near),
            3: (lambda: self.came(6),),
            5: (lambda: self.came(4),),
            6: (self.far,),
            7: (lambda: self.came(7, 8),),
        }.get(n, ())


class Collect:
    def __init__(self, part, seg, total, pair, near, joined, send, recv):
        self.part, self.seg, self.total = part, seg, total
        self.pair, self.near, self.joined, self.send, self.recv = pair, near, joined, send, recv
        _, self.shard, self.inner, core = place()
        self.twin_shard = self.shard + 1 - 2 * core
        self.low, self.high, self.whole = (0, SPLIT), (SPLIT, seg - SPLIT), (0, seg)
        self.cols = pl.ds(0, D)

    def index(self, s, k):
        row, flip = 1 - k % 2, 1 - k // 2
        return 2 * lax.rem(s + 2 * row, 4) + self.inner + flip * (1 - 2 * self.inner)

    def pair_copy(self, k):
        src = self.part.at[aligned(self.index(self.twin_shard, k) * self.seg, self.seg), self.cols]
        return remote(src, self.pair.at[k], self.send.at[k], self.recv.at[k], partners()[2])

    def copy(self, slot):
        across, beside, _ = partners()
        src, dst, (first, size), device = {
            4: (self.pair.at[0], self.joined, self.low, across),
            5: (self.pair.at[0], self.joined, self.high, beside),
            6: (self.pair.at[1], self.near.at[0], self.low, across),
            7: (self.pair.at[2], self.near.at[1], self.high, beside),
            8: (self.pair.at[2], self.near.at[1], self.low, beside),
            9: (self.pair.at[1], self.near.at[0], self.high, across),
        }[slot]
        rows = pl.ds(first, size)
        return remote(src.at[rows], dst.at[rows], self.send.at[slot], self.recv.at[slot], device)

    def over(self, span, body):
        def step(n, _):
            body(aligned(span[0] + n * 16, 16))
            return 0

        lax.fori_loop(0, span[1] // 16, step, 0)

    def mine(self, k, rows):
        return self.part[aligned(self.index(self.shard, k) * self.seg + rows.start, 16), self.cols].astype(F32)

    def add_pair(self, k):
        def add(rows):
            self.pair[k, rows] = (self.mine(k, rows) + self.pair[k, rows].astype(F32)).astype(BF16)

        self.pair_copy(k).wait_recv()
        self.over(self.whole, add)
        for slot in ((4, 5), (6,), (7,))[k]:
            self.copy(slot).start()

    def add_own(self):
        def add(rows):
            self.total[rows] = self.mine(3, rows) + self.pair[3, rows].astype(F32)

        self.pair_copy(3).wait_recv()
        self.over(self.whole, add)

    def pass_on(self):
        for slot, k, span, after in ((4, 2, self.low, 8), (5, 1, self.high, 9)):

            def add(rows):
                self.pair[k, rows] = (self.pair[k, rows].astype(F32) + self.joined[rows].astype(F32)).astype(BF16)

            self.copy(slot).wait_recv()
            self.over(span, add)
            self.copy(after).start()

    def push(self):
        for k in range(4):
            self.pair_copy(k).start()

    def make(self, n, produce):
        k, own = n // 2, n % 2
        produce(self.index(jnp.where(own == 1, self.shard, self.twin_shard), k))

        @pl.when(own == 0)
        def _():
            self.pair_copy(k).start()

        for m in range(3):

            @pl.when(n == 2 * m + 1)
            def _():
                self.add_pair(m)
                if m == 2:
                    self.pass_on()

        pl.when(n == 7)(self.add_own)

    def end(self):
        def add(rows):
            near = self.near[0, rows].astype(F32) + self.near[1, rows].astype(F32)
            self.total[rows] = self.total[rows] + near

        for slots, span in (((6, 8), self.low), ((7, 9), self.high)):
            for slot in slots:
                self.copy(slot).wait_recv()
            self.over(span, add)
        for k in range(4):
            self.pair_copy(k).wait_send()
        for slot in range(4, 10):
            self.copy(slot).wait_send()


def norm_scale(values):
    return lax.rsqrt(jnp.mean(values * values, axis=-1, keepdims=True) + NORM_EPSILON)


def by_rows(rows, body, carry=0):
    def step(n, carry):
        return body(aligned(n * ROWS, ROWS), carry)

    return lax.fori_loop(0, rows // ROWS, step, carry)


def norm_back(values, gain, upstream):
    scale = norm_scale(values)
    scaled = gain * upstream
    inner = jnp.mean(scaled * values, axis=-1, keepdims=True)
    return (
        scale * scaled - values * scale * scale * scale * inner,
        jnp.sum(upstream * values * scale, axis=0, keepdims=True),
    )


REFS = (
    "tok", "cot", "gains", "own", "oth",
    "block_out", "input_grad", "gain_sums", "mine", "theirs", "n1_held", "slot0", "slot1", "slot2", "slot3",
    "w0", "w1", "w2", "w3", "seq_a", "seq_b", "du", "act", "c_all", "gated", "mixed", "resid", "dresid", "total",
    "pair", "near", "joined", "g1", "g2", "g3", "stage", "sum", "outgoing", "tap_sums", "gain_in", "gain_line",
    "held", "local", "send_x", "recv_x", "send_z", "recv_z", "send_s", "recv_s", "send_c", "recv_c", "credit",
    "halo_send", "halo_recv", "send_g", "recv_g", "fetched", "fetches", "stored", "send_o", "recv_o",
    "send_a", "recv_a", "send_l", "recv_l",
)


def block_kernel(layers, rows, *all_refs):
    r = dict(zip(REFS, all_refs, strict=True))
    tok, cot, gains = r["tok"], r["cot"], r["gains"]
    seq_a, seq_b, du, act = r["seq_a"], r["seq_b"], r["du"], r["act"]
    c_all, gated, mixed, total = r["c_all"], r["gated"], r["mixed"], r["total"]
    weights = (r["w0"], r["w1"], r["w2"], r["w3"])
    seg = tok.shape[0]
    _, shard, inner, _ = place()
    outer, at = line()
    me = 2 * shard + inner
    my_rows = aligned(me * seg, seg)
    chunks = list(zip(range(1, 1 + len(UNIT_CHUNKS)), UNIT_STARTS, UNIT_CHUNKS))
    gather = Gather(
        layers, rows, r["own"], r["oth"], weights,
        r["send_x"], r["recv_x"], r["send_z"], r["recv_z"], r["local"],
    )
    reduce = Reduce(
        layers, rows, (r["w2"], r["g1"], r["g2"], r["g3"]), (r["slot0"], r["slot1"], r["slot2"], r["slot3"]),
        r["stage"], r["w1"], r["sum"], r["outgoing"], r["mine"], r["theirs"],
        (r["send_g"], r["recv_g"], r["fetched"], r["fetches"], r["stored"], r["send_o"], r["recv_o"]),
    )

    def spread(buf, n):
        return Spread(buf, seg, r["send_s"].at[n], r["recv_s"].at[n])

    def collect(part, n):
        return Collect(part, seg, total, r["pair"], r["near"], r["joined"], r["send_c"].at[n], r["recv_c"].at[n])

    one, up, two, three = spread(seq_a, 0), spread(seq_b, 1), spread(seq_a, 2), spread(seq_a, 3)
    branch, down, feed, inputs = collect(seq_a, 0), collect(seq_b, 1), collect(du, 2), collect(seq_a, 3)
    lanes = lax.broadcasted_iota(jnp.int32, (seg, WIDE), 1) < HALF_Q
    taps = pltpu.roll(gains[...], lax.rem(D - shard * QUARTER - inner * HALF_Q, D), 1)[2:5, :WIDE]
    kept = pl.ds(D, WIDE)
    sums, tap_sums = r["gain_sums"], r["tap_sums"]

    def block(t):
        return aligned(t * seg, seg)

    def mine(part):
        return pl.ds(pl.multiple_of(me * seg + part.start, 16), part.size)

    def first_norm():
        def rows(part, _):
            values = tok[part].astype(F32)
            seq_a[mine(part)] = (values * norm_scale(values) * gains[0:1, :]).astype(BF16)
            return 0

        by_rows(seg, rows)

    def up_start():
        seq_b[my_rows] = cot[...]
        up.start()

    def held():
        return pltpu.make_async_copy(seq_a, r["n1_held"], r["held"])

    def reload():
        return pltpu.make_async_copy(r["n1_held"], seq_b, r["held"])

    def project(s):
        for i in (0, 1):
            parts = dot(seq_a[block(2 * s + i)], weights[0][...])
            b = jnp.where(lanes, parts[:, :WIDE], 0.0)
            c = pltpu.roll(parts[:, 128 : 128 + 384], 384 - 64, 1)[:, :WIDE]
            x = parts[:, 384 : 384 + WIDE]
            c_all[s, pl.ds(i * seg, seg)] = jnp.where(lanes, c, 0.0)
            gated[s, pl.ds(8 + i * seg, seg)] = (b * x).astype(BF16).astype(F32)

    def ahead():
        return remote(
            gated.at[:, pl.ds(2 * seg, 8)], gated.at[:, pl.ds(0, 8)], r["halo_send"].at[0], r["halo_recv"].at[0], at(1)
        )

    def halo():
        pl.when(outer < layers - 1)(lambda: ahead().start())

        @pl.when(outer == 0)
        def _():
            gated[:, pl.ds(0, 8)] = jnp.zeros((GROUPS, 8, WIDE), F32)

    def convolved(s, i):
        return (
            taps[0:1, :] * gated[s, pl.ds(6 + i * seg, seg)]
            + taps[1:2, :] * gated[s, pl.ds(7 + i * seg, seg)]
            + taps[2:3, :] * gated[s, pl.ds(8 + i * seg, seg)]
        )

    def convolve(t):
        for i in (0, 1):

            @pl.when(t % 2 == i)
            def _():
                s = t // 2
                mixed[block(t)] = pltpu.roll(c_all[s, pl.ds(i * seg, seg)] * convolved(s, i), 64, 1).astype(BF16)

        seq_a[block(t)] = dot_rows(mixed[block(t)], weights[0][:, pl.ds(512, WIDE)]).astype(BF16)

    def branch_end():
        branch.end()
        allow(r["credit"].at[0])

    def second_norm():
        def rows(part, _):
            values = tok[part].astype(F32) + total[part]
            r["resid"][part] = values
            seq_a[mine(part)] = (values * norm_scale(values) * gains[1:2, :]).astype(BF16)
            return 0

        by_rows(seg, rows)
        pl.semaphore_wait(r["credit"].at[0], 3)

    def hidden(k, start, units, t):
        ref, here = weights[k], block(t)
        gate = dot(seq_a[here], ref[:, pl.ds(0, units)])
        upval = dot(seq_a[here], ref[:, pl.ds(units, units)])
        dact = dot(seq_b[here], ref[:, pl.ds(2 * units, units)])
        sigma = jax.nn.sigmoid(gate)
        silu = gate * sigma
        act[here, pl.ds(start, units)] = (silu * upval).astype(BF16)
        dgate = dact * upval * sigma * (1.0 + gate * (1.0 - sigma))
        du[here, pl.ds(2 * start, units)] = dgate.astype(BF16)
        du[here, pl.ds(2 * start + units, units)] = (dact * silu).astype(BF16)

    def slice_of(n):
        return jnp.where(outer < layers // 2, D // SLICE - 1 - n, n)

    def gate_up_grads(k, start, units, n):
        part = slice_of(n)
        left = seq_a[:, aligned(part * SLICE, SLICE, 128)]
        reduce.grads[k][aligned(part * SLICE, SLICE), pl.ds(0, 2 * units)] = dot_columns(
            left, du[:, pl.ds(2 * start, 2 * units)]
        ).astype(BF16)

    def down_grads(k, start, units, n):
        part = slice_of(n)
        left = seq_b[:, aligned(part * SLICE, SLICE, 128)]
        reduce.grads[k][aligned(part * SLICE, SLICE), pl.ds(2 * units, units)] = dot_columns(
            left, act[:, pl.ds(start, units)]
        ).astype(BF16)

    def grads(k, start, units, n):
        gate_up_grads(k, start, units, n)
        down_grads(k, start, units, n)
        reduce.direct(k, slice_of(n), ends=True)

    def second(t):
        here = block(t)
        seq_b[here] = sum(
            dot_rows(du[here, pl.ds(2 * start, 2 * units)], weights[k][:, pl.ds(0, 2 * units)])
            for k, start, units in chunks
        ).astype(BF16)

    def down_end():
        down.end()
        reload().start()
        allow(r["credit"].at[1])

    def forward(t):
        here = block(t)
        du[here, pl.ds(0, D)] = sum(
            dot_rows(act[here, pl.ds(start, units)], weights[k][:, pl.ds(2 * units, units)])
            for k, start, units in chunks
        ).astype(BF16)

    def second_back():
        def rows(part, gain):
            dpart, dgain = norm_back(r["resid"][part], gains[1:2, :], total[part])
            dresid = cot[part].astype(F32) + dpart
            r["dresid"][part] = dresid
            seq_a[mine(part)] = dresid.astype(BF16)
            return gain + dgain

        sums[...] = jnp.zeros(sums.shape, F32)
        tap_sums[...] = jnp.zeros(tap_sums.shape, F32)
        sums[1:2, pl.ds(0, D)] = by_rows(seg, rows, jnp.zeros((1, D), F32))
        pl.semaphore_wait(r["credit"].at[1], 3)

    def mix_back(t):
        s, here = t // 2, block(t)
        dmixed = pltpu.roll(dot(seq_a[here], weights[0][:, pl.ds(512, WIDE)]), WIDE - 64, 1)
        dmixed = jnp.where(lanes, dmixed, 0.0)
        for i in (0, 1):

            @pl.when(t % 2 == i)
            def _():
                du[here, kept] = (dmixed * convolved(s, i)).astype(BF16)
                c_all[s, pl.ds(i * seg, seg)] = dmixed * c_all[s, pl.ds(i * seg, seg)]

    def after():
        return remote(
            c_all.at[:, pl.ds(0, 8)], c_all.at[:, pl.ds(2 * seg, 8)], r["halo_send"].at[1], r["halo_recv"].at[1], at(-1)
        )

    def halo_back():
        pl.when(outer > 0)(lambda: after().start())

        @pl.when(outer == layers - 1)
        def _():
            c_all[:, pl.ds(2 * seg, 8)] = jnp.zeros((GROUPS, 8, WIDE), F32)

    def conv_back(n):
        for i in (0, 1):
            pl.when(n // GROUPS == i)(functools.partial(conv_back_half, n % GROUPS, i))

    def conv_back_half(s, i):
        t = block(2 * s + i)
        dconv = c_all[s, pl.ds(i * seg, seg)]
        dgated = (
            taps[2:3, :] * dconv
            + taps[1:2, :] * c_all[s, pl.ds(1 + i * seg, seg)]
            + taps[0:1, :] * c_all[s, pl.ds(2 + i * seg, seg)]
        )
        parts = dot(seq_b[t], weights[0][:, pl.ds(0, 640)])
        db = dgated * parts[:, 384:640]
        dx = dgated * parts[:, :WIDE]
        dc = jnp.concatenate([du[t, kept].astype(F32), jnp.zeros((seg, 128), F32)], axis=1)
        dc = pltpu.roll(dc, 64, 1)
        act[t, pl.ds(0, 128)] = db[:, :128].astype(BF16)
        act[t, pl.ds(128, 128)] = (db[:, 128:] + dc[:, :128]).astype(BF16)
        act[t, pl.ds(256, 128)] = dc[:, 128:256].astype(BF16)
        act[t, pl.ds(384, WIDE)] = dx.astype(BF16)
        act[t, pl.ds(640, 128)] = jnp.zeros((seg, 128), BF16)
        for k in range(3):
            moved = gated[s, pl.ds(6 + k + i * seg, seg)]
            tap_sums[k : k + 1] = tap_sums[k : k + 1] + jnp.sum(dconv * moved, axis=0, keepdims=True)

    def conv_grads(n):
        part = slice_of(n)
        held_rows, cols = aligned(part * SLICE, SLICE), aligned(part * SLICE, SLICE, 128)
        ref = reduce.grads[0]
        of_parts = dot_columns(seq_b[:, cols], act[:, pl.ds(0, CONV_COLS)])
        ref[held_rows, pl.ds(0, 512)] = of_parts[:, :512].astype(BF16)
        of_mixed = dot_columns(seq_a[:, cols], mixed[...])
        ref[held_rows, pl.ds(512, WIDE)] = (of_parts[:, 512:] + of_mixed).astype(BF16)
        reduce.direct(0, part)

    def feed_end():
        feed.end()
        allow(r["credit"].at[2])
        r["block_out"][...] = (r["resid"][...] + total[...]).astype(BF16)

    def first(t):
        here = block(t)
        seq_a[here] = dot_rows(act[here, pl.ds(0, 640)], weights[0][:, pl.ds(0, 640)]).astype(BF16)

    def first_back():
        def rows(part, gain):
            dpart, dgain = norm_back(tok[part].astype(F32), gains[0:1, :], total[part])
            r["input_grad"][part] = (r["dresid"][part] + dpart).astype(BF16)
            return gain + dgain

        sums[0:1, pl.ds(0, D)] = by_rows(seg, rows, jnp.zeros((1, D), F32))
        sums[2:5, aligned(me * WIDE, WIDE, 128)] = tap_sums[0:3]

    def gains_across(n):
        return remote(sums, r["gain_in"].at[n], r["send_a"].at[n], r["recv_a"].at[n], partners()[n])

    def gains_add(n):
        gains_across(n).wait()
        sums[...] = sums[...] + r["gain_in"][n]

    def line_copy(sign, steps):
        slot = (0 if sign > 0 else 1, steps - 1)
        return remote(
            sums, r["gain_line"].at[slot], r["send_l"].at[slot], r["recv_l"].at[slot], at(sign * steps)
        )

    def gains_line():
        for steps in range(1, layers):
            for sign in (1, -1):
                pl.when(in_line(outer + sign * steps, layers))(line_copy(sign, steps).start)

    def gains_end():
        for steps in range(1, layers):
            for sign in (1, -1):
                pl.when(in_line(outer + sign * steps, layers))(line_copy(sign, steps).wait_send)
                pl.when(in_line(outer - sign * steps, layers))(line_copy(sign, steps).wait_recv)

        own_sums = sums[...]
        for origin in range(layers):
            for steps in range(1, layers):
                for sign in (1, -1):

                    @pl.when((outer - sign * steps == origin))
                    def _():
                        came = r["gain_line"][0 if sign > 0 else 1, steps - 1]
                        sums[...] = came if origin == 0 else sums[...] + came

            if origin > 0:

                @pl.when(outer == origin)
                def _():
                    sums[...] = sums[...] + own_sums

    def end():
        reduce.finish(0)
        for k in range(len(WIDTHS)):
            reduce.wait_sent(k)
        pl.when(outer < layers - 1)(lambda: ahead().wait_send())
        pl.when(outer > 0)(lambda: after().wait_send())

    def start():
        greet(layers)

    def hold():
        held().start()

    def hold_end():
        held().wait()

    def halo_end():
        pl.when(outer > 0)(lambda: ahead().wait_recv())

    def reload_end():
        reload().wait()

    def halo_back_end():
        pl.when(outer < layers - 1)(lambda: after().wait_recv())

    def feed_credit():
        pl.semaphore_wait(r["credit"].at[2], 3)

    def from_spread(moved, body):
        def step(n):
            for m in range(8):
                if moved.before(m):

                    @pl.when(n == m)
                    def _():
                        for act in moved.before(m):
                            act()

            body(moved.index(n))

        return step

    def each(body, *cases):
        return [functools.partial(body, *(case if isinstance(case, tuple) else (case,))) for case in cases]

    every = range(len(WIDTHS))
    exchange, send_own, send_other = (
        each(body, *every) for body in (gather.exchange, gather.send_own, gather.send_other)
    )
    step = [each(gather.steps, (k, 1, 1), (k, 2, 2), (k, 3)) for k in every]
    join = each(reduce.join, *every)
    final = each(reduce.final, (0, 3), 1, (2, 1), (3, 2))
    feed_pair = each(feed.add_pair, 0, 1, 2)
    gain_send = [lambda n=n: gains_across(n).start() for n in range(3)]
    gain_add = each(gains_add, 0, 1, 2)
    d1 = functools.partial(reduce.direct, 1, ends=False)
    d2 = functools.partial(reduce.direct, 2, ends=False)
    d3_far = functools.partial(reduce.direct, 3, least=2)
    d3_near = functools.partial(reduce.direct, 3, most=1)
    blocks, parts = 2 * GROUPS, D // SLICE
    proj = Loop(GROUPS, project)
    mix = Loop(blocks, lambda n: branch.make(n, convolve))
    hid1 = Loop(blocks, from_spread(two, functools.partial(hidden, *chunks[0])))
    hid2, hid3 = (Loop(blocks, functools.partial(hidden, *chunk)) for chunk in chunks[1:])
    grad1, grad2 = (Loop(parts, functools.partial(grads, *chunk)) for chunk in chunks[:2])
    down3 = Loop(parts, functools.partial(down_grads, *chunks[2]))
    back2 = Loop(blocks, lambda n: down.make(n, second))
    gate3 = Loop(parts, functools.partial(gate_up_grads, *chunks[2]))
    ffn = Loop(blocks, forward)
    back_mix = Loop(blocks, from_spread(three, mix_back))
    back_conv = Loop(blocks, conv_back)
    grad0 = Loop(parts, conv_grads)
    back1 = Loop(blocks, lambda n: inputs.make(n, first))
    play(
        [
            start, send_own[0], exchange[0], first_norm, send_own[3], one.start, send_other[0], exchange[1],
            step[0][0], one.first, up_start, step[0][1], send_other[1], exchange[2], one.near, one.far, send_own[1],
            step[0][2], one.end, proj[0], proj[1], hold, proj[2], up.first, proj[3], halo, halo_end, step[1][0],
            hold_end, mix[0], mix[1], mix[2], mix[3], send_own[2], mix[4], mix[5], mix[6], up.near, step[1][1],
            exchange[3], up.far, up.end, mix[7], branch_end, second_norm, send_other[2], two.start, step[1][2],
            hid1[0], send_other[3], hid1[1], hid1[2], step[2][0], hid1[3], hid1[4], hid1[5], step[3][0], hid1[6],
            hid1[7], two.sent, grad1[0], grad1[1], grad1[2], step[2][1], grad1[3], step[2][2], hid2[0], hid2[1],
            hid2[2], hid2[3], hid2[4], step[3][1], d1, hid2[5], hid2[6], hid2[7], grad2[0], grad2[1], grad2[2],
            step[3][2], grad2[3], hid3[0], hid3[1], hid3[2], hid3[3], hid3[4], hid3[5], hid3[6], hid3[7], down3[0],
            down3[1], down3[2], down3[3], d2, back2[0], back2[1], back2[2], join[1], back2[3], back2[4], back2[5],
            back2[6], back2[7], gate3[0], gate3[1], gate3[2], gate3[3], d3_far, down_end, second_back, join[2],
            three.start, back_mix[0], ffn[0], ffn[1], ffn[2], ffn[3], ffn[4], ffn[5], ffn[6], ffn[7], feed.push,
            reload_end, back_mix[1], back_mix[2], back_mix[3], feed_pair[0], back_mix[4], back_mix[5], feed_pair[1],
            gather.finish, back_mix[6], final[1], back_mix[7], three.sent, halo_back, back_conv[0], back_conv[1],
            back_conv[2], feed_pair[2], halo_back_end, d3_near, back_conv[3], back_conv[4], feed.pass_on, join[3],
            final[2], back_conv[5], back_conv[6], back_conv[7], grad0[0], feed.add_own, grad0[1], grad0[2],
            grad0[3], feed_end, feed_credit, back1[0], back1[1], back1[2], join[0], back1[3], back1[4], back1[5],
            back1[6], back1[7], final[3], inputs.end, first_back, gain_send[0], gain_add[0], gain_send[1], final[0],
            gain_add[1], gain_send[2], gain_add[2], gains_line, gains_end, end,
        ]
    )


class Loop:
    def __init__(self, count, body):
        self.count, self.body = count, body

    def __getitem__(self, n):
        return (self, n)


def play(order):
    order = list(order)
    while order:
        entry = order.pop(0)
        if not isinstance(entry, tuple):
            entry()
            continue
        loop, _ = entry
        between = {}
        for n in range(1, loop.count):
            between[n] = []
            while order[0] != (loop, n):
                between[n].append(order.pop(0))
            order.pop(0)

        def turn(n, _):
            for m, acts in between.items():
                if acts:

                    @pl.when(n == m)
                    def _():
                        play(acts)

            loop.body(n)
            return 0

        lax.fori_loop(0, loop.count, turn, 0)


def block_step(tok, cot, gains, own, oth, layers):
    rows, seg = own.shape[0], tok.shape[0]
    count = len(WIDTHS)
    tokens = 2 * GROUPS * seg
    vmem, anywhere = pl.BlockSpec(memory_space=pltpu.VMEM), pl.BlockSpec(memory_space=pl.ANY)
    shape, scratch = jax.ShapeDtypeStruct, pltpu.VMEM
    dma, regular = pltpu.SemaphoreType.DMA, pltpu.SemaphoreType.REGULAR
    hops = layers - 1
    wide, biggest = sum(WIDTHS), max(WIDTHS)
    out_shape = [
        shape((seg, D), BF16),
        shape((seg, D), BF16),
        shape((8, 2 * GROUPS * WIDE), F32),
        shape((rows, wide), F32),
        shape((rows, wide), BF16),
        shape((tokens, D), BF16),
    ] + [shape((2, hops, 2 * rows, width), BF16) for width in WIDTHS]
    scratch_shapes = (
        [scratch((D, width), BF16) for width in WIDTHS]
        + [
            scratch((tokens, D), BF16),
            scratch((tokens, D), BF16),
            scratch((tokens, 2 * PAD_F), BF16),
            scratch((tokens, PAD_F), BF16),
            scratch((GROUPS, 8 + 2 * seg, WIDE), F32),
            scratch((GROUPS, 8 + 2 * seg, WIDE), F32),
            scratch((tokens, WIDE), BF16),
            scratch((seg, D), F32),
            scratch((seg, D), F32),
            scratch((seg, D), F32),
            scratch((4, seg, D), BF16),
            scratch((2, seg, D), BF16),
            scratch((seg, D), BF16),
        ]
        + [scratch((D, width), BF16) for width in WIDTHS[1:]]
        + [
            scratch((2 * rows, biggest), BF16),
            scratch((rows, biggest), F32),
            scratch((rows, wide), BF16),
            scratch((8, WIDE), F32),
            scratch((3, 8, 2 * GROUPS * WIDE), F32),
            scratch((2, hops, 8, 2 * GROUPS * WIDE), F32),
            dma,
            dma((count,)),
            dma((count,)),
            dma((count,)),
            dma((count, 2, hops, 2)),
            dma((count, 2, hops, 2)),
            dma((4, 11)),
            dma((4, 11)),
            dma((4, 10)),
            dma((4, 10)),
            regular((3,)),
            dma((2,)),
            dma((2,)),
            dma((count, 2, hops)),
            dma((count, 2, hops)),
            dma,
            dma((4,)),
            dma((count,)),
            dma((count,)),
            dma((count,)),
            dma((3,)),
            dma((3,)),
            dma((2, hops)),
            dma((2, hops)),
        ]
    )
    return pl.pallas_call(
        functools.partial(block_kernel, layers, rows),
        out_shape=out_shape,
        in_specs=[vmem] * 3 + [anywhere] * 2,
        out_specs=[vmem] * 3 + [anywhere] * (3 + count),
        scratch_shapes=scratch_shapes,
        compiler_params=pltpu.CompilerParams(
            collective_id=0, has_side_effects=True, vmem_limit_bytes=VMEM_BYTES
        ),
        name="block_step",
    )(tok, cot, gains, own, oth)[:5]


def column_pieces(half):
    pieces = [(m * QUARTER + half * HALF_Q, m * HALF_Q, HALF_Q, 0) for m in range(4)]
    for k, (start, units) in enumerate(zip(UNIT_STARTS, UNIT_CHUNKS), 1):
        real = min(units, HALF_F - start)
        for m in range(3):
            first = 4 * QUARTER + m * UNITS + half * HALF_F + start
            pieces.append((first, STARTS[k] + m * units, real, units - real))
    return pieces


def halves_kernel(inner_ref, weights_ref, own_ref, oth_ref):
    is_low = inner_ref[0] == 0

    def half(h):
        parts = []
        for first, _, width, padding in column_pieces(h):
            parts.append(weights_ref[:, first : first + width])
            if padding:
                parts.append(jnp.zeros((parts[-1].shape[0], padding), F32))
        return jnp.concatenate(parts, axis=1)

    low, high = half(0), half(1)
    own_ref[...] = jnp.where(is_low, low, high).astype(BF16)
    oth_ref[...] = jnp.where(is_low, high, low).astype(BF16)


def band(rows, most):
    return max(size for size in range(16, most + 1, 16) if rows % size == 0)


def halves(weights, inner):
    rows, cols = weights.shape
    wide = sum(WIDTHS)
    size = band(rows, 96)
    by_row = lambda width: pl.BlockSpec((size, width), lambda n: (n, 0))
    return pl.pallas_call(
        halves_kernel,
        grid=(rows // size,),
        out_shape=[jax.ShapeDtypeStruct((rows, wide), BF16)] * 2,
        in_specs=[pl.BlockSpec(memory_space=pltpu.SMEM), by_row(cols)],
        out_specs=[by_row(wide)] * 2,
        compiler_params=pltpu.CompilerParams(vmem_limit_bytes=VMEM_BYTES),
        name="halves",
    )(inner, weights)


def adam_update(param, grad, first, second, rate, decay):
    first_new = MOMENT_DECAY * first + (1.0 - MOMENT_DECAY) * grad
    second_new = SQUARE_DECAY * second + (1.0 - SQUARE_DECAY) * grad * grad
    root = jnp.sqrt(second_new * (1.0 / (1.0 - SQUARE_DECAY**STEP))) + ADAM_EPSILON
    step = first_new * (rate / (1.0 - MOMENT_DECAY**STEP)) / root
    return (first_new, second_new, param * (1.0 - rate * decay) - step)


def update_kernel(
    inner_ref, mine_ref, theirs_ref, weights_ref, first_ref, second_ref, sums_ref, gains_ref, gains_first_ref,
    gains_second_ref, block_ref, input_ref, grad_out, first_out, second_out, weights_out, gains_grad_out,
    gains_first_out, gains_second_out, gains_out, block_out, input_out,
):
    is_low = inner_ref[0] == 0
    mine, theirs = mine_ref[...], theirs_ref[...].astype(F32)
    for half in (0, 1):
        chosen = jnp.where(is_low, mine, theirs) if half == 0 else jnp.where(is_low, theirs, mine)
        for first, own, width, _ in column_pieces(half):
            grad_out[:, first : first + width] = chosen[:, own : own + width]
    first_out[...], second_out[...], weights_out[...] = adam_update(
        weights_ref[...], grad_out[...], first_ref[...], second_ref[...], WEIGHT_RATE, WEIGHT_DECAY
    )

    @pl.when(pl.program_id(0) == 0)
    def _():
        gains_grad_out[0:2] = sums_ref[0:2, :D]
        for n in range(2 * GROUPS):
            gains_grad_out[2:5, n * HALF_Q : (n + 1) * HALF_Q] = sums_ref[2:5, n * WIDE : n * WIDE + HALF_Q]
        gains_first_out[...], gains_second_out[...], gains_out[...] = adam_update(
            gains_ref[...], gains_grad_out[...], gains_first_ref[...], gains_second_ref[...], GAIN_RATE, 0.0
        )
        block_out[...] = block_ref[...]
        input_out[...] = input_ref[...]


def update(inner, mine, theirs, weights, first, second, sums, gains, gains_first, gains_second, block, grad):
    rows, cols = weights.shape
    wide = mine.shape[1]
    size = band(rows, 32)
    by_row = lambda width: pl.BlockSpec((size, width), lambda n: (n, 0))
    whole = lambda values: pl.BlockSpec(values.shape, lambda n: (0, 0))
    shape = jax.ShapeDtypeStruct
    return pl.pallas_call(
        update_kernel,
        grid=(rows // size,),
        out_shape=[shape((rows, cols), F32)] * 4 + [shape(gains.shape, F32)] * 4 + [shape(block.shape, BF16)] * 2,
        in_specs=[pl.BlockSpec(memory_space=pltpu.SMEM)]
        + [by_row(wide)] * 2
        + [by_row(cols)] * 3
        + [whole(sums)]
        + [whole(gains)] * 3
        + [whole(block)] * 2,
        out_specs=[by_row(cols)] * 4 + [whole(gains)] * 4 + [whole(block)] * 2,
        compiler_params=pltpu.CompilerParams(vmem_limit_bytes=VMEM_BYTES),
        name="update",
    )(inner, mine, theirs, weights, first, second, sums, gains, gains_first, gains_second, block, grad)


def on_device(
    tokens, gains_taps, weights, cotangent, weight_first, weight_second, gains_first, gains_second
):
    layers = lax.axis_size("seq") // 2
    inner_word = (lax.axis_index("seq") % 2).astype(jnp.int32).reshape(1)
    own, oth = halves(weights, inner_word)
    block_out, input_grad, gain_sums, mine, theirs = block_step(
        tokens[0], cotangent[0], gains_taps, own, oth, layers
    )
    (
        weight_grad, weight_first_new, weight_second_new, weight_new,
        gains_grad, gains_first_new, gains_second_new, gains_new, block_out, input_grad,
    ) = update(
        inner_word, mine, theirs, weights, weight_first, weight_second,
        gain_sums, gains_taps, gains_first, gains_second, block_out, input_grad,
    )
    return (
        block_out[None],
        input_grad[None],
        weight_grad,
        weight_first_new,
        weight_second_new,
        weight_new,
        gains_grad,
        gains_first_new,
        gains_second_new,
        gains_new,
    )


def solution(mesh):
    tokens, rows, whole = P("shard", "seq", None), P("seq", "shard"), P()
    return jax.shard_map(
        on_device,
        mesh=mesh,
        in_specs=(tokens, whole, rows, tokens, rows, rows, whole, whole),
        out_specs=(tokens, tokens, rows, rows, rows, rows, whole, whole, whole, whole),
        check_vma=False,
    )
```

```python
import functools

import jax
import jax.numpy as jnp
from jax import lax
from jax.experimental import pallas as pl
from jax.experimental.pallas import tpu as pltpu
from jax.sharding import PartitionSpec as P

D = 1536
FF = 6912
STEP = 10
GROUPS = 4
QUARTER = D // GROUPS
UNITS = FF // GROUPS
HALF_Q = QUARTER // 2
HALF_F = UNITS // 2
LANES = 128
PAD_F = -(-HALF_F // LANES) * LANES
WIDE = 256
CONV_COLS = 4 * HALF_Q
UNIT_CHUNKS = (384, 256, PAD_F - 640)
UNIT_STARTS = (0, 384, 640)
WIDTHS = (CONV_COLS,) + tuple(3 * units for units in UNIT_CHUNKS)
STARTS = tuple(sum(WIDTHS[:k]) for k in range(len(WIDTHS)))
SPLIT = 128
REACH = (1, 1, 1, 1)
SLICE = 384
TILE = 16
ROWS = 48

MOMENT_DECAY = 0.9
SQUARE_DECAY = 0.95
ADAM_EPSILON = 1e-08
NORM_EPSILON = 1e-05
WEIGHT_RATE = 0.02
GAIN_RATE = 0.2
WEIGHT_DECAY = 0.1

BF16 = jnp.bfloat16
F32 = jnp.float32
MESH = pl.DeviceIdType.MESH
VMEM_BYTES = 63 * 1024 * 1024


def place():
    seq, shard = lax.axis_index("seq"), lax.axis_index("shard")
    inner, core = lax.rem(seq, 2), lax.rem(shard, 2)
    return seq, shard, inner, core


def partners():
    seq, shard, inner, core = place()
    across = {"seq": seq + 1 - 2 * inner, "shard": shard}
    beside = {"seq": seq, "shard": lax.rem(shard + 2, 4)}
    twin = {"seq": seq, "shard": shard + 1 - 2 * core}
    return across, beside, twin


def remote(src, dst, send, recv, device):
    return pltpu.make_async_remote_copy(
        src_ref=src, dst_ref=dst, send_sem=send, recv_sem=recv, device_id=device, device_id_type=MESH
    )


def line():
    seq, shard, _, _ = place()
    return seq // 2, lambda steps: {"seq": seq + 2 * steps, "shard": shard}


def greet(layers):
    outer, at = line()
    barrier = pltpu.get_barrier_semaphore()
    for device in partners():
        pl.semaphore_signal(barrier, inc=1, device_id=device, device_id_type=MESH)
    for steps in range(1, layers):
        for sign in (1, -1):

            @pl.when(in_line(outer + sign * steps, layers))
            def _():
                pl.semaphore_signal(barrier, inc=1, device_id=at(sign * steps), device_id_type=MESH)

    pl.semaphore_wait(barrier, 3 + layers - 1)


def in_line(index, layers):
    return (index >= 0) & (index < layers)


def allow(credit):
    for device in partners():
        pl.semaphore_signal(credit, inc=1, device_id=device, device_id_type=MESH)


def dot(left, right):
    return jnp.dot(left, right, preferred_element_type=F32)


def dot_rows(left, right):
    return lax.dot_general(left, right, (((1,), (1,)), ((), ())), preferred_element_type=F32)


def dot_columns(left, right):
    return lax.dot_general(left, right, (((0,), (0,)), ((), ())), preferred_element_type=F32)


def aligned(start, size, multiple=16):
    return pl.ds(pl.multiple_of(start, multiple), size)


class Gather:
    def __init__(self, layers, rows, own, oth, outs, send_x, recv_x, send_z, recv_z, local):
        self.layers, self.rows, self.own, self.oth, self.outs = layers, rows, own, oth, outs
        self.send_x, self.recv_x, self.send_z, self.recv_z, self.local = send_x, recv_x, send_z, recv_z, local
        self.seq, _, self.inner, _ = place()
        self.outer, self.at = line()
        self.across = partners()[0]

    def seq_rows(self, index):
        return aligned(index * self.rows, self.rows)

    def layer_rows(self, direction, distance):
        origin = self.outer - distance if direction == 0 else self.outer + distance
        return aligned(origin * 2 * self.rows, 2 * self.rows)

    def copy(self, k, src, dst, direction, distance, hop, piece):
        slot = (k, direction, distance + hop - 1, piece)
        return remote(
            src, dst, self.send_z.at[slot], self.recv_z.at[slot], self.at(hop if direction == 0 else -hop)
        )

    def goes(self, direction, hop):
        return in_line(self.outer + (hop if direction == 0 else -hop), self.layers)

    def has_come(self, direction, distance):
        return in_line(self.outer + (-distance if direction == 0 else distance), self.layers)

    def hops(self, k, distance):
        return range(1, min(REACH[k], self.layers - 1 - distance) + 1)

    def own_copy(self, k, direction, hop):
        src = self.own.at[:, pl.ds(STARTS[k], WIDTHS[k])]
        return self.copy(k, src, self.outs[k].at[self.seq_rows(self.seq)], direction, 0, hop, 0)

    def other_copy(self, k, direction, hop):
        there = self.outs[k].at[self.seq_rows(self.seq + 1 - 2 * self.inner)]
        return self.copy(k, there, there, direction, 0, hop, 1)

    def pass_copy(self, k, direction, distance, hop):
        ref = self.outs[k].at[self.layer_rows(direction, distance)]
        return self.copy(k, ref, ref, direction, distance, hop, 0)

    def x_copy(self, k):
        return remote(
            self.oth.at[:, pl.ds(STARTS[k], WIDTHS[k])],
            self.outs[k].at[self.seq_rows(self.seq)],
            self.send_x.at[k],
            self.recv_x.at[k],
            self.across,
        )

    def l_copy(self, k):
        return pltpu.make_async_copy(
            self.own.at[:, pl.ds(STARTS[k], WIDTHS[k])], self.outs[k].at[self.seq_rows(self.seq)], self.local.at[k]
        )

    def exchange(self, k):
        self.x_copy(k).start()
        self.l_copy(k).start()

    def send_own(self, k):
        for hop in self.hops(k, 0):
            for direction in (0, 1):

                @pl.when(self.goes(direction, hop))
                def _():
                    self.own_copy(k, direction, hop).start()

    def send_other(self, k):
        self.x_copy(k).wait_recv()
        for hop in self.hops(k, 0):
            for direction in (0, 1):

                @pl.when(self.goes(direction, hop))
                def _():
                    self.other_copy(k, direction, hop).start()

    def step(self, k, distance):
        for direction in (0, 1):

            @pl.when(self.has_come(direction, distance))
            def _():
                if distance <= REACH[k]:
                    origin = self.outer - distance if direction == 0 else self.outer + distance
                    for piece in (0, 1):
                        index = 2 * origin + (self.inner if piece == 0 else 1 - self.inner)
                        ref = self.outs[k].at[self.seq_rows(index)]
                        self.copy(k, ref, ref, direction, distance - 1, 1, piece).wait_recv()
                else:
                    ref = self.outs[k].at[self.layer_rows(direction, distance)]
                    self.copy(k, ref, ref, direction, distance - 1, 1, 0).wait_recv()
                if distance % REACH[k] == 0:
                    for hop in self.hops(k, distance):

                        @pl.when(self.goes(direction, hop))
                        def _():
                            self.pass_copy(k, direction, distance, hop).start()

        if distance == self.layers - 1:
            self.l_copy(k).wait()

    def steps(self, k, first, last=None):
        last = self.layers - 1 if last is None else min(last, self.layers - 1)
        for distance in range(first, last + 1):
            self.step(k, distance)

    def finish(self):
        for k in range(len(self.outs)):
            self.x_copy(k).wait_send()
            for distance in range(0, self.layers - 1, REACH[k]):
                for hop in self.hops(k, distance):
                    for direction in (0, 1):

                        @pl.when(self.goes(direction, hop) & self.has_come(direction, distance))
                        def _():
                            if distance == 0:
                                self.own_copy(k, direction, hop).wait_send()
                                self.other_copy(k, direction, hop).wait_send()
                            else:
                                self.pass_copy(k, direction, distance, hop).wait_send()


class Reduce:
    def __init__(self, layers, rows, grads, slots, stage, spare, total, outgoing, mine, theirs, sems):
        self.layers, self.rows, self.grads, self.slots = layers, rows, grads, slots
        self.stage, self.spare, self.total, self.outgoing = stage, spare, total, outgoing
        self.mine, self.theirs = mine, theirs
        self.send_g, self.recv_g, self.fetched, self.fetches, self.stored, self.send_o, self.recv_o = sems
        _, _, self.inner, _ = place()
        self.outer, self.at = line()
        self.across = partners()[0]

    def owner(self, direction, distance):
        return self.outer + distance if direction == 0 else self.outer - distance

    def upstream(self, direction, steps):
        return in_line(self.outer - steps if direction == 0 else self.outer + steps, self.layers)

    def block(self, k, owner):
        return self.grads[k].at[aligned(owner * 2 * self.rows, 2 * self.rows), pl.ds(0, WIDTHS[k])]

    def copy(self, k, src, direction, distance):
        hop = 1 if distance % 2 else 2
        slot = (direction, distance - 1)
        return remote(
            src,
            self.slots[k].at[slot],
            self.send_g.at[(k,) + slot],
            self.recv_g.at[(k,) + slot],
            self.at(hop if direction == 0 else -hop),
        )

    def send(self, k, direction, distance):
        self.copy(k, self.block(k, self.owner(direction, distance)), direction, distance).start()

    def direct(self, k, part=None, ends=None, least=1, most=None):
        at_end = (self.outer == 0) | (self.outer == self.layers - 1)
        for distance in range(most or self.layers - 1, least - 1, -1):
            for direction in (0, 1):
                owner = self.owner(direction, distance)
                here = in_line(owner, self.layers)
                if part is not None:
                    here = here & (owner * 2 * self.rows // SLICE == part)
                if ends is not None:
                    here = here & (at_end if ends else jnp.logical_not(at_end))
                if distance % 2 == 0:
                    here = here & jnp.logical_not(self.upstream(direction, 1))

                @pl.when(here)
                def _():
                    self.send(k, direction, distance)

    def fetch(self, k, direction, distance):
        slot = self.slots[k].at[direction, distance - 1]
        self.copy(k, slot, direction, distance).wait_recv()
        held = self.stage.at[:, pl.ds(0, WIDTHS[k])]
        copy = pltpu.make_async_copy(slot, held, self.fetched)
        copy.start()
        copy.wait()

    def tiles(self, body):
        def step(n, _):
            body(aligned(n * TILE, TILE))
            return 0

        lax.fori_loop(0, 2 * self.rows // TILE, step, 0)

    def join(self, k):
        cols = pl.ds(0, WIDTHS[k])
        for distance in range((self.layers - 1) // 2 * 2, 0, -2):
            for direction in (0, 1):
                owner = self.owner(direction, distance)

                @pl.when(in_line(owner, self.layers) & self.upstream(direction, 1))
                def _():
                    def add(tile):
                        base = self.owner(direction, distance) * 2 * self.rows
                        rows = pl.ds(pl.multiple_of(base + tile.start, 16), TILE)
                        ref = self.grads[k]
                        ref[rows, cols] = (
                            ref[rows, cols].astype(F32) + self.stage[tile, cols].astype(F32)
                        ).astype(BF16)

                    self.fetch(k, direction, distance + 1)
                    self.tiles(add)
                    if distance + 2 < self.layers:

                        @pl.when(self.upstream(direction, 2))
                        def _():
                            self.fetch(k, direction, distance + 2)
                            self.tiles(add)

                    self.send(k, direction, distance)

    def final(self, k, before=None):
        cols = pl.ds(0, WIDTHS[k])
        came = [(distance, direction) for distance in (1, 2) for direction in (0, 1) if distance < self.layers]

        def fetch(n, distance, direction):
            return pltpu.make_async_copy(
                self.slots[k].at[direction, distance - 1],
                self.spare.at[pl.ds(n * 2 * self.rows, 2 * self.rows), cols],
                self.fetches.at[n],
            )

        for n, (distance, direction) in enumerate(came):

            @pl.when(self.upstream(direction, distance))
            def _():
                self.copy(k, self.slots[k].at[direction, distance - 1], direction, distance).wait_recv()
                fetch(n, distance, direction).start()

        if before is not None:
            self.store(before).wait()

        here, there = self.inner * self.rows, (1 - self.inner) * self.rows

        def each(base, body):
            def step(n, _):
                body(base + n * TILE, n * TILE)
                return 0

            lax.fori_loop(0, self.rows // TILE, step, 0)

        for n, (distance, direction) in enumerate(came):

            @pl.when(self.upstream(direction, distance))
            def _():
                fetch(n, distance, direction).wait()

        def add_up(flags):
            def total(rows):
                value = self.grads[k][aligned(self.outer * 2 * self.rows + rows, TILE), cols].astype(F32)
                for n, flag in enumerate(flags):
                    if flag:
                        value = value + self.spare[aligned(n * 2 * self.rows + rows, TILE), cols].astype(F32)
                return value

            def send(rows, at):
                self.outgoing[aligned(at, TILE), pl.ds(STARTS[k], WIDTHS[k])] = total(rows).astype(BF16)

            def keep(rows, at):
                self.total[aligned(at, TILE), cols] = total(rows)

            each(there, send)
            self.over(k).start()
            each(here, keep)
            self.store(k).start()

        patterns = {}
        for place_in_line in range(self.layers):
            flags = tuple(
                0 <= (place_in_line - distance if direction == 0 else place_in_line + distance) < self.layers
                for distance, direction in came
            )
            patterns.setdefault(flags, []).append(place_in_line)
        for flags, places in patterns.items():
            here_now = functools.reduce(jnp.logical_or, [self.outer == p for p in places])

            @pl.when(here_now)
            def _():
                add_up(flags)

    def over(self, k):
        wide = pl.ds(STARTS[k], WIDTHS[k])
        return remote(
            self.outgoing.at[:, wide], self.theirs.at[:, wide], self.send_o.at[k], self.recv_o.at[k], self.across
        )

    def store(self, k):
        return pltpu.make_async_copy(
            self.total.at[:, pl.ds(0, WIDTHS[k])], self.mine.at[:, pl.ds(STARTS[k], WIDTHS[k])], self.stored.at[k]
        )

    def wait_sent(self, k):
        for distance in range(1, self.layers):
            for direction in (0, 1):
                owner = self.owner(direction, distance)

                @pl.when(in_line(owner, self.layers))
                def _():
                    self.copy(k, self.block(k, owner), direction, distance).wait_send()

    def finish(self, before):
        self.store(before).wait()
        for k in range(len(self.grads)):
            self.over(k).wait()


class Spread:
    slots = range(11)

    def __init__(self, buf, seg, send, recv):
        self.buf, self.seg, self.send, self.recv = buf, seg, send, recv

    def index(self, n):
        _, shard, inner, core = place()
        row, flip, other = (n // 2) % 2, n // 4, n % 2
        return 2 * (lax.rem(shard + 2 * row, 4) + other * (1 - 2 * core)) + inner + flip * (1 - 2 * inner)

    def copy(self, slot):
        across, beside, twin = partners()
        low, high, whole = (0, SPLIT), (SPLIT, self.seg - SPLIT), (0, self.seg)
        n, (first, size), device = {
            0: (0, low, across),
            9: (0, high, across),
            1: (0, high, beside),
            10: (0, low, beside),
            2: (0, whole, twin),
            3: (4, low, beside),
            4: (4, whole, twin),
            5: (2, high, across),
            6: (2, whole, twin),
            7: (6, low, twin),
            8: (6, high, twin),
        }[slot]
        ref = self.buf.at[aligned(self.index(n) * self.seg + first, size)]
        return remote(ref, ref, self.send.at[slot], self.recv.at[slot], device)

    def push(self, *slots):
        for slot in slots:
            self.copy(slot).start()

    def came(self, *slots):
        for slot in slots:
            self.copy(slot).wait_recv()

    def start(self):
        self.push(0, 1, 9, 10, 2)

    def first(self):
        self.came(1)
        self.push(5)
        self.came(0)
        self.push(3)

    def near(self):
        self.came(10)
        self.push(6)
        self.came(9)
        self.push(4)

    def far(self):
        self.came(3)
        self.push(7)
        self.came(5)
        self.push(8)

    def sent(self):
        for slot in self.slots:
            self.copy(slot).wait_send()

    def end(self):
        self.came(2, 4, 6, 7, 8)
        self.sent()

    def before(self, n):
        return {
            1: (lambda: self.came(2),),
            2: (self.first, self.near),
            3: (lambda: self.came(6),),
            5: (lambda: self.came(4),),
            6: (self.far,),
            7: (lambda: self.came(7, 8),),
        }.get(n, ())


class Collect:
    def __init__(self, part, seg, total, pair, near, joined, send, recv):
        self.part, self.seg, self.total = part, seg, total
        self.pair, self.near, self.joined, self.send, self.recv = pair, near, joined, send, recv
        _, self.shard, self.inner, core = place()
        self.twin_shard = self.shard + 1 - 2 * core
        self.low, self.high, self.whole = (0, SPLIT), (SPLIT, seg - SPLIT), (0, seg)
        self.cols = pl.ds(0, D)

    def index(self, s, k):
        row, flip = 1 - k % 2, 1 - k // 2
        return 2 * lax.rem(s + 2 * row, 4) + self.inner + flip * (1 - 2 * self.inner)

    def pair_copy(self, k):
        src = self.part.at[aligned(self.index(self.twin_shard, k) * self.seg, self.seg), self.cols]
        return remote(src, self.pair.at[k], self.send.at[k], self.recv.at[k], partners()[2])

    def copy(self, slot):
        across, beside, _ = partners()
        src, dst, (first, size), device = {
            4: (self.pair.at[0], self.joined, self.low, across),
            5: (self.pair.at[0], self.joined, self.high, beside),
            6: (self.pair.at[1], self.near.at[0], self.low, across),
            7: (self.pair.at[2], self.near.at[1], self.high, beside),
            8: (self.pair.at[2], self.near.at[1], self.low, beside),
            9: (self.pair.at[1], self.near.at[0], self.high, across),
        }[slot]
        rows = pl.ds(first, size)
        return remote(src.at[rows], dst.at[rows], self.send.at[slot], self.recv.at[slot], device)

    def over(self, span, body):
        def step(n, _):
            body(aligned(span[0] + n * 16, 16))
            return 0

        lax.fori_loop(0, span[1] // 16, step, 0)

    def mine(self, k, rows):
        return self.part[aligned(self.index(self.shard, k) * self.seg + rows.start, 16), self.cols].astype(F32)

    def add_pair(self, k):
        def add(rows):
            self.pair[k, rows] = (self.mine(k, rows) + self.pair[k, rows].astype(F32)).astype(BF16)

        self.pair_copy(k).wait_recv()
        self.over(self.whole, add)
        for slot in ((4, 5), (6,), (7,))[k]:
            self.copy(slot).start()

    def add_own(self):
        def add(rows):
            self.total[rows] = self.mine(3, rows) + self.pair[3, rows].astype(F32)

        self.pair_copy(3).wait_recv()
        self.over(self.whole, add)

    def pass_on(self):
        for slot, k, span, after in ((4, 2, self.low, 8), (5, 1, self.high, 9)):

            def add(rows):
                self.pair[k, rows] = (self.pair[k, rows].astype(F32) + self.joined[rows].astype(F32)).astype(BF16)

            self.copy(slot).wait_recv()
            self.over(span, add)
            self.copy(after).start()

    def push(self):
        for k in range(4):
            self.pair_copy(k).start()

    def make(self, n, produce):
        k, own = n // 2, n % 2
        produce(self.index(jnp.where(own == 1, self.shard, self.twin_shard), k))

        @pl.when(own == 0)
        def _():
            self.pair_copy(k).start()

        for m in range(3):

            @pl.when(n == 2 * m + 1)
            def _():
                self.add_pair(m)
                if m == 2:
                    self.pass_on()

        pl.when(n == 7)(self.add_own)

    def end(self):
        def add(rows):
            near = self.near[0, rows].astype(F32) + self.near[1, rows].astype(F32)
            self.total[rows] = self.total[rows] + near

        for slots, span in (((6, 8), self.low), ((7, 9), self.high)):
            for slot in slots:
                self.copy(slot).wait_recv()
            self.over(span, add)
        for k in range(4):
            self.pair_copy(k).wait_send()
        for slot in range(4, 10):
            self.copy(slot).wait_send()


def norm_scale(values):
    return lax.rsqrt(jnp.mean(values * values, axis=-1, keepdims=True) + NORM_EPSILON)


def by_rows(rows, body, carry=0):
    def step(n, carry):
        return body(aligned(n * ROWS, ROWS), carry)

    return lax.fori_loop(0, rows // ROWS, step, carry)


def norm_back(values, gain, upstream):
    scale = norm_scale(values)
    scaled = gain * upstream
    inner = jnp.mean(scaled * values, axis=-1, keepdims=True)
    return (
        scale * scaled - values * scale * scale * scale * inner,
        jnp.sum(upstream * values * scale, axis=0, keepdims=True),
    )


REFS = (
    "tok", "cot", "gains", "own", "oth",
    "block_out", "input_grad", "gain_sums", "mine", "theirs", "n1_held", "slot0", "slot1", "slot2", "slot3",
    "w0", "w1", "w2", "w3", "seq_a", "seq_b", "du", "act", "c_all", "gated", "mixed", "resid", "dresid", "total",
    "pair", "near", "joined", "g1", "g2", "g3", "stage", "sum", "outgoing", "tap_sums", "gain_in", "gain_line",
    "held", "local", "send_x", "recv_x", "send_z", "recv_z", "send_s", "recv_s", "send_c", "recv_c", "credit",
    "halo_send", "halo_recv", "send_g", "recv_g", "fetched", "fetches", "stored", "send_o", "recv_o",
    "send_a", "recv_a", "send_l", "recv_l",
)


def block_kernel(layers, rows, *all_refs):
    r = dict(zip(REFS, all_refs, strict=True))
    tok, cot, gains = r["tok"], r["cot"], r["gains"]
    seq_a, seq_b, du, act = r["seq_a"], r["seq_b"], r["du"], r["act"]
    c_all, gated, mixed, total = r["c_all"], r["gated"], r["mixed"], r["total"]
    weights = (r["w0"], r["w1"], r["w2"], r["w3"])
    seg = tok.shape[0]
    _, shard, inner, _ = place()
    outer, at = line()
    me = 2 * shard + inner
    my_rows = aligned(me * seg, seg)
    chunks = list(zip(range(1, 1 + len(UNIT_CHUNKS)), UNIT_STARTS, UNIT_CHUNKS))
    gather = Gather(
        layers, rows, r["own"], r["oth"], weights,
        r["send_x"], r["recv_x"], r["send_z"], r["recv_z"], r["local"],
    )
    reduce = Reduce(
        layers, rows, (r["w2"], r["g1"], r["g2"], r["g3"]), (r["slot0"], r["slot1"], r["slot2"], r["slot3"]),
        r["stage"], r["w1"], r["sum"], r["outgoing"], r["mine"], r["theirs"],
        (r["send_g"], r["recv_g"], r["fetched"], r["fetches"], r["stored"], r["send_o"], r["recv_o"]),
    )

    def spread(buf, n):
        return Spread(buf, seg, r["send_s"].at[n], r["recv_s"].at[n])

    def collect(part, n):
        return Collect(part, seg, total, r["pair"], r["near"], r["joined"], r["send_c"].at[n], r["recv_c"].at[n])

    one, up, two, three = spread(seq_a, 0), spread(seq_b, 1), spread(seq_a, 2), spread(seq_a, 3)
    branch, down, feed, inputs = collect(seq_a, 0), collect(seq_b, 1), collect(du, 2), collect(seq_a, 3)
    lanes = lax.broadcasted_iota(jnp.int32, (seg, WIDE), 1) < HALF_Q
    taps = pltpu.roll(gains[...], lax.rem(D - shard * QUARTER - inner * HALF_Q, D), 1)[2:5, :WIDE]
    kept = pl.ds(D, WIDE)
    sums, tap_sums = r["gain_sums"], r["tap_sums"]

    def block(t):
        return aligned(t * seg, seg)

    def mine(part):
        return pl.ds(pl.multiple_of(me * seg + part.start, 16), part.size)

    def first_norm():
        def rows(part, _):
            values = tok[part].astype(F32)
            seq_a[mine(part)] = (values * norm_scale(values) * gains[0:1, :]).astype(BF16)
            return 0

        by_rows(seg, rows)

    def up_start():
        seq_b[my_rows] = cot[...]
        up.start()

    def held():
        return pltpu.make_async_copy(seq_a, r["n1_held"], r["held"])

    def reload():
        return pltpu.make_async_copy(r["n1_held"], seq_b, r["held"])

    def project(s):
        for i in (0, 1):
            parts = dot(seq_a[block(2 * s + i)], weights[0][...])
            b = jnp.where(lanes, parts[:, :WIDE], 0.0)
            c = pltpu.roll(parts[:, 128 : 128 + 384], 384 - 64, 1)[:, :WIDE]
            x = parts[:, 384 : 384 + WIDE]
            c_all[s, pl.ds(i * seg, seg)] = jnp.where(lanes, c, 0.0)
            gated[s, pl.ds(8 + i * seg, seg)] = (b * x).astype(BF16).astype(F32)

    def ahead():
        return remote(
            gated.at[:, pl.ds(2 * seg, 8)], gated.at[:, pl.ds(0, 8)], r["halo_send"].at[0], r["halo_recv"].at[0], at(1)
        )

    def halo():
        pl.when(outer < layers - 1)(lambda: ahead().start())

        @pl.when(outer == 0)
        def _():
            gated[:, pl.ds(0, 8)] = jnp.zeros((GROUPS, 8, WIDE), F32)

    def convolved(s, i):
        return (
            taps[0:1, :] * gated[s, pl.ds(6 + i * seg, seg)]
            + taps[1:2, :] * gated[s, pl.ds(7 + i * seg, seg)]
            + taps[2:3, :] * gated[s, pl.ds(8 + i * seg, seg)]
        )

    def convolve(t):
        for i in (0, 1):

            @pl.when(t % 2 == i)
            def _():
                s = t // 2
                mixed[block(t)] = pltpu.roll(c_all[s, pl.ds(i * seg, seg)] * convolved(s, i), 64, 1).astype(BF16)

        seq_a[block(t)] = dot_rows(mixed[block(t)], weights[0][:, pl.ds(512, WIDE)]).astype(BF16)

    def branch_end():
        branch.end()
        allow(r["credit"].at[0])

    def second_norm():
        def rows(part, _):
            values = tok[part].astype(F32) + total[part]
            r["resid"][part] = values
            seq_a[mine(part)] = (values * norm_scale(values) * gains[1:2, :]).astype(BF16)
            return 0

        by_rows(seg, rows)
        pl.semaphore_wait(r["credit"].at[0], 3)

    def hidden(k, start, units, t):
        ref, here = weights[k], block(t)
        gate = dot(seq_a[here], ref[:, pl.ds(0, units)])
        upval = dot(seq_a[here], ref[:, pl.ds(units, units)])
        dact = dot(seq_b[here], ref[:, pl.ds(2 * units, units)])
        sigma = jax.nn.sigmoid(gate)
        silu = gate * sigma
        act[here, pl.ds(start, units)] = (silu * upval).astype(BF16)
        dgate = dact * upval * sigma * (1.0 + gate * (1.0 - sigma))
        du[here, pl.ds(2 * start, units)] = dgate.astype(BF16)
        du[here, pl.ds(2 * start + units, units)] = (dact * silu).astype(BF16)

    def slice_of(n):
        return jnp.where(outer < layers // 2, D // SLICE - 1 - n, n)

    def gate_up_grads(k, start, units, n):
        part = slice_of(n)
        left = seq_a[:, aligned(part * SLICE, SLICE, 128)]
        reduce.grads[k][aligned(part * SLICE, SLICE), pl.ds(0, 2 * units)] = dot_columns(
            left, du[:, pl.ds(2 * start, 2 * units)]
        ).astype(BF16)

    def down_grads(k, start, units, n):
        part = slice_of(n)
        left = seq_b[:, aligned(part * SLICE, SLICE, 128)]
        reduce.grads[k][aligned(part * SLICE, SLICE), pl.ds(2 * units, units)] = dot_columns(
            left, act[:, pl.ds(start, units)]
        ).astype(BF16)

    def grads(k, start, units, n):
        gate_up_grads(k, start, units, n)
        down_grads(k, start, units, n)
        reduce.direct(k, slice_of(n), ends=True)

    def second(t):
        here = block(t)
        seq_b[here] = sum(
            dot_rows(du[here, pl.ds(2 * start, 2 * units)], weights[k][:, pl.ds(0, 2 * units)])
            for k, start, units in chunks
        ).astype(BF16)

    def down_end():
        down.end()
        reload().start()
        allow(r["credit"].at[1])

    def forward(t):
        here = block(t)
        du[here, pl.ds(0, D)] = sum(
            dot_rows(act[here, pl.ds(start, units)], weights[k][:, pl.ds(2 * units, units)])
            for k, start, units in chunks
        ).astype(BF16)

    def second_back():
        def rows(part, gain):
            dpart, dgain = norm_back(r["resid"][part], gains[1:2, :], total[part])
            dresid = cot[part].astype(F32) + dpart
            r["dresid"][part] = dresid
            seq_a[mine(part)] = dresid.astype(BF16)
            return gain + dgain

        sums[...] = jnp.zeros(sums.shape, F32)
        tap_sums[...] = jnp.zeros(tap_sums.shape, F32)
        sums[1:2, pl.ds(0, D)] = by_rows(seg, rows, jnp.zeros((1, D), F32))
        pl.semaphore_wait(r["credit"].at[1], 3)

    def mix_back(t):
        s, here = t // 2, block(t)
        dmixed = pltpu.roll(dot(seq_a[here], weights[0][:, pl.ds(512, WIDE)]), WIDE - 64, 1)
        dmixed = jnp.where(lanes, dmixed, 0.0)
        for i in (0, 1):

            @pl.when(t % 2 == i)
            def _():
                du[here, kept] = (dmixed * convolved(s, i)).astype(BF16)
                c_all[s, pl.ds(i * seg, seg)] = dmixed * c_all[s, pl.ds(i * seg, seg)]

    def after():
        return remote(
            c_all.at[:, pl.ds(0, 8)], c_all.at[:, pl.ds(2 * seg, 8)], r["halo_send"].at[1], r["halo_recv"].at[1], at(-1)
        )

    def halo_back():
        pl.when(outer > 0)(lambda: after().start())

        @pl.when(outer == layers - 1)
        def _():
            c_all[:, pl.ds(2 * seg, 8)] = jnp.zeros((GROUPS, 8, WIDE), F32)

    def conv_back(n):
        for i in (0, 1):
            pl.when(n // GROUPS == i)(functools.partial(conv_back_half, n % GROUPS, i))

    def conv_back_half(s, i):
        t = block(2 * s + i)
        dconv = c_all[s, pl.ds(i * seg, seg)]
        dgated = (
            taps[2:3, :] * dconv
            + taps[1:2, :] * c_all[s, pl.ds(1 + i * seg, seg)]
            + taps[0:1, :] * c_all[s, pl.ds(2 + i * seg, seg)]
        )
        parts = dot(seq_b[t], weights[0][:, pl.ds(0, 640)])
        db = dgated * parts[:, 384:640]
        dx = dgated * parts[:, :WIDE]
        dc = jnp.concatenate([du[t, kept].astype(F32), jnp.zeros((seg, 128), F32)], axis=1)
        dc = pltpu.roll(dc, 64, 1)
        act[t, pl.ds(0, 128)] = db[:, :128].astype(BF16)
        act[t, pl.ds(128, 128)] = (db[:, 128:] + dc[:, :128]).astype(BF16)
        act[t, pl.ds(256, 128)] = dc[:, 128:256].astype(BF16)
        act[t, pl.ds(384, WIDE)] = dx.astype(BF16)
        act[t, pl.ds(640, 128)] = jnp.zeros((seg, 128), BF16)
        for k in range(3):
            moved = gated[s, pl.ds(6 + k + i * seg, seg)]
            tap_sums[k : k + 1] = tap_sums[k : k + 1] + jnp.sum(dconv * moved, axis=0, keepdims=True)

    def conv_grads(n):
        part = slice_of(n)
        held_rows, cols = aligned(part * SLICE, SLICE), aligned(part * SLICE, SLICE, 128)
        ref = reduce.grads[0]
        of_parts = dot_columns(seq_b[:, cols], act[:, pl.ds(0, CONV_COLS)])
        ref[held_rows, pl.ds(0, 512)] = of_parts[:, :512].astype(BF16)
        of_mixed = dot_columns(seq_a[:, cols], mixed[...])
        ref[held_rows, pl.ds(512, WIDE)] = (of_parts[:, 512:] + of_mixed).astype(BF16)
        reduce.direct(0, part)

    def feed_end():
        feed.end()
        allow(r["credit"].at[2])
        r["block_out"][...] = (r["resid"][...] + total[...]).astype(BF16)

    def first(t):
        here = block(t)
        seq_a[here] = dot_rows(act[here, pl.ds(0, 640)], weights[0][:, pl.ds(0, 640)]).astype(BF16)

    def first_back():
        def rows(part, gain):
            dpart, dgain = norm_back(tok[part].astype(F32), gains[0:1, :], total[part])
            r["input_grad"][part] = (r["dresid"][part] + dpart).astype(BF16)
            return gain + dgain

        sums[0:1, pl.ds(0, D)] = by_rows(seg, rows, jnp.zeros((1, D), F32))
        sums[2:5, aligned(me * WIDE, WIDE, 128)] = tap_sums[0:3]

    def gains_across(n):
        return remote(sums, r["gain_in"].at[n], r["send_a"].at[n], r["recv_a"].at[n], partners()[n])

    def gains_add(n):
        gains_across(n).wait()
        sums[...] = sums[...] + r["gain_in"][n]

    def line_copy(sign, steps):
        slot = (0 if sign > 0 else 1, steps - 1)
        return remote(
            sums, r["gain_line"].at[slot], r["send_l"].at[slot], r["recv_l"].at[slot], at(sign * steps)
        )

    def gains_line():
        for steps in range(1, layers):
            for sign in (1, -1):
                pl.when(in_line(outer + sign * steps, layers))(line_copy(sign, steps).start)

    def gains_end():
        for steps in range(1, layers):
            for sign in (1, -1):
                pl.when(in_line(outer + sign * steps, layers))(line_copy(sign, steps).wait_send)
                pl.when(in_line(outer - sign * steps, layers))(line_copy(sign, steps).wait_recv)

        own_sums = sums[...]
        for origin in range(layers):
            for steps in range(1, layers):
                for sign in (1, -1):

                    @pl.when((outer - sign * steps == origin))
                    def _():
                        came = r["gain_line"][0 if sign > 0 else 1, steps - 1]
                        sums[...] = came if origin == 0 else sums[...] + came

            if origin > 0:

                @pl.when(outer == origin)
                def _():
                    sums[...] = sums[...] + own_sums

    def end():
        reduce.finish(0)
        for k in range(len(WIDTHS)):
            reduce.wait_sent(k)
        pl.when(outer < layers - 1)(lambda: ahead().wait_send())
        pl.when(outer > 0)(lambda: after().wait_send())

    def start():
        greet(layers)

    def hold():
        held().start()

    def hold_end():
        held().wait()

    def halo_end():
        pl.when(outer > 0)(lambda: ahead().wait_recv())

    def reload_end():
        reload().wait()

    def halo_back_end():
        pl.when(outer < layers - 1)(lambda: after().wait_recv())

    def feed_credit():
        pl.semaphore_wait(r["credit"].at[2], 3)

    def from_spread(moved, body):
        def step(n):
            for m in range(8):
                if moved.before(m):

                    @pl.when(n == m)
                    def _():
                        for act in moved.before(m):
                            act()

            body(moved.index(n))

        return step

    def each(body, *cases):
        return [functools.partial(body, *(case if isinstance(case, tuple) else (case,))) for case in cases]

    every = range(len(WIDTHS))
    exchange, send_own, send_other = (
        each(body, *every) for body in (gather.exchange, gather.send_own, gather.send_other)
    )
    step = [each(gather.steps, (k, 1, 1), (k, 2, 2), (k, 3)) for k in every]
    join = each(reduce.join, *every)
    final = each(reduce.final, (0, 3), 1, (2, 1), (3, 2))
    feed_pair = each(feed.add_pair, 0, 1, 2)
    gain_send = [lambda n=n: gains_across(n).start() for n in range(3)]
    gain_add = each(gains_add, 0, 1, 2)
    d1 = functools.partial(reduce.direct, 1, ends=False)
    d2 = functools.partial(reduce.direct, 2, ends=False)
    d3_far = functools.partial(reduce.direct, 3, least=2)
    d3_near = functools.partial(reduce.direct, 3, most=1)
    blocks, parts = 2 * GROUPS, D // SLICE
    proj = Loop(GROUPS, project)
    mix = Loop(blocks, lambda n: branch.make(n, convolve))
    hid1 = Loop(blocks, from_spread(two, functools.partial(hidden, *chunks[0])))
    hid2, hid3 = (Loop(blocks, functools.partial(hidden, *chunk)) for chunk in chunks[1:])
    grad1, grad2 = (Loop(parts, functools.partial(grads, *chunk)) for chunk in chunks[:2])
    down3 = Loop(parts, functools.partial(down_grads, *chunks[2]))
    back2 = Loop(blocks, lambda n: down.make(n, second))
    gate3 = Loop(parts, functools.partial(gate_up_grads, *chunks[2]))
    ffn = Loop(blocks, forward)
    back_mix = Loop(blocks, from_spread(three, mix_back))
    back_conv = Loop(blocks, conv_back)
    grad0 = Loop(parts, conv_grads)
    back1 = Loop(blocks, lambda n: inputs.make(n, first))
    play(
        [
            start, send_own[0], send_own[1], exchange[0], exchange[1], send_other[0], first_norm, exchange[2],
            one.start, step[0][0], send_own[2], step[0][1], send_other[2], one.first, one.near, up_start, one.far,
            step[0][2], one.end, send_other[1], hold, proj[0], up.first, proj[1], proj[2], up.near, hold_end,
            proj[3], exchange[3], halo, halo_end, mix[0], step[1][0], mix[1], mix[2], mix[3], mix[4], mix[5],
            mix[6], mix[7], step[1][1], branch_end, up.far, second_norm, two.start, up.end, step[1][2], send_own[3],
            hid1[0], hid1[1], step[2][0], hid1[2], hid1[3], hid1[4], send_other[3], hid1[5], hid1[6], step[2][1],
            hid1[7], two.sent, grad1[0], step[3][0], grad1[1], step[2][2], grad1[2], grad1[3], hid2[0], hid2[1],
            hid2[2], hid2[3], step[3][1], d1, hid2[4], hid2[5], hid2[6], hid2[7], grad2[0], grad2[1], grad2[2],
            grad2[3], step[3][2], hid3[0], hid3[1], hid3[2], hid3[3], hid3[4], hid3[5], hid3[6], hid3[7], down3[0],
            d2, down3[1], down3[2], down3[3], back2[0], back2[1], join[1], back2[2], back2[3], back2[4], back2[5],
            back2[6], back2[7], gate3[0], gate3[1], gate3[2], gate3[3], d3_far, down_end, second_back, three.start,
            ffn[0], ffn[1], ffn[2], ffn[3], ffn[4], ffn[5], ffn[6], ffn[7], back_mix[0], join[2], back_mix[1],
            reload_end, gather.finish, back_mix[2], feed.push, final[1], back_mix[3], feed_pair[0], back_mix[4],
            back_mix[5], feed_pair[1], back_mix[6], back_mix[7], three.sent, halo_back, back_conv[0], final[2],
            back_conv[1], d3_near, back_conv[2], back_conv[3], halo_back_end, back_conv[4], feed_pair[2],
            back_conv[5], back_conv[6], back_conv[7], grad0[0], feed.pass_on, grad0[1], grad0[2], grad0[3],
            feed.add_own, feed_end, feed_credit, back1[0], join[3], back1[1], back1[2], back1[3], back1[4],
            back1[5], join[0], back1[6], back1[7], final[3], inputs.end, first_back, gain_send[0], gain_add[0],
            gain_send[1], final[0], gain_add[1], gain_send[2], gain_add[2], gains_line, gains_end, end,
        ]
    )


class Loop:
    def __init__(self, count, body):
        self.count, self.body = count, body

    def __getitem__(self, n):
        return (self, n)


def play(order):
    order = list(order)
    while order:
        entry = order.pop(0)
        if not isinstance(entry, tuple):
            entry()
            continue
        loop, _ = entry
        between = {}
        for n in range(1, loop.count):
            between[n] = []
            while order[0] != (loop, n):
                between[n].append(order.pop(0))
            order.pop(0)

        def turn(n, _):
            for m, acts in between.items():
                if acts:

                    @pl.when(n == m)
                    def _():
                        play(acts)

            loop.body(n)
            return 0

        lax.fori_loop(0, loop.count, turn, 0)


def block_step(tok, cot, gains, own, oth, layers):
    rows, seg = own.shape[0], tok.shape[0]
    count = len(WIDTHS)
    tokens = 2 * GROUPS * seg
    vmem, anywhere = pl.BlockSpec(memory_space=pltpu.VMEM), pl.BlockSpec(memory_space=pl.ANY)
    shape, scratch = jax.ShapeDtypeStruct, pltpu.VMEM
    dma, regular = pltpu.SemaphoreType.DMA, pltpu.SemaphoreType.REGULAR
    hops = layers - 1
    wide, biggest = sum(WIDTHS), max(WIDTHS)
    out_shape = [
        shape((seg, D), BF16),
        shape((seg, D), BF16),
        shape((8, 2 * GROUPS * WIDE), F32),
        shape((rows, wide), F32),
        shape((rows, wide), BF16),
        shape((tokens, D), BF16),
    ] + [shape((2, hops, 2 * rows, width), BF16) for width in WIDTHS]
    scratch_shapes = (
        [scratch((D, width), BF16) for width in WIDTHS]
        + [
            scratch((tokens, D), BF16),
            scratch((tokens, D), BF16),
            scratch((tokens, 2 * PAD_F), BF16),
            scratch((tokens, PAD_F), BF16),
            scratch((GROUPS, 8 + 2 * seg, WIDE), F32),
            scratch((GROUPS, 8 + 2 * seg, WIDE), F32),
            scratch((tokens, WIDE), BF16),
            scratch((seg, D), F32),
            scratch((seg, D), F32),
            scratch((seg, D), F32),
            scratch((4, seg, D), BF16),
            scratch((2, seg, D), BF16),
            scratch((seg, D), BF16),
        ]
        + [scratch((D, width), BF16) for width in WIDTHS[1:]]
        + [
            scratch((2 * rows, biggest), BF16),
            scratch((rows, biggest), F32),
            scratch((rows, wide), BF16),
            scratch((8, WIDE), F32),
            scratch((3, 8, 2 * GROUPS * WIDE), F32),
            scratch((2, hops, 8, 2 * GROUPS * WIDE), F32),
            dma,
            dma((count,)),
            dma((count,)),
            dma((count,)),
            dma((count, 2, hops, 2)),
            dma((count, 2, hops, 2)),
            dma((4, 11)),
            dma((4, 11)),
            dma((4, 10)),
            dma((4, 10)),
            regular((3,)),
            dma((2,)),
            dma((2,)),
            dma((count, 2, hops)),
            dma((count, 2, hops)),
            dma,
            dma((4,)),
            dma((count,)),
            dma((count,)),
            dma((count,)),
            dma((3,)),
            dma((3,)),
            dma((2, hops)),
            dma((2, hops)),
        ]
    )
    return pl.pallas_call(
        functools.partial(block_kernel, layers, rows),
        out_shape=out_shape,
        in_specs=[vmem] * 3 + [anywhere] * 2,
        out_specs=[vmem] * 3 + [anywhere] * (3 + count),
        scratch_shapes=scratch_shapes,
        compiler_params=pltpu.CompilerParams(
            collective_id=0, has_side_effects=True, vmem_limit_bytes=VMEM_BYTES
        ),
        name="block_step",
    )(tok, cot, gains, own, oth)[:5]


def column_pieces(half):
    pieces = [(m * QUARTER + half * HALF_Q, m * HALF_Q, HALF_Q, 0) for m in range(4)]
    for k, (start, units) in enumerate(zip(UNIT_STARTS, UNIT_CHUNKS), 1):
        real = min(units, HALF_F - start)
        for m in range(3):
            first = 4 * QUARTER + m * UNITS + half * HALF_F + start
            pieces.append((first, STARTS[k] + m * units, real, units - real))
    return pieces


def halves_kernel(inner_ref, weights_ref, own_ref, oth_ref):
    is_low = inner_ref[0] == 0

    def half(h):
        parts = []
        for first, _, width, padding in column_pieces(h):
            parts.append(weights_ref[:, first : first + width])
            if padding:
                parts.append(jnp.zeros((parts[-1].shape[0], padding), F32))
        return jnp.concatenate(parts, axis=1)

    low, high = half(0), half(1)
    own_ref[...] = jnp.where(is_low, low, high).astype(BF16)
    oth_ref[...] = jnp.where(is_low, high, low).astype(BF16)


def band(rows, most):
    return max(size for size in range(16, most + 1, 16) if rows % size == 0)


def halves(weights, inner):
    rows, cols = weights.shape
    wide = sum(WIDTHS)
    size = band(rows, 96)
    by_row = lambda width: pl.BlockSpec((size, width), lambda n: (n, 0))
    return pl.pallas_call(
        halves_kernel,
        grid=(rows // size,),
        out_shape=[jax.ShapeDtypeStruct((rows, wide), BF16)] * 2,
        in_specs=[pl.BlockSpec(memory_space=pltpu.SMEM), by_row(cols)],
        out_specs=[by_row(wide)] * 2,
        compiler_params=pltpu.CompilerParams(vmem_limit_bytes=VMEM_BYTES),
        name="halves",
    )(inner, weights)


def adam_update(param, grad, first, second, rate, decay):
    first_new = MOMENT_DECAY * first + (1.0 - MOMENT_DECAY) * grad
    second_new = SQUARE_DECAY * second + (1.0 - SQUARE_DECAY) * grad * grad
    root = jnp.sqrt(second_new * (1.0 / (1.0 - SQUARE_DECAY**STEP))) + ADAM_EPSILON
    step = first_new * (rate / (1.0 - MOMENT_DECAY**STEP)) / root
    return (first_new, second_new, param * (1.0 - rate * decay) - step)


def update_kernel(
    inner_ref, mine_ref, theirs_ref, weights_ref, first_ref, second_ref, sums_ref, gains_ref, gains_first_ref,
    gains_second_ref, block_ref, input_ref, grad_out, first_out, second_out, weights_out, gains_grad_out,
    gains_first_out, gains_second_out, gains_out, block_out, input_out,
):
    is_low = inner_ref[0] == 0
    mine, theirs = mine_ref[...], theirs_ref[...].astype(F32)
    for half in (0, 1):
        chosen = jnp.where(is_low, mine, theirs) if half == 0 else jnp.where(is_low, theirs, mine)
        for first, own, width, _ in column_pieces(half):
            grad_out[:, first : first + width] = chosen[:, own : own + width]
    first_out[...], second_out[...], weights_out[...] = adam_update(
        weights_ref[...], grad_out[...], first_ref[...], second_ref[...], WEIGHT_RATE, WEIGHT_DECAY
    )

    @pl.when(pl.program_id(0) == 0)
    def _():
        gains_grad_out[0:2] = sums_ref[0:2, :D]
        for n in range(2 * GROUPS):
            gains_grad_out[2:5, n * HALF_Q : (n + 1) * HALF_Q] = sums_ref[2:5, n * WIDE : n * WIDE + HALF_Q]
        gains_first_out[...], gains_second_out[...], gains_out[...] = adam_update(
            gains_ref[...], gains_grad_out[...], gains_first_ref[...], gains_second_ref[...], GAIN_RATE, 0.0
        )
        block_out[...] = block_ref[...]
        input_out[...] = input_ref[...]


def update(inner, mine, theirs, weights, first, second, sums, gains, gains_first, gains_second, block, grad):
    rows, cols = weights.shape
    wide = mine.shape[1]
    size = band(rows, 32)
    by_row = lambda width: pl.BlockSpec((size, width), lambda n: (n, 0))
    whole = lambda values: pl.BlockSpec(values.shape, lambda n: (0, 0))
    shape = jax.ShapeDtypeStruct
    return pl.pallas_call(
        update_kernel,
        grid=(rows // size,),
        out_shape=[shape((rows, cols), F32)] * 4 + [shape(gains.shape, F32)] * 4 + [shape(block.shape, BF16)] * 2,
        in_specs=[pl.BlockSpec(memory_space=pltpu.SMEM)]
        + [by_row(wide)] * 2
        + [by_row(cols)] * 3
        + [whole(sums)]
        + [whole(gains)] * 3
        + [whole(block)] * 2,
        out_specs=[by_row(cols)] * 4 + [whole(gains)] * 4 + [whole(block)] * 2,
        compiler_params=pltpu.CompilerParams(vmem_limit_bytes=VMEM_BYTES),
        name="update",
    )(inner, mine, theirs, weights, first, second, sums, gains, gains_first, gains_second, block, grad)


def on_device(
    tokens, gains_taps, weights, cotangent, weight_first, weight_second, gains_first, gains_second
):
    layers = lax.axis_size("seq") // 2
    inner_word = (lax.axis_index("seq") % 2).astype(jnp.int32).reshape(1)
    own, oth = halves(weights, inner_word)
    block_out, input_grad, gain_sums, mine, theirs = block_step(
        tokens[0], cotangent[0], gains_taps, own, oth, layers
    )
    (
        weight_grad, weight_first_new, weight_second_new, weight_new,
        gains_grad, gains_first_new, gains_second_new, gains_new, block_out, input_grad,
    ) = update(
        inner_word, mine, theirs, weights, weight_first, weight_second,
        gain_sums, gains_taps, gains_first, gains_second, block_out, input_grad,
    )
    return (
        block_out[None],
        input_grad[None],
        weight_grad,
        weight_first_new,
        weight_second_new,
        weight_new,
        gains_grad,
        gains_first_new,
        gains_second_new,
        gains_new,
    )


def solution(mesh):
    tokens, rows, whole = P("shard", "seq", None), P("seq", "shard"), P()
    return jax.shard_map(
        on_device,
        mesh=mesh,
        in_specs=(tokens, whole, rows, tokens, rows, rows, whole, whole),
        out_specs=(tokens, tokens, rows, rows, rows, rows, whole, whole, whole, whole),
        check_vma=False,
    )
```

```python
import functools

import jax
import jax.numpy as jnp
from jax import lax
from jax.experimental import pallas as pl
from jax.experimental.pallas import tpu as pltpu
from jax.sharding import PartitionSpec as P

D = 1536
FF = 6912
STEP = 10
GROUPS = 4
QUARTER = D // GROUPS
UNITS = FF // GROUPS
HALF_Q = QUARTER // 2
HALF_F = UNITS // 2
LANES = 128
PAD_F = -(-HALF_F // LANES) * LANES
WIDE = 256
CONV_COLS = 4 * HALF_Q
UNIT_CHUNKS = (384, 256, PAD_F - 640)
UNIT_STARTS = (0, 384, 640)
WIDTHS = (CONV_COLS,) + tuple(3 * units for units in UNIT_CHUNKS)
STARTS = tuple(sum(WIDTHS[:k]) for k in range(len(WIDTHS)))
SPLIT = 128
REACH = (1, 1, 1, 1)
SLICE = 384
TILE = 16
ROWS = 48

MOMENT_DECAY = 0.9
SQUARE_DECAY = 0.95
ADAM_EPSILON = 1e-08
NORM_EPSILON = 1e-05
WEIGHT_RATE = 0.02
GAIN_RATE = 0.2
WEIGHT_DECAY = 0.1

BF16 = jnp.bfloat16
F32 = jnp.float32
MESH = pl.DeviceIdType.MESH
VMEM_BYTES = 63 * 1024 * 1024


def place():
    seq, shard = lax.axis_index("seq"), lax.axis_index("shard")
    inner, core = lax.rem(seq, 2), lax.rem(shard, 2)
    return seq, shard, inner, core


def partners():
    seq, shard, inner, core = place()
    across = {"seq": seq + 1 - 2 * inner, "shard": shard}
    beside = {"seq": seq, "shard": lax.rem(shard + 2, 4)}
    twin = {"seq": seq, "shard": shard + 1 - 2 * core}
    return across, beside, twin


def remote(src, dst, send, recv, device):
    return pltpu.make_async_remote_copy(
        src_ref=src, dst_ref=dst, send_sem=send, recv_sem=recv, device_id=device, device_id_type=MESH
    )


def line():
    seq, shard, _, _ = place()
    return seq // 2, lambda steps: {"seq": seq + 2 * steps, "shard": shard}


def greet(layers):
    outer, at = line()
    barrier = pltpu.get_barrier_semaphore()
    for device in partners():
        pl.semaphore_signal(barrier, inc=1, device_id=device, device_id_type=MESH)
    for steps in range(1, layers):
        for sign in (1, -1):

            @pl.when(in_line(outer + sign * steps, layers))
            def _():
                pl.semaphore_signal(barrier, inc=1, device_id=at(sign * steps), device_id_type=MESH)

    pl.semaphore_wait(barrier, 3 + layers - 1)


def in_line(index, layers):
    return (index >= 0) & (index < layers)


def allow(credit):
    for device in partners():
        pl.semaphore_signal(credit, inc=1, device_id=device, device_id_type=MESH)


def dot(left, right):
    return jnp.dot(left, right, preferred_element_type=F32)


def dot_rows(left, right):
    return lax.dot_general(left, right, (((1,), (1,)), ((), ())), preferred_element_type=F32)


def dot_columns(left, right):
    return lax.dot_general(left, right, (((0,), (0,)), ((), ())), preferred_element_type=F32)


def aligned(start, size, multiple=16):
    return pl.ds(pl.multiple_of(start, multiple), size)


class Gather:
    def __init__(self, layers, rows, own, oth, outs, send_x, recv_x, send_z, recv_z, local):
        self.layers, self.rows, self.own, self.oth, self.outs = layers, rows, own, oth, outs
        self.send_x, self.recv_x, self.send_z, self.recv_z, self.local = send_x, recv_x, send_z, recv_z, local
        self.seq, _, self.inner, _ = place()
        self.outer, self.at = line()
        self.across = partners()[0]

    def seq_rows(self, index):
        return aligned(index * self.rows, self.rows)

    def layer_rows(self, direction, distance):
        origin = self.outer - distance if direction == 0 else self.outer + distance
        return aligned(origin * 2 * self.rows, 2 * self.rows)

    def copy(self, k, src, dst, direction, distance, hop, piece):
        slot = (k, direction, distance + hop - 1, piece)
        return remote(
            src, dst, self.send_z.at[slot], self.recv_z.at[slot], self.at(hop if direction == 0 else -hop)
        )

    def goes(self, direction, hop):
        return in_line(self.outer + (hop if direction == 0 else -hop), self.layers)

    def has_come(self, direction, distance):
        return in_line(self.outer + (-distance if direction == 0 else distance), self.layers)

    def hops(self, k, distance):
        return range(1, min(REACH[k], self.layers - 1 - distance) + 1)

    def own_copy(self, k, direction, hop):
        src = self.own.at[:, pl.ds(STARTS[k], WIDTHS[k])]
        return self.copy(k, src, self.outs[k].at[self.seq_rows(self.seq)], direction, 0, hop, 0)

    def other_copy(self, k, direction, hop):
        there = self.outs[k].at[self.seq_rows(self.seq + 1 - 2 * self.inner)]
        return self.copy(k, there, there, direction, 0, hop, 1)

    def pass_copy(self, k, direction, distance, hop):
        ref = self.outs[k].at[self.layer_rows(direction, distance)]
        return self.copy(k, ref, ref, direction, distance, hop, 0)

    def x_copy(self, k):
        return remote(
            self.oth.at[:, pl.ds(STARTS[k], WIDTHS[k])],
            self.outs[k].at[self.seq_rows(self.seq)],
            self.send_x.at[k],
            self.recv_x.at[k],
            self.across,
        )

    def l_copy(self, k):
        return pltpu.make_async_copy(
            self.own.at[:, pl.ds(STARTS[k], WIDTHS[k])], self.outs[k].at[self.seq_rows(self.seq)], self.local.at[k]
        )

    def exchange(self, k):
        self.x_copy(k).start()
        self.l_copy(k).start()

    def send_own(self, k):
        for hop in self.hops(k, 0):
            for direction in (0, 1):

                @pl.when(self.goes(direction, hop))
                def _():
                    self.own_copy(k, direction, hop).start()

    def send_other(self, k):
        self.x_copy(k).wait_recv()
        for hop in self.hops(k, 0):
            for direction in (0, 1):

                @pl.when(self.goes(direction, hop))
                def _():
                    self.other_copy(k, direction, hop).start()

    def step(self, k, distance):
        for direction in (0, 1):

            @pl.when(self.has_come(direction, distance))
            def _():
                if distance <= REACH[k]:
                    origin = self.outer - distance if direction == 0 else self.outer + distance
                    for piece in (0, 1):
                        index = 2 * origin + (self.inner if piece == 0 else 1 - self.inner)
                        ref = self.outs[k].at[self.seq_rows(index)]
                        self.copy(k, ref, ref, direction, distance - 1, 1, piece).wait_recv()
                else:
                    ref = self.outs[k].at[self.layer_rows(direction, distance)]
                    self.copy(k, ref, ref, direction, distance - 1, 1, 0).wait_recv()
                if distance % REACH[k] == 0:
                    for hop in self.hops(k, distance):

                        @pl.when(self.goes(direction, hop))
                        def _():
                            self.pass_copy(k, direction, distance, hop).start()

        if distance == self.layers - 1:
            self.l_copy(k).wait()

    def steps(self, k, first, last=None):
        last = self.layers - 1 if last is None else min(last, self.layers - 1)
        for distance in range(first, last + 1):
            self.step(k, distance)

    def finish(self):
        for k in range(len(self.outs)):
            self.x_copy(k).wait_send()
            for distance in range(0, self.layers - 1, REACH[k]):
                for hop in self.hops(k, distance):
                    for direction in (0, 1):

                        @pl.when(self.goes(direction, hop) & self.has_come(direction, distance))
                        def _():
                            if distance == 0:
                                self.own_copy(k, direction, hop).wait_send()
                                self.other_copy(k, direction, hop).wait_send()
                            else:
                                self.pass_copy(k, direction, distance, hop).wait_send()


class Reduce:
    def __init__(self, layers, rows, grads, slots, stage, spare, total, outgoing, mine, theirs, sems):
        self.layers, self.rows, self.grads, self.slots = layers, rows, grads, slots
        self.stage, self.spare, self.total, self.outgoing = stage, spare, total, outgoing
        self.mine, self.theirs = mine, theirs
        self.send_g, self.recv_g, self.fetched, self.fetches, self.stored, self.send_o, self.recv_o = sems
        _, _, self.inner, _ = place()
        self.outer, self.at = line()
        self.across = partners()[0]

    def owner(self, direction, distance):
        return self.outer + distance if direction == 0 else self.outer - distance

    def upstream(self, direction, steps):
        return in_line(self.outer - steps if direction == 0 else self.outer + steps, self.layers)

    def block(self, k, owner):
        return self.grads[k].at[aligned(owner * 2 * self.rows, 2 * self.rows), pl.ds(0, WIDTHS[k])]

    def copy(self, k, src, direction, distance):
        slot = (direction, distance - 1)
        return remote(
            src,
            self.slots[k].at[slot],
            self.send_g.at[(k,) + slot],
            self.recv_g.at[(k,) + slot],
            self.at(1 if direction == 0 else -1),
        )

    def send(self, k, direction, distance):
        self.copy(k, self.block(k, self.owner(direction, distance)), direction, distance).start()

    def direct(self, k, part=None, least=1, most=None):
        for distance in range(most or self.layers - 1, least - 1, -1):
            for direction in (0, 1):
                owner = self.owner(direction, distance)
                here = in_line(owner, self.layers) & jnp.logical_not(self.upstream(direction, 1))
                if part is not None:
                    here = here & (owner * 2 * self.rows // SLICE == part)

                @pl.when(here)
                def _():
                    self.send(k, direction, distance)

    def fetch(self, k, direction, distance):
        slot = self.slots[k].at[direction, distance - 1]
        self.copy(k, slot, direction, distance).wait_recv()
        held = self.stage.at[:, pl.ds(0, WIDTHS[k])]
        copy = pltpu.make_async_copy(slot, held, self.fetched)
        copy.start()
        copy.wait()

    def tiles(self, body):
        def step(n, _):
            body(aligned(n * TILE, TILE))
            return 0

        lax.fori_loop(0, 2 * self.rows // TILE, step, 0)

    def join(self, k, most, least):
        cols = pl.ds(0, WIDTHS[k])
        for distance in range(most, least - 1, -1):
            for direction in (0, 1):
                owner = self.owner(direction, distance)

                @pl.when(in_line(owner, self.layers) & self.upstream(direction, 1))
                def _():
                    def add(tile):
                        base = self.owner(direction, distance) * 2 * self.rows
                        rows = pl.ds(pl.multiple_of(base + tile.start, 16), TILE)
                        ref = self.grads[k]
                        ref[rows, cols] = (
                            ref[rows, cols].astype(F32) + self.stage[tile, cols].astype(F32)
                        ).astype(BF16)

                    self.fetch(k, direction, distance + 1)
                    self.tiles(add)
                    self.send(k, direction, distance)

    def final(self, k, before=None):
        cols = pl.ds(0, WIDTHS[k])
        came = [(1, 0), (1, 1)]

        def fetch(n, distance, direction):
            return pltpu.make_async_copy(
                self.slots[k].at[direction, distance - 1],
                self.spare.at[pl.ds(n * 2 * self.rows, 2 * self.rows), cols],
                self.fetches.at[n],
            )

        for n, (distance, direction) in enumerate(came):

            @pl.when(self.upstream(direction, distance))
            def _():
                self.copy(k, self.slots[k].at[direction, distance - 1], direction, distance).wait_recv()
                fetch(n, distance, direction).start()

        if before is not None:
            self.store(before).wait()

        here, there = self.inner * self.rows, (1 - self.inner) * self.rows

        def each(base, body):
            def step(n, _):
                body(base + n * TILE, n * TILE)
                return 0

            lax.fori_loop(0, self.rows // TILE, step, 0)

        for n, (distance, direction) in enumerate(came):

            @pl.when(self.upstream(direction, distance))
            def _():
                fetch(n, distance, direction).wait()

        def add_up(flags):
            def total(rows):
                value = self.grads[k][aligned(self.outer * 2 * self.rows + rows, TILE), cols].astype(F32)
                for n, flag in enumerate(flags):
                    if flag:
                        value = value + self.spare[aligned(n * 2 * self.rows + rows, TILE), cols].astype(F32)
                return value

            def send(rows, at):
                self.outgoing[aligned(at, TILE), pl.ds(STARTS[k], WIDTHS[k])] = total(rows).astype(BF16)

            def keep(rows, at):
                self.total[aligned(at, TILE), cols] = total(rows)

            each(there, send)
            self.over(k).start()
            each(here, keep)
            self.store(k).start()

        patterns = {}
        for place_in_line in range(self.layers):
            flags = tuple(
                0 <= (place_in_line - distance if direction == 0 else place_in_line + distance) < self.layers
                for distance, direction in came
            )
            patterns.setdefault(flags, []).append(place_in_line)
        for flags, places in patterns.items():
            here_now = functools.reduce(jnp.logical_or, [self.outer == p for p in places])

            @pl.when(here_now)
            def _():
                add_up(flags)

    def over(self, k):
        wide = pl.ds(STARTS[k], WIDTHS[k])
        return remote(
            self.outgoing.at[:, wide], self.theirs.at[:, wide], self.send_o.at[k], self.recv_o.at[k], self.across
        )

    def store(self, k):
        return pltpu.make_async_copy(
            self.total.at[:, pl.ds(0, WIDTHS[k])], self.mine.at[:, pl.ds(STARTS[k], WIDTHS[k])], self.stored.at[k]
        )

    def wait_sent(self, k):
        for distance in range(1, self.layers):
            for direction in (0, 1):
                owner = self.owner(direction, distance)

                @pl.when(in_line(owner, self.layers))
                def _():
                    self.copy(k, self.block(k, owner), direction, distance).wait_send()

    def finish(self, before):
        self.store(before).wait()
        for k in range(len(self.grads)):
            self.over(k).wait()


class Spread:
    slots = range(11)

    def __init__(self, buf, seg, send, recv):
        self.buf, self.seg, self.send, self.recv = buf, seg, send, recv

    def index(self, n):
        _, shard, inner, core = place()
        row, flip, other = (n // 2) % 2, n // 4, n % 2
        return 2 * (lax.rem(shard + 2 * row, 4) + other * (1 - 2 * core)) + inner + flip * (1 - 2 * inner)

    def copy(self, slot):
        across, beside, twin = partners()
        low, high, whole = (0, SPLIT), (SPLIT, self.seg - SPLIT), (0, self.seg)
        n, (first, size), device = {
            0: (0, low, across),
            9: (0, high, across),
            1: (0, high, beside),
            10: (0, low, beside),
            2: (0, whole, twin),
            3: (4, low, beside),
            4: (4, whole, twin),
            5: (2, high, across),
            6: (2, whole, twin),
            7: (6, low, twin),
            8: (6, high, twin),
        }[slot]
        ref = self.buf.at[aligned(self.index(n) * self.seg + first, size)]
        return remote(ref, ref, self.send.at[slot], self.recv.at[slot], device)

    def push(self, *slots):
        for slot in slots:
            self.copy(slot).start()

    def came(self, *slots):
        for slot in slots:
            self.copy(slot).wait_recv()

    def start(self):
        self.push(0, 1, 9, 10, 2)

    def first(self):
        self.came(1)
        self.push(5)
        self.came(0)
        self.push(3)

    def near(self):
        self.came(10)
        self.push(6)
        self.came(9)
        self.push(4)

    def far(self):
        self.came(3)
        self.push(7)
        self.came(5)
        self.push(8)

    def sent(self):
        for slot in self.slots:
            self.copy(slot).wait_send()

    def end(self):
        self.came(2, 4, 6, 7, 8)
        self.sent()

    def before(self, n):
        return {
            1: (lambda: self.came(2),),
            2: (self.first, self.near),
            3: (lambda: self.came(6),),
            5: (lambda: self.came(4),),
            6: (self.far,),
            7: (lambda: self.came(7, 8),),
        }.get(n, ())


class Collect:
    def __init__(self, part, seg, total, pair, near, joined, send, recv):
        self.part, self.seg, self.total = part, seg, total
        self.pair, self.near, self.joined, self.send, self.recv = pair, near, joined, send, recv
        _, self.shard, self.inner, core = place()
        self.twin_shard = self.shard + 1 - 2 * core
        self.low, self.high, self.whole = (0, SPLIT), (SPLIT, seg - SPLIT), (0, seg)
        self.cols = pl.ds(0, D)

    def index(self, s, k):
        row, flip = 1 - k % 2, 1 - k // 2
        return 2 * lax.rem(s + 2 * row, 4) + self.inner + flip * (1 - 2 * self.inner)

    def pair_copy(self, k):
        src = self.part.at[aligned(self.index(self.twin_shard, k) * self.seg, self.seg), self.cols]
        return remote(src, self.pair.at[k], self.send.at[k], self.recv.at[k], partners()[2])

    def copy(self, slot):
        across, beside, _ = partners()
        src, dst, (first, size), device = {
            4: (self.pair.at[0], self.joined, self.low, across),
            5: (self.pair.at[0], self.joined, self.high, beside),
            6: (self.pair.at[1], self.near.at[0], self.low, across),
            7: (self.pair.at[2], self.near.at[1], self.high, beside),
            8: (self.pair.at[2], self.near.at[1], self.low, beside),
            9: (self.pair.at[1], self.near.at[0], self.high, across),
        }[slot]
        rows = pl.ds(first, size)
        return remote(src.at[rows], dst.at[rows], self.send.at[slot], self.recv.at[slot], device)

    def over(self, span, body):
        def step(n, _):
            body(aligned(span[0] + n * 16, 16))
            return 0

        lax.fori_loop(0, span[1] // 16, step, 0)

    def mine(self, k, rows):
        return self.part[aligned(self.index(self.shard, k) * self.seg + rows.start, 16), self.cols].astype(F32)

    def add_pair(self, k):
        def add(rows):
            self.pair[k, rows] = (self.mine(k, rows) + self.pair[k, rows].astype(F32)).astype(BF16)

        self.pair_copy(k).wait_recv()
        self.over(self.whole, add)
        for slot in ((4, 5), (6,), (7,))[k]:
            self.copy(slot).start()

    def add_own(self):
        def add(rows):
            self.total[rows] = self.mine(3, rows) + self.pair[3, rows].astype(F32)

        self.pair_copy(3).wait_recv()
        self.over(self.whole, add)

    def pass_on(self):
        for slot, k, span, after in ((4, 2, self.low, 8), (5, 1, self.high, 9)):

            def add(rows):
                self.pair[k, rows] = (self.pair[k, rows].astype(F32) + self.joined[rows].astype(F32)).astype(BF16)

            self.copy(slot).wait_recv()
            self.over(span, add)
            self.copy(after).start()

    def push(self):
        for k in range(4):
            self.pair_copy(k).start()

    def make(self, n, produce):
        k, own = n // 2, n % 2
        produce(self.index(jnp.where(own == 1, self.shard, self.twin_shard), k))

        @pl.when(own == 0)
        def _():
            self.pair_copy(k).start()

        for m in range(3):

            @pl.when(n == 2 * m + 1)
            def _():
                self.add_pair(m)
                if m == 2:
                    self.pass_on()

        pl.when(n == 7)(self.add_own)

    def end(self):
        def add(rows):
            near = self.near[0, rows].astype(F32) + self.near[1, rows].astype(F32)
            self.total[rows] = self.total[rows] + near

        for slots, span in (((6, 8), self.low), ((7, 9), self.high)):
            for slot in slots:
                self.copy(slot).wait_recv()
            self.over(span, add)
        for k in range(4):
            self.pair_copy(k).wait_send()
        for slot in range(4, 10):
            self.copy(slot).wait_send()


def norm_scale(values):
    return lax.rsqrt(jnp.mean(values * values, axis=-1, keepdims=True) + NORM_EPSILON)


def by_rows(rows, body, carry=0):
    def step(n, carry):
        return body(aligned(n * ROWS, ROWS), carry)

    return lax.fori_loop(0, rows // ROWS, step, carry)


def norm_back(values, gain, upstream):
    scale = norm_scale(values)
    scaled = gain * upstream
    inner = jnp.mean(scaled * values, axis=-1, keepdims=True)
    return (
        scale * scaled - values * scale * scale * scale * inner,
        jnp.sum(upstream * values * scale, axis=0, keepdims=True),
    )


REFS = (
    "tok", "cot", "gains", "own", "oth",
    "block_out", "input_grad", "gain_sums", "mine", "theirs", "n1_held", "slot0", "slot1", "slot2", "slot3",
    "w0", "w1", "w2", "w3", "seq_a", "seq_b", "du", "act", "c_all", "gated", "mixed", "resid", "dresid", "total",
    "pair", "near", "joined", "g1", "g2", "g3", "stage", "sum", "outgoing", "tap_sums", "gain_in", "gain_line",
    "held", "local", "send_x", "recv_x", "send_z", "recv_z", "send_s", "recv_s", "send_c", "recv_c", "credit",
    "halo_send", "halo_recv", "send_g", "recv_g", "fetched", "fetches", "stored", "send_o", "recv_o",
    "send_a", "recv_a", "send_l", "recv_l",
)


def block_kernel(layers, rows, *all_refs):
    r = dict(zip(REFS, all_refs, strict=True))
    tok, cot, gains = r["tok"], r["cot"], r["gains"]
    seq_a, seq_b, du, act = r["seq_a"], r["seq_b"], r["du"], r["act"]
    c_all, gated, mixed, total = r["c_all"], r["gated"], r["mixed"], r["total"]
    weights = (r["w0"], r["w1"], r["w2"], r["w3"])
    seg = tok.shape[0]
    _, shard, inner, _ = place()
    outer, at = line()
    me = 2 * shard + inner
    my_rows = aligned(me * seg, seg)
    chunks = list(zip(range(1, 1 + len(UNIT_CHUNKS)), UNIT_STARTS, UNIT_CHUNKS))
    gather = Gather(
        layers, rows, r["own"], r["oth"], weights,
        r["send_x"], r["recv_x"], r["send_z"], r["recv_z"], r["local"],
    )
    reduce = Reduce(
        layers, rows, (r["w2"], r["g1"], r["g2"], r["g3"]), (r["slot0"], r["slot1"], r["slot2"], r["slot3"]),
        r["stage"], r["w1"], r["sum"], r["outgoing"], r["mine"], r["theirs"],
        (r["send_g"], r["recv_g"], r["fetched"], r["fetches"], r["stored"], r["send_o"], r["recv_o"]),
    )

    def spread(buf, n):
        return Spread(buf, seg, r["send_s"].at[n], r["recv_s"].at[n])

    def collect(part, n):
        return Collect(part, seg, total, r["pair"], r["near"], r["joined"], r["send_c"].at[n], r["recv_c"].at[n])

    one, up, two, three = spread(seq_a, 0), spread(seq_b, 1), spread(seq_a, 2), spread(seq_a, 3)
    branch, down, feed, inputs = collect(seq_a, 0), collect(seq_b, 1), collect(du, 2), collect(seq_a, 3)
    lanes = lax.broadcasted_iota(jnp.int32, (seg, WIDE), 1) < HALF_Q
    taps = pltpu.roll(gains[...], lax.rem(D - shard * QUARTER - inner * HALF_Q, D), 1)[2:5, :WIDE]
    kept = pl.ds(D, WIDE)
    sums, tap_sums = r["gain_sums"], r["tap_sums"]

    def block(t):
        return aligned(t * seg, seg)

    def mine(part):
        return pl.ds(pl.multiple_of(me * seg + part.start, 16), part.size)

    def first_norm():
        def rows(part, _):
            values = tok[part].astype(F32)
            seq_a[mine(part)] = (values * norm_scale(values) * gains[0:1, :]).astype(BF16)
            return 0

        by_rows(seg, rows)

    def up_start():
        seq_b[my_rows] = cot[...]
        up.start()

    def held():
        return pltpu.make_async_copy(seq_a, r["n1_held"], r["held"])

    def reload():
        return pltpu.make_async_copy(r["n1_held"], seq_b, r["held"])

    def project(s):
        for i in (0, 1):
            parts = dot(seq_a[block(2 * s + i)], weights[0][...])
            b = jnp.where(lanes, parts[:, :WIDE], 0.0)
            c = pltpu.roll(parts[:, 128 : 128 + 384], 384 - 64, 1)[:, :WIDE]
            x = parts[:, 384 : 384 + WIDE]
            c_all[s, pl.ds(i * seg, seg)] = jnp.where(lanes, c, 0.0)
            gated[s, pl.ds(8 + i * seg, seg)] = (b * x).astype(BF16).astype(F32)

    def ahead():
        return remote(
            gated.at[:, pl.ds(2 * seg, 8)], gated.at[:, pl.ds(0, 8)], r["halo_send"].at[0], r["halo_recv"].at[0], at(1)
        )

    def halo():
        pl.when(outer < layers - 1)(lambda: ahead().start())

        @pl.when(outer == 0)
        def _():
            gated[:, pl.ds(0, 8)] = jnp.zeros((GROUPS, 8, WIDE), F32)

    def convolved(s, i):
        return (
            taps[0:1, :] * gated[s, pl.ds(6 + i * seg, seg)]
            + taps[1:2, :] * gated[s, pl.ds(7 + i * seg, seg)]
            + taps[2:3, :] * gated[s, pl.ds(8 + i * seg, seg)]
        )

    def convolve(t):
        for i in (0, 1):

            @pl.when(t % 2 == i)
            def _():
                s = t // 2
                mixed[block(t)] = pltpu.roll(c_all[s, pl.ds(i * seg, seg)] * convolved(s, i), 64, 1).astype(BF16)

        seq_a[block(t)] = dot_rows(mixed[block(t)], weights[0][:, pl.ds(512, WIDE)]).astype(BF16)

    def branch_end():
        branch.end()
        allow(r["credit"].at[0])

    def second_norm():
        def rows(part, _):
            values = tok[part].astype(F32) + total[part]
            r["resid"][part] = values
            seq_a[mine(part)] = (values * norm_scale(values) * gains[1:2, :]).astype(BF16)
            return 0

        by_rows(seg, rows)
        pl.semaphore_wait(r["credit"].at[0], 3)

    def hidden(k, start, units, t):
        ref, here = weights[k], block(t)
        gate = dot(seq_a[here], ref[:, pl.ds(0, units)])
        upval = dot(seq_a[here], ref[:, pl.ds(units, units)])
        dact = dot(seq_b[here], ref[:, pl.ds(2 * units, units)])
        sigma = jax.nn.sigmoid(gate)
        silu = gate * sigma
        act[here, pl.ds(start, units)] = (silu * upval).astype(BF16)
        dgate = dact * upval * sigma * (1.0 + gate * (1.0 - sigma))
        du[here, pl.ds(2 * start, units)] = dgate.astype(BF16)
        du[here, pl.ds(2 * start + units, units)] = (dact * silu).astype(BF16)

    def slice_of(n):
        return jnp.where(outer < layers // 2, D // SLICE - 1 - n, n)

    def gate_up_grads(k, start, units, n):
        part = slice_of(n)
        left = seq_a[:, aligned(part * SLICE, SLICE, 128)]
        reduce.grads[k][aligned(part * SLICE, SLICE), pl.ds(0, 2 * units)] = dot_columns(
            left, du[:, pl.ds(2 * start, 2 * units)]
        ).astype(BF16)

    def down_grads(k, start, units, n):
        part = slice_of(n)
        left = seq_b[:, aligned(part * SLICE, SLICE, 128)]
        reduce.grads[k][aligned(part * SLICE, SLICE), pl.ds(2 * units, units)] = dot_columns(
            left, act[:, pl.ds(start, units)]
        ).astype(BF16)

    def grads(k, start, units, n):
        gate_up_grads(k, start, units, n)
        down_grads(k, start, units, n)
        reduce.direct(k, slice_of(n))

    def second(t):
        here = block(t)
        seq_b[here] = sum(
            dot_rows(du[here, pl.ds(2 * start, 2 * units)], weights[k][:, pl.ds(0, 2 * units)])
            for k, start, units in chunks
        ).astype(BF16)

    def down_end():
        down.end()
        reload().start()
        allow(r["credit"].at[1])

    def forward(t):
        here = block(t)
        du[here, pl.ds(0, D)] = sum(
            dot_rows(act[here, pl.ds(start, units)], weights[k][:, pl.ds(2 * units, units)])
            for k, start, units in chunks
        ).astype(BF16)

    def second_back():
        def rows(part, gain):
            dpart, dgain = norm_back(r["resid"][part], gains[1:2, :], total[part])
            dresid = cot[part].astype(F32) + dpart
            r["dresid"][part] = dresid
            seq_a[mine(part)] = dresid.astype(BF16)
            return gain + dgain

        sums[...] = jnp.zeros(sums.shape, F32)
        tap_sums[...] = jnp.zeros(tap_sums.shape, F32)
        sums[1:2, pl.ds(0, D)] = by_rows(seg, rows, jnp.zeros((1, D), F32))
        pl.semaphore_wait(r["credit"].at[1], 3)

    def mix_back(t):
        s, here = t // 2, block(t)
        dmixed = pltpu.roll(dot(seq_a[here], weights[0][:, pl.ds(512, WIDE)]), WIDE - 64, 1)
        dmixed = jnp.where(lanes, dmixed, 0.0)
        for i in (0, 1):

            @pl.when(t % 2 == i)
            def _():
                du[here, kept] = (dmixed * convolved(s, i)).astype(BF16)
                c_all[s, pl.ds(i * seg, seg)] = dmixed * c_all[s, pl.ds(i * seg, seg)]

    def after():
        return remote(
            c_all.at[:, pl.ds(0, 8)], c_all.at[:, pl.ds(2 * seg, 8)], r["halo_send"].at[1], r["halo_recv"].at[1], at(-1)
        )

    def halo_back():
        pl.when(outer > 0)(lambda: after().start())

        @pl.when(outer == layers - 1)
        def _():
            c_all[:, pl.ds(2 * seg, 8)] = jnp.zeros((GROUPS, 8, WIDE), F32)

    def conv_back(n):
        for i in (0, 1):
            pl.when(n // GROUPS == i)(functools.partial(conv_back_half, n % GROUPS, i))

    def conv_back_half(s, i):
        t = block(2 * s + i)
        dconv = c_all[s, pl.ds(i * seg, seg)]
        dgated = (
            taps[2:3, :] * dconv
            + taps[1:2, :] * c_all[s, pl.ds(1 + i * seg, seg)]
            + taps[0:1, :] * c_all[s, pl.ds(2 + i * seg, seg)]
        )
        parts = dot(seq_b[t], weights[0][:, pl.ds(0, 640)])
        db = dgated * parts[:, 384:640]
        dx = dgated * parts[:, :WIDE]
        dc = jnp.concatenate([du[t, kept].astype(F32), jnp.zeros((seg, 128), F32)], axis=1)
        dc = pltpu.roll(dc, 64, 1)
        act[t, pl.ds(0, 128)] = db[:, :128].astype(BF16)
        act[t, pl.ds(128, 128)] = (db[:, 128:] + dc[:, :128]).astype(BF16)
        act[t, pl.ds(256, 128)] = dc[:, 128:256].astype(BF16)
        act[t, pl.ds(384, WIDE)] = dx.astype(BF16)
        act[t, pl.ds(640, 128)] = jnp.zeros((seg, 128), BF16)
        for k in range(3):
            moved = gated[s, pl.ds(6 + k + i * seg, seg)]
            tap_sums[k : k + 1] = tap_sums[k : k + 1] + jnp.sum(dconv * moved, axis=0, keepdims=True)

    def conv_grads(n):
        part = slice_of(n)
        held_rows, cols = aligned(part * SLICE, SLICE), aligned(part * SLICE, SLICE, 128)
        ref = reduce.grads[0]
        of_parts = dot_columns(seq_b[:, cols], act[:, pl.ds(0, CONV_COLS)])
        ref[held_rows, pl.ds(0, 512)] = of_parts[:, :512].astype(BF16)
        of_mixed = dot_columns(seq_a[:, cols], mixed[...])
        ref[held_rows, pl.ds(512, WIDE)] = (of_parts[:, 512:] + of_mixed).astype(BF16)
        reduce.direct(0, part)

    def feed_end():
        feed.end()
        allow(r["credit"].at[2])
        r["block_out"][...] = (r["resid"][...] + total[...]).astype(BF16)

    def first(t):
        here = block(t)
        seq_a[here] = dot_rows(act[here, pl.ds(0, 640)], weights[0][:, pl.ds(0, 640)]).astype(BF16)

    def first_back():
        def rows(part, gain):
            dpart, dgain = norm_back(tok[part].astype(F32), gains[0:1, :], total[part])
            r["input_grad"][part] = (r["dresid"][part] + dpart).astype(BF16)
            return gain + dgain

        sums[0:1, pl.ds(0, D)] = by_rows(seg, rows, jnp.zeros((1, D), F32))
        sums[2:5, aligned(me * WIDE, WIDE, 128)] = tap_sums[0:3]

    def gains_across(n):
        return remote(sums, r["gain_in"].at[n], r["send_a"].at[n], r["recv_a"].at[n], partners()[n])

    def gains_add(n):
        gains_across(n).wait()
        sums[...] = sums[...] + r["gain_in"][n]

    def line_copy(sign, steps):
        slot = (0 if sign > 0 else 1, steps - 1)
        return remote(
            sums, r["gain_line"].at[slot], r["send_l"].at[slot], r["recv_l"].at[slot], at(sign * steps)
        )

    def gains_line():
        for steps in range(1, layers):
            for sign in (1, -1):
                pl.when(in_line(outer + sign * steps, layers))(line_copy(sign, steps).start)

    def gains_end():
        for steps in range(1, layers):
            for sign in (1, -1):
                pl.when(in_line(outer + sign * steps, layers))(line_copy(sign, steps).wait_send)
                pl.when(in_line(outer - sign * steps, layers))(line_copy(sign, steps).wait_recv)

        own_sums = sums[...]
        for origin in range(layers):
            for steps in range(1, layers):
                for sign in (1, -1):

                    @pl.when((outer - sign * steps == origin))
                    def _():
                        came = r["gain_line"][0 if sign > 0 else 1, steps - 1]
                        sums[...] = came if origin == 0 else sums[...] + came

            if origin > 0:

                @pl.when(outer == origin)
                def _():
                    sums[...] = sums[...] + own_sums

    def end():
        reduce.finish(0)
        for k in range(len(WIDTHS)):
            reduce.wait_sent(k)
        pl.when(outer < layers - 1)(lambda: ahead().wait_send())
        pl.when(outer > 0)(lambda: after().wait_send())

    def start():
        greet(layers)

    def hold():
        held().start()

    def hold_end():
        held().wait()

    def halo_end():
        pl.when(outer > 0)(lambda: ahead().wait_recv())

    def reload_end():
        reload().wait()

    def halo_back_end():
        pl.when(outer < layers - 1)(lambda: after().wait_recv())

    def feed_credit():
        pl.semaphore_wait(r["credit"].at[2], 3)

    def from_spread(moved, body):
        def step(n):
            for m in range(8):
                if moved.before(m):

                    @pl.when(n == m)
                    def _():
                        for act in moved.before(m):
                            act()

            body(moved.index(n))

        return step

    def each(body, *cases):
        return [functools.partial(body, *(case if isinstance(case, tuple) else (case,))) for case in cases]

    every = range(len(WIDTHS))
    exchange, send_own, send_other = (
        each(body, *every) for body in (gather.exchange, gather.send_own, gather.send_other)
    )
    step = [each(gather.steps, (k, 1, 1), (k, 2, 2), (k, 3)) for k in every]
    join_far = each(reduce.join, *((k, layers - 2, 2) for k in every))
    join_near = each(reduce.join, *((k, 1, 1) for k in every))
    final = each(reduce.final, (0, 3), 1, (2, 1), (3, 2))
    feed_pair = each(feed.add_pair, 0, 1, 2)
    gain_send = [lambda n=n: gains_across(n).start() for n in range(3)]
    gain_add = each(gains_add, 0, 1, 2)
    d3_far = functools.partial(reduce.direct, 3, least=2)
    d3_near = functools.partial(reduce.direct, 3, most=1)
    blocks, parts = 2 * GROUPS, D // SLICE
    proj = Loop(GROUPS, project)
    mix = Loop(blocks, lambda n: branch.make(n, convolve))
    hid1 = Loop(blocks, from_spread(two, functools.partial(hidden, *chunks[0])))
    hid2, hid3 = (Loop(blocks, functools.partial(hidden, *chunk)) for chunk in chunks[1:])
    grad1, grad2 = (Loop(parts, functools.partial(grads, *chunk)) for chunk in chunks[:2])
    down3 = Loop(parts, functools.partial(down_grads, *chunks[2]))
    back2 = Loop(blocks, lambda n: down.make(n, second))
    gate3 = Loop(parts, functools.partial(gate_up_grads, *chunks[2]))
    ffn = Loop(blocks, forward)
    back_mix = Loop(blocks, from_spread(three, mix_back))
    back_conv = Loop(blocks, conv_back)
    grad0 = Loop(parts, conv_grads)
    back1 = Loop(blocks, lambda n: inputs.make(n, first))
    play(
        [
            start, exchange[0], send_own[2], send_own[0], first_norm, exchange[2], one.start, send_other[0],
            send_own[3], one.first, step[0][0], exchange[1], up_start, step[0][1], one.near, send_own[1], one.far,
            one.end, step[0][2], proj[0], hold, up.first, send_other[1], exchange[3], proj[1], proj[2], proj[3],
            halo, up.near, step[1][0], halo_end, hold_end, mix[0], up.far, mix[1], mix[2], mix[3], up.end, mix[4],
            mix[5], mix[6], mix[7], step[1][1], branch_end, second_norm, two.start, send_other[2], step[2][0],
            step[1][2], hid1[0], hid1[1], send_other[3], hid1[2], hid1[3], hid1[4], hid1[5], hid1[6], hid1[7],
            two.sent, step[2][1], grad1[0], step[2][2], step[3][0], grad1[1], grad1[2], grad1[3], hid2[0], hid2[1],
            hid2[2], hid2[3], hid2[4], hid2[5], hid2[6], hid2[7], grad2[0], grad2[1], grad2[2], step[3][1],
            grad2[3], step[3][2], hid3[0], hid3[1], hid3[2], hid3[3], hid3[4], hid3[5], hid3[6], hid3[7], down3[0],
            down3[1], down3[2], down3[3], back2[0], join_far[1], back2[1], back2[2], back2[3], back2[4], back2[5],
            back2[6], gather.finish, back2[7], gate3[0], gate3[1], gate3[2], gate3[3], down_end, second_back,
            three.start, back_mix[0], join_near[1], d3_far, ffn[0], ffn[1], ffn[2], ffn[3], ffn[4], ffn[5], ffn[6],
            ffn[7], back_mix[1], reload_end, back_mix[2], join_far[2], final[1], back_mix[3], join_near[2],
            feed.push, back_mix[4], feed_pair[0], back_mix[5], back_mix[6], back_mix[7], three.sent, halo_back,
            back_conv[0], d3_near, feed_pair[1], back_conv[1], back_conv[2], feed_pair[2], join_far[3],
            halo_back_end, back_conv[3], back_conv[4], back_conv[5], back_conv[6], back_conv[7], feed.pass_on,
            grad0[0], grad0[1], join_near[3], grad0[2], grad0[3], feed.add_own, feed_end, feed_credit, back1[0],
            back1[1], back1[2], back1[3], back1[4], join_far[0], back1[5], back1[6], join_near[0], back1[7],
            final[2], inputs.end, first_back, gain_send[0], final[3], gain_add[0], gain_send[1], gain_add[1],
            final[0], gain_send[2], gain_add[2], gains_line, gains_end, end,
        ]
    )


class Loop:
    def __init__(self, count, body):
        self.count, self.body = count, body

    def __getitem__(self, n):
        return (self, n)


def play(order):
    order = list(order)
    while order:
        entry = order.pop(0)
        if not isinstance(entry, tuple):
            entry()
            continue
        loop, _ = entry
        between = {}
        for n in range(1, loop.count):
            between[n] = []
            while order[0] != (loop, n):
                between[n].append(order.pop(0))
            order.pop(0)

        def turn(n, _):
            for m, acts in between.items():
                if acts:

                    @pl.when(n == m)
                    def _():
                        play(acts)

            loop.body(n)
            return 0

        lax.fori_loop(0, loop.count, turn, 0)


def block_step(tok, cot, gains, own, oth, layers):
    rows, seg = own.shape[0], tok.shape[0]
    count = len(WIDTHS)
    tokens = 2 * GROUPS * seg
    vmem, anywhere = pl.BlockSpec(memory_space=pltpu.VMEM), pl.BlockSpec(memory_space=pl.ANY)
    shape, scratch = jax.ShapeDtypeStruct, pltpu.VMEM
    dma, regular = pltpu.SemaphoreType.DMA, pltpu.SemaphoreType.REGULAR
    hops = layers - 1
    wide, biggest = sum(WIDTHS), max(WIDTHS)
    out_shape = [
        shape((seg, D), BF16),
        shape((seg, D), BF16),
        shape((8, 2 * GROUPS * WIDE), F32),
        shape((rows, wide), F32),
        shape((rows, wide), BF16),
        shape((tokens, D), BF16),
    ] + [shape((2, hops, 2 * rows, width), BF16) for width in WIDTHS]
    scratch_shapes = (
        [scratch((D, width), BF16) for width in WIDTHS]
        + [
            scratch((tokens, D), BF16),
            scratch((tokens, D), BF16),
            scratch((tokens, 2 * PAD_F), BF16),
            scratch((tokens, PAD_F), BF16),
            scratch((GROUPS, 8 + 2 * seg, WIDE), F32),
            scratch((GROUPS, 8 + 2 * seg, WIDE), F32),
            scratch((tokens, WIDE), BF16),
            scratch((seg, D), F32),
            scratch((seg, D), F32),
            scratch((seg, D), F32),
            scratch((4, seg, D), BF16),
            scratch((2, seg, D), BF16),
            scratch((seg, D), BF16),
        ]
        + [scratch((D, width), BF16) for width in WIDTHS[1:]]
        + [
            scratch((2 * rows, biggest), BF16),
            scratch((rows, biggest), F32),
            scratch((rows, wide), BF16),
            scratch((8, WIDE), F32),
            scratch((3, 8, 2 * GROUPS * WIDE), F32),
            scratch((2, hops, 8, 2 * GROUPS * WIDE), F32),
            dma,
            dma((count,)),
            dma((count,)),
            dma((count,)),
            dma((count, 2, hops, 2)),
            dma((count, 2, hops, 2)),
            dma((4, 11)),
            dma((4, 11)),
            dma((4, 10)),
            dma((4, 10)),
            regular((3,)),
            dma((2,)),
            dma((2,)),
            dma((count, 2, hops)),
            dma((count, 2, hops)),
            dma,
            dma((4,)),
            dma((count,)),
            dma((count,)),
            dma((count,)),
            dma((3,)),
            dma((3,)),
            dma((2, hops)),
            dma((2, hops)),
        ]
    )
    return pl.pallas_call(
        functools.partial(block_kernel, layers, rows),
        out_shape=out_shape,
        in_specs=[vmem] * 3 + [anywhere] * 2,
        out_specs=[vmem] * 3 + [anywhere] * (3 + count),
        scratch_shapes=scratch_shapes,
        compiler_params=pltpu.CompilerParams(
            collective_id=0, has_side_effects=True, vmem_limit_bytes=VMEM_BYTES
        ),
        name="block_step",
    )(tok, cot, gains, own, oth)[:5]


def column_pieces(half):
    pieces = [(m * QUARTER + half * HALF_Q, m * HALF_Q, HALF_Q, 0) for m in range(4)]
    for k, (start, units) in enumerate(zip(UNIT_STARTS, UNIT_CHUNKS), 1):
        real = min(units, HALF_F - start)
        for m in range(3):
            first = 4 * QUARTER + m * UNITS + half * HALF_F + start
            pieces.append((first, STARTS[k] + m * units, real, units - real))
    return pieces


def halves_kernel(inner_ref, weights_ref, own_ref, oth_ref):
    is_low = inner_ref[0] == 0

    def half(h):
        parts = []
        for first, _, width, padding in column_pieces(h):
            parts.append(weights_ref[:, first : first + width])
            if padding:
                parts.append(jnp.zeros((parts[-1].shape[0], padding), F32))
        return jnp.concatenate(parts, axis=1)

    low, high = half(0), half(1)
    own_ref[...] = jnp.where(is_low, low, high).astype(BF16)
    oth_ref[...] = jnp.where(is_low, high, low).astype(BF16)


def band(rows, most):
    return max(size for size in range(16, most + 1, 16) if rows % size == 0)


def halves(weights, inner):
    rows, cols = weights.shape
    wide = sum(WIDTHS)
    size = band(rows, 96)
    by_row = lambda width: pl.BlockSpec((size, width), lambda n: (n, 0))
    return pl.pallas_call(
        halves_kernel,
        grid=(rows // size,),
        out_shape=[jax.ShapeDtypeStruct((rows, wide), BF16)] * 2,
        in_specs=[pl.BlockSpec(memory_space=pltpu.SMEM), by_row(cols)],
        out_specs=[by_row(wide)] * 2,
        compiler_params=pltpu.CompilerParams(vmem_limit_bytes=VMEM_BYTES),
        name="halves",
    )(inner, weights)


def adam_update(param, grad, first, second, rate, decay):
    first_new = MOMENT_DECAY * first + (1.0 - MOMENT_DECAY) * grad
    second_new = SQUARE_DECAY * second + (1.0 - SQUARE_DECAY) * grad * grad
    root = jnp.sqrt(second_new * (1.0 / (1.0 - SQUARE_DECAY**STEP))) + ADAM_EPSILON
    step = first_new * (rate / (1.0 - MOMENT_DECAY**STEP)) / root
    return (first_new, second_new, param * (1.0 - rate * decay) - step)


def update_kernel(
    inner_ref, mine_ref, theirs_ref, weights_ref, first_ref, second_ref, sums_ref, gains_ref, gains_first_ref,
    gains_second_ref, block_ref, input_ref, grad_out, first_out, second_out, weights_out, gains_grad_out,
    gains_first_out, gains_second_out, gains_out, block_out, input_out,
):
    is_low = inner_ref[0] == 0
    mine, theirs = mine_ref[...], theirs_ref[...].astype(F32)
    for half in (0, 1):
        chosen = jnp.where(is_low, mine, theirs) if half == 0 else jnp.where(is_low, theirs, mine)
        for first, own, width, _ in column_pieces(half):
            grad_out[:, first : first + width] = chosen[:, own : own + width]
    first_out[...], second_out[...], weights_out[...] = adam_update(
        weights_ref[...], grad_out[...], first_ref[...], second_ref[...], WEIGHT_RATE, WEIGHT_DECAY
    )

    @pl.when(pl.program_id(0) == 0)
    def _():
        gains_grad_out[0:2] = sums_ref[0:2, :D]
        for n in range(2 * GROUPS):
            gains_grad_out[2:5, n * HALF_Q : (n + 1) * HALF_Q] = sums_ref[2:5, n * WIDE : n * WIDE + HALF_Q]
        gains_first_out[...], gains_second_out[...], gains_out[...] = adam_update(
            gains_ref[...], gains_grad_out[...], gains_first_ref[...], gains_second_ref[...], GAIN_RATE, 0.0
        )
        block_out[...] = block_ref[...]
        input_out[...] = input_ref[...]


def update(inner, mine, theirs, weights, first, second, sums, gains, gains_first, gains_second, block, grad):
    rows, cols = weights.shape
    wide = mine.shape[1]
    size = band(rows, 32)
    by_row = lambda width: pl.BlockSpec((size, width), lambda n: (n, 0))
    whole = lambda values: pl.BlockSpec(values.shape, lambda n: (0, 0))
    shape = jax.ShapeDtypeStruct
    return pl.pallas_call(
        update_kernel,
        grid=(rows // size,),
        out_shape=[shape((rows, cols), F32)] * 4 + [shape(gains.shape, F32)] * 4 + [shape(block.shape, BF16)] * 2,
        in_specs=[pl.BlockSpec(memory_space=pltpu.SMEM)]
        + [by_row(wide)] * 2
        + [by_row(cols)] * 3
        + [whole(sums)]
        + [whole(gains)] * 3
        + [whole(block)] * 2,
        out_specs=[by_row(cols)] * 4 + [whole(gains)] * 4 + [whole(block)] * 2,
        compiler_params=pltpu.CompilerParams(vmem_limit_bytes=VMEM_BYTES),
        name="update",
    )(inner, mine, theirs, weights, first, second, sums, gains, gains_first, gains_second, block, grad)


def on_device(
    tokens, gains_taps, weights, cotangent, weight_first, weight_second, gains_first, gains_second
):
    layers = lax.axis_size("seq") // 2
    inner_word = (lax.axis_index("seq") % 2).astype(jnp.int32).reshape(1)
    own, oth = halves(weights, inner_word)
    block_out, input_grad, gain_sums, mine, theirs = block_step(
        tokens[0], cotangent[0], gains_taps, own, oth, layers
    )
    (
        weight_grad, weight_first_new, weight_second_new, weight_new,
        gains_grad, gains_first_new, gains_second_new, gains_new, block_out, input_grad,
    ) = update(
        inner_word, mine, theirs, weights, weight_first, weight_second,
        gain_sums, gains_taps, gains_first, gains_second, block_out, input_grad,
    )
    return (
        block_out[None],
        input_grad[None],
        weight_grad,
        weight_first_new,
        weight_second_new,
        weight_new,
        gains_grad,
        gains_first_new,
        gains_second_new,
        gains_new,
    )


def solution(mesh):
    tokens, rows, whole = P("shard", "seq", None), P("seq", "shard"), P()
    return jax.shard_map(
        on_device,
        mesh=mesh,
        in_specs=(tokens, whole, rows, tokens, rows, rows, whole, whole),
        out_specs=(tokens, tokens, rows, rows, rows, rows, whole, whole, whole, whole),
        check_vma=False,
    )
```

```python
import functools

import jax
import jax.numpy as jnp
from jax import lax
from jax.experimental import pallas as pl
from jax.experimental.pallas import tpu as pltpu
from jax.sharding import PartitionSpec as P

D = 1536
FF = 6912
STEP = 10
GROUPS = 4
QUARTER = D // GROUPS
UNITS = FF // GROUPS
GROUP_COLS = 4 * QUARTER + 3 * UNITS
HALF_Q = QUARTER // 2
HALF_F = UNITS // 2
LANES = 128
PAD_F = -(-HALF_F // LANES) * LANES
WIDE = 256
CONV_COLS = 4 * HALF_Q
UNIT_CHUNKS = (384, 384, PAD_F - 768)
UNIT_STARTS = (0, 384, 768)
WIDTHS = (CONV_COLS,) + tuple(3 * units for units in UNIT_CHUNKS)
STARTS = tuple(sum(WIDTHS[:k]) for k in range(len(WIDTHS)))
SPREAD_SPLIT = 128
COLLECT_SPLIT = 128
REACH = (1, 1, 1, 1)
CUT_FIRST = 2
SLICE = 384
TILE = 16
ROWS = 48

MOMENT_DECAY = 0.9
SQUARE_DECAY = 0.95
ADAM_EPSILON = 1e-08
NORM_EPSILON = 1e-05
WEIGHT_RATE = 0.02
GAIN_RATE = 0.2
WEIGHT_DECAY = 0.1

BF16 = jnp.bfloat16
F32 = jnp.float32
MESH = pl.DeviceIdType.MESH
VMEM_BYTES = 63 * 1024 * 1024


def place():
    seq, shard = lax.axis_index("seq"), lax.axis_index("shard")
    inner, core = lax.rem(seq, 2), lax.rem(shard, 2)
    return seq, shard, inner, core


def partners():
    seq, shard, inner, core = place()
    across = {"seq": seq + 1 - 2 * inner, "shard": shard}
    beside = {"seq": seq, "shard": lax.rem(shard + 2, 4)}
    twin = {"seq": seq, "shard": shard + 1 - 2 * core}
    return across, beside, twin


def remote(src, dst, send, recv, device):
    return pltpu.make_async_remote_copy(
        src_ref=src, dst_ref=dst, send_sem=send, recv_sem=recv, device_id=device, device_id_type=MESH
    )


def line():
    seq, shard, _, _ = place()
    return seq // 2, lambda steps: {"seq": seq + 2 * steps, "shard": shard}


def greet(layers):
    outer, at = line()
    barrier = pltpu.get_barrier_semaphore()
    for device in partners():
        pl.semaphore_signal(barrier, inc=1, device_id=device, device_id_type=MESH)
    for steps in range(1, layers):
        for sign in (1, -1):

            @pl.when(in_line(outer + sign * steps, layers))
            def _():
                pl.semaphore_signal(barrier, inc=1, device_id=at(sign * steps), device_id_type=MESH)

    pl.semaphore_wait(barrier, 3 + layers - 1)


def in_line(index, layers):
    return (index >= 0) & (index < layers)


def allow(credit):
    for device in partners():
        pl.semaphore_signal(credit, inc=1, device_id=device, device_id_type=MESH)


def dot(left, right):
    return jnp.dot(left, right, preferred_element_type=F32)


def dot_rows(left, right):
    return lax.dot_general(left, right, (((1,), (1,)), ((), ())), preferred_element_type=F32)


def dot_columns(left, right):
    return lax.dot_general(left, right, (((0,), (0,)), ((), ())), preferred_element_type=F32)


def aligned(start, size, multiple=16):
    return pl.ds(pl.multiple_of(start, multiple), size)


class Gather:
    def __init__(self, layers, rows, oth, outs, send_x, recv_x, send_z, recv_z):
        self.layers, self.rows, self.oth, self.outs = layers, rows, oth, outs
        self.send_x, self.recv_x, self.send_z, self.recv_z = send_x, recv_x, send_z, recv_z
        self.seq, _, self.inner, _ = place()
        self.outer, self.at = line()
        self.across = partners()[0]

    def seq_rows(self, index):
        return aligned(index * self.rows, self.rows)

    def layer_rows(self, direction, distance):
        origin = self.outer - distance if direction == 0 else self.outer + distance
        return aligned(origin * 2 * self.rows, 2 * self.rows)

    def copy(self, k, src, dst, direction, distance, hop, piece):
        slot = (k, direction, distance + hop - 1, piece)
        return remote(
            src, dst, self.send_z.at[slot], self.recv_z.at[slot], self.at(hop if direction == 0 else -hop)
        )

    def goes(self, direction, hop):
        return in_line(self.outer + (hop if direction == 0 else -hop), self.layers)

    def has_come(self, direction, distance):
        return in_line(self.outer + (-distance if direction == 0 else distance), self.layers)

    def hops(self, k, distance):
        return range(1, min(REACH[k], self.layers - 1 - distance) + 1)

    def own_copy(self, k, direction, hop):
        here = self.outs[k].at[self.seq_rows(self.seq)]
        return self.copy(k, here, here, direction, 0, hop, 0)

    def other_copy(self, k, direction, hop):
        there = self.outs[k].at[self.seq_rows(self.seq + 1 - 2 * self.inner)]
        return self.copy(k, there, there, direction, 0, hop, 1)

    def pass_copy(self, k, direction, distance, hop):
        ref = self.outs[k].at[self.layer_rows(direction, distance)]
        return self.copy(k, ref, ref, direction, distance, hop, 0)

    def other_rows(self, k):
        return self.oth.at[pl.ds(k * self.rows, self.rows), pl.ds(0, WIDTHS[k])]

    def exchange(self, k):
        self.x_copy(k).start()

    def x_copy(self, k):
        here = self.outs[k].at[self.seq_rows(self.seq)]
        return remote(self.other_rows(k), here, self.send_x.at[k], self.recv_x.at[k], self.across)

    def crossed(self):
        for k in range(len(self.outs)):
            self.x_copy(k).wait_send()

    def send_own(self, k):
        for hop in self.hops(k, 0):
            for direction in (0, 1):

                @pl.when(self.goes(direction, hop))
                def _():
                    self.own_copy(k, direction, hop).start()

    def send_other(self, k):
        self.x_copy(k).wait_recv()
        for hop in self.hops(k, 0):
            for direction in (0, 1):

                @pl.when(self.goes(direction, hop))
                def _():
                    self.other_copy(k, direction, hop).start()

    def step(self, k, distance):
        for direction in (0, 1):

            @pl.when(self.has_come(direction, distance))
            def _():
                if distance <= REACH[k]:
                    origin = self.outer - distance if direction == 0 else self.outer + distance
                    for piece in (0, 1):
                        index = 2 * origin + (self.inner if piece == 0 else 1 - self.inner)
                        ref = self.outs[k].at[self.seq_rows(index)]
                        self.copy(k, ref, ref, direction, distance - 1, 1, piece).wait_recv()
                else:
                    ref = self.outs[k].at[self.layer_rows(direction, distance)]
                    self.copy(k, ref, ref, direction, distance - 1, 1, 0).wait_recv()
                if distance % REACH[k] == 0:
                    for hop in self.hops(k, distance):

                        @pl.when(self.goes(direction, hop))
                        def _():
                            self.pass_copy(k, direction, distance, hop).start()

    def steps(self, k, first, last=None):
        last = self.layers - 1 if last is None else min(last, self.layers - 1)
        for distance in range(first, last + 1):
            self.step(k, distance)

    def finish(self):
        for k in range(len(self.outs)):
            for distance in range(0, self.layers - 1, REACH[k]):
                for hop in self.hops(k, distance):
                    for direction in (0, 1):

                        @pl.when(self.goes(direction, hop) & self.has_come(direction, distance))
                        def _():
                            if distance == 0:
                                self.own_copy(k, direction, hop).wait_send()
                                self.other_copy(k, direction, hop).wait_send()
                            else:
                                self.pass_copy(k, direction, distance, hop).wait_send()


class Reduce:
    def __init__(self, layers, rows, grads, slots, stage, spare, total, outgoing, mine, theirs, sems):
        self.layers, self.rows, self.grads, self.slots = layers, rows, grads, slots
        self.stage, self.spare, self.total, self.outgoing = stage, spare, total, outgoing
        self.mine, self.theirs = mine, theirs
        self.send_g, self.recv_g, self.fetched, self.fetches, self.stored, self.send_o, self.recv_o = sems
        _, _, self.inner, _ = place()
        self.outer, self.at = line()
        self.across = partners()[0]

    def owner(self, direction, distance):
        return self.outer + distance if direction == 0 else self.outer - distance

    def upstream(self, direction, steps):
        return in_line(self.outer - steps if direction == 0 else self.outer + steps, self.layers)

    def block(self, k, owner):
        return self.grads[k].at[aligned(owner * 2 * self.rows, 2 * self.rows), pl.ds(0, WIDTHS[k])]

    def copy(self, k, src, direction, distance):
        slot = (direction, distance - 1)
        return remote(
            src,
            self.slots[k].at[slot],
            self.send_g.at[(k,) + slot],
            self.recv_g.at[(k,) + slot],
            self.at(1 if direction == 0 else -1),
        )

    def send(self, k, direction, distance):
        self.copy(k, self.block(k, self.owner(direction, distance)), direction, distance).start()

    def direct(self, k, part=None, least=1, most=None):
        for distance in range(most or self.layers - 1, least - 1, -1):
            for direction in (0, 1):
                owner = self.owner(direction, distance)
                here = in_line(owner, self.layers) & jnp.logical_not(self.upstream(direction, 1))
                if part is not None:
                    here = here & (owner * 2 * self.rows // SLICE == part)

                @pl.when(here)
                def _():
                    self.send(k, direction, distance)

    def fetch(self, k, direction, distance):
        slot = self.slots[k].at[direction, distance - 1]
        self.copy(k, slot, direction, distance).wait_recv()
        held = self.stage.at[:, pl.ds(0, WIDTHS[k])]
        copy = pltpu.make_async_copy(slot, held, self.fetched)
        copy.start()
        copy.wait()

    def tiles(self, body):
        def step(n, _):
            body(aligned(n * TILE, TILE))
            return 0

        lax.fori_loop(0, 2 * self.rows // TILE, step, 0)

    def join(self, k, most, least):
        cols = pl.ds(0, WIDTHS[k])
        for distance in range(most, least - 1, -1):
            for direction in (0, 1):
                owner = self.owner(direction, distance)

                @pl.when(in_line(owner, self.layers) & self.upstream(direction, 1))
                def _():
                    def add(tile):
                        base = self.owner(direction, distance) * 2 * self.rows
                        rows = pl.ds(pl.multiple_of(base + tile.start, 16), TILE)
                        ref = self.grads[k]
                        ref[rows, cols] = (
                            ref[rows, cols].astype(F32) + self.stage[tile, cols].astype(F32)
                        ).astype(BF16)

                    self.fetch(k, direction, distance + 1)
                    self.tiles(add)
                    self.send(k, direction, distance)

    def final(self, k, before=None):
        cols = pl.ds(0, WIDTHS[k])
        came = [(1, 0), (1, 1)]

        def fetch(n, distance, direction):
            return pltpu.make_async_copy(
                self.slots[k].at[direction, distance - 1],
                self.spare.at[pl.ds(n * 2 * self.rows, 2 * self.rows), cols],
                self.fetches.at[n],
            )

        for n, (distance, direction) in enumerate(came):

            @pl.when(self.upstream(direction, distance))
            def _():
                self.copy(k, self.slots[k].at[direction, distance - 1], direction, distance).wait_recv()
                fetch(n, distance, direction).start()

        if before is not None:
            self.store(before).wait()

        here, there = self.inner * self.rows, (1 - self.inner) * self.rows

        def each(base, body):
            def step(n, _):
                body(base + n * TILE, n * TILE)
                return 0

            lax.fori_loop(0, self.rows // TILE, step, 0)

        for n, (distance, direction) in enumerate(came):

            @pl.when(self.upstream(direction, distance))
            def _():
                fetch(n, distance, direction).wait()

        def add_up(flags):
            def total(rows):
                value = self.grads[k][aligned(self.outer * 2 * self.rows + rows, TILE), cols].astype(F32)
                for n, flag in enumerate(flags):
                    if flag:
                        value = value + self.spare[aligned(n * 2 * self.rows + rows, TILE), cols].astype(F32)
                return value

            def send(rows, at):
                self.outgoing[aligned(at, TILE), pl.ds(STARTS[k], WIDTHS[k])] = total(rows).astype(BF16)

            def keep(rows, at):
                self.total[aligned(at, TILE), cols] = total(rows)

            each(there, send)
            self.over(k).start()
            each(here, keep)
            self.store(k).start()

        patterns = {}
        for place_in_line in range(self.layers):
            flags = tuple(
                0 <= (place_in_line - distance if direction == 0 else place_in_line + distance) < self.layers
                for distance, direction in came
            )
            patterns.setdefault(flags, []).append(place_in_line)
        for flags, places in patterns.items():
            here_now = functools.reduce(jnp.logical_or, [self.outer == p for p in places])

            @pl.when(here_now)
            def _():
                add_up(flags)

    def over(self, k):
        wide = pl.ds(STARTS[k], WIDTHS[k])
        return remote(
            self.outgoing.at[:, wide], self.theirs.at[:, wide], self.send_o.at[k], self.recv_o.at[k], self.across
        )

    def store(self, k):
        return pltpu.make_async_copy(
            self.total.at[:, pl.ds(0, WIDTHS[k])], self.mine.at[:, pl.ds(STARTS[k], WIDTHS[k])], self.stored.at[k]
        )

    def wait_sent(self, k):
        for distance in range(1, self.layers):
            for direction in (0, 1):
                owner = self.owner(direction, distance)

                @pl.when(in_line(owner, self.layers))
                def _():
                    self.copy(k, self.block(k, owner), direction, distance).wait_send()

    def finish(self, before):
        self.store(before).wait()
        for k in range(len(self.grads)):
            self.over(k).wait()


class Spread:
    slots = range(11)

    def __init__(self, buf, seg, send, recv):
        self.buf, self.seg, self.send, self.recv = buf, seg, send, recv

    def index(self, n):
        _, shard, inner, core = place()
        row, flip, other = (n // 2) % 2, n // 4, n % 2
        return 2 * (lax.rem(shard + 2 * row, 4) + other * (1 - 2 * core)) + inner + flip * (1 - 2 * inner)

    def copy(self, slot):
        across, beside, twin = partners()
        low, high, whole = (0, SPREAD_SPLIT), (SPREAD_SPLIT, self.seg - SPREAD_SPLIT), (0, self.seg)
        n, (first, size), device = {
            0: (0, low, across),
            9: (0, high, across),
            1: (0, high, beside),
            10: (0, low, beside),
            2: (0, whole, twin),
            3: (4, low, beside),
            4: (4, whole, twin),
            5: (2, high, across),
            6: (2, whole, twin),
            7: (6, low, twin),
            8: (6, high, twin),
        }[slot]
        ref = self.buf.at[aligned(self.index(n) * self.seg + first, size)]
        return remote(ref, ref, self.send.at[slot], self.recv.at[slot], device)

    def push(self, *slots):
        for slot in slots:
            self.copy(slot).start()

    def came(self, *slots):
        for slot in slots:
            self.copy(slot).wait_recv()

    def start(self):
        self.push(0, 1, 9, 10, 2)

    def first(self):
        self.came(1)
        self.push(5)
        self.came(0)
        self.push(3)

    def near(self):
        self.came(10)
        self.push(6)
        self.came(9)
        self.push(4)

    def far(self):
        self.came(3)
        self.push(7)
        self.came(5)
        self.push(8)

    def sent(self):
        for slot in self.slots:
            self.copy(slot).wait_send()

    def end(self):
        self.came(2, 4, 6, 7, 8)
        self.sent()

    def before(self, n):
        return {
            1: (lambda: self.came(2),),
            2: (self.first, self.near),
            3: (lambda: self.came(6),),
            5: (lambda: self.came(4),),
            6: (self.far,),
            7: (lambda: self.came(7, 8),),
        }.get(n, ())


class Collect:
    def __init__(self, part, seg, total, pair, near, joined, send, recv):
        self.part, self.seg, self.total = part, seg, total
        self.pair, self.near, self.joined, self.send, self.recv = pair, near, joined, send, recv
        _, self.shard, self.inner, core = place()
        self.twin_shard = self.shard + 1 - 2 * core
        self.low, self.high, self.whole = (0, COLLECT_SPLIT), (COLLECT_SPLIT, seg - COLLECT_SPLIT), (0, seg)
        self.cols = pl.ds(0, D)

    def index(self, s, k):
        row, flip = 1 - k % 2, 1 - k // 2
        return 2 * lax.rem(s + 2 * row, 4) + self.inner + flip * (1 - 2 * self.inner)

    def pair_copy(self, k):
        src = self.part.at[aligned(self.index(self.twin_shard, k) * self.seg, self.seg), self.cols]
        return remote(src, self.pair.at[k], self.send.at[k], self.recv.at[k], partners()[2])

    def copy(self, slot):
        across, beside, _ = partners()
        src, dst, (first, size), device = {
            4: (self.pair.at[0], self.joined, self.low, across),
            5: (self.pair.at[0], self.joined, self.high, beside),
            6: (self.pair.at[1], self.near.at[0], self.low, across),
            7: (self.pair.at[2], self.near.at[1], self.high, beside),
            8: (self.pair.at[2], self.near.at[1], self.low, beside),
            9: (self.pair.at[1], self.near.at[0], self.high, across),
        }[slot]
        rows = pl.ds(first, size)
        return remote(src.at[rows], dst.at[rows], self.send.at[slot], self.recv.at[slot], device)

    def over(self, span, body):
        def step(n, _):
            body(aligned(span[0] + n * 16, 16))
            return 0

        lax.fori_loop(0, span[1] // 16, step, 0)

    def mine(self, k, rows):
        return self.part[aligned(self.index(self.shard, k) * self.seg + rows.start, 16), self.cols].astype(F32)

    def add_pair(self, k):
        def add(rows):
            self.pair[k, rows] = (self.mine(k, rows) + self.pair[k, rows].astype(F32)).astype(BF16)

        self.pair_copy(k).wait_recv()
        self.over(self.whole, add)
        for slot in ((4, 5), (6,), (7,))[k]:
            self.copy(slot).start()

    def add_own(self):
        def add(rows):
            self.total[rows] = self.mine(3, rows) + self.pair[3, rows].astype(F32)

        self.pair_copy(3).wait_recv()
        self.over(self.whole, add)

    def pass_on(self):
        for slot, k, span, after in ((4, 2, self.low, 8), (5, 1, self.high, 9)):

            def add(rows):
                self.pair[k, rows] = (self.pair[k, rows].astype(F32) + self.joined[rows].astype(F32)).astype(BF16)

            self.copy(slot).wait_recv()
            self.over(span, add)
            self.copy(after).start()

    def push(self):
        for k in range(4):
            self.pair_copy(k).start()

    def make(self, n, produce):
        k, own = n // 2, n % 2
        produce(self.index(jnp.where(own == 1, self.shard, self.twin_shard), k))

        @pl.when(own == 0)
        def _():
            self.pair_copy(k).start()

        for m in range(3):

            @pl.when(n == 2 * m + 1)
            def _():
                self.add_pair(m)
                if m == 2:
                    self.pass_on()

        pl.when(n == 7)(self.add_own)

    def end(self):
        def add(rows):
            near = self.near[0, rows].astype(F32) + self.near[1, rows].astype(F32)
            self.total[rows] = self.total[rows] + near

        for slots, span in (((6, 8), self.low), ((7, 9), self.high)):
            for slot in slots:
                self.copy(slot).wait_recv()
            self.over(span, add)
        for k in range(4):
            self.pair_copy(k).wait_send()
        for slot in range(4, 10):
            self.copy(slot).wait_send()


def norm_scale(values):
    return lax.rsqrt(jnp.mean(values * values, axis=-1, keepdims=True) + NORM_EPSILON)


def by_rows(rows, body, carry=0):
    def step(n, carry):
        return body(aligned(n * ROWS, ROWS), carry)

    return lax.fori_loop(0, rows // ROWS, step, carry)


def norm_back(values, gain, upstream):
    scale = norm_scale(values)
    scaled = gain * upstream
    inner = jnp.mean(scaled * values, axis=-1, keepdims=True)
    return (
        scale * scaled - values * scale * scale * scale * inner,
        jnp.sum(upstream * values * scale, axis=0, keepdims=True),
    )


REFS = (
    "tok", "cot", "gains", "weights",
    "block_out", "input_grad", "gain_sums", "mine", "theirs", "n1_held", "slot0", "slot1", "slot2", "slot3",
    "w0", "w1", "w2", "w3", "seq_a", "seq_b", "du", "act", "c_all", "gated", "mixed", "resid", "dresid", "total",
    "pair", "near", "joined", "g1", "g2", "g3", "stage", "sum", "tail", "outgoing", "tap_sums", "gain_in", "gain_line",
    "held", "loaded", "send_x", "recv_x", "send_z", "recv_z", "send_s", "recv_s", "send_c", "recv_c", "credit",
    "halo_send", "halo_recv", "send_g", "recv_g", "fetched", "fetches", "stored", "send_o", "recv_o",
    "send_a", "recv_a", "send_l", "recv_l",
)


def column_pieces(half):
    pieces = [(m * QUARTER + half * HALF_Q, m * HALF_Q, HALF_Q, 0) for m in range(4)]
    for k, (start, units) in enumerate(zip(UNIT_STARTS, UNIT_CHUNKS), 1):
        real = min(units, HALF_F - start)
        for m in range(3):
            first = 4 * QUARTER + m * UNITS + half * HALF_F + start
            pieces.append((first, STARTS[k] + m * units, real, units - real))
    return pieces


def block_kernel(layers, rows, *all_refs):
    r = dict(zip(REFS, all_refs, strict=True))
    tok, cot, gains = r["tok"], r["cot"], r["gains"]
    seq_a, seq_b, du, act = r["seq_a"], r["seq_b"], r["du"], r["act"]
    c_all, gated, mixed, total = r["c_all"], r["gated"], r["mixed"], r["total"]
    weights = (r["w0"], r["w1"], r["w2"], r["w3"])
    seg = tok.shape[0]
    _, shard, inner, _ = place()
    outer, at = line()
    me = 2 * shard + inner
    my_rows = aligned(me * seg, seg)
    chunks = list(zip(range(1, 1 + len(UNIT_CHUNKS)), UNIT_STARTS, UNIT_CHUNKS))
    gather = Gather(
        layers, rows, r["g1"], weights, r["send_x"], r["recv_x"], r["send_z"], r["recv_z"]
    )
    reduce = Reduce(
        layers, rows, (r["w2"], r["g1"], r["g2"], r["g3"]), (r["slot0"], r["slot1"], r["slot2"], r["slot3"]),
        r["stage"], r["w1"], r["sum"], r["outgoing"], r["mine"], r["theirs"],
        (r["send_g"], r["recv_g"], r["fetched"], r["fetches"], r["stored"], r["send_o"], r["recv_o"]),
    )

    def spread(buf, n):
        return Spread(buf, seg, r["send_s"].at[n], r["recv_s"].at[n])

    def collect(part, n):
        return Collect(part, seg, total, r["pair"], r["near"], r["joined"], r["send_c"].at[n], r["recv_c"].at[n])

    one, up, two, three = spread(seq_a, 0), spread(seq_b, 1), spread(seq_a, 2), spread(seq_a, 3)
    branch, down, feed, inputs = collect(seq_a, 0), collect(seq_b, 1), collect(du, 2), collect(seq_a, 3)
    lanes = lax.broadcasted_iota(jnp.int32, (seg, WIDE), 1) < HALF_Q
    taps = pltpu.roll(gains[...], lax.rem(D - shard * QUARTER - inner * HALF_Q, D), 1)[2:5, :WIDE]
    kept = pl.ds(D, WIDE)
    sums, tap_sums = r["gain_sums"], r["tap_sums"]

    def block(t):
        return aligned(t * seg, seg)

    def mine(part):
        return pl.ds(pl.multiple_of(me * seg + part.start, 16), part.size)

    def first_norm():
        def rows(part, _):
            values = tok[part].astype(F32)
            seq_a[mine(part)] = (values * norm_scale(values) * gains[0:1, :]).astype(BF16)
            return 0

        by_rows(seg, rows)

    def up_start():
        seq_b[my_rows] = cot[...]
        up.start()

    def held():
        return pltpu.make_async_copy(seq_a, r["n1_held"], r["held"])

    def reload():
        return pltpu.make_async_copy(r["n1_held"], seq_b, r["held"])

    def project(s):
        for i in (0, 1):
            parts = dot(seq_a[block(2 * s + i)], weights[0][...])
            b = jnp.where(lanes, parts[:, :WIDE], 0.0)
            c = pltpu.roll(parts[:, 128 : 128 + 384], 384 - 64, 1)[:, :WIDE]
            x = parts[:, 384 : 384 + WIDE]
            c_all[s, pl.ds(i * seg, seg)] = jnp.where(lanes, c, 0.0)
            gated[s, pl.ds(8 + i * seg, seg)] = (b * x).astype(BF16).astype(F32)

    def ahead():
        return remote(
            gated.at[:, pl.ds(2 * seg, 8)], gated.at[:, pl.ds(0, 8)], r["halo_send"].at[0], r["halo_recv"].at[0], at(1)
        )

    def halo():
        pl.when(outer < layers - 1)(lambda: ahead().start())

        @pl.when(outer == 0)
        def _():
            gated[:, pl.ds(0, 8)] = jnp.zeros((GROUPS, 8, WIDE), F32)

    def convolved(s, i):
        return (
            taps[0:1, :] * gated[s, pl.ds(6 + i * seg, seg)]
            + taps[1:2, :] * gated[s, pl.ds(7 + i * seg, seg)]
            + taps[2:3, :] * gated[s, pl.ds(8 + i * seg, seg)]
        )

    def convolve(t):
        for i in (0, 1):

            @pl.when(t % 2 == i)
            def _():
                s = t // 2
                mixed[block(t)] = pltpu.roll(c_all[s, pl.ds(i * seg, seg)] * convolved(s, i), 64, 1).astype(BF16)

        seq_a[block(t)] = dot_rows(mixed[block(t)], weights[0][:, pl.ds(512, WIDE)]).astype(BF16)

    def branch_end():
        branch.end()
        allow(r["credit"].at[0])

    def second_norm():
        def rows(part, _):
            values = tok[part].astype(F32) + total[part]
            r["resid"][part] = values
            seq_a[mine(part)] = (values * norm_scale(values) * gains[1:2, :]).astype(BF16)
            return 0

        by_rows(seg, rows)
        pl.semaphore_wait(r["credit"].at[0], 3)

    def hidden(k, start, units, t):
        ref, here = weights[k], block(t)
        gate = dot(seq_a[here], ref[:, pl.ds(0, units)])
        upval = dot(seq_a[here], ref[:, pl.ds(units, units)])
        dact = dot(seq_b[here], ref[:, pl.ds(2 * units, units)])
        sigma = jax.nn.sigmoid(gate)
        silu = gate * sigma
        act[here, pl.ds(start, units)] = (silu * upval).astype(BF16)
        dgate = dact * upval * sigma * (1.0 + gate * (1.0 - sigma))
        du[here, pl.ds(2 * start, units)] = dgate.astype(BF16)
        du[here, pl.ds(2 * start + units, units)] = (dact * silu).astype(BF16)

    def slice_of(n):
        return jnp.where(outer < layers // 2, D // SLICE - 1 - n, n)

    def gate_up_grads(k, start, units, n):
        part = slice_of(n)
        left = seq_a[:, aligned(part * SLICE, SLICE, 128)]
        reduce.grads[k][aligned(part * SLICE, SLICE), pl.ds(0, 2 * units)] = dot_columns(
            left, du[:, pl.ds(2 * start, 2 * units)]
        ).astype(BF16)

    def down_grads(k, start, units, n):
        part = slice_of(n)
        left = seq_b[:, aligned(part * SLICE, SLICE, 128)]
        reduce.grads[k][aligned(part * SLICE, SLICE), pl.ds(2 * units, units)] = dot_columns(
            left, act[:, pl.ds(start, units)]
        ).astype(BF16)

    def grads(k, start, units, n):
        gate_up_grads(k, start, units, n)
        down_grads(k, start, units, n)
        reduce.direct(k, slice_of(n))

    def second(t):
        here = block(t)
        seq_b[here] = sum(
            dot_rows(du[here, pl.ds(2 * start, 2 * units)], weights[k][:, pl.ds(0, 2 * units)])
            for k, start, units in chunks
        ).astype(BF16)

    def down_end():
        down.end()
        reload().start()
        allow(r["credit"].at[1])

    def forward(t):
        here = block(t)
        du[here, pl.ds(0, D)] = sum(
            dot_rows(act[here, pl.ds(start, units)], weights[k][:, pl.ds(2 * units, units)])
            for k, start, units in chunks
        ).astype(BF16)

    def second_back():
        def rows(part, gain):
            dpart, dgain = norm_back(r["resid"][part], gains[1:2, :], total[part])
            dresid = cot[part].astype(F32) + dpart
            r["dresid"][part] = dresid
            seq_a[mine(part)] = dresid.astype(BF16)
            return gain + dgain

        sums[...] = jnp.zeros(sums.shape, F32)
        tap_sums[...] = jnp.zeros(tap_sums.shape, F32)
        sums[1:2, pl.ds(0, D)] = by_rows(seg, rows, jnp.zeros((1, D), F32))
        pl.semaphore_wait(r["credit"].at[1], 3)

    def mix_back(t):
        s, here = t // 2, block(t)
        dmixed = pltpu.roll(dot(seq_a[here], weights[0][:, pl.ds(512, WIDE)]), WIDE - 64, 1)
        dmixed = jnp.where(lanes, dmixed, 0.0)
        for i in (0, 1):

            @pl.when(t % 2 == i)
            def _():
                du[here, kept] = (dmixed * convolved(s, i)).astype(BF16)
                c_all[s, pl.ds(i * seg, seg)] = dmixed * c_all[s, pl.ds(i * seg, seg)]

    def after():
        return remote(
            c_all.at[:, pl.ds(0, 8)], c_all.at[:, pl.ds(2 * seg, 8)], r["halo_send"].at[1], r["halo_recv"].at[1], at(-1)
        )

    def halo_back():
        pl.when(outer > 0)(lambda: after().start())

        @pl.when(outer == layers - 1)
        def _():
            c_all[:, pl.ds(2 * seg, 8)] = jnp.zeros((GROUPS, 8, WIDE), F32)

    def conv_back(n):
        for i in (0, 1):
            pl.when(n // GROUPS == i)(functools.partial(conv_back_half, n % GROUPS, i))

    def conv_back_half(s, i):
        t = block(2 * s + i)
        dconv = c_all[s, pl.ds(i * seg, seg)]
        dgated = (
            taps[2:3, :] * dconv
            + taps[1:2, :] * c_all[s, pl.ds(1 + i * seg, seg)]
            + taps[0:1, :] * c_all[s, pl.ds(2 + i * seg, seg)]
        )
        parts = dot(seq_b[t], weights[0][:, pl.ds(0, 640)])
        db = dgated * parts[:, 384:640]
        dx = dgated * parts[:, :WIDE]
        dc = jnp.concatenate([du[t, kept].astype(F32), jnp.zeros((seg, 128), F32)], axis=1)
        dc = pltpu.roll(dc, 64, 1)
        act[t, pl.ds(0, 128)] = db[:, :128].astype(BF16)
        act[t, pl.ds(128, 128)] = (db[:, 128:] + dc[:, :128]).astype(BF16)
        act[t, pl.ds(256, 128)] = dc[:, 128:256].astype(BF16)
        act[t, pl.ds(384, WIDE)] = dx.astype(BF16)
        act[t, pl.ds(640, 128)] = jnp.zeros((seg, 128), BF16)
        for k in range(3):
            moved = gated[s, pl.ds(6 + k + i * seg, seg)]
            tap_sums[k : k + 1] = tap_sums[k : k + 1] + jnp.sum(dconv * moved, axis=0, keepdims=True)

    def conv_grads(n):
        part = slice_of(n)
        held_rows, cols = aligned(part * SLICE, SLICE), aligned(part * SLICE, SLICE, 128)
        ref = reduce.grads[0]
        of_parts = dot_columns(seq_b[:, cols], act[:, pl.ds(0, CONV_COLS)])
        ref[held_rows, pl.ds(0, 512)] = of_parts[:, :512].astype(BF16)
        of_mixed = dot_columns(seq_a[:, cols], mixed[...])
        ref[held_rows, pl.ds(512, WIDE)] = (of_parts[:, 512:] + of_mixed).astype(BF16)
        reduce.direct(0, part)

    def feed_end():
        feed.end()
        allow(r["credit"].at[2])
        r["block_out"][...] = (r["resid"][...] + total[...]).astype(BF16)

    def first(t):
        here = block(t)
        seq_a[here] = dot_rows(act[here, pl.ds(0, 640)], weights[0][:, pl.ds(0, 640)]).astype(BF16)

    def first_back():
        def rows(part, gain):
            dpart, dgain = norm_back(tok[part].astype(F32), gains[0:1, :], total[part])
            r["input_grad"][part] = (r["dresid"][part] + dpart).astype(BF16)
            return gain + dgain

        sums[0:1, pl.ds(0, D)] = by_rows(seg, rows, jnp.zeros((1, D), F32))
        sums[2:5, aligned(me * WIDE, WIDE, 128)] = tap_sums[0:3]

    def gains_across(n):
        return remote(sums, r["gain_in"].at[n], r["send_a"].at[n], r["recv_a"].at[n], partners()[n])

    def gains_add(n):
        gains_across(n).wait()
        sums[...] = sums[...] + r["gain_in"][n]

    def line_copy(sign, steps):
        slot = (0 if sign > 0 else 1, steps - 1)
        return remote(
            sums, r["gain_line"].at[slot], r["send_l"].at[slot], r["recv_l"].at[slot], at(sign * steps)
        )

    def gains_line():
        for steps in range(1, layers):
            for sign in (1, -1):
                pl.when(in_line(outer + sign * steps, layers))(line_copy(sign, steps).start)

    def gains_end():
        for steps in range(1, layers):
            for sign in (1, -1):
                pl.when(in_line(outer + sign * steps, layers))(line_copy(sign, steps).wait_send)
                pl.when(in_line(outer - sign * steps, layers))(line_copy(sign, steps).wait_recv)

        own_sums = sums[...]
        for origin in range(layers):
            for steps in range(1, layers):
                for sign in (1, -1):

                    @pl.when((outer - sign * steps == origin))
                    def _():
                        came = r["gain_line"][0 if sign > 0 else 1, steps - 1]
                        sums[...] = came if origin == 0 else sums[...] + came

            if origin > 0:

                @pl.when(outer == origin)
                def _():
                    sums[...] = sums[...] + own_sums

    def end():
        reduce.finish(0)
        for k in range(len(WIDTHS)):
            reduce.wait_sent(k)
        pl.when(outer < layers - 1)(lambda: ahead().wait_send())
        pl.when(outer > 0)(lambda: after().wait_send())

    windows = [
        (r["resid"], 0, D), (r["dresid"], D, D), (total, 2 * D, D), (r["resid"], 3 * D, D),
        (r["tail"], 4 * D, GROUP_COLS - 4 * D),
    ]

    def load(n):
        ref, first, width = windows[n]
        return pltpu.make_async_copy(
            r["weights"].at[:, pl.ds(first, width)], ref.at[pl.ds(0, rows)], r["loaded"].at[n]
        )

    def start():
        for n in (0, 1, 2, 4):
            load(n).start()
        greet(layers)

    def cut(k):
        def read(part, first, width):
            found = []
            for n, (ref, low, size) in enumerate(windows):
                start, stop = max(first, low), min(first + width, low + size)
                if start < stop and (n == 0) == (k == 0):
                    found.append(ref[part, start - low : stop - low])
            return found

        def band(n, _):
            part = aligned(n * 16, 16)
            halves = []
            for half in (0, 1):
                pieces = []
                for first, own, width, padding in column_pieces(half):
                    if STARTS[k] <= own < STARTS[k] + WIDTHS[k]:
                        pieces += read(part, first, width)
                        if padding:
                            pieces.append(jnp.zeros((16, padding), F32))
                halves.append(jnp.concatenate(pieces, axis=1))
            is_low = inner == 0
            seq = lax.axis_index("seq")
            own_rows = aligned(seq * rows + n * 16, 16)
            weights[k][own_rows, :] = jnp.where(is_low, halves[0], halves[1]).astype(BF16)
            gather.other_rows(k)[part, :] = jnp.where(is_low, halves[1], halves[0]).astype(BF16)
            return 0

        for n in (0,) if k == 0 else (1, 2, 3, 4) if k == CUT_FIRST else ():
            load(n).wait()
        lax.fori_loop(0, rows // 16, band, 0)
        if k == 0:
            load(3).start()

    def hold():
        held().start()

    def hold_end():
        held().wait()

    def halo_end():
        pl.when(outer > 0)(lambda: ahead().wait_recv())

    def reload_end():
        reload().wait()

    def halo_back_end():
        pl.when(outer < layers - 1)(lambda: after().wait_recv())

    def feed_credit():
        pl.semaphore_wait(r["credit"].at[2], 3)

    def from_spread(moved, body):
        def step(n):
            for m in range(8):
                if moved.before(m):

                    @pl.when(n == m)
                    def _():
                        for act in moved.before(m):
                            act()

            body(moved.index(n))

        return step

    def each(body, *cases):
        return [functools.partial(body, *(case if isinstance(case, tuple) else (case,))) for case in cases]

    every = range(len(WIDTHS))
    cuts = each(cut, *every)
    exchange, send_own, send_other = (
        each(body, *every) for body in (gather.exchange, gather.send_own, gather.send_other)
    )
    step = [each(gather.steps, (k, 1, 1), (k, 2, 2), (k, 3)) for k in every]
    join_far = each(reduce.join, *((k, layers - 2, 2) for k in every))
    join_near = each(reduce.join, *((k, 1, 1) for k in every))
    final = each(reduce.final, (0, 3), 1, (2, 1), (3, 2))
    feed_pair = each(feed.add_pair, 0, 1, 2)
    gain_send = [lambda n=n: gains_across(n).start() for n in range(3)]
    gain_add = each(gains_add, 0, 1, 2)
    d3_far = functools.partial(reduce.direct, 3, least=2)
    d3_near = functools.partial(reduce.direct, 3, most=1)
    blocks, parts = 2 * GROUPS, D // SLICE
    proj = Loop(GROUPS, project)
    mix = Loop(blocks, lambda n: branch.make(n, convolve))
    hid1 = Loop(blocks, from_spread(two, functools.partial(hidden, *chunks[0])))
    hid2, hid3 = (Loop(blocks, functools.partial(hidden, *chunk)) for chunk in chunks[1:])
    grad1, grad2 = (Loop(parts, functools.partial(grads, *chunk)) for chunk in chunks[:2])
    down3 = Loop(parts, functools.partial(down_grads, *chunks[2]))
    back2 = Loop(blocks, lambda n: down.make(n, second))
    gate3 = Loop(parts, functools.partial(gate_up_grads, *chunks[2]))
    ffn = Loop(blocks, forward)
    back_mix = Loop(blocks, from_spread(three, mix_back))
    back_conv = Loop(blocks, conv_back)
    grad0 = Loop(parts, conv_grads)
    back1 = Loop(blocks, lambda n: inputs.make(n, first))
    play(
        [
            start, cuts[0], exchange[0], send_own[0], first_norm, one.start, cuts[2], send_other[0], cuts[1],
            send_own[1], exchange[2], one.first, step[0][0], exchange[1], cuts[3], one.near, send_other[2], one.far,
            step[0][1], up_start, step[0][2], one.end, hold, proj[0], proj[1], proj[2], proj[3], halo,
            send_other[1], hold_end, up.first, send_own[2], halo_end, mix[0], mix[1], mix[2], mix[3], send_own[3],
            step[1][0], mix[4], mix[5], mix[6], up.near, exchange[3], up.far, mix[7], step[1][1], branch_end,
            send_other[3], second_norm, step[2][0], two.start, step[1][2], up.end, hid1[0], hid1[1], hid1[2],
            hid1[3], hid1[4], gather.crossed, hid1[5], hid1[6], hid1[7], two.sent, grad1[0], grad1[1], grad1[2],
            grad1[3], step[2][1], step[2][2], hid2[0], hid2[1], hid2[2], hid2[3], hid2[4], hid2[5], hid2[6],
            hid2[7], grad2[0], grad2[1], step[3][0], grad2[2], grad2[3], step[3][1], step[3][2], hid3[0], hid3[1],
            hid3[2], hid3[3], hid3[4], hid3[5], hid3[6], hid3[7], down3[0], down3[1], down3[2], down3[3], back2[0],
            join_far[1], back2[1], back2[2], back2[3], back2[4], back2[5], back2[6], back2[7], gate3[0], gate3[1],
            gate3[2], gate3[3], ffn[0], ffn[1], ffn[2], ffn[3], ffn[4], ffn[5], ffn[6], ffn[7], down_end,
            second_back, three.start, join_near[1], back_mix[0], join_far[2], feed.push, back_mix[1], back_mix[2],
            back_mix[3], back_mix[4], back_mix[5], feed_pair[0], back_mix[6], back_mix[7], three.sent, halo_back,
            gather.finish, feed_pair[1], feed_pair[2], reload_end, back_conv[0], back_conv[1], d3_far, back_conv[2],
            feed.pass_on, back_conv[3], join_near[2], final[1], halo_back_end, back_conv[4], back_conv[5],
            feed.add_own, back_conv[6], back_conv[7], grad0[0], grad0[1], d3_near, grad0[2], join_far[3], grad0[3],
            feed_end, feed_credit, back1[0], back1[1], back1[2], back1[3], join_near[3], join_far[0], back1[4],
            back1[5], back1[6], final[2], join_near[0], back1[7], inputs.end, first_back, gain_send[0], final[3],
            gain_add[0], gain_send[1], gain_add[1], gain_send[2], gain_add[2], gains_line, final[0], gains_end, end,
        ]
    )


class Loop:
    def __init__(self, count, body):
        self.count, self.body = count, body

    def __getitem__(self, n):
        return (self, n)


def play(order):
    order = list(order)
    while order:
        entry = order.pop(0)
        if not isinstance(entry, tuple):
            entry()
            continue
        loop, _ = entry
        between = {}
        for n in range(1, loop.count):
            between[n] = []
            while order[0] != (loop, n):
                between[n].append(order.pop(0))
            order.pop(0)

        def turn(n, _):
            for m, acts in between.items():
                if acts:

                    @pl.when(n == m)
                    def _():
                        play(acts)

            loop.body(n)
            return 0

        lax.fori_loop(0, loop.count, turn, 0)


def block_step(tok, cot, gains, weights, layers):
    rows, seg = weights.shape[0], tok.shape[0]
    count = len(WIDTHS)
    tokens = 2 * GROUPS * seg
    vmem, anywhere = pl.BlockSpec(memory_space=pltpu.VMEM), pl.BlockSpec(memory_space=pl.ANY)
    shape, scratch = jax.ShapeDtypeStruct, pltpu.VMEM
    dma, regular = pltpu.SemaphoreType.DMA, pltpu.SemaphoreType.REGULAR
    hops = layers - 1
    wide, biggest = sum(WIDTHS), max(WIDTHS)
    out_shape = [
        shape((seg, D), BF16),
        shape((seg, D), BF16),
        shape((8, 2 * GROUPS * WIDE), F32),
        shape((rows, wide), F32),
        shape((rows, wide), BF16),
        shape((tokens, D), BF16),
    ] + [shape((2, hops, 2 * rows, width), BF16) for width in WIDTHS]
    scratch_shapes = (
        [scratch((D, width), BF16) for width in WIDTHS]
        + [
            scratch((tokens, D), BF16),
            scratch((tokens, D), BF16),
            scratch((tokens, 2 * PAD_F), BF16),
            scratch((tokens, PAD_F), BF16),
            scratch((GROUPS, 8 + 2 * seg, WIDE), F32),
            scratch((GROUPS, 8 + 2 * seg, WIDE), F32),
            scratch((tokens, WIDE), BF16),
            scratch((seg, D), F32),
            scratch((seg, D), F32),
            scratch((seg, D), F32),
            scratch((4, seg, D), BF16),
            scratch((2, seg, D), BF16),
            scratch((seg, D), BF16),
        ]
        + [scratch((D, width), BF16) for width in WIDTHS[1:]]
        + [
            scratch((2 * rows, biggest), BF16),
            scratch((rows, biggest), F32),
            scratch((rows, GROUP_COLS - 4 * D), F32),
            scratch((rows, wide), BF16),
            scratch((8, WIDE), F32),
            scratch((3, 8, 2 * GROUPS * WIDE), F32),
            scratch((2, hops, 8, 2 * GROUPS * WIDE), F32),
            dma,
            dma((5,)),
            dma((count,)),
            dma((count,)),
            dma((count, 2, hops, 2)),
            dma((count, 2, hops, 2)),
            dma((4, 11)),
            dma((4, 11)),
            dma((4, 10)),
            dma((4, 10)),
            regular((3,)),
            dma((2,)),
            dma((2,)),
            dma((count, 2, hops)),
            dma((count, 2, hops)),
            dma,
            dma((4,)),
            dma((count,)),
            dma((count,)),
            dma((count,)),
            dma((3,)),
            dma((3,)),
            dma((2, hops)),
            dma((2, hops)),
        ]
    )
    return pl.pallas_call(
        functools.partial(block_kernel, layers, rows),
        out_shape=out_shape,
        in_specs=[vmem] * 3 + [anywhere],
        out_specs=[vmem] * 3 + [anywhere] * (3 + count),
        scratch_shapes=scratch_shapes,
        compiler_params=pltpu.CompilerParams(
            collective_id=0, has_side_effects=True, vmem_limit_bytes=VMEM_BYTES
        ),
        name="block_step",
    )(tok, cot, gains, weights)[:5]


def band(rows, most):
    return max(size for size in range(16, most + 1, 16) if rows % size == 0)


def adam_update(param, grad, first, second, rate, decay):
    first_new = MOMENT_DECAY * first + (1.0 - MOMENT_DECAY) * grad
    second_new = SQUARE_DECAY * second + (1.0 - SQUARE_DECAY) * grad * grad
    root = jnp.sqrt(second_new * (1.0 / (1.0 - SQUARE_DECAY**STEP))) + ADAM_EPSILON
    step = first_new * (rate / (1.0 - MOMENT_DECAY**STEP)) / root
    return (first_new, second_new, param * (1.0 - rate * decay) - step)


def update_kernel(
    inner_ref, mine_ref, theirs_ref, weights_ref, first_ref, second_ref, sums_ref, gains_ref, gains_first_ref,
    gains_second_ref, block_ref, input_ref, grad_out, first_out, second_out, weights_out, gains_grad_out,
    gains_first_out, gains_second_out, gains_out, block_out, input_out,
):
    is_low = inner_ref[0] == 0
    mine, theirs = mine_ref[...], theirs_ref[...].astype(F32)
    for half in (0, 1):
        chosen = jnp.where(is_low, mine, theirs) if half == 0 else jnp.where(is_low, theirs, mine)
        for first, own, width, _ in column_pieces(half):
            grad_out[:, first : first + width] = chosen[:, own : own + width]
    first_out[...], second_out[...], weights_out[...] = adam_update(
        weights_ref[...], grad_out[...], first_ref[...], second_ref[...], WEIGHT_RATE, WEIGHT_DECAY
    )

    @pl.when(pl.program_id(0) == 0)
    def _():
        gains_grad_out[0:2] = sums_ref[0:2, :D]
        for n in range(2 * GROUPS):
            gains_grad_out[2:5, n * HALF_Q : (n + 1) * HALF_Q] = sums_ref[2:5, n * WIDE : n * WIDE + HALF_Q]
        gains_first_out[...], gains_second_out[...], gains_out[...] = adam_update(
            gains_ref[...], gains_grad_out[...], gains_first_ref[...], gains_second_ref[...], GAIN_RATE, 0.0
        )
        block_out[...] = block_ref[...]
        input_out[...] = input_ref[...]


def update(inner, mine, theirs, weights, first, second, sums, gains, gains_first, gains_second, block, grad):
    rows, cols = weights.shape
    wide = mine.shape[1]
    size = band(rows, 32)
    by_row = lambda width: pl.BlockSpec((size, width), lambda n: (n, 0))
    whole = lambda values: pl.BlockSpec(values.shape, lambda n: (0, 0))
    shape = jax.ShapeDtypeStruct
    return pl.pallas_call(
        update_kernel,
        grid=(rows // size,),
        out_shape=[shape((rows, cols), F32)] * 4 + [shape(gains.shape, F32)] * 4 + [shape(block.shape, BF16)] * 2,
        in_specs=[pl.BlockSpec(memory_space=pltpu.SMEM)]
        + [by_row(wide)] * 2
        + [by_row(cols)] * 3
        + [whole(sums)]
        + [whole(gains)] * 3
        + [whole(block)] * 2,
        out_specs=[by_row(cols)] * 4 + [whole(gains)] * 4 + [whole(block)] * 2,
        compiler_params=pltpu.CompilerParams(vmem_limit_bytes=VMEM_BYTES),
        name="update",
    )(inner, mine, theirs, weights, first, second, sums, gains, gains_first, gains_second, block, grad)


def on_device(
    tokens, gains_taps, weights, cotangent, weight_first, weight_second, gains_first, gains_second
):
    layers = lax.axis_size("seq") // 2
    inner_word = (lax.axis_index("seq") % 2).astype(jnp.int32).reshape(1)
    block_out, input_grad, gain_sums, mine, theirs = block_step(
        tokens[0], cotangent[0], gains_taps, weights, layers
    )
    (
        weight_grad, weight_first_new, weight_second_new, weight_new,
        gains_grad, gains_first_new, gains_second_new, gains_new, block_out, input_grad,
    ) = update(
        inner_word, mine, theirs, weights, weight_first, weight_second,
        gain_sums, gains_taps, gains_first, gains_second, block_out, input_grad,
    )
    return (
        block_out[None],
        input_grad[None],
        weight_grad,
        weight_first_new,
        weight_second_new,
        weight_new,
        gains_grad,
        gains_first_new,
        gains_second_new,
        gains_new,
    )


def solution(mesh):
    tokens, rows, whole = P("shard", "seq", None), P("seq", "shard"), P()
    return jax.shard_map(
        on_device,
        mesh=mesh,
        in_specs=(tokens, whole, rows, tokens, rows, rows, whole, whole),
        out_specs=(tokens, tokens, rows, rows, rows, rows, whole, whole, whole, whole),
        check_vma=False,
    )
```

```python
import functools

import jax
import jax.numpy as jnp
from jax import lax
from jax.experimental import pallas as pl
from jax.experimental.pallas import tpu as pltpu
from jax.sharding import PartitionSpec as P

D = 1536
FF = 6912
STEP = 10
GROUPS = 4
QUARTER = D // GROUPS
UNITS = FF // GROUPS
GROUP_COLS = 4 * QUARTER + 3 * UNITS
HALF_Q = QUARTER // 2
HALF_F = UNITS // 2
LANES = 128
PAD_F = -(-HALF_F // LANES) * LANES
WIDE = 256
CONV_COLS = 4 * HALF_Q
UNIT_CHUNKS = (384, 256, PAD_F - 640)
UNIT_STARTS = (0, 384, 640)
WIDTHS = (CONV_COLS,) + tuple(3 * units for units in UNIT_CHUNKS)
STARTS = tuple(sum(WIDTHS[:k]) for k in range(len(WIDTHS)))
SPREAD_SPLIT = 144
COLLECT_SPLIT = 112
REACH = (1, 1, 1, 1)
CUT_FIRST = 3
SLICE = 384
TILE = 16
ROWS = 48

MOMENT_DECAY = 0.9
SQUARE_DECAY = 0.95
ADAM_EPSILON = 1e-08
NORM_EPSILON = 1e-05
WEIGHT_RATE = 0.02
GAIN_RATE = 0.2
WEIGHT_DECAY = 0.1

BF16 = jnp.bfloat16
F32 = jnp.float32
MESH = pl.DeviceIdType.MESH
VMEM_BYTES = 63 * 1024 * 1024


def place():
    seq, shard = lax.axis_index("seq"), lax.axis_index("shard")
    inner, core = lax.rem(seq, 2), lax.rem(shard, 2)
    return seq, shard, inner, core


def partners():
    seq, shard, inner, core = place()
    across = {"seq": seq + 1 - 2 * inner, "shard": shard}
    beside = {"seq": seq, "shard": lax.rem(shard + 2, 4)}
    twin = {"seq": seq, "shard": shard + 1 - 2 * core}
    return across, beside, twin


def remote(src, dst, send, recv, device):
    return pltpu.make_async_remote_copy(
        src_ref=src, dst_ref=dst, send_sem=send, recv_sem=recv, device_id=device, device_id_type=MESH
    )


def line():
    seq, shard, _, _ = place()
    return seq // 2, lambda steps: {"seq": seq + 2 * steps, "shard": shard}


def greet(layers):
    outer, at = line()
    barrier = pltpu.get_barrier_semaphore()
    for device in partners():
        pl.semaphore_signal(barrier, inc=1, device_id=device, device_id_type=MESH)
    for steps in range(1, layers):
        for sign in (1, -1):

            @pl.when(in_line(outer + sign * steps, layers))
            def _():
                pl.semaphore_signal(barrier, inc=1, device_id=at(sign * steps), device_id_type=MESH)

    pl.semaphore_wait(barrier, 3 + layers - 1)


def in_line(index, layers):
    return (index >= 0) & (index < layers)


def allow(credit):
    for device in partners():
        pl.semaphore_signal(credit, inc=1, device_id=device, device_id_type=MESH)


def dot(left, right):
    return jnp.dot(left, right, preferred_element_type=F32)


def dot_rows(left, right):
    return lax.dot_general(left, right, (((1,), (1,)), ((), ())), preferred_element_type=F32)


def dot_columns(left, right):
    return lax.dot_general(left, right, (((0,), (0,)), ((), ())), preferred_element_type=F32)


def aligned(start, size, multiple=16):
    return pl.ds(pl.multiple_of(start, multiple), size)


class Gather:
    def __init__(self, layers, rows, oth, outs, send_x, recv_x, send_z, recv_z):
        self.layers, self.rows, self.oth, self.outs = layers, rows, oth, outs
        self.send_x, self.recv_x, self.send_z, self.recv_z = send_x, recv_x, send_z, recv_z
        self.seq, _, self.inner, _ = place()
        self.outer, self.at = line()
        self.across = partners()[0]

    def seq_rows(self, index):
        return aligned(index * self.rows, self.rows)

    def layer_rows(self, direction, distance):
        origin = self.outer - distance if direction == 0 else self.outer + distance
        return aligned(origin * 2 * self.rows, 2 * self.rows)

    def copy(self, k, src, dst, direction, distance, hop, piece):
        slot = (k, direction, distance + hop - 1, piece)
        return remote(
            src, dst, self.send_z.at[slot], self.recv_z.at[slot], self.at(hop if direction == 0 else -hop)
        )

    def goes(self, direction, hop):
        return in_line(self.outer + (hop if direction == 0 else -hop), self.layers)

    def has_come(self, direction, distance):
        return in_line(self.outer + (-distance if direction == 0 else distance), self.layers)

    def hops(self, k, distance):
        return range(1, min(REACH[k], self.layers - 1 - distance) + 1)

    def own_copy(self, k, direction, hop):
        here = self.outs[k].at[self.seq_rows(self.seq)]
        return self.copy(k, here, here, direction, 0, hop, 0)

    def other_copy(self, k, direction, hop):
        there = self.outs[k].at[self.seq_rows(self.seq + 1 - 2 * self.inner)]
        return self.copy(k, there, there, direction, 0, hop, 1)

    def pass_copy(self, k, direction, distance, hop):
        ref = self.outs[k].at[self.layer_rows(direction, distance)]
        return self.copy(k, ref, ref, direction, distance, hop, 0)

    def other_rows(self, k):
        return self.oth.at[pl.ds(k * self.rows, self.rows), pl.ds(0, WIDTHS[k])]

    def exchange(self, k):
        self.x_copy(k).start()

    def x_copy(self, k):
        here = self.outs[k].at[self.seq_rows(self.seq)]
        return remote(self.other_rows(k), here, self.send_x.at[k], self.recv_x.at[k], self.across)

    def crossed(self):
        for k in range(len(self.outs)):
            self.x_copy(k).wait_send()

    def send_own(self, k):
        for hop in self.hops(k, 0):
            for direction in (0, 1):

                @pl.when(self.goes(direction, hop))
                def _():
                    self.own_copy(k, direction, hop).start()

    def send_other(self, k):
        self.x_copy(k).wait_recv()
        for hop in self.hops(k, 0):
            for direction in (0, 1):

                @pl.when(self.goes(direction, hop))
                def _():
                    self.other_copy(k, direction, hop).start()

    def step(self, k, distance):
        for direction in (0, 1):

            @pl.when(self.has_come(direction, distance))
            def _():
                if distance <= REACH[k]:
                    origin = self.outer - distance if direction == 0 else self.outer + distance
                    for piece in (0, 1):
                        index = 2 * origin + (self.inner if piece == 0 else 1 - self.inner)
                        ref = self.outs[k].at[self.seq_rows(index)]
                        self.copy(k, ref, ref, direction, distance - 1, 1, piece).wait_recv()
                else:
                    ref = self.outs[k].at[self.layer_rows(direction, distance)]
                    self.copy(k, ref, ref, direction, distance - 1, 1, 0).wait_recv()
                if distance % REACH[k] == 0:
                    for hop in self.hops(k, distance):

                        @pl.when(self.goes(direction, hop))
                        def _():
                            self.pass_copy(k, direction, distance, hop).start()

    def steps(self, k, first, last=None):
        last = self.layers - 1 if last is None else min(last, self.layers - 1)
        for distance in range(first, last + 1):
            self.step(k, distance)

    def finish(self):
        for k in range(len(self.outs)):
            for distance in range(0, self.layers - 1, REACH[k]):
                for hop in self.hops(k, distance):
                    for direction in (0, 1):

                        @pl.when(self.goes(direction, hop) & self.has_come(direction, distance))
                        def _():
                            if distance == 0:
                                self.own_copy(k, direction, hop).wait_send()
                                self.other_copy(k, direction, hop).wait_send()
                            else:
                                self.pass_copy(k, direction, distance, hop).wait_send()


class Reduce:
    def __init__(self, layers, rows, grads, slots, stage, spare, total, outgoing, mine, theirs, sems):
        self.layers, self.rows, self.grads, self.slots = layers, rows, grads, slots
        self.stage, self.spare, self.total, self.outgoing = stage, spare, total, outgoing
        self.mine, self.theirs = mine, theirs
        self.send_g, self.recv_g, self.fetched, self.fetches, self.stored, self.send_o, self.recv_o = sems
        _, _, self.inner, _ = place()
        self.outer, self.at = line()
        self.across = partners()[0]

    def owner(self, direction, distance):
        return self.outer + distance if direction == 0 else self.outer - distance

    def upstream(self, direction, steps):
        return in_line(self.outer - steps if direction == 0 else self.outer + steps, self.layers)

    def block(self, k, owner):
        return self.grads[k].at[aligned(owner * 2 * self.rows, 2 * self.rows), pl.ds(0, WIDTHS[k])]

    def copy(self, k, src, direction, distance):
        slot = (direction, distance - 1)
        return remote(
            src,
            self.slots[k].at[slot],
            self.send_g.at[(k,) + slot],
            self.recv_g.at[(k,) + slot],
            self.at(1 if direction == 0 else -1),
        )

    def send(self, k, direction, distance):
        self.copy(k, self.block(k, self.owner(direction, distance)), direction, distance).start()

    def direct(self, k, part=None, least=1, most=None):
        for distance in range(most or self.layers - 1, least - 1, -1):
            for direction in (0, 1):
                owner = self.owner(direction, distance)
                here = in_line(owner, self.layers) & jnp.logical_not(self.upstream(direction, 1))
                if part is not None:
                    here = here & (owner * 2 * self.rows // SLICE == part)

                @pl.when(here)
                def _():
                    self.send(k, direction, distance)

    def fetch(self, k, direction, distance):
        slot = self.slots[k].at[direction, distance - 1]
        self.copy(k, slot, direction, distance).wait_recv()
        held = self.stage.at[:, pl.ds(0, WIDTHS[k])]
        copy = pltpu.make_async_copy(slot, held, self.fetched)
        copy.start()
        copy.wait()

    def tiles(self, body):
        def step(n, _):
            body(aligned(n * TILE, TILE))
            return 0

        lax.fori_loop(0, 2 * self.rows // TILE, step, 0)

    def join(self, k, most, least):
        cols = pl.ds(0, WIDTHS[k])
        for distance in range(most, least - 1, -1):
            for direction in (0, 1):
                owner = self.owner(direction, distance)

                @pl.when(in_line(owner, self.layers) & self.upstream(direction, 1))
                def _():
                    def add(tile):
                        base = self.owner(direction, distance) * 2 * self.rows
                        rows = pl.ds(pl.multiple_of(base + tile.start, 16), TILE)
                        ref = self.grads[k]
                        ref[rows, cols] = (
                            ref[rows, cols].astype(F32) + self.stage[tile, cols].astype(F32)
                        ).astype(BF16)

                    self.fetch(k, direction, distance + 1)
                    self.tiles(add)
                    self.send(k, direction, distance)

    def final(self, k, before=None):
        cols = pl.ds(0, WIDTHS[k])
        came = [(1, 0), (1, 1)]

        def fetch(n, distance, direction):
            return pltpu.make_async_copy(
                self.slots[k].at[direction, distance - 1],
                self.spare.at[pl.ds(n * 2 * self.rows, 2 * self.rows), cols],
                self.fetches.at[n],
            )

        for n, (distance, direction) in enumerate(came):

            @pl.when(self.upstream(direction, distance))
            def _():
                self.copy(k, self.slots[k].at[direction, distance - 1], direction, distance).wait_recv()
                fetch(n, distance, direction).start()

        if before is not None:
            self.store(before).wait()

        here, there = self.inner * self.rows, (1 - self.inner) * self.rows

        def each(base, body):
            def step(n, _):
                body(base + n * TILE, n * TILE)
                return 0

            lax.fori_loop(0, self.rows // TILE, step, 0)

        for n, (distance, direction) in enumerate(came):

            @pl.when(self.upstream(direction, distance))
            def _():
                fetch(n, distance, direction).wait()

        def add_up(flags):
            def total(rows):
                value = self.grads[k][aligned(self.outer * 2 * self.rows + rows, TILE), cols].astype(F32)
                for n, flag in enumerate(flags):
                    if flag:
                        value = value + self.spare[aligned(n * 2 * self.rows + rows, TILE), cols].astype(F32)
                return value

            def send(rows, at):
                self.outgoing[aligned(at, TILE), pl.ds(STARTS[k], WIDTHS[k])] = total(rows).astype(BF16)

            def keep(rows, at):
                self.total[aligned(at, TILE), cols] = total(rows)

            each(there, send)
            self.over(k).start()
            each(here, keep)
            self.store(k).start()

        patterns = {}
        for place_in_line in range(self.layers):
            flags = tuple(
                0 <= (place_in_line - distance if direction == 0 else place_in_line + distance) < self.layers
                for distance, direction in came
            )
            patterns.setdefault(flags, []).append(place_in_line)
        for flags, places in patterns.items():
            here_now = functools.reduce(jnp.logical_or, [self.outer == p for p in places])

            @pl.when(here_now)
            def _():
                add_up(flags)

    def over(self, k):
        wide = pl.ds(STARTS[k], WIDTHS[k])
        return remote(
            self.outgoing.at[:, wide], self.theirs.at[:, wide], self.send_o.at[k], self.recv_o.at[k], self.across
        )

    def store(self, k):
        return pltpu.make_async_copy(
            self.total.at[:, pl.ds(0, WIDTHS[k])], self.mine.at[:, pl.ds(STARTS[k], WIDTHS[k])], self.stored.at[k]
        )

    def wait_sent(self, k):
        for distance in range(1, self.layers):
            for direction in (0, 1):
                owner = self.owner(direction, distance)

                @pl.when(in_line(owner, self.layers))
                def _():
                    self.copy(k, self.block(k, owner), direction, distance).wait_send()

    def finish(self, before):
        self.store(before).wait()
        for k in range(len(self.grads)):
            self.over(k).wait()


class Spread:
    slots = range(11)

    def __init__(self, buf, seg, send, recv):
        self.buf, self.seg, self.send, self.recv = buf, seg, send, recv

    def index(self, n):
        _, shard, inner, core = place()
        row, flip, other = (n // 2) % 2, n // 4, n % 2
        return 2 * (lax.rem(shard + 2 * row, 4) + other * (1 - 2 * core)) + inner + flip * (1 - 2 * inner)

    def copy(self, slot):
        across, beside, twin = partners()
        low, high, whole = (0, SPREAD_SPLIT), (SPREAD_SPLIT, self.seg - SPREAD_SPLIT), (0, self.seg)
        n, (first, size), device = {
            0: (0, low, across),
            9: (0, high, across),
            1: (0, high, beside),
            10: (0, low, beside),
            2: (0, whole, twin),
            3: (4, low, beside),
            4: (4, whole, twin),
            5: (2, high, across),
            6: (2, whole, twin),
            7: (6, low, twin),
            8: (6, high, twin),
        }[slot]
        ref = self.buf.at[aligned(self.index(n) * self.seg + first, size)]
        return remote(ref, ref, self.send.at[slot], self.recv.at[slot], device)

    def push(self, *slots):
        for slot in slots:
            self.copy(slot).start()

    def came(self, *slots):
        for slot in slots:
            self.copy(slot).wait_recv()

    def start(self):
        self.push(0, 1, 9, 10, 2)

    def first(self):
        self.came(1)
        self.push(5)
        self.came(0)
        self.push(3)

    def near(self):
        self.came(10)
        self.push(6)
        self.came(9)
        self.push(4)

    def far(self):
        self.came(3)
        self.push(7)
        self.came(5)
        self.push(8)

    def sent(self):
        for slot in self.slots:
            self.copy(slot).wait_send()

    def end(self):
        self.came(2, 4, 6, 7, 8)
        self.sent()

    def before(self, n):
        return {
            1: (lambda: self.came(2),),
            2: (self.first, self.near),
            3: (lambda: self.came(6),),
            5: (lambda: self.came(4),),
            6: (self.far,),
            7: (lambda: self.came(7, 8),),
        }.get(n, ())


class Collect:
    def __init__(self, part, seg, total, pair, near, joined, send, recv):
        self.part, self.seg, self.total = part, seg, total
        self.pair, self.near, self.joined, self.send, self.recv = pair, near, joined, send, recv
        _, self.shard, self.inner, core = place()
        self.twin_shard = self.shard + 1 - 2 * core
        self.low, self.high, self.whole = (0, COLLECT_SPLIT), (COLLECT_SPLIT, seg - COLLECT_SPLIT), (0, seg)
        self.cols = pl.ds(0, D)

    def index(self, s, k):
        row, flip = 1 - k % 2, 1 - k // 2
        return 2 * lax.rem(s + 2 * row, 4) + self.inner + flip * (1 - 2 * self.inner)

    def pair_copy(self, k):
        src = self.part.at[aligned(self.index(self.twin_shard, k) * self.seg, self.seg), self.cols]
        return remote(src, self.pair.at[k], self.send.at[k], self.recv.at[k], partners()[2])

    def copy(self, slot):
        across, beside, _ = partners()
        src, dst, (first, size), device = {
            4: (self.pair.at[0], self.joined, self.low, across),
            5: (self.pair.at[0], self.joined, self.high, beside),
            6: (self.pair.at[1], self.near.at[0], self.low, across),
            7: (self.pair.at[2], self.near.at[1], self.high, beside),
            8: (self.pair.at[2], self.near.at[1], self.low, beside),
            9: (self.pair.at[1], self.near.at[0], self.high, across),
        }[slot]
        rows = pl.ds(first, size)
        return remote(src.at[rows], dst.at[rows], self.send.at[slot], self.recv.at[slot], device)

    def over(self, span, body):
        def step(n, _):
            body(aligned(span[0] + n * 16, 16))
            return 0

        lax.fori_loop(0, span[1] // 16, step, 0)

    def mine(self, k, rows):
        return self.part[aligned(self.index(self.shard, k) * self.seg + rows.start, 16), self.cols].astype(F32)

    def add_pair(self, k):
        def add(rows):
            self.pair[k, rows] = (self.mine(k, rows) + self.pair[k, rows].astype(F32)).astype(BF16)

        self.pair_copy(k).wait_recv()
        self.over(self.whole, add)
        for slot in ((4, 5), (6,), (7,))[k]:
            self.copy(slot).start()

    def add_own(self):
        def add(rows):
            self.total[rows] = self.mine(3, rows) + self.pair[3, rows].astype(F32)

        self.pair_copy(3).wait_recv()
        self.over(self.whole, add)

    def pass_on(self):
        for slot, k, span, after in ((4, 2, self.low, 8), (5, 1, self.high, 9)):

            def add(rows):
                self.pair[k, rows] = (self.pair[k, rows].astype(F32) + self.joined[rows].astype(F32)).astype(BF16)

            self.copy(slot).wait_recv()
            self.over(span, add)
            self.copy(after).start()

    def push(self):
        for k in range(4):
            self.pair_copy(k).start()

    def make(self, n, produce):
        k, own = n // 2, n % 2
        produce(self.index(jnp.where(own == 1, self.shard, self.twin_shard), k))

        @pl.when(own == 0)
        def _():
            self.pair_copy(k).start()

        for m in range(3):

            @pl.when(n == 2 * m + 1)
            def _():
                self.add_pair(m)
                if m == 2:
                    self.pass_on()

        pl.when(n == 7)(self.add_own)

    def end(self):
        def add(rows):
            near = self.near[0, rows].astype(F32) + self.near[1, rows].astype(F32)
            self.total[rows] = self.total[rows] + near

        for slots, span in (((6, 8), self.low), ((7, 9), self.high)):
            for slot in slots:
                self.copy(slot).wait_recv()
            self.over(span, add)
        for k in range(4):
            self.pair_copy(k).wait_send()
        for slot in range(4, 10):
            self.copy(slot).wait_send()


def norm_scale(values):
    return lax.rsqrt(jnp.mean(values * values, axis=-1, keepdims=True) + NORM_EPSILON)


def by_rows(rows, body, carry=0):
    def step(n, carry):
        return body(aligned(n * ROWS, ROWS), carry)

    return lax.fori_loop(0, rows // ROWS, step, carry)


def norm_back(values, gain, upstream):
    scale = norm_scale(values)
    scaled = gain * upstream
    inner = jnp.mean(scaled * values, axis=-1, keepdims=True)
    return (
        scale * scaled - values * scale * scale * scale * inner,
        jnp.sum(upstream * values * scale, axis=0, keepdims=True),
    )


REFS = (
    "tok", "cot", "gains", "weights",
    "block_out", "input_grad", "gain_sums", "mine", "theirs", "n1_held", "slot0", "slot1", "slot2", "slot3",
    "w0", "w1", "w2", "w3", "seq_a", "seq_b", "du", "act", "c_all", "gated", "mixed", "resid", "dresid", "total",
    "pair", "near", "joined", "g1", "g2", "g3", "stage", "sum", "tail", "outgoing", "tap_sums", "gain_in", "gain_line",
    "held", "loaded", "send_x", "recv_x", "send_z", "recv_z", "send_s", "recv_s", "send_c", "recv_c", "credit",
    "halo_send", "halo_recv", "send_g", "recv_g", "fetched", "fetches", "stored", "send_o", "recv_o",
    "send_a", "recv_a", "send_l", "recv_l",
)


def column_pieces(half):
    pieces = [(m * QUARTER + half * HALF_Q, m * HALF_Q, HALF_Q, 0) for m in range(4)]
    for k, (start, units) in enumerate(zip(UNIT_STARTS, UNIT_CHUNKS), 1):
        real = min(units, HALF_F - start)
        for m in range(3):
            first = 4 * QUARTER + m * UNITS + half * HALF_F + start
            pieces.append((first, STARTS[k] + m * units, real, units - real))
    return pieces


def block_kernel(layers, rows, *all_refs):
    r = dict(zip(REFS, all_refs, strict=True))
    tok, cot, gains = r["tok"], r["cot"], r["gains"]
    seq_a, seq_b, du, act = r["seq_a"], r["seq_b"], r["du"], r["act"]
    c_all, gated, mixed, total = r["c_all"], r["gated"], r["mixed"], r["total"]
    weights = (r["w0"], r["w1"], r["w2"], r["w3"])
    seg = tok.shape[0]
    _, shard, inner, _ = place()
    outer, at = line()
    me = 2 * shard + inner
    my_rows = aligned(me * seg, seg)
    chunks = list(zip(range(1, 1 + len(UNIT_CHUNKS)), UNIT_STARTS, UNIT_CHUNKS))
    gather = Gather(
        layers, rows, r["g1"], weights, r["send_x"], r["recv_x"], r["send_z"], r["recv_z"]
    )
    reduce = Reduce(
        layers, rows, (r["w2"], r["g1"], r["g2"], r["g3"]), (r["slot0"], r["slot1"], r["slot2"], r["slot3"]),
        r["stage"], r["w1"], r["sum"], r["outgoing"], r["mine"], r["theirs"],
        (r["send_g"], r["recv_g"], r["fetched"], r["fetches"], r["stored"], r["send_o"], r["recv_o"]),
    )

    def spread(buf, n):
        return Spread(buf, seg, r["send_s"].at[n], r["recv_s"].at[n])

    def collect(part, n):
        return Collect(part, seg, total, r["pair"], r["near"], r["joined"], r["send_c"].at[n], r["recv_c"].at[n])

    one, up, two, three = spread(seq_a, 0), spread(seq_b, 1), spread(seq_a, 2), spread(seq_a, 3)
    branch, down, feed, inputs = collect(seq_a, 0), collect(seq_b, 1), collect(du, 2), collect(seq_a, 3)
    lanes = lax.broadcasted_iota(jnp.int32, (seg, WIDE), 1) < HALF_Q
    taps = pltpu.roll(gains[...], lax.rem(D - shard * QUARTER - inner * HALF_Q, D), 1)[2:5, :WIDE]
    kept = pl.ds(D, WIDE)
    sums, tap_sums = r["gain_sums"], r["tap_sums"]

    def block(t):
        return aligned(t * seg, seg)

    def mine(part):
        return pl.ds(pl.multiple_of(me * seg + part.start, 16), part.size)

    def first_norm():
        def rows(part, _):
            values = tok[part].astype(F32)
            seq_a[mine(part)] = (values * norm_scale(values) * gains[0:1, :]).astype(BF16)
            return 0

        by_rows(seg, rows)

    def up_start():
        seq_b[my_rows] = cot[...]
        up.start()

    def held():
        return pltpu.make_async_copy(seq_a, r["n1_held"], r["held"])

    def reload():
        return pltpu.make_async_copy(r["n1_held"], seq_b, r["held"])

    def project(s):
        for i in (0, 1):
            parts = dot(seq_a[block(2 * s + i)], weights[0][...])
            b = jnp.where(lanes, parts[:, :WIDE], 0.0)
            c = pltpu.roll(parts[:, 128 : 128 + 384], 384 - 64, 1)[:, :WIDE]
            x = parts[:, 384 : 384 + WIDE]
            c_all[s, pl.ds(i * seg, seg)] = jnp.where(lanes, c, 0.0)
            gated[s, pl.ds(8 + i * seg, seg)] = (b * x).astype(BF16).astype(F32)

    def ahead():
        return remote(
            gated.at[:, pl.ds(2 * seg, 8)], gated.at[:, pl.ds(0, 8)], r["halo_send"].at[0], r["halo_recv"].at[0], at(1)
        )

    def halo():
        pl.when(outer < layers - 1)(lambda: ahead().start())

        @pl.when(outer == 0)
        def _():
            gated[:, pl.ds(0, 8)] = jnp.zeros((GROUPS, 8, WIDE), F32)

    def convolved(s, i):
        return (
            taps[0:1, :] * gated[s, pl.ds(6 + i * seg, seg)]
            + taps[1:2, :] * gated[s, pl.ds(7 + i * seg, seg)]
            + taps[2:3, :] * gated[s, pl.ds(8 + i * seg, seg)]
        )

    def convolve(t):
        for i in (0, 1):

            @pl.when(t % 2 == i)
            def _():
                s = t // 2
                mixed[block(t)] = pltpu.roll(c_all[s, pl.ds(i * seg, seg)] * convolved(s, i), 64, 1).astype(BF16)

        seq_a[block(t)] = dot_rows(mixed[block(t)], weights[0][:, pl.ds(512, WIDE)]).astype(BF16)

    def branch_end():
        branch.end()
        allow(r["credit"].at[0])

    def second_norm():
        def rows(part, _):
            values = tok[part].astype(F32) + total[part]
            r["resid"][part] = values
            seq_a[mine(part)] = (values * norm_scale(values) * gains[1:2, :]).astype(BF16)
            return 0

        by_rows(seg, rows)
        pl.semaphore_wait(r["credit"].at[0], 3)

    def hidden(k, start, units, t):
        ref, here = weights[k], block(t)
        gate = dot(seq_a[here], ref[:, pl.ds(0, units)])
        upval = dot(seq_a[here], ref[:, pl.ds(units, units)])
        dact = dot(seq_b[here], ref[:, pl.ds(2 * units, units)])
        sigma = jax.nn.sigmoid(gate)
        silu = gate * sigma
        act[here, pl.ds(start, units)] = (silu * upval).astype(BF16)
        dgate = dact * upval * sigma * (1.0 + gate * (1.0 - sigma))
        du[here, pl.ds(2 * start, units)] = dgate.astype(BF16)
        du[here, pl.ds(2 * start + units, units)] = (dact * silu).astype(BF16)

    def slice_of(n):
        return jnp.where(outer < layers // 2, D // SLICE - 1 - n, n)

    def gate_up_grads(k, start, units, n):
        part = slice_of(n)
        left = seq_a[:, aligned(part * SLICE, SLICE, 128)]
        reduce.grads[k][aligned(part * SLICE, SLICE), pl.ds(0, 2 * units)] = dot_columns(
            left, du[:, pl.ds(2 * start, 2 * units)]
        ).astype(BF16)

    def down_grads(k, start, units, n):
        part = slice_of(n)
        left = seq_b[:, aligned(part * SLICE, SLICE, 128)]
        reduce.grads[k][aligned(part * SLICE, SLICE), pl.ds(2 * units, units)] = dot_columns(
            left, act[:, pl.ds(start, units)]
        ).astype(BF16)

    def grads(k, start, units, n):
        gate_up_grads(k, start, units, n)
        down_grads(k, start, units, n)
        reduce.direct(k, slice_of(n))

    def second(t):
        here = block(t)
        seq_b[here] = sum(
            dot_rows(du[here, pl.ds(2 * start, 2 * units)], weights[k][:, pl.ds(0, 2 * units)])
            for k, start, units in chunks
        ).astype(BF16)

    def down_end():
        down.end()
        reload().start()
        allow(r["credit"].at[1])

    def forward(t):
        here = block(t)
        du[here, pl.ds(0, D)] = sum(
            dot_rows(act[here, pl.ds(start, units)], weights[k][:, pl.ds(2 * units, units)])
            for k, start, units in chunks
        ).astype(BF16)

    def second_back():
        def rows(part, gain):
            dpart, dgain = norm_back(r["resid"][part], gains[1:2, :], total[part])
            dresid = cot[part].astype(F32) + dpart
            r["dresid"][part] = dresid
            seq_a[mine(part)] = dresid.astype(BF16)
            return gain + dgain

        sums[...] = jnp.zeros(sums.shape, F32)
        tap_sums[...] = jnp.zeros(tap_sums.shape, F32)
        sums[1:2, pl.ds(0, D)] = by_rows(seg, rows, jnp.zeros((1, D), F32))
        pl.semaphore_wait(r["credit"].at[1], 3)

    def mix_back(t):
        s, here = t // 2, block(t)
        dmixed = pltpu.roll(dot(seq_a[here], weights[0][:, pl.ds(512, WIDE)]), WIDE - 64, 1)
        dmixed = jnp.where(lanes, dmixed, 0.0)
        for i in (0, 1):

            @pl.when(t % 2 == i)
            def _():
                du[here, kept] = (dmixed * convolved(s, i)).astype(BF16)
                c_all[s, pl.ds(i * seg, seg)] = dmixed * c_all[s, pl.ds(i * seg, seg)]

    def after():
        return remote(
            c_all.at[:, pl.ds(0, 8)], c_all.at[:, pl.ds(2 * seg, 8)], r["halo_send"].at[1], r["halo_recv"].at[1], at(-1)
        )

    def halo_back():
        pl.when(outer > 0)(lambda: after().start())

        @pl.when(outer == layers - 1)
        def _():
            c_all[:, pl.ds(2 * seg, 8)] = jnp.zeros((GROUPS, 8, WIDE), F32)

    def conv_back(n):
        for i in (0, 1):
            pl.when(n // GROUPS == i)(functools.partial(conv_back_half, n % GROUPS, i))

    def conv_back_half(s, i):
        t = block(2 * s + i)
        dconv = c_all[s, pl.ds(i * seg, seg)]
        dgated = (
            taps[2:3, :] * dconv
            + taps[1:2, :] * c_all[s, pl.ds(1 + i * seg, seg)]
            + taps[0:1, :] * c_all[s, pl.ds(2 + i * seg, seg)]
        )
        parts = dot(seq_b[t], weights[0][:, pl.ds(0, 640)])
        db = dgated * parts[:, 384:640]
        dx = dgated * parts[:, :WIDE]
        dc = jnp.concatenate([du[t, kept].astype(F32), jnp.zeros((seg, 128), F32)], axis=1)
        dc = pltpu.roll(dc, 64, 1)
        act[t, pl.ds(0, 128)] = db[:, :128].astype(BF16)
        act[t, pl.ds(128, 128)] = (db[:, 128:] + dc[:, :128]).astype(BF16)
        act[t, pl.ds(256, 128)] = dc[:, 128:256].astype(BF16)
        act[t, pl.ds(384, WIDE)] = dx.astype(BF16)
        act[t, pl.ds(640, 128)] = jnp.zeros((seg, 128), BF16)
        for k in range(3):
            moved = gated[s, pl.ds(6 + k + i * seg, seg)]
            tap_sums[k : k + 1] = tap_sums[k : k + 1] + jnp.sum(dconv * moved, axis=0, keepdims=True)

    def conv_grads(n):
        part = slice_of(n)
        held_rows, cols = aligned(part * SLICE, SLICE), aligned(part * SLICE, SLICE, 128)
        ref = reduce.grads[0]
        of_parts = dot_columns(seq_b[:, cols], act[:, pl.ds(0, CONV_COLS)])
        ref[held_rows, pl.ds(0, 512)] = of_parts[:, :512].astype(BF16)
        of_mixed = dot_columns(seq_a[:, cols], mixed[...])
        ref[held_rows, pl.ds(512, WIDE)] = (of_parts[:, 512:] + of_mixed).astype(BF16)
        reduce.direct(0, part)

    def feed_end():
        feed.end()
        allow(r["credit"].at[2])
        r["block_out"][...] = (r["resid"][...] + total[...]).astype(BF16)

    def first(t):
        here = block(t)
        seq_a[here] = dot_rows(act[here, pl.ds(0, 640)], weights[0][:, pl.ds(0, 640)]).astype(BF16)

    def first_back():
        def rows(part, gain):
            dpart, dgain = norm_back(tok[part].astype(F32), gains[0:1, :], total[part])
            r["input_grad"][part] = (r["dresid"][part] + dpart).astype(BF16)
            return gain + dgain

        sums[0:1, pl.ds(0, D)] = by_rows(seg, rows, jnp.zeros((1, D), F32))
        sums[2:5, aligned(me * WIDE, WIDE, 128)] = tap_sums[0:3]

    def gains_across(n):
        return remote(sums, r["gain_in"].at[n], r["send_a"].at[n], r["recv_a"].at[n], partners()[n])

    def gains_add(n):
        gains_across(n).wait()
        sums[...] = sums[...] + r["gain_in"][n]

    def line_copy(sign, steps):
        slot = (0 if sign > 0 else 1, steps - 1)
        return remote(
            sums, r["gain_line"].at[slot], r["send_l"].at[slot], r["recv_l"].at[slot], at(sign * steps)
        )

    def gains_line():
        for steps in range(1, layers):
            for sign in (1, -1):
                pl.when(in_line(outer + sign * steps, layers))(line_copy(sign, steps).start)

    def gains_end():
        for steps in range(1, layers):
            for sign in (1, -1):
                pl.when(in_line(outer + sign * steps, layers))(line_copy(sign, steps).wait_send)
                pl.when(in_line(outer - sign * steps, layers))(line_copy(sign, steps).wait_recv)

        own_sums = sums[...]
        for origin in range(layers):
            for steps in range(1, layers):
                for sign in (1, -1):

                    @pl.when((outer - sign * steps == origin))
                    def _():
                        came = r["gain_line"][0 if sign > 0 else 1, steps - 1]
                        sums[...] = came if origin == 0 else sums[...] + came

            if origin > 0:

                @pl.when(outer == origin)
                def _():
                    sums[...] = sums[...] + own_sums

    def end():
        reduce.finish(0)
        for k in range(len(WIDTHS)):
            reduce.wait_sent(k)
        pl.when(outer < layers - 1)(lambda: ahead().wait_send())
        pl.when(outer > 0)(lambda: after().wait_send())

    windows = [
        (r["resid"], 0, D), (r["dresid"], D, D), (total, 2 * D, D), (r["resid"], 3 * D, D),
        (r["tail"], 4 * D, GROUP_COLS - 4 * D),
    ]

    def load(n):
        ref, first, width = windows[n]
        return pltpu.make_async_copy(
            r["weights"].at[:, pl.ds(first, width)], ref.at[pl.ds(0, rows)], r["loaded"].at[n]
        )

    def start():
        for n in (0, 1, 2, 4):
            load(n).start()
        greet(layers)

    def cut(k):
        def read(part, first, width):
            found = []
            for n, (ref, low, size) in enumerate(windows):
                start, stop = max(first, low), min(first + width, low + size)
                if start < stop and (n == 0) == (k == 0):
                    found.append(ref[part, start - low : stop - low])
            return found

        def band(n, _):
            part = aligned(n * 16, 16)
            halves = []
            for half in (0, 1):
                pieces = []
                for first, own, width, padding in column_pieces(half):
                    if STARTS[k] <= own < STARTS[k] + WIDTHS[k]:
                        pieces += read(part, first, width)
                        if padding:
                            pieces.append(jnp.zeros((16, padding), F32))
                halves.append(jnp.concatenate(pieces, axis=1))
            is_low = inner == 0
            seq = lax.axis_index("seq")
            own_rows = aligned(seq * rows + n * 16, 16)
            weights[k][own_rows, :] = jnp.where(is_low, halves[0], halves[1]).astype(BF16)
            gather.other_rows(k)[part, :] = jnp.where(is_low, halves[1], halves[0]).astype(BF16)
            return 0

        for n in (0,) if k == 0 else (1, 2, 3, 4) if k == CUT_FIRST else ():
            load(n).wait()
        lax.fori_loop(0, rows // 16, band, 0)
        if k == 0:
            load(3).start()

    def hold():
        held().start()

    def hold_end():
        held().wait()

    def halo_end():
        pl.when(outer > 0)(lambda: ahead().wait_recv())

    def reload_end():
        reload().wait()

    def halo_back_end():
        pl.when(outer < layers - 1)(lambda: after().wait_recv())

    def feed_credit():
        pl.semaphore_wait(r["credit"].at[2], 3)

    def from_spread(moved, body):
        def step(n):
            for m in range(8):
                if moved.before(m):

                    @pl.when(n == m)
                    def _():
                        for act in moved.before(m):
                            act()

            body(moved.index(n))

        return step

    def each(body, *cases):
        return [functools.partial(body, *(case if isinstance(case, tuple) else (case,))) for case in cases]

    every = range(len(WIDTHS))
    cuts = each(cut, *every)
    exchange, send_own, send_other = (
        each(body, *every) for body in (gather.exchange, gather.send_own, gather.send_other)
    )
    step = [each(gather.steps, (k, 1, 1), (k, 2, 2), (k, 3)) for k in every]
    join_far = each(reduce.join, *((k, layers - 2, 2) for k in every))
    join_near = each(reduce.join, *((k, 1, 1) for k in every))
    final = each(reduce.final, (0, 3), 1, (2, 1), (3, 2))
    feed_pair = each(feed.add_pair, 0, 1, 2)
    gain_send = [lambda n=n: gains_across(n).start() for n in range(3)]
    gain_add = each(gains_add, 0, 1, 2)
    d3_far = functools.partial(reduce.direct, 3, least=2)
    d3_near = functools.partial(reduce.direct, 3, most=1)
    blocks, parts = 2 * GROUPS, D // SLICE
    proj = Loop(GROUPS, project)
    mix = Loop(blocks, lambda n: branch.make(n, convolve))
    hid1 = Loop(blocks, from_spread(two, functools.partial(hidden, *chunks[0])))
    hid2, hid3 = (Loop(blocks, functools.partial(hidden, *chunk)) for chunk in chunks[1:])
    grad1, grad2 = (Loop(parts, functools.partial(grads, *chunk)) for chunk in chunks[:2])
    down3 = Loop(parts, functools.partial(down_grads, *chunks[2]))
    back2 = Loop(blocks, lambda n: down.make(n, second))
    gate3 = Loop(parts, functools.partial(gate_up_grads, *chunks[2]))
    ffn = Loop(blocks, forward)
    back_mix = Loop(blocks, from_spread(three, mix_back))
    back_conv = Loop(blocks, conv_back)
    grad0 = Loop(parts, conv_grads)
    back1 = Loop(blocks, lambda n: inputs.make(n, first))
    play(
        [
            start, cuts[0], exchange[0], up_start, send_own[0], cuts[3], first_norm, cuts[1], send_other[0],
            send_own[1], one.start, step[0][0], send_own[3], exchange[1], one.first, cuts[2], up.first, step[0][1],
            one.near, send_other[1], one.far, one.end, step[0][2], proj[0], hold, exchange[3], proj[1], proj[2],
            proj[3], halo, up.near, step[1][0], halo_end, hold_end, mix[0], up.far, mix[1], mix[2], mix[3], mix[4],
            mix[5], step[1][1], exchange[2], mix[6], mix[7], send_other[3], branch_end, second_norm, two.start,
            send_other[2], send_own[2], gather.crossed, step[1][2], up.end, hid1[0], hid1[1], hid1[2], hid1[3],
            hid1[4], step[2][0], hid1[5], hid1[6], hid1[7], two.sent, grad1[0], grad1[1], step[3][0], step[2][1],
            grad1[2], grad1[3], step[2][2], hid2[0], hid2[1], hid2[2], hid2[3], hid2[4], step[3][1], hid2[5],
            hid2[6], hid2[7], join_far[1], grad2[0], grad2[1], grad2[2], grad2[3], step[3][2], hid3[0], hid3[1],
            hid3[2], hid3[3], hid3[4], hid3[5], hid3[6], hid3[7], down3[0], down3[1], down3[2], down3[3], back2[0],
            back2[1], back2[2], join_near[1], back2[3], back2[4], back2[5], back2[6], gather.finish, back2[7],
            gate3[0], gate3[1], gate3[2], gate3[3], ffn[0], ffn[1], ffn[2], ffn[3], ffn[4], ffn[5], ffn[6], ffn[7],
            d3_far, down_end, second_back, feed.push, three.start, back_mix[0], back_mix[1], join_far[2],
            back_mix[2], back_mix[3], feed_pair[0], feed_pair[1], feed_pair[2], back_mix[4], back_mix[5], final[1],
            back_mix[6], reload_end, back_mix[7], three.sent, halo_back, back_conv[0], join_near[2], back_conv[1],
            back_conv[2], back_conv[3], feed.pass_on, feed.add_own, halo_back_end, back_conv[4], back_conv[5],
            back_conv[6], back_conv[7], grad0[0], d3_near, join_far[3], grad0[1], grad0[2], grad0[3], feed_end,
            feed_credit, back1[0], back1[1], join_far[0], back1[2], join_near[3], back1[3], back1[4], back1[5],
            back1[6], final[2], join_near[0], back1[7], inputs.end, first_back, gain_send[0], final[3], gain_add[0],
            gain_send[1], gain_add[1], gain_send[2], gain_add[2], gains_line, final[0], gains_end, end,
        ]
    )


class Loop:
    def __init__(self, count, body):
        self.count, self.body = count, body

    def __getitem__(self, n):
        return (self, n)


def play(order):
    order = list(order)
    while order:
        entry = order.pop(0)
        if not isinstance(entry, tuple):
            entry()
            continue
        loop, _ = entry
        between = {}
        for n in range(1, loop.count):
            between[n] = []
            while order[0] != (loop, n):
                between[n].append(order.pop(0))
            order.pop(0)

        def turn(n, _):
            for m, acts in between.items():
                if acts:

                    @pl.when(n == m)
                    def _():
                        play(acts)

            loop.body(n)
            return 0

        lax.fori_loop(0, loop.count, turn, 0)


def block_step(tok, cot, gains, weights, layers):
    rows, seg = weights.shape[0], tok.shape[0]
    count = len(WIDTHS)
    tokens = 2 * GROUPS * seg
    vmem, anywhere = pl.BlockSpec(memory_space=pltpu.VMEM), pl.BlockSpec(memory_space=pl.ANY)
    shape, scratch = jax.ShapeDtypeStruct, pltpu.VMEM
    dma, regular = pltpu.SemaphoreType.DMA, pltpu.SemaphoreType.REGULAR
    hops = layers - 1
    wide, biggest = sum(WIDTHS), max(WIDTHS)
    out_shape = [
        shape((seg, D), BF16),
        shape((seg, D), BF16),
        shape((8, 2 * GROUPS * WIDE), F32),
        shape((rows, wide), F32),
        shape((rows, wide), BF16),
        shape((tokens, D), BF16),
    ] + [shape((2, hops, 2 * rows, width), BF16) for width in WIDTHS]
    scratch_shapes = (
        [scratch((D, width), BF16) for width in WIDTHS]
        + [
            scratch((tokens, D), BF16),
            scratch((tokens, D), BF16),
            scratch((tokens, 2 * PAD_F), BF16),
            scratch((tokens, PAD_F), BF16),
            scratch((GROUPS, 8 + 2 * seg, WIDE), F32),
            scratch((GROUPS, 8 + 2 * seg, WIDE), F32),
            scratch((tokens, WIDE), BF16),
            scratch((seg, D), F32),
            scratch((seg, D), F32),
            scratch((seg, D), F32),
            scratch((4, seg, D), BF16),
            scratch((2, seg, D), BF16),
            scratch((seg, D), BF16),
        ]
        + [scratch((D, width), BF16) for width in WIDTHS[1:]]
        + [
            scratch((2 * rows, biggest), BF16),
            scratch((rows, biggest), F32),
            scratch((rows, GROUP_COLS - 4 * D), F32),
            scratch((rows, wide), BF16),
            scratch((8, WIDE), F32),
            scratch((3, 8, 2 * GROUPS * WIDE), F32),
            scratch((2, hops, 8, 2 * GROUPS * WIDE), F32),
            dma,
            dma((5,)),
            dma((count,)),
            dma((count,)),
            dma((count, 2, hops, 2)),
            dma((count, 2, hops, 2)),
            dma((4, 11)),
            dma((4, 11)),
            dma((4, 10)),
            dma((4, 10)),
            regular((3,)),
            dma((2,)),
            dma((2,)),
            dma((count, 2, hops)),
            dma((count, 2, hops)),
            dma,
            dma((4,)),
            dma((count,)),
            dma((count,)),
            dma((count,)),
            dma((3,)),
            dma((3,)),
            dma((2, hops)),
            dma((2, hops)),
        ]
    )
    return pl.pallas_call(
        functools.partial(block_kernel, layers, rows),
        out_shape=out_shape,
        in_specs=[vmem] * 3 + [anywhere],
        out_specs=[vmem] * 3 + [anywhere] * (3 + count),
        scratch_shapes=scratch_shapes,
        compiler_params=pltpu.CompilerParams(
            collective_id=0, has_side_effects=True, vmem_limit_bytes=VMEM_BYTES
        ),
        name="block_step",
    )(tok, cot, gains, weights)[:5]


def band(rows, most):
    return max(size for size in range(16, most + 1, 16) if rows % size == 0)


def adam_update(param, grad, first, second, rate, decay):
    first_new = MOMENT_DECAY * first + (1.0 - MOMENT_DECAY) * grad
    second_new = SQUARE_DECAY * second + (1.0 - SQUARE_DECAY) * grad * grad
    root = jnp.sqrt(second_new * (1.0 / (1.0 - SQUARE_DECAY**STEP))) + ADAM_EPSILON
    step = first_new * (rate / (1.0 - MOMENT_DECAY**STEP)) / root
    return (first_new, second_new, param * (1.0 - rate * decay) - step)


def update_kernel(
    inner_ref, mine_ref, theirs_ref, weights_ref, first_ref, second_ref, sums_ref, gains_ref, gains_first_ref,
    gains_second_ref, block_ref, input_ref, grad_out, first_out, second_out, weights_out, gains_grad_out,
    gains_first_out, gains_second_out, gains_out, block_out, input_out,
):
    is_low = inner_ref[0] == 0
    mine, theirs = mine_ref[...], theirs_ref[...].astype(F32)
    for half in (0, 1):
        chosen = jnp.where(is_low, mine, theirs) if half == 0 else jnp.where(is_low, theirs, mine)
        for first, own, width, _ in column_pieces(half):
            grad_out[:, first : first + width] = chosen[:, own : own + width]
    first_out[...], second_out[...], weights_out[...] = adam_update(
        weights_ref[...], grad_out[...], first_ref[...], second_ref[...], WEIGHT_RATE, WEIGHT_DECAY
    )

    @pl.when(pl.program_id(0) == 0)
    def _():
        gains_grad_out[0:2] = sums_ref[0:2, :D]
        for n in range(2 * GROUPS):
            gains_grad_out[2:5, n * HALF_Q : (n + 1) * HALF_Q] = sums_ref[2:5, n * WIDE : n * WIDE + HALF_Q]
        gains_first_out[...], gains_second_out[...], gains_out[...] = adam_update(
            gains_ref[...], gains_grad_out[...], gains_first_ref[...], gains_second_ref[...], GAIN_RATE, 0.0
        )
        block_out[...] = block_ref[...]
        input_out[...] = input_ref[...]


def update(inner, mine, theirs, weights, first, second, sums, gains, gains_first, gains_second, block, grad):
    rows, cols = weights.shape
    wide = mine.shape[1]
    size = band(rows, 32)
    by_row = lambda width: pl.BlockSpec((size, width), lambda n: (n, 0))
    whole = lambda values: pl.BlockSpec(values.shape, lambda n: (0, 0))
    shape = jax.ShapeDtypeStruct
    return pl.pallas_call(
        update_kernel,
        grid=(rows // size,),
        out_shape=[shape((rows, cols), F32)] * 4 + [shape(gains.shape, F32)] * 4 + [shape(block.shape, BF16)] * 2,
        in_specs=[pl.BlockSpec(memory_space=pltpu.SMEM)]
        + [by_row(wide)] * 2
        + [by_row(cols)] * 3
        + [whole(sums)]
        + [whole(gains)] * 3
        + [whole(block)] * 2,
        out_specs=[by_row(cols)] * 4 + [whole(gains)] * 4 + [whole(block)] * 2,
        compiler_params=pltpu.CompilerParams(vmem_limit_bytes=VMEM_BYTES),
        name="update",
    )(inner, mine, theirs, weights, first, second, sums, gains, gains_first, gains_second, block, grad)


def on_device(
    tokens, gains_taps, weights, cotangent, weight_first, weight_second, gains_first, gains_second
):
    layers = lax.axis_size("seq") // 2
    inner_word = (lax.axis_index("seq") % 2).astype(jnp.int32).reshape(1)
    block_out, input_grad, gain_sums, mine, theirs = block_step(
        tokens[0], cotangent[0], gains_taps, weights, layers
    )
    (
        weight_grad, weight_first_new, weight_second_new, weight_new,
        gains_grad, gains_first_new, gains_second_new, gains_new, block_out, input_grad,
    ) = update(
        inner_word, mine, theirs, weights, weight_first, weight_second,
        gain_sums, gains_taps, gains_first, gains_second, block_out, input_grad,
    )
    return (
        block_out[None],
        input_grad[None],
        weight_grad,
        weight_first_new,
        weight_second_new,
        weight_new,
        gains_grad,
        gains_first_new,
        gains_second_new,
        gains_new,
    )


def solution(mesh):
    tokens, rows, whole = P("shard", "seq", None), P("seq", "shard"), P()
    return jax.shard_map(
        on_device,
        mesh=mesh,
        in_specs=(tokens, whole, rows, tokens, rows, rows, whole, whole),
        out_specs=(tokens, tokens, rows, rows, rows, rows, whole, whole, whole, whole),
        check_vma=False,
    )
```

```python
import functools

import jax
import jax.numpy as jnp
from jax import lax
from jax.experimental import pallas as pl
from jax.experimental.pallas import tpu as pltpu
from jax.sharding import PartitionSpec as P

D = 1536
FF = 6912
STEP = 10
GROUPS = 4
QUARTER = D // GROUPS
UNITS = FF // GROUPS
GROUP_COLS = 4 * QUARTER + 3 * UNITS
HALF_Q = QUARTER // 2
HALF_F = UNITS // 2
LANES = 128
PAD_F = -(-HALF_F // LANES) * LANES
WIDE = 256
CONV_COLS = 4 * HALF_Q
UNIT_CHUNKS = (384, 256, PAD_F - 640)
UNIT_STARTS = (0, 384, 640)
WIDTHS = (CONV_COLS,) + tuple(3 * units for units in UNIT_CHUNKS)
STARTS = tuple(sum(WIDTHS[:k]) for k in range(len(WIDTHS)))
SPREAD_SPLITS = (208, 208, 64, 128)
COLLECT_SPLITS = (128, 128, 112, 112)
REACH = (1, 1, 1, 1)
CUT_FIRST = 1
SLICE = 384
TILE = 16
ROWS = 48

MOMENT_DECAY = 0.9
SQUARE_DECAY = 0.95
ADAM_EPSILON = 1e-08
NORM_EPSILON = 1e-05
WEIGHT_RATE = 0.02
GAIN_RATE = 0.2
WEIGHT_DECAY = 0.1

BF16 = jnp.bfloat16
F32 = jnp.float32
MESH = pl.DeviceIdType.MESH
VMEM_BYTES = 63 * 1024 * 1024


def place():
    seq, shard = lax.axis_index("seq"), lax.axis_index("shard")
    inner, core = lax.rem(seq, 2), lax.rem(shard, 2)
    return seq, shard, inner, core


def partners():
    seq, shard, inner, core = place()
    across = {"seq": seq + 1 - 2 * inner, "shard": shard}
    beside = {"seq": seq, "shard": lax.rem(shard + 2, 4)}
    twin = {"seq": seq, "shard": shard + 1 - 2 * core}
    return across, beside, twin


def remote(src, dst, send, recv, device):
    return pltpu.make_async_remote_copy(
        src_ref=src, dst_ref=dst, send_sem=send, recv_sem=recv, device_id=device, device_id_type=MESH
    )


def line():
    seq, shard, _, _ = place()
    size = lax.axis_size("seq")
    return seq // 2, lambda steps: {"seq": lax.rem(seq + 2 * steps + size, size), "shard": shard}


def greet(layers):
    outer, at = line()
    barrier = pltpu.get_barrier_semaphore()
    for device in partners():
        pl.semaphore_signal(barrier, inc=1, device_id=device, device_id_type=MESH)
    for steps in range(1, layers):
        for sign in (1, -1):

            @pl.when(in_line(outer + sign * steps, layers))
            def _():
                pl.semaphore_signal(barrier, inc=1, device_id=at(sign * steps), device_id_type=MESH)


def greeted(layers):
    pl.semaphore_wait(pltpu.get_barrier_semaphore(), 3 + layers - 1)


def in_line(index, layers):
    return (index >= 0) & (index < layers)


def allow(credit):
    for device in partners():
        pl.semaphore_signal(credit, inc=1, device_id=device, device_id_type=MESH)


def dot(left, right):
    return jnp.dot(left, right, preferred_element_type=F32)


def dot_rows(left, right):
    return lax.dot_general(left, right, (((1,), (1,)), ((), ())), preferred_element_type=F32)


def dot_columns(left, right):
    return lax.dot_general(left, right, (((0,), (0,)), ((), ())), preferred_element_type=F32)


def aligned(start, size, multiple=16):
    return pl.ds(pl.multiple_of(start, multiple), size)


class Gather:
    def __init__(self, layers, rows, oth, outs, send_x, recv_x, send_z, recv_z):
        self.layers, self.rows, self.oth, self.outs = layers, rows, oth, outs
        self.send_x, self.recv_x, self.send_z, self.recv_z = send_x, recv_x, send_z, recv_z
        self.seq, _, self.inner, _ = place()
        self.outer, self.at = line()
        self.across = partners()[0]

    def seq_rows(self, index):
        return aligned(index * self.rows, self.rows)

    def layer_rows(self, direction, distance):
        origin = self.outer - distance if direction == 0 else self.outer + distance
        return aligned(origin * 2 * self.rows, 2 * self.rows)

    def copy(self, k, src, dst, direction, distance, hop, piece):
        slot = (k, direction, distance + hop - 1, piece)
        return remote(
            src, dst, self.send_z.at[slot], self.recv_z.at[slot], self.at(hop if direction == 0 else -hop)
        )

    def goes(self, direction, hop):
        return in_line(self.outer + (hop if direction == 0 else -hop), self.layers)

    def has_come(self, direction, distance):
        return in_line(self.outer + (-distance if direction == 0 else distance), self.layers)

    def hops(self, k, distance):
        return range(1, min(REACH[k], self.layers - 1 - distance) + 1)

    def own_copy(self, k, direction, hop):
        here = self.outs[k].at[self.seq_rows(self.seq)]
        return self.copy(k, here, here, direction, 0, hop, 0)

    def other_copy(self, k, direction, hop):
        there = self.outs[k].at[self.seq_rows(self.seq + 1 - 2 * self.inner)]
        return self.copy(k, there, there, direction, 0, hop, 1)

    def pass_copy(self, k, direction, distance, hop):
        ref = self.outs[k].at[self.layer_rows(direction, distance)]
        return self.copy(k, ref, ref, direction, distance, hop, 0)

    def other_rows(self, k):
        return self.oth.at[pl.ds(k * self.rows, self.rows), pl.ds(0, WIDTHS[k])]

    def exchange(self, k):
        self.x_copy(k).start()

    def x_copy(self, k):
        here = self.outs[k].at[self.seq_rows(self.seq)]
        return remote(self.other_rows(k), here, self.send_x.at[k], self.recv_x.at[k], self.across)

    def crossed(self):
        for k in range(len(self.outs)):
            self.x_copy(k).wait_send()

    def send_own(self, k):
        for hop in self.hops(k, 0):
            for direction in (0, 1):

                @pl.when(self.goes(direction, hop))
                def _():
                    self.own_copy(k, direction, hop).start()

    def send_other(self, k):
        self.x_copy(k).wait_recv()
        for hop in self.hops(k, 0):
            for direction in (0, 1):

                @pl.when(self.goes(direction, hop))
                def _():
                    self.other_copy(k, direction, hop).start()

    def step(self, k, distance):
        for direction in (0, 1):

            @pl.when(self.has_come(direction, distance))
            def _():
                if distance <= REACH[k]:
                    origin = self.outer - distance if direction == 0 else self.outer + distance
                    for piece in (0, 1):
                        index = 2 * origin + (self.inner if piece == 0 else 1 - self.inner)
                        ref = self.outs[k].at[self.seq_rows(index)]
                        self.copy(k, ref, ref, direction, distance - 1, 1, piece).wait_recv()
                else:
                    ref = self.outs[k].at[self.layer_rows(direction, distance)]
                    self.copy(k, ref, ref, direction, distance - 1, 1, 0).wait_recv()
                if distance % REACH[k] == 0:
                    for hop in self.hops(k, distance):

                        @pl.when(self.goes(direction, hop))
                        def _():
                            self.pass_copy(k, direction, distance, hop).start()

    def steps(self, k, first, last=None):
        last = self.layers - 1 if last is None else min(last, self.layers - 1)
        for distance in range(first, last + 1):
            self.step(k, distance)

    def finish(self):
        for k in range(len(self.outs)):
            for distance in range(0, self.layers - 1, REACH[k]):
                for hop in self.hops(k, distance):
                    for direction in (0, 1):

                        @pl.when(self.goes(direction, hop) & self.has_come(direction, distance))
                        def _():
                            if distance == 0:
                                self.own_copy(k, direction, hop).wait_send()
                                self.other_copy(k, direction, hop).wait_send()
                            else:
                                self.pass_copy(k, direction, distance, hop).wait_send()


class Reduce:
    def __init__(self, layers, rows, grads, slots, stage, spare, total, outgoing, mine, theirs, sems):
        self.layers, self.rows, self.grads, self.slots = layers, rows, grads, slots
        self.stage, self.spare, self.total, self.outgoing = stage, spare, total, outgoing
        self.mine, self.theirs = mine, theirs
        self.send_g, self.recv_g, self.fetched, self.fetches, self.stored, self.send_o, self.recv_o = sems
        _, _, self.inner, _ = place()
        self.outer, self.at = line()
        self.across = partners()[0]

    def owner(self, direction, distance):
        return self.outer + distance if direction == 0 else self.outer - distance

    def upstream(self, direction, steps):
        return in_line(self.outer - steps if direction == 0 else self.outer + steps, self.layers)

    def block(self, k, owner):
        return self.grads[k].at[aligned(owner * 2 * self.rows, 2 * self.rows), pl.ds(0, WIDTHS[k])]

    def copy(self, k, src, direction, distance):
        slot = (direction, distance - 1)
        return remote(
            src,
            self.slots[k].at[slot],
            self.send_g.at[(k,) + slot],
            self.recv_g.at[(k,) + slot],
            self.at(1 if direction == 0 else -1),
        )

    def send(self, k, direction, distance):
        self.copy(k, self.block(k, self.owner(direction, distance)), direction, distance).start()

    def direct(self, k, part=None, least=1, most=None):
        for distance in range(most or self.layers - 1, least - 1, -1):
            for direction in (0, 1):
                owner = self.owner(direction, distance)
                here = in_line(owner, self.layers) & jnp.logical_not(self.upstream(direction, 1))
                if part is not None:
                    here = here & (owner * 2 * self.rows // SLICE == part)

                @pl.when(here)
                def _():
                    self.send(k, direction, distance)

    def fetch(self, k, direction, distance):
        slot = self.slots[k].at[direction, distance - 1]
        self.copy(k, slot, direction, distance).wait_recv()
        held = self.stage.at[:, pl.ds(0, WIDTHS[k])]
        copy = pltpu.make_async_copy(slot, held, self.fetched)
        copy.start()
        copy.wait()

    def tiles(self, body):
        def step(n, _):
            body(aligned(n * TILE, TILE))
            return 0

        lax.fori_loop(0, 2 * self.rows // TILE, step, 0)

    def join(self, k, most, least):
        cols = pl.ds(0, WIDTHS[k])
        for distance in range(most, least - 1, -1):
            for direction in (0, 1):
                owner = self.owner(direction, distance)

                @pl.when(in_line(owner, self.layers) & self.upstream(direction, 1))
                def _():
                    def add(tile):
                        base = self.owner(direction, distance) * 2 * self.rows
                        rows = pl.ds(pl.multiple_of(base + tile.start, 16), TILE)
                        ref = self.grads[k]
                        ref[rows, cols] = (
                            ref[rows, cols].astype(F32) + self.stage[tile, cols].astype(F32)
                        ).astype(BF16)

                    self.fetch(k, direction, distance + 1)
                    self.tiles(add)
                    self.send(k, direction, distance)

    def final(self, k, before=None):
        cols = pl.ds(0, WIDTHS[k])
        came = [(1, 0), (1, 1)]

        def fetch(n, distance, direction):
            return pltpu.make_async_copy(
                self.slots[k].at[direction, distance - 1],
                self.spare.at[pl.ds(n * 2 * self.rows, 2 * self.rows), cols],
                self.fetches.at[n],
            )

        for n, (distance, direction) in enumerate(came):

            @pl.when(self.upstream(direction, distance))
            def _():
                self.copy(k, self.slots[k].at[direction, distance - 1], direction, distance).wait_recv()
                fetch(n, distance, direction).start()

        if before is not None:
            self.store(before).wait()

        here, there = self.inner * self.rows, (1 - self.inner) * self.rows

        def each(base, body):
            def step(n, _):
                body(base + n * TILE, n * TILE)
                return 0

            lax.fori_loop(0, self.rows // TILE, step, 0)

        for n, (distance, direction) in enumerate(came):

            @pl.when(self.upstream(direction, distance))
            def _():
                fetch(n, distance, direction).wait()

        def add_up(flags):
            def total(rows):
                value = self.grads[k][aligned(self.outer * 2 * self.rows + rows, TILE), cols].astype(F32)
                for n, flag in enumerate(flags):
                    if flag:
                        value = value + self.spare[aligned(n * 2 * self.rows + rows, TILE), cols].astype(F32)
                return value

            def send(rows, at):
                self.outgoing[aligned(at, TILE), pl.ds(STARTS[k], WIDTHS[k])] = total(rows).astype(BF16)

            def keep(rows, at):
                self.total[aligned(at, TILE), cols] = total(rows)

            each(there, send)
            self.over(k).start()
            each(here, keep)
            self.store(k).start()

        patterns = {}
        for place_in_line in range(self.layers):
            flags = tuple(
                0 <= (place_in_line - distance if direction == 0 else place_in_line + distance) < self.layers
                for distance, direction in came
            )
            patterns.setdefault(flags, []).append(place_in_line)
        for flags, places in patterns.items():
            here_now = functools.reduce(jnp.logical_or, [self.outer == p for p in places])

            @pl.when(here_now)
            def _():
                add_up(flags)

    def over(self, k):
        wide = pl.ds(STARTS[k], WIDTHS[k])
        return remote(
            self.outgoing.at[:, wide], self.theirs.at[:, wide], self.send_o.at[k], self.recv_o.at[k], self.across
        )

    def store(self, k):
        return pltpu.make_async_copy(
            self.total.at[:, pl.ds(0, WIDTHS[k])], self.mine.at[:, pl.ds(STARTS[k], WIDTHS[k])], self.stored.at[k]
        )

    def wait_sent(self, k):
        for distance in range(1, self.layers):
            for direction in (0, 1):
                owner = self.owner(direction, distance)

                @pl.when(in_line(owner, self.layers))
                def _():
                    self.copy(k, self.block(k, owner), direction, distance).wait_send()

    def finish(self, before):
        self.store(before).wait()
        for k in range(len(self.grads)):
            self.over(k).wait()


class Spread:
    slots = range(11)

    def __init__(self, buf, seg, split, send, recv):
        self.buf, self.seg, self.split, self.send, self.recv = buf, seg, split, send, recv

    def index(self, n):
        _, shard, inner, core = place()
        row, flip, other = (n // 2) % 2, n // 4, n % 2
        return 2 * (lax.rem(shard + 2 * row, 4) + other * (1 - 2 * core)) + inner + flip * (1 - 2 * inner)

    def copy(self, slot):
        across, beside, twin = partners()
        low, high, whole = (0, self.split), (self.split, self.seg - self.split), (0, self.seg)
        n, (first, size), device = {
            0: (0, low, across),
            9: (0, high, across),
            1: (0, high, beside),
            10: (0, low, beside),
            2: (0, whole, twin),
            3: (4, low, beside),
            4: (4, whole, twin),
            5: (2, high, across),
            6: (2, whole, twin),
            7: (6, low, twin),
            8: (6, high, twin),
        }[slot]
        ref = self.buf.at[aligned(self.index(n) * self.seg + first, size)]
        return remote(ref, ref, self.send.at[slot], self.recv.at[slot], device)

    def push(self, *slots):
        for slot in slots:
            self.copy(slot).start()

    def came(self, *slots):
        for slot in slots:
            self.copy(slot).wait_recv()

    def start(self):
        self.push(0, 1, 9, 10, 2)

    def first(self):
        self.came(1)
        self.push(5)
        self.came(0)
        self.push(3)

    def near(self):
        self.came(10)
        self.push(6)
        self.came(9)
        self.push(4)

    def far(self):
        self.came(3)
        self.push(7)
        self.came(5)
        self.push(8)

    def sent(self):
        for slot in self.slots:
            self.copy(slot).wait_send()

    def end(self):
        self.came(2, 4, 6, 7, 8)
        self.sent()

    def before(self, n):
        return {
            1: (lambda: self.came(2),),
            2: (self.first, self.near),
            3: (lambda: self.came(6),),
            5: (lambda: self.came(4),),
            6: (self.far,),
            7: (lambda: self.came(7, 8),),
        }.get(n, ())


class Collect:
    def __init__(self, part, seg, split, total, pair, near, joined, send, recv):
        self.part, self.seg, self.total = part, seg, total
        self.pair, self.near, self.joined, self.send, self.recv = pair, near, joined, send, recv
        _, self.shard, self.inner, core = place()
        self.twin_shard = self.shard + 1 - 2 * core
        self.low, self.high, self.whole = (0, split), (split, seg - split), (0, seg)
        self.cols = pl.ds(0, D)

    def index(self, s, k):
        row, flip = 1 - k % 2, 1 - k // 2
        return 2 * lax.rem(s + 2 * row, 4) + self.inner + flip * (1 - 2 * self.inner)

    def pair_copy(self, k):
        src = self.part.at[aligned(self.index(self.twin_shard, k) * self.seg, self.seg), self.cols]
        return remote(src, self.pair.at[k], self.send.at[k], self.recv.at[k], partners()[2])

    def copy(self, slot):
        across, beside, _ = partners()
        src, dst, (first, size), device = {
            4: (self.pair.at[0], self.joined, self.low, across),
            5: (self.pair.at[0], self.joined, self.high, beside),
            6: (self.pair.at[1], self.near.at[0], self.low, across),
            7: (self.pair.at[2], self.near.at[1], self.high, beside),
            8: (self.pair.at[2], self.near.at[1], self.low, beside),
            9: (self.pair.at[1], self.near.at[0], self.high, across),
        }[slot]
        rows = pl.ds(first, size)
        return remote(src.at[rows], dst.at[rows], self.send.at[slot], self.recv.at[slot], device)

    def over(self, span, body):
        def step(n, _):
            body(aligned(span[0] + n * 16, 16))
            return 0

        lax.fori_loop(0, span[1] // 16, step, 0)

    def mine(self, k, rows):
        return self.part[aligned(self.index(self.shard, k) * self.seg + rows.start, 16), self.cols].astype(F32)

    def add_pair(self, k):
        def add(rows):
            self.pair[k, rows] = (self.mine(k, rows) + self.pair[k, rows].astype(F32)).astype(BF16)

        self.pair_copy(k).wait_recv()
        self.over(self.whole, add)
        for slot in ((4, 5), (6,), (7,))[k]:
            self.copy(slot).start()

    def add_own(self):
        def add(rows):
            self.total[rows] = self.mine(3, rows) + self.pair[3, rows].astype(F32)

        self.pair_copy(3).wait_recv()
        self.over(self.whole, add)

    def pass_on(self):
        for slot, k, span, after in ((4, 2, self.low, 8), (5, 1, self.high, 9)):

            def add(rows):
                self.pair[k, rows] = (self.pair[k, rows].astype(F32) + self.joined[rows].astype(F32)).astype(BF16)

            self.copy(slot).wait_recv()
            self.over(span, add)
            self.copy(after).start()

    def push(self):
        for k in range(4):
            self.pair_copy(k).start()

    def make(self, n, produce):
        k, own = n // 2, n % 2
        produce(self.index(jnp.where(own == 1, self.shard, self.twin_shard), k))

        @pl.when(own == 0)
        def _():
            self.pair_copy(k).start()

        for m in range(3):

            @pl.when(n == 2 * m + 1)
            def _():
                self.add_pair(m)
                if m == 2:
                    self.pass_on()

        pl.when(n == 7)(self.add_own)

    def end(self):
        def add(rows):
            near = self.near[0, rows].astype(F32) + self.near[1, rows].astype(F32)
            self.total[rows] = self.total[rows] + near

        for slots, span in (((6, 8), self.low), ((7, 9), self.high)):
            for slot in slots:
                self.copy(slot).wait_recv()
            self.over(span, add)
        for k in range(4):
            self.pair_copy(k).wait_send()
        for slot in range(4, 10):
            self.copy(slot).wait_send()


def norm_scale(values):
    return lax.rsqrt(jnp.mean(values * values, axis=-1, keepdims=True) + NORM_EPSILON)


def by_rows(rows, body, carry=0):
    def step(n, carry):
        return body(aligned(n * ROWS, ROWS), carry)

    return lax.fori_loop(0, rows // ROWS, step, carry)


def norm_back(values, gain, upstream):
    scale = norm_scale(values)
    scaled = gain * upstream
    inner = jnp.mean(scaled * values, axis=-1, keepdims=True)
    return (
        scale * scaled - values * scale * scale * scale * inner,
        jnp.sum(upstream * values * scale, axis=0, keepdims=True),
    )


REFS = (
    "tok", "cot", "gains", "weights",
    "block_out", "input_grad", "gain_sums", "mine", "theirs", "n1_held", "slot0", "slot1", "slot2", "slot3",
    "w0", "w1", "w2", "w3", "seq_a", "seq_b", "du", "act", "c_all", "gated", "mixed", "resid", "dresid", "total",
    "pair", "near", "joined", "g1", "g2", "g3", "stage", "sum", "tail", "outgoing", "tap_sums", "gain_in", "gain_line",
    "held", "loaded", "send_x", "recv_x", "send_z", "recv_z", "send_s", "recv_s", "send_c", "recv_c", "credit",
    "halo_send", "halo_recv", "send_g", "recv_g", "fetched", "fetches", "stored", "send_o", "recv_o",
    "send_a", "recv_a", "send_l", "recv_l",
)


def column_pieces(half):
    pieces = [(m * QUARTER + half * HALF_Q, m * HALF_Q, HALF_Q, 0) for m in range(4)]
    for k, (start, units) in enumerate(zip(UNIT_STARTS, UNIT_CHUNKS), 1):
        real = min(units, HALF_F - start)
        for m in range(3):
            first = 4 * QUARTER + m * UNITS + half * HALF_F + start
            pieces.append((first, STARTS[k] + m * units, real, units - real))
    return pieces


def block_kernel(layers, rows, *all_refs):
    r = dict(zip(REFS, all_refs, strict=True))
    tok, cot, gains = r["tok"], r["cot"], r["gains"]
    seq_a, seq_b, du, act = r["seq_a"], r["seq_b"], r["du"], r["act"]
    c_all, gated, mixed, total = r["c_all"], r["gated"], r["mixed"], r["total"]
    weights = (r["w0"], r["w1"], r["w2"], r["w3"])
    seg = tok.shape[0]
    _, shard, inner, _ = place()
    outer, at = line()
    me = 2 * shard + inner
    my_rows = aligned(me * seg, seg)
    chunks = list(zip(range(1, 1 + len(UNIT_CHUNKS)), UNIT_STARTS, UNIT_CHUNKS))
    gather = Gather(
        layers, rows, r["g1"], weights, r["send_x"], r["recv_x"], r["send_z"], r["recv_z"]
    )
    reduce = Reduce(
        layers, rows, (r["w2"], r["g1"], r["g2"], r["g3"]), (r["slot0"], r["slot1"], r["slot2"], r["slot3"]),
        r["stage"], r["w1"], r["sum"], r["outgoing"], r["mine"], r["theirs"],
        (r["send_g"], r["recv_g"], r["fetched"], r["fetches"], r["stored"], r["send_o"], r["recv_o"]),
    )

    def spread(buf, n):
        return Spread(buf, seg, SPREAD_SPLITS[n], r["send_s"].at[n], r["recv_s"].at[n])

    def collect(part, n):
        sems = r["send_c"].at[n], r["recv_c"].at[n]
        return Collect(part, seg, COLLECT_SPLITS[n], total, r["pair"], r["near"], r["joined"], *sems)

    one, up, two, three = spread(seq_a, 0), spread(seq_b, 1), spread(seq_a, 2), spread(seq_a, 3)
    branch, down, feed, inputs = collect(seq_a, 0), collect(seq_b, 1), collect(du, 2), collect(seq_a, 3)
    lanes = lax.broadcasted_iota(jnp.int32, (seg, WIDE), 1) < HALF_Q
    taps = pltpu.roll(gains[...], lax.rem(D - shard * QUARTER - inner * HALF_Q, D), 1)[2:5, :WIDE]
    kept = pl.ds(D, WIDE)
    sums, tap_sums = r["gain_sums"], r["tap_sums"]

    def block(t):
        return aligned(t * seg, seg)

    def mine(part):
        return pl.ds(pl.multiple_of(me * seg + part.start, 16), part.size)

    def first_norm():
        def rows(part, _):
            values = tok[part].astype(F32)
            seq_a[mine(part)] = (values * norm_scale(values) * gains[0:1, :]).astype(BF16)
            return 0

        by_rows(seg, rows)

    def up_start():
        seq_b[my_rows] = cot[...]
        up.start()

    def held():
        return pltpu.make_async_copy(seq_a, r["n1_held"], r["held"])

    def reload():
        return pltpu.make_async_copy(r["n1_held"], seq_b, r["held"])

    def project(s):
        for i in (0, 1):
            parts = dot(seq_a[block(2 * s + i)], weights[0][...])
            b = jnp.where(lanes, parts[:, :WIDE], 0.0)
            c = pltpu.roll(parts[:, 128 : 128 + 384], 384 - 64, 1)[:, :WIDE]
            x = parts[:, 384 : 384 + WIDE]
            c_all[s, pl.ds(i * seg, seg)] = jnp.where(lanes, c, 0.0)
            gated[s, pl.ds(8 + i * seg, seg)] = (b * x).astype(BF16).astype(F32)

    def ahead():
        return remote(
            gated.at[:, pl.ds(2 * seg, 8)], gated.at[:, pl.ds(0, 8)], r["halo_send"].at[0], r["halo_recv"].at[0], at(1)
        )

    def halo():
        pl.when(outer < layers - 1)(lambda: ahead().start())

        @pl.when(outer == 0)
        def _():
            gated[:, pl.ds(0, 8)] = jnp.zeros((GROUPS, 8, WIDE), F32)

    def convolved(s, i):
        return (
            taps[0:1, :] * gated[s, pl.ds(6 + i * seg, seg)]
            + taps[1:2, :] * gated[s, pl.ds(7 + i * seg, seg)]
            + taps[2:3, :] * gated[s, pl.ds(8 + i * seg, seg)]
        )

    def convolve(t):
        for i in (0, 1):

            @pl.when(t % 2 == i)
            def _():
                s = t // 2
                mixed[block(t)] = pltpu.roll(c_all[s, pl.ds(i * seg, seg)] * convolved(s, i), 64, 1).astype(BF16)

        seq_a[block(t)] = dot_rows(mixed[block(t)], weights[0][:, pl.ds(512, WIDE)]).astype(BF16)

    def branch_end():
        branch.end()
        allow(r["credit"].at[0])

    def second_norm():
        def rows(part, _):
            values = tok[part].astype(F32) + total[part]
            r["resid"][part] = values
            seq_a[mine(part)] = (values * norm_scale(values) * gains[1:2, :]).astype(BF16)
            return 0

        by_rows(seg, rows)
        pl.semaphore_wait(r["credit"].at[0], 3)

    def hidden(k, start, units, t):
        ref, here = weights[k], block(t)
        gate = dot(seq_a[here], ref[:, pl.ds(0, units)])
        upval = dot(seq_a[here], ref[:, pl.ds(units, units)])
        dact = dot(seq_b[here], ref[:, pl.ds(2 * units, units)])
        sigma = jax.nn.sigmoid(gate)
        silu = gate * sigma
        act[here, pl.ds(start, units)] = (silu * upval).astype(BF16)
        dgate = dact * upval * sigma * (1.0 + gate * (1.0 - sigma))
        du[here, pl.ds(2 * start, units)] = dgate.astype(BF16)
        du[here, pl.ds(2 * start + units, units)] = (dact * silu).astype(BF16)

    def slice_of(n):
        return jnp.where(outer < layers // 2, D // SLICE - 1 - n, n)

    def gate_up_grads(k, start, units, n):
        part = slice_of(n)
        left = seq_a[:, aligned(part * SLICE, SLICE, 128)]
        reduce.grads[k][aligned(part * SLICE, SLICE), pl.ds(0, 2 * units)] = dot_columns(
            left, du[:, pl.ds(2 * start, 2 * units)]
        ).astype(BF16)

    def down_grads(k, start, units, n):
        part = slice_of(n)
        left = seq_b[:, aligned(part * SLICE, SLICE, 128)]
        reduce.grads[k][aligned(part * SLICE, SLICE), pl.ds(2 * units, units)] = dot_columns(
            left, act[:, pl.ds(start, units)]
        ).astype(BF16)

    def grads(k, start, units, n):
        gate_up_grads(k, start, units, n)
        down_grads(k, start, units, n)
        reduce.direct(k, slice_of(n))

    def second(t):
        here = block(t)
        seq_b[here] = sum(
            dot_rows(du[here, pl.ds(2 * start, 2 * units)], weights[k][:, pl.ds(0, 2 * units)])
            for k, start, units in chunks
        ).astype(BF16)

    def down_end():
        down.end()
        reload().start()
        allow(r["credit"].at[1])

    def forward(t):
        here = block(t)
        du[here, pl.ds(0, D)] = sum(
            dot_rows(act[here, pl.ds(start, units)], weights[k][:, pl.ds(2 * units, units)])
            for k, start, units in chunks
        ).astype(BF16)

    def second_back():
        def rows(part, gain):
            dpart, dgain = norm_back(r["resid"][part], gains[1:2, :], total[part])
            dresid = cot[part].astype(F32) + dpart
            r["dresid"][part] = dresid
            seq_a[mine(part)] = dresid.astype(BF16)
            return gain + dgain

        sums[...] = jnp.zeros(sums.shape, F32)
        tap_sums[...] = jnp.zeros(tap_sums.shape, F32)
        sums[1:2, pl.ds(0, D)] = by_rows(seg, rows, jnp.zeros((1, D), F32))
        pl.semaphore_wait(r["credit"].at[1], 3)

    def mix_back(t):
        s, here = t // 2, block(t)
        dmixed = pltpu.roll(dot(seq_a[here], weights[0][:, pl.ds(512, WIDE)]), WIDE - 64, 1)
        dmixed = jnp.where(lanes, dmixed, 0.0)
        for i in (0, 1):

            @pl.when(t % 2 == i)
            def _():
                du[here, kept] = (dmixed * convolved(s, i)).astype(BF16)
                c_all[s, pl.ds(i * seg, seg)] = dmixed * c_all[s, pl.ds(i * seg, seg)]

    def after():
        return remote(
            c_all.at[:, pl.ds(0, 8)], c_all.at[:, pl.ds(2 * seg, 8)], r["halo_send"].at[1], r["halo_recv"].at[1], at(-1)
        )

    def halo_back():
        pl.when(outer > 0)(lambda: after().start())

        @pl.when(outer == layers - 1)
        def _():
            c_all[:, pl.ds(2 * seg, 8)] = jnp.zeros((GROUPS, 8, WIDE), F32)

    def conv_back(n):
        for i in (0, 1):
            pl.when(n // GROUPS == i)(functools.partial(conv_back_half, n % GROUPS, i))

    def conv_back_half(s, i):
        t = block(2 * s + i)
        dconv = c_all[s, pl.ds(i * seg, seg)]
        dgated = (
            taps[2:3, :] * dconv
            + taps[1:2, :] * c_all[s, pl.ds(1 + i * seg, seg)]
            + taps[0:1, :] * c_all[s, pl.ds(2 + i * seg, seg)]
        )
        parts = dot(seq_b[t], weights[0][:, pl.ds(0, 640)])
        db = dgated * parts[:, 384:640]
        dx = dgated * parts[:, :WIDE]
        dc = jnp.concatenate([du[t, kept].astype(F32), jnp.zeros((seg, 128), F32)], axis=1)
        dc = pltpu.roll(dc, 64, 1)
        act[t, pl.ds(0, 128)] = db[:, :128].astype(BF16)
        act[t, pl.ds(128, 128)] = (db[:, 128:] + dc[:, :128]).astype(BF16)
        act[t, pl.ds(256, 128)] = dc[:, 128:256].astype(BF16)
        act[t, pl.ds(384, WIDE)] = dx.astype(BF16)
        act[t, pl.ds(640, 128)] = jnp.zeros((seg, 128), BF16)
        for k in range(3):
            moved = gated[s, pl.ds(6 + k + i * seg, seg)]
            tap_sums[k : k + 1] = tap_sums[k : k + 1] + jnp.sum(dconv * moved, axis=0, keepdims=True)

    def conv_grads(n):
        part = slice_of(n)
        held_rows, cols = aligned(part * SLICE, SLICE), aligned(part * SLICE, SLICE, 128)
        ref = reduce.grads[0]
        of_parts = dot_columns(seq_b[:, cols], act[:, pl.ds(0, CONV_COLS)])
        ref[held_rows, pl.ds(0, 512)] = of_parts[:, :512].astype(BF16)
        of_mixed = dot_columns(seq_a[:, cols], mixed[...])
        ref[held_rows, pl.ds(512, WIDE)] = (of_parts[:, 512:] + of_mixed).astype(BF16)
        reduce.direct(0, part)

    def feed_end():
        feed.end()
        allow(r["credit"].at[2])
        r["block_out"][...] = (r["resid"][...] + total[...]).astype(BF16)

    def first(t):
        here = block(t)
        seq_a[here] = dot_rows(act[here, pl.ds(0, 640)], weights[0][:, pl.ds(0, 640)]).astype(BF16)

    def first_back():
        def rows(part, gain):
            dpart, dgain = norm_back(tok[part].astype(F32), gains[0:1, :], total[part])
            r["input_grad"][part] = (r["dresid"][part] + dpart).astype(BF16)
            return gain + dgain

        sums[0:1, pl.ds(0, D)] = by_rows(seg, rows, jnp.zeros((1, D), F32))
        sums[2:5, aligned(me * WIDE, WIDE, 128)] = tap_sums[0:3]

    def gains_across(n):
        return remote(sums, r["gain_in"].at[n], r["send_a"].at[n], r["recv_a"].at[n], partners()[n])

    def gains_add(n):
        gains_across(n).wait()
        sums[...] = sums[...] + r["gain_in"][n]

    def line_copy(sign, steps):
        slot = (0 if sign > 0 else 1, steps - 1)
        return remote(
            sums, r["gain_line"].at[slot], r["send_l"].at[slot], r["recv_l"].at[slot], at(sign * steps)
        )

    def gains_line():
        for steps in range(1, layers):
            for sign in (1, -1):
                pl.when(in_line(outer + sign * steps, layers))(line_copy(sign, steps).start)

    def gains_end():
        for steps in range(1, layers):
            for sign in (1, -1):
                pl.when(in_line(outer + sign * steps, layers))(line_copy(sign, steps).wait_send)
                pl.when(in_line(outer - sign * steps, layers))(line_copy(sign, steps).wait_recv)

        own_sums = sums[...]
        for origin in range(layers):
            for steps in range(1, layers):
                for sign in (1, -1):

                    @pl.when((outer - sign * steps == origin))
                    def _():
                        came = r["gain_line"][0 if sign > 0 else 1, steps - 1]
                        sums[...] = came if origin == 0 else sums[...] + came

            if origin > 0:

                @pl.when(outer == origin)
                def _():
                    sums[...] = sums[...] + own_sums

    def end():
        reduce.finish(0)
        for k in range(len(WIDTHS)):
            reduce.wait_sent(k)
        pl.when(outer < layers - 1)(lambda: ahead().wait_send())
        pl.when(outer > 0)(lambda: after().wait_send())

    windows = [
        (r["resid"], 0, D), (r["dresid"], D, D), (total, 2 * D, D), (r["resid"], 3 * D, D),
        (r["tail"], 4 * D, GROUP_COLS - 4 * D),
    ]

    def load(n):
        ref, first, width = windows[n]
        return pltpu.make_async_copy(
            r["weights"].at[:, pl.ds(first, width)], ref.at[pl.ds(0, rows)], r["loaded"].at[n]
        )

    def start():
        for n in (0, 1, 2, 4):
            load(n).start()
        greet(layers)
        load(0).wait()
        cut(0)
        load(3).start()
        greeted(layers)

    def cut(k):
        def read(part, first, width):
            found = []
            for n, (ref, low, size) in enumerate(windows):
                start, stop = max(first, low), min(first + width, low + size)
                if start < stop and (n == 0) == (k == 0):
                    found.append(ref[part, start - low : stop - low])
            return found

        def band(n, _):
            part = aligned(n * 16, 16)
            halves = []
            for half in (0, 1):
                pieces = []
                for first, own, width, padding in column_pieces(half):
                    if STARTS[k] <= own < STARTS[k] + WIDTHS[k]:
                        pieces += read(part, first, width)
                        if padding:
                            pieces.append(jnp.zeros((16, padding), F32))
                halves.append(jnp.concatenate(pieces, axis=1))
            is_low = inner == 0
            seq = lax.axis_index("seq")
            own_rows = aligned(seq * rows + n * 16, 16)
            weights[k][own_rows, :] = jnp.where(is_low, halves[0], halves[1]).astype(BF16)
            gather.other_rows(k)[part, :] = jnp.where(is_low, halves[1], halves[0]).astype(BF16)
            return 0

        for n in (1, 2, 3, 4) if k == CUT_FIRST else ():
            load(n).wait()
        lax.fori_loop(0, rows // 16, band, 0)

    def hold():
        held().start()

    def hold_end():
        held().wait()

    def halo_end():
        pl.when(outer > 0)(lambda: ahead().wait_recv())

    def reload_end():
        reload().wait()

    def halo_back_end():
        pl.when(outer < layers - 1)(lambda: after().wait_recv())

    def feed_credit():
        pl.semaphore_wait(r["credit"].at[2], 3)

    def from_spread(moved, body):
        def step(n):
            for m in range(8):
                if moved.before(m):

                    @pl.when(n == m)
                    def _():
                        for act in moved.before(m):
                            act()

            body(moved.index(n))

        return step

    def each(body, *cases):
        return [functools.partial(body, *(case if isinstance(case, tuple) else (case,))) for case in cases]

    every = range(len(WIDTHS))
    cuts = each(cut, *every)
    exchange, send_own, send_other = (
        each(body, *every) for body in (gather.exchange, gather.send_own, gather.send_other)
    )
    step = [each(gather.steps, (k, 1, 1), (k, 2, 2), (k, 3)) for k in every]
    join_far = each(reduce.join, *((k, layers - 2, 2) for k in every))
    join_near = each(reduce.join, *((k, 1, 1) for k in every))
    final = each(reduce.final, (0, 3), 1, (2, 1), (3, 2))
    feed_pair = each(feed.add_pair, 0, 1, 2)
    gain_send = [lambda n=n: gains_across(n).start() for n in range(3)]
    gain_add = each(gains_add, 0, 1, 2)
    d3_far = functools.partial(reduce.direct, 3, least=2)
    d3_near = functools.partial(reduce.direct, 3, most=1)
    blocks, parts = 2 * GROUPS, D // SLICE
    proj = Loop(GROUPS, project)
    mix = Loop(blocks, lambda n: branch.make(n, convolve))
    hid1 = Loop(blocks, from_spread(two, functools.partial(hidden, *chunks[0])))
    hid2, hid3 = (Loop(blocks, functools.partial(hidden, *chunk)) for chunk in chunks[1:])
    grad1, grad2 = (Loop(parts, functools.partial(grads, *chunk)) for chunk in chunks[:2])
    down3 = Loop(parts, functools.partial(down_grads, *chunks[2]))
    back2 = Loop(blocks, lambda n: down.make(n, second))
    gate3 = Loop(parts, functools.partial(gate_up_grads, *chunks[2]))
    ffn = Loop(blocks, forward)
    back_mix = Loop(blocks, from_spread(three, mix_back))
    back_conv = Loop(blocks, conv_back)
    grad0 = Loop(parts, conv_grads)
    back1 = Loop(blocks, lambda n: inputs.make(n, first))
    play(
        [
            start, send_own[0], exchange[0], cuts[1], first_norm, one.start, exchange[1], send_other[0], step[0][0],
            cuts[3], one.first, cuts[2], step[0][1], up_start, send_own[1], one.near, one.far, step[0][2], one.end,
            hold, proj[0], proj[1], exchange[3], hold_end, proj[2], proj[3], up.first, halo, exchange[2],
            send_other[1], halo_end, mix[0], step[1][0], mix[1], up.near, mix[2], mix[3], mix[4], up.far, up.end,
            mix[5], send_other[2], step[1][1], mix[6], send_own[2], mix[7], branch_end, second_norm, two.start,
            step[1][2], send_own[3], hid1[0], hid1[1], hid1[2], hid1[3], send_other[3], step[2][0], hid1[4],
            hid1[5], hid1[6], hid1[7], two.sent, gather.crossed, grad1[0], grad1[1], step[2][1], grad1[2],
            step[2][2], grad1[3], hid2[0], hid2[1], hid2[2], hid2[3], step[3][0], hid2[4], hid2[5], hid2[6],
            hid2[7], join_far[1], grad2[0], grad2[1], grad2[2], grad2[3], step[3][1], step[3][2], hid3[0], hid3[1],
            hid3[2], hid3[3], hid3[4], hid3[5], hid3[6], hid3[7], down3[0], down3[1], down3[2], down3[3], back2[0],
            back2[1], back2[2], back2[3], back2[4], back2[5], back2[6], back2[7], gate3[0], join_near[1],
            join_far[2], gate3[1], gather.finish, gate3[2], gate3[3], down_end, second_back, three.start, ffn[0],
            ffn[1], ffn[2], ffn[3], ffn[4], ffn[5], ffn[6], ffn[7], back_mix[0], d3_far, back_mix[1], feed.push,
            join_near[2], back_mix[2], back_mix[3], reload_end, feed_pair[0], back_mix[4], feed_pair[1],
            back_mix[5], back_mix[6], feed_pair[2], back_mix[7], three.sent, halo_back, back_conv[0], back_conv[1],
            back_conv[2], d3_near, back_conv[3], feed.pass_on, join_far[3], feed.add_own, final[1], halo_back_end,
            back_conv[4], back_conv[5], back_conv[6], join_near[3], back_conv[7], grad0[0], grad0[1], grad0[2],
            grad0[3], feed_end, feed_credit, back1[0], back1[1], back1[2], back1[3], back1[4], join_far[0],
            back1[5], back1[6], final[2], back1[7], join_near[0], inputs.end, first_back, gain_send[0], final[3],
            gain_add[0], gain_send[1], gain_add[1], gain_send[2], gain_add[2], gains_line, final[0], gains_end, end,
        ]
    )


class Loop:
    def __init__(self, count, body):
        self.count, self.body = count, body

    def __getitem__(self, n):
        return (self, n)


def play(order):
    order = list(order)
    while order:
        entry = order.pop(0)
        if not isinstance(entry, tuple):
            entry()
            continue
        loop, _ = entry
        between = {}
        for n in range(1, loop.count):
            between[n] = []
            while order[0] != (loop, n):
                between[n].append(order.pop(0))
            order.pop(0)

        def turn(n, _):
            for m, acts in between.items():
                if acts:

                    @pl.when(n == m)
                    def _():
                        play(acts)

            loop.body(n)
            return 0

        lax.fori_loop(0, loop.count, turn, 0)


def block_step(tok, cot, gains, weights, layers):
    rows, seg = weights.shape[0], tok.shape[0]
    count = len(WIDTHS)
    tokens = 2 * GROUPS * seg
    vmem, anywhere = pl.BlockSpec(memory_space=pltpu.VMEM), pl.BlockSpec(memory_space=pl.ANY)
    shape, scratch = jax.ShapeDtypeStruct, pltpu.VMEM
    dma, regular = pltpu.SemaphoreType.DMA, pltpu.SemaphoreType.REGULAR
    hops = layers - 1
    wide, biggest = sum(WIDTHS), max(WIDTHS)
    out_shape = [
        shape((seg, D), BF16),
        shape((seg, D), BF16),
        shape((8, 2 * GROUPS * WIDE), F32),
        shape((rows, wide), F32),
        shape((rows, wide), BF16),
        shape((tokens, D), BF16),
    ] + [shape((2, hops, 2 * rows, width), BF16) for width in WIDTHS]
    scratch_shapes = (
        [scratch((D, width), BF16) for width in WIDTHS]
        + [
            scratch((tokens, D), BF16),
            scratch((tokens, D), BF16),
            scratch((tokens, 2 * PAD_F), BF16),
            scratch((tokens, PAD_F), BF16),
            scratch((GROUPS, 8 + 2 * seg, WIDE), F32),
            scratch((GROUPS, 8 + 2 * seg, WIDE), F32),
            scratch((tokens, WIDE), BF16),
            scratch((seg, D), F32),
            scratch((seg, D), F32),
            scratch((seg, D), F32),
            scratch((4, seg, D), BF16),
            scratch((2, seg, D), BF16),
            scratch((seg, D), BF16),
        ]
        + [scratch((D, width), BF16) for width in WIDTHS[1:]]
        + [
            scratch((2 * rows, biggest), BF16),
            scratch((rows, biggest), F32),
            scratch((rows, GROUP_COLS - 4 * D), F32),
            scratch((rows, wide), BF16),
            scratch((8, WIDE), F32),
            scratch((3, 8, 2 * GROUPS * WIDE), F32),
            scratch((2, hops, 8, 2 * GROUPS * WIDE), F32),
            dma,
            dma((5,)),
            dma((count,)),
            dma((count,)),
            dma((count, 2, hops, 2)),
            dma((count, 2, hops, 2)),
            dma((4, 11)),
            dma((4, 11)),
            dma((4, 10)),
            dma((4, 10)),
            regular((3,)),
            dma((2,)),
            dma((2,)),
            dma((count, 2, hops)),
            dma((count, 2, hops)),
            dma,
            dma((4,)),
            dma((count,)),
            dma((count,)),
            dma((count,)),
            dma((3,)),
            dma((3,)),
            dma((2, hops)),
            dma((2, hops)),
        ]
    )
    return pl.pallas_call(
        functools.partial(block_kernel, layers, rows),
        out_shape=out_shape,
        in_specs=[vmem] * 3 + [anywhere],
        out_specs=[vmem] * 3 + [anywhere] * (3 + count),
        scratch_shapes=scratch_shapes,
        compiler_params=pltpu.CompilerParams(
            collective_id=0, has_side_effects=True, vmem_limit_bytes=VMEM_BYTES
        ),
        name="block_step",
    )(tok, cot, gains, weights)[:5]


def band(rows, most):
    return max(size for size in range(16, most + 1, 16) if rows % size == 0)


def adam_update(param, grad, first, second, rate, decay):
    first_new = MOMENT_DECAY * first + (1.0 - MOMENT_DECAY) * grad
    second_new = SQUARE_DECAY * second + (1.0 - SQUARE_DECAY) * grad * grad
    root = jnp.sqrt(second_new * (1.0 / (1.0 - SQUARE_DECAY**STEP))) + ADAM_EPSILON
    step = first_new * (rate / (1.0 - MOMENT_DECAY**STEP)) / root
    return (first_new, second_new, param * (1.0 - rate * decay) - step)


def update_kernel(
    inner_ref, mine_ref, theirs_ref, weights_ref, first_ref, second_ref, sums_ref, gains_ref, gains_first_ref,
    gains_second_ref, block_ref, input_ref, grad_out, first_out, second_out, weights_out, gains_grad_out,
    gains_first_out, gains_second_out, gains_out, block_out, input_out,
):
    is_low = inner_ref[0] == 0
    mine, theirs = mine_ref[...], theirs_ref[...].astype(F32)
    for half in (0, 1):
        chosen = jnp.where(is_low, mine, theirs) if half == 0 else jnp.where(is_low, theirs, mine)
        for first, own, width, _ in column_pieces(half):
            grad_out[:, first : first + width] = chosen[:, own : own + width]
    first_out[...], second_out[...], weights_out[...] = adam_update(
        weights_ref[...], grad_out[...], first_ref[...], second_ref[...], WEIGHT_RATE, WEIGHT_DECAY
    )

    @pl.when(pl.program_id(0) == 0)
    def _():
        gains_grad_out[0:2] = sums_ref[0:2, :D]
        for n in range(2 * GROUPS):
            gains_grad_out[2:5, n * HALF_Q : (n + 1) * HALF_Q] = sums_ref[2:5, n * WIDE : n * WIDE + HALF_Q]
        gains_first_out[...], gains_second_out[...], gains_out[...] = adam_update(
            gains_ref[...], gains_grad_out[...], gains_first_ref[...], gains_second_ref[...], GAIN_RATE, 0.0
        )
        block_out[...] = block_ref[...]
        input_out[...] = input_ref[...]


def update(inner, mine, theirs, weights, first, second, sums, gains, gains_first, gains_second, block, grad):
    rows, cols = weights.shape
    wide = mine.shape[1]
    size = band(rows, 32)
    by_row = lambda width: pl.BlockSpec((size, width), lambda n: (n, 0))
    whole = lambda values: pl.BlockSpec(values.shape, lambda n: (0, 0))
    shape = jax.ShapeDtypeStruct
    return pl.pallas_call(
        update_kernel,
        grid=(rows // size,),
        out_shape=[shape((rows, cols), F32)] * 4 + [shape(gains.shape, F32)] * 4 + [shape(block.shape, BF16)] * 2,
        in_specs=[pl.BlockSpec(memory_space=pltpu.SMEM)]
        + [by_row(wide)] * 2
        + [by_row(cols)] * 3
        + [whole(sums)]
        + [whole(gains)] * 3
        + [whole(block)] * 2,
        out_specs=[by_row(cols)] * 4 + [whole(gains)] * 4 + [whole(block)] * 2,
        compiler_params=pltpu.CompilerParams(vmem_limit_bytes=VMEM_BYTES),
        name="update",
    )(inner, mine, theirs, weights, first, second, sums, gains, gains_first, gains_second, block, grad)


def on_device(
    tokens, gains_taps, weights, cotangent, weight_first, weight_second, gains_first, gains_second
):
    layers = lax.axis_size("seq") // 2
    inner_word = (lax.axis_index("seq") % 2).astype(jnp.int32).reshape(1)
    block_out, input_grad, gain_sums, mine, theirs = block_step(
        tokens[0], cotangent[0], gains_taps, weights, layers
    )
    (
        weight_grad, weight_first_new, weight_second_new, weight_new,
        gains_grad, gains_first_new, gains_second_new, gains_new, block_out, input_grad,
    ) = update(
        inner_word, mine, theirs, weights, weight_first, weight_second,
        gain_sums, gains_taps, gains_first, gains_second, block_out, input_grad,
    )
    return (
        block_out[None],
        input_grad[None],
        weight_grad,
        weight_first_new,
        weight_second_new,
        weight_new,
        gains_grad,
        gains_first_new,
        gains_second_new,
        gains_new,
    )


def solution(mesh):
    tokens, rows, whole = P("shard", "seq", None), P("seq", "shard"), P()
    return jax.shard_map(
        on_device,
        mesh=mesh,
        in_specs=(tokens, whole, rows, tokens, rows, rows, whole, whole),
        out_specs=(tokens, tokens, rows, rows, rows, rows, whole, whole, whole, whole),
        check_vma=False,
    )
```

```python
import functools

import jax
import jax.numpy as jnp
from jax import lax
from jax.experimental import pallas as pl
from jax.experimental.pallas import tpu as pltpu
from jax.sharding import PartitionSpec as P

D = 1536
FF = 6912
STEP = 10
GROUPS = 4
QUARTER = D // GROUPS
UNITS = FF // GROUPS
GROUP_COLS = 4 * QUARTER + 3 * UNITS
HALF_Q = QUARTER // 2
HALF_F = UNITS // 2
LANES = 128
PAD_F = -(-HALF_F // LANES) * LANES
WIDE = 256
CONV_COLS = 4 * HALF_Q
UNIT_CHUNKS = (384, 256, PAD_F - 640)
UNIT_STARTS = (0, 384, 640)
CUT = 640
WIDTHS = (CUT,) + tuple(3 * units for units in UNIT_CHUNKS) + (CONV_COLS - CUT,)
STARTS = tuple(sum(WIDTHS[:k]) for k in range(len(WIDTHS)))
SPREAD_SPLITS = (208, 176, 128, 112)
COLLECT_SPLITS = (128, 128, 96, 96)
REACH = (1, 1, 1, 1, 1)
CUT_FIRST = 3
SLICE = 384
TILE = 16
ROWS = 48

MOMENT_DECAY = 0.9
SQUARE_DECAY = 0.95
ADAM_EPSILON = 1e-08
NORM_EPSILON = 1e-05
WEIGHT_RATE = 0.02
GAIN_RATE = 0.2
WEIGHT_DECAY = 0.1

BF16 = jnp.bfloat16
F32 = jnp.float32
MESH = pl.DeviceIdType.MESH
VMEM_BYTES = 63 * 1024 * 1024


def place():
    seq, shard = lax.axis_index("seq"), lax.axis_index("shard")
    inner, core = lax.rem(seq, 2), lax.rem(shard, 2)
    return seq, shard, inner, core


def partners():
    seq, shard, inner, core = place()
    across = {"seq": seq + 1 - 2 * inner, "shard": shard}
    beside = {"seq": seq, "shard": lax.rem(shard + 2, 4)}
    twin = {"seq": seq, "shard": shard + 1 - 2 * core}
    return across, beside, twin


def remote(src, dst, send, recv, device):
    return pltpu.make_async_remote_copy(
        src_ref=src, dst_ref=dst, send_sem=send, recv_sem=recv, device_id=device, device_id_type=MESH
    )


def line():
    seq, shard, _, _ = place()
    size = lax.axis_size("seq")
    return seq // 2, lambda steps: {"seq": lax.rem(seq + 2 * steps + size, size), "shard": shard}


def greet(layers):
    outer, at = line()
    barrier = pltpu.get_barrier_semaphore()
    for device in partners():
        pl.semaphore_signal(barrier, inc=1, device_id=device, device_id_type=MESH)
    for steps in range(1, layers):
        for sign in (1, -1):

            @pl.when(in_line(outer + sign * steps, layers))
            def _():
                pl.semaphore_signal(barrier, inc=1, device_id=at(sign * steps), device_id_type=MESH)


def greeted(layers):
    pl.semaphore_wait(pltpu.get_barrier_semaphore(), 3 + layers - 1)


def in_line(index, layers):
    return (index >= 0) & (index < layers)


def allow(credit):
    for device in partners():
        pl.semaphore_signal(credit, inc=1, device_id=device, device_id_type=MESH)


def dot(left, right):
    return jnp.dot(left, right, preferred_element_type=F32)


def dot_rows(left, right):
    return lax.dot_general(left, right, (((1,), (1,)), ((), ())), preferred_element_type=F32)


def dot_columns(left, right):
    return lax.dot_general(left, right, (((0,), (0,)), ((), ())), preferred_element_type=F32)


def aligned(start, size, multiple=16):
    return pl.ds(pl.multiple_of(start, multiple), size)


class Gather:
    def __init__(self, layers, rows, oth, outs, send_x, recv_x, send_z, recv_z):
        self.layers, self.rows, self.oth, self.outs = layers, rows, oth, outs
        self.send_x, self.recv_x, self.send_z, self.recv_z = send_x, recv_x, send_z, recv_z
        self.seq, _, self.inner, _ = place()
        self.outer, self.at = line()
        self.across = partners()[0]

    def seq_rows(self, index):
        return aligned(index * self.rows, self.rows)

    def layer_rows(self, direction, distance):
        origin = self.outer - distance if direction == 0 else self.outer + distance
        return aligned(origin * 2 * self.rows, 2 * self.rows)

    def copy(self, k, src, dst, direction, distance, hop, piece):
        slot = (k, direction, distance + hop - 1, piece)
        return remote(
            src, dst, self.send_z.at[slot], self.recv_z.at[slot], self.at(hop if direction == 0 else -hop)
        )

    def goes(self, direction, hop):
        return in_line(self.outer + (hop if direction == 0 else -hop), self.layers)

    def has_come(self, direction, distance):
        return in_line(self.outer + (-distance if direction == 0 else distance), self.layers)

    def hops(self, k, distance):
        return range(1, min(REACH[k], self.layers - 1 - distance) + 1)

    def own_copy(self, k, direction, hop):
        here = self.outs[k].at[self.seq_rows(self.seq)]
        return self.copy(k, here, here, direction, 0, hop, 0)

    def other_copy(self, k, direction, hop):
        there = self.outs[k].at[self.seq_rows(self.seq + 1 - 2 * self.inner)]
        return self.copy(k, there, there, direction, 0, hop, 1)

    def pass_copy(self, k, direction, distance, hop):
        ref = self.outs[k].at[self.layer_rows(direction, distance)]
        return self.copy(k, ref, ref, direction, distance, hop, 0)

    def other_rows(self, k):
        return self.oth.at[pl.ds(k * self.rows, self.rows), pl.ds(0, WIDTHS[k])]

    def exchange(self, k):
        self.x_copy(k).start()

    def x_copy(self, k):
        here = self.outs[k].at[self.seq_rows(self.seq)]
        return remote(self.other_rows(k), here, self.send_x.at[k], self.recv_x.at[k], self.across)

    def crossed(self):
        for k in range(len(self.outs)):
            self.x_copy(k).wait_send()

    def send_own(self, k):
        for hop in self.hops(k, 0):
            for direction in (0, 1):

                @pl.when(self.goes(direction, hop))
                def _():
                    self.own_copy(k, direction, hop).start()

    def send_other(self, k):
        self.x_copy(k).wait_recv()
        for hop in self.hops(k, 0):
            for direction in (0, 1):

                @pl.when(self.goes(direction, hop))
                def _():
                    self.other_copy(k, direction, hop).start()

    def step(self, k, distance):
        for direction in (0, 1):

            @pl.when(self.has_come(direction, distance))
            def _():
                if distance <= REACH[k]:
                    origin = self.outer - distance if direction == 0 else self.outer + distance
                    for piece in (0, 1):
                        index = 2 * origin + (self.inner if piece == 0 else 1 - self.inner)
                        ref = self.outs[k].at[self.seq_rows(index)]
                        self.copy(k, ref, ref, direction, distance - 1, 1, piece).wait_recv()
                else:
                    ref = self.outs[k].at[self.layer_rows(direction, distance)]
                    self.copy(k, ref, ref, direction, distance - 1, 1, 0).wait_recv()
                if distance % REACH[k] == 0:
                    for hop in self.hops(k, distance):

                        @pl.when(self.goes(direction, hop))
                        def _():
                            self.pass_copy(k, direction, distance, hop).start()

    def steps(self, k, first, last=None):
        last = self.layers - 1 if last is None else min(last, self.layers - 1)
        for distance in range(first, last + 1):
            self.step(k, distance)

    def finish(self):
        for k in range(len(self.outs)):
            for distance in range(0, self.layers - 1, REACH[k]):
                for hop in self.hops(k, distance):
                    for direction in (0, 1):

                        @pl.when(self.goes(direction, hop) & self.has_come(direction, distance))
                        def _():
                            if distance == 0:
                                self.own_copy(k, direction, hop).wait_send()
                                self.other_copy(k, direction, hop).wait_send()
                            else:
                                self.pass_copy(k, direction, distance, hop).wait_send()


class Reduce:
    def __init__(self, layers, rows, grads, slots, stage, spare, total, outgoing, mine, theirs, sems):
        self.layers, self.rows, self.grads, self.slots = layers, rows, grads, slots
        self.stage, self.spare, self.total, self.outgoing = stage, spare, total, outgoing
        self.mine, self.theirs = mine, theirs
        self.send_g, self.recv_g, self.fetched, self.fetches, self.stored, self.send_o, self.recv_o = sems
        _, _, self.inner, _ = place()
        self.outer, self.at = line()
        self.across = partners()[0]

    def owner(self, direction, distance):
        return self.outer + distance if direction == 0 else self.outer - distance

    def upstream(self, direction, steps):
        return in_line(self.outer - steps if direction == 0 else self.outer + steps, self.layers)

    def block(self, k, owner):
        return self.grads[k].at[aligned(owner * 2 * self.rows, 2 * self.rows), pl.ds(0, WIDTHS[k])]

    def copy(self, k, src, direction, distance):
        slot = (direction, distance - 1)
        return remote(
            src,
            self.slots[k].at[slot],
            self.send_g.at[(k,) + slot],
            self.recv_g.at[(k,) + slot],
            self.at(1 if direction == 0 else -1),
        )

    def send(self, k, direction, distance):
        self.copy(k, self.block(k, self.owner(direction, distance)), direction, distance).start()

    def direct(self, k, part=None, least=1, most=None):
        for distance in range(most or self.layers - 1, least - 1, -1):
            for direction in (0, 1):
                owner = self.owner(direction, distance)
                here = in_line(owner, self.layers) & jnp.logical_not(self.upstream(direction, 1))
                if part is not None:
                    here = here & (owner * 2 * self.rows // SLICE == part)

                @pl.when(here)
                def _():
                    self.send(k, direction, distance)

    def fetch(self, k, direction, distance):
        slot = self.slots[k].at[direction, distance - 1]
        self.copy(k, slot, direction, distance).wait_recv()
        held = self.stage.at[:, pl.ds(0, WIDTHS[k])]
        copy = pltpu.make_async_copy(slot, held, self.fetched)
        copy.start()
        copy.wait()

    def tiles(self, body):
        def step(n, _):
            body(aligned(n * TILE, TILE))
            return 0

        lax.fori_loop(0, 2 * self.rows // TILE, step, 0)

    def join(self, k, most, least):
        cols = pl.ds(0, WIDTHS[k])
        for distance in range(most, least - 1, -1):
            for direction in (0, 1):
                owner = self.owner(direction, distance)

                @pl.when(in_line(owner, self.layers) & self.upstream(direction, 1))
                def _():
                    def add(tile):
                        base = self.owner(direction, distance) * 2 * self.rows
                        rows = pl.ds(pl.multiple_of(base + tile.start, 16), TILE)
                        ref = self.grads[k]
                        ref[rows, cols] = (
                            ref[rows, cols].astype(F32) + self.stage[tile, cols].astype(F32)
                        ).astype(BF16)

                    self.fetch(k, direction, distance + 1)
                    self.tiles(add)
                    self.send(k, direction, distance)

    def final(self, k, before=None):
        cols = pl.ds(0, WIDTHS[k])
        came = [(1, 0), (1, 1)]

        def fetch(n, distance, direction):
            return pltpu.make_async_copy(
                self.slots[k].at[direction, distance - 1],
                self.spare.at[pl.ds(n * 2 * self.rows, 2 * self.rows), cols],
                self.fetches.at[n],
            )

        for n, (distance, direction) in enumerate(came):

            @pl.when(self.upstream(direction, distance))
            def _():
                self.copy(k, self.slots[k].at[direction, distance - 1], direction, distance).wait_recv()
                fetch(n, distance, direction).start()

        if before is not None:
            self.store(before).wait()

        here, there = self.inner * self.rows, (1 - self.inner) * self.rows

        def each(base, body):
            def step(n, _):
                body(base + n * TILE, n * TILE)
                return 0

            lax.fori_loop(0, self.rows // TILE, step, 0)

        for n, (distance, direction) in enumerate(came):

            @pl.when(self.upstream(direction, distance))
            def _():
                fetch(n, distance, direction).wait()

        def add_up(flags):
            def total(rows):
                value = self.grads[k][aligned(self.outer * 2 * self.rows + rows, TILE), cols].astype(F32)
                for n, flag in enumerate(flags):
                    if flag:
                        value = value + self.spare[aligned(n * 2 * self.rows + rows, TILE), cols].astype(F32)
                return value

            def send(rows, at):
                self.outgoing[aligned(at, TILE), pl.ds(STARTS[k], WIDTHS[k])] = total(rows).astype(BF16)

            def keep(rows, at):
                self.total[aligned(at, TILE), cols] = total(rows)

            each(there, send)
            self.over(k).start()
            each(here, keep)
            self.store(k).start()

        patterns = {}
        for place_in_line in range(self.layers):
            flags = tuple(
                0 <= (place_in_line - distance if direction == 0 else place_in_line + distance) < self.layers
                for distance, direction in came
            )
            patterns.setdefault(flags, []).append(place_in_line)
        for flags, places in patterns.items():
            here_now = functools.reduce(jnp.logical_or, [self.outer == p for p in places])

            @pl.when(here_now)
            def _():
                add_up(flags)

    def over(self, k):
        wide = pl.ds(STARTS[k], WIDTHS[k])
        return remote(
            self.outgoing.at[:, wide], self.theirs.at[:, wide], self.send_o.at[k], self.recv_o.at[k], self.across
        )

    def store(self, k):
        return pltpu.make_async_copy(
            self.total.at[:, pl.ds(0, WIDTHS[k])], self.mine.at[:, pl.ds(STARTS[k], WIDTHS[k])], self.stored.at[k]
        )

    def wait_sent(self, k):
        for distance in range(1, self.layers):
            for direction in (0, 1):
                owner = self.owner(direction, distance)

                @pl.when(in_line(owner, self.layers))
                def _():
                    self.copy(k, self.block(k, owner), direction, distance).wait_send()

    def finish(self, before):
        self.store(before).wait()
        for k in range(len(self.grads)):
            self.over(k).wait()


class Spread:
    slots = range(11)

    def __init__(self, buf, seg, split, send, recv):
        self.buf, self.seg, self.split, self.send, self.recv = buf, seg, split, send, recv

    def index(self, n):
        _, shard, inner, core = place()
        row, flip, other = (n // 2) % 2, n // 4, n % 2
        return 2 * (lax.rem(shard + 2 * row, 4) + other * (1 - 2 * core)) + inner + flip * (1 - 2 * inner)

    def copy(self, slot):
        across, beside, twin = partners()
        low, high, whole = (0, self.split), (self.split, self.seg - self.split), (0, self.seg)
        n, (first, size), device = {
            0: (0, low, across),
            9: (0, high, across),
            1: (0, high, beside),
            10: (0, low, beside),
            2: (0, whole, twin),
            3: (4, low, beside),
            4: (4, whole, twin),
            5: (2, high, across),
            6: (2, whole, twin),
            7: (6, low, twin),
            8: (6, high, twin),
        }[slot]
        ref = self.buf.at[aligned(self.index(n) * self.seg + first, size)]
        return remote(ref, ref, self.send.at[slot], self.recv.at[slot], device)

    def push(self, *slots):
        for slot in slots:
            self.copy(slot).start()

    def came(self, *slots):
        for slot in slots:
            self.copy(slot).wait_recv()

    def start(self):
        self.push(0, 1, 9, 10, 2)

    def first(self):
        self.came(1)
        self.push(5)
        self.came(0)
        self.push(3)

    def near(self):
        self.came(10)
        self.push(6)
        self.came(9)
        self.push(4)

    def far(self):
        self.came(3)
        self.push(7)
        self.came(5)
        self.push(8)

    def sent(self):
        for slot in self.slots:
            self.copy(slot).wait_send()

    def end(self):
        self.came(2, 4, 6, 7, 8)
        self.sent()

    def before(self, n):
        return {
            1: (lambda: self.came(2),),
            2: (self.first, self.near),
            3: (lambda: self.came(6),),
            5: (lambda: self.came(4),),
            6: (self.far,),
            7: (lambda: self.came(7, 8),),
        }.get(n, ())


class Collect:
    def __init__(self, part, seg, split, total, pair, near, joined, send, recv):
        self.part, self.seg, self.total = part, seg, total
        self.pair, self.near, self.joined, self.send, self.recv = pair, near, joined, send, recv
        _, self.shard, self.inner, core = place()
        self.twin_shard = self.shard + 1 - 2 * core
        self.low, self.high, self.whole = (0, split), (split, seg - split), (0, seg)
        self.cols = pl.ds(0, D)

    def index(self, s, k):
        row, flip = 1 - k % 2, 1 - k // 2
        return 2 * lax.rem(s + 2 * row, 4) + self.inner + flip * (1 - 2 * self.inner)

    def pair_copy(self, k):
        src = self.part.at[aligned(self.index(self.twin_shard, k) * self.seg, self.seg), self.cols]
        return remote(src, self.pair.at[k], self.send.at[k], self.recv.at[k], partners()[2])

    def copy(self, slot):
        across, beside, _ = partners()
        src, dst, (first, size), device = {
            4: (self.pair.at[0], self.joined, self.low, across),
            5: (self.pair.at[0], self.joined, self.high, beside),
            6: (self.pair.at[1], self.near.at[0], self.low, across),
            7: (self.pair.at[2], self.near.at[1], self.high, beside),
            8: (self.pair.at[2], self.near.at[1], self.low, beside),
            9: (self.pair.at[1], self.near.at[0], self.high, across),
        }[slot]
        rows = pl.ds(first, size)
        return remote(src.at[rows], dst.at[rows], self.send.at[slot], self.recv.at[slot], device)

    def over(self, span, body):
        def step(n, _):
            body(aligned(span[0] + n * 16, 16))
            return 0

        lax.fori_loop(0, span[1] // 16, step, 0)

    def mine(self, k, rows):
        return self.part[aligned(self.index(self.shard, k) * self.seg + rows.start, 16), self.cols].astype(F32)

    def add_pair(self, k):
        def add(rows):
            self.pair[k, rows] = (self.mine(k, rows) + self.pair[k, rows].astype(F32)).astype(BF16)

        self.pair_copy(k).wait_recv()
        self.over(self.whole, add)
        for slot in ((4, 5), (6,), (7,))[k]:
            self.copy(slot).start()

    def add_own(self):
        def add(rows):
            self.total[rows] = self.mine(3, rows) + self.pair[3, rows].astype(F32)

        self.pair_copy(3).wait_recv()
        self.over(self.whole, add)

    def pass_on(self):
        for slot, k, span, after in ((4, 2, self.low, 8), (5, 1, self.high, 9)):

            def add(rows):
                self.pair[k, rows] = (self.pair[k, rows].astype(F32) + self.joined[rows].astype(F32)).astype(BF16)

            self.copy(slot).wait_recv()
            self.over(span, add)
            self.copy(after).start()

    def push(self):
        for k in range(4):
            self.pair_copy(k).start()

    def make(self, n, produce):
        k, own = n // 2, n % 2
        produce(self.index(jnp.where(own == 1, self.shard, self.twin_shard), k))

        @pl.when(own == 0)
        def _():
            self.pair_copy(k).start()

        for m in range(3):

            @pl.when(n == 2 * m + 1)
            def _():
                self.add_pair(m)
                if m == 2:
                    self.pass_on()

        pl.when(n == 7)(self.add_own)

    def end(self):
        def add(rows):
            near = self.near[0, rows].astype(F32) + self.near[1, rows].astype(F32)
            self.total[rows] = self.total[rows] + near

        for slots, span in (((6, 8), self.low), ((7, 9), self.high)):
            for slot in slots:
                self.copy(slot).wait_recv()
            self.over(span, add)
        for k in range(4):
            self.pair_copy(k).wait_send()
        for slot in range(4, 10):
            self.copy(slot).wait_send()


def norm_scale(values):
    return lax.rsqrt(jnp.mean(values * values, axis=-1, keepdims=True) + NORM_EPSILON)


def by_rows(rows, body, carry=0):
    def step(n, carry):
        return body(aligned(n * ROWS, ROWS), carry)

    return lax.fori_loop(0, rows // ROWS, step, carry)


def norm_back(values, gain, upstream):
    scale = norm_scale(values)
    scaled = gain * upstream
    inner = jnp.mean(scaled * values, axis=-1, keepdims=True)
    return (
        scale * scaled - values * scale * scale * scale * inner,
        jnp.sum(upstream * values * scale, axis=0, keepdims=True),
    )


REFS = (
    "tok", "cot", "gains", "weights",
    "block_out", "input_grad", "gain_sums", "mine", "theirs", "n1_held", "slot0", "slot1", "slot2", "slot3", "slot4",
    "w0", "w1", "w2", "w3", "w4", "seq_a", "seq_b", "du", "act", "c_all", "gated", "mixed", "resid", "dresid", "total",
    "pair", "near", "joined", "g1", "g2", "g3", "g4", "stage", "sum", "tail", "outgoing", "tap_sums", "gain_in", "gain_line",
    "held", "loaded", "send_x", "recv_x", "send_z", "recv_z", "send_s", "recv_s", "send_c", "recv_c", "credit",
    "halo_send", "halo_recv", "send_g", "recv_g", "fetched", "fetches", "stored", "send_o", "recv_o",
    "send_a", "recv_a", "send_l", "recv_l",
)


def column_pieces(half):
    pieces = [(m * QUARTER + half * HALF_Q, m * HALF_Q, HALF_Q, 0) for m in range(3)]
    first, left = 3 * QUARTER + half * HALF_Q, CUT - 3 * HALF_Q
    pieces += [(first, 3 * HALF_Q, left, 0), (first + left, STARTS[-1], HALF_Q - left, 0)]
    for k, (start, units) in enumerate(zip(UNIT_STARTS, UNIT_CHUNKS), 1):
        real = min(units, HALF_F - start)
        for m in range(3):
            first = 4 * QUARTER + m * UNITS + half * HALF_F + start
            pieces.append((first, STARTS[k] + m * units, real, units - real))
    return pieces


def block_kernel(layers, rows, *all_refs):
    r = dict(zip(REFS, all_refs, strict=True))
    tok, cot, gains = r["tok"], r["cot"], r["gains"]
    seq_a, seq_b, du, act = r["seq_a"], r["seq_b"], r["du"], r["act"]
    c_all, gated, mixed, total = r["c_all"], r["gated"], r["mixed"], r["total"]
    weights = (r["w0"], r["w1"], r["w2"], r["w3"], r["w4"])
    seg = tok.shape[0]
    _, shard, inner, _ = place()
    outer, at = line()
    me = 2 * shard + inner
    my_rows = aligned(me * seg, seg)
    chunks = list(zip(range(1, 1 + len(UNIT_CHUNKS)), UNIT_STARTS, UNIT_CHUNKS))
    gather = Gather(
        layers, rows, r["g1"], weights, r["send_x"], r["recv_x"], r["send_z"], r["recv_z"]
    )
    reduce = Reduce(
        layers, rows, (r["w2"], r["g1"], r["g2"], r["g3"], r["g4"]), [r[f"slot{k}"] for k in range(len(WIDTHS))],
        r["stage"], r["w1"], r["sum"], r["outgoing"], r["mine"], r["theirs"],
        (r["send_g"], r["recv_g"], r["fetched"], r["fetches"], r["stored"], r["send_o"], r["recv_o"]),
    )

    def spread(buf, n):
        return Spread(buf, seg, SPREAD_SPLITS[n], r["send_s"].at[n], r["recv_s"].at[n])

    def collect(part, n):
        sems = r["send_c"].at[n], r["recv_c"].at[n]
        return Collect(part, seg, COLLECT_SPLITS[n], total, r["pair"], r["near"], r["joined"], *sems)

    one, up, two, three = spread(seq_a, 0), spread(seq_b, 1), spread(seq_a, 2), spread(seq_a, 3)
    branch, down, feed, inputs = collect(seq_a, 0), collect(seq_b, 1), collect(du, 2), collect(seq_a, 3)
    lanes = lax.broadcasted_iota(jnp.int32, (seg, WIDE), 1) < HALF_Q
    taps = pltpu.roll(gains[...], lax.rem(D - shard * QUARTER - inner * HALF_Q, D), 1)[2:5, :WIDE]
    kept = pl.ds(D, WIDE)
    sums, tap_sums = r["gain_sums"], r["tap_sums"]

    def block(t):
        return aligned(t * seg, seg)

    def mine(part):
        return pl.ds(pl.multiple_of(me * seg + part.start, 16), part.size)

    def first_norm():
        def rows(part, _):
            values = tok[part].astype(F32)
            seq_a[mine(part)] = (values * norm_scale(values) * gains[0:1, :]).astype(BF16)
            return 0

        by_rows(seg, rows)

    def up_start():
        seq_b[my_rows] = cot[...]
        up.start()

    def held():
        return pltpu.make_async_copy(seq_a, r["n1_held"], r["held"])

    def reload():
        return pltpu.make_async_copy(r["n1_held"], seq_b, r["held"])

    def project(s):
        for i in (0, 1):
            parts = dot(seq_a[block(2 * s + i)], weights[0][...])
            b = jnp.where(lanes, parts[:, :WIDE], 0.0)
            c = pltpu.roll(parts[:, 128 : 128 + 384], 384 - 64, 1)[:, :WIDE]
            x = parts[:, 384 : 384 + WIDE]
            c_all[s, pl.ds(i * seg, seg)] = jnp.where(lanes, c, 0.0)
            gated[s, pl.ds(8 + i * seg, seg)] = (b * x).astype(BF16).astype(F32)

    def ahead():
        return remote(
            gated.at[:, pl.ds(2 * seg, 8)], gated.at[:, pl.ds(0, 8)], r["halo_send"].at[0], r["halo_recv"].at[0], at(1)
        )

    def halo():
        pl.when(outer < layers - 1)(lambda: ahead().start())

        @pl.when(outer == 0)
        def _():
            gated[:, pl.ds(0, 8)] = jnp.zeros((GROUPS, 8, WIDE), F32)

    def convolved(s, i):
        return (
            taps[0:1, :] * gated[s, pl.ds(6 + i * seg, seg)]
            + taps[1:2, :] * gated[s, pl.ds(7 + i * seg, seg)]
            + taps[2:3, :] * gated[s, pl.ds(8 + i * seg, seg)]
        )

    def convolve(t):
        for i in (0, 1):

            @pl.when(t % 2 == i)
            def _():
                s = t // 2
                mixed[block(t)] = pltpu.roll(c_all[s, pl.ds(i * seg, seg)] * convolved(s, i), 64, 1).astype(BF16)

        here, half = block(t), WIDE // 2
        part = dot_rows(mixed[here, pl.ds(0, half)], weights[0][:, pl.ds(512, half)])
        seq_a[here] = (part + dot_rows(mixed[here, pl.ds(half, half)], weights[4][...])).astype(BF16)

    def branch_end():
        branch.end()
        allow(r["credit"].at[0])

    def second_norm():
        def rows(part, _):
            values = tok[part].astype(F32) + total[part]
            r["resid"][part] = values
            seq_a[mine(part)] = (values * norm_scale(values) * gains[1:2, :]).astype(BF16)
            return 0

        by_rows(seg, rows)
        pl.semaphore_wait(r["credit"].at[0], 3)

    def hidden(k, start, units, t):
        ref, here = weights[k], block(t)
        gate = dot(seq_a[here], ref[:, pl.ds(0, units)])
        upval = dot(seq_a[here], ref[:, pl.ds(units, units)])
        dact = dot(seq_b[here], ref[:, pl.ds(2 * units, units)])
        sigma = jax.nn.sigmoid(gate)
        silu = gate * sigma
        act[here, pl.ds(start, units)] = (silu * upval).astype(BF16)
        dgate = dact * upval * sigma * (1.0 + gate * (1.0 - sigma))
        du[here, pl.ds(2 * start, units)] = dgate.astype(BF16)
        du[here, pl.ds(2 * start + units, units)] = (dact * silu).astype(BF16)

    def slice_of(n):
        return jnp.where(outer < layers // 2, D // SLICE - 1 - n, n)

    def gate_up_grads(k, start, units, n):
        part = slice_of(n)
        left = seq_a[:, aligned(part * SLICE, SLICE, 128)]
        reduce.grads[k][aligned(part * SLICE, SLICE), pl.ds(0, 2 * units)] = dot_columns(
            left, du[:, pl.ds(2 * start, 2 * units)]
        ).astype(BF16)

    def down_grads(k, start, units, n):
        part = slice_of(n)
        left = seq_b[:, aligned(part * SLICE, SLICE, 128)]
        reduce.grads[k][aligned(part * SLICE, SLICE), pl.ds(2 * units, units)] = dot_columns(
            left, act[:, pl.ds(start, units)]
        ).astype(BF16)

    def grads(k, start, units, n):
        gate_up_grads(k, start, units, n)
        down_grads(k, start, units, n)
        reduce.direct(k, slice_of(n))

    def second(t):
        here = block(t)
        seq_b[here] = sum(
            dot_rows(du[here, pl.ds(2 * start, 2 * units)], weights[k][:, pl.ds(0, 2 * units)])
            for k, start, units in chunks
        ).astype(BF16)

    def down_end():
        down.end()
        reload().start()
        allow(r["credit"].at[1])

    def forward(t):
        here = block(t)
        du[here, pl.ds(0, D)] = sum(
            dot_rows(act[here, pl.ds(start, units)], weights[k][:, pl.ds(2 * units, units)])
            for k, start, units in chunks
        ).astype(BF16)

    def second_back():
        def rows(part, gain):
            dpart, dgain = norm_back(r["resid"][part], gains[1:2, :], total[part])
            dresid = cot[part].astype(F32) + dpart
            r["dresid"][part] = dresid
            seq_a[mine(part)] = dresid.astype(BF16)
            return gain + dgain

        sums[...] = jnp.zeros(sums.shape, F32)
        tap_sums[...] = jnp.zeros(tap_sums.shape, F32)
        sums[1:2, pl.ds(0, D)] = by_rows(seg, rows, jnp.zeros((1, D), F32))
        pl.semaphore_wait(r["credit"].at[1], 3)

    def mix_back(t):
        s, here = t // 2, block(t)
        held_parts = [dot(seq_a[here], weights[0][:, pl.ds(512, WIDE // 2)]), dot(seq_a[here], weights[4][...])]
        dmixed = pltpu.roll(jnp.concatenate(held_parts, axis=1), WIDE - 64, 1)
        dmixed = jnp.where(lanes, dmixed, 0.0)
        for i in (0, 1):

            @pl.when(t % 2 == i)
            def _():
                du[here, kept] = (dmixed * convolved(s, i)).astype(BF16)
                c_all[s, pl.ds(i * seg, seg)] = dmixed * c_all[s, pl.ds(i * seg, seg)]

    def after():
        return remote(
            c_all.at[:, pl.ds(0, 8)], c_all.at[:, pl.ds(2 * seg, 8)], r["halo_send"].at[1], r["halo_recv"].at[1], at(-1)
        )

    def halo_back():
        pl.when(outer > 0)(lambda: after().start())

        @pl.when(outer == layers - 1)
        def _():
            c_all[:, pl.ds(2 * seg, 8)] = jnp.zeros((GROUPS, 8, WIDE), F32)

    def conv_back(n):
        for i in (0, 1):
            pl.when(n // GROUPS == i)(functools.partial(conv_back_half, n % GROUPS, i))

    def conv_back_half(s, i):
        t = block(2 * s + i)
        dconv = c_all[s, pl.ds(i * seg, seg)]
        dgated = (
            taps[2:3, :] * dconv
            + taps[1:2, :] * c_all[s, pl.ds(1 + i * seg, seg)]
            + taps[0:1, :] * c_all[s, pl.ds(2 + i * seg, seg)]
        )
        parts = dot(seq_b[t], weights[0][:, pl.ds(0, 640)])
        db = dgated * parts[:, 384:640]
        dx = dgated * parts[:, :WIDE]
        dc = jnp.concatenate([du[t, kept].astype(F32), jnp.zeros((seg, 128), F32)], axis=1)
        dc = pltpu.roll(dc, 64, 1)
        act[t, pl.ds(0, 128)] = db[:, :128].astype(BF16)
        act[t, pl.ds(128, 128)] = (db[:, 128:] + dc[:, :128]).astype(BF16)
        act[t, pl.ds(256, 128)] = dc[:, 128:256].astype(BF16)
        act[t, pl.ds(384, WIDE)] = dx.astype(BF16)
        act[t, pl.ds(640, 128)] = jnp.zeros((seg, 128), BF16)
        for k in range(3):
            moved = gated[s, pl.ds(6 + k + i * seg, seg)]
            tap_sums[k : k + 1] = tap_sums[k : k + 1] + jnp.sum(dconv * moved, axis=0, keepdims=True)

    def conv_grads(n):
        part = slice_of(n)
        held_rows, cols = aligned(part * SLICE, SLICE), aligned(part * SLICE, SLICE, 128)
        ref = reduce.grads[0]
        of_parts = dot_columns(seq_b[:, cols], act[:, pl.ds(0, CUT)])
        ref[held_rows, pl.ds(0, 512)] = of_parts[:, :512].astype(BF16)
        of_mixed = dot_columns(seq_a[:, cols], mixed[:, pl.ds(0, CUT - 512)])
        ref[held_rows, pl.ds(512, CUT - 512)] = (of_parts[:, 512:] + of_mixed).astype(BF16)
        reduce.direct(0, part)

    def out_grads(n):
        part = slice_of(n)
        reduce.grads[4][aligned(part * SLICE, SLICE), :] = dot_columns(
            seq_a[:, aligned(part * SLICE, SLICE, 128)], mixed[:, pl.ds(CUT - 512, WIDE - CUT + 512)]
        ).astype(BF16)
        reduce.direct(4, part)

    def feed_end():
        feed.end()
        allow(r["credit"].at[2])
        r["block_out"][...] = (r["resid"][...] + total[...]).astype(BF16)

    def first(t):
        here = block(t)
        seq_a[here] = dot_rows(act[here, pl.ds(0, 640)], weights[0][:, pl.ds(0, 640)]).astype(BF16)

    def first_back():
        def rows(part, gain):
            dpart, dgain = norm_back(tok[part].astype(F32), gains[0:1, :], total[part])
            r["input_grad"][part] = (r["dresid"][part] + dpart).astype(BF16)
            return gain + dgain

        sums[0:1, pl.ds(0, D)] = by_rows(seg, rows, jnp.zeros((1, D), F32))
        sums[2:5, aligned(me * WIDE, WIDE, 128)] = tap_sums[0:3]

    def gains_across(n):
        return remote(sums, r["gain_in"].at[n], r["send_a"].at[n], r["recv_a"].at[n], partners()[n])

    def gains_add(n):
        gains_across(n).wait()
        sums[...] = sums[...] + r["gain_in"][n]

    def line_copy(sign, steps):
        slot = (0 if sign > 0 else 1, steps - 1)
        return remote(
            sums, r["gain_line"].at[slot], r["send_l"].at[slot], r["recv_l"].at[slot], at(sign * steps)
        )

    def gains_line():
        for steps in range(1, layers):
            for sign in (1, -1):
                pl.when(in_line(outer + sign * steps, layers))(line_copy(sign, steps).start)

    def gains_end():
        for steps in range(1, layers):
            for sign in (1, -1):
                pl.when(in_line(outer + sign * steps, layers))(line_copy(sign, steps).wait_send)
                pl.when(in_line(outer - sign * steps, layers))(line_copy(sign, steps).wait_recv)

        own_sums = sums[...]
        for origin in range(layers):
            for steps in range(1, layers):
                for sign in (1, -1):

                    @pl.when((outer - sign * steps == origin))
                    def _():
                        came = r["gain_line"][0 if sign > 0 else 1, steps - 1]
                        sums[...] = came if origin == 0 else sums[...] + came

            if origin > 0:

                @pl.when(outer == origin)
                def _():
                    sums[...] = sums[...] + own_sums

    def end():
        reduce.finish(0)
        for k in range(len(WIDTHS)):
            reduce.wait_sent(k)
        pl.when(outer < layers - 1)(lambda: ahead().wait_send())
        pl.when(outer > 0)(lambda: after().wait_send())

    windows = [
        (r["resid"], 0, D), (r["dresid"], D, D), (total, 2 * D, D), (r["resid"], 3 * D, D),
        (r["tail"], 4 * D, GROUP_COLS - 4 * D),
    ]

    def load(n):
        ref, first, width = windows[n]
        return pltpu.make_async_copy(
            r["weights"].at[:, pl.ds(first, width)], ref.at[pl.ds(0, rows)], r["loaded"].at[n]
        )

    def start():
        for n in (0, 1, 2, 4):
            load(n).start()
        greet(layers)
        load(0).wait()
        cut(0)
        cut(4)
        load(3).start()
        greeted(layers)

    def cut(k):
        def read(part, first, width):
            found = []
            for n, (ref, low, size) in enumerate(windows):
                start, stop = max(first, low), min(first + width, low + size)
                if start < stop and (n == 0) == (k in (0, 4)):
                    found.append(ref[part, start - low : stop - low])
            return found

        def band(n, _):
            part = aligned(n * 16, 16)
            halves = []
            for half in (0, 1):
                pieces = []
                for first, own, width, padding in column_pieces(half):
                    if STARTS[k] <= own < STARTS[k] + WIDTHS[k]:
                        pieces += read(part, first, width)
                        if padding:
                            pieces.append(jnp.zeros((16, padding), F32))
                halves.append(jnp.concatenate(pieces, axis=1))
            is_low = inner == 0
            seq = lax.axis_index("seq")
            own_rows = aligned(seq * rows + n * 16, 16)
            weights[k][own_rows, :] = jnp.where(is_low, halves[0], halves[1]).astype(BF16)
            gather.other_rows(k)[part, :] = jnp.where(is_low, halves[1], halves[0]).astype(BF16)
            return 0

        for n in (1, 2, 3, 4) if k == CUT_FIRST else ():
            load(n).wait()
        lax.fori_loop(0, rows // 16, band, 0)

    def hold():
        held().start()

    def hold_end():
        held().wait()

    def halo_end():
        pl.when(outer > 0)(lambda: ahead().wait_recv())

    def reload_end():
        reload().wait()

    def halo_back_end():
        pl.when(outer < layers - 1)(lambda: after().wait_recv())

    def feed_credit():
        pl.semaphore_wait(r["credit"].at[2], 3)

    def from_spread(moved, body):
        def step(n):
            for m in range(8):
                if moved.before(m):

                    @pl.when(n == m)
                    def _():
                        for act in moved.before(m):
                            act()

            body(moved.index(n))

        return step

    def each(body, *cases):
        return [functools.partial(body, *(case if isinstance(case, tuple) else (case,))) for case in cases]

    every = range(len(WIDTHS))
    cuts = each(cut, *every)
    exchange, send_own, send_other = (
        each(body, *every) for body in (gather.exchange, gather.send_own, gather.send_other)
    )
    step = [each(gather.steps, (k, 1, 1), (k, 2, 2), (k, 3)) for k in every]
    join_far = each(reduce.join, *((k, layers - 2, 2) for k in every))
    join_near = each(reduce.join, *((k, 1, 1) for k in every))
    final = each(reduce.final, (0, 3), 1, (2, 1), (3, 4), (4, 2))
    feed_pair = each(feed.add_pair, 0, 1, 2)
    gain_send = [lambda n=n: gains_across(n).start() for n in range(3)]
    gain_add = each(gains_add, 0, 1, 2)
    d3_far = functools.partial(reduce.direct, 3, least=2)
    d3_near = functools.partial(reduce.direct, 3, most=1)
    blocks, parts = 2 * GROUPS, D // SLICE
    proj = Loop(GROUPS, project)
    mix = Loop(blocks, lambda n: branch.make(n, convolve))
    hid1 = Loop(blocks, from_spread(two, functools.partial(hidden, *chunks[0])))
    hid2, hid3 = (Loop(blocks, functools.partial(hidden, *chunk)) for chunk in chunks[1:])
    grad1, grad2 = (Loop(parts, functools.partial(grads, *chunk)) for chunk in chunks[:2])
    down3 = Loop(parts, functools.partial(down_grads, *chunks[2]))
    back2 = Loop(blocks, lambda n: down.make(n, second))
    gate3 = Loop(parts, functools.partial(gate_up_grads, *chunks[2]))
    ffn = Loop(blocks, forward)
    back_mix = Loop(blocks, from_spread(three, mix_back))
    back_conv = Loop(blocks, conv_back)
    grad0, grad4 = Loop(parts, conv_grads), Loop(parts, out_grads)
    back1 = Loop(blocks, lambda n: inputs.make(n, first))
    play(
        [
            start, send_own[0], send_own[4], exchange[0], exchange[4], first_norm, one.start, send_other[0],
            cuts[3], cuts[1], send_other[4], cuts[2], step[0][0], one.first, step[4][0], exchange[1], step[0][1],
            one.near, up_start, send_other[1], one.far, step[4][1], step[0][2], one.end, up.first, hold,
            send_own[1], proj[0], proj[1], proj[2], proj[3], step[4][2], halo, exchange[3], hold_end, send_own[3],
            halo_end, up.near, mix[0], mix[1], step[1][0], mix[2], mix[3], mix[4], send_own[2], mix[5], step[1][1],
            send_other[3], up.far, mix[6], mix[7], branch_end, exchange[2], second_norm, two.start, step[1][2],
            send_other[2], up.end, hid1[0], hid1[1], hid1[2], gather.crossed, hid1[3], hid1[4], hid1[5], step[2][0],
            hid1[6], hid1[7], two.sent, grad1[0], grad1[1], step[2][1], step[2][2], step[3][0], grad1[2], grad1[3],
            hid2[0], hid2[1], hid2[2], hid2[3], hid2[4], hid2[5], hid2[6], hid2[7], grad2[0], grad2[1], grad2[2],
            grad2[3], step[3][1], step[3][2], hid3[0], hid3[1], hid3[2], hid3[3], hid3[4], hid3[5], hid3[6],
            hid3[7], down3[0], gather.finish, down3[1], join_far[1], down3[2], down3[3], back2[0], back2[1],
            back2[2], back2[3], back2[4], back2[5], back2[6], back2[7], gate3[0], gate3[1], gate3[2], gate3[3],
            ffn[0], ffn[1], ffn[2], ffn[3], ffn[4], ffn[5], ffn[6], ffn[7], down_end, second_back, three.start,
            feed.push, back_mix[0], join_near[1], d3_far, back_mix[1], back_mix[2], back_mix[3], feed_pair[0],
            back_mix[4], join_far[2], feed_pair[1], back_mix[5], back_mix[6], back_mix[7], three.sent, halo_back,
            grad4[0], reload_end, grad4[1], grad4[2], grad4[3], feed_pair[2], back_conv[0], join_near[2],
            back_conv[1], back_conv[2], d3_near, feed.pass_on, final[1], join_far[3], back_conv[3], halo_back_end,
            back_conv[4], back_conv[5], back_conv[6], back_conv[7], grad0[0], grad0[1], grad0[2], grad0[3],
            feed.add_own, join_near[3], feed_end, feed_credit, back1[0], back1[1], back1[2], back1[3], back1[4],
            join_far[4], back1[5], join_near[4], join_far[0], final[2], back1[6], back1[7], final[4], join_near[0],
            inputs.end, first_back, gain_send[0], final[3], gain_add[0], gain_send[1], gain_add[1], gain_send[2],
            gain_add[2], gains_line, final[0], gains_end, end,
        ]
    )


class Loop:
    def __init__(self, count, body):
        self.count, self.body = count, body

    def __getitem__(self, n):
        return (self, n)


def play(order):
    order = list(order)
    while order:
        entry = order.pop(0)
        if not isinstance(entry, tuple):
            entry()
            continue
        loop, _ = entry
        between = {}
        for n in range(1, loop.count):
            between[n] = []
            while order[0] != (loop, n):
                between[n].append(order.pop(0))
            order.pop(0)

        def turn(n, _):
            for m, acts in between.items():
                if acts:

                    @pl.when(n == m)
                    def _():
                        play(acts)

            loop.body(n)
            return 0

        lax.fori_loop(0, loop.count, turn, 0)


def block_step(tok, cot, gains, weights, layers):
    rows, seg = weights.shape[0], tok.shape[0]
    count = len(WIDTHS)
    tokens = 2 * GROUPS * seg
    vmem, anywhere = pl.BlockSpec(memory_space=pltpu.VMEM), pl.BlockSpec(memory_space=pl.ANY)
    shape, scratch = jax.ShapeDtypeStruct, pltpu.VMEM
    dma, regular = pltpu.SemaphoreType.DMA, pltpu.SemaphoreType.REGULAR
    hops = layers - 1
    wide, biggest = sum(WIDTHS), max(WIDTHS)
    out_shape = [
        shape((seg, D), BF16),
        shape((seg, D), BF16),
        shape((8, 2 * GROUPS * WIDE), F32),
        shape((rows, wide), F32),
        shape((rows, wide), BF16),
        shape((tokens, D), BF16),
    ] + [shape((2, hops, 2 * rows, width), BF16) for width in WIDTHS]
    scratch_shapes = (
        [scratch((D, width), BF16) for width in WIDTHS]
        + [
            scratch((tokens, D), BF16),
            scratch((tokens, D), BF16),
            scratch((tokens, 2 * PAD_F), BF16),
            scratch((tokens, PAD_F), BF16),
            scratch((GROUPS, 8 + 2 * seg, WIDE), F32),
            scratch((GROUPS, 8 + 2 * seg, WIDE), F32),
            scratch((tokens, WIDE), BF16),
            scratch((seg, D), F32),
            scratch((seg, D), F32),
            scratch((seg, D), F32),
            scratch((4, seg, D), BF16),
            scratch((2, seg, D), BF16),
            scratch((seg, D), BF16),
        ]
        + [scratch((D, width), BF16) for width in WIDTHS[1:]]
        + [
            scratch((2 * rows, biggest), BF16),
            scratch((rows, biggest), F32),
            scratch((rows, GROUP_COLS - 4 * D), F32),
            scratch((rows, wide), BF16),
            scratch((8, WIDE), F32),
            scratch((3, 8, 2 * GROUPS * WIDE), F32),
            scratch((2, hops, 8, 2 * GROUPS * WIDE), F32),
            dma,
            dma((5,)),
            dma((count,)),
            dma((count,)),
            dma((count, 2, hops, 2)),
            dma((count, 2, hops, 2)),
            dma((4, 11)),
            dma((4, 11)),
            dma((4, 10)),
            dma((4, 10)),
            regular((3,)),
            dma((2,)),
            dma((2,)),
            dma((count, 2, hops)),
            dma((count, 2, hops)),
            dma,
            dma((4,)),
            dma((count,)),
            dma((count,)),
            dma((count,)),
            dma((3,)),
            dma((3,)),
            dma((2, hops)),
            dma((2, hops)),
        ]
    )
    return pl.pallas_call(
        functools.partial(block_kernel, layers, rows),
        out_shape=out_shape,
        in_specs=[vmem] * 3 + [anywhere],
        out_specs=[vmem] * 3 + [anywhere] * (3 + count),
        scratch_shapes=scratch_shapes,
        compiler_params=pltpu.CompilerParams(
            collective_id=0, has_side_effects=True, vmem_limit_bytes=VMEM_BYTES
        ),
        name="block_step",
    )(tok, cot, gains, weights)[:5]


def band(rows, most):
    return max(size for size in range(16, most + 1, 16) if rows % size == 0)


def adam_update(param, grad, first, second, rate, decay):
    first_new = MOMENT_DECAY * first + (1.0 - MOMENT_DECAY) * grad
    second_new = SQUARE_DECAY * second + (1.0 - SQUARE_DECAY) * grad * grad
    root = jnp.sqrt(second_new * (1.0 / (1.0 - SQUARE_DECAY**STEP))) + ADAM_EPSILON
    step = first_new * (rate / (1.0 - MOMENT_DECAY**STEP)) / root
    return (first_new, second_new, param * (1.0 - rate * decay) - step)


def update_kernel(
    inner_ref, mine_ref, theirs_ref, weights_ref, first_ref, second_ref, sums_ref, gains_ref, gains_first_ref,
    gains_second_ref, block_ref, input_ref, grad_out, first_out, second_out, weights_out, gains_grad_out,
    gains_first_out, gains_second_out, gains_out, block_out, input_out,
):
    is_low = inner_ref[0] == 0
    mine, theirs = mine_ref[...], theirs_ref[...].astype(F32)
    for half in (0, 1):
        chosen = jnp.where(is_low, mine, theirs) if half == 0 else jnp.where(is_low, theirs, mine)
        for first, own, width, _ in column_pieces(half):
            grad_out[:, first : first + width] = chosen[:, own : own + width]
    first_out[...], second_out[...], weights_out[...] = adam_update(
        weights_ref[...], grad_out[...], first_ref[...], second_ref[...], WEIGHT_RATE, WEIGHT_DECAY
    )

    @pl.when(pl.program_id(0) == 0)
    def _():
        gains_grad_out[0:2] = sums_ref[0:2, :D]
        for n in range(2 * GROUPS):
            gains_grad_out[2:5, n * HALF_Q : (n + 1) * HALF_Q] = sums_ref[2:5, n * WIDE : n * WIDE + HALF_Q]
        gains_first_out[...], gains_second_out[...], gains_out[...] = adam_update(
            gains_ref[...], gains_grad_out[...], gains_first_ref[...], gains_second_ref[...], GAIN_RATE, 0.0
        )
        block_out[...] = block_ref[...]
        input_out[...] = input_ref[...]


def update(inner, mine, theirs, weights, first, second, sums, gains, gains_first, gains_second, block, grad):
    rows, cols = weights.shape
    wide = mine.shape[1]
    size = band(rows, 32)
    by_row = lambda width: pl.BlockSpec((size, width), lambda n: (n, 0))
    whole = lambda values: pl.BlockSpec(values.shape, lambda n: (0, 0))
    shape = jax.ShapeDtypeStruct
    return pl.pallas_call(
        update_kernel,
        grid=(rows // size,),
        out_shape=[shape((rows, cols), F32)] * 4 + [shape(gains.shape, F32)] * 4 + [shape(block.shape, BF16)] * 2,
        in_specs=[pl.BlockSpec(memory_space=pltpu.SMEM)]
        + [by_row(wide)] * 2
        + [by_row(cols)] * 3
        + [whole(sums)]
        + [whole(gains)] * 3
        + [whole(block)] * 2,
        out_specs=[by_row(cols)] * 4 + [whole(gains)] * 4 + [whole(block)] * 2,
        compiler_params=pltpu.CompilerParams(vmem_limit_bytes=VMEM_BYTES),
        name="update",
    )(inner, mine, theirs, weights, first, second, sums, gains, gains_first, gains_second, block, grad)


def on_device(
    tokens, gains_taps, weights, cotangent, weight_first, weight_second, gains_first, gains_second
):
    layers = lax.axis_size("seq") // 2
    inner_word = (lax.axis_index("seq") % 2).astype(jnp.int32).reshape(1)
    block_out, input_grad, gain_sums, mine, theirs = block_step(
        tokens[0], cotangent[0], gains_taps, weights, layers
    )
    (
        weight_grad, weight_first_new, weight_second_new, weight_new,
        gains_grad, gains_first_new, gains_second_new, gains_new, block_out, input_grad,
    ) = update(
        inner_word, mine, theirs, weights, weight_first, weight_second,
        gain_sums, gains_taps, gains_first, gains_second, block_out, input_grad,
    )
    return (
        block_out[None],
        input_grad[None],
        weight_grad,
        weight_first_new,
        weight_second_new,
        weight_new,
        gains_grad,
        gains_first_new,
        gains_second_new,
        gains_new,
    )


def solution(mesh):
    tokens, rows, whole = P("shard", "seq", None), P("seq", "shard"), P()
    return jax.shard_map(
        on_device,
        mesh=mesh,
        in_specs=(tokens, whole, rows, tokens, rows, rows, whole, whole),
        out_specs=(tokens, tokens, rows, rows, rows, rows, whole, whole, whole, whole),
        check_vma=False,
    )
```

```python
import functools

import jax
import jax.numpy as jnp
from jax import lax
from jax.experimental import pallas as pl
from jax.experimental.pallas import tpu as pltpu
from jax.sharding import PartitionSpec as P

D = 1536
FF = 6912
STEP = 10
GROUPS = 4
QUARTER = D // GROUPS
UNITS = FF // GROUPS
GROUP_COLS = 4 * QUARTER + 3 * UNITS
HALF_Q = QUARTER // 2
HALF_F = UNITS // 2
LANES = 128
PAD_F = -(-HALF_F // LANES) * LANES
WIDE = 256
CONV_COLS = 4 * HALF_Q
UNIT_CHUNKS = (384, 256, PAD_F - 640)
UNIT_STARTS = (0, 384, 640)
WIDTHS = (CONV_COLS,) + tuple(3 * units for units in UNIT_CHUNKS)
STARTS = tuple(sum(WIDTHS[:k]) for k in range(len(WIDTHS)))
SPREAD_SPLITS = (208, 208, 64, 128)
COLLECT_SPLITS = (128, 128, 112, 112)
REACH = (1, 1, 1, 1)
CUT_FIRST = 1
SLICE = 384
TILE = 16
ROWS = 48

MOMENT_DECAY = 0.9
SQUARE_DECAY = 0.95
ADAM_EPSILON = 1e-08
NORM_EPSILON = 1e-05
WEIGHT_RATE = 0.02
GAIN_RATE = 0.2
WEIGHT_DECAY = 0.1

BF16 = jnp.bfloat16
F32 = jnp.float32
MESH = pl.DeviceIdType.MESH
VMEM_BYTES = 63 * 1024 * 1024


def place():
    seq, shard = lax.axis_index("seq"), lax.axis_index("shard")
    inner, core = lax.rem(seq, 2), lax.rem(shard, 2)
    return seq, shard, inner, core


def partners():
    seq, shard, inner, core = place()
    across = {"seq": seq + 1 - 2 * inner, "shard": shard}
    beside = {"seq": seq, "shard": lax.rem(shard + 2, 4)}
    twin = {"seq": seq, "shard": shard + 1 - 2 * core}
    return across, beside, twin


def remote(src, dst, send, recv, device):
    return pltpu.make_async_remote_copy(
        src_ref=src, dst_ref=dst, send_sem=send, recv_sem=recv, device_id=device, device_id_type=MESH
    )


def line():
    seq, shard, _, _ = place()
    size = lax.axis_size("seq")
    return seq // 2, lambda steps: {"seq": lax.rem(seq + 2 * steps + size, size), "shard": shard}


def greet(layers):
    outer, at = line()
    barrier = pltpu.get_barrier_semaphore()
    for device in partners():
        pl.semaphore_signal(barrier, inc=1, device_id=device, device_id_type=MESH)
    for steps in range(1, layers):
        for sign in (1, -1):

            @pl.when(in_line(outer + sign * steps, layers))
            def _():
                pl.semaphore_signal(barrier, inc=1, device_id=at(sign * steps), device_id_type=MESH)


def greeted(layers):
    pl.semaphore_wait(pltpu.get_barrier_semaphore(), 3 + layers - 1)


def in_line(index, layers):
    return (index >= 0) & (index < layers)


def allow(credit):
    for device in partners():
        pl.semaphore_signal(credit, inc=1, device_id=device, device_id_type=MESH)


def dot(left, right):
    return jnp.dot(left, right, preferred_element_type=F32)


def dot_rows(left, right):
    return lax.dot_general(left, right, (((1,), (1,)), ((), ())), preferred_element_type=F32)


def dot_columns(left, right):
    return lax.dot_general(left, right, (((0,), (0,)), ((), ())), preferred_element_type=F32)


def aligned(start, size, multiple=16):
    return pl.ds(pl.multiple_of(start, multiple), size)


class Gather:
    def __init__(self, layers, rows, oth, outs, send_x, recv_x, send_z, recv_z):
        self.layers, self.rows, self.oth, self.outs = layers, rows, oth, outs
        self.send_x, self.recv_x, self.send_z, self.recv_z = send_x, recv_x, send_z, recv_z
        self.seq, _, self.inner, _ = place()
        self.outer, self.at = line()
        self.across = partners()[0]

    def seq_rows(self, index):
        return aligned(index * self.rows, self.rows)

    def layer_rows(self, direction, distance):
        origin = self.outer - distance if direction == 0 else self.outer + distance
        return aligned(origin * 2 * self.rows, 2 * self.rows)

    def copy(self, k, src, dst, direction, distance, hop, piece):
        slot = (k, direction, distance + hop - 1, piece)
        return remote(
            src, dst, self.send_z.at[slot], self.recv_z.at[slot], self.at(hop if direction == 0 else -hop)
        )

    def goes(self, direction, hop):
        return in_line(self.outer + (hop if direction == 0 else -hop), self.layers)

    def has_come(self, direction, distance):
        return in_line(self.outer + (-distance if direction == 0 else distance), self.layers)

    def hops(self, k, distance):
        return range(1, min(REACH[k], self.layers - 1 - distance) + 1)

    def own_copy(self, k, direction, hop):
        here = self.outs[k].at[self.seq_rows(self.seq)]
        return self.copy(k, here, here, direction, 0, hop, 0)

    def other_copy(self, k, direction, hop):
        there = self.outs[k].at[self.seq_rows(self.seq + 1 - 2 * self.inner)]
        return self.copy(k, there, there, direction, 0, hop, 1)

    def pass_copy(self, k, direction, distance, hop):
        ref = self.outs[k].at[self.layer_rows(direction, distance)]
        return self.copy(k, ref, ref, direction, distance, hop, 0)

    def other_rows(self, k):
        return self.oth.at[pl.ds(k * self.rows, self.rows), pl.ds(0, WIDTHS[k])]

    def exchange(self, k):
        self.x_copy(k).start()

    def x_copy(self, k):
        here = self.outs[k].at[self.seq_rows(self.seq)]
        return remote(self.other_rows(k), here, self.send_x.at[k], self.recv_x.at[k], self.across)

    def crossed(self):
        for k in range(len(self.outs)):
            self.x_copy(k).wait_send()

    def send_own(self, k):
        for hop in self.hops(k, 0):
            for direction in (0, 1):

                @pl.when(self.goes(direction, hop))
                def _():
                    self.own_copy(k, direction, hop).start()

    def send_other(self, k):
        self.x_copy(k).wait_recv()
        for hop in self.hops(k, 0):
            for direction in (0, 1):

                @pl.when(self.goes(direction, hop))
                def _():
                    self.other_copy(k, direction, hop).start()

    def step(self, k, distance):
        for direction in (0, 1):

            @pl.when(self.has_come(direction, distance))
            def _():
                if distance <= REACH[k]:
                    origin = self.outer - distance if direction == 0 else self.outer + distance
                    for piece in (0, 1):
                        index = 2 * origin + (self.inner if piece == 0 else 1 - self.inner)
                        ref = self.outs[k].at[self.seq_rows(index)]
                        self.copy(k, ref, ref, direction, distance - 1, 1, piece).wait_recv()
                else:
                    ref = self.outs[k].at[self.layer_rows(direction, distance)]
                    self.copy(k, ref, ref, direction, distance - 1, 1, 0).wait_recv()
                if distance % REACH[k] == 0:
                    for hop in self.hops(k, distance):

                        @pl.when(self.goes(direction, hop))
                        def _():
                            self.pass_copy(k, direction, distance, hop).start()

    def steps(self, k, first, last=None):
        last = self.layers - 1 if last is None else min(last, self.layers - 1)
        for distance in range(first, last + 1):
            self.step(k, distance)

    def finish(self):
        for k in range(len(self.outs)):
            for distance in range(0, self.layers - 1, REACH[k]):
                for hop in self.hops(k, distance):
                    for direction in (0, 1):

                        @pl.when(self.goes(direction, hop) & self.has_come(direction, distance))
                        def _():
                            if distance == 0:
                                self.own_copy(k, direction, hop).wait_send()
                                self.other_copy(k, direction, hop).wait_send()
                            else:
                                self.pass_copy(k, direction, distance, hop).wait_send()


class Reduce:
    def __init__(self, layers, rows, grads, slots, stage, spare, total, outgoing, mine, theirs, sems):
        self.layers, self.rows, self.grads, self.slots = layers, rows, grads, slots
        self.stage, self.spare, self.total, self.outgoing = stage, spare, total, outgoing
        self.mine, self.theirs = mine, theirs
        self.send_g, self.recv_g, self.fetched, self.fetches, self.stored, self.send_o, self.recv_o = sems
        _, _, self.inner, _ = place()
        self.outer, self.at = line()
        self.across = partners()[0]

    def owner(self, direction, distance):
        return self.outer + distance if direction == 0 else self.outer - distance

    def upstream(self, direction, steps):
        return in_line(self.outer - steps if direction == 0 else self.outer + steps, self.layers)

    def block(self, k, owner):
        return self.grads[k].at[aligned(owner * 2 * self.rows, 2 * self.rows), pl.ds(0, WIDTHS[k])]

    def copy(self, k, src, direction, distance):
        slot = (direction, distance - 1)
        return remote(
            src,
            self.slots[k].at[slot],
            self.send_g.at[(k,) + slot],
            self.recv_g.at[(k,) + slot],
            self.at(1 if direction == 0 else -1),
        )

    def send(self, k, direction, distance):
        self.copy(k, self.block(k, self.owner(direction, distance)), direction, distance).start()

    def direct(self, k, part=None, least=1, most=None):
        for distance in range(most or self.layers - 1, least - 1, -1):
            for direction in (0, 1):
                owner = self.owner(direction, distance)
                here = in_line(owner, self.layers) & jnp.logical_not(self.upstream(direction, 1))
                if part is not None:
                    here = here & (owner * 2 * self.rows // SLICE == part)

                @pl.when(here)
                def _():
                    self.send(k, direction, distance)

    def fetch(self, k, direction, distance):
        slot = self.slots[k].at[direction, distance - 1]
        self.copy(k, slot, direction, distance).wait_recv()
        held = self.stage.at[:, pl.ds(0, WIDTHS[k])]
        copy = pltpu.make_async_copy(slot, held, self.fetched)
        copy.start()
        copy.wait()

    def tiles(self, body):
        def step(n, _):
            body(aligned(n * TILE, TILE))
            return 0

        lax.fori_loop(0, 2 * self.rows // TILE, step, 0)

    def join(self, k, most, least):
        cols = pl.ds(0, WIDTHS[k])
        for distance in range(most, least - 1, -1):
            for direction in (0, 1):
                owner = self.owner(direction, distance)

                @pl.when(in_line(owner, self.layers) & self.upstream(direction, 1))
                def _():
                    def add(tile):
                        base = self.owner(direction, distance) * 2 * self.rows
                        rows = pl.ds(pl.multiple_of(base + tile.start, 16), TILE)
                        ref = self.grads[k]
                        ref[rows, cols] = (
                            ref[rows, cols].astype(F32) + self.stage[tile, cols].astype(F32)
                        ).astype(BF16)

                    self.fetch(k, direction, distance + 1)
                    self.tiles(add)
                    self.send(k, direction, distance)

    def final(self, k, before=None):
        cols = pl.ds(0, WIDTHS[k])
        came = [(1, 0), (1, 1)]

        def fetch(n, distance, direction):
            return pltpu.make_async_copy(
                self.slots[k].at[direction, distance - 1],
                self.spare.at[pl.ds(n * 2 * self.rows, 2 * self.rows), cols],
                self.fetches.at[n],
            )

        for n, (distance, direction) in enumerate(came):

            @pl.when(self.upstream(direction, distance))
            def _():
                self.copy(k, self.slots[k].at[direction, distance - 1], direction, distance).wait_recv()
                fetch(n, distance, direction).start()

        if before is not None:
            self.store(before).wait()

        here, there = self.inner * self.rows, (1 - self.inner) * self.rows

        def each(base, body):
            def step(n, _):
                body(base + n * TILE, n * TILE)
                return 0

            lax.fori_loop(0, self.rows // TILE, step, 0)

        for n, (distance, direction) in enumerate(came):

            @pl.when(self.upstream(direction, distance))
            def _():
                fetch(n, distance, direction).wait()

        def add_up(flags):
            def total(rows):
                value = self.grads[k][aligned(self.outer * 2 * self.rows + rows, TILE), cols].astype(F32)
                for n, flag in enumerate(flags):
                    if flag:
                        value = value + self.spare[aligned(n * 2 * self.rows + rows, TILE), cols].astype(F32)
                return value

            def send(rows, at):
                self.outgoing[aligned(at, TILE), pl.ds(STARTS[k], WIDTHS[k])] = total(rows).astype(BF16)

            def keep(rows, at):
                self.total[aligned(at, TILE), cols] = total(rows)

            each(there, send)
            self.over(k).start()
            each(here, keep)
            self.store(k).start()

        patterns = {}
        for place_in_line in range(self.layers):
            flags = tuple(
                0 <= (place_in_line - distance if direction == 0 else place_in_line + distance) < self.layers
                for distance, direction in came
            )
            patterns.setdefault(flags, []).append(place_in_line)
        for flags, places in patterns.items():
            here_now = functools.reduce(jnp.logical_or, [self.outer == p for p in places])

            @pl.when(here_now)
            def _():
                add_up(flags)

    def over(self, k):
        wide = pl.ds(STARTS[k], WIDTHS[k])
        return remote(
            self.outgoing.at[:, wide], self.theirs.at[:, wide], self.send_o.at[k], self.recv_o.at[k], self.across
        )

    def store(self, k):
        return pltpu.make_async_copy(
            self.total.at[:, pl.ds(0, WIDTHS[k])], self.mine.at[:, pl.ds(STARTS[k], WIDTHS[k])], self.stored.at[k]
        )

    def wait_sent(self, k):
        for distance in range(1, self.layers):
            for direction in (0, 1):
                owner = self.owner(direction, distance)

                @pl.when(in_line(owner, self.layers))
                def _():
                    self.copy(k, self.block(k, owner), direction, distance).wait_send()

    def finish(self, before):
        self.store(before).wait()
        for k in range(len(self.grads)):
            self.over(k).wait()


class Spread:
    slots = range(11)

    def __init__(self, buf, seg, split, send, recv):
        self.buf, self.seg, self.split, self.send, self.recv = buf, seg, split, send, recv

    def index(self, n):
        _, shard, inner, core = place()
        row, flip, other = (n // 2) % 2, n // 4, n % 2
        return 2 * (lax.rem(shard + 2 * row, 4) + other * (1 - 2 * core)) + inner + flip * (1 - 2 * inner)

    def copy(self, slot):
        across, beside, twin = partners()
        low, high, whole = (0, self.split), (self.split, self.seg - self.split), (0, self.seg)
        n, (first, size), device = {
            0: (0, low, across),
            9: (0, high, across),
            1: (0, high, beside),
            10: (0, low, beside),
            2: (0, whole, twin),
            3: (4, low, beside),
            4: (4, whole, twin),
            5: (2, high, across),
            6: (2, whole, twin),
            7: (6, low, twin),
            8: (6, high, twin),
        }[slot]
        ref = self.buf.at[aligned(self.index(n) * self.seg + first, size)]
        return remote(ref, ref, self.send.at[slot], self.recv.at[slot], device)

    def push(self, *slots):
        for slot in slots:
            self.copy(slot).start()

    def came(self, *slots):
        for slot in slots:
            self.copy(slot).wait_recv()

    def start(self):
        self.push(0, 1, 9, 10, 2)

    def first(self):
        self.came(1)
        self.push(5)
        self.came(0)
        self.push(3)

    def near(self):
        self.came(10)
        self.push(6)
        self.came(9)
        self.push(4)

    def far(self):
        self.came(3)
        self.push(7)
        self.came(5)
        self.push(8)

    def sent(self):
        for slot in self.slots:
            self.copy(slot).wait_send()

    def end(self):
        self.came(2, 4, 6, 7, 8)
        self.sent()

    def before(self, n):
        return {
            1: (lambda: self.came(2),),
            2: (self.first, self.near),
            3: (lambda: self.came(6),),
            5: (lambda: self.came(4),),
            6: (self.far,),
            7: (lambda: self.came(7, 8),),
        }.get(n, ())


class Collect:
    def __init__(self, part, seg, split, total, pair, near, joined, send, recv):
        self.part, self.seg, self.total = part, seg, total
        self.pair, self.near, self.joined, self.send, self.recv = pair, near, joined, send, recv
        _, self.shard, self.inner, core = place()
        self.twin_shard = self.shard + 1 - 2 * core
        self.low, self.high, self.whole = (0, split), (split, seg - split), (0, seg)
        self.cols = pl.ds(0, D)

    def index(self, s, k):
        row, flip = 1 - k % 2, 1 - k // 2
        return 2 * lax.rem(s + 2 * row, 4) + self.inner + flip * (1 - 2 * self.inner)

    def pair_copy(self, k):
        src = self.part.at[aligned(self.index(self.twin_shard, k) * self.seg, self.seg), self.cols]
        return remote(src, self.pair.at[k], self.send.at[k], self.recv.at[k], partners()[2])

    def copy(self, slot):
        across, beside, _ = partners()
        src, dst, (first, size), device = {
            4: (self.pair.at[0], self.joined, self.low, across),
            5: (self.pair.at[0], self.joined, self.high, beside),
            6: (self.pair.at[1], self.near.at[0], self.low, across),
            7: (self.pair.at[2], self.near.at[1], self.high, beside),
            8: (self.pair.at[2], self.near.at[1], self.low, beside),
            9: (self.pair.at[1], self.near.at[0], self.high, across),
        }[slot]
        rows = pl.ds(first, size)
        return remote(src.at[rows], dst.at[rows], self.send.at[slot], self.recv.at[slot], device)

    def over(self, span, body):
        def step(n, _):
            body(aligned(span[0] + n * 16, 16))
            return 0

        lax.fori_loop(0, span[1] // 16, step, 0)

    def mine(self, k, rows):
        return self.part[aligned(self.index(self.shard, k) * self.seg + rows.start, 16), self.cols].astype(F32)

    def add_pair(self, k):
        def add(rows):
            self.pair[k, rows] = (self.mine(k, rows) + self.pair[k, rows].astype(F32)).astype(BF16)

        self.pair_copy(k).wait_recv()
        self.over(self.whole, add)
        for slot in ((4, 5), (6,), (7,))[k]:
            self.copy(slot).start()

    def add_own(self):
        def add(rows):
            self.total[rows] = self.mine(3, rows) + self.pair[3, rows].astype(F32)

        self.pair_copy(3).wait_recv()
        self.over(self.whole, add)

    def pass_on(self):
        for slot, k, span, after in ((4, 2, self.low, 8), (5, 1, self.high, 9)):

            def add(rows):
                self.pair[k, rows] = (self.pair[k, rows].astype(F32) + self.joined[rows].astype(F32)).astype(BF16)

            self.copy(slot).wait_recv()
            self.over(span, add)
            self.copy(after).start()

    def push(self):
        for k in range(4):
            self.pair_copy(k).start()

    def make(self, n, produce):
        k, own = n // 2, n % 2
        produce(self.index(jnp.where(own == 1, self.shard, self.twin_shard), k))

        @pl.when(own == 0)
        def _():
            self.pair_copy(k).start()

        for m in range(3):

            @pl.when(n == 2 * m + 1)
            def _():
                self.add_pair(m)
                if m == 2:
                    self.pass_on()

        pl.when(n == 7)(self.add_own)

    def end(self):
        def add(rows):
            near = self.near[0, rows].astype(F32) + self.near[1, rows].astype(F32)
            self.total[rows] = self.total[rows] + near

        for slots, span in (((6, 8), self.low), ((7, 9), self.high)):
            for slot in slots:
                self.copy(slot).wait_recv()
            self.over(span, add)
        for k in range(4):
            self.pair_copy(k).wait_send()
        for slot in range(4, 10):
            self.copy(slot).wait_send()


def norm_scale(values):
    return lax.rsqrt(jnp.mean(values * values, axis=-1, keepdims=True) + NORM_EPSILON)


def by_rows(rows, body, carry=0):
    def step(n, carry):
        return body(aligned(n * ROWS, ROWS), carry)

    return lax.fori_loop(0, rows // ROWS, step, carry)


def norm_back(values, gain, upstream):
    scale = norm_scale(values)
    scaled = gain * upstream
    inner = jnp.mean(scaled * values, axis=-1, keepdims=True)
    return (
        scale * scaled - values * scale * scale * scale * inner,
        jnp.sum(upstream * values * scale, axis=0, keepdims=True),
    )


REFS = (
    "tok", "cot", "gains", "weights",
    "block_out", "input_grad", "gain_sums", "mine", "theirs", "n1_held", "slot0", "slot1", "slot2", "slot3",
    "w0", "w1", "w2", "w3", "seq_a", "seq_b", "du", "act", "c_all", "gated", "mixed", "resid", "dresid", "total",
    "pair", "near", "joined", "g1", "g2", "g3", "stage", "sum", "tail", "outgoing", "tap_sums", "gain_in", "gain_line",
    "held", "loaded", "send_x", "recv_x", "send_z", "recv_z", "send_s", "recv_s", "send_c", "recv_c", "credit",
    "halo_send", "halo_recv", "send_g", "recv_g", "fetched", "fetches", "stored", "send_o", "recv_o",
    "send_a", "recv_a", "send_l", "recv_l",
)


def column_pieces(half):
    pieces = [(m * QUARTER + half * HALF_Q, m * HALF_Q, HALF_Q, 0) for m in range(4)]
    for k, (start, units) in enumerate(zip(UNIT_STARTS, UNIT_CHUNKS), 1):
        real = min(units, HALF_F - start)
        for m in range(3):
            first = 4 * QUARTER + m * UNITS + half * HALF_F + start
            pieces.append((first, STARTS[k] + m * units, real, units - real))
    return pieces


def block_kernel(layers, rows, *all_refs):
    r = dict(zip(REFS, all_refs, strict=True))
    tok, cot, gains = r["tok"], r["cot"], r["gains"]
    seq_a, seq_b, du, act = r["seq_a"], r["seq_b"], r["du"], r["act"]
    c_all, gated, mixed, total = r["c_all"], r["gated"], r["mixed"], r["total"]
    weights = (r["w0"], r["w1"], r["w2"], r["w3"])
    seg = tok.shape[0]
    _, shard, inner, _ = place()
    outer, at = line()
    me = 2 * shard + inner
    my_rows = aligned(me * seg, seg)
    chunks = list(zip(range(1, 1 + len(UNIT_CHUNKS)), UNIT_STARTS, UNIT_CHUNKS))
    gather = Gather(
        layers, rows, r["g1"], weights, r["send_x"], r["recv_x"], r["send_z"], r["recv_z"]
    )
    reduce = Reduce(
        layers, rows, (r["w2"], r["g1"], r["g2"], r["g3"]), (r["slot0"], r["slot1"], r["slot2"], r["slot3"]),
        r["stage"], r["w1"], r["sum"], r["outgoing"], r["mine"], r["theirs"],
        (r["send_g"], r["recv_g"], r["fetched"], r["fetches"], r["stored"], r["send_o"], r["recv_o"]),
    )

    def spread(buf, n):
        return Spread(buf, seg, SPREAD_SPLITS[n], r["send_s"].at[n], r["recv_s"].at[n])

    def collect(part, n):
        sems = r["send_c"].at[n], r["recv_c"].at[n]
        return Collect(part, seg, COLLECT_SPLITS[n], total, r["pair"], r["near"], r["joined"], *sems)

    one, up, two, three = spread(seq_a, 0), spread(seq_b, 1), spread(seq_a, 2), spread(seq_a, 3)
    branch, down, feed, inputs = collect(seq_a, 0), collect(seq_b, 1), collect(du, 2), collect(seq_a, 3)
    lanes = lax.broadcasted_iota(jnp.int32, (seg, WIDE), 1) < HALF_Q
    taps = pltpu.roll(gains[...], lax.rem(D - shard * QUARTER - inner * HALF_Q, D), 1)[2:5, :WIDE]
    kept = pl.ds(D, WIDE)
    sums, tap_sums = r["gain_sums"], r["tap_sums"]

    def block(t):
        return aligned(t * seg, seg)

    def mine(part):
        return pl.ds(pl.multiple_of(me * seg + part.start, 16), part.size)

    def first_norm():
        def rows(part, _):
            values = tok[part].astype(F32)
            seq_a[mine(part)] = (values * norm_scale(values) * gains[0:1, :]).astype(BF16)
            return 0

        by_rows(seg, rows)

    def up_start():
        seq_b[my_rows] = cot[...]
        up.start()

    def held():
        return pltpu.make_async_copy(seq_a, r["n1_held"], r["held"])

    def reload():
        return pltpu.make_async_copy(r["n1_held"], seq_b, r["held"])

    def project(s):
        for i in (0, 1):
            parts = dot(seq_a[block(2 * s + i)], weights[0][...])
            b = jnp.where(lanes, parts[:, :WIDE], 0.0)
            c = pltpu.roll(parts[:, 128 : 128 + 384], 384 - 64, 1)[:, :WIDE]
            x = parts[:, 384 : 384 + WIDE]
            c_all[s, pl.ds(i * seg, seg)] = jnp.where(lanes, c, 0.0)
            gated[s, pl.ds(8 + i * seg, seg)] = (b * x).astype(BF16).astype(F32)

    def ahead():
        return remote(
            gated.at[:, pl.ds(2 * seg, 8)], gated.at[:, pl.ds(0, 8)], r["halo_send"].at[0], r["halo_recv"].at[0], at(1)
        )

    def halo():
        pl.when(outer < layers - 1)(lambda: ahead().start())

        @pl.when(outer == 0)
        def _():
            gated[:, pl.ds(0, 8)] = jnp.zeros((GROUPS, 8, WIDE), F32)

    def convolved(s, i):
        return (
            taps[0:1, :] * gated[s, pl.ds(6 + i * seg, seg)]
            + taps[1:2, :] * gated[s, pl.ds(7 + i * seg, seg)]
            + taps[2:3, :] * gated[s, pl.ds(8 + i * seg, seg)]
        )

    def convolve(t):
        for i in (0, 1):

            @pl.when(t % 2 == i)
            def _():
                s = t // 2
                mixed[block(t)] = pltpu.roll(c_all[s, pl.ds(i * seg, seg)] * convolved(s, i), 64, 1).astype(BF16)

        seq_a[block(t)] = dot_rows(mixed[block(t)], weights[0][:, pl.ds(512, WIDE)]).astype(BF16)

    def branch_end():
        branch.end()
        allow(r["credit"].at[0])

    def second_norm():
        def rows(part, _):
            values = tok[part].astype(F32) + total[part]
            r["resid"][part] = values
            seq_a[mine(part)] = (values * norm_scale(values) * gains[1:2, :]).astype(BF16)
            return 0

        by_rows(seg, rows)
        pl.semaphore_wait(r["credit"].at[0], 3)

    def hidden(k, start, units, t):
        ref, here = weights[k], block(t)
        gate = dot(seq_a[here], ref[:, pl.ds(0, units)])
        upval = dot(seq_a[here], ref[:, pl.ds(units, units)])
        dact = dot(seq_b[here], ref[:, pl.ds(2 * units, units)])
        sigma = jax.nn.sigmoid(gate)
        silu = gate * sigma
        act[here, pl.ds(start, units)] = (silu * upval).astype(BF16)
        dgate = dact * upval * sigma * (1.0 + gate * (1.0 - sigma))
        du[here, pl.ds(2 * start, units)] = dgate.astype(BF16)
        du[here, pl.ds(2 * start + units, units)] = (dact * silu).astype(BF16)

    def slice_of(n):
        return jnp.where(outer < layers // 2, D // SLICE - 1 - n, n)

    def gate_up_grads(k, start, units, n):
        part = slice_of(n)
        left = seq_a[:, aligned(part * SLICE, SLICE, 128)]
        reduce.grads[k][aligned(part * SLICE, SLICE), pl.ds(0, 2 * units)] = dot_columns(
            left, du[:, pl.ds(2 * start, 2 * units)]
        ).astype(BF16)

    def down_grads(k, start, units, n):
        part = slice_of(n)
        left = seq_b[:, aligned(part * SLICE, SLICE, 128)]
        reduce.grads[k][aligned(part * SLICE, SLICE), pl.ds(2 * units, units)] = dot_columns(
            left, act[:, pl.ds(start, units)]
        ).astype(BF16)

    def grads(k, start, units, n):
        gate_up_grads(k, start, units, n)
        down_grads(k, start, units, n)
        reduce.direct(k, slice_of(n))

    def second(t):
        here = block(t)
        seq_b[here] = sum(
            dot_rows(du[here, pl.ds(2 * start, 2 * units)], weights[k][:, pl.ds(0, 2 * units)])
            for k, start, units in chunks
        ).astype(BF16)

    def down_end():
        down.end()
        reload().start()
        allow(r["credit"].at[1])

    def forward(t):
        here = block(t)
        du[here, pl.ds(0, D)] = sum(
            dot_rows(act[here, pl.ds(start, units)], weights[k][:, pl.ds(2 * units, units)])
            for k, start, units in chunks
        ).astype(BF16)

    def second_back():
        def rows(part, gain):
            dpart, dgain = norm_back(r["resid"][part], gains[1:2, :], total[part])
            dresid = cot[part].astype(F32) + dpart
            r["dresid"][part] = dresid
            seq_a[mine(part)] = dresid.astype(BF16)
            return gain + dgain

        sums[...] = jnp.zeros(sums.shape, F32)
        tap_sums[...] = jnp.zeros(tap_sums.shape, F32)
        sums[1:2, pl.ds(0, D)] = by_rows(seg, rows, jnp.zeros((1, D), F32))
        pl.semaphore_wait(r["credit"].at[1], 3)

    def mix_back(t):
        s, here = t // 2, block(t)
        dmixed = pltpu.roll(dot(seq_a[here], weights[0][:, pl.ds(512, WIDE)]), WIDE - 64, 1)
        dmixed = jnp.where(lanes, dmixed, 0.0)
        for i in (0, 1):

            @pl.when(t % 2 == i)
            def _():
                du[here, kept] = (dmixed * convolved(s, i)).astype(BF16)
                c_all[s, pl.ds(i * seg, seg)] = dmixed * c_all[s, pl.ds(i * seg, seg)]

    def after():
        return remote(
            c_all.at[:, pl.ds(0, 8)], c_all.at[:, pl.ds(2 * seg, 8)], r["halo_send"].at[1], r["halo_recv"].at[1], at(-1)
        )

    def halo_back():
        pl.when(outer > 0)(lambda: after().start())

        @pl.when(outer == layers - 1)
        def _():
            c_all[:, pl.ds(2 * seg, 8)] = jnp.zeros((GROUPS, 8, WIDE), F32)

    def conv_back(n):
        for i in (0, 1):
            pl.when(n // GROUPS == i)(functools.partial(conv_back_half, n % GROUPS, i))

    def conv_back_half(s, i):
        t = block(2 * s + i)
        dconv = c_all[s, pl.ds(i * seg, seg)]
        dgated = (
            taps[2:3, :] * dconv
            + taps[1:2, :] * c_all[s, pl.ds(1 + i * seg, seg)]
            + taps[0:1, :] * c_all[s, pl.ds(2 + i * seg, seg)]
        )
        parts = dot(seq_b[t], weights[0][:, pl.ds(0, 640)])
        db = dgated * parts[:, 384:640]
        dx = dgated * parts[:, :WIDE]
        dc = jnp.concatenate([du[t, kept].astype(F32), jnp.zeros((seg, 128), F32)], axis=1)
        dc = pltpu.roll(dc, 64, 1)
        act[t, pl.ds(0, 128)] = db[:, :128].astype(BF16)
        act[t, pl.ds(128, 128)] = (db[:, 128:] + dc[:, :128]).astype(BF16)
        act[t, pl.ds(256, 128)] = dc[:, 128:256].astype(BF16)
        act[t, pl.ds(384, WIDE)] = dx.astype(BF16)
        act[t, pl.ds(640, 128)] = jnp.zeros((seg, 128), BF16)
        for k in range(3):
            moved = gated[s, pl.ds(6 + k + i * seg, seg)]
            tap_sums[k : k + 1] = tap_sums[k : k + 1] + jnp.sum(dconv * moved, axis=0, keepdims=True)

    def conv_grads(n):
        part = slice_of(n)
        held_rows, cols = aligned(part * SLICE, SLICE), aligned(part * SLICE, SLICE, 128)
        ref = reduce.grads[0]
        of_parts = dot_columns(seq_b[:, cols], act[:, pl.ds(0, CONV_COLS)])
        ref[held_rows, pl.ds(0, 512)] = of_parts[:, :512].astype(BF16)
        of_mixed = dot_columns(seq_a[:, cols], mixed[...])
        ref[held_rows, pl.ds(512, WIDE)] = (of_parts[:, 512:] + of_mixed).astype(BF16)
        reduce.direct(0, part)

    def feed_end():
        feed.end()
        allow(r["credit"].at[2])
        r["block_out"][...] = (r["resid"][...] + total[...]).astype(BF16)

    def first(t):
        here = block(t)
        seq_a[here] = dot_rows(act[here, pl.ds(0, 640)], weights[0][:, pl.ds(0, 640)]).astype(BF16)

    def first_back():
        def rows(part, gain):
            dpart, dgain = norm_back(tok[part].astype(F32), gains[0:1, :], total[part])
            r["input_grad"][part] = (r["dresid"][part] + dpart).astype(BF16)
            return gain + dgain

        sums[0:1, pl.ds(0, D)] = by_rows(seg, rows, jnp.zeros((1, D), F32))
        sums[2:5, aligned(me * WIDE, WIDE, 128)] = tap_sums[0:3]

    def gains_across(n):
        return remote(sums, r["gain_in"].at[n], r["send_a"].at[n], r["recv_a"].at[n], partners()[n])

    def gains_add(n):
        gains_across(n).wait()
        sums[...] = sums[...] + r["gain_in"][n]

    def line_copy(sign, steps):
        slot = (0 if sign > 0 else 1, steps - 1)
        return remote(
            sums, r["gain_line"].at[slot], r["send_l"].at[slot], r["recv_l"].at[slot], at(sign * steps)
        )

    def gains_line():
        for steps in range(1, layers):
            for sign in (1, -1):
                pl.when(in_line(outer + sign * steps, layers))(line_copy(sign, steps).start)

    def gains_end():
        for steps in range(1, layers):
            for sign in (1, -1):
                pl.when(in_line(outer + sign * steps, layers))(line_copy(sign, steps).wait_send)
                pl.when(in_line(outer - sign * steps, layers))(line_copy(sign, steps).wait_recv)

        own_sums = sums[...]
        for origin in range(layers):
            for steps in range(1, layers):
                for sign in (1, -1):

                    @pl.when((outer - sign * steps == origin))
                    def _():
                        came = r["gain_line"][0 if sign > 0 else 1, steps - 1]
                        sums[...] = came if origin == 0 else sums[...] + came

            if origin > 0:

                @pl.when(outer == origin)
                def _():
                    sums[...] = sums[...] + own_sums

    def end():
        reduce.finish(0)
        for k in range(len(WIDTHS)):
            reduce.wait_sent(k)
        pl.when(outer < layers - 1)(lambda: ahead().wait_send())
        pl.when(outer > 0)(lambda: after().wait_send())

    windows = [
        (r["resid"], 0, D), (r["dresid"], D, D), (total, 2 * D, D), (r["resid"], 3 * D, D),
        (r["tail"], 4 * D, GROUP_COLS - 4 * D),
    ]

    def load(n):
        ref, first, width = windows[n]
        return pltpu.make_async_copy(
            r["weights"].at[:, pl.ds(first, width)], ref.at[pl.ds(0, rows)], r["loaded"].at[n]
        )

    def start():
        for n in (0, 1, 2, 4):
            load(n).start()
        greet(layers)
        load(0).wait()
        cut(0)
        load(3).start()
        greeted(layers)

    def cut(k):
        def read(part, first, width):
            found = []
            for n, (ref, low, size) in enumerate(windows):
                start, stop = max(first, low), min(first + width, low + size)
                if start < stop and (n == 0) == (k == 0):
                    found.append(ref[part, start - low : stop - low])
            return found

        def band(n, _):
            part = aligned(n * 16, 16)
            halves = []
            for half in (0, 1):
                pieces = []
                for first, own, width, padding in column_pieces(half):
                    if STARTS[k] <= own < STARTS[k] + WIDTHS[k]:
                        pieces += read(part, first, width)
                        if padding:
                            pieces.append(jnp.zeros((16, padding), F32))
                halves.append(jnp.concatenate(pieces, axis=1))
            is_low = inner == 0
            seq = lax.axis_index("seq")
            own_rows = aligned(seq * rows + n * 16, 16)
            weights[k][own_rows, :] = jnp.where(is_low, halves[0], halves[1]).astype(BF16)
            gather.other_rows(k)[part, :] = jnp.where(is_low, halves[1], halves[0]).astype(BF16)
            return 0

        for n in (1, 2, 3, 4) if k == CUT_FIRST else ():
            load(n).wait()
        lax.fori_loop(0, rows // 16, band, 0)

    def hold():
        held().start()

    def hold_end():
        held().wait()

    def halo_end():
        pl.when(outer > 0)(lambda: ahead().wait_recv())

    def reload_end():
        reload().wait()

    def halo_back_end():
        pl.when(outer < layers - 1)(lambda: after().wait_recv())

    def feed_credit():
        pl.semaphore_wait(r["credit"].at[2], 3)

    def from_spread(moved, body):
        def step(n):
            for m in range(8):
                if moved.before(m):

                    @pl.when(n == m)
                    def _():
                        for act in moved.before(m):
                            act()

            body(moved.index(n))

        return step

    def each(body, *cases):
        return [functools.partial(body, *(case if isinstance(case, tuple) else (case,))) for case in cases]

    every = range(len(WIDTHS))
    cuts = each(cut, *every)
    exchange, send_own, send_other = (
        each(body, *every) for body in (gather.exchange, gather.send_own, gather.send_other)
    )
    step = [each(gather.steps, (k, 1, 1), (k, 2, 2), (k, 3)) for k in every]
    join_far = each(reduce.join, *((k, layers - 2, 2) for k in every))
    join_near = each(reduce.join, *((k, 1, 1) for k in every))
    final = each(reduce.final, (0, 3), 1, (2, 1), (3, 2))
    feed_pair = each(feed.add_pair, 0, 1, 2)
    gain_send = [lambda n=n: gains_across(n).start() for n in range(3)]
    gain_add = each(gains_add, 0, 1, 2)
    d3_far = functools.partial(reduce.direct, 3, least=2)
    d3_near = functools.partial(reduce.direct, 3, most=1)
    blocks, parts = 2 * GROUPS, D // SLICE
    proj = Loop(GROUPS, project)
    mix = Loop(blocks, lambda n: branch.make(n, convolve))
    hid1 = Loop(blocks, from_spread(two, functools.partial(hidden, *chunks[0])))
    hid2, hid3 = (Loop(blocks, functools.partial(hidden, *chunk)) for chunk in chunks[1:])
    grad1, grad2 = (Loop(parts, functools.partial(grads, *chunk)) for chunk in chunks[:2])
    down3 = Loop(parts // 2, lambda n: [down_grads(*chunks[2], 2 * n + m) for m in (0, 1)])
    back2 = Loop(blocks, lambda n: down.make(n, second))
    gate3 = Loop(parts // 2, lambda n: [gate_up_grads(*chunks[2], 2 * n + m) for m in (0, 1)])
    ffn = Loop(blocks, forward)
    back_mix = Loop(blocks, from_spread(three, mix_back))
    back_conv = Loop(blocks, conv_back)
    grad0 = Loop(parts // 2, lambda n: [conv_grads(2 * n + m) for m in (0, 1)])
    back1 = Loop(blocks, lambda n: inputs.make(n, first))
    play(
        [
            start, send_own[0], exchange[0], cuts[1], first_norm, one.start, exchange[1], send_other[0], step[0][0],
            cuts[3], one.first, cuts[2], step[0][1], up_start, send_own[1], one.near, one.far, step[0][2], one.end,
            hold, proj[0], proj[1], exchange[3], hold_end, proj[2], proj[3], up.first, halo, exchange[2],
            send_other[1], halo_end, mix[0], step[1][0], mix[1], up.near, mix[2], mix[3], mix[4], up.far, up.end,
            mix[5], send_other[2], step[1][1], mix[6], send_own[2], mix[7], branch_end, second_norm, two.start,
            step[1][2], send_own[3], hid1[0], hid1[1], hid1[2], hid1[3], send_other[3], step[2][0], hid1[4],
            hid1[5], hid1[6], hid1[7], two.sent, gather.crossed, grad1[0], grad1[1], step[2][1], grad1[2],
            step[2][2], grad1[3], hid2[0], hid2[1], hid2[2], hid2[3], step[3][0], hid2[4], hid2[5], hid2[6],
            hid2[7], join_far[1], grad2[0], grad2[1], grad2[2], grad2[3], step[3][1], step[3][2], hid3[0], hid3[1],
            hid3[2], hid3[3], hid3[4], hid3[5], hid3[6], hid3[7], down3[0], down3[1], back2[0],
            back2[1], back2[2], back2[3], back2[4], back2[5], back2[6], back2[7], gate3[0], join_near[1],
            join_far[2], gate3[1], gather.finish, down_end, second_back, three.start, ffn[0],
            ffn[1], ffn[2], ffn[3], ffn[4], ffn[5], ffn[6], ffn[7], back_mix[0], d3_far, back_mix[1], feed.push,
            join_near[2], back_mix[2], back_mix[3], reload_end, feed_pair[0], back_mix[4], feed_pair[1],
            back_mix[5], back_mix[6], feed_pair[2], back_mix[7], three.sent, halo_back, back_conv[0], back_conv[1],
            back_conv[2], d3_near, back_conv[3], feed.pass_on, join_far[3], feed.add_own, final[1], halo_back_end,
            back_conv[4], back_conv[5], back_conv[6], join_near[3], back_conv[7], grad0[0], grad0[1],
            feed_end, feed_credit, back1[0], back1[1], back1[2], back1[3], back1[4], join_far[0],
            back1[5], back1[6], final[2], back1[7], join_near[0], inputs.end, first_back, gain_send[0], final[3],
            gain_add[0], gain_send[1], gain_add[1], gain_send[2], gain_add[2], gains_line, final[0], gains_end, end,
        ]
    )


class Loop:
    def __init__(self, count, body):
        self.count, self.body = count, body

    def __getitem__(self, n):
        return (self, n)


def play(order):
    order = list(order)
    while order:
        entry = order.pop(0)
        if not isinstance(entry, tuple):
            entry()
            continue
        loop, _ = entry
        between = {}
        for n in range(1, loop.count):
            between[n] = []
            while order[0] != (loop, n):
                between[n].append(order.pop(0))
            order.pop(0)

        def turn(n, _):
            for m, acts in between.items():
                if acts:

                    @pl.when(n == m)
                    def _():
                        play(acts)

            loop.body(n)
            return 0

        lax.fori_loop(0, loop.count, turn, 0)


def block_step(tok, cot, gains, weights, layers):
    rows, seg = weights.shape[0], tok.shape[0]
    count = len(WIDTHS)
    tokens = 2 * GROUPS * seg
    vmem, anywhere = pl.BlockSpec(memory_space=pltpu.VMEM), pl.BlockSpec(memory_space=pl.ANY)
    shape, scratch = jax.ShapeDtypeStruct, pltpu.VMEM
    dma, regular = pltpu.SemaphoreType.DMA, pltpu.SemaphoreType.REGULAR
    hops = layers - 1
    wide, biggest = sum(WIDTHS), max(WIDTHS)
    out_shape = [
        shape((seg, D), BF16),
        shape((seg, D), BF16),
        shape((8, 2 * GROUPS * WIDE), F32),
        shape((rows, wide), F32),
        shape((rows, wide), BF16),
        shape((tokens, D), BF16),
    ] + [shape((2, hops, 2 * rows, width), BF16) for width in WIDTHS]
    scratch_shapes = (
        [scratch((D, width), BF16) for width in WIDTHS]
        + [
            scratch((tokens, D), BF16),
            scratch((tokens, D), BF16),
            scratch((tokens, 2 * PAD_F), BF16),
            scratch((tokens, PAD_F), BF16),
            scratch((GROUPS, 8 + 2 * seg, WIDE), F32),
            scratch((GROUPS, 8 + 2 * seg, WIDE), F32),
            scratch((tokens, WIDE), BF16),
            scratch((seg, D), F32),
            scratch((seg, D), F32),
            scratch((seg, D), F32),
            scratch((4, seg, D), BF16),
            scratch((2, seg, D), BF16),
            scratch((seg, D), BF16),
        ]
        + [scratch((D, width), BF16) for width in WIDTHS[1:]]
        + [
            scratch((2 * rows, biggest), BF16),
            scratch((rows, biggest), F32),
            scratch((rows, GROUP_COLS - 4 * D), F32),
            scratch((rows, wide), BF16),
            scratch((8, WIDE), F32),
            scratch((3, 8, 2 * GROUPS * WIDE), F32),
            scratch((2, hops, 8, 2 * GROUPS * WIDE), F32),
            dma,
            dma((5,)),
            dma((count,)),
            dma((count,)),
            dma((count, 2, hops, 2)),
            dma((count, 2, hops, 2)),
            dma((4, 11)),
            dma((4, 11)),
            dma((4, 10)),
            dma((4, 10)),
            regular((3,)),
            dma((2,)),
            dma((2,)),
            dma((count, 2, hops)),
            dma((count, 2, hops)),
            dma,
            dma((4,)),
            dma((count,)),
            dma((count,)),
            dma((count,)),
            dma((3,)),
            dma((3,)),
            dma((2, hops)),
            dma((2, hops)),
        ]
    )
    return pl.pallas_call(
        functools.partial(block_kernel, layers, rows),
        out_shape=out_shape,
        in_specs=[vmem] * 3 + [anywhere],
        out_specs=[vmem] * 3 + [anywhere] * (3 + count),
        scratch_shapes=scratch_shapes,
        compiler_params=pltpu.CompilerParams(
            collective_id=0, has_side_effects=True, vmem_limit_bytes=VMEM_BYTES
        ),
        name="block_step",
    )(tok, cot, gains, weights)[:5]


def band(rows, most):
    return max(size for size in range(16, most + 1, 16) if rows % size == 0)


def adam_update(param, grad, first, second, rate, decay):
    first_new = MOMENT_DECAY * first + (1.0 - MOMENT_DECAY) * grad
    second_new = SQUARE_DECAY * second + (1.0 - SQUARE_DECAY) * grad * grad
    root = jnp.sqrt(second_new * (1.0 / (1.0 - SQUARE_DECAY**STEP))) + ADAM_EPSILON
    step = first_new * (rate / (1.0 - MOMENT_DECAY**STEP)) / root
    return (first_new, second_new, param * (1.0 - rate * decay) - step)


def update_kernel(
    inner_ref, mine_ref, theirs_ref, weights_ref, first_ref, second_ref, sums_ref, gains_ref, gains_first_ref,
    gains_second_ref, block_ref, input_ref, grad_out, first_out, second_out, weights_out, gains_grad_out,
    gains_first_out, gains_second_out, gains_out, block_out, input_out,
):
    is_low = inner_ref[0] == 0
    mine, theirs = mine_ref[...], theirs_ref[...].astype(F32)
    for half in (0, 1):
        chosen = jnp.where(is_low, mine, theirs) if half == 0 else jnp.where(is_low, theirs, mine)
        for first, own, width, _ in column_pieces(half):
            grad_out[:, first : first + width] = chosen[:, own : own + width]
    first_out[...], second_out[...], weights_out[...] = adam_update(
        weights_ref[...], grad_out[...], first_ref[...], second_ref[...], WEIGHT_RATE, WEIGHT_DECAY
    )

    @pl.when(pl.program_id(0) == 0)
    def _():
        gains_grad_out[0:2] = sums_ref[0:2, :D]
        for n in range(2 * GROUPS):
            gains_grad_out[2:5, n * HALF_Q : (n + 1) * HALF_Q] = sums_ref[2:5, n * WIDE : n * WIDE + HALF_Q]
        gains_first_out[...], gains_second_out[...], gains_out[...] = adam_update(
            gains_ref[...], gains_grad_out[...], gains_first_ref[...], gains_second_ref[...], GAIN_RATE, 0.0
        )
        block_out[...] = block_ref[...]
        input_out[...] = input_ref[...]


def update(inner, mine, theirs, weights, first, second, sums, gains, gains_first, gains_second, block, grad):
    rows, cols = weights.shape
    wide = mine.shape[1]
    size = band(rows, 32)
    by_row = lambda width: pl.BlockSpec((size, width), lambda n: (n, 0))
    whole = lambda values: pl.BlockSpec(values.shape, lambda n: (0, 0))
    shape = jax.ShapeDtypeStruct
    return pl.pallas_call(
        update_kernel,
        grid=(rows // size,),
        out_shape=[shape((rows, cols), F32)] * 4 + [shape(gains.shape, F32)] * 4 + [shape(block.shape, BF16)] * 2,
        in_specs=[pl.BlockSpec(memory_space=pltpu.SMEM)]
        + [by_row(wide)] * 2
        + [by_row(cols)] * 3
        + [whole(sums)]
        + [whole(gains)] * 3
        + [whole(block)] * 2,
        out_specs=[by_row(cols)] * 4 + [whole(gains)] * 4 + [whole(block)] * 2,
        compiler_params=pltpu.CompilerParams(vmem_limit_bytes=VMEM_BYTES),
        name="update",
    )(inner, mine, theirs, weights, first, second, sums, gains, gains_first, gains_second, block, grad)


def on_device(
    tokens, gains_taps, weights, cotangent, weight_first, weight_second, gains_first, gains_second
):
    layers = lax.axis_size("seq") // 2
    inner_word = (lax.axis_index("seq") % 2).astype(jnp.int32).reshape(1)
    block_out, input_grad, gain_sums, mine, theirs = block_step(
        tokens[0], cotangent[0], gains_taps, weights, layers
    )
    (
        weight_grad, weight_first_new, weight_second_new, weight_new,
        gains_grad, gains_first_new, gains_second_new, gains_new, block_out, input_grad,
    ) = update(
        inner_word, mine, theirs, weights, weight_first, weight_second,
        gain_sums, gains_taps, gains_first, gains_second, block_out, input_grad,
    )
    return (
        block_out[None],
        input_grad[None],
        weight_grad,
        weight_first_new,
        weight_second_new,
        weight_new,
        gains_grad,
        gains_first_new,
        gains_second_new,
        gains_new,
    )


def solution(mesh):
    tokens, rows, whole = P("shard", "seq", None), P("seq", "shard"), P()
    return jax.shard_map(
        on_device,
        mesh=mesh,
        in_specs=(tokens, whole, rows, tokens, rows, rows, whole, whole),
        out_specs=(tokens, tokens, rows, rows, rows, rows, whole, whole, whole, whole),
        check_vma=False,
    )
```

```python
import functools

import jax
import jax.numpy as jnp
from jax import lax
from jax.experimental import pallas as pl
from jax.experimental.pallas import tpu as pltpu
from jax.sharding import PartitionSpec as P

D = 1536
FF = 6912
STEP = 10
GROUPS = 4
QUARTER = D // GROUPS
UNITS = FF // GROUPS
GROUP_COLS = 4 * QUARTER + 3 * UNITS
HALF_Q = QUARTER // 2
HALF_F = UNITS // 2
LANES = 128
PAD_F = -(-HALF_F // LANES) * LANES
WIDE = 256
CONV_COLS = 4 * HALF_Q
UNIT_CHUNKS = (384, 256, PAD_F - 640)
UNIT_STARTS = (0, 384, 640)
WIDTHS = (CONV_COLS,) + tuple(3 * units for units in UNIT_CHUNKS)
STARTS = tuple(sum(WIDTHS[:k]) for k in range(len(WIDTHS)))
SPREAD_SPLITS = (208, 144, 112, 112)
COLLECT_SPLITS = (64, 128, 48, 112)
REACH = (1, 1, 1, 1)
CUT_FIRST = 1
SLICE = 384
TILE = 16
ROWS = 48

MOMENT_DECAY = 0.9
SQUARE_DECAY = 0.95
ADAM_EPSILON = 1e-08
NORM_EPSILON = 1e-05
WEIGHT_RATE = 0.02
GAIN_RATE = 0.2
WEIGHT_DECAY = 0.1

BF16 = jnp.bfloat16
F32 = jnp.float32
MESH = pl.DeviceIdType.MESH
VMEM_BYTES = 63 * 1024 * 1024


def place():
    seq, shard = lax.axis_index("seq"), lax.axis_index("shard")
    inner, core = lax.rem(seq, 2), lax.rem(shard, 2)
    return seq, shard, inner, core


def partners():
    seq, shard, inner, core = place()
    across = {"seq": seq + 1 - 2 * inner, "shard": shard}
    beside = {"seq": seq, "shard": lax.rem(shard + 2, 4)}
    twin = {"seq": seq, "shard": shard + 1 - 2 * core}
    return across, beside, twin


def remote(src, dst, send, recv, device):
    return pltpu.make_async_remote_copy(
        src_ref=src, dst_ref=dst, send_sem=send, recv_sem=recv, device_id=device, device_id_type=MESH
    )


def line():
    seq, shard, _, _ = place()
    size = lax.axis_size("seq")
    return seq // 2, lambda steps: {"seq": lax.rem(seq + 2 * steps + size, size), "shard": shard}


def greet(layers):
    outer, at = line()
    barrier = pltpu.get_barrier_semaphore()
    for device in partners():
        pl.semaphore_signal(barrier, inc=1, device_id=device, device_id_type=MESH)
    for steps in range(1, layers):
        for sign in (1, -1):

            @pl.when(in_line(outer + sign * steps, layers))
            def _():
                pl.semaphore_signal(barrier, inc=1, device_id=at(sign * steps), device_id_type=MESH)


def greeted(layers):
    pl.semaphore_wait(pltpu.get_barrier_semaphore(), 3 + layers - 1)


def in_line(index, layers):
    return (index >= 0) & (index < layers)


def allow(credit):
    for device in partners():
        pl.semaphore_signal(credit, inc=1, device_id=device, device_id_type=MESH)


def dot(left, right):
    return jnp.dot(left, right, preferred_element_type=F32)


def dot_rows(left, right):
    return lax.dot_general(left, right, (((1,), (1,)), ((), ())), preferred_element_type=F32)


def dot_columns(left, right):
    return lax.dot_general(left, right, (((0,), (0,)), ((), ())), preferred_element_type=F32)


def aligned(start, size, multiple=16):
    return pl.ds(pl.multiple_of(start, multiple), size)


class Gather:
    def __init__(self, layers, rows, oth, outs, send_x, recv_x, send_z, recv_z):
        self.layers, self.rows, self.oth, self.outs = layers, rows, oth, outs
        self.send_x, self.recv_x, self.send_z, self.recv_z = send_x, recv_x, send_z, recv_z
        self.seq, _, self.inner, _ = place()
        self.outer, self.at = line()
        self.across = partners()[0]

    def seq_rows(self, index):
        return aligned(index * self.rows, self.rows)

    def layer_rows(self, direction, distance):
        origin = self.outer - distance if direction == 0 else self.outer + distance
        return aligned(origin * 2 * self.rows, 2 * self.rows)

    def copy(self, k, src, dst, direction, distance, hop, piece):
        slot = (k, direction, distance + hop - 1, piece)
        return remote(
            src, dst, self.send_z.at[slot], self.recv_z.at[slot], self.at(hop if direction == 0 else -hop)
        )

    def goes(self, direction, hop):
        return in_line(self.outer + (hop if direction == 0 else -hop), self.layers)

    def has_come(self, direction, distance):
        return in_line(self.outer + (-distance if direction == 0 else distance), self.layers)

    def hops(self, k, distance):
        return range(1, min(REACH[k], self.layers - 1 - distance) + 1)

    def own_copy(self, k, direction, hop):
        here = self.outs[k].at[self.seq_rows(self.seq)]
        return self.copy(k, here, here, direction, 0, hop, 0)

    def other_copy(self, k, direction, hop):
        there = self.outs[k].at[self.seq_rows(self.seq + 1 - 2 * self.inner)]
        return self.copy(k, there, there, direction, 0, hop, 1)

    def pass_copy(self, k, direction, distance, hop):
        ref = self.outs[k].at[self.layer_rows(direction, distance)]
        return self.copy(k, ref, ref, direction, distance, hop, 0)

    def other_rows(self, k):
        return self.oth.at[pl.ds(k * self.rows, self.rows), pl.ds(0, WIDTHS[k])]

    def exchange(self, k):
        self.x_copy(k).start()

    def x_copy(self, k):
        here = self.outs[k].at[self.seq_rows(self.seq)]
        return remote(self.other_rows(k), here, self.send_x.at[k], self.recv_x.at[k], self.across)

    def crossed(self):
        for k in range(len(self.outs)):
            self.x_copy(k).wait_send()

    def send_own(self, k):
        for hop in self.hops(k, 0):
            for direction in (0, 1):

                @pl.when(self.goes(direction, hop))
                def _():
                    self.own_copy(k, direction, hop).start()

    def send_other(self, k):
        self.x_copy(k).wait_recv()
        for hop in self.hops(k, 0):
            for direction in (0, 1):

                @pl.when(self.goes(direction, hop))
                def _():
                    self.other_copy(k, direction, hop).start()

    def step(self, k, distance):
        for direction in (0, 1):

            @pl.when(self.has_come(direction, distance))
            def _():
                if distance <= REACH[k]:
                    origin = self.outer - distance if direction == 0 else self.outer + distance
                    for piece in (0, 1):
                        index = 2 * origin + (self.inner if piece == 0 else 1 - self.inner)
                        ref = self.outs[k].at[self.seq_rows(index)]
                        self.copy(k, ref, ref, direction, distance - 1, 1, piece).wait_recv()
                else:
                    ref = self.outs[k].at[self.layer_rows(direction, distance)]
                    self.copy(k, ref, ref, direction, distance - 1, 1, 0).wait_recv()
                if distance % REACH[k] == 0:
                    for hop in self.hops(k, distance):

                        @pl.when(self.goes(direction, hop))
                        def _():
                            self.pass_copy(k, direction, distance, hop).start()

    def steps(self, k, first, last=None):
        last = self.layers - 1 if last is None else min(last, self.layers - 1)
        for distance in range(first, last + 1):
            self.step(k, distance)

    def finish(self):
        for k in range(len(self.outs)):
            for distance in range(0, self.layers - 1, REACH[k]):
                for hop in self.hops(k, distance):
                    for direction in (0, 1):

                        @pl.when(self.goes(direction, hop) & self.has_come(direction, distance))
                        def _():
                            if distance == 0:
                                self.own_copy(k, direction, hop).wait_send()
                                self.other_copy(k, direction, hop).wait_send()
                            else:
                                self.pass_copy(k, direction, distance, hop).wait_send()


class Reduce:
    def __init__(self, layers, rows, grads, slots, stage, spare, total, outgoing, mine, theirs, sems):
        self.layers, self.rows, self.grads, self.slots = layers, rows, grads, slots
        self.stage, self.spare, self.total, self.outgoing = stage, spare, total, outgoing
        self.mine, self.theirs = mine, theirs
        self.send_g, self.recv_g, self.fetched, self.fetches, self.stored, self.send_o, self.recv_o = sems
        _, _, self.inner, _ = place()
        self.outer, self.at = line()
        self.across = partners()[0]

    def owner(self, direction, distance):
        return self.outer + distance if direction == 0 else self.outer - distance

    def upstream(self, direction, steps):
        return in_line(self.outer - steps if direction == 0 else self.outer + steps, self.layers)

    def block(self, k, owner):
        return self.grads[k].at[aligned(owner * 2 * self.rows, 2 * self.rows), pl.ds(0, WIDTHS[k])]

    def copy(self, k, src, direction, distance):
        slot = (direction, distance - 1)
        return remote(
            src,
            self.slots[k].at[slot],
            self.send_g.at[(k,) + slot],
            self.recv_g.at[(k,) + slot],
            self.at(1 if direction == 0 else -1),
        )

    def send(self, k, direction, distance):
        self.copy(k, self.block(k, self.owner(direction, distance)), direction, distance).start()

    def direct(self, k, part=None, least=1, most=None):
        for distance in range(most or self.layers - 1, least - 1, -1):
            for direction in (0, 1):
                owner = self.owner(direction, distance)
                here = in_line(owner, self.layers) & jnp.logical_not(self.upstream(direction, 1))
                if part is not None:
                    here = here & (owner * 2 * self.rows // SLICE == part)

                @pl.when(here)
                def _():
                    self.send(k, direction, distance)

    def fetch(self, k, direction, distance):
        slot = self.slots[k].at[direction, distance - 1]
        self.copy(k, slot, direction, distance).wait_recv()
        held = self.stage.at[:, pl.ds(0, WIDTHS[k])]
        copy = pltpu.make_async_copy(slot, held, self.fetched)
        copy.start()
        copy.wait()

    def tiles(self, body):
        def step(n, _):
            body(aligned(n * TILE, TILE))
            return 0

        lax.fori_loop(0, 2 * self.rows // TILE, step, 0)

    def join(self, k, most, least):
        cols = pl.ds(0, WIDTHS[k])
        for distance in range(most, least - 1, -1):
            for direction in (0, 1):
                owner = self.owner(direction, distance)

                @pl.when(in_line(owner, self.layers) & self.upstream(direction, 1))
                def _():
                    def add(tile):
                        base = self.owner(direction, distance) * 2 * self.rows
                        rows = pl.ds(pl.multiple_of(base + tile.start, 16), TILE)
                        ref = self.grads[k]
                        ref[rows, cols] = (
                            ref[rows, cols].astype(F32) + self.stage[tile, cols].astype(F32)
                        ).astype(BF16)

                    self.fetch(k, direction, distance + 1)
                    self.tiles(add)
                    self.send(k, direction, distance)

    def final(self, k, before=None):
        cols = pl.ds(0, WIDTHS[k])
        came = [(1, 0), (1, 1)]

        def fetch(n, distance, direction):
            return pltpu.make_async_copy(
                self.slots[k].at[direction, distance - 1],
                self.spare.at[pl.ds(n * 2 * self.rows, 2 * self.rows), cols],
                self.fetches.at[n],
            )

        for n, (distance, direction) in enumerate(came):

            @pl.when(self.upstream(direction, distance))
            def _():
                self.copy(k, self.slots[k].at[direction, distance - 1], direction, distance).wait_recv()
                fetch(n, distance, direction).start()

        if before is not None:
            self.store(before).wait()

        here, there = self.inner * self.rows, (1 - self.inner) * self.rows

        def each(base, body):
            def step(n, _):
                body(base + n * TILE, n * TILE)
                return 0

            lax.fori_loop(0, self.rows // TILE, step, 0)

        for n, (distance, direction) in enumerate(came):

            @pl.when(self.upstream(direction, distance))
            def _():
                fetch(n, distance, direction).wait()

        def add_up(flags):
            def total(rows):
                value = self.grads[k][aligned(self.outer * 2 * self.rows + rows, TILE), cols].astype(F32)
                for n, flag in enumerate(flags):
                    if flag:
                        value = value + self.spare[aligned(n * 2 * self.rows + rows, TILE), cols].astype(F32)
                return value

            def send(rows, at):
                self.outgoing[aligned(at, TILE), pl.ds(STARTS[k], WIDTHS[k])] = total(rows).astype(BF16)

            def keep(rows, at):
                self.total[aligned(at, TILE), cols] = total(rows)

            each(there, send)
            self.over(k).start()
            each(here, keep)
            self.store(k).start()

        patterns = {}
        for place_in_line in range(self.layers):
            flags = tuple(
                0 <= (place_in_line - distance if direction == 0 else place_in_line + distance) < self.layers
                for distance, direction in came
            )
            patterns.setdefault(flags, []).append(place_in_line)
        for flags, places in patterns.items():
            here_now = functools.reduce(jnp.logical_or, [self.outer == p for p in places])

            @pl.when(here_now)
            def _():
                add_up(flags)

    def over(self, k):
        wide = pl.ds(STARTS[k], WIDTHS[k])
        return remote(
            self.outgoing.at[:, wide], self.theirs.at[:, wide], self.send_o.at[k], self.recv_o.at[k], self.across
        )

    def store(self, k):
        return pltpu.make_async_copy(
            self.total.at[:, pl.ds(0, WIDTHS[k])], self.mine.at[:, pl.ds(STARTS[k], WIDTHS[k])], self.stored.at[k]
        )

    def wait_sent(self, k):
        for distance in range(1, self.layers):
            for direction in (0, 1):
                owner = self.owner(direction, distance)

                @pl.when(in_line(owner, self.layers))
                def _():
                    self.copy(k, self.block(k, owner), direction, distance).wait_send()

    def finish(self, before):
        self.store(before).wait()
        for k in range(len(self.grads)):
            self.over(k).wait()


class Spread:
    slots = range(11)

    def __init__(self, buf, seg, split, send, recv):
        self.buf, self.seg, self.split, self.send, self.recv = buf, seg, split, send, recv

    def index(self, n):
        _, shard, inner, core = place()
        row, flip, other = (n // 2) % 2, n // 4, n % 2
        return 2 * (lax.rem(shard + 2 * row, 4) + other * (1 - 2 * core)) + inner + flip * (1 - 2 * inner)

    def copy(self, slot):
        across, beside, twin = partners()
        low, high, whole = (0, self.split), (self.split, self.seg - self.split), (0, self.seg)
        n, (first, size), device = {
            0: (0, low, across),
            9: (0, high, across),
            1: (0, high, beside),
            10: (0, low, beside),
            2: (0, whole, twin),
            3: (4, low, beside),
            4: (4, whole, twin),
            5: (2, high, across),
            6: (2, whole, twin),
            7: (6, low, twin),
            8: (6, high, twin),
        }[slot]
        ref = self.buf.at[aligned(self.index(n) * self.seg + first, size)]
        return remote(ref, ref, self.send.at[slot], self.recv.at[slot], device)

    def push(self, *slots):
        for slot in slots:
            self.copy(slot).start()

    def came(self, *slots):
        for slot in slots:
            self.copy(slot).wait_recv()

    def start(self):
        self.push(0, 1, 9, 10, 2)

    def first(self):
        self.came(1)
        self.push(5)
        self.came(0)
        self.push(3)

    def near(self):
        self.came(10)
        self.push(6)
        self.came(9)
        self.push(4)

    def far(self):
        self.came(3)
        self.push(7)
        self.came(5)
        self.push(8)

    def sent(self):
        for slot in self.slots:
            self.copy(slot).wait_send()

    def end(self):
        self.came(2, 4, 6, 7, 8)
        self.sent()

    def before(self, n):
        return {
            1: (lambda: self.came(2),),
            2: (self.first, self.near),
            3: (lambda: self.came(6),),
            5: (lambda: self.came(4),),
            6: (self.far,),
            7: (lambda: self.came(7, 8),),
        }.get(n, ())


class Collect:
    def __init__(self, part, seg, split, total, pair, near, joined, send, recv):
        self.part, self.seg, self.total = part, seg, total
        self.pair, self.near, self.joined, self.send, self.recv = pair, near, joined, send, recv
        _, self.shard, self.inner, core = place()
        self.twin_shard = self.shard + 1 - 2 * core
        self.low, self.high, self.whole = (0, split), (split, seg - split), (0, seg)
        self.cols = pl.ds(0, D)

    def index(self, s, k):
        row, flip = 1 - k % 2, 1 - k // 2
        return 2 * lax.rem(s + 2 * row, 4) + self.inner + flip * (1 - 2 * self.inner)

    def pair_copy(self, k):
        src = self.part.at[aligned(self.index(self.twin_shard, k) * self.seg, self.seg), self.cols]
        return remote(src, self.pair.at[k], self.send.at[k], self.recv.at[k], partners()[2])

    def copy(self, slot):
        across, beside, _ = partners()
        src, dst, (first, size), device = {
            4: (self.pair.at[0], self.joined, self.low, across),
            5: (self.pair.at[0], self.joined, self.high, beside),
            6: (self.pair.at[1], self.near.at[0], self.low, across),
            7: (self.pair.at[2], self.near.at[1], self.high, beside),
            8: (self.pair.at[2], self.near.at[1], self.low, beside),
            9: (self.pair.at[1], self.near.at[0], self.high, across),
        }[slot]
        rows = pl.ds(first, size)
        return remote(src.at[rows], dst.at[rows], self.send.at[slot], self.recv.at[slot], device)

    def over(self, span, body):
        def step(n, _):
            body(aligned(span[0] + n * 16, 16))
            return 0

        lax.fori_loop(0, span[1] // 16, step, 0)

    def mine(self, k, rows):
        return self.part[aligned(self.index(self.shard, k) * self.seg + rows.start, 16), self.cols].astype(F32)

    def add_pair(self, k):
        def add(rows):
            self.pair[k, rows] = (self.mine(k, rows) + self.pair[k, rows].astype(F32)).astype(BF16)

        self.pair_copy(k).wait_recv()
        self.over(self.whole, add)
        for slot in ((4, 5), (6,), (7,))[k]:
            self.copy(slot).start()

    def add_own(self):
        def add(rows):
            self.total[rows] = self.mine(3, rows) + self.pair[3, rows].astype(F32)

        self.pair_copy(3).wait_recv()
        self.over(self.whole, add)

    def pass_on(self):
        for slot, k, span, after in ((4, 2, self.low, 8), (5, 1, self.high, 9)):

            def add(rows):
                self.pair[k, rows] = (self.pair[k, rows].astype(F32) + self.joined[rows].astype(F32)).astype(BF16)

            self.copy(slot).wait_recv()
            self.over(span, add)
            self.copy(after).start()

    def push(self):
        for k in range(4):
            self.pair_copy(k).start()

    def make(self, n, produce):
        k, own = n // 2, n % 2
        produce(self.index(jnp.where(own == 1, self.shard, self.twin_shard), k))

        @pl.when(own == 0)
        def _():
            self.pair_copy(k).start()

        for m in range(3):

            @pl.when(n == 2 * m + 1)
            def _():
                self.add_pair(m)
                if m == 2:
                    self.pass_on()

        pl.when(n == 7)(self.add_own)

    def end(self):
        def add(rows):
            near = self.near[0, rows].astype(F32) + self.near[1, rows].astype(F32)
            self.total[rows] = self.total[rows] + near

        for slots, span in (((6, 8), self.low), ((7, 9), self.high)):
            for slot in slots:
                self.copy(slot).wait_recv()
            self.over(span, add)
        for k in range(4):
            self.pair_copy(k).wait_send()
        for slot in range(4, 10):
            self.copy(slot).wait_send()


def norm_scale(values):
    return lax.rsqrt(jnp.mean(values * values, axis=-1, keepdims=True) + NORM_EPSILON)


def by_rows(rows, body, carry=0):
    def step(n, carry):
        return body(aligned(n * ROWS, ROWS), carry)

    return lax.fori_loop(0, rows // ROWS, step, carry)


def norm_back(values, gain, upstream):
    scale = norm_scale(values)
    scaled = gain * upstream
    inner = jnp.mean(scaled * values, axis=-1, keepdims=True)
    return (
        scale * scaled - values * scale * scale * scale * inner,
        jnp.sum(upstream * values * scale, axis=0, keepdims=True),
    )


REFS = (
    "tok", "cot", "gains", "weights",
    "block_out", "input_grad", "gain_sums", "mine", "theirs", "n1_held", "slot0", "slot1", "slot2", "slot3",
    "w0", "w1", "w2", "w3", "seq_a", "seq_b", "du", "act", "c_all", "gated", "mixed", "resid", "dresid", "total",
    "pair", "near", "joined", "g1", "g2", "g3", "stage", "sum", "tail", "outgoing", "tap_sums", "gain_in", "gain_line",
    "held", "loaded", "send_x", "recv_x", "send_z", "recv_z", "send_s", "recv_s", "send_c", "recv_c", "credit",
    "halo_send", "halo_recv", "send_g", "recv_g", "fetched", "fetches", "stored", "send_o", "recv_o",
    "send_a", "recv_a", "send_l", "recv_l",
)


def column_pieces(half):
    pieces = [(m * QUARTER + half * HALF_Q, m * HALF_Q, HALF_Q, 0) for m in range(4)]
    for k, (start, units) in enumerate(zip(UNIT_STARTS, UNIT_CHUNKS), 1):
        real = min(units, HALF_F - start)
        for m in range(3):
            first = 4 * QUARTER + m * UNITS + half * HALF_F + start
            pieces.append((first, STARTS[k] + m * units, real, units - real))
    return pieces


def block_kernel(layers, rows, *all_refs):
    r = dict(zip(REFS, all_refs, strict=True))
    tok, cot, gains = r["tok"], r["cot"], r["gains"]
    seq_a, seq_b, du, act = r["seq_a"], r["seq_b"], r["du"], r["act"]
    c_all, gated, mixed, total = r["c_all"], r["gated"], r["mixed"], r["total"]
    weights = (r["w0"], r["w1"], r["w2"], r["w3"])
    seg = tok.shape[0]
    _, shard, inner, _ = place()
    outer, at = line()
    me = 2 * shard + inner
    my_rows = aligned(me * seg, seg)
    chunks = list(zip(range(1, 1 + len(UNIT_CHUNKS)), UNIT_STARTS, UNIT_CHUNKS))
    gather = Gather(
        layers, rows, r["g1"], weights, r["send_x"], r["recv_x"], r["send_z"], r["recv_z"]
    )
    reduce = Reduce(
        layers, rows, (r["w2"], r["g1"], r["g2"], r["g3"]), (r["slot0"], r["slot1"], r["slot2"], r["slot3"]),
        r["stage"], r["w1"], r["sum"], r["outgoing"], r["mine"], r["theirs"],
        (r["send_g"], r["recv_g"], r["fetched"], r["fetches"], r["stored"], r["send_o"], r["recv_o"]),
    )

    def spread(buf, n):
        return Spread(buf, seg, SPREAD_SPLITS[n], r["send_s"].at[n], r["recv_s"].at[n])

    def collect(part, n):
        sems = r["send_c"].at[n], r["recv_c"].at[n]
        return Collect(part, seg, COLLECT_SPLITS[n], total, r["pair"], r["near"], r["joined"], *sems)

    one, up, two, three = spread(seq_a, 0), spread(seq_b, 1), spread(seq_a, 2), spread(seq_a, 3)
    branch, down, feed, inputs = collect(seq_a, 0), collect(seq_b, 1), collect(du, 2), collect(seq_a, 3)
    lanes = lax.broadcasted_iota(jnp.int32, (seg, WIDE), 1) < HALF_Q
    taps = pltpu.roll(gains[...], lax.rem(D - shard * QUARTER - inner * HALF_Q, D), 1)[2:5, :WIDE]
    kept = pl.ds(D, WIDE)
    sums, tap_sums = r["gain_sums"], r["tap_sums"]

    def block(t):
        return aligned(t * seg, seg)

    def mine(part):
        return pl.ds(pl.multiple_of(me * seg + part.start, 16), part.size)

    def first_norm():
        def rows(part, _):
            values = tok[part].astype(F32)
            seq_a[mine(part)] = (values * norm_scale(values) * gains[0:1, :]).astype(BF16)
            return 0

        by_rows(seg, rows)

    def up_start():
        seq_b[my_rows] = cot[...]
        up.start()

    def held():
        return pltpu.make_async_copy(seq_a, r["n1_held"], r["held"])

    def reload():
        return pltpu.make_async_copy(r["n1_held"], seq_b, r["held"])

    def project(s):
        for i in (0, 1):
            parts = dot(seq_a[block(2 * s + i)], weights[0][...])
            b = jnp.where(lanes, parts[:, :WIDE], 0.0)
            c = pltpu.roll(parts[:, 128 : 128 + 384], 384 - 64, 1)[:, :WIDE]
            x = parts[:, 384 : 384 + WIDE]
            c_all[s, pl.ds(i * seg, seg)] = jnp.where(lanes, c, 0.0)
            gated[s, pl.ds(8 + i * seg, seg)] = (b * x).astype(BF16).astype(F32)

    def ahead():
        return remote(
            gated.at[:, pl.ds(2 * seg, 8)], gated.at[:, pl.ds(0, 8)], r["halo_send"].at[0], r["halo_recv"].at[0], at(1)
        )

    def halo():
        pl.when(outer < layers - 1)(lambda: ahead().start())

        @pl.when(outer == 0)
        def _():
            gated[:, pl.ds(0, 8)] = jnp.zeros((GROUPS, 8, WIDE), F32)

    def convolved(s, i):
        return (
            taps[0:1, :] * gated[s, pl.ds(6 + i * seg, seg)]
            + taps[1:2, :] * gated[s, pl.ds(7 + i * seg, seg)]
            + taps[2:3, :] * gated[s, pl.ds(8 + i * seg, seg)]
        )

    def convolve(t):
        for i in (0, 1):

            @pl.when(t % 2 == i)
            def _():
                s = t // 2
                mixed[block(t)] = pltpu.roll(c_all[s, pl.ds(i * seg, seg)] * convolved(s, i), 64, 1).astype(BF16)

        seq_a[block(t)] = dot_rows(mixed[block(t)], weights[0][:, pl.ds(512, WIDE)]).astype(BF16)

    def branch_end():
        branch.end()
        allow(r["credit"].at[0])

    def second_norm():
        def rows(part, _):
            values = tok[part].astype(F32) + total[part]
            r["resid"][part] = values
            seq_a[mine(part)] = (values * norm_scale(values) * gains[1:2, :]).astype(BF16)
            return 0

        by_rows(seg, rows)
        pl.semaphore_wait(r["credit"].at[0], 3)

    def hidden(k, start, units, t):
        ref, here = weights[k], block(t)
        gate = dot(seq_a[here], ref[:, pl.ds(0, units)])
        upval = dot(seq_a[here], ref[:, pl.ds(units, units)])
        dact = dot(seq_b[here], ref[:, pl.ds(2 * units, units)])
        sigma = jax.nn.sigmoid(gate)
        silu = gate * sigma
        act[here, pl.ds(start, units)] = (silu * upval).astype(BF16)
        dgate = dact * upval * sigma * (1.0 + gate * (1.0 - sigma))
        du[here, pl.ds(2 * start, units)] = dgate.astype(BF16)
        du[here, pl.ds(2 * start + units, units)] = (dact * silu).astype(BF16)

    def slice_of(n):
        return jnp.where(outer < layers // 2, D // SLICE - 1 - n, n)

    def gate_up_grads(k, start, units, n):
        part = slice_of(n)
        left = seq_a[:, aligned(part * SLICE, SLICE, 128)]
        reduce.grads[k][aligned(part * SLICE, SLICE), pl.ds(0, 2 * units)] = dot_columns(
            left, du[:, pl.ds(2 * start, 2 * units)]
        ).astype(BF16)

    def down_grads(k, start, units, n):
        part = slice_of(n)
        left = seq_b[:, aligned(part * SLICE, SLICE, 128)]
        reduce.grads[k][aligned(part * SLICE, SLICE), pl.ds(2 * units, units)] = dot_columns(
            left, act[:, pl.ds(start, units)]
        ).astype(BF16)

    def grads(k, start, units, n):
        gate_up_grads(k, start, units, n)
        down_grads(k, start, units, n)
        reduce.direct(k, slice_of(n))

    def second(t):
        here = block(t)
        seq_b[here] = sum(
            dot_rows(du[here, pl.ds(2 * start, 2 * units)], weights[k][:, pl.ds(0, 2 * units)])
            for k, start, units in chunks
        ).astype(BF16)

    def down_end():
        down.end()
        reload().start()
        allow(r["credit"].at[1])

    def forward(t):
        here = block(t)
        du[here, pl.ds(0, D)] = sum(
            dot_rows(act[here, pl.ds(start, units)], weights[k][:, pl.ds(2 * units, units)])
            for k, start, units in chunks
        ).astype(BF16)

    def second_back():
        def rows(part, gain):
            dpart, dgain = norm_back(r["resid"][part], gains[1:2, :], total[part])
            dresid = cot[part].astype(F32) + dpart
            r["dresid"][part] = dresid
            seq_a[mine(part)] = dresid.astype(BF16)
            return gain + dgain

        sums[...] = jnp.zeros(sums.shape, F32)
        tap_sums[...] = jnp.zeros(tap_sums.shape, F32)
        sums[1:2, pl.ds(0, D)] = by_rows(seg, rows, jnp.zeros((1, D), F32))
        pl.semaphore_wait(r["credit"].at[1], 3)

    def mix_back(t):
        s, here = t // 2, block(t)
        dmixed = pltpu.roll(dot(seq_a[here], weights[0][:, pl.ds(512, WIDE)]), WIDE - 64, 1)
        dmixed = jnp.where(lanes, dmixed, 0.0)
        for i in (0, 1):

            @pl.when(t % 2 == i)
            def _():
                du[here, kept] = (dmixed * convolved(s, i)).astype(BF16)
                c_all[s, pl.ds(i * seg, seg)] = dmixed * c_all[s, pl.ds(i * seg, seg)]

    def after():
        return remote(
            c_all.at[:, pl.ds(0, 8)], c_all.at[:, pl.ds(2 * seg, 8)], r["halo_send"].at[1], r["halo_recv"].at[1], at(-1)
        )

    def halo_back():
        pl.when(outer > 0)(lambda: after().start())

        @pl.when(outer == layers - 1)
        def _():
            c_all[:, pl.ds(2 * seg, 8)] = jnp.zeros((GROUPS, 8, WIDE), F32)

    def conv_back(n):
        for i in (0, 1):
            pl.when(n // GROUPS == i)(functools.partial(conv_back_half, n % GROUPS, i))

    def conv_back_half(s, i):
        t = block(2 * s + i)
        dconv = c_all[s, pl.ds(i * seg, seg)]
        dgated = (
            taps[2:3, :] * dconv
            + taps[1:2, :] * c_all[s, pl.ds(1 + i * seg, seg)]
            + taps[0:1, :] * c_all[s, pl.ds(2 + i * seg, seg)]
        )
        parts = dot(seq_b[t], weights[0][:, pl.ds(0, 640)])
        db = dgated * parts[:, 384:640]
        dx = dgated * parts[:, :WIDE]
        dc = jnp.concatenate([du[t, kept].astype(F32), jnp.zeros((seg, 128), F32)], axis=1)
        dc = pltpu.roll(dc, 64, 1)
        act[t, pl.ds(0, 128)] = db[:, :128].astype(BF16)
        act[t, pl.ds(128, 128)] = (db[:, 128:] + dc[:, :128]).astype(BF16)
        act[t, pl.ds(256, 128)] = dc[:, 128:256].astype(BF16)
        act[t, pl.ds(384, WIDE)] = dx.astype(BF16)
        act[t, pl.ds(640, 128)] = jnp.zeros((seg, 128), BF16)
        for k in range(3):
            moved = gated[s, pl.ds(6 + k + i * seg, seg)]
            tap_sums[k : k + 1] = tap_sums[k : k + 1] + jnp.sum(dconv * moved, axis=0, keepdims=True)

    def conv_grads(n):
        part = slice_of(n)
        held_rows, cols = aligned(part * SLICE, SLICE), aligned(part * SLICE, SLICE, 128)
        ref = reduce.grads[0]
        of_parts = dot_columns(seq_b[:, cols], act[:, pl.ds(0, CONV_COLS)])
        ref[held_rows, pl.ds(0, 512)] = of_parts[:, :512].astype(BF16)
        of_mixed = dot_columns(seq_a[:, cols], mixed[...])
        ref[held_rows, pl.ds(512, WIDE)] = (of_parts[:, 512:] + of_mixed).astype(BF16)
        reduce.direct(0, part)

    def feed_end():
        feed.end()
        allow(r["credit"].at[2])
        r["block_out"][...] = (r["resid"][...] + total[...]).astype(BF16)

    def first(t):
        here = block(t)
        seq_a[here] = dot_rows(act[here, pl.ds(0, 640)], weights[0][:, pl.ds(0, 640)]).astype(BF16)

    def first_back():
        def rows(part, gain):
            dpart, dgain = norm_back(tok[part].astype(F32), gains[0:1, :], total[part])
            r["input_grad"][part] = (r["dresid"][part] + dpart).astype(BF16)
            return gain + dgain

        sums[0:1, pl.ds(0, D)] = by_rows(seg, rows, jnp.zeros((1, D), F32))
        sums[2:5, aligned(me * WIDE, WIDE, 128)] = tap_sums[0:3]

    def gains_across(n):
        return remote(sums, r["gain_in"].at[n], r["send_a"].at[n], r["recv_a"].at[n], partners()[n])

    def gains_add(n):
        gains_across(n).wait()
        sums[...] = sums[...] + r["gain_in"][n]

    def line_copy(sign, steps):
        slot = (0 if sign > 0 else 1, steps - 1)
        return remote(
            sums, r["gain_line"].at[slot], r["send_l"].at[slot], r["recv_l"].at[slot], at(sign * steps)
        )

    def gains_line():
        for steps in range(1, layers):
            for sign in (1, -1):
                pl.when(in_line(outer + sign * steps, layers))(line_copy(sign, steps).start)

    def gains_end():
        for steps in range(1, layers):
            for sign in (1, -1):
                pl.when(in_line(outer + sign * steps, layers))(line_copy(sign, steps).wait_send)
                pl.when(in_line(outer - sign * steps, layers))(line_copy(sign, steps).wait_recv)

        own_sums = sums[...]
        for origin in range(layers):
            for steps in range(1, layers):
                for sign in (1, -1):

                    @pl.when((outer - sign * steps == origin))
                    def _():
                        came = r["gain_line"][0 if sign > 0 else 1, steps - 1]
                        sums[...] = came if origin == 0 else sums[...] + came

            if origin > 0:

                @pl.when(outer == origin)
                def _():
                    sums[...] = sums[...] + own_sums

    def end():
        reduce.finish(0)
        for k in range(len(WIDTHS)):
            reduce.wait_sent(k)
        pl.when(outer < layers - 1)(lambda: ahead().wait_send())
        pl.when(outer > 0)(lambda: after().wait_send())

    windows = [
        (r["resid"], 0, D), (r["dresid"], D, D), (total, 2 * D, D), (r["resid"], 3 * D, D),
        (r["tail"], 4 * D, GROUP_COLS - 4 * D),
    ]

    def load(n):
        ref, first, width = windows[n]
        return pltpu.make_async_copy(
            r["weights"].at[:, pl.ds(first, width)], ref.at[pl.ds(0, rows)], r["loaded"].at[n]
        )

    def start():
        for n in (0, 1, 2, 4):
            load(n).start()
        greet(layers)
        load(0).wait()
        cut(0)
        load(3).start()
        greeted(layers)

    def cut(k):
        def read(part, first, width):
            found = []
            for n, (ref, low, size) in enumerate(windows):
                start, stop = max(first, low), min(first + width, low + size)
                if start < stop and (n == 0) == (k == 0):
                    found.append(ref[part, start - low : stop - low])
            return found

        def band(n, _):
            part = aligned(n * 16, 16)
            halves = []
            for half in (0, 1):
                pieces = []
                for first, own, width, padding in column_pieces(half):
                    if STARTS[k] <= own < STARTS[k] + WIDTHS[k]:
                        pieces += read(part, first, width)
                        if padding:
                            pieces.append(jnp.zeros((16, padding), F32))
                halves.append(jnp.concatenate(pieces, axis=1))
            is_low = inner == 0
            seq = lax.axis_index("seq")
            own_rows = aligned(seq * rows + n * 16, 16)
            weights[k][own_rows, :] = jnp.where(is_low, halves[0], halves[1]).astype(BF16)
            gather.other_rows(k)[part, :] = jnp.where(is_low, halves[1], halves[0]).astype(BF16)
            return 0

        for n in (1, 2, 3, 4) if k == CUT_FIRST else ():
            load(n).wait()
        lax.fori_loop(0, rows // 16, band, 0)

    def hold():
        held().start()

    def hold_end():
        held().wait()

    def halo_end():
        pl.when(outer > 0)(lambda: ahead().wait_recv())

    def reload_end():
        reload().wait()

    def halo_back_end():
        pl.when(outer < layers - 1)(lambda: after().wait_recv())

    def feed_credit():
        pl.semaphore_wait(r["credit"].at[2], 3)

    def from_spread(moved, body):
        def step(n):
            for m in range(8):
                if moved.before(m):

                    @pl.when(n == m)
                    def _():
                        for act in moved.before(m):
                            act()

            body(moved.index(n))

        return step

    def each(body, *cases):
        return [functools.partial(body, *(case if isinstance(case, tuple) else (case,))) for case in cases]

    every = range(len(WIDTHS))
    cuts = each(cut, *every)
    exchange, send_own, send_other = (
        each(body, *every) for body in (gather.exchange, gather.send_own, gather.send_other)
    )
    step = [each(gather.steps, (k, 1, 1), (k, 2, 2), (k, 3)) for k in every]
    join_far = each(reduce.join, *((k, layers - 2, 2) for k in every))
    join_near = each(reduce.join, *((k, 1, 1) for k in every))
    final = each(reduce.final, (0, 3), 1, (2, 1), (3, 2))
    feed_pair = each(feed.add_pair, 0, 1, 2)
    gain_send = [lambda n=n: gains_across(n).start() for n in range(3)]
    gain_add = each(gains_add, 0, 1, 2)
    d3_far = functools.partial(reduce.direct, 3, least=2)
    d3_near = functools.partial(reduce.direct, 3, most=1)
    blocks, parts = 2 * GROUPS, D // SLICE
    proj = Loop(GROUPS, project)
    mix = Loop(blocks, lambda n: branch.make(n, convolve))
    hid1 = Loop(blocks, from_spread(two, functools.partial(hidden, *chunks[0])))
    hid2, hid3 = (Loop(blocks, functools.partial(hidden, *chunk)) for chunk in chunks[1:])
    grad1, grad2 = (Loop(parts, functools.partial(grads, *chunk)) for chunk in chunks[:2])
    down3 = Loop(parts, functools.partial(down_grads, *chunks[2]))
    back2 = Loop(blocks, lambda n: down.make(n, second))
    gate3 = Loop(parts, functools.partial(gate_up_grads, *chunks[2]))
    ffn = Loop(blocks, forward)
    back_mix = Loop(blocks, from_spread(three, mix_back))
    back_conv = Loop(blocks, conv_back)
    grad0 = Loop(parts, conv_grads)
    back1 = Loop(blocks, lambda n: inputs.make(n, first))
    play(
        [
            start, send_own[0], exchange[0], cuts[1], first_norm, one.start, cuts[3], cuts[2], send_other[0],
            step[0][0], one.first, send_own[1], exchange[1], step[0][1], one.near, up_start, one.far, up.first,
            send_other[1], step[0][2], one.end, exchange[3], proj[0], proj[1], proj[2], hold, proj[3], halo,
            hold_end, halo_end, mix[0], step[1][0], exchange[2], send_own[2], mix[1], mix[2], mix[3], mix[4],
            mix[5], step[1][1], up.near, up.far, mix[6], mix[7], send_other[3], branch_end, send_other[2],
            second_norm, up.end, send_own[3], two.start, step[1][2], hid1[0], hid1[1], gather.crossed, hid1[2],
            hid1[3], hid1[4], hid1[5], step[2][0], hid1[6], hid1[7], two.sent, grad1[0], grad1[1], grad1[2],
            step[2][1], step[2][2], grad1[3], hid2[0], step[3][0], hid2[1], hid2[2], hid2[3], hid2[4], hid2[5],
            hid2[6], hid2[7], grad2[0], grad2[1], grad2[2], step[3][1], grad2[3], step[3][2], gather.finish,
            hid3[0], hid3[1], hid3[2], hid3[3], hid3[4], hid3[5], hid3[6], hid3[7], down3[0], down3[1], down3[2],
            down3[3], back2[0], back2[1], join_far[1], back2[2], back2[3], back2[4], back2[5], back2[6], back2[7],
            gate3[0], gate3[1], gate3[2], gate3[3], down_end, second_back, three.start, join_near[1], join_far[2],
            back_mix[0], d3_far, ffn[0], ffn[1], ffn[2], ffn[3], ffn[4], ffn[5], ffn[6], ffn[7], back_mix[1],
            back_mix[2], feed.push, back_mix[3], back_mix[4], back_mix[5], reload_end, feed_pair[0], final[1],
            back_mix[6], back_mix[7], three.sent, halo_back, back_conv[0], d3_near, back_conv[1], back_conv[2],
            join_far[3], back_conv[3], join_near[2], halo_back_end, feed_pair[1], feed_pair[2], back_conv[4],
            back_conv[5], feed.pass_on, back_conv[6], back_conv[7], grad0[0], grad0[1], grad0[2], join_near[3],
            grad0[3], feed.add_own, feed_end, feed_credit, back1[0], back1[1], join_far[0], back1[2], back1[3],
            back1[4], back1[5], final[2], back1[6], back1[7], join_near[0], inputs.end, first_back, gain_send[0],
            final[3], gain_add[0], gain_send[1], gain_add[1], gain_send[2], gain_add[2], gains_line, final[0],
            gains_end, end,
        ]
    )


class Loop:
    def __init__(self, count, body):
        self.count, self.body = count, body

    def __getitem__(self, n):
        return (self, n)


def play(order):
    order = list(order)
    while order:
        entry = order.pop(0)
        if not isinstance(entry, tuple):
            entry()
            continue
        loop, _ = entry
        between = {}
        for n in range(1, loop.count):
            between[n] = []
            while order[0] != (loop, n):
                between[n].append(order.pop(0))
            order.pop(0)

        def turn(n, _):
            for m, acts in between.items():
                if acts:

                    @pl.when(n == m)
                    def _():
                        play(acts)

            loop.body(n)
            return 0

        lax.fori_loop(0, loop.count, turn, 0)


def block_step(tok, cot, gains, weights, layers):
    rows, seg = weights.shape[0], tok.shape[0]
    count = len(WIDTHS)
    tokens = 2 * GROUPS * seg
    vmem, anywhere = pl.BlockSpec(memory_space=pltpu.VMEM), pl.BlockSpec(memory_space=pl.ANY)
    shape, scratch = jax.ShapeDtypeStruct, pltpu.VMEM
    dma, regular = pltpu.SemaphoreType.DMA, pltpu.SemaphoreType.REGULAR
    hops = layers - 1
    wide, biggest = sum(WIDTHS), max(WIDTHS)
    out_shape = [
        shape((seg, D), BF16),
        shape((seg, D), BF16),
        shape((8, 2 * GROUPS * WIDE), F32),
        shape((rows, wide), F32),
        shape((rows, wide), BF16),
        shape((tokens, D), BF16),
    ] + [shape((2, hops, 2 * rows, width), BF16) for width in WIDTHS]
    scratch_shapes = (
        [scratch((D, width), BF16) for width in WIDTHS]
        + [
            scratch((tokens, D), BF16),
            scratch((tokens, D), BF16),
            scratch((tokens, 2 * PAD_F), BF16),
            scratch((tokens, PAD_F), BF16),
            scratch((GROUPS, 8 + 2 * seg, WIDE), F32),
            scratch((GROUPS, 8 + 2 * seg, WIDE), F32),
            scratch((tokens, WIDE), BF16),
            scratch((seg, D), F32),
            scratch((seg, D), F32),
            scratch((seg, D), F32),
            scratch((4, seg, D), BF16),
            scratch((2, seg, D), BF16),
            scratch((seg, D), BF16),
        ]
        + [scratch((D, width), BF16) for width in WIDTHS[1:]]
        + [
            scratch((2 * rows, biggest), BF16),
            scratch((rows, biggest), F32),
            scratch((rows, GROUP_COLS - 4 * D), F32),
            scratch((rows, wide), BF16),
            scratch((8, WIDE), F32),
            scratch((3, 8, 2 * GROUPS * WIDE), F32),
            scratch((2, hops, 8, 2 * GROUPS * WIDE), F32),
            dma,
            dma((5,)),
            dma((count,)),
            dma((count,)),
            dma((count, 2, hops, 2)),
            dma((count, 2, hops, 2)),
            dma((4, 11)),
            dma((4, 11)),
            dma((4, 10)),
            dma((4, 10)),
            regular((3,)),
            dma((2,)),
            dma((2,)),
            dma((count, 2, hops)),
            dma((count, 2, hops)),
            dma,
            dma((4,)),
            dma((count,)),
            dma((count,)),
            dma((count,)),
            dma((3,)),
            dma((3,)),
            dma((2, hops)),
            dma((2, hops)),
        ]
    )
    return pl.pallas_call(
        functools.partial(block_kernel, layers, rows),
        out_shape=out_shape,
        in_specs=[vmem] * 3 + [anywhere],
        out_specs=[vmem] * 3 + [anywhere] * (3 + count),
        scratch_shapes=scratch_shapes,
        compiler_params=pltpu.CompilerParams(
            collective_id=0, has_side_effects=True, vmem_limit_bytes=VMEM_BYTES
        ),
        name="block_step",
    )(tok, cot, gains, weights)[:5]


def band(rows, most):
    return max(size for size in range(16, most + 1, 16) if rows % size == 0)


def adam_update(param, grad, first, second, rate, decay):
    first_new = MOMENT_DECAY * first + (1.0 - MOMENT_DECAY) * grad
    second_new = SQUARE_DECAY * second + (1.0 - SQUARE_DECAY) * grad * grad
    root = jnp.sqrt(second_new * (1.0 / (1.0 - SQUARE_DECAY**STEP))) + ADAM_EPSILON
    step = first_new * (rate / (1.0 - MOMENT_DECAY**STEP)) / root
    return (first_new, second_new, param * (1.0 - rate * decay) - step)


def update_kernel(
    inner_ref, mine_ref, theirs_ref, weights_ref, first_ref, second_ref, sums_ref, gains_ref, gains_first_ref,
    gains_second_ref, block_ref, input_ref, grad_out, first_out, second_out, weights_out, gains_grad_out,
    gains_first_out, gains_second_out, gains_out, block_out, input_out,
):
    is_low = inner_ref[0] == 0
    mine, theirs = mine_ref[...], theirs_ref[...].astype(F32)
    for half in (0, 1):
        chosen = jnp.where(is_low, mine, theirs) if half == 0 else jnp.where(is_low, theirs, mine)
        for first, own, width, _ in column_pieces(half):
            grad_out[:, first : first + width] = chosen[:, own : own + width]
    first_out[...], second_out[...], weights_out[...] = adam_update(
        weights_ref[...], grad_out[...], first_ref[...], second_ref[...], WEIGHT_RATE, WEIGHT_DECAY
    )

    @pl.when(pl.program_id(0) == 0)
    def _():
        gains_grad_out[0:2] = sums_ref[0:2, :D]
        for n in range(2 * GROUPS):
            gains_grad_out[2:5, n * HALF_Q : (n + 1) * HALF_Q] = sums_ref[2:5, n * WIDE : n * WIDE + HALF_Q]
        gains_first_out[...], gains_second_out[...], gains_out[...] = adam_update(
            gains_ref[...], gains_grad_out[...], gains_first_ref[...], gains_second_ref[...], GAIN_RATE, 0.0
        )
        block_out[...] = block_ref[...]
        input_out[...] = input_ref[...]


def update(inner, mine, theirs, weights, first, second, sums, gains, gains_first, gains_second, block, grad):
    rows, cols = weights.shape
    wide = mine.shape[1]
    size = band(rows, 32)
    by_row = lambda width: pl.BlockSpec((size, width), lambda n: (n, 0))
    whole = lambda values: pl.BlockSpec(values.shape, lambda n: (0, 0))
    shape = jax.ShapeDtypeStruct
    return pl.pallas_call(
        update_kernel,
        grid=(rows // size,),
        out_shape=[shape((rows, cols), F32)] * 4 + [shape(gains.shape, F32)] * 4 + [shape(block.shape, BF16)] * 2,
        in_specs=[pl.BlockSpec(memory_space=pltpu.SMEM)]
        + [by_row(wide)] * 2
        + [by_row(cols)] * 3
        + [whole(sums)]
        + [whole(gains)] * 3
        + [whole(block)] * 2,
        out_specs=[by_row(cols)] * 4 + [whole(gains)] * 4 + [whole(block)] * 2,
        compiler_params=pltpu.CompilerParams(vmem_limit_bytes=VMEM_BYTES),
        name="update",
    )(inner, mine, theirs, weights, first, second, sums, gains, gains_first, gains_second, block, grad)


def on_device(
    tokens, gains_taps, weights, cotangent, weight_first, weight_second, gains_first, gains_second
):
    layers = lax.axis_size("seq") // 2
    inner_word = (lax.axis_index("seq") % 2).astype(jnp.int32).reshape(1)
    block_out, input_grad, gain_sums, mine, theirs = block_step(
        tokens[0], cotangent[0], gains_taps, weights, layers
    )
    (
        weight_grad, weight_first_new, weight_second_new, weight_new,
        gains_grad, gains_first_new, gains_second_new, gains_new, block_out, input_grad,
    ) = update(
        inner_word, mine, theirs, weights, weight_first, weight_second,
        gain_sums, gains_taps, gains_first, gains_second, block_out, input_grad,
    )
    return (
        block_out[None],
        input_grad[None],
        weight_grad,
        weight_first_new,
        weight_second_new,
        weight_new,
        gains_grad,
        gains_first_new,
        gains_second_new,
        gains_new,
    )


def solution(mesh):
    tokens, rows, whole = P("shard", "seq", None), P("seq", "shard"), P()
    return jax.shard_map(
        on_device,
        mesh=mesh,
        in_specs=(tokens, whole, rows, tokens, rows, rows, whole, whole),
        out_specs=(tokens, tokens, rows, rows, rows, rows, whole, whole, whole, whole),
        check_vma=False,
    )
```

```python
import functools

import jax
import jax.numpy as jnp
from jax import lax
from jax.experimental import pallas as pl
from jax.experimental.pallas import tpu as pltpu
from jax.sharding import PartitionSpec as P

D = 1536
FF = 6912
STEP = 10
GROUPS = 4
QUARTER = D // GROUPS
UNITS = FF // GROUPS
GROUP_COLS = 4 * QUARTER + 3 * UNITS
HALF_Q = QUARTER // 2
HALF_F = UNITS // 2
LANES = 128
PAD_F = -(-HALF_F // LANES) * LANES
WIDE = 256
CONV_COLS = 4 * HALF_Q
UNIT_CHUNKS = (384, 256, PAD_F - 640)
UNIT_STARTS = (0, 384, 640)
WIDTHS = (CONV_COLS,) + tuple(3 * units for units in UNIT_CHUNKS)
STARTS = tuple(sum(WIDTHS[:k]) for k in range(len(WIDTHS)))
SPREAD_SPLITS = (208, 208, 64, 128)
COLLECT_SPLITS = (128, 128, 112, 112)
REACH = (1, 1, 1, 1)
CUT_FIRST = 1
SLICE = 384
TILE = 16
ROWS = 48

MOMENT_DECAY = 0.9
SQUARE_DECAY = 0.95
ADAM_EPSILON = 1e-08
NORM_EPSILON = 1e-05
WEIGHT_RATE = 0.02
GAIN_RATE = 0.2
WEIGHT_DECAY = 0.1

BF16 = jnp.bfloat16
F32 = jnp.float32
MESH = pl.DeviceIdType.MESH
VMEM_BYTES = 63 * 1024 * 1024


def place():
    seq, shard = lax.axis_index("seq"), lax.axis_index("shard")
    inner, core = lax.rem(seq, 2), lax.rem(shard, 2)
    return seq, shard, inner, core


def partners():
    seq, shard, inner, core = place()
    across = {"seq": seq + 1 - 2 * inner, "shard": shard}
    beside = {"seq": seq, "shard": lax.rem(shard + 2, 4)}
    twin = {"seq": seq, "shard": shard + 1 - 2 * core}
    return across, beside, twin


def remote(src, dst, send, recv, device):
    return pltpu.make_async_remote_copy(
        src_ref=src, dst_ref=dst, send_sem=send, recv_sem=recv, device_id=device, device_id_type=MESH
    )


def line():
    seq, shard, _, _ = place()
    size = lax.axis_size("seq")
    return seq // 2, lambda steps: {"seq": lax.rem(seq + 2 * steps + size, size), "shard": shard}


def greet(layers):
    outer, at = line()
    barrier = pltpu.get_barrier_semaphore()
    for device in partners():
        pl.semaphore_signal(barrier, inc=1, device_id=device, device_id_type=MESH)
    for steps in range(1, layers):
        for sign in (1, -1):

            @pl.when(in_line(outer + sign * steps, layers))
            def _():
                pl.semaphore_signal(barrier, inc=1, device_id=at(sign * steps), device_id_type=MESH)


def greeted(layers):
    pl.semaphore_wait(pltpu.get_barrier_semaphore(), 3 + layers - 1)


def in_line(index, layers):
    return (index >= 0) & (index < layers)


def allow(credit):
    for device in partners():
        pl.semaphore_signal(credit, inc=1, device_id=device, device_id_type=MESH)


def dot(left, right):
    return jnp.dot(left, right, preferred_element_type=F32)


def dot_rows(left, right):
    return lax.dot_general(left, right, (((1,), (1,)), ((), ())), preferred_element_type=F32)


def dot_columns(left, right):
    return lax.dot_general(left, right, (((0,), (0,)), ((), ())), preferred_element_type=F32)


def aligned(start, size, multiple=16):
    return pl.ds(pl.multiple_of(start, multiple), size)


class Gather:
    def __init__(self, layers, rows, oth, outs, send_x, recv_x, send_z, recv_z):
        self.layers, self.rows, self.oth, self.outs = layers, rows, oth, outs
        self.send_x, self.recv_x, self.send_z, self.recv_z = send_x, recv_x, send_z, recv_z
        self.seq, _, self.inner, _ = place()
        self.outer, self.at = line()
        self.across = partners()[0]

    def seq_rows(self, index):
        return aligned(index * self.rows, self.rows)

    def layer_rows(self, direction, distance):
        origin = self.outer - distance if direction == 0 else self.outer + distance
        return aligned(origin * 2 * self.rows, 2 * self.rows)

    def copy(self, k, src, dst, direction, distance, hop, piece):
        slot = (k, direction, distance + hop - 1, piece)
        return remote(
            src, dst, self.send_z.at[slot], self.recv_z.at[slot], self.at(hop if direction == 0 else -hop)
        )

    def goes(self, direction, hop):
        return in_line(self.outer + (hop if direction == 0 else -hop), self.layers)

    def has_come(self, direction, distance):
        return in_line(self.outer + (-distance if direction == 0 else distance), self.layers)

    def hops(self, k, distance):
        return range(1, min(REACH[k], self.layers - 1 - distance) + 1)

    def own_copy(self, k, direction, hop):
        here = self.outs[k].at[self.seq_rows(self.seq)]
        return self.copy(k, here, here, direction, 0, hop, 0)

    def other_copy(self, k, direction, hop):
        there = self.outs[k].at[self.seq_rows(self.seq + 1 - 2 * self.inner)]
        return self.copy(k, there, there, direction, 0, hop, 1)

    def pass_copy(self, k, direction, distance, hop):
        ref = self.outs[k].at[self.layer_rows(direction, distance)]
        return self.copy(k, ref, ref, direction, distance, hop, 0)

    def other_rows(self, k):
        return self.oth.at[pl.ds(k * self.rows, self.rows), pl.ds(0, WIDTHS[k])]

    def exchange(self, k):
        self.x_copy(k).start()

    def x_copy(self, k):
        here = self.outs[k].at[self.seq_rows(self.seq)]
        return remote(self.other_rows(k), here, self.send_x.at[k], self.recv_x.at[k], self.across)

    def crossed(self):
        for k in range(len(self.outs)):
            self.x_copy(k).wait_send()

    def send_own(self, k):
        for hop in self.hops(k, 0):
            for direction in (0, 1):

                @pl.when(self.goes(direction, hop))
                def _():
                    self.own_copy(k, direction, hop).start()

    def send_other(self, k):
        self.x_copy(k).wait_recv()
        for hop in self.hops(k, 0):
            for direction in (0, 1):

                @pl.when(self.goes(direction, hop))
                def _():
                    self.other_copy(k, direction, hop).start()

    def step(self, k, distance):
        for direction in (0, 1):

            @pl.when(self.has_come(direction, distance))
            def _():
                if distance <= REACH[k]:
                    origin = self.outer - distance if direction == 0 else self.outer + distance
                    for piece in (0, 1):
                        index = 2 * origin + (self.inner if piece == 0 else 1 - self.inner)
                        ref = self.outs[k].at[self.seq_rows(index)]
                        self.copy(k, ref, ref, direction, distance - 1, 1, piece).wait_recv()
                else:
                    ref = self.outs[k].at[self.layer_rows(direction, distance)]
                    self.copy(k, ref, ref, direction, distance - 1, 1, 0).wait_recv()
                if distance % REACH[k] == 0:
                    for hop in self.hops(k, distance):

                        @pl.when(self.goes(direction, hop))
                        def _():
                            self.pass_copy(k, direction, distance, hop).start()

    def steps(self, k, first, last=None):
        last = self.layers - 1 if last is None else min(last, self.layers - 1)
        for distance in range(first, last + 1):
            self.step(k, distance)

    def finish(self):
        for k in range(len(self.outs)):
            for distance in range(0, self.layers - 1, REACH[k]):
                for hop in self.hops(k, distance):
                    for direction in (0, 1):

                        @pl.when(self.goes(direction, hop) & self.has_come(direction, distance))
                        def _():
                            if distance == 0:
                                self.own_copy(k, direction, hop).wait_send()
                                self.other_copy(k, direction, hop).wait_send()
                            else:
                                self.pass_copy(k, direction, distance, hop).wait_send()


class Reduce:
    def __init__(self, layers, rows, grads, slots, stage, spare, total, outgoing, mine, theirs, sems):
        self.layers, self.rows, self.grads, self.slots = layers, rows, grads, slots
        self.stage, self.spare, self.total, self.outgoing = stage, spare, total, outgoing
        self.mine, self.theirs = mine, theirs
        self.send_g, self.recv_g, self.fetched, self.fetches, self.stored, self.send_o, self.recv_o = sems
        _, _, self.inner, _ = place()
        self.outer, self.at = line()
        self.across = partners()[0]

    def owner(self, direction, distance):
        return self.outer + distance if direction == 0 else self.outer - distance

    def upstream(self, direction, steps):
        return in_line(self.outer - steps if direction == 0 else self.outer + steps, self.layers)

    def block(self, k, owner):
        return self.grads[k].at[aligned(owner * 2 * self.rows, 2 * self.rows), pl.ds(0, WIDTHS[k])]

    def copy(self, k, src, direction, distance):
        slot = (direction, distance - 1)
        return remote(
            src,
            self.slots[k].at[slot],
            self.send_g.at[(k,) + slot],
            self.recv_g.at[(k,) + slot],
            self.at(1 if direction == 0 else -1),
        )

    def send(self, k, direction, distance):
        self.copy(k, self.block(k, self.owner(direction, distance)), direction, distance).start()

    def direct(self, k, part=None, least=1, most=None):
        for distance in range(most or self.layers - 1, least - 1, -1):
            for direction in (0, 1):
                owner = self.owner(direction, distance)
                here = in_line(owner, self.layers) & jnp.logical_not(self.upstream(direction, 1))
                if part is not None:
                    here = here & (owner * 2 * self.rows // SLICE == part)

                @pl.when(here)
                def _():
                    self.send(k, direction, distance)

    def fetch(self, k, direction, distance):
        slot = self.slots[k].at[direction, distance - 1]
        self.copy(k, slot, direction, distance).wait_recv()
        held = self.stage.at[:, pl.ds(0, WIDTHS[k])]
        copy = pltpu.make_async_copy(slot, held, self.fetched)
        copy.start()
        copy.wait()

    def tiles(self, body):
        def step(n, _):
            body(aligned(n * TILE, TILE))
            return 0

        lax.fori_loop(0, 2 * self.rows // TILE, step, 0)

    def join(self, k, most, least):
        cols = pl.ds(0, WIDTHS[k])
        for distance in range(most, least - 1, -1):
            for direction in (0, 1):
                owner = self.owner(direction, distance)

                @pl.when(in_line(owner, self.layers) & self.upstream(direction, 1))
                def _():
                    def add(tile):
                        base = self.owner(direction, distance) * 2 * self.rows
                        rows = pl.ds(pl.multiple_of(base + tile.start, 16), TILE)
                        ref = self.grads[k]
                        ref[rows, cols] = (
                            ref[rows, cols].astype(F32) + self.stage[tile, cols].astype(F32)
                        ).astype(BF16)

                    self.fetch(k, direction, distance + 1)
                    self.tiles(add)
                    self.send(k, direction, distance)

    def final(self, k, before=None):
        cols = pl.ds(0, WIDTHS[k])
        came = [(1, 0), (1, 1)]

        def fetch(n, distance, direction):
            return pltpu.make_async_copy(
                self.slots[k].at[direction, distance - 1],
                self.spare.at[pl.ds(n * 2 * self.rows, 2 * self.rows), cols],
                self.fetches.at[n],
            )

        for n, (distance, direction) in enumerate(came):

            @pl.when(self.upstream(direction, distance))
            def _():
                self.copy(k, self.slots[k].at[direction, distance - 1], direction, distance).wait_recv()
                fetch(n, distance, direction).start()

        if before is not None:
            self.store(before).wait()

        here, there = self.inner * self.rows, (1 - self.inner) * self.rows

        def each(base, body):
            def step(n, _):
                body(base + n * TILE, n * TILE)
                return 0

            lax.fori_loop(0, self.rows // TILE, step, 0)

        for n, (distance, direction) in enumerate(came):

            @pl.when(self.upstream(direction, distance))
            def _():
                fetch(n, distance, direction).wait()

        def add_up(flags):
            def total(rows):
                value = self.grads[k][aligned(self.outer * 2 * self.rows + rows, TILE), cols].astype(F32)
                for n, flag in enumerate(flags):
                    if flag:
                        value = value + self.spare[aligned(n * 2 * self.rows + rows, TILE), cols].astype(F32)
                return value

            def send(rows, at):
                self.outgoing[aligned(at, TILE), pl.ds(STARTS[k], WIDTHS[k])] = total(rows).astype(BF16)

            def keep(rows, at):
                self.total[aligned(at, TILE), cols] = total(rows)

            each(there, send)
            self.over(k).start()
            each(here, keep)
            self.store(k).start()

        patterns = {}
        for place_in_line in range(self.layers):
            flags = tuple(
                0 <= (place_in_line - distance if direction == 0 else place_in_line + distance) < self.layers
                for distance, direction in came
            )
            patterns.setdefault(flags, []).append(place_in_line)
        for flags, places in patterns.items():
            here_now = functools.reduce(jnp.logical_or, [self.outer == p for p in places])

            @pl.when(here_now)
            def _():
                add_up(flags)

    def over(self, k):
        wide = pl.ds(STARTS[k], WIDTHS[k])
        return remote(
            self.outgoing.at[:, wide], self.theirs.at[:, wide], self.send_o.at[k], self.recv_o.at[k], self.across
        )

    def store(self, k):
        return pltpu.make_async_copy(
            self.total.at[:, pl.ds(0, WIDTHS[k])], self.mine.at[:, pl.ds(STARTS[k], WIDTHS[k])], self.stored.at[k]
        )

    def wait_sent(self, k):
        for distance in range(1, self.layers):
            for direction in (0, 1):
                owner = self.owner(direction, distance)

                @pl.when(in_line(owner, self.layers))
                def _():
                    self.copy(k, self.block(k, owner), direction, distance).wait_send()

    def finish(self, before):
        self.store(before).wait()
        for k in range(len(self.grads)):
            self.over(k).wait()


class Spread:
    slots = range(11)

    def __init__(self, buf, seg, split, send, recv):
        self.buf, self.seg, self.split, self.send, self.recv = buf, seg, split, send, recv

    def index(self, n):
        _, shard, inner, core = place()
        row, flip, other = (n // 2) % 2, n // 4, n % 2
        return 2 * (lax.rem(shard + 2 * row, 4) + other * (1 - 2 * core)) + inner + flip * (1 - 2 * inner)

    def copy(self, slot):
        across, beside, twin = partners()
        low, high, whole = (0, self.split), (self.split, self.seg - self.split), (0, self.seg)
        n, (first, size), device = {
            0: (0, low, across),
            9: (0, high, across),
            1: (0, high, beside),
            10: (0, low, beside),
            2: (0, whole, twin),
            3: (4, low, beside),
            4: (4, whole, twin),
            5: (2, high, across),
            6: (2, whole, twin),
            7: (6, low, twin),
            8: (6, high, twin),
        }[slot]
        ref = self.buf.at[aligned(self.index(n) * self.seg + first, size)]
        return remote(ref, ref, self.send.at[slot], self.recv.at[slot], device)

    def push(self, *slots):
        for slot in slots:
            self.copy(slot).start()

    def came(self, *slots):
        for slot in slots:
            self.copy(slot).wait_recv()

    def start(self):
        self.push(0, 1, 9, 10, 2)

    def first(self):
        self.came(1)
        self.push(5)
        self.came(0)
        self.push(3)

    def near(self):
        self.came(10)
        self.push(6)
        self.came(9)
        self.push(4)

    def far(self):
        self.came(3)
        self.push(7)
        self.came(5)
        self.push(8)

    def sent(self):
        for slot in self.slots:
            self.copy(slot).wait_send()

    def end(self):
        self.came(2, 4, 6, 7, 8)
        self.sent()

    def before(self, n):
        return {
            1: (lambda: self.came(2),),
            2: (self.first, self.near),
            3: (lambda: self.came(6),),
            5: (lambda: self.came(4),),
            6: (self.far,),
            7: (lambda: self.came(7, 8),),
        }.get(n, ())


class Collect:
    def __init__(self, part, seg, split, total, pair, near, joined, send, recv):
        self.part, self.seg, self.total = part, seg, total
        self.pair, self.near, self.joined, self.send, self.recv = pair, near, joined, send, recv
        _, self.shard, self.inner, core = place()
        self.twin_shard = self.shard + 1 - 2 * core
        self.low, self.high, self.whole = (0, split), (split, seg - split), (0, seg)
        self.cols = pl.ds(0, D)

    def index(self, s, k):
        row, flip = 1 - k % 2, 1 - k // 2
        return 2 * lax.rem(s + 2 * row, 4) + self.inner + flip * (1 - 2 * self.inner)

    def pair_copy(self, k):
        src = self.part.at[aligned(self.index(self.twin_shard, k) * self.seg, self.seg), self.cols]
        return remote(src, self.pair.at[k], self.send.at[k], self.recv.at[k], partners()[2])

    def copy(self, slot):
        across, beside, _ = partners()
        src, dst, (first, size), device = {
            4: (self.pair.at[0], self.joined, self.low, across),
            5: (self.pair.at[0], self.joined, self.high, beside),
            6: (self.pair.at[1], self.near.at[0], self.low, across),
            7: (self.pair.at[2], self.near.at[1], self.high, beside),
            8: (self.pair.at[2], self.near.at[1], self.low, beside),
            9: (self.pair.at[1], self.near.at[0], self.high, across),
        }[slot]
        rows = pl.ds(first, size)
        return remote(src.at[rows], dst.at[rows], self.send.at[slot], self.recv.at[slot], device)

    def over(self, span, body):
        def step(n, _):
            body(aligned(span[0] + n * 16, 16))
            return 0

        lax.fori_loop(0, span[1] // 16, step, 0)

    def mine(self, k, rows):
        return self.part[aligned(self.index(self.shard, k) * self.seg + rows.start, 16), self.cols].astype(F32)

    def add_pair(self, k):
        def add(rows):
            self.pair[k, rows] = (self.mine(k, rows) + self.pair[k, rows].astype(F32)).astype(BF16)

        self.pair_copy(k).wait_recv()
        self.over(self.whole, add)
        for slot in ((4, 5), (6,), (7,))[k]:
            self.copy(slot).start()

    def add_own(self):
        def add(rows):
            self.total[rows] = self.mine(3, rows) + self.pair[3, rows].astype(F32)

        self.pair_copy(3).wait_recv()
        self.over(self.whole, add)

    def pass_on(self):
        for slot, k, span, after in ((4, 2, self.low, 8), (5, 1, self.high, 9)):

            def add(rows):
                self.pair[k, rows] = (self.pair[k, rows].astype(F32) + self.joined[rows].astype(F32)).astype(BF16)

            self.copy(slot).wait_recv()
            self.over(span, add)
            self.copy(after).start()

    def push(self):
        for k in range(4):
            self.pair_copy(k).start()

    def make(self, n, produce):
        k, own = n // 2, n % 2
        produce(self.index(jnp.where(own == 1, self.shard, self.twin_shard), k))

        @pl.when(own == 0)
        def _():
            self.pair_copy(k).start()

        for m in range(3):

            @pl.when(n == 2 * m + 1)
            def _():
                self.add_pair(m)
                if m == 2:
                    self.pass_on()

        pl.when(n == 7)(self.add_own)

    def end(self):
        def add(rows):
            near = self.near[0, rows].astype(F32) + self.near[1, rows].astype(F32)
            self.total[rows] = self.total[rows] + near

        for slots, span in (((6, 8), self.low), ((7, 9), self.high)):
            for slot in slots:
                self.copy(slot).wait_recv()
            self.over(span, add)
        for k in range(4):
            self.pair_copy(k).wait_send()
        for slot in range(4, 10):
            self.copy(slot).wait_send()


def norm_scale(values):
    return lax.rsqrt(jnp.mean(values * values, axis=-1, keepdims=True) + NORM_EPSILON)


def by_rows(rows, body, carry=0):
    def step(n, carry):
        return body(aligned(n * ROWS, ROWS), carry)

    return lax.fori_loop(0, rows // ROWS, step, carry)


def norm_back(values, gain, upstream):
    scale = norm_scale(values)
    scaled = gain * upstream
    inner = jnp.mean(scaled * values, axis=-1, keepdims=True)
    return (
        scale * scaled - values * scale * scale * scale * inner,
        jnp.sum(upstream * values * scale, axis=0, keepdims=True),
    )


REFS = (
    "tok", "cot", "gains", "weights",
    "block_out", "input_grad", "gain_sums", "mine", "theirs", "n1_held", "slot0", "slot1", "slot2", "slot3",
    "w0", "w1", "w2", "w3", "seq_a", "seq_b", "du", "act", "c_all", "gated", "mixed", "resid", "dresid", "total",
    "pair", "near", "joined", "g1", "g2", "g3", "stage", "sum", "tail", "outgoing", "tap_sums", "gain_in", "gain_line",
    "held", "loaded", "send_x", "recv_x", "send_z", "recv_z", "send_s", "recv_s", "send_c", "recv_c", "credit",
    "halo_send", "halo_recv", "send_g", "recv_g", "fetched", "fetches", "stored", "send_o", "recv_o",
    "send_a", "recv_a", "send_l", "recv_l",
)


def column_pieces(half):
    pieces = [(m * QUARTER + half * HALF_Q, m * HALF_Q, HALF_Q, 0) for m in range(4)]
    for k, (start, units) in enumerate(zip(UNIT_STARTS, UNIT_CHUNKS), 1):
        real = min(units, HALF_F - start)
        for m in range(3):
            first = 4 * QUARTER + m * UNITS + half * HALF_F + start
            pieces.append((first, STARTS[k] + m * units, real, units - real))
    return pieces


def block_kernel(layers, rows, *all_refs):
    r = dict(zip(REFS, all_refs, strict=True))
    tok, cot, gains = r["tok"], r["cot"], r["gains"]
    seq_a, seq_b, du, act = r["seq_a"], r["seq_b"], r["du"], r["act"]
    c_all, gated, mixed, total = r["c_all"], r["gated"], r["mixed"], r["total"]
    weights = (r["w0"], r["w1"], r["w2"], r["w3"])
    seg = tok.shape[0]
    _, shard, inner, _ = place()
    outer, at = line()
    me = 2 * shard + inner
    my_rows = aligned(me * seg, seg)
    chunks = list(zip(range(1, 1 + len(UNIT_CHUNKS)), UNIT_STARTS, UNIT_CHUNKS))
    gather = Gather(
        layers, rows, r["g1"], weights, r["send_x"], r["recv_x"], r["send_z"], r["recv_z"]
    )
    reduce = Reduce(
        layers, rows, (r["w2"], r["g1"], r["g2"], r["g3"]), (r["slot0"], r["slot1"], r["slot2"], r["slot3"]),
        r["stage"], r["w1"], r["sum"], r["outgoing"], r["mine"], r["theirs"],
        (r["send_g"], r["recv_g"], r["fetched"], r["fetches"], r["stored"], r["send_o"], r["recv_o"]),
    )

    def spread(buf, n):
        return Spread(buf, seg, SPREAD_SPLITS[n], r["send_s"].at[n], r["recv_s"].at[n])

    def collect(part, n):
        sems = r["send_c"].at[n], r["recv_c"].at[n]
        return Collect(part, seg, COLLECT_SPLITS[n], total, r["pair"], r["near"], r["joined"], *sems)

    one, up, two, three = spread(seq_a, 0), spread(seq_b, 1), spread(seq_a, 2), spread(seq_a, 3)
    branch, down, feed, inputs = collect(seq_a, 0), collect(seq_b, 1), collect(du, 2), collect(seq_a, 3)
    lanes = lax.broadcasted_iota(jnp.int32, (seg, WIDE), 1) < HALF_Q
    taps = pltpu.roll(gains[...], lax.rem(D - shard * QUARTER - inner * HALF_Q, D), 1)[2:5, :WIDE]
    kept = pl.ds(D, WIDE)
    sums, tap_sums = r["gain_sums"], r["tap_sums"]

    def block(t):
        return aligned(t * seg, seg)

    def mine(part):
        return pl.ds(pl.multiple_of(me * seg + part.start, 16), part.size)

    def first_norm():
        def rows(part, _):
            values = tok[part].astype(F32)
            seq_a[mine(part)] = (values * norm_scale(values) * gains[0:1, :]).astype(BF16)
            return 0

        by_rows(seg, rows)

    def up_start():
        seq_b[my_rows] = cot[...]
        up.start()

    def held():
        return pltpu.make_async_copy(seq_a, r["n1_held"], r["held"])

    def reload():
        return pltpu.make_async_copy(r["n1_held"], seq_b, r["held"])

    def project(s):
        for i in (0, 1):
            parts = dot(seq_a[block(2 * s + i)], weights[0][...])
            b = jnp.where(lanes, parts[:, :WIDE], 0.0)
            c = pltpu.roll(parts[:, 128 : 128 + 384], 384 - 64, 1)[:, :WIDE]
            x = parts[:, 384 : 384 + WIDE]
            c_all[s, pl.ds(i * seg, seg)] = jnp.where(lanes, c, 0.0)
            gated[s, pl.ds(8 + i * seg, seg)] = (b * x).astype(BF16).astype(F32)

    def ahead():
        return remote(
            gated.at[:, pl.ds(2 * seg, 8)], gated.at[:, pl.ds(0, 8)], r["halo_send"].at[0], r["halo_recv"].at[0], at(1)
        )

    def halo():
        pl.when(outer < layers - 1)(lambda: ahead().start())

        @pl.when(outer == 0)
        def _():
            gated[:, pl.ds(0, 8)] = jnp.zeros((GROUPS, 8, WIDE), F32)

    def convolved(s, i):
        return (
            taps[0:1, :] * gated[s, pl.ds(6 + i * seg, seg)]
            + taps[1:2, :] * gated[s, pl.ds(7 + i * seg, seg)]
            + taps[2:3, :] * gated[s, pl.ds(8 + i * seg, seg)]
        )

    def convolve(t):
        for i in (0, 1):

            @pl.when(t % 2 == i)
            def _():
                s = t // 2
                mixed[block(t)] = pltpu.roll(c_all[s, pl.ds(i * seg, seg)] * convolved(s, i), 64, 1).astype(BF16)

        seq_a[block(t)] = dot_rows(mixed[block(t)], weights[0][:, pl.ds(512, WIDE)]).astype(BF16)

    def branch_end():
        branch.end()
        allow(r["credit"].at[0])

    def second_norm():
        def rows(part, _):
            values = tok[part].astype(F32) + total[part]
            r["resid"][part] = values
            seq_a[mine(part)] = (values * norm_scale(values) * gains[1:2, :]).astype(BF16)
            return 0

        by_rows(seg, rows)
        pl.semaphore_wait(r["credit"].at[0], 3)

    def hidden(k, start, units, t):
        ref, here = weights[k], block(t)
        gate = dot(seq_a[here], ref[:, pl.ds(0, units)])
        upval = dot(seq_a[here], ref[:, pl.ds(units, units)])
        dact = dot(seq_b[here], ref[:, pl.ds(2 * units, units)])
        sigma = jax.nn.sigmoid(gate)
        silu = gate * sigma
        act[here, pl.ds(start, units)] = (silu * upval).astype(BF16)
        dgate = dact * upval * sigma * (1.0 + gate * (1.0 - sigma))
        du[here, pl.ds(2 * start, units)] = dgate.astype(BF16)
        du[here, pl.ds(2 * start + units, units)] = (dact * silu).astype(BF16)

    def slice_of(n):
        return jnp.where(outer < layers // 2, D // SLICE - 1 - n, n)

    def gate_up_grads(k, start, units, n):
        part = slice_of(n)
        left = seq_a[:, aligned(part * SLICE, SLICE, 128)]
        reduce.grads[k][aligned(part * SLICE, SLICE), pl.ds(0, 2 * units)] = dot_columns(
            left, du[:, pl.ds(2 * start, 2 * units)]
        ).astype(BF16)

    def down_grads(k, start, units, n):
        part = slice_of(n)
        left = seq_b[:, aligned(part * SLICE, SLICE, 128)]
        reduce.grads[k][aligned(part * SLICE, SLICE), pl.ds(2 * units, units)] = dot_columns(
            left, act[:, pl.ds(start, units)]
        ).astype(BF16)

    def grads(k, start, units, n):
        gate_up_grads(k, start, units, n)
        down_grads(k, start, units, n)
        reduce.direct(k, slice_of(n))

    def second(t):
        here = block(t)
        seq_b[here] = sum(
            dot_rows(du[here, pl.ds(2 * start, 2 * units)], weights[k][:, pl.ds(0, 2 * units)])
            for k, start, units in chunks
        ).astype(BF16)

    def down_end():
        down.end()
        reload().start()
        allow(r["credit"].at[1])

    def forward(t):
        here = block(t)
        du[here, pl.ds(0, D)] = sum(
            dot_rows(act[here, pl.ds(start, units)], weights[k][:, pl.ds(2 * units, units)])
            for k, start, units in chunks
        ).astype(BF16)

    def second_back():
        def rows(part, gain):
            dpart, dgain = norm_back(r["resid"][part], gains[1:2, :], total[part])
            dresid = cot[part].astype(F32) + dpart
            r["dresid"][part] = dresid
            seq_a[mine(part)] = dresid.astype(BF16)
            return gain + dgain

        sums[...] = jnp.zeros(sums.shape, F32)
        tap_sums[...] = jnp.zeros(tap_sums.shape, F32)
        sums[1:2, pl.ds(0, D)] = by_rows(seg, rows, jnp.zeros((1, D), F32))
        pl.semaphore_wait(r["credit"].at[1], 3)

    def mix_back(t):
        s, here = t // 2, block(t)
        dmixed = pltpu.roll(dot(seq_a[here], weights[0][:, pl.ds(512, WIDE)]), WIDE - 64, 1)
        dmixed = jnp.where(lanes, dmixed, 0.0)
        for i in (0, 1):

            @pl.when(t % 2 == i)
            def _():
                du[here, kept] = (dmixed * convolved(s, i)).astype(BF16)
                c_all[s, pl.ds(i * seg, seg)] = dmixed * c_all[s, pl.ds(i * seg, seg)]

    def after():
        return remote(
            c_all.at[:, pl.ds(0, 8)], c_all.at[:, pl.ds(2 * seg, 8)], r["halo_send"].at[1], r["halo_recv"].at[1], at(-1)
        )

    def halo_back():
        pl.when(outer > 0)(lambda: after().start())

        @pl.when(outer == layers - 1)
        def _():
            c_all[:, pl.ds(2 * seg, 8)] = jnp.zeros((GROUPS, 8, WIDE), F32)

    def conv_back(n):
        for i in (0, 1):
            pl.when(n // GROUPS == i)(functools.partial(conv_back_half, n % GROUPS, i))

    def conv_back_half(s, i):
        t = block(2 * s + i)
        dconv = c_all[s, pl.ds(i * seg, seg)]
        dgated = (
            taps[2:3, :] * dconv
            + taps[1:2, :] * c_all[s, pl.ds(1 + i * seg, seg)]
            + taps[0:1, :] * c_all[s, pl.ds(2 + i * seg, seg)]
        )
        parts = dot(seq_b[t], weights[0][:, pl.ds(0, 640)])
        db = dgated * parts[:, 384:640]
        dx = dgated * parts[:, :WIDE]
        dc = jnp.concatenate([du[t, kept].astype(F32), jnp.zeros((seg, 128), F32)], axis=1)
        dc = pltpu.roll(dc, 64, 1)
        act[t, pl.ds(0, 128)] = db[:, :128].astype(BF16)
        act[t, pl.ds(128, 128)] = (db[:, 128:] + dc[:, :128]).astype(BF16)
        act[t, pl.ds(256, 128)] = dc[:, 128:256].astype(BF16)
        act[t, pl.ds(384, WIDE)] = dx.astype(BF16)
        act[t, pl.ds(640, 128)] = jnp.zeros((seg, 128), BF16)
        for k in range(3):
            moved = gated[s, pl.ds(6 + k + i * seg, seg)]
            tap_sums[k : k + 1] = tap_sums[k : k + 1] + jnp.sum(dconv * moved, axis=0, keepdims=True)

    def conv_grads(n):
        part = slice_of(n)
        held_rows, cols = aligned(part * SLICE, SLICE), aligned(part * SLICE, SLICE, 128)
        ref = reduce.grads[0]
        of_parts = dot_columns(seq_b[:, cols], act[:, pl.ds(0, CONV_COLS)])
        ref[held_rows, pl.ds(0, 512)] = of_parts[:, :512].astype(BF16)
        of_mixed = dot_columns(seq_a[:, cols], mixed[...])
        ref[held_rows, pl.ds(512, WIDE)] = (of_parts[:, 512:] + of_mixed).astype(BF16)
        reduce.direct(0, part)

    def feed_end():
        feed.end()
        allow(r["credit"].at[2])
        r["block_out"][...] = (r["resid"][...] + total[...]).astype(BF16)

    def first(t):
        here = block(t)
        seq_a[here] = dot_rows(act[here, pl.ds(0, 640)], weights[0][:, pl.ds(0, 640)]).astype(BF16)

    def first_back():
        def rows(part, gain):
            dpart, dgain = norm_back(tok[part].astype(F32), gains[0:1, :], total[part])
            r["input_grad"][part] = (r["dresid"][part] + dpart).astype(BF16)
            return gain + dgain

        sums[0:1, pl.ds(0, D)] = by_rows(seg, rows, jnp.zeros((1, D), F32))
        sums[2:5, aligned(me * WIDE, WIDE, 128)] = tap_sums[0:3]

    def gains_across(n):
        return remote(sums, r["gain_in"].at[n], r["send_a"].at[n], r["recv_a"].at[n], partners()[n])

    def gains_add(n):
        gains_across(n).wait()
        sums[...] = sums[...] + r["gain_in"][n]

    def line_copy(sign, steps):
        slot = (0 if sign > 0 else 1, steps - 1)
        return remote(
            sums, r["gain_line"].at[slot], r["send_l"].at[slot], r["recv_l"].at[slot], at(sign * steps)
        )

    def gains_line():
        for steps in range(1, layers):
            for sign in (1, -1):
                pl.when(in_line(outer + sign * steps, layers))(line_copy(sign, steps).start)

    def gains_end():
        for steps in range(1, layers):
            for sign in (1, -1):
                pl.when(in_line(outer + sign * steps, layers))(line_copy(sign, steps).wait_send)
                pl.when(in_line(outer - sign * steps, layers))(line_copy(sign, steps).wait_recv)

        own_sums = sums[...]
        for origin in range(layers):
            for steps in range(1, layers):
                for sign in (1, -1):

                    @pl.when((outer - sign * steps == origin))
                    def _():
                        came = r["gain_line"][0 if sign > 0 else 1, steps - 1]
                        sums[...] = came if origin == 0 else sums[...] + came

            if origin > 0:

                @pl.when(outer == origin)
                def _():
                    sums[...] = sums[...] + own_sums

    def end():
        reduce.finish(0)
        for k in range(len(WIDTHS)):
            reduce.wait_sent(k)
        pl.when(outer < layers - 1)(lambda: ahead().wait_send())
        pl.when(outer > 0)(lambda: after().wait_send())

    windows = [
        (r["resid"], 0, D), (r["dresid"], D, D), (total, 2 * D, D), (r["resid"], 3 * D, D),
        (r["tail"], 4 * D, GROUP_COLS - 4 * D),
    ]

    def load(n):
        ref, first, width = windows[n]
        return pltpu.make_async_copy(
            r["weights"].at[:, pl.ds(first, width)], ref.at[pl.ds(0, rows)], r["loaded"].at[n]
        )

    def start():
        for n in (0, 1, 2, 4):
            load(n).start()
        greet(layers)
        load(0).wait()
        cut(0)
        load(3).start()
        greeted(layers)

    def cut(k):
        def read(part, first, width):
            found = []
            for n, (ref, low, size) in enumerate(windows):
                start, stop = max(first, low), min(first + width, low + size)
                if start < stop and (n == 0) == (k == 0):
                    found.append(ref[part, start - low : stop - low])
            return found

        size = band(rows, 96)

        def cut_band(n, _):
            part = aligned(n * size, size)
            halves = []
            for half in (0, 1):
                pieces = []
                for first, own, width, padding in column_pieces(half):
                    if STARTS[k] <= own < STARTS[k] + WIDTHS[k]:
                        pieces += read(part, first, width)
                        if padding:
                            pieces.append(jnp.zeros((size, padding), F32))
                halves.append(jnp.concatenate(pieces, axis=1))
            is_low = inner == 0
            seq = lax.axis_index("seq")
            own_rows = aligned(seq * rows + n * size, size)
            weights[k][own_rows, :] = jnp.where(is_low, halves[0], halves[1]).astype(BF16)
            gather.other_rows(k)[part, :] = jnp.where(is_low, halves[1], halves[0]).astype(BF16)
            return 0

        for n in (1, 2, 3, 4) if k == CUT_FIRST else ():
            load(n).wait()
        lax.fori_loop(0, rows // size, cut_band, 0)

    def hold():
        held().start()

    def hold_end():
        held().wait()

    def halo_end():
        pl.when(outer > 0)(lambda: ahead().wait_recv())

    def reload_end():
        reload().wait()

    def halo_back_end():
        pl.when(outer < layers - 1)(lambda: after().wait_recv())

    def feed_credit():
        pl.semaphore_wait(r["credit"].at[2], 3)

    def from_spread(moved, body):
        def step(n):
            for m in range(8):
                if moved.before(m):

                    @pl.when(n == m)
                    def _():
                        for act in moved.before(m):
                            act()

            body(moved.index(n))

        return step

    def each(body, *cases):
        return [functools.partial(body, *(case if isinstance(case, tuple) else (case,))) for case in cases]

    every = range(len(WIDTHS))
    cuts = each(cut, *every)
    exchange, send_own, send_other = (
        each(body, *every) for body in (gather.exchange, gather.send_own, gather.send_other)
    )
    step = [each(gather.steps, (k, 1, 1), (k, 2, 2), (k, 3)) for k in every]
    join_far = each(reduce.join, *((k, layers - 2, 2) for k in every))
    join_near = each(reduce.join, *((k, 1, 1) for k in every))
    final = each(reduce.final, (0, 3), 1, (2, 1), (3, 2))
    feed_pair = each(feed.add_pair, 0, 1, 2)
    gain_send = [lambda n=n: gains_across(n).start() for n in range(3)]
    gain_add = each(gains_add, 0, 1, 2)
    d3_far = functools.partial(reduce.direct, 3, least=2)
    d3_near = functools.partial(reduce.direct, 3, most=1)
    blocks, parts = 2 * GROUPS, D // SLICE
    proj = Loop(GROUPS, project)
    mix = Loop(blocks, lambda n: branch.make(n, convolve))
    hid1 = Loop(blocks, from_spread(two, functools.partial(hidden, *chunks[0])))
    hid2, hid3 = (Loop(blocks, functools.partial(hidden, *chunk)) for chunk in chunks[1:])
    grad1, grad2 = (Loop(parts, functools.partial(grads, *chunk)) for chunk in chunks[:2])
    down3 = Loop(parts, functools.partial(down_grads, *chunks[2]))
    back2 = Loop(blocks, lambda n: down.make(n, second))
    gate3 = Loop(parts, functools.partial(gate_up_grads, *chunks[2]))
    ffn = Loop(blocks, forward)
    back_mix = Loop(blocks, from_spread(three, mix_back))
    back_conv = Loop(blocks, conv_back)
    grad0 = Loop(parts, conv_grads)
    back1 = Loop(blocks, lambda n: inputs.make(n, first))
    play(
        [
            start, send_own[0], exchange[0], cuts[1], first_norm, one.start, exchange[1], send_other[0], step[0][0],
            cuts[3], one.first, cuts[2], step[0][1], up_start, send_own[1], one.near, one.far, step[0][2], one.end,
            hold, proj[0], proj[1], exchange[3], hold_end, proj[2], proj[3], up.first, halo, exchange[2],
            send_other[1], halo_end, mix[0], step[1][0], mix[1], up.near, mix[2], mix[3], mix[4], up.far, up.end,
            mix[5], send_other[2], step[1][1], mix[6], send_own[2], mix[7], branch_end, second_norm, two.start,
            step[1][2], send_own[3], hid1[0], hid1[1], hid1[2], hid1[3], send_other[3], step[2][0], hid1[4],
            hid1[5], hid1[6], hid1[7], two.sent, gather.crossed, grad1[0], grad1[1], step[2][1], grad1[2],
            step[2][2], grad1[3], hid2[0], hid2[1], hid2[2], hid2[3], step[3][0], hid2[4], hid2[5], hid2[6],
            hid2[7], join_far[1], grad2[0], grad2[1], grad2[2], grad2[3], step[3][1], step[3][2], hid3[0], hid3[1],
            hid3[2], hid3[3], hid3[4], hid3[5], hid3[6], hid3[7], down3[0], down3[1], down3[2], down3[3], back2[0],
            back2[1], back2[2], back2[3], back2[4], back2[5], back2[6], back2[7], gate3[0], join_near[1],
            join_far[2], gate3[1], gather.finish, gate3[2], gate3[3], down_end, second_back, three.start, ffn[0],
            ffn[1], ffn[2], ffn[3], ffn[4], ffn[5], ffn[6], ffn[7], back_mix[0], d3_far, back_mix[1], feed.push,
            join_near[2], back_mix[2], back_mix[3], reload_end, feed_pair[0], back_mix[4], feed_pair[1],
            back_mix[5], back_mix[6], feed_pair[2], back_mix[7], three.sent, halo_back, back_conv[0], back_conv[1],
            back_conv[2], d3_near, back_conv[3], feed.pass_on, join_far[3], feed.add_own, final[1], halo_back_end,
            back_conv[4], back_conv[5], back_conv[6], join_near[3], back_conv[7], grad0[0], grad0[1], grad0[2],
            grad0[3], feed_end, feed_credit, back1[0], back1[1], back1[2], back1[3], back1[4], join_far[0],
            back1[5], back1[6], final[2], back1[7], join_near[0], inputs.end, first_back, gain_send[0], final[3],
            gain_add[0], gain_send[1], gain_add[1], gain_send[2], gain_add[2], gains_line, final[0], gains_end, end,
        ]
    )


class Loop:
    def __init__(self, count, body):
        self.count, self.body = count, body

    def __getitem__(self, n):
        return (self, n)


def play(order):
    order = list(order)
    while order:
        entry = order.pop(0)
        if not isinstance(entry, tuple):
            entry()
            continue
        loop, _ = entry
        between = {}
        for n in range(1, loop.count):
            between[n] = []
            while order[0] != (loop, n):
                between[n].append(order.pop(0))
            order.pop(0)

        def turn(n, _):
            for m, acts in between.items():
                if acts:

                    @pl.when(n == m)
                    def _():
                        play(acts)

            loop.body(n)
            return 0

        lax.fori_loop(0, loop.count, turn, 0)


def block_step(tok, cot, gains, weights, layers):
    rows, seg = weights.shape[0], tok.shape[0]
    count = len(WIDTHS)
    tokens = 2 * GROUPS * seg
    vmem, anywhere = pl.BlockSpec(memory_space=pltpu.VMEM), pl.BlockSpec(memory_space=pl.ANY)
    shape, scratch = jax.ShapeDtypeStruct, pltpu.VMEM
    dma, regular = pltpu.SemaphoreType.DMA, pltpu.SemaphoreType.REGULAR
    hops = layers - 1
    wide, biggest = sum(WIDTHS), max(WIDTHS)
    out_shape = [
        shape((seg, D), BF16),
        shape((seg, D), BF16),
        shape((8, 2 * GROUPS * WIDE), F32),
        shape((rows, wide), F32),
        shape((rows, wide), BF16),
        shape((tokens, D), BF16),
    ] + [shape((2, hops, 2 * rows, width), BF16) for width in WIDTHS]
    scratch_shapes = (
        [scratch((D, width), BF16) for width in WIDTHS]
        + [
            scratch((tokens, D), BF16),
            scratch((tokens, D), BF16),
            scratch((tokens, 2 * PAD_F), BF16),
            scratch((tokens, PAD_F), BF16),
            scratch((GROUPS, 8 + 2 * seg, WIDE), F32),
            scratch((GROUPS, 8 + 2 * seg, WIDE), F32),
            scratch((tokens, WIDE), BF16),
            scratch((seg, D), F32),
            scratch((seg, D), F32),
            scratch((seg, D), F32),
            scratch((4, seg, D), BF16),
            scratch((2, seg, D), BF16),
            scratch((seg, D), BF16),
        ]
        + [scratch((D, width), BF16) for width in WIDTHS[1:]]
        + [
            scratch((2 * rows, biggest), BF16),
            scratch((rows, biggest), F32),
            scratch((rows, GROUP_COLS - 4 * D), F32),
            scratch((rows, wide), BF16),
            scratch((8, WIDE), F32),
            scratch((3, 8, 2 * GROUPS * WIDE), F32),
            scratch((2, hops, 8, 2 * GROUPS * WIDE), F32),
            dma,
            dma((5,)),
            dma((count,)),
            dma((count,)),
            dma((count, 2, hops, 2)),
            dma((count, 2, hops, 2)),
            dma((4, 11)),
            dma((4, 11)),
            dma((4, 10)),
            dma((4, 10)),
            regular((3,)),
            dma((2,)),
            dma((2,)),
            dma((count, 2, hops)),
            dma((count, 2, hops)),
            dma,
            dma((4,)),
            dma((count,)),
            dma((count,)),
            dma((count,)),
            dma((3,)),
            dma((3,)),
            dma((2, hops)),
            dma((2, hops)),
        ]
    )
    return pl.pallas_call(
        functools.partial(block_kernel, layers, rows),
        out_shape=out_shape,
        in_specs=[vmem] * 3 + [anywhere],
        out_specs=[vmem] * 3 + [anywhere] * (3 + count),
        scratch_shapes=scratch_shapes,
        compiler_params=pltpu.CompilerParams(
            collective_id=0, has_side_effects=True, vmem_limit_bytes=VMEM_BYTES
        ),
        name="block_step",
    )(tok, cot, gains, weights)[:5]


def band(rows, most):
    return max(size for size in range(16, most + 1, 16) if rows % size == 0)


def adam_update(param, grad, first, second, rate, decay):
    first_new = MOMENT_DECAY * first + (1.0 - MOMENT_DECAY) * grad
    second_new = SQUARE_DECAY * second + (1.0 - SQUARE_DECAY) * grad * grad
    root = jnp.sqrt(second_new * (1.0 / (1.0 - SQUARE_DECAY**STEP))) + ADAM_EPSILON
    step = first_new * (rate / (1.0 - MOMENT_DECAY**STEP)) / root
    return (first_new, second_new, param * (1.0 - rate * decay) - step)


def update_kernel(
    inner_ref, mine_ref, theirs_ref, weights_ref, first_ref, second_ref, sums_ref, gains_ref, gains_first_ref,
    gains_second_ref, block_ref, input_ref, grad_out, first_out, second_out, weights_out, gains_grad_out,
    gains_first_out, gains_second_out, gains_out, block_out, input_out,
):
    is_low = inner_ref[0] == 0
    mine, theirs = mine_ref[...], theirs_ref[...].astype(F32)
    for half in (0, 1):
        chosen = jnp.where(is_low, mine, theirs) if half == 0 else jnp.where(is_low, theirs, mine)
        for first, own, width, _ in column_pieces(half):
            grad_out[:, first : first + width] = chosen[:, own : own + width]
    first_out[...], second_out[...], weights_out[...] = adam_update(
        weights_ref[...], grad_out[...], first_ref[...], second_ref[...], WEIGHT_RATE, WEIGHT_DECAY
    )

    @pl.when(pl.program_id(0) == 0)
    def _():
        gains_grad_out[0:2] = sums_ref[0:2, :D]
        for n in range(2 * GROUPS):
            gains_grad_out[2:5, n * HALF_Q : (n + 1) * HALF_Q] = sums_ref[2:5, n * WIDE : n * WIDE + HALF_Q]
        gains_first_out[...], gains_second_out[...], gains_out[...] = adam_update(
            gains_ref[...], gains_grad_out[...], gains_first_ref[...], gains_second_ref[...], GAIN_RATE, 0.0
        )
        block_out[...] = block_ref[...]
        input_out[...] = input_ref[...]


def update(inner, mine, theirs, weights, first, second, sums, gains, gains_first, gains_second, block, grad):
    rows, cols = weights.shape
    wide = mine.shape[1]
    size = band(rows, 32)
    by_row = lambda width: pl.BlockSpec((size, width), lambda n: (n, 0))
    whole = lambda values: pl.BlockSpec(values.shape, lambda n: (0, 0))
    shape = jax.ShapeDtypeStruct
    return pl.pallas_call(
        update_kernel,
        grid=(rows // size,),
        out_shape=[shape((rows, cols), F32)] * 4 + [shape(gains.shape, F32)] * 4 + [shape(block.shape, BF16)] * 2,
        in_specs=[pl.BlockSpec(memory_space=pltpu.SMEM)]
        + [by_row(wide)] * 2
        + [by_row(cols)] * 3
        + [whole(sums)]
        + [whole(gains)] * 3
        + [whole(block)] * 2,
        out_specs=[by_row(cols)] * 4 + [whole(gains)] * 4 + [whole(block)] * 2,
        compiler_params=pltpu.CompilerParams(vmem_limit_bytes=VMEM_BYTES),
        name="update",
    )(inner, mine, theirs, weights, first, second, sums, gains, gains_first, gains_second, block, grad)


def on_device(
    tokens, gains_taps, weights, cotangent, weight_first, weight_second, gains_first, gains_second
):
    layers = lax.axis_size("seq") // 2
    inner_word = (lax.axis_index("seq") % 2).astype(jnp.int32).reshape(1)
    block_out, input_grad, gain_sums, mine, theirs = block_step(
        tokens[0], cotangent[0], gains_taps, weights, layers
    )
    (
        weight_grad, weight_first_new, weight_second_new, weight_new,
        gains_grad, gains_first_new, gains_second_new, gains_new, block_out, input_grad,
    ) = update(
        inner_word, mine, theirs, weights, weight_first, weight_second,
        gain_sums, gains_taps, gains_first, gains_second, block_out, input_grad,
    )
    return (
        block_out[None],
        input_grad[None],
        weight_grad,
        weight_first_new,
        weight_second_new,
        weight_new,
        gains_grad,
        gains_first_new,
        gains_second_new,
        gains_new,
    )


def solution(mesh):
    tokens, rows, whole = P("shard", "seq", None), P("seq", "shard"), P()
    return jax.shard_map(
        on_device,
        mesh=mesh,
        in_specs=(tokens, whole, rows, tokens, rows, rows, whole, whole),
        out_specs=(tokens, tokens, rows, rows, rows, rows, whole, whole, whole, whole),
        check_vma=False,
    )
```

```python
import functools

import jax
import jax.numpy as jnp
from jax import lax
from jax.experimental import pallas as pl
from jax.experimental.pallas import tpu as pltpu
from jax.sharding import PartitionSpec as P

D = 1536
FF = 6912
STEP = 10
GROUPS = 4
QUARTER = D // GROUPS
UNITS = FF // GROUPS
GROUP_COLS = 4 * QUARTER + 3 * UNITS
HALF_Q = QUARTER // 2
HALF_F = UNITS // 2
LANES = 128
PAD_F = -(-HALF_F // LANES) * LANES
WIDE = 256
CONV_COLS = 4 * HALF_Q
UNIT_CHUNKS = (384, 256, PAD_F - 640)
UNIT_STARTS = (0, 384, 640)
WIDTHS = (CONV_COLS,) + tuple(3 * units for units in UNIT_CHUNKS)
STARTS = tuple(sum(WIDTHS[:k]) for k in range(len(WIDTHS)))
SPREAD_SPLITS = (176, 208, 112, 128)
COLLECT_SPLITS = (80, 128, 64, 96)
SUM_WIDTHS = (384,) + WIDTHS[1:] + (CONV_COLS - 384,)
SUM_FIRST = (0,) * len(WIDTHS) + (384,)
SUM_STARTS = STARTS + (384,)
REACH = (1, 1, 1, 1)
CUT_FIRST = 1
SLICE = 384
TILE = 16
ROWS = 48

MOMENT_DECAY = 0.9
SQUARE_DECAY = 0.95
ADAM_EPSILON = 1e-08
NORM_EPSILON = 1e-05
WEIGHT_RATE = 0.02
GAIN_RATE = 0.2
WEIGHT_DECAY = 0.1

BF16 = jnp.bfloat16
F32 = jnp.float32
MESH = pl.DeviceIdType.MESH
VMEM_BYTES = 63 * 1024 * 1024


def place():
    seq, shard = lax.axis_index("seq"), lax.axis_index("shard")
    inner, core = lax.rem(seq, 2), lax.rem(shard, 2)
    return seq, shard, inner, core


def partners():
    seq, shard, inner, core = place()
    across = {"seq": seq + 1 - 2 * inner, "shard": shard}
    beside = {"seq": seq, "shard": lax.rem(shard + 2, 4)}
    twin = {"seq": seq, "shard": shard + 1 - 2 * core}
    return across, beside, twin


def remote(src, dst, send, recv, device):
    return pltpu.make_async_remote_copy(
        src_ref=src, dst_ref=dst, send_sem=send, recv_sem=recv, device_id=device, device_id_type=MESH
    )


def line():
    seq, shard, _, _ = place()
    size = lax.axis_size("seq")
    return seq // 2, lambda steps: {"seq": lax.rem(seq + 2 * steps + size, size), "shard": shard}


def greet(layers):
    outer, at = line()
    barrier = pltpu.get_barrier_semaphore()
    for device in partners():
        pl.semaphore_signal(barrier, inc=1, device_id=device, device_id_type=MESH)
    for steps in range(1, layers):
        for sign in (1, -1):

            @pl.when(in_line(outer + sign * steps, layers))
            def _():
                pl.semaphore_signal(barrier, inc=1, device_id=at(sign * steps), device_id_type=MESH)


def greeted(layers):
    pl.semaphore_wait(pltpu.get_barrier_semaphore(), 3 + layers - 1)


def in_line(index, layers):
    return (index >= 0) & (index < layers)


def allow(credit):
    for device in partners():
        pl.semaphore_signal(credit, inc=1, device_id=device, device_id_type=MESH)


def dot(left, right):
    return jnp.dot(left, right, preferred_element_type=F32)


def dot_rows(left, right):
    return lax.dot_general(left, right, (((1,), (1,)), ((), ())), preferred_element_type=F32)


def dot_columns(left, right):
    return lax.dot_general(left, right, (((0,), (0,)), ((), ())), preferred_element_type=F32)


def aligned(start, size, multiple=16):
    return pl.ds(pl.multiple_of(start, multiple), size)


class Gather:
    def __init__(self, layers, rows, oth, outs, send_x, recv_x, send_z, recv_z):
        self.layers, self.rows, self.oth, self.outs = layers, rows, oth, outs
        self.send_x, self.recv_x, self.send_z, self.recv_z = send_x, recv_x, send_z, recv_z
        self.seq, _, self.inner, _ = place()
        self.outer, self.at = line()
        self.across = partners()[0]

    def seq_rows(self, index):
        return aligned(index * self.rows, self.rows)

    def layer_rows(self, direction, distance):
        origin = self.outer - distance if direction == 0 else self.outer + distance
        return aligned(origin * 2 * self.rows, 2 * self.rows)

    def copy(self, k, src, dst, direction, distance, hop, piece):
        slot = (k, direction, distance + hop - 1, piece)
        return remote(
            src, dst, self.send_z.at[slot], self.recv_z.at[slot], self.at(hop if direction == 0 else -hop)
        )

    def goes(self, direction, hop):
        return in_line(self.outer + (hop if direction == 0 else -hop), self.layers)

    def has_come(self, direction, distance):
        return in_line(self.outer + (-distance if direction == 0 else distance), self.layers)

    def hops(self, k, distance):
        return range(1, min(REACH[k], self.layers - 1 - distance) + 1)

    def own_copy(self, k, direction, hop):
        here = self.outs[k].at[self.seq_rows(self.seq)]
        return self.copy(k, here, here, direction, 0, hop, 0)

    def other_copy(self, k, direction, hop):
        there = self.outs[k].at[self.seq_rows(self.seq + 1 - 2 * self.inner)]
        return self.copy(k, there, there, direction, 0, hop, 1)

    def pass_copy(self, k, direction, distance, hop):
        ref = self.outs[k].at[self.layer_rows(direction, distance)]
        return self.copy(k, ref, ref, direction, distance, hop, 0)

    def other_rows(self, k):
        return self.oth.at[pl.ds(k * self.rows, self.rows), pl.ds(0, WIDTHS[k])]

    def exchange(self, k):
        self.x_copy(k).start()

    def x_copy(self, k):
        here = self.outs[k].at[self.seq_rows(self.seq)]
        return remote(self.other_rows(k), here, self.send_x.at[k], self.recv_x.at[k], self.across)

    def crossed(self):
        for k in range(len(self.outs)):
            self.x_copy(k).wait_send()

    def send_own(self, k):
        for hop in self.hops(k, 0):
            for direction in (0, 1):

                @pl.when(self.goes(direction, hop))
                def _():
                    self.own_copy(k, direction, hop).start()

    def send_other(self, k):
        self.x_copy(k).wait_recv()
        for hop in self.hops(k, 0):
            for direction in (0, 1):

                @pl.when(self.goes(direction, hop))
                def _():
                    self.other_copy(k, direction, hop).start()

    def step(self, k, distance):
        for direction in (0, 1):

            @pl.when(self.has_come(direction, distance))
            def _():
                if distance <= REACH[k]:
                    origin = self.outer - distance if direction == 0 else self.outer + distance
                    for piece in (0, 1):
                        index = 2 * origin + (self.inner if piece == 0 else 1 - self.inner)
                        ref = self.outs[k].at[self.seq_rows(index)]
                        self.copy(k, ref, ref, direction, distance - 1, 1, piece).wait_recv()
                else:
                    ref = self.outs[k].at[self.layer_rows(direction, distance)]
                    self.copy(k, ref, ref, direction, distance - 1, 1, 0).wait_recv()
                if distance % REACH[k] == 0:
                    for hop in self.hops(k, distance):

                        @pl.when(self.goes(direction, hop))
                        def _():
                            self.pass_copy(k, direction, distance, hop).start()

    def steps(self, k, first, last=None):
        last = self.layers - 1 if last is None else min(last, self.layers - 1)
        for distance in range(first, last + 1):
            self.step(k, distance)

    def finish(self):
        for k in range(len(self.outs)):
            for distance in range(0, self.layers - 1, REACH[k]):
                for hop in self.hops(k, distance):
                    for direction in (0, 1):

                        @pl.when(self.goes(direction, hop) & self.has_come(direction, distance))
                        def _():
                            if distance == 0:
                                self.own_copy(k, direction, hop).wait_send()
                                self.other_copy(k, direction, hop).wait_send()
                            else:
                                self.pass_copy(k, direction, distance, hop).wait_send()


class Reduce:
    def __init__(self, layers, rows, grads, slots, stage, spare, total, outgoing, mine, theirs, sems):
        self.layers, self.rows, self.grads, self.slots = layers, rows, grads, slots
        self.stage, self.spare, self.total, self.outgoing = stage, spare, total, outgoing
        self.mine, self.theirs = mine, theirs
        self.send_g, self.recv_g, self.fetched, self.fetches, self.stored, self.send_o, self.recv_o = sems
        _, _, self.inner, _ = place()
        self.outer, self.at = line()
        self.across = partners()[0]

    def owner(self, direction, distance):
        return self.outer + distance if direction == 0 else self.outer - distance

    def upstream(self, direction, steps):
        return in_line(self.outer - steps if direction == 0 else self.outer + steps, self.layers)

    def block(self, k, owner):
        return self.grads[k].at[aligned(owner * 2 * self.rows, 2 * self.rows), self.own_cols(k)]

    def own_cols(self, k):
        return pl.ds(SUM_FIRST[k], SUM_WIDTHS[k])

    def copy(self, k, src, direction, distance):
        slot = (direction, distance - 1)
        return remote(
            src,
            self.slots[k].at[slot],
            self.send_g.at[(k,) + slot],
            self.recv_g.at[(k,) + slot],
            self.at(1 if direction == 0 else -1),
        )

    def send(self, k, direction, distance):
        self.copy(k, self.block(k, self.owner(direction, distance)), direction, distance).start()

    def direct(self, k, part=None, least=1, most=None):
        for distance in range(most or self.layers - 1, least - 1, -1):
            for direction in (0, 1):
                owner = self.owner(direction, distance)
                here = in_line(owner, self.layers) & jnp.logical_not(self.upstream(direction, 1))
                if part is not None:
                    here = here & (owner * 2 * self.rows // SLICE == part)

                @pl.when(here)
                def _():
                    self.send(k, direction, distance)

    def fetch(self, k, direction, distance):
        slot = self.slots[k].at[direction, distance - 1]
        self.copy(k, slot, direction, distance).wait_recv()
        held = self.stage.at[:, pl.ds(0, SUM_WIDTHS[k])]
        copy = pltpu.make_async_copy(slot, held, self.fetched)
        copy.start()
        copy.wait()

    def tiles(self, body):
        def step(n, _):
            body(aligned(n * TILE, TILE))
            return 0

        lax.fori_loop(0, 2 * self.rows // TILE, step, 0)

    def join(self, k, most, least):
        cols = pl.ds(0, SUM_WIDTHS[k])
        for distance in range(most, least - 1, -1):
            for direction in (0, 1):
                owner = self.owner(direction, distance)

                @pl.when(in_line(owner, self.layers) & self.upstream(direction, 1))
                def _():
                    def add(tile):
                        base = self.owner(direction, distance) * 2 * self.rows
                        rows = pl.ds(pl.multiple_of(base + tile.start, 16), TILE)
                        ref = self.grads[k]
                        own_cols = self.own_cols(k)
                        ref[rows, own_cols] = (
                            ref[rows, own_cols].astype(F32) + self.stage[tile, cols].astype(F32)
                        ).astype(BF16)

                    self.fetch(k, direction, distance + 1)
                    self.tiles(add)
                    self.send(k, direction, distance)

    def final(self, k, before=None):
        cols = pl.ds(0, SUM_WIDTHS[k])
        came = [(1, 0), (1, 1)]

        def fetch(n, distance, direction):
            return pltpu.make_async_copy(
                self.slots[k].at[direction, distance - 1],
                self.spare.at[pl.ds(n * 2 * self.rows, 2 * self.rows), cols],
                self.fetches.at[n],
            )

        for n, (distance, direction) in enumerate(came):

            @pl.when(self.upstream(direction, distance))
            def _():
                self.copy(k, self.slots[k].at[direction, distance - 1], direction, distance).wait_recv()
                fetch(n, distance, direction).start()

        if before is not None:
            self.store(before).wait()

        here, there = self.inner * self.rows, (1 - self.inner) * self.rows

        def each(base, body):
            def step(n, _):
                body(base + n * TILE, n * TILE)
                return 0

            lax.fori_loop(0, self.rows // TILE, step, 0)

        for n, (distance, direction) in enumerate(came):

            @pl.when(self.upstream(direction, distance))
            def _():
                fetch(n, distance, direction).wait()

        def add_up(flags):
            def total(rows):
                own_rows = aligned(self.outer * 2 * self.rows + rows, TILE)
                value = self.grads[k][own_rows, self.own_cols(k)].astype(F32)
                for n, flag in enumerate(flags):
                    if flag:
                        value = value + self.spare[aligned(n * 2 * self.rows + rows, TILE), cols].astype(F32)
                return value

            def send(rows, at):
                self.outgoing[aligned(at, TILE), pl.ds(SUM_STARTS[k], SUM_WIDTHS[k])] = total(rows).astype(BF16)

            def keep(rows, at):
                self.total[aligned(at, TILE), cols] = total(rows)

            each(there, send)
            self.over(k).start()
            each(here, keep)
            self.store(k).start()

        patterns = {}
        for place_in_line in range(self.layers):
            flags = tuple(
                0 <= (place_in_line - distance if direction == 0 else place_in_line + distance) < self.layers
                for distance, direction in came
            )
            patterns.setdefault(flags, []).append(place_in_line)
        for flags, places in patterns.items():
            here_now = functools.reduce(jnp.logical_or, [self.outer == p for p in places])

            @pl.when(here_now)
            def _():
                add_up(flags)

    def over(self, k):
        wide = pl.ds(SUM_STARTS[k], SUM_WIDTHS[k])
        return remote(
            self.outgoing.at[:, wide], self.theirs.at[:, wide], self.send_o.at[k], self.recv_o.at[k], self.across
        )

    def store(self, k):
        return pltpu.make_async_copy(
            self.total.at[:, pl.ds(0, SUM_WIDTHS[k])], self.mine.at[:, pl.ds(SUM_STARTS[k], SUM_WIDTHS[k])], self.stored.at[k]
        )

    def wait_sent(self, k):
        for distance in range(1, self.layers):
            for direction in (0, 1):
                owner = self.owner(direction, distance)

                @pl.when(in_line(owner, self.layers))
                def _():
                    self.copy(k, self.block(k, owner), direction, distance).wait_send()

    def finish(self, before):
        self.store(before).wait()
        for k in range(len(self.grads)):
            self.over(k).wait()


class Spread:
    slots = range(11)

    def __init__(self, buf, seg, split, send, recv):
        self.buf, self.seg, self.split, self.send, self.recv = buf, seg, split, send, recv

    def index(self, n):
        _, shard, inner, core = place()
        row, flip, other = (n // 2) % 2, n // 4, n % 2
        return 2 * (lax.rem(shard + 2 * row, 4) + other * (1 - 2 * core)) + inner + flip * (1 - 2 * inner)

    def copy(self, slot):
        across, beside, twin = partners()
        low, high, whole = (0, self.split), (self.split, self.seg - self.split), (0, self.seg)
        n, (first, size), device = {
            0: (0, low, across),
            9: (0, high, across),
            1: (0, high, beside),
            10: (0, low, beside),
            2: (0, whole, twin),
            3: (4, low, beside),
            4: (4, whole, twin),
            5: (2, high, across),
            6: (2, whole, twin),
            7: (6, low, twin),
            8: (6, high, twin),
        }[slot]
        ref = self.buf.at[aligned(self.index(n) * self.seg + first, size)]
        return remote(ref, ref, self.send.at[slot], self.recv.at[slot], device)

    def push(self, *slots):
        for slot in slots:
            self.copy(slot).start()

    def came(self, *slots):
        for slot in slots:
            self.copy(slot).wait_recv()

    def start(self):
        self.push(0, 1, 9, 10, 2)

    def first(self):
        self.came(1)
        self.push(5)
        self.came(0)
        self.push(3)

    def near(self):
        self.came(10)
        self.push(6)
        self.came(9)
        self.push(4)

    def far(self):
        self.came(3)
        self.push(7)
        self.came(5)
        self.push(8)

    def sent(self):
        for slot in self.slots:
            self.copy(slot).wait_send()

    def end(self):
        self.came(2, 4, 6, 7, 8)
        self.sent()

    def before(self, n):
        return {
            1: (lambda: self.came(2),),
            2: (self.first, self.near),
            3: (lambda: self.came(6),),
            5: (lambda: self.came(4),),
            6: (self.far,),
            7: (lambda: self.came(7, 8),),
        }.get(n, ())


class Collect:
    def __init__(self, part, seg, split, total, pair, near, joined, send, recv):
        self.part, self.seg, self.total = part, seg, total
        self.pair, self.near, self.joined, self.send, self.recv = pair, near, joined, send, recv
        _, self.shard, self.inner, core = place()
        self.twin_shard = self.shard + 1 - 2 * core
        self.low, self.high, self.whole = (0, split), (split, seg - split), (0, seg)
        self.cols = pl.ds(0, D)

    def index(self, s, k):
        row, flip = 1 - k % 2, 1 - k // 2
        return 2 * lax.rem(s + 2 * row, 4) + self.inner + flip * (1 - 2 * self.inner)

    def pair_copy(self, k):
        src = self.part.at[aligned(self.index(self.twin_shard, k) * self.seg, self.seg), self.cols]
        return remote(src, self.pair.at[k], self.send.at[k], self.recv.at[k], partners()[2])

    def copy(self, slot):
        across, beside, _ = partners()
        src, dst, (first, size), device = {
            4: (self.pair.at[0], self.joined, self.low, across),
            5: (self.pair.at[0], self.joined, self.high, beside),
            6: (self.pair.at[1], self.near.at[0], self.low, across),
            7: (self.pair.at[2], self.near.at[1], self.high, beside),
            8: (self.pair.at[2], self.near.at[1], self.low, beside),
            9: (self.pair.at[1], self.near.at[0], self.high, across),
        }[slot]
        rows = pl.ds(first, size)
        return remote(src.at[rows], dst.at[rows], self.send.at[slot], self.recv.at[slot], device)

    def over(self, span, body):
        def step(n, _):
            body(aligned(span[0] + n * 16, 16))
            return 0

        lax.fori_loop(0, span[1] // 16, step, 0)

    def mine(self, k, rows):
        return self.part[aligned(self.index(self.shard, k) * self.seg + rows.start, 16), self.cols].astype(F32)

    def add_pair(self, k):
        def add(rows):
            self.pair[k, rows] = (self.mine(k, rows) + self.pair[k, rows].astype(F32)).astype(BF16)

        self.pair_copy(k).wait_recv()
        self.over(self.whole, add)
        for slot in ((4, 5), (6,), (7,))[k]:
            self.copy(slot).start()

    def add_own(self):
        def add(rows):
            self.total[rows] = self.mine(3, rows) + self.pair[3, rows].astype(F32)

        self.pair_copy(3).wait_recv()
        self.over(self.whole, add)

    def pass_on(self):
        for slot, k, span, after in ((4, 2, self.low, 8), (5, 1, self.high, 9)):

            def add(rows):
                self.pair[k, rows] = (self.pair[k, rows].astype(F32) + self.joined[rows].astype(F32)).astype(BF16)

            self.copy(slot).wait_recv()
            self.over(span, add)
            self.copy(after).start()

    def push(self):
        for k in range(4):
            self.pair_copy(k).start()

    def make(self, n, produce):
        k, own = n // 2, n % 2
        produce(self.index(jnp.where(own == 1, self.shard, self.twin_shard), k))

        @pl.when(own == 0)
        def _():
            self.pair_copy(k).start()

        for m in range(3):

            @pl.when(n == 2 * m + 1)
            def _():
                self.add_pair(m)
                if m == 2:
                    self.pass_on()

        pl.when(n == 7)(self.add_own)

    def end(self):
        def add(rows):
            near = self.near[0, rows].astype(F32) + self.near[1, rows].astype(F32)
            self.total[rows] = self.total[rows] + near

        for slots, span in (((6, 8), self.low), ((7, 9), self.high)):
            for slot in slots:
                self.copy(slot).wait_recv()
            self.over(span, add)
        for k in range(4):
            self.pair_copy(k).wait_send()
        for slot in range(4, 10):
            self.copy(slot).wait_send()


def norm_scale(values):
    return lax.rsqrt(jnp.mean(values * values, axis=-1, keepdims=True) + NORM_EPSILON)


def by_rows(rows, body, carry=0):
    def step(n, carry):
        return body(aligned(n * ROWS, ROWS), carry)

    return lax.fori_loop(0, rows // ROWS, step, carry)


def norm_back(values, gain, upstream):
    scale = norm_scale(values)
    scaled = gain * upstream
    inner = jnp.mean(scaled * values, axis=-1, keepdims=True)
    return (
        scale * scaled - values * scale * scale * scale * inner,
        jnp.sum(upstream * values * scale, axis=0, keepdims=True),
    )


REFS = (
    "tok", "cot", "gains", "weights",
    "block_out", "input_grad", "gain_sums", "gain_late", "mine", "theirs", "n1_held", "slot0", "slot1", "slot2", "slot3", "slot4",
    "w0", "w1", "w2", "w3", "seq_a", "seq_b", "du", "act", "c_all", "gated", "mixed", "resid", "dresid", "total",
    "pair", "near", "joined", "g1", "g2", "g3", "stage", "sum", "tail", "outgoing", "tap_sums", "gain_in", "gain_line", "late_in", "late_line",
    "held", "loaded", "send_x", "recv_x", "send_z", "recv_z", "send_s", "recv_s", "send_c", "recv_c", "credit",
    "halo_send", "halo_recv", "send_g", "recv_g", "fetched", "fetches", "stored", "send_o", "recv_o",
    "send_a", "recv_a", "send_l", "recv_l",
)


def column_pieces(half):
    pieces = [(m * QUARTER + half * HALF_Q, m * HALF_Q, HALF_Q, 0) for m in range(4)]
    for k, (start, units) in enumerate(zip(UNIT_STARTS, UNIT_CHUNKS), 1):
        real = min(units, HALF_F - start)
        for m in range(3):
            first = 4 * QUARTER + m * UNITS + half * HALF_F + start
            pieces.append((first, STARTS[k] + m * units, real, units - real))
    return pieces


def block_kernel(layers, rows, *all_refs):
    r = dict(zip(REFS, all_refs, strict=True))
    tok, cot, gains = r["tok"], r["cot"], r["gains"]
    seq_a, seq_b, du, act = r["seq_a"], r["seq_b"], r["du"], r["act"]
    c_all, gated, mixed, total = r["c_all"], r["gated"], r["mixed"], r["total"]
    weights = (r["w0"], r["w1"], r["w2"], r["w3"])
    seg = tok.shape[0]
    _, shard, inner, _ = place()
    outer, at = line()
    me = 2 * shard + inner
    my_rows = aligned(me * seg, seg)
    chunks = list(zip(range(1, 1 + len(UNIT_CHUNKS)), UNIT_STARTS, UNIT_CHUNKS))
    gather = Gather(
        layers, rows, r["g1"], weights, r["send_x"], r["recv_x"], r["send_z"], r["recv_z"]
    )
    reduce = Reduce(
        layers, rows, (r["w2"], r["g1"], r["g2"], r["g3"], r["w2"]),
        (r["slot0"], r["slot1"], r["slot2"], r["slot3"], r["slot4"]),
        r["stage"], r["w1"], r["sum"], r["outgoing"], r["mine"], r["theirs"],
        (r["send_g"], r["recv_g"], r["fetched"], r["fetches"], r["stored"], r["send_o"], r["recv_o"]),
    )

    def spread(buf, n):
        return Spread(buf, seg, SPREAD_SPLITS[n], r["send_s"].at[n], r["recv_s"].at[n])

    def collect(part, n):
        sems = r["send_c"].at[n], r["recv_c"].at[n]
        return Collect(part, seg, COLLECT_SPLITS[n], total, r["pair"], r["near"], r["joined"], *sems)

    one, up, two, three = spread(seq_a, 0), spread(seq_b, 1), spread(seq_a, 2), spread(seq_a, 3)
    branch, down, feed, inputs = collect(seq_a, 0), collect(seq_b, 1), collect(du, 2), collect(seq_a, 3)
    lanes = lax.broadcasted_iota(jnp.int32, (seg, WIDE), 1) < HALF_Q
    taps = pltpu.roll(gains[...], lax.rem(D - shard * QUARTER - inner * HALF_Q, D), 1)[2:5, :WIDE]
    kept = pl.ds(D, WIDE)
    sums, tap_sums = r["gain_sums"], r["tap_sums"]

    def block(t):
        return aligned(t * seg, seg)

    def mine(part):
        return pl.ds(pl.multiple_of(me * seg + part.start, 16), part.size)

    def first_norm():
        def rows(part, _):
            values = tok[part].astype(F32)
            seq_a[mine(part)] = (values * norm_scale(values) * gains[0:1, :]).astype(BF16)
            return 0

        by_rows(seg, rows)

    def up_start():
        seq_b[my_rows] = cot[...]
        up.start()

    def held():
        return pltpu.make_async_copy(seq_a, r["n1_held"], r["held"])

    def reload():
        return pltpu.make_async_copy(r["n1_held"], seq_b, r["held"])

    def project(s):
        for i in (0, 1):
            parts = dot(seq_a[block(2 * s + i)], weights[0][...])
            b = jnp.where(lanes, parts[:, :WIDE], 0.0)
            c = pltpu.roll(parts[:, 128 : 128 + 384], 384 - 64, 1)[:, :WIDE]
            x = parts[:, 384 : 384 + WIDE]
            c_all[s, pl.ds(i * seg, seg)] = jnp.where(lanes, c, 0.0)
            gated[s, pl.ds(8 + i * seg, seg)] = (b * x).astype(BF16).astype(F32)

    def ahead():
        return remote(
            gated.at[:, pl.ds(2 * seg, 8)], gated.at[:, pl.ds(0, 8)], r["halo_send"].at[0], r["halo_recv"].at[0], at(1)
        )

    def halo():
        pl.when(outer < layers - 1)(lambda: ahead().start())

        @pl.when(outer == 0)
        def _():
            gated[:, pl.ds(0, 8)] = jnp.zeros((GROUPS, 8, WIDE), F32)

    def convolved(s, i):
        return (
            taps[0:1, :] * gated[s, pl.ds(6 + i * seg, seg)]
            + taps[1:2, :] * gated[s, pl.ds(7 + i * seg, seg)]
            + taps[2:3, :] * gated[s, pl.ds(8 + i * seg, seg)]
        )

    def convolve(t):
        for i in (0, 1):

            @pl.when(t % 2 == i)
            def _():
                s = t // 2
                mixed[block(t)] = pltpu.roll(c_all[s, pl.ds(i * seg, seg)] * convolved(s, i), 64, 1).astype(BF16)

        seq_a[block(t)] = dot_rows(mixed[block(t)], weights[0][:, pl.ds(512, WIDE)]).astype(BF16)

    def branch_end():
        branch.end()
        allow(r["credit"].at[0])

    def second_norm():
        def rows(part, _):
            values = tok[part].astype(F32) + total[part]
            r["resid"][part] = values
            seq_a[mine(part)] = (values * norm_scale(values) * gains[1:2, :]).astype(BF16)
            return 0

        by_rows(seg, rows)
        pl.semaphore_wait(r["credit"].at[0], 3)

    def hidden(k, start, units, t):
        ref, here = weights[k], block(t)
        gate = dot(seq_a[here], ref[:, pl.ds(0, units)])
        upval = dot(seq_a[here], ref[:, pl.ds(units, units)])
        dact = dot(seq_b[here], ref[:, pl.ds(2 * units, units)])
        sigma = jax.nn.sigmoid(gate)
        silu = gate * sigma
        act[here, pl.ds(start, units)] = (silu * upval).astype(BF16)
        dgate = dact * upval * sigma * (1.0 + gate * (1.0 - sigma))
        du[here, pl.ds(2 * start, units)] = dgate.astype(BF16)
        du[here, pl.ds(2 * start + units, units)] = (dact * silu).astype(BF16)

    def slice_of(n):
        return jnp.where(outer < layers // 2, D // SLICE - 1 - n, n)

    def gate_up_grads(k, start, units, n):
        part = slice_of(n)
        left = seq_a[:, aligned(part * SLICE, SLICE, 128)]
        reduce.grads[k][aligned(part * SLICE, SLICE), pl.ds(0, 2 * units)] = dot_columns(
            left, du[:, pl.ds(2 * start, 2 * units)]
        ).astype(BF16)

    def down_grads(k, start, units, n):
        part = slice_of(n)
        left = seq_b[:, aligned(part * SLICE, SLICE, 128)]
        reduce.grads[k][aligned(part * SLICE, SLICE), pl.ds(2 * units, units)] = dot_columns(
            left, act[:, pl.ds(start, units)]
        ).astype(BF16)

    def grads(k, start, units, n):
        gate_up_grads(k, start, units, n)
        down_grads(k, start, units, n)
        reduce.direct(k, slice_of(n))

    def second(t):
        here = block(t)
        seq_b[here] = sum(
            dot_rows(du[here, pl.ds(2 * start, 2 * units)], weights[k][:, pl.ds(0, 2 * units)])
            for k, start, units in chunks
        ).astype(BF16)

    def down_end():
        down.end()
        reload().start()
        allow(r["credit"].at[1])

    def forward(t):
        here = block(t)
        du[here, pl.ds(0, D)] = sum(
            dot_rows(act[here, pl.ds(start, units)], weights[k][:, pl.ds(2 * units, units)])
            for k, start, units in chunks
        ).astype(BF16)

    def second_back():
        def rows(part, gain):
            dpart, dgain = norm_back(r["resid"][part], gains[1:2, :], total[part])
            dresid = cot[part].astype(F32) + dpart
            r["dresid"][part] = dresid
            seq_a[mine(part)] = dresid.astype(BF16)
            return gain + dgain

        sums[...] = jnp.zeros(sums.shape, F32)
        tap_sums[...] = jnp.zeros(tap_sums.shape, F32)
        sums[1:2, pl.ds(0, D)] = by_rows(seg, rows, jnp.zeros((1, D), F32))
        pl.semaphore_wait(r["credit"].at[1], 3)

    def mix_back(t):
        s, here = t // 2, block(t)
        dmixed = pltpu.roll(dot(seq_a[here], weights[0][:, pl.ds(512, WIDE)]), WIDE - 64, 1)
        dmixed = jnp.where(lanes, dmixed, 0.0)
        for i in (0, 1):

            @pl.when(t % 2 == i)
            def _():
                du[here, kept] = (dmixed * convolved(s, i)).astype(BF16)
                c_all[s, pl.ds(i * seg, seg)] = dmixed * c_all[s, pl.ds(i * seg, seg)]

    def after():
        return remote(
            c_all.at[:, pl.ds(0, 8)], c_all.at[:, pl.ds(2 * seg, 8)], r["halo_send"].at[1], r["halo_recv"].at[1], at(-1)
        )

    def halo_back():
        pl.when(outer > 0)(lambda: after().start())

        @pl.when(outer == layers - 1)
        def _():
            c_all[:, pl.ds(2 * seg, 8)] = jnp.zeros((GROUPS, 8, WIDE), F32)

    def conv_back(n):
        for i in (0, 1):
            pl.when(n // GROUPS == i)(functools.partial(conv_back_half, n % GROUPS, i))

    def conv_back_half(s, i):
        t = block(2 * s + i)
        dconv = c_all[s, pl.ds(i * seg, seg)]
        dgated = (
            taps[2:3, :] * dconv
            + taps[1:2, :] * c_all[s, pl.ds(1 + i * seg, seg)]
            + taps[0:1, :] * c_all[s, pl.ds(2 + i * seg, seg)]
        )
        parts = dot(seq_b[t], weights[0][:, pl.ds(0, 640)])
        db = dgated * parts[:, 384:640]
        dx = dgated * parts[:, :WIDE]
        dc = jnp.concatenate([du[t, kept].astype(F32), jnp.zeros((seg, 128), F32)], axis=1)
        dc = pltpu.roll(dc, 64, 1)
        act[t, pl.ds(0, 128)] = db[:, :128].astype(BF16)
        act[t, pl.ds(128, 128)] = (db[:, 128:] + dc[:, :128]).astype(BF16)
        act[t, pl.ds(256, 128)] = dc[:, 128:256].astype(BF16)
        act[t, pl.ds(384, WIDE)] = dx.astype(BF16)
        act[t, pl.ds(640, 128)] = jnp.zeros((seg, 128), BF16)
        for k in range(3):
            moved = gated[s, pl.ds(6 + k + i * seg, seg)]
            tap_sums[k : k + 1] = tap_sums[k : k + 1] + jnp.sum(dconv * moved, axis=0, keepdims=True)

    def conv_grads(n):
        part = slice_of(n)
        held_rows, cols = aligned(part * SLICE, SLICE), aligned(part * SLICE, SLICE, 128)
        ref = reduce.grads[0]
        of_parts = dot_columns(seq_b[:, cols], act[:, pl.ds(0, CONV_COLS)])
        ref[held_rows, pl.ds(0, 512)] = of_parts[:, :512].astype(BF16)
        of_mixed = dot_columns(seq_a[:, cols], mixed[...])
        ref[held_rows, pl.ds(512, WIDE)] = (of_parts[:, 512:] + of_mixed).astype(BF16)
        reduce.direct(0, part)
        reduce.direct(4, part)

    def feed_end():
        feed.end()
        allow(r["credit"].at[2])
        r["block_out"][...] = (r["resid"][...] + total[...]).astype(BF16)

    def first(t):
        here = block(t)
        seq_a[here] = dot_rows(act[here, pl.ds(0, 640)], weights[0][:, pl.ds(0, 640)]).astype(BF16)

    def taps_send():
        sums[2:5, aligned(me * WIDE, WIDE, 128)] = tap_sums[0:3]
        early.send(0)

    def first_back():
        def rows(part, gain):
            dpart, dgain = norm_back(tok[part].astype(F32), gains[0:1, :], total[part])
            r["input_grad"][part] = (r["dresid"][part] + dpart).astype(BF16)
            return gain + dgain

        gain_one = by_rows(seg, rows, jnp.zeros((1, D), F32))
        r["gain_late"][...] = jnp.zeros((8, WIDE), F32)
        for n in range(D // WIDE):
            r["gain_late"][n : n + 1] = gain_one[:, n * WIDE : (n + 1) * WIDE]

    class Sum:
        def __init__(self, n, ref, came, line):
            self.n, self.ref, self.came, self.line = n, ref, came, line

        def copy(self, m):
            sems = r["send_a"].at[self.n, m], r["recv_a"].at[self.n, m]
            return remote(self.ref, self.came.at[m], *sems, partners()[m])

        def send(self, m):
            self.copy(m).start()

        def add(self, m):
            self.copy(m).wait()
            self.ref[...] = self.ref[...] + self.came[m]

        def line_copy(self, sign, steps):
            slot = (0 if sign > 0 else 1, steps - 1)
            sems = r["send_l"].at[(self.n,) + slot], r["recv_l"].at[(self.n,) + slot]
            return remote(self.ref, self.line.at[slot], *sems, at(sign * steps))

        def line_send(self):
            for steps in range(1, layers):
                for sign in (1, -1):
                    pl.when(in_line(outer + sign * steps, layers))(self.line_copy(sign, steps).start)

        def line_add(self):
            for steps in range(1, layers):
                for sign in (1, -1):
                    pl.when(in_line(outer + sign * steps, layers))(self.line_copy(sign, steps).wait_send)
                    pl.when(in_line(outer - sign * steps, layers))(self.line_copy(sign, steps).wait_recv)

            own = self.ref[...]
            for origin in range(layers):
                for steps in range(1, layers):
                    for sign in (1, -1):

                        @pl.when(outer - sign * steps == origin)
                        def _():
                            came = self.line[0 if sign > 0 else 1, steps - 1]
                            self.ref[...] = came if origin == 0 else self.ref[...] + came

                if origin > 0:

                    @pl.when(outer == origin)
                    def _():
                        self.ref[...] = self.ref[...] + own

    early = Sum(0, sums, r["gain_in"], r["gain_line"])
    late = Sum(1, r["gain_late"], r["late_in"], r["late_line"])

    def end():
        reduce.finish(4)
        for k in range(len(SUM_WIDTHS)):
            reduce.wait_sent(k)
        pl.when(outer < layers - 1)(lambda: ahead().wait_send())
        pl.when(outer > 0)(lambda: after().wait_send())

    windows = [
        (r["resid"], 0, D), (r["dresid"], D, D), (total, 2 * D, D), (r["resid"], 3 * D, D),
        (r["tail"], 4 * D, GROUP_COLS - 4 * D),
    ]

    def load(n):
        ref, first, width = windows[n]
        return pltpu.make_async_copy(
            r["weights"].at[:, pl.ds(first, width)], ref.at[pl.ds(0, rows)], r["loaded"].at[n]
        )

    def start():
        for n in (0, 1, 2, 4):
            load(n).start()
        greet(layers)
        load(0).wait()
        cut(0)
        load(3).start()
        greeted(layers)

    def cut(k):
        def read(part, first, width):
            found = []
            for n, (ref, low, size) in enumerate(windows):
                start, stop = max(first, low), min(first + width, low + size)
                if start < stop and (n == 0) == (k == 0):
                    found.append(ref[part, start - low : stop - low])
            return found

        size = band(rows, 96)

        def cut_band(n, _):
            part = aligned(n * size, size)
            halves = []
            for half in (0, 1):
                pieces = []
                for first, own, width, padding in column_pieces(half):
                    if STARTS[k] <= own < STARTS[k] + WIDTHS[k]:
                        pieces += read(part, first, width)
                        if padding:
                            pieces.append(jnp.zeros((size, padding), F32))
                halves.append(jnp.concatenate(pieces, axis=1))
            is_low = inner == 0
            seq = lax.axis_index("seq")
            own_rows = aligned(seq * rows + n * size, size)
            weights[k][own_rows, :] = jnp.where(is_low, halves[0], halves[1]).astype(BF16)
            gather.other_rows(k)[part, :] = jnp.where(is_low, halves[1], halves[0]).astype(BF16)
            return 0

        for n in (1, 2, 3, 4) if k == CUT_FIRST else ():
            load(n).wait()
        lax.fori_loop(0, rows // size, cut_band, 0)

    def hold():
        held().start()

    def hold_end():
        held().wait()

    def halo_end():
        pl.when(outer > 0)(lambda: ahead().wait_recv())

    def reload_end():
        reload().wait()

    def halo_back_end():
        pl.when(outer < layers - 1)(lambda: after().wait_recv())

    def feed_credit():
        pl.semaphore_wait(r["credit"].at[2], 3)

    def from_spread(moved, body):
        def step(n):
            for m in range(8):
                if moved.before(m):

                    @pl.when(n == m)
                    def _():
                        for act in moved.before(m):
                            act()

            body(moved.index(n))

        return step

    def each(body, *cases):
        return [functools.partial(body, *(case if isinstance(case, tuple) else (case,))) for case in cases]

    every = range(len(WIDTHS))
    cuts = each(cut, *every)
    exchange, send_own, send_other = (
        each(body, *every) for body in (gather.exchange, gather.send_own, gather.send_other)
    )
    step = [each(gather.steps, (k, 1, 1), (k, 2, 2), (k, 3)) for k in every]
    join_far = each(reduce.join, *((k, layers - 2, 2) for k in range(len(SUM_WIDTHS))))
    join_near = each(reduce.join, *((k, 1, 1) for k in range(len(SUM_WIDTHS))))
    final = each(reduce.final, (0, 3), 1, (2, 1), (3, 2), (4, 0))
    feed_pair = each(feed.add_pair, 0, 1, 2)
    gain_send, gain_add = each(late.send, 0, 1, 2), each(late.add, 0, 1, 2)
    taps_add, taps_next = each(early.add, 0, 1, 2), each(early.send, 0, 1, 2)
    d3_far = functools.partial(reduce.direct, 3, least=2)
    d3_near = functools.partial(reduce.direct, 3, most=1)
    blocks, parts = 2 * GROUPS, D // SLICE
    proj = Loop(GROUPS, project)
    mix = Loop(blocks, lambda n: branch.make(n, convolve))
    hid1 = Loop(blocks, from_spread(two, functools.partial(hidden, *chunks[0])))
    hid2, hid3 = (Loop(blocks, functools.partial(hidden, *chunk)) for chunk in chunks[1:])
    grad1, grad2 = (Loop(parts, functools.partial(grads, *chunk)) for chunk in chunks[:2])
    down3 = Loop(parts, functools.partial(down_grads, *chunks[2]))
    back2 = Loop(blocks, lambda n: down.make(n, second))
    gate3 = Loop(parts, functools.partial(gate_up_grads, *chunks[2]))
    ffn = Loop(blocks, forward)
    back_mix = Loop(blocks, from_spread(three, mix_back))
    back_conv = Loop(blocks, conv_back)
    grad0 = Loop(parts, conv_grads)
    back1 = Loop(blocks, lambda n: inputs.make(n, first))
    play(
        [
            start, exchange[0], send_own[0], first_norm, one.start, send_other[0], step[0][0], one.first, cuts[1],
            up_start, exchange[1], step[0][1], send_own[1], cuts[2], step[0][2], one.near, cuts[3], up.first,
            send_own[2], one.far, one.end, proj[0], hold, proj[1], exchange[2], proj[2], up.near, hold_end, proj[3],
            halo, send_other[1], halo_end, mix[0], mix[1], exchange[3], up.far, mix[2], step[1][0], send_other[2],
            mix[3], mix[4], mix[5], mix[6], step[1][1], mix[7], branch_end, second_norm, step[2][0], up.end,
            two.start, send_own[3], step[1][2], hid1[0], hid1[1], hid1[2], hid1[3], send_other[3], hid1[4], hid1[5],
            hid1[6], gather.crossed, hid1[7], two.sent, grad1[0], grad1[1], step[2][1], grad1[2], step[3][0],
            step[2][2], grad1[3], hid2[0], hid2[1], hid2[2], hid2[3], hid2[4], hid2[5], hid2[6], hid2[7], grad2[0],
            grad2[1], grad2[2], grad2[3], step[3][1], step[3][2], hid3[0], hid3[1], hid3[2], hid3[3], hid3[4],
            gather.finish, hid3[5], hid3[6], hid3[7], down3[0], down3[1], join_far[1], down3[2], down3[3], back2[0],
            back2[1], back2[2], back2[3], back2[4], back2[5], back2[6], back2[7], gate3[0], join_near[1], gate3[1],
            gate3[2], gate3[3], d3_far, down_end, second_back, three.start, ffn[0], ffn[1], ffn[2], ffn[3], ffn[4],
            ffn[5], ffn[6], ffn[7], back_mix[0], back_mix[1], feed.push, join_far[2], reload_end, back_mix[2],
            final[1], feed_pair[0], back_mix[3], back_mix[4], back_mix[5], back_mix[6], back_mix[7], three.sent,
            join_near[2], halo_back, d3_near, feed_pair[1], back_conv[0], back_conv[1], back_conv[2], back_conv[3],
            feed_pair[2], halo_back_end, back_conv[4], back_conv[5], feed.pass_on, back_conv[6], back_conv[7],
            feed.add_own, join_far[3], grad0[0], grad0[1], grad0[2], grad0[3], feed_end, taps_send, feed_credit,
            back1[0], join_far[0], back1[1], taps_add[0], back1[2], join_far[4], back1[3], taps_next[1],
            join_near[3], back1[4], join_near[0], back1[5], back1[6], final[2], back1[7], join_near[4], final[3],
            taps_add[1], inputs.end, taps_next[2], first_back, taps_add[2], early.line_send, gain_send[0], final[0],
            gain_add[0], gain_send[1], gain_add[1], gain_send[2], final[4], gain_add[2], late.line_send, late.line_add,
            early.line_add, end,
        ]
    )


class Loop:
    def __init__(self, count, body):
        self.count, self.body = count, body

    def __getitem__(self, n):
        return (self, n)


def play(order):
    order = list(order)
    while order:
        entry = order.pop(0)
        if not isinstance(entry, tuple):
            entry()
            continue
        loop, _ = entry
        between = {}
        for n in range(1, loop.count):
            between[n] = []
            while order[0] != (loop, n):
                between[n].append(order.pop(0))
            order.pop(0)

        def turn(n, _):
            for m, acts in between.items():
                if acts:

                    @pl.when(n == m)
                    def _():
                        play(acts)

            loop.body(n)
            return 0

        lax.fori_loop(0, loop.count, turn, 0)


def block_step(tok, cot, gains, weights, layers):
    rows, seg = weights.shape[0], tok.shape[0]
    count, sums = len(WIDTHS), len(SUM_WIDTHS)
    tokens = 2 * GROUPS * seg
    vmem, anywhere = pl.BlockSpec(memory_space=pltpu.VMEM), pl.BlockSpec(memory_space=pl.ANY)
    shape, scratch = jax.ShapeDtypeStruct, pltpu.VMEM
    dma, regular = pltpu.SemaphoreType.DMA, pltpu.SemaphoreType.REGULAR
    hops = layers - 1
    wide, biggest = sum(WIDTHS), max(WIDTHS)
    out_shape = [
        shape((seg, D), BF16),
        shape((seg, D), BF16),
        shape((8, 2 * GROUPS * WIDE), F32),
        shape((8, WIDE), F32),
        shape((rows, wide), F32),
        shape((rows, wide), BF16),
        shape((tokens, D), BF16),
    ] + [shape((2, hops, 2 * rows, width), BF16) for width in SUM_WIDTHS]
    scratch_shapes = (
        [scratch((D, width), BF16) for width in WIDTHS]
        + [
            scratch((tokens, D), BF16),
            scratch((tokens, D), BF16),
            scratch((tokens, 2 * PAD_F), BF16),
            scratch((tokens, PAD_F), BF16),
            scratch((GROUPS, 8 + 2 * seg, WIDE), F32),
            scratch((GROUPS, 8 + 2 * seg, WIDE), F32),
            scratch((tokens, WIDE), BF16),
            scratch((seg, D), F32),
            scratch((seg, D), F32),
            scratch((seg, D), F32),
            scratch((4, seg, D), BF16),
            scratch((2, seg, D), BF16),
            scratch((seg, D), BF16),
        ]
        + [scratch((D, width), BF16) for width in WIDTHS[1:]]
        + [
            scratch((2 * rows, biggest), BF16),
            scratch((rows, biggest), F32),
            scratch((rows, GROUP_COLS - 4 * D), F32),
            scratch((rows, wide), BF16),
            scratch((8, WIDE), F32),
            scratch((3, 8, 2 * GROUPS * WIDE), F32),
            scratch((2, hops, 8, 2 * GROUPS * WIDE), F32),
            scratch((3, 8, WIDE), F32),
            scratch((2, hops, 8, WIDE), F32),
            dma,
            dma((5,)),
            dma((count,)),
            dma((count,)),
            dma((count, 2, hops, 2)),
            dma((count, 2, hops, 2)),
            dma((4, 11)),
            dma((4, 11)),
            dma((4, 10)),
            dma((4, 10)),
            regular((3,)),
            dma((2,)),
            dma((2,)),
            dma((sums, 2, hops)),
            dma((sums, 2, hops)),
            dma,
            dma((4,)),
            dma((sums,)),
            dma((sums,)),
            dma((sums,)),
            dma((2, 3)),
            dma((2, 3)),
            dma((2, 2, hops)),
            dma((2, 2, hops)),
        ]
    )
    return pl.pallas_call(
        functools.partial(block_kernel, layers, rows),
        out_shape=out_shape,
        in_specs=[vmem] * 3 + [anywhere],
        out_specs=[vmem] * 4 + [anywhere] * (3 + sums),
        scratch_shapes=scratch_shapes,
        compiler_params=pltpu.CompilerParams(
            collective_id=0, has_side_effects=True, vmem_limit_bytes=VMEM_BYTES
        ),
        name="block_step",
    )(tok, cot, gains, weights)[:6]


def band(rows, most):
    return max(size for size in range(16, most + 1, 16) if rows % size == 0)


def adam_update(param, grad, first, second, rate, decay):
    first_new = MOMENT_DECAY * first + (1.0 - MOMENT_DECAY) * grad
    second_new = SQUARE_DECAY * second + (1.0 - SQUARE_DECAY) * grad * grad
    root = jnp.sqrt(second_new * (1.0 / (1.0 - SQUARE_DECAY**STEP))) + ADAM_EPSILON
    step = first_new * (rate / (1.0 - MOMENT_DECAY**STEP)) / root
    return (first_new, second_new, param * (1.0 - rate * decay) - step)


def update_kernel(
    inner_ref, mine_ref, theirs_ref, weights_ref, first_ref, second_ref, sums_ref, late_ref, gains_ref, gains_first_ref,
    gains_second_ref, block_ref, input_ref, grad_out, first_out, second_out, weights_out, gains_grad_out,
    gains_first_out, gains_second_out, gains_out, block_out, input_out,
):
    is_low = inner_ref[0] == 0
    mine, theirs = mine_ref[...], theirs_ref[...].astype(F32)
    for half in (0, 1):
        chosen = jnp.where(is_low, mine, theirs) if half == 0 else jnp.where(is_low, theirs, mine)
        for first, own, width, _ in column_pieces(half):
            grad_out[:, first : first + width] = chosen[:, own : own + width]
    first_out[...], second_out[...], weights_out[...] = adam_update(
        weights_ref[...], grad_out[...], first_ref[...], second_ref[...], WEIGHT_RATE, WEIGHT_DECAY
    )

    @pl.when(pl.program_id(0) == 0)
    def _():
        gains_grad_out[1:2] = sums_ref[1:2, :D]
        for n in range(D // WIDE):
            gains_grad_out[0:1, n * WIDE : (n + 1) * WIDE] = late_ref[n : n + 1]
        for n in range(2 * GROUPS):
            gains_grad_out[2:5, n * HALF_Q : (n + 1) * HALF_Q] = sums_ref[2:5, n * WIDE : n * WIDE + HALF_Q]
        gains_first_out[...], gains_second_out[...], gains_out[...] = adam_update(
            gains_ref[...], gains_grad_out[...], gains_first_ref[...], gains_second_ref[...], GAIN_RATE, 0.0
        )
        block_out[...] = block_ref[...]
        input_out[...] = input_ref[...]


def update(inner, mine, theirs, weights, first, second, sums, late, gains, gains_first, gains_second, block, grad):
    rows, cols = weights.shape
    wide = mine.shape[1]
    size = band(rows, 32)
    by_row = lambda width: pl.BlockSpec((size, width), lambda n: (n, 0))
    whole = lambda values: pl.BlockSpec(values.shape, lambda n: (0, 0))
    shape = jax.ShapeDtypeStruct
    return pl.pallas_call(
        update_kernel,
        grid=(rows // size,),
        out_shape=[shape((rows, cols), F32)] * 4 + [shape(gains.shape, F32)] * 4 + [shape(block.shape, BF16)] * 2,
        in_specs=[pl.BlockSpec(memory_space=pltpu.SMEM)]
        + [by_row(wide)] * 2
        + [by_row(cols)] * 3
        + [whole(sums), whole(late)]
        + [whole(gains)] * 3
        + [whole(block)] * 2,
        out_specs=[by_row(cols)] * 4 + [whole(gains)] * 4 + [whole(block)] * 2,
        compiler_params=pltpu.CompilerParams(vmem_limit_bytes=VMEM_BYTES),
        name="update",
    )(inner, mine, theirs, weights, first, second, sums, late, gains, gains_first, gains_second, block, grad)


def on_device(
    tokens, gains_taps, weights, cotangent, weight_first, weight_second, gains_first, gains_second
):
    layers = lax.axis_size("seq") // 2
    inner_word = (lax.axis_index("seq") % 2).astype(jnp.int32).reshape(1)
    block_out, input_grad, gain_sums, gain_late, mine, theirs = block_step(
        tokens[0], cotangent[0], gains_taps, weights, layers
    )
    (
        weight_grad, weight_first_new, weight_second_new, weight_new,
        gains_grad, gains_first_new, gains_second_new, gains_new, block_out, input_grad,
    ) = update(
        inner_word, mine, theirs, weights, weight_first, weight_second,
        gain_sums, gain_late, gains_taps, gains_first, gains_second, block_out, input_grad,
    )
    return (
        block_out[None],
        input_grad[None],
        weight_grad,
        weight_first_new,
        weight_second_new,
        weight_new,
        gains_grad,
        gains_first_new,
        gains_second_new,
        gains_new,
    )


def solution(mesh):
    tokens, rows, whole = P("shard", "seq", None), P("seq", "shard"), P()
    return jax.shard_map(
        on_device,
        mesh=mesh,
        in_specs=(tokens, whole, rows, tokens, rows, rows, whole, whole),
        out_specs=(tokens, tokens, rows, rows, rows, rows, whole, whole, whole, whole),
        check_vma=False,
    )
```

```python
import functools

import jax
import jax.numpy as jnp
from jax import lax
from jax.experimental import pallas as pl
from jax.experimental.pallas import tpu as pltpu
from jax.sharding import PartitionSpec as P

D = 1536
FF = 6912
STEP = 10
GROUPS = 4
QUARTER = D // GROUPS
UNITS = FF // GROUPS
GROUP_COLS = 4 * QUARTER + 3 * UNITS
HALF_Q = QUARTER // 2
HALF_F = UNITS // 2
LANES = 128
PAD_F = -(-HALF_F // LANES) * LANES
WIDE = 256
CONV_COLS = 4 * HALF_Q
UNIT_CHUNKS = (384, 256, PAD_F - 640)
UNIT_STARTS = (0, 384, 640)
WIDTHS = (CONV_COLS,) + tuple(3 * units for units in UNIT_CHUNKS)
STARTS = tuple(sum(WIDTHS[:k]) for k in range(len(WIDTHS)))
SPREAD_SPLITS = (208, 160, 112, 112)
COLLECT_SPLITS = (128, 128, 96, 112)
REACH = (1, 1, 1, 1)
CUT_FIRST = 1
SLICE = 384
TILE = 16
ROWS = 48

MOMENT_DECAY = 0.9
SQUARE_DECAY = 0.95
ADAM_EPSILON = 1e-08
NORM_EPSILON = 1e-05
WEIGHT_RATE = 0.02
GAIN_RATE = 0.2
WEIGHT_DECAY = 0.1

BF16 = jnp.bfloat16
F32 = jnp.float32
MESH = pl.DeviceIdType.MESH
VMEM_BYTES = 63 * 1024 * 1024


def place():
    seq, shard = lax.axis_index("seq"), lax.axis_index("shard")
    inner, core = lax.rem(seq, 2), lax.rem(shard, 2)
    return seq, shard, inner, core


def partners():
    seq, shard, inner, core = place()
    across = {"seq": seq + 1 - 2 * inner, "shard": shard}
    beside = {"seq": seq, "shard": lax.rem(shard + 2, 4)}
    twin = {"seq": seq, "shard": shard + 1 - 2 * core}
    return across, beside, twin


def remote(src, dst, send, recv, device):
    return pltpu.make_async_remote_copy(
        src_ref=src, dst_ref=dst, send_sem=send, recv_sem=recv, device_id=device, device_id_type=MESH
    )


def line():
    seq, shard, _, _ = place()
    size = lax.axis_size("seq")
    return seq // 2, lambda steps: {"seq": lax.rem(seq + 2 * steps + size, size), "shard": shard}


def greet(layers):
    outer, at = line()
    barrier = pltpu.get_barrier_semaphore()
    for device in partners():
        pl.semaphore_signal(barrier, inc=1, device_id=device, device_id_type=MESH)
    for steps in range(1, layers):
        for sign in (1, -1):

            @pl.when(in_line(outer + sign * steps, layers))
            def _():
                pl.semaphore_signal(barrier, inc=1, device_id=at(sign * steps), device_id_type=MESH)


def greeted(layers):
    pl.semaphore_wait(pltpu.get_barrier_semaphore(), 3 + layers - 1)


def in_line(index, layers):
    return (index >= 0) & (index < layers)


def allow(credit):
    for device in partners():
        pl.semaphore_signal(credit, inc=1, device_id=device, device_id_type=MESH)


def dot(left, right):
    return jnp.dot(left, right, preferred_element_type=F32)


def dot_rows(left, right):
    return lax.dot_general(left, right, (((1,), (1,)), ((), ())), preferred_element_type=F32)


def dot_columns(left, right):
    return lax.dot_general(left, right, (((0,), (0,)), ((), ())), preferred_element_type=F32)


def aligned(start, size, multiple=16):
    return pl.ds(pl.multiple_of(start, multiple), size)


class Gather:
    def __init__(self, layers, rows, oth, outs, send_x, recv_x, send_z, recv_z):
        self.layers, self.rows, self.oth, self.outs = layers, rows, oth, outs
        self.send_x, self.recv_x, self.send_z, self.recv_z = send_x, recv_x, send_z, recv_z
        self.seq, _, self.inner, _ = place()
        self.outer, self.at = line()
        self.across = partners()[0]

    def seq_rows(self, index):
        return aligned(index * self.rows, self.rows)

    def layer_rows(self, direction, distance):
        origin = self.outer - distance if direction == 0 else self.outer + distance
        return aligned(origin * 2 * self.rows, 2 * self.rows)

    def copy(self, k, src, dst, direction, distance, hop, piece):
        slot = (k, direction, distance + hop - 1, piece)
        return remote(
            src, dst, self.send_z.at[slot], self.recv_z.at[slot], self.at(hop if direction == 0 else -hop)
        )

    def goes(self, direction, hop):
        return in_line(self.outer + (hop if direction == 0 else -hop), self.layers)

    def has_come(self, direction, distance):
        return in_line(self.outer + (-distance if direction == 0 else distance), self.layers)

    def hops(self, k, distance):
        return range(1, min(REACH[k], self.layers - 1 - distance) + 1)

    def own_copy(self, k, direction, hop):
        here = self.outs[k].at[self.seq_rows(self.seq)]
        return self.copy(k, here, here, direction, 0, hop, 0)

    def other_copy(self, k, direction, hop):
        there = self.outs[k].at[self.seq_rows(self.seq + 1 - 2 * self.inner)]
        return self.copy(k, there, there, direction, 0, hop, 1)

    def pass_copy(self, k, direction, distance, hop):
        ref = self.outs[k].at[self.layer_rows(direction, distance)]
        return self.copy(k, ref, ref, direction, distance, hop, 0)

    def other_rows(self, k):
        return self.oth.at[pl.ds(k * self.rows, self.rows), pl.ds(0, WIDTHS[k])]

    def exchange(self, k):
        self.x_copy(k).start()

    def x_copy(self, k):
        here = self.outs[k].at[self.seq_rows(self.seq)]
        return remote(self.other_rows(k), here, self.send_x.at[k], self.recv_x.at[k], self.across)

    def crossed(self):
        for k in range(len(self.outs)):
            self.x_copy(k).wait_send()

    def send_own(self, k):
        for hop in self.hops(k, 0):
            for direction in (0, 1):

                @pl.when(self.goes(direction, hop))
                def _():
                    self.own_copy(k, direction, hop).start()

    def send_other(self, k):
        self.x_copy(k).wait_recv()
        for hop in self.hops(k, 0):
            for direction in (0, 1):

                @pl.when(self.goes(direction, hop))
                def _():
                    self.other_copy(k, direction, hop).start()

    def step(self, k, distance):
        for direction in (0, 1):

            @pl.when(self.has_come(direction, distance))
            def _():
                if distance <= REACH[k]:
                    origin = self.outer - distance if direction == 0 else self.outer + distance
                    for piece in (0, 1):
                        index = 2 * origin + (self.inner if piece == 0 else 1 - self.inner)
                        ref = self.outs[k].at[self.seq_rows(index)]
                        self.copy(k, ref, ref, direction, distance - 1, 1, piece).wait_recv()
                else:
                    ref = self.outs[k].at[self.layer_rows(direction, distance)]
                    self.copy(k, ref, ref, direction, distance - 1, 1, 0).wait_recv()
                if distance % REACH[k] == 0:
                    for hop in self.hops(k, distance):

                        @pl.when(self.goes(direction, hop))
                        def _():
                            self.pass_copy(k, direction, distance, hop).start()

    def steps(self, k, first, last=None):
        last = self.layers - 1 if last is None else min(last, self.layers - 1)
        for distance in range(first, last + 1):
            self.step(k, distance)

    def finish(self):
        for k in range(len(self.outs)):
            for distance in range(0, self.layers - 1, REACH[k]):
                for hop in self.hops(k, distance):
                    for direction in (0, 1):

                        @pl.when(self.goes(direction, hop) & self.has_come(direction, distance))
                        def _():
                            if distance == 0:
                                self.own_copy(k, direction, hop).wait_send()
                                self.other_copy(k, direction, hop).wait_send()
                            else:
                                self.pass_copy(k, direction, distance, hop).wait_send()


class Reduce:
    def __init__(self, layers, rows, grads, slots, stage, spare, total, outgoing, mine, theirs, sems):
        self.layers, self.rows, self.grads, self.slots = layers, rows, grads, slots
        self.stage, self.spare, self.total, self.outgoing = stage, spare, total, outgoing
        self.mine, self.theirs = mine, theirs
        self.send_g, self.recv_g, self.fetched, self.fetches, self.stored, self.send_o, self.recv_o = sems
        _, _, self.inner, _ = place()
        self.outer, self.at = line()
        self.across = partners()[0]

    def owner(self, direction, distance):
        return self.outer + distance if direction == 0 else self.outer - distance

    def upstream(self, direction, steps):
        return in_line(self.outer - steps if direction == 0 else self.outer + steps, self.layers)

    def block(self, k, owner):
        return self.grads[k].at[aligned(owner * 2 * self.rows, 2 * self.rows), pl.ds(0, WIDTHS[k])]

    def copy(self, k, src, direction, distance):
        slot = (direction, distance - 1)
        return remote(
            src,
            self.slots[k].at[slot],
            self.send_g.at[(k,) + slot],
            self.recv_g.at[(k,) + slot],
            self.at(1 if direction == 0 else -1),
        )

    def send(self, k, direction, distance):
        self.copy(k, self.block(k, self.owner(direction, distance)), direction, distance).start()

    def direct(self, k, part=None, least=1, most=None):
        for distance in range(most or self.layers - 1, least - 1, -1):
            for direction in (0, 1):
                owner = self.owner(direction, distance)
                here = in_line(owner, self.layers) & jnp.logical_not(self.upstream(direction, 1))
                if part is not None:
                    here = here & (owner * 2 * self.rows // SLICE == part)

                @pl.when(here)
                def _():
                    self.send(k, direction, distance)

    def fetch(self, k, direction, distance):
        slot = self.slots[k].at[direction, distance - 1]
        self.copy(k, slot, direction, distance).wait_recv()
        held = self.stage.at[:, pl.ds(0, WIDTHS[k])]
        copy = pltpu.make_async_copy(slot, held, self.fetched)
        copy.start()
        copy.wait()

    def tiles(self, body):
        def step(n, _):
            body(aligned(n * TILE, TILE))
            return 0

        lax.fori_loop(0, 2 * self.rows // TILE, step, 0)

    def join(self, k, most, least):
        cols = pl.ds(0, WIDTHS[k])
        for distance in range(most, least - 1, -1):
            for direction in (0, 1):
                owner = self.owner(direction, distance)

                @pl.when(in_line(owner, self.layers) & self.upstream(direction, 1))
                def _():
                    def add(tile):
                        base = self.owner(direction, distance) * 2 * self.rows
                        rows = pl.ds(pl.multiple_of(base + tile.start, 16), TILE)
                        ref = self.grads[k]
                        ref[rows, cols] = (
                            ref[rows, cols].astype(F32) + self.stage[tile, cols].astype(F32)
                        ).astype(BF16)

                    self.fetch(k, direction, distance + 1)
                    self.tiles(add)
                    self.send(k, direction, distance)

    def final(self, k, before=None):
        cols = pl.ds(0, WIDTHS[k])
        came = [(1, 0), (1, 1)]

        def fetch(n, distance, direction):
            return pltpu.make_async_copy(
                self.slots[k].at[direction, distance - 1],
                self.spare.at[pl.ds(n * 2 * self.rows, 2 * self.rows), cols],
                self.fetches.at[n],
            )

        for n, (distance, direction) in enumerate(came):

            @pl.when(self.upstream(direction, distance))
            def _():
                self.copy(k, self.slots[k].at[direction, distance - 1], direction, distance).wait_recv()
                fetch(n, distance, direction).start()

        if before is not None:
            self.store(before).wait()

        here, there = self.inner * self.rows, (1 - self.inner) * self.rows

        def each(base, body):
            def step(n, _):
                body(base + n * TILE, n * TILE)
                return 0

            lax.fori_loop(0, self.rows // TILE, step, 0)

        for n, (distance, direction) in enumerate(came):

            @pl.when(self.upstream(direction, distance))
            def _():
                fetch(n, distance, direction).wait()

        def add_up(flags):
            def total(rows):
                value = self.grads[k][aligned(self.outer * 2 * self.rows + rows, TILE), cols].astype(F32)
                for n, flag in enumerate(flags):
                    if flag:
                        value = value + self.spare[aligned(n * 2 * self.rows + rows, TILE), cols].astype(F32)
                return value

            def send(rows, at):
                self.outgoing[aligned(at, TILE), pl.ds(STARTS[k], WIDTHS[k])] = total(rows).astype(BF16)

            def keep(rows, at):
                self.total[aligned(at, TILE), cols] = total(rows)

            each(there, send)
            self.over(k).start()
            each(here, keep)
            self.store(k).start()

        patterns = {}
        for place_in_line in range(self.layers):
            flags = tuple(
                0 <= (place_in_line - distance if direction == 0 else place_in_line + distance) < self.layers
                for distance, direction in came
            )
            patterns.setdefault(flags, []).append(place_in_line)
        for flags, places in patterns.items():
            here_now = functools.reduce(jnp.logical_or, [self.outer == p for p in places])

            @pl.when(here_now)
            def _():
                add_up(flags)

    def over(self, k):
        wide = pl.ds(STARTS[k], WIDTHS[k])
        return remote(
            self.outgoing.at[:, wide], self.theirs.at[:, wide], self.send_o.at[k], self.recv_o.at[k], self.across
        )

    def store(self, k):
        return pltpu.make_async_copy(
            self.total.at[:, pl.ds(0, WIDTHS[k])], self.mine.at[:, pl.ds(STARTS[k], WIDTHS[k])], self.stored.at[k]
        )

    def wait_sent(self, k):
        for distance in range(1, self.layers):
            for direction in (0, 1):
                owner = self.owner(direction, distance)

                @pl.when(in_line(owner, self.layers))
                def _():
                    self.copy(k, self.block(k, owner), direction, distance).wait_send()

    def finish(self, before):
        self.store(before).wait()
        for k in range(len(self.grads)):
            self.over(k).wait()


class Spread:
    slots = range(11)

    def __init__(self, buf, seg, split, send, recv):
        self.buf, self.seg, self.split, self.send, self.recv = buf, seg, split, send, recv

    def index(self, n):
        _, shard, inner, core = place()
        row, flip, other = (n // 2) % 2, n // 4, n % 2
        return 2 * (lax.rem(shard + 2 * row, 4) + other * (1 - 2 * core)) + inner + flip * (1 - 2 * inner)

    def copy(self, slot):
        across, beside, twin = partners()
        low, high, whole = (0, self.split), (self.split, self.seg - self.split), (0, self.seg)
        n, (first, size), device = {
            0: (0, low, across),
            9: (0, high, across),
            1: (0, high, beside),
            10: (0, low, beside),
            2: (0, whole, twin),
            3: (4, low, beside),
            4: (4, whole, twin),
            5: (2, high, across),
            6: (2, whole, twin),
            7: (6, low, twin),
            8: (6, high, twin),
        }[slot]
        ref = self.buf.at[aligned(self.index(n) * self.seg + first, size)]
        return remote(ref, ref, self.send.at[slot], self.recv.at[slot], device)

    def push(self, *slots):
        for slot in slots:
            self.copy(slot).start()

    def came(self, *slots):
        for slot in slots:
            self.copy(slot).wait_recv()

    def start(self):
        self.push(0, 1, 9, 10, 2)

    def first(self):
        self.came(1)
        self.push(5)
        self.came(0)
        self.push(3)

    def near(self):
        self.came(10)
        self.push(6)
        self.came(9)
        self.push(4)

    def far(self):
        self.came(3)
        self.push(7)
        self.came(5)
        self.push(8)

    def sent(self):
        for slot in self.slots:
            self.copy(slot).wait_send()

    def end(self):
        self.came(2, 4, 6, 7, 8)
        self.sent()

    def before(self, n):
        return {
            1: (lambda: self.came(2),),
            2: (self.first, self.near),
            3: (lambda: self.came(6),),
            5: (lambda: self.came(4),),
            6: (self.far,),
            7: (lambda: self.came(7, 8),),
        }.get(n, ())


class Collect:
    def __init__(self, part, seg, split, total, pair, near, joined, send, recv):
        self.part, self.seg, self.total = part, seg, total
        self.pair, self.near, self.joined, self.send, self.recv = pair, near, joined, send, recv
        _, self.shard, self.inner, core = place()
        self.twin_shard = self.shard + 1 - 2 * core
        self.low, self.high, self.whole = (0, split), (split, seg - split), (0, seg)
        self.cols = pl.ds(0, D)

    def index(self, s, k):
        row, flip = 1 - k % 2, 1 - k // 2
        return 2 * lax.rem(s + 2 * row, 4) + self.inner + flip * (1 - 2 * self.inner)

    def pair_copy(self, k):
        src = self.part.at[aligned(self.index(self.twin_shard, k) * self.seg, self.seg), self.cols]
        return remote(src, self.pair.at[k], self.send.at[k], self.recv.at[k], partners()[2])

    def copy(self, slot):
        across, beside, _ = partners()
        src, dst, (first, size), device = {
            4: (self.pair.at[0], self.joined, self.low, across),
            5: (self.pair.at[0], self.joined, self.high, beside),
            6: (self.pair.at[1], self.near.at[0], self.low, across),
            7: (self.pair.at[2], self.near.at[1], self.high, beside),
            8: (self.pair.at[2], self.near.at[1], self.low, beside),
            9: (self.pair.at[1], self.near.at[0], self.high, across),
        }[slot]
        rows = pl.ds(first, size)
        return remote(src.at[rows], dst.at[rows], self.send.at[slot], self.recv.at[slot], device)

    def over(self, span, body):
        def step(n, _):
            body(aligned(span[0] + n * 16, 16))
            return 0

        lax.fori_loop(0, span[1] // 16, step, 0)

    def mine(self, k, rows):
        return self.part[aligned(self.index(self.shard, k) * self.seg + rows.start, 16), self.cols].astype(F32)

    def add_pair(self, k):
        def add(rows):
            self.pair[k, rows] = (self.mine(k, rows) + self.pair[k, rows].astype(F32)).astype(BF16)

        self.pair_copy(k).wait_recv()
        self.over(self.whole, add)
        for slot in ((4, 5), (6,), (7,))[k]:
            self.copy(slot).start()

    def add_own(self):
        def add(rows):
            self.total[rows] = self.mine(3, rows) + self.pair[3, rows].astype(F32)

        self.pair_copy(3).wait_recv()
        self.over(self.whole, add)

    def pass_on(self):
        for slot, k, span, after in ((4, 2, self.low, 8), (5, 1, self.high, 9)):

            def add(rows):
                self.pair[k, rows] = (self.pair[k, rows].astype(F32) + self.joined[rows].astype(F32)).astype(BF16)

            self.copy(slot).wait_recv()
            self.over(span, add)
            self.copy(after).start()

    def push(self):
        for k in range(4):
            self.pair_copy(k).start()

    def make(self, n, produce):
        k, own = n // 2, n % 2
        produce(self.index(jnp.where(own == 1, self.shard, self.twin_shard), k))

        @pl.when(own == 0)
        def _():
            self.pair_copy(k).start()

        for m in range(3):

            @pl.when(n == 2 * m + 1)
            def _():
                self.add_pair(m)
                if m == 2:
                    self.pass_on()

        pl.when(n == 7)(self.add_own)

    def end(self):
        def add(rows):
            near = self.near[0, rows].astype(F32) + self.near[1, rows].astype(F32)
            self.total[rows] = self.total[rows] + near

        for slots, span in (((6, 8), self.low), ((7, 9), self.high)):
            for slot in slots:
                self.copy(slot).wait_recv()
            self.over(span, add)
        for k in range(4):
            self.pair_copy(k).wait_send()
        for slot in range(4, 10):
            self.copy(slot).wait_send()


def norm_scale(values):
    return lax.rsqrt(jnp.mean(values * values, axis=-1, keepdims=True) + NORM_EPSILON)


def by_rows(rows, body, carry=0):
    def step(n, carry):
        return body(aligned(n * ROWS, ROWS), carry)

    return lax.fori_loop(0, rows // ROWS, step, carry)


def norm_back(values, gain, upstream):
    scale = norm_scale(values)
    scaled = gain * upstream
    inner = jnp.mean(scaled * values, axis=-1, keepdims=True)
    return (
        scale * scaled - values * scale * scale * scale * inner,
        jnp.sum(upstream * values * scale, axis=0, keepdims=True),
    )


REFS = (
    "tok", "cot", "gains", "weights",
    "block_out", "input_grad", "gain_sums", "mine", "theirs", "n1_held", "slot0", "slot1", "slot2", "slot3",
    "w0", "w1", "w2", "w3", "seq_a", "seq_b", "du", "act", "c_all", "gated", "mixed", "resid", "dresid", "total",
    "pair", "near", "joined", "g1", "g2", "g3", "stage", "sum", "tail", "outgoing", "tap_sums", "gain_in", "gain_line",
    "held", "loaded", "send_x", "recv_x", "send_z", "recv_z", "send_s", "recv_s", "send_c", "recv_c", "credit",
    "halo_send", "halo_recv", "send_g", "recv_g", "fetched", "fetches", "stored", "send_o", "recv_o",
    "send_a", "recv_a", "send_l", "recv_l",
)


def column_pieces(half):
    pieces = [(m * QUARTER + half * HALF_Q, m * HALF_Q, HALF_Q, 0) for m in range(4)]
    for k, (start, units) in enumerate(zip(UNIT_STARTS, UNIT_CHUNKS), 1):
        real = min(units, HALF_F - start)
        for m in range(3):
            first = 4 * QUARTER + m * UNITS + half * HALF_F + start
            pieces.append((first, STARTS[k] + m * units, real, units - real))
    return pieces


def block_kernel(layers, rows, *all_refs):
    r = dict(zip(REFS, all_refs, strict=True))
    tok, cot, gains = r["tok"], r["cot"], r["gains"]
    seq_a, seq_b, du, act = r["seq_a"], r["seq_b"], r["du"], r["act"]
    c_all, gated, mixed, total = r["c_all"], r["gated"], r["mixed"], r["total"]
    weights = (r["w0"], r["w1"], r["w2"], r["w3"])
    seg = tok.shape[0]
    _, shard, inner, _ = place()
    outer, at = line()
    me = 2 * shard + inner
    my_rows = aligned(me * seg, seg)
    chunks = list(zip(range(1, 1 + len(UNIT_CHUNKS)), UNIT_STARTS, UNIT_CHUNKS))
    gather = Gather(
        layers, rows, r["g1"], weights, r["send_x"], r["recv_x"], r["send_z"], r["recv_z"]
    )
    reduce = Reduce(
        layers, rows, (r["w2"], r["g1"], r["g2"], r["g3"]), (r["slot0"], r["slot1"], r["slot2"], r["slot3"]),
        r["stage"], r["w1"], r["sum"], r["outgoing"], r["mine"], r["theirs"],
        (r["send_g"], r["recv_g"], r["fetched"], r["fetches"], r["stored"], r["send_o"], r["recv_o"]),
    )

    def spread(buf, n):
        return Spread(buf, seg, SPREAD_SPLITS[n], r["send_s"].at[n], r["recv_s"].at[n])

    def collect(part, n):
        sems = r["send_c"].at[n], r["recv_c"].at[n]
        return Collect(part, seg, COLLECT_SPLITS[n], total, r["pair"], r["near"], r["joined"], *sems)

    one, up, two, three = spread(seq_a, 0), spread(seq_b, 1), spread(seq_a, 2), spread(seq_a, 3)
    branch, down, feed, inputs = collect(seq_a, 0), collect(seq_b, 1), collect(du, 2), collect(seq_a, 3)
    lanes = lax.broadcasted_iota(jnp.int32, (seg, WIDE), 1) < HALF_Q
    taps = pltpu.roll(gains[...], lax.rem(D - shard * QUARTER - inner * HALF_Q, D), 1)[2:5, :WIDE]
    kept = pl.ds(D, WIDE)
    sums, tap_sums = r["gain_sums"], r["tap_sums"]

    def block(t):
        return aligned(t * seg, seg)

    def mine(part):
        return pl.ds(pl.multiple_of(me * seg + part.start, 16), part.size)

    def first_norm():
        def rows(part, _):
            values = tok[part].astype(F32)
            seq_a[mine(part)] = (values * norm_scale(values) * gains[0:1, :]).astype(BF16)
            return 0

        by_rows(seg, rows)

    def up_start():
        seq_b[my_rows] = cot[...]
        up.start()

    def held():
        return pltpu.make_async_copy(seq_a, r["n1_held"], r["held"])

    def reload():
        return pltpu.make_async_copy(r["n1_held"], seq_b, r["held"])

    def project(s):
        for i in (0, 1):
            parts = dot(seq_a[block(2 * s + i)], weights[0][...])
            b = jnp.where(lanes, parts[:, :WIDE], 0.0)
            c = pltpu.roll(parts[:, 128 : 128 + 384], 384 - 64, 1)[:, :WIDE]
            x = parts[:, 384 : 384 + WIDE]
            c_all[s, pl.ds(i * seg, seg)] = jnp.where(lanes, c, 0.0)
            gated[s, pl.ds(8 + i * seg, seg)] = (b * x).astype(BF16).astype(F32)

    def ahead():
        return remote(
            gated.at[:, pl.ds(2 * seg, 8)], gated.at[:, pl.ds(0, 8)], r["halo_send"].at[0], r["halo_recv"].at[0], at(1)
        )

    def halo():
        pl.when(outer < layers - 1)(lambda: ahead().start())

        @pl.when(outer == 0)
        def _():
            gated[:, pl.ds(0, 8)] = jnp.zeros((GROUPS, 8, WIDE), F32)

    def convolved(s, i):
        return (
            taps[0:1, :] * gated[s, pl.ds(6 + i * seg, seg)]
            + taps[1:2, :] * gated[s, pl.ds(7 + i * seg, seg)]
            + taps[2:3, :] * gated[s, pl.ds(8 + i * seg, seg)]
        )

    def convolve(t):
        for i in (0, 1):

            @pl.when(t % 2 == i)
            def _():
                s = t // 2
                mixed[block(t)] = pltpu.roll(c_all[s, pl.ds(i * seg, seg)] * convolved(s, i), 64, 1).astype(BF16)

        seq_a[block(t)] = dot_rows(mixed[block(t)], weights[0][:, pl.ds(512, WIDE)]).astype(BF16)

    def branch_end():
        branch.end()
        allow(r["credit"].at[0])

    def second_norm():
        def rows(part, _):
            values = tok[part].astype(F32) + total[part]
            r["resid"][part] = values
            seq_a[mine(part)] = (values * norm_scale(values) * gains[1:2, :]).astype(BF16)
            return 0

        by_rows(seg, rows)
        pl.semaphore_wait(r["credit"].at[0], 3)

    def hidden(k, start, units, t):
        ref, here = weights[k], block(t)
        gate = dot(seq_a[here], ref[:, pl.ds(0, units)])
        upval = dot(seq_a[here], ref[:, pl.ds(units, units)])
        dact = dot(seq_b[here], ref[:, pl.ds(2 * units, units)])
        sigma = jax.nn.sigmoid(gate)
        silu = gate * sigma
        act[here, pl.ds(start, units)] = (silu * upval).astype(BF16)
        dgate = dact * upval * sigma * (1.0 + gate * (1.0 - sigma))
        du[here, pl.ds(2 * start, units)] = dgate.astype(BF16)
        du[here, pl.ds(2 * start + units, units)] = (dact * silu).astype(BF16)

    def slice_of(n):
        return jnp.where(outer < layers // 2, D // SLICE - 1 - n, n)

    def gate_up_grads(k, start, units, n):
        part = slice_of(n)
        left = seq_a[:, aligned(part * SLICE, SLICE, 128)]
        reduce.grads[k][aligned(part * SLICE, SLICE), pl.ds(0, 2 * units)] = dot_columns(
            left, du[:, pl.ds(2 * start, 2 * units)]
        ).astype(BF16)

    def down_grads(k, start, units, n):
        part = slice_of(n)
        left = seq_b[:, aligned(part * SLICE, SLICE, 128)]
        reduce.grads[k][aligned(part * SLICE, SLICE), pl.ds(2 * units, units)] = dot_columns(
            left, act[:, pl.ds(start, units)]
        ).astype(BF16)

    def grads(k, start, units, n):
        gate_up_grads(k, start, units, n)
        down_grads(k, start, units, n)
        reduce.direct(k, slice_of(n))

    def second(t):
        here = block(t)
        seq_b[here] = sum(
            dot_rows(du[here, pl.ds(2 * start, 2 * units)], weights[k][:, pl.ds(0, 2 * units)])
            for k, start, units in chunks
        ).astype(BF16)

    def down_end():
        down.end()
        reload().start()
        allow(r["credit"].at[1])

    def forward(t):
        here = block(t)
        du[here, pl.ds(0, D)] = sum(
            dot_rows(act[here, pl.ds(start, units)], weights[k][:, pl.ds(2 * units, units)])
            for k, start, units in chunks
        ).astype(BF16)

    def second_back():
        def rows(part, gain):
            dpart, dgain = norm_back(r["resid"][part], gains[1:2, :], total[part])
            dresid = cot[part].astype(F32) + dpart
            r["dresid"][part] = dresid
            seq_a[mine(part)] = dresid.astype(BF16)
            return gain + dgain

        sums[...] = jnp.zeros(sums.shape, F32)
        tap_sums[...] = jnp.zeros(tap_sums.shape, F32)
        sums[1:2, pl.ds(0, D)] = by_rows(seg, rows, jnp.zeros((1, D), F32))
        pl.semaphore_wait(r["credit"].at[1], 3)

    def mix_back(t):
        s, here = t // 2, block(t)
        dmixed = pltpu.roll(dot(seq_a[here], weights[0][:, pl.ds(512, WIDE)]), WIDE - 64, 1)
        dmixed = jnp.where(lanes, dmixed, 0.0)
        for i in (0, 1):

            @pl.when(t % 2 == i)
            def _():
                du[here, kept] = (dmixed * convolved(s, i)).astype(BF16)
                c_all[s, pl.ds(i * seg, seg)] = dmixed * c_all[s, pl.ds(i * seg, seg)]

    def after():
        return remote(
            c_all.at[:, pl.ds(0, 8)], c_all.at[:, pl.ds(2 * seg, 8)], r["halo_send"].at[1], r["halo_recv"].at[1], at(-1)
        )

    def halo_back():
        pl.when(outer > 0)(lambda: after().start())

        @pl.when(outer == layers - 1)
        def _():
            c_all[:, pl.ds(2 * seg, 8)] = jnp.zeros((GROUPS, 8, WIDE), F32)

    def conv_back(n):
        for i in (0, 1):
            pl.when(n // GROUPS == i)(functools.partial(conv_back_half, n % GROUPS, i))

    def conv_back_half(s, i):
        t = block(2 * s + i)
        dconv = c_all[s, pl.ds(i * seg, seg)]
        dgated = (
            taps[2:3, :] * dconv
            + taps[1:2, :] * c_all[s, pl.ds(1 + i * seg, seg)]
            + taps[0:1, :] * c_all[s, pl.ds(2 + i * seg, seg)]
        )
        parts = dot(seq_b[t], weights[0][:, pl.ds(0, 640)])
        db = dgated * parts[:, 384:640]
        dx = dgated * parts[:, :WIDE]
        dc = jnp.concatenate([du[t, kept].astype(F32), jnp.zeros((seg, 128), F32)], axis=1)
        dc = pltpu.roll(dc, 64, 1)
        act[t, pl.ds(0, 128)] = db[:, :128].astype(BF16)
        act[t, pl.ds(128, 128)] = (db[:, 128:] + dc[:, :128]).astype(BF16)
        act[t, pl.ds(256, 128)] = dc[:, 128:256].astype(BF16)
        act[t, pl.ds(384, WIDE)] = dx.astype(BF16)
        act[t, pl.ds(640, 128)] = jnp.zeros((seg, 128), BF16)
        for k in range(3):
            moved = gated[s, pl.ds(6 + k + i * seg, seg)]
            tap_sums[k : k + 1] = tap_sums[k : k + 1] + jnp.sum(dconv * moved, axis=0, keepdims=True)

    def conv_grads(n):
        part = slice_of(n)
        held_rows, cols = aligned(part * SLICE, SLICE), aligned(part * SLICE, SLICE, 128)
        ref = reduce.grads[0]
        of_parts = dot_columns(seq_b[:, cols], act[:, pl.ds(0, CONV_COLS)])
        ref[held_rows, pl.ds(0, 512)] = of_parts[:, :512].astype(BF16)
        of_mixed = dot_columns(seq_a[:, cols], mixed[...])
        ref[held_rows, pl.ds(512, WIDE)] = (of_parts[:, 512:] + of_mixed).astype(BF16)
        reduce.direct(0, part)

    def feed_end():
        feed.end()
        allow(r["credit"].at[2])
        r["block_out"][...] = (r["resid"][...] + total[...]).astype(BF16)

    def first(t):
        here = block(t)
        seq_a[here] = dot_rows(act[here, pl.ds(0, 640)], weights[0][:, pl.ds(0, 640)]).astype(BF16)

    def first_back():
        def rows(part, gain):
            dpart, dgain = norm_back(tok[part].astype(F32), gains[0:1, :], total[part])
            r["input_grad"][part] = (r["dresid"][part] + dpart).astype(BF16)
            return gain + dgain

        sums[0:1, pl.ds(0, D)] = by_rows(seg, rows, jnp.zeros((1, D), F32))
        sums[2:5, aligned(me * WIDE, WIDE, 128)] = tap_sums[0:3]

    def gains_across(n):
        return remote(sums, r["gain_in"].at[n], r["send_a"].at[n], r["recv_a"].at[n], partners()[n])

    def gains_add(n):
        gains_across(n).wait()
        sums[...] = sums[...] + r["gain_in"][n]

    def line_copy(sign, steps):
        slot = (0 if sign > 0 else 1, steps - 1)
        return remote(
            sums, r["gain_line"].at[slot], r["send_l"].at[slot], r["recv_l"].at[slot], at(sign * steps)
        )

    def gains_line():
        for steps in range(1, layers):
            for sign in (1, -1):
                pl.when(in_line(outer + sign * steps, layers))(line_copy(sign, steps).start)

    def gains_end():
        for steps in range(1, layers):
            for sign in (1, -1):
                pl.when(in_line(outer + sign * steps, layers))(line_copy(sign, steps).wait_send)
                pl.when(in_line(outer - sign * steps, layers))(line_copy(sign, steps).wait_recv)

        own_sums = sums[...]
        for origin in range(layers):
            for steps in range(1, layers):
                for sign in (1, -1):

                    @pl.when((outer - sign * steps == origin))
                    def _():
                        came = r["gain_line"][0 if sign > 0 else 1, steps - 1]
                        sums[...] = came if origin == 0 else sums[...] + came

            if origin > 0:

                @pl.when(outer == origin)
                def _():
                    sums[...] = sums[...] + own_sums

    def end():
        reduce.finish(0)
        for k in range(len(WIDTHS)):
            reduce.wait_sent(k)
        pl.when(outer < layers - 1)(lambda: ahead().wait_send())
        pl.when(outer > 0)(lambda: after().wait_send())

    windows = [
        (r["resid"], 0, D), (r["dresid"], D, D), (total, 2 * D, D), (r["resid"], 3 * D, D),
        (r["tail"], 4 * D, GROUP_COLS - 4 * D),
    ]

    def load(n):
        ref, first, width = windows[n]
        return pltpu.make_async_copy(
            r["weights"].at[:, pl.ds(first, width)], ref.at[pl.ds(0, rows)], r["loaded"].at[n]
        )

    def start():
        for n in (0, 1, 2, 4):
            load(n).start()
        greet(layers)
        load(0).wait()
        cut(0)
        load(3).start()
        greeted(layers)

    def cut(k):
        def read(part, first, width):
            found = []
            for n, (ref, low, size) in enumerate(windows):
                start, stop = max(first, low), min(first + width, low + size)
                if start < stop and (n == 0) == (k == 0):
                    found.append(ref[part, start - low : stop - low])
            return found

        size = band(rows, 96)

        def cut_band(n, _):
            part = aligned(n * size, size)
            halves = []
            for half in (0, 1):
                pieces = []
                for first, own, width, padding in column_pieces(half):
                    if STARTS[k] <= own < STARTS[k] + WIDTHS[k]:
                        pieces += read(part, first, width)
                        if padding:
                            pieces.append(jnp.zeros((size, padding), F32))
                halves.append(jnp.concatenate(pieces, axis=1))
            is_low = inner == 0
            seq = lax.axis_index("seq")
            own_rows = aligned(seq * rows + n * size, size)
            weights[k][own_rows, :] = jnp.where(is_low, halves[0], halves[1]).astype(BF16)
            gather.other_rows(k)[part, :] = jnp.where(is_low, halves[1], halves[0]).astype(BF16)
            return 0

        for n in (1, 2, 3, 4) if k == CUT_FIRST else ():
            load(n).wait()
        lax.fori_loop(0, rows // size, cut_band, 0)

    def hold():
        held().start()

    def hold_end():
        held().wait()

    def halo_end():
        pl.when(outer > 0)(lambda: ahead().wait_recv())

    def reload_end():
        reload().wait()

    def halo_back_end():
        pl.when(outer < layers - 1)(lambda: after().wait_recv())

    def feed_credit():
        pl.semaphore_wait(r["credit"].at[2], 3)

    def from_spread(moved, body):
        def step(n):
            for m in range(8):
                if moved.before(m):

                    @pl.when(n == m)
                    def _():
                        for act in moved.before(m):
                            act()

            body(moved.index(n))

        return step

    def each(body, *cases):
        return [functools.partial(body, *(case if isinstance(case, tuple) else (case,))) for case in cases]

    every = range(len(WIDTHS))
    cuts = each(cut, *every)
    exchange, send_own, send_other = (
        each(body, *every) for body in (gather.exchange, gather.send_own, gather.send_other)
    )
    step = [each(gather.steps, (k, 1, 1), (k, 2, 2), (k, 3)) for k in every]
    join_far = each(reduce.join, *((k, layers - 2, 2) for k in every))
    join_near = each(reduce.join, *((k, 1, 1) for k in every))
    final = each(reduce.final, (0, 3), 1, (2, 1), (3, 2))
    feed_pair = each(feed.add_pair, 0, 1, 2)
    gain_send = [lambda n=n: gains_across(n).start() for n in range(3)]
    gain_add = each(gains_add, 0, 1, 2)
    d3_far = functools.partial(reduce.direct, 3, least=2)
    d3_near = functools.partial(reduce.direct, 3, most=1)
    blocks, parts = 2 * GROUPS, D // SLICE
    proj = Loop(GROUPS, project)
    mix = Loop(blocks, lambda n: branch.make(n, convolve))
    hid1 = Loop(blocks, from_spread(two, functools.partial(hidden, *chunks[0])))
    hid2, hid3 = (Loop(blocks, functools.partial(hidden, *chunk)) for chunk in chunks[1:])
    grad1, grad2 = (Loop(parts, functools.partial(grads, *chunk)) for chunk in chunks[:2])
    down3 = Loop(parts, functools.partial(down_grads, *chunks[2]))
    back2 = Loop(blocks, lambda n: down.make(n, second))
    gate3 = Loop(parts, functools.partial(gate_up_grads, *chunks[2]))
    ffn = Loop(blocks, forward)
    back_mix = Loop(blocks, from_spread(three, mix_back))
    back_conv = Loop(blocks, conv_back)
    grad0 = Loop(parts, conv_grads)
    back1 = Loop(blocks, lambda n: inputs.make(n, first))
    play(
        [
            start, exchange[0], send_own[0], first_norm, cuts[1], send_other[0], one.start, send_own[1], cuts[2],
            exchange[1], step[0][0], one.first, up_start, one.near, exchange[2], step[0][1], cuts[3], send_other[1],
            one.far, step[0][2], one.end, proj[0], proj[1], up.first, up.near, hold, proj[2], proj[3], halo,
            step[1][0], hold_end, halo_end, mix[0], mix[1], mix[2], mix[3], mix[4], up.far, mix[5], mix[6], mix[7],
            step[1][1], up.end, exchange[3], send_own[3], send_other[2], send_own[2], branch_end, second_norm,
            two.start, step[1][2], send_other[3], hid1[0], hid1[1], hid1[2], hid1[3], hid1[4], step[2][0], hid1[5],
            gather.crossed, hid1[6], hid1[7], two.sent, grad1[0], grad1[1], grad1[2], step[2][1], step[3][0],
            step[2][2], grad1[3], hid2[0], hid2[1], hid2[2], hid2[3], hid2[4], hid2[5], hid2[6], hid2[7], grad2[0],
            grad2[1], grad2[2], grad2[3], step[3][1], step[3][2], hid3[0], hid3[1], hid3[2], hid3[3], hid3[4],
            hid3[5], hid3[6], hid3[7], down3[0], down3[1], down3[2], down3[3], back2[0], back2[1], join_far[1],
            back2[2], back2[3], back2[4], back2[5], back2[6], back2[7], gate3[0], gate3[1], join_near[1], gate3[2],
            gate3[3], down_end, second_back, three.start, d3_far, ffn[0], ffn[1], ffn[2], ffn[3], ffn[4], ffn[5],
            ffn[6], ffn[7], back_mix[0], back_mix[1], feed.push, back_mix[2], join_far[2], feed_pair[0],
            back_mix[3], gather.finish, back_mix[4], feed_pair[1], back_mix[5], reload_end, back_mix[6],
            feed_pair[2], back_mix[7], three.sent, halo_back, back_conv[0], join_near[2], back_conv[1], d3_near,
            back_conv[2], back_conv[3], feed.pass_on, final[1], feed.add_own, halo_back_end, back_conv[4],
            join_far[3], back_conv[5], back_conv[6], back_conv[7], grad0[0], grad0[1], grad0[2], grad0[3], feed_end,
            join_near[3], feed_credit, back1[0], back1[1], back1[2], back1[3], back1[4], join_far[0], back1[5],
            back1[6], final[2], back1[7], join_near[0], inputs.end, first_back, gain_send[0], final[3], gain_add[0],
            gain_send[1], gain_add[1], gain_send[2], gain_add[2], gains_line, final[0], gains_end, end,
        ]
    )


class Loop:
    def __init__(self, count, body):
        self.count, self.body = count, body

    def __getitem__(self, n):
        return (self, n)


def play(order):
    order = list(order)
    while order:
        entry = order.pop(0)
        if not isinstance(entry, tuple):
            entry()
            continue
        loop, _ = entry
        between = {}
        for n in range(1, loop.count):
            between[n] = []
            while order[0] != (loop, n):
                between[n].append(order.pop(0))
            order.pop(0)

        def turn(n, _):
            for m, acts in between.items():
                if acts:

                    @pl.when(n == m)
                    def _():
                        play(acts)

            loop.body(n)
            return 0

        lax.fori_loop(0, loop.count, turn, 0)


def block_step(tok, cot, gains, weights, layers):
    rows, seg = weights.shape[0], tok.shape[0]
    count = len(WIDTHS)
    tokens = 2 * GROUPS * seg
    vmem, anywhere = pl.BlockSpec(memory_space=pltpu.VMEM), pl.BlockSpec(memory_space=pl.ANY)
    shape, scratch = jax.ShapeDtypeStruct, pltpu.VMEM
    dma, regular = pltpu.SemaphoreType.DMA, pltpu.SemaphoreType.REGULAR
    hops = layers - 1
    wide, biggest = sum(WIDTHS), max(WIDTHS)
    out_shape = [
        shape((seg, D), BF16),
        shape((seg, D), BF16),
        shape((8, 2 * GROUPS * WIDE), F32),
        shape((rows, wide), F32),
        shape((rows, wide), BF16),
        shape((tokens, D), BF16),
    ] + [shape((2, hops, 2 * rows, width), BF16) for width in WIDTHS]
    scratch_shapes = (
        [scratch((D, width), BF16) for width in WIDTHS]
        + [
            scratch((tokens, D), BF16),
            scratch((tokens, D), BF16),
            scratch((tokens, 2 * PAD_F), BF16),
            scratch((tokens, PAD_F), BF16),
            scratch((GROUPS, 8 + 2 * seg, WIDE), F32),
            scratch((GROUPS, 8 + 2 * seg, WIDE), F32),
            scratch((tokens, WIDE), BF16),
            scratch((seg, D), F32),
            scratch((seg, D), F32),
            scratch((seg, D), F32),
            scratch((4, seg, D), BF16),
            scratch((2, seg, D), BF16),
            scratch((seg, D), BF16),
        ]
        + [scratch((D, width), BF16) for width in WIDTHS[1:]]
        + [
            scratch((2 * rows, biggest), BF16),
            scratch((rows, biggest), F32),
            scratch((rows, GROUP_COLS - 4 * D), F32),
            scratch((rows, wide), BF16),
            scratch((8, WIDE), F32),
            scratch((3, 8, 2 * GROUPS * WIDE), F32),
            scratch((2, hops, 8, 2 * GROUPS * WIDE), F32),
            dma,
            dma((5,)),
            dma((count,)),
            dma((count,)),
            dma((count, 2, hops, 2)),
            dma((count, 2, hops, 2)),
            dma((4, 11)),
            dma((4, 11)),
            dma((4, 10)),
            dma((4, 10)),
            regular((3,)),
            dma((2,)),
            dma((2,)),
            dma((count, 2, hops)),
            dma((count, 2, hops)),
            dma,
            dma((4,)),
            dma((count,)),
            dma((count,)),
            dma((count,)),
            dma((3,)),
            dma((3,)),
            dma((2, hops)),
            dma((2, hops)),
        ]
    )
    return pl.pallas_call(
        functools.partial(block_kernel, layers, rows),
        out_shape=out_shape,
        in_specs=[vmem] * 3 + [anywhere],
        out_specs=[vmem] * 3 + [anywhere] * (3 + count),
        scratch_shapes=scratch_shapes,
        compiler_params=pltpu.CompilerParams(
            collective_id=0, has_side_effects=True, vmem_limit_bytes=VMEM_BYTES
        ),
        name="block_step",
    )(tok, cot, gains, weights)[:5]


def band(rows, most):
    return max(size for size in range(16, most + 1, 16) if rows % size == 0)


def adam_update(param, grad, first, second, rate, decay):
    first_new = MOMENT_DECAY * first + (1.0 - MOMENT_DECAY) * grad
    second_new = SQUARE_DECAY * second + (1.0 - SQUARE_DECAY) * grad * grad
    root = jnp.sqrt(second_new * (1.0 / (1.0 - SQUARE_DECAY**STEP))) + ADAM_EPSILON
    step = first_new * (rate / (1.0 - MOMENT_DECAY**STEP)) / root
    return (first_new, second_new, param * (1.0 - rate * decay) - step)


def update_kernel(
    inner_ref, mine_ref, theirs_ref, weights_ref, first_ref, second_ref, sums_ref, gains_ref, gains_first_ref,
    gains_second_ref, block_ref, input_ref, grad_out, first_out, second_out, weights_out, gains_grad_out,
    gains_first_out, gains_second_out, gains_out, block_out, input_out,
):
    is_low = inner_ref[0] == 0
    mine, theirs = mine_ref[...], theirs_ref[...].astype(F32)
    for half in (0, 1):
        chosen = jnp.where(is_low, mine, theirs) if half == 0 else jnp.where(is_low, theirs, mine)
        for first, own, width, _ in column_pieces(half):
            grad_out[:, first : first + width] = chosen[:, own : own + width]
    first_out[...], second_out[...], weights_out[...] = adam_update(
        weights_ref[...], grad_out[...], first_ref[...], second_ref[...], WEIGHT_RATE, WEIGHT_DECAY
    )

    @pl.when(pl.program_id(0) == 0)
    def _():
        gains_grad_out[0:2] = sums_ref[0:2, :D]
        for n in range(2 * GROUPS):
            gains_grad_out[2:5, n * HALF_Q : (n + 1) * HALF_Q] = sums_ref[2:5, n * WIDE : n * WIDE + HALF_Q]
        gains_first_out[...], gains_second_out[...], gains_out[...] = adam_update(
            gains_ref[...], gains_grad_out[...], gains_first_ref[...], gains_second_ref[...], GAIN_RATE, 0.0
        )
        block_out[...] = block_ref[...]
        input_out[...] = input_ref[...]


def update(inner, mine, theirs, weights, first, second, sums, gains, gains_first, gains_second, block, grad):
    rows, cols = weights.shape
    wide = mine.shape[1]
    size = band(rows, 32)
    by_row = lambda width: pl.BlockSpec((size, width), lambda n: (n, 0))
    whole = lambda values: pl.BlockSpec(values.shape, lambda n: (0, 0))
    shape = jax.ShapeDtypeStruct
    return pl.pallas_call(
        update_kernel,
        grid=(rows // size,),
        out_shape=[shape((rows, cols), F32)] * 4 + [shape(gains.shape, F32)] * 4 + [shape(block.shape, BF16)] * 2,
        in_specs=[pl.BlockSpec(memory_space=pltpu.SMEM)]
        + [by_row(wide)] * 2
        + [by_row(cols)] * 3
        + [whole(sums)]
        + [whole(gains)] * 3
        + [whole(block)] * 2,
        out_specs=[by_row(cols)] * 4 + [whole(gains)] * 4 + [whole(block)] * 2,
        compiler_params=pltpu.CompilerParams(vmem_limit_bytes=VMEM_BYTES),
        name="update",
    )(inner, mine, theirs, weights, first, second, sums, gains, gains_first, gains_second, block, grad)


def on_device(
    tokens, gains_taps, weights, cotangent, weight_first, weight_second, gains_first, gains_second
):
    layers = lax.axis_size("seq") // 2
    inner_word = (lax.axis_index("seq") % 2).astype(jnp.int32).reshape(1)
    block_out, input_grad, gain_sums, mine, theirs = block_step(
        tokens[0], cotangent[0], gains_taps, weights, layers
    )
    (
        weight_grad, weight_first_new, weight_second_new, weight_new,
        gains_grad, gains_first_new, gains_second_new, gains_new, block_out, input_grad,
    ) = update(
        inner_word, mine, theirs, weights, weight_first, weight_second,
        gain_sums, gains_taps, gains_first, gains_second, block_out, input_grad,
    )
    return (
        block_out[None],
        input_grad[None],
        weight_grad,
        weight_first_new,
        weight_second_new,
        weight_new,
        gains_grad,
        gains_first_new,
        gains_second_new,
        gains_new,
    )


def solution(mesh):
    tokens, rows, whole = P("shard", "seq", None), P("seq", "shard"), P()
    return jax.shard_map(
        on_device,
        mesh=mesh,
        in_specs=(tokens, whole, rows, tokens, rows, rows, whole, whole),
        out_specs=(tokens, tokens, rows, rows, rows, rows, whole, whole, whole, whole),
        check_vma=False,
    )
```

```python
import functools

import jax
import jax.numpy as jnp
from jax import lax
from jax.experimental import pallas as pl
from jax.experimental.pallas import tpu as pltpu
from jax.sharding import PartitionSpec as P

D = 1536
FF = 6912
STEP = 10
GROUPS = 4
QUARTER = D // GROUPS
UNITS = FF // GROUPS
GROUP_COLS = 4 * QUARTER + 3 * UNITS
HALF_Q = QUARTER // 2
HALF_F = UNITS // 2
LANES = 128
PAD_F = -(-HALF_F // LANES) * LANES
WIDE = 256
CONV_COLS = 4 * HALF_Q
UNIT_CHUNKS = (384, 256, PAD_F - 640)
UNIT_STARTS = (0, 384, 640)
WIDTHS = (CONV_COLS,) + tuple(3 * units for units in UNIT_CHUNKS)
STARTS = tuple(sum(WIDTHS[:k]) for k in range(len(WIDTHS)))
SPREAD_SPLITS = (208, 160, 112, 112)
COLLECT_SPLITS = (128, 128, 96, 112)
REACH = (1, 1, 1, 1)
CUT_FIRST = 1
SLICE = 384
TILE = 16
ROWS = 48

MOMENT_DECAY = 0.9
SQUARE_DECAY = 0.95
ADAM_EPSILON = 1e-08
NORM_EPSILON = 1e-05
WEIGHT_RATE = 0.02
GAIN_RATE = 0.2
WEIGHT_DECAY = 0.1

BF16 = jnp.bfloat16
F32 = jnp.float32
MESH = pl.DeviceIdType.MESH
VMEM_BYTES = 63 * 1024 * 1024


def place():
    seq, shard = lax.axis_index("seq"), lax.axis_index("shard")
    inner, core = lax.rem(seq, 2), lax.rem(shard, 2)
    return seq, shard, inner, core


def partners():
    seq, shard, inner, core = place()
    across = {"seq": seq + 1 - 2 * inner, "shard": shard}
    beside = {"seq": seq, "shard": lax.rem(shard + 2, 4)}
    twin = {"seq": seq, "shard": shard + 1 - 2 * core}
    return across, beside, twin


def remote(src, dst, send, recv, device):
    return pltpu.make_async_remote_copy(
        src_ref=src, dst_ref=dst, send_sem=send, recv_sem=recv, device_id=device, device_id_type=MESH
    )


def line():
    seq, shard, _, _ = place()
    size = lax.axis_size("seq")
    return seq // 2, lambda steps: {"seq": lax.rem(seq + 2 * steps + size, size), "shard": shard}


def greet(layers):
    outer, at = line()
    barrier = pltpu.get_barrier_semaphore()
    for device in partners():
        pl.semaphore_signal(barrier, inc=1, device_id=device, device_id_type=MESH)
    for steps in range(1, layers):
        for sign in (1, -1):

            @pl.when(in_line(outer + sign * steps, layers))
            def _():
                pl.semaphore_signal(barrier, inc=1, device_id=at(sign * steps), device_id_type=MESH)


def greeted(layers):
    pl.semaphore_wait(pltpu.get_barrier_semaphore(), 3 + layers - 1)


def in_line(index, layers):
    return (index >= 0) & (index < layers)


def allow(credit):
    for device in partners():
        pl.semaphore_signal(credit, inc=1, device_id=device, device_id_type=MESH)


def dot(left, right):
    return jnp.dot(left, right, preferred_element_type=F32)


def dot_rows(left, right):
    return lax.dot_general(left, right, (((1,), (1,)), ((), ())), preferred_element_type=F32)


def dot_columns(left, right):
    return lax.dot_general(left, right, (((0,), (0,)), ((), ())), preferred_element_type=F32)


def aligned(start, size, multiple=16):
    return pl.ds(pl.multiple_of(start, multiple), size)


class Gather:
    def __init__(self, layers, rows, oth, outs, send_x, recv_x, send_z, recv_z):
        self.layers, self.rows, self.oth, self.outs = layers, rows, oth, outs
        self.send_x, self.recv_x, self.send_z, self.recv_z = send_x, recv_x, send_z, recv_z
        self.seq, _, self.inner, _ = place()
        self.outer, self.at = line()
        self.across = partners()[0]

    def seq_rows(self, index):
        return aligned(index * self.rows, self.rows)

    def layer_rows(self, direction, distance):
        origin = self.outer - distance if direction == 0 else self.outer + distance
        return aligned(origin * 2 * self.rows, 2 * self.rows)

    def copy(self, k, src, dst, direction, distance, hop, piece):
        slot = (k, direction, distance + hop - 1, piece)
        return remote(
            src, dst, self.send_z.at[slot], self.recv_z.at[slot], self.at(hop if direction == 0 else -hop)
        )

    def goes(self, direction, hop):
        return in_line(self.outer + (hop if direction == 0 else -hop), self.layers)

    def has_come(self, direction, distance):
        return in_line(self.outer + (-distance if direction == 0 else distance), self.layers)

    def hops(self, k, distance):
        return range(1, min(REACH[k], self.layers - 1 - distance) + 1)

    def own_copy(self, k, direction, hop):
        here = self.outs[k].at[self.seq_rows(self.seq)]
        return self.copy(k, here, here, direction, 0, hop, 0)

    def other_copy(self, k, direction, hop):
        there = self.outs[k].at[self.seq_rows(self.seq + 1 - 2 * self.inner)]
        return self.copy(k, there, there, direction, 0, hop, 1)

    def pass_copy(self, k, direction, distance, hop):
        ref = self.outs[k].at[self.layer_rows(direction, distance)]
        return self.copy(k, ref, ref, direction, distance, hop, 0)

    def other_rows(self, k):
        return self.oth.at[pl.ds(k * self.rows, self.rows), pl.ds(0, WIDTHS[k])]

    def exchange(self, k):
        self.x_copy(k).start()

    def x_copy(self, k):
        here = self.outs[k].at[self.seq_rows(self.seq)]
        return remote(self.other_rows(k), here, self.send_x.at[k], self.recv_x.at[k], self.across)

    def crossed(self):
        for k in range(len(self.outs)):
            self.x_copy(k).wait_send()

    def send_own(self, k):
        for hop in self.hops(k, 0):
            for direction in (0, 1):

                @pl.when(self.goes(direction, hop))
                def _():
                    self.own_copy(k, direction, hop).start()

    def send_other(self, k):
        self.x_copy(k).wait_recv()
        for hop in self.hops(k, 0):
            for direction in (0, 1):

                @pl.when(self.goes(direction, hop))
                def _():
                    self.other_copy(k, direction, hop).start()

    def step(self, k, distance):
        for direction in (0, 1):

            @pl.when(self.has_come(direction, distance))
            def _():
                if distance <= REACH[k]:
                    origin = self.outer - distance if direction == 0 else self.outer + distance
                    for piece in (0, 1):
                        index = 2 * origin + (self.inner if piece == 0 else 1 - self.inner)
                        ref = self.outs[k].at[self.seq_rows(index)]
                        self.copy(k, ref, ref, direction, distance - 1, 1, piece).wait_recv()
                else:
                    ref = self.outs[k].at[self.layer_rows(direction, distance)]
                    self.copy(k, ref, ref, direction, distance - 1, 1, 0).wait_recv()
                if distance % REACH[k] == 0:
                    for hop in self.hops(k, distance):

                        @pl.when(self.goes(direction, hop))
                        def _():
                            self.pass_copy(k, direction, distance, hop).start()

    def steps(self, k, first, last=None):
        last = self.layers - 1 if last is None else min(last, self.layers - 1)
        for distance in range(first, last + 1):
            self.step(k, distance)

    def finish(self):
        for k in range(len(self.outs)):
            for distance in range(0, self.layers - 1, REACH[k]):
                for hop in self.hops(k, distance):
                    for direction in (0, 1):

                        @pl.when(self.goes(direction, hop) & self.has_come(direction, distance))
                        def _():
                            if distance == 0:
                                self.own_copy(k, direction, hop).wait_send()
                                self.other_copy(k, direction, hop).wait_send()
                            else:
                                self.pass_copy(k, direction, distance, hop).wait_send()


class Reduce:
    def __init__(self, layers, rows, grads, slots, stage, spare, total, outgoing, mine, theirs, sems):
        self.layers, self.rows, self.grads, self.slots = layers, rows, grads, slots
        self.stage, self.spare, self.total, self.outgoing = stage, spare, total, outgoing
        self.mine, self.theirs = mine, theirs
        self.send_g, self.recv_g, self.fetched, self.fetches, self.stored, self.send_o, self.recv_o = sems
        _, _, self.inner, _ = place()
        self.outer, self.at = line()
        self.across = partners()[0]

    def owner(self, direction, distance):
        return self.outer + distance if direction == 0 else self.outer - distance

    def upstream(self, direction, steps):
        return in_line(self.outer - steps if direction == 0 else self.outer + steps, self.layers)

    def block(self, k, owner):
        return self.grads[k].at[aligned(owner * 2 * self.rows, 2 * self.rows), pl.ds(0, WIDTHS[k])]

    def copy(self, k, src, direction, distance):
        slot = (direction, distance - 1)
        return remote(
            src,
            self.slots[k].at[slot],
            self.send_g.at[(k,) + slot],
            self.recv_g.at[(k,) + slot],
            self.at(1 if direction == 0 else -1),
        )

    def send(self, k, direction, distance):
        self.copy(k, self.block(k, self.owner(direction, distance)), direction, distance).start()

    def direct(self, k, part=None, least=1, most=None):
        for distance in range(most or self.layers - 1, least - 1, -1):
            for direction in (0, 1):
                owner = self.owner(direction, distance)
                here = in_line(owner, self.layers) & jnp.logical_not(self.upstream(direction, 1))
                if part is not None:
                    here = here & (owner * 2 * self.rows // SLICE == part)

                @pl.when(here)
                def _():
                    self.send(k, direction, distance)

    def fetch(self, k, direction, distance):
        slot = self.slots[k].at[direction, distance - 1]
        self.copy(k, slot, direction, distance).wait_recv()
        held = self.stage.at[:, pl.ds(0, WIDTHS[k])]
        copy = pltpu.make_async_copy(slot, held, self.fetched)
        copy.start()
        copy.wait()

    def tiles(self, body):
        def step(n, _):
            body(aligned(n * TILE, TILE))
            return 0

        lax.fori_loop(0, 2 * self.rows // TILE, step, 0)

    def join(self, k, most, least):
        cols = pl.ds(0, WIDTHS[k])
        for distance in range(most, least - 1, -1):
            for direction in (0, 1):
                owner = self.owner(direction, distance)

                @pl.when(in_line(owner, self.layers) & self.upstream(direction, 1))
                def _():
                    def add(tile):
                        base = self.owner(direction, distance) * 2 * self.rows
                        rows = pl.ds(pl.multiple_of(base + tile.start, 16), TILE)
                        ref = self.grads[k]
                        ref[rows, cols] = (
                            ref[rows, cols].astype(F32) + self.stage[tile, cols].astype(F32)
                        ).astype(BF16)

                    self.fetch(k, direction, distance + 1)
                    self.tiles(add)
                    self.send(k, direction, distance)

    def final(self, k, before=None):
        cols = pl.ds(0, WIDTHS[k])
        came = [(1, 0), (1, 1)]

        def fetch(n, distance, direction):
            return pltpu.make_async_copy(
                self.slots[k].at[direction, distance - 1],
                self.spare.at[pl.ds(n * 2 * self.rows, 2 * self.rows), cols],
                self.fetches.at[n],
            )

        for n, (distance, direction) in enumerate(came):

            @pl.when(self.upstream(direction, distance))
            def _():
                self.copy(k, self.slots[k].at[direction, distance - 1], direction, distance).wait_recv()
                fetch(n, distance, direction).start()

        if before is not None:
            self.store(before).wait()

        here, there = self.inner * self.rows, (1 - self.inner) * self.rows

        def each(base, body):
            def step(n, _):
                body(base + n * TILE, n * TILE)
                return 0

            lax.fori_loop(0, self.rows // TILE, step, 0)

        for n, (distance, direction) in enumerate(came):

            @pl.when(self.upstream(direction, distance))
            def _():
                fetch(n, distance, direction).wait()

        def add_up(flags):
            def total(rows):
                value = self.grads[k][aligned(self.outer * 2 * self.rows + rows, TILE), cols].astype(F32)
                for n, flag in enumerate(flags):
                    if flag:
                        value = value + self.spare[aligned(n * 2 * self.rows + rows, TILE), cols].astype(F32)
                return value

            def send(rows, at):
                self.outgoing[aligned(at, TILE), pl.ds(STARTS[k], WIDTHS[k])] = total(rows).astype(BF16)

            def keep(rows, at):
                self.total[aligned(at, TILE), cols] = total(rows)

            each(there, send)
            self.over(k).start()
            each(here, keep)
            self.store(k).start()

        patterns = {}
        for place_in_line in range(self.layers):
            flags = tuple(
                0 <= (place_in_line - distance if direction == 0 else place_in_line + distance) < self.layers
                for distance, direction in came
            )
            patterns.setdefault(flags, []).append(place_in_line)
        for flags, places in patterns.items():
            here_now = functools.reduce(jnp.logical_or, [self.outer == p for p in places])

            @pl.when(here_now)
            def _():
                add_up(flags)

    def over(self, k):
        wide = pl.ds(STARTS[k], WIDTHS[k])
        return remote(
            self.outgoing.at[:, wide], self.theirs.at[:, wide], self.send_o.at[k], self.recv_o.at[k], self.across
        )

    def store(self, k):
        return pltpu.make_async_copy(
            self.total.at[:, pl.ds(0, WIDTHS[k])], self.mine.at[:, pl.ds(STARTS[k], WIDTHS[k])], self.stored.at[k]
        )

    def wait_sent(self, k):
        for distance in range(1, self.layers):
            for direction in (0, 1):
                owner = self.owner(direction, distance)

                @pl.when(in_line(owner, self.layers))
                def _():
                    self.copy(k, self.block(k, owner), direction, distance).wait_send()

    def finish(self, before):
        self.store(before).wait()
        for k in range(len(self.grads)):
            self.over(k).wait()


class Spread:
    slots = range(11)

    def __init__(self, buf, seg, split, send, recv):
        self.buf, self.seg, self.split, self.send, self.recv = buf, seg, split, send, recv

    def index(self, n):
        _, shard, inner, core = place()
        row, flip, other = (n // 2) % 2, n // 4, n % 2
        return 2 * (lax.rem(shard + 2 * row, 4) + other * (1 - 2 * core)) + inner + flip * (1 - 2 * inner)

    def copy(self, slot):
        across, beside, twin = partners()
        low, high, whole = (0, self.split), (self.split, self.seg - self.split), (0, self.seg)
        n, (first, size), device = {
            0: (0, low, across),
            9: (0, high, across),
            1: (0, high, beside),
            10: (0, low, beside),
            2: (0, whole, twin),
            3: (4, low, beside),
            4: (4, whole, twin),
            5: (2, high, across),
            6: (2, whole, twin),
            7: (6, low, twin),
            8: (6, high, twin),
        }[slot]
        ref = self.buf.at[aligned(self.index(n) * self.seg + first, size)]
        return remote(ref, ref, self.send.at[slot], self.recv.at[slot], device)

    def push(self, *slots):
        for slot in slots:
            self.copy(slot).start()

    def came(self, *slots):
        for slot in slots:
            self.copy(slot).wait_recv()

    def start(self):
        self.push(0, 1, 9, 10, 2)

    def first(self):
        self.came(1)
        self.push(5)
        self.came(0)
        self.push(3)

    def near(self):
        self.came(10)
        self.push(6)
        self.came(9)
        self.push(4)

    def far(self):
        self.came(3)
        self.push(7)
        self.came(5)
        self.push(8)

    def sent(self):
        for slot in self.slots:
            self.copy(slot).wait_send()

    def end(self):
        self.came(2, 4, 6, 7, 8)
        self.sent()

    def before(self, n):
        return {
            1: (lambda: self.came(2),),
            2: (self.first, self.near),
            3: (lambda: self.came(6),),
            5: (lambda: self.came(4),),
            6: (self.far,),
            7: (lambda: self.came(7, 8),),
        }.get(n, ())


class Collect:
    def __init__(self, part, seg, split, total, pair, near, joined, send, recv):
        self.part, self.seg, self.total = part, seg, total
        self.pair, self.near, self.joined, self.send, self.recv = pair, near, joined, send, recv
        _, self.shard, self.inner, core = place()
        self.twin_shard = self.shard + 1 - 2 * core
        self.low, self.high, self.whole = (0, split), (split, seg - split), (0, seg)
        self.cols = pl.ds(0, D)

    def index(self, s, k):
        row, flip = 1 - k % 2, 1 - k // 2
        return 2 * lax.rem(s + 2 * row, 4) + self.inner + flip * (1 - 2 * self.inner)

    def pair_copy(self, k):
        src = self.part.at[aligned(self.index(self.twin_shard, k) * self.seg, self.seg), self.cols]
        return remote(src, self.pair.at[k], self.send.at[k], self.recv.at[k], partners()[2])

    def copy(self, slot):
        across, beside, _ = partners()
        src, dst, (first, size), device = {
            4: (self.pair.at[0], self.joined, self.low, across),
            5: (self.pair.at[0], self.joined, self.high, beside),
            6: (self.pair.at[1], self.near.at[0], self.low, across),
            7: (self.pair.at[2], self.near.at[1], self.high, beside),
            8: (self.pair.at[2], self.near.at[1], self.low, beside),
            9: (self.pair.at[1], self.near.at[0], self.high, across),
        }[slot]
        rows = pl.ds(first, size)
        return remote(src.at[rows], dst.at[rows], self.send.at[slot], self.recv.at[slot], device)

    def over(self, span, body):
        def step(n, _):
            body(aligned(span[0] + n * 16, 16))
            return 0

        lax.fori_loop(0, span[1] // 16, step, 0)

    def mine(self, k, rows):
        return self.part[aligned(self.index(self.shard, k) * self.seg + rows.start, 16), self.cols].astype(F32)

    def add_pair(self, k):
        def add(rows):
            self.pair[k, rows] = (self.mine(k, rows) + self.pair[k, rows].astype(F32)).astype(BF16)

        self.pair_copy(k).wait_recv()
        self.over(self.whole, add)
        for slot in ((4, 5), (6,), (7,))[k]:
            self.copy(slot).start()

    def add_own(self):
        def add(rows):
            self.total[rows] = self.mine(3, rows) + self.pair[3, rows].astype(F32)

        self.pair_copy(3).wait_recv()
        self.over(self.whole, add)

    def pass_on(self):
        for slot, k, span, after in ((4, 2, self.low, 8), (5, 1, self.high, 9)):

            def add(rows):
                self.pair[k, rows] = (self.pair[k, rows].astype(F32) + self.joined[rows].astype(F32)).astype(BF16)

            self.copy(slot).wait_recv()
            self.over(span, add)
            self.copy(after).start()

    def push(self):
        for k in range(4):
            self.pair_copy(k).start()

    def make(self, n, produce):
        k, own = n // 2, n % 2
        produce(self.index(jnp.where(own == 1, self.shard, self.twin_shard), k))

        @pl.when(own == 0)
        def _():
            self.pair_copy(k).start()

        for m in range(3):

            @pl.when(n == 2 * m + 1)
            def _():
                self.add_pair(m)
                if m == 2:
                    self.pass_on()

        pl.when(n == 7)(self.add_own)

    def end(self):
        def add(rows):
            near = self.near[0, rows].astype(F32) + self.near[1, rows].astype(F32)
            self.total[rows] = self.total[rows] + near

        for slots, span in (((6, 8), self.low), ((7, 9), self.high)):
            for slot in slots:
                self.copy(slot).wait_recv()
            self.over(span, add)
        for k in range(4):
            self.pair_copy(k).wait_send()
        for slot in range(4, 10):
            self.copy(slot).wait_send()


def norm_scale(values):
    return lax.rsqrt(jnp.mean(values * values, axis=-1, keepdims=True) + NORM_EPSILON)


def by_rows(rows, body, carry=0):
    def step(n, carry):
        return body(aligned(n * ROWS, ROWS), carry)

    return lax.fori_loop(0, rows // ROWS, step, carry)


def norm_back(values, gain, upstream):
    scale = norm_scale(values)
    scaled = gain * upstream
    inner = jnp.mean(scaled * values, axis=-1, keepdims=True)
    return (
        scale * scaled - values * scale * scale * scale * inner,
        jnp.sum(upstream * values * scale, axis=0, keepdims=True),
    )


REFS = (
    "tok", "cot", "gains", "weights",
    "block_out", "input_grad", "gain_sums", "mine", "theirs", "n1_held", "slot0", "slot1", "slot2", "slot3",
    "w0", "w1", "w2", "w3", "seq_a", "seq_b", "du", "act", "c_all", "gated", "mixed", "resid", "dresid", "total",
    "pair", "near", "joined", "g1", "g2", "g3", "stage", "sum", "tail", "outgoing", "tap_sums", "gain_in", "gain_line",
    "held", "loaded", "send_x", "recv_x", "send_z", "recv_z", "send_s", "recv_s", "send_c", "recv_c", "credit",
    "halo_send", "halo_recv", "send_g", "recv_g", "fetched", "fetches", "stored", "send_o", "recv_o",
    "send_a", "recv_a", "send_l", "recv_l",
)


def column_pieces(half):
    pieces = [(m * QUARTER + half * HALF_Q, m * HALF_Q, HALF_Q, 0) for m in range(4)]
    for k, (start, units) in enumerate(zip(UNIT_STARTS, UNIT_CHUNKS), 1):
        real = min(units, HALF_F - start)
        for m in range(3):
            first = 4 * QUARTER + m * UNITS + half * HALF_F + start
            pieces.append((first, STARTS[k] + m * units, real, units - real))
    return pieces


def block_kernel(layers, rows, *all_refs):
    r = dict(zip(REFS, all_refs, strict=True))
    tok, cot, gains = r["tok"], r["cot"], r["gains"]
    seq_a, seq_b, du, act = r["seq_a"], r["seq_b"], r["du"], r["act"]
    c_all, gated, mixed, total = r["c_all"], r["gated"], r["mixed"], r["total"]
    weights = (r["w0"], r["w1"], r["w2"], r["w3"])
    seg = tok.shape[0]
    _, shard, inner, _ = place()
    outer, at = line()
    me = 2 * shard + inner
    my_rows = aligned(me * seg, seg)
    chunks = list(zip(range(1, 1 + len(UNIT_CHUNKS)), UNIT_STARTS, UNIT_CHUNKS))
    gather = Gather(
        layers, rows, r["g1"], weights, r["send_x"], r["recv_x"], r["send_z"], r["recv_z"]
    )
    reduce = Reduce(
        layers, rows, (r["w2"], r["g1"], r["g2"], r["g3"]), (r["slot0"], r["slot1"], r["slot2"], r["slot3"]),
        r["stage"], r["w1"], r["sum"], r["outgoing"], r["mine"], r["theirs"],
        (r["send_g"], r["recv_g"], r["fetched"], r["fetches"], r["stored"], r["send_o"], r["recv_o"]),
    )

    def spread(buf, n):
        return Spread(buf, seg, SPREAD_SPLITS[n], r["send_s"].at[n], r["recv_s"].at[n])

    def collect(part, n):
        sems = r["send_c"].at[n], r["recv_c"].at[n]
        return Collect(part, seg, COLLECT_SPLITS[n], total, r["pair"], r["near"], r["joined"], *sems)

    one, up, two, three = spread(seq_a, 0), spread(seq_b, 1), spread(seq_a, 2), spread(seq_a, 3)
    branch, down, feed, inputs = collect(seq_a, 0), collect(seq_b, 1), collect(du, 2), collect(seq_a, 3)
    lanes = lax.broadcasted_iota(jnp.int32, (seg, WIDE), 1) < HALF_Q
    taps = pltpu.roll(gains[...], lax.rem(D - shard * QUARTER - inner * HALF_Q, D), 1)[2:5, :WIDE]
    kept = pl.ds(D, WIDE)
    sums, tap_sums = r["gain_sums"], r["tap_sums"]

    def block(t):
        return aligned(t * seg, seg)

    def mine(part):
        return pl.ds(pl.multiple_of(me * seg + part.start, 16), part.size)

    def first_norm():
        def rows(part, _):
            values = tok[part].astype(F32)
            seq_a[mine(part)] = (values * norm_scale(values) * gains[0:1, :]).astype(BF16)
            return 0

        by_rows(seg, rows)

    def up_start():
        seq_b[my_rows] = cot[...]
        up.start()

    def held():
        return pltpu.make_async_copy(seq_a, r["n1_held"], r["held"])

    def reload():
        return pltpu.make_async_copy(r["n1_held"], seq_b, r["held"])

    def project(s):
        for i in (0, 1):
            parts = dot(seq_a[block(2 * s + i)], weights[0][...])
            b = jnp.where(lanes, parts[:, :WIDE], 0.0)
            c = pltpu.roll(parts[:, 128 : 128 + 384], 384 - 64, 1)[:, :WIDE]
            x = parts[:, 384 : 384 + WIDE]
            c_all[s, pl.ds(i * seg, seg)] = jnp.where(lanes, c, 0.0)
            gated[s, pl.ds(8 + i * seg, seg)] = (b * x).astype(BF16).astype(F32)

    def ahead():
        return remote(
            gated.at[:, pl.ds(2 * seg, 8)], gated.at[:, pl.ds(0, 8)], r["halo_send"].at[0], r["halo_recv"].at[0], at(1)
        )

    def halo():
        pl.when(outer < layers - 1)(lambda: ahead().start())

        @pl.when(outer == 0)
        def _():
            gated[:, pl.ds(0, 8)] = jnp.zeros((GROUPS, 8, WIDE), F32)

    def convolved(s, i):
        return (
            taps[0:1, :] * gated[s, pl.ds(6 + i * seg, seg)]
            + taps[1:2, :] * gated[s, pl.ds(7 + i * seg, seg)]
            + taps[2:3, :] * gated[s, pl.ds(8 + i * seg, seg)]
        )

    def convolve(t):
        for i in (0, 1):

            @pl.when(t % 2 == i)
            def _():
                s = t // 2
                mixed[block(t)] = pltpu.roll(c_all[s, pl.ds(i * seg, seg)] * convolved(s, i), 64, 1).astype(BF16)

        seq_a[block(t)] = dot_rows(mixed[block(t)], weights[0][:, pl.ds(512, WIDE)]).astype(BF16)

    def branch_end():
        branch.end()
        allow(r["credit"].at[0])

    def second_norm():
        def rows(part, _):
            values = tok[part].astype(F32) + total[part]
            r["resid"][part] = values
            seq_a[mine(part)] = (values * norm_scale(values) * gains[1:2, :]).astype(BF16)
            return 0

        by_rows(seg, rows)
        pl.semaphore_wait(r["credit"].at[0], 3)

    def hidden(k, start, units, t):
        ref, here = weights[k], block(t)
        gate = dot(seq_a[here], ref[:, pl.ds(0, units)])
        upval = dot(seq_a[here], ref[:, pl.ds(units, units)])
        dact = dot(seq_b[here], ref[:, pl.ds(2 * units, units)])
        sigma = jax.nn.sigmoid(gate)
        silu = gate * sigma
        act[here, pl.ds(start, units)] = (silu * upval).astype(BF16)
        dgate = dact * upval * sigma * (1.0 + gate * (1.0 - sigma))
        du[here, pl.ds(2 * start, units)] = dgate.astype(BF16)
        du[here, pl.ds(2 * start + units, units)] = (dact * silu).astype(BF16)

    def slice_of(n):
        return jnp.where(outer < layers // 2, D // SLICE - 1 - n, n)

    def gate_up_grads(k, start, units, n):
        part = slice_of(n)
        left = seq_a[:, aligned(part * SLICE, SLICE, 128)]
        reduce.grads[k][aligned(part * SLICE, SLICE), pl.ds(0, 2 * units)] = dot_columns(
            left, du[:, pl.ds(2 * start, 2 * units)]
        ).astype(BF16)

    def down_grads(k, start, units, n):
        part = slice_of(n)
        left = seq_b[:, aligned(part * SLICE, SLICE, 128)]
        reduce.grads[k][aligned(part * SLICE, SLICE), pl.ds(2 * units, units)] = dot_columns(
            left, act[:, pl.ds(start, units)]
        ).astype(BF16)

    def grads(k, start, units, n):
        gate_up_grads(k, start, units, n)
        down_grads(k, start, units, n)
        reduce.direct(k, slice_of(n))

    def second(t):
        here = block(t)
        seq_b[here] = sum(
            dot_rows(du[here, pl.ds(2 * start, 2 * units)], weights[k][:, pl.ds(0, 2 * units)])
            for k, start, units in chunks
        ).astype(BF16)

    def down_end():
        down.end()
        reload().start()
        allow(r["credit"].at[1])

    def forward(t):
        here = block(t)
        du[here, pl.ds(0, D)] = sum(
            dot_rows(act[here, pl.ds(start, units)], weights[k][:, pl.ds(2 * units, units)])
            for k, start, units in chunks
        ).astype(BF16)

    def second_back():
        def rows(part, gain):
            dpart, dgain = norm_back(r["resid"][part], gains[1:2, :], total[part])
            dresid = cot[part].astype(F32) + dpart
            r["dresid"][part] = dresid
            seq_a[mine(part)] = dresid.astype(BF16)
            return gain + dgain

        sums[...] = jnp.zeros(sums.shape, F32)
        tap_sums[...] = jnp.zeros(tap_sums.shape, F32)
        sums[1:2, pl.ds(0, D)] = by_rows(seg, rows, jnp.zeros((1, D), F32))
        pl.semaphore_wait(r["credit"].at[1], 3)

    def mix_back(t):
        s, here = t // 2, block(t)
        dmixed = pltpu.roll(dot(seq_a[here], weights[0][:, pl.ds(512, WIDE)]), WIDE - 64, 1)
        dmixed = jnp.where(lanes, dmixed, 0.0)
        for i in (0, 1):

            @pl.when(t % 2 == i)
            def _():
                du[here, kept] = (dmixed * convolved(s, i)).astype(BF16)
                c_all[s, pl.ds(i * seg, seg)] = dmixed * c_all[s, pl.ds(i * seg, seg)]

    def after():
        return remote(
            c_all.at[:, pl.ds(0, 8)], c_all.at[:, pl.ds(2 * seg, 8)], r["halo_send"].at[1], r["halo_recv"].at[1], at(-1)
        )

    def halo_back():
        pl.when(outer > 0)(lambda: after().start())

        @pl.when(outer == layers - 1)
        def _():
            c_all[:, pl.ds(2 * seg, 8)] = jnp.zeros((GROUPS, 8, WIDE), F32)

    def conv_back(n):
        for i in (0, 1):
            pl.when(n // GROUPS == i)(functools.partial(conv_back_half, n % GROUPS, i))

    def conv_back_half(s, i):
        t = block(2 * s + i)
        dconv = c_all[s, pl.ds(i * seg, seg)]
        dgated = (
            taps[2:3, :] * dconv
            + taps[1:2, :] * c_all[s, pl.ds(1 + i * seg, seg)]
            + taps[0:1, :] * c_all[s, pl.ds(2 + i * seg, seg)]
        )
        parts = dot(seq_b[t], weights[0][:, pl.ds(0, 640)])
        db = dgated * parts[:, 384:640]
        dx = dgated * parts[:, :WIDE]
        dc = jnp.concatenate([du[t, kept].astype(F32), jnp.zeros((seg, 128), F32)], axis=1)
        dc = pltpu.roll(dc, 64, 1)
        act[t, pl.ds(0, 128)] = db[:, :128].astype(BF16)
        act[t, pl.ds(128, 128)] = (db[:, 128:] + dc[:, :128]).astype(BF16)
        act[t, pl.ds(256, 128)] = dc[:, 128:256].astype(BF16)
        act[t, pl.ds(384, WIDE)] = dx.astype(BF16)
        act[t, pl.ds(640, 128)] = jnp.zeros((seg, 128), BF16)
        for k in range(3):
            moved = gated[s, pl.ds(6 + k + i * seg, seg)]
            tap_sums[k : k + 1] = tap_sums[k : k + 1] + jnp.sum(dconv * moved, axis=0, keepdims=True)

    def conv_grads(n):
        part = slice_of(n)
        held_rows, cols = aligned(part * SLICE, SLICE), aligned(part * SLICE, SLICE, 128)
        ref = reduce.grads[0]
        of_parts = dot_columns(seq_b[:, cols], act[:, pl.ds(0, CONV_COLS)])
        ref[held_rows, pl.ds(0, 512)] = of_parts[:, :512].astype(BF16)
        of_mixed = dot_columns(seq_a[:, cols], mixed[...])
        ref[held_rows, pl.ds(512, WIDE)] = (of_parts[:, 512:] + of_mixed).astype(BF16)
        reduce.direct(0, part)

    def feed_end():
        feed.end()
        allow(r["credit"].at[2])
        r["block_out"][...] = (r["resid"][...] + total[...]).astype(BF16)

    def first(t):
        here = block(t)
        seq_a[here] = dot_rows(act[here, pl.ds(0, 640)], weights[0][:, pl.ds(0, 640)]).astype(BF16)

    def first_back():
        def rows(part, gain):
            dpart, dgain = norm_back(tok[part].astype(F32), gains[0:1, :], total[part])
            r["input_grad"][part] = (r["dresid"][part] + dpart).astype(BF16)
            return gain + dgain

        sums[0:1, pl.ds(0, D)] = by_rows(seg, rows, jnp.zeros((1, D), F32))
        sums[2:5, aligned(me * WIDE, WIDE, 128)] = tap_sums[0:3]

    def gains_across(n):
        return remote(sums, r["gain_in"].at[n], r["send_a"].at[n], r["recv_a"].at[n], partners()[n])

    def gains_add(n):
        gains_across(n).wait()
        sums[...] = sums[...] + r["gain_in"][n]

    def line_copy(sign, steps):
        slot = (0 if sign > 0 else 1, steps - 1)
        return remote(
            sums, r["gain_line"].at[slot], r["send_l"].at[slot], r["recv_l"].at[slot], at(sign * steps)
        )

    def gains_line():
        for steps in range(1, layers):
            for sign in (1, -1):
                pl.when(in_line(outer + sign * steps, layers))(line_copy(sign, steps).start)

    def gains_end():
        for steps in range(1, layers):
            for sign in (1, -1):
                pl.when(in_line(outer + sign * steps, layers))(line_copy(sign, steps).wait_send)
                pl.when(in_line(outer - sign * steps, layers))(line_copy(sign, steps).wait_recv)

        own_sums = sums[...]
        for origin in range(layers):
            for steps in range(1, layers):
                for sign in (1, -1):

                    @pl.when((outer - sign * steps == origin))
                    def _():
                        came = r["gain_line"][0 if sign > 0 else 1, steps - 1]
                        sums[...] = came if origin == 0 else sums[...] + came

            if origin > 0:

                @pl.when(outer == origin)
                def _():
                    sums[...] = sums[...] + own_sums

    def end():
        reduce.finish(0)
        for k in range(len(WIDTHS)):
            reduce.wait_sent(k)
        pl.when(outer < layers - 1)(lambda: ahead().wait_send())
        pl.when(outer > 0)(lambda: after().wait_send())

    windows = [
        (r["resid"], 0, D), (r["dresid"], D, D), (total, 2 * D, D), (r["resid"], 3 * D, D),
        (r["tail"], 4 * D, GROUP_COLS - 4 * D),
    ]

    def load(n):
        ref, first, width = windows[n]
        return pltpu.make_async_copy(
            r["weights"].at[:, pl.ds(first, width)], ref.at[pl.ds(0, rows)], r["loaded"].at[n]
        )

    def start():
        for n in (0, 1, 2, 4):
            load(n).start()
        greet(layers)
        load(0).wait()
        cut(0)
        load(3).start()
        greeted(layers)

    def cut(k):
        def read(part, first, width):
            found = []
            for n, (ref, low, size) in enumerate(windows):
                start, stop = max(first, low), min(first + width, low + size)
                if start < stop and (n == 0) == (k == 0):
                    found.append(ref[part, start - low : stop - low])
            return found

        size = band(rows, 96)

        def cut_band(n, _):
            part = aligned(n * size, size)
            halves = []
            for half in (0, 1):
                pieces = []
                for first, own, width, padding in column_pieces(half):
                    if STARTS[k] <= own < STARTS[k] + WIDTHS[k]:
                        pieces += read(part, first, width)
                        if padding:
                            pieces.append(jnp.zeros((size, padding), F32))
                halves.append(jnp.concatenate(pieces, axis=1))
            is_low = inner == 0
            seq = lax.axis_index("seq")
            own_rows = aligned(seq * rows + n * size, size)
            weights[k][own_rows, :] = jnp.where(is_low, halves[0], halves[1]).astype(BF16)
            gather.other_rows(k)[part, :] = jnp.where(is_low, halves[1], halves[0]).astype(BF16)
            return 0

        for n in (1, 2, 3, 4) if k == CUT_FIRST else ():
            load(n).wait()
        lax.fori_loop(0, rows // size, cut_band, 0)

    def hold():
        held().start()

    def hold_end():
        held().wait()

    def halo_end():
        pl.when(outer > 0)(lambda: ahead().wait_recv())

    def reload_end():
        reload().wait()

    def halo_back_end():
        pl.when(outer < layers - 1)(lambda: after().wait_recv())

    def feed_credit():
        pl.semaphore_wait(r["credit"].at[2], 3)

    def from_spread(moved, body):
        def step(n):
            for m in range(8):
                if moved.before(m):

                    @pl.when(n == m)
                    def _():
                        for act in moved.before(m):
                            act()

            body(moved.index(n))

        return step

    def each(body, *cases):
        return [functools.partial(body, *(case if isinstance(case, tuple) else (case,))) for case in cases]

    every = range(len(WIDTHS))
    cuts = each(cut, *every)
    exchange, send_own, send_other = (
        each(body, *every) for body in (gather.exchange, gather.send_own, gather.send_other)
    )
    step = [each(gather.steps, (k, 1, 1), (k, 2, 2), (k, 3)) for k in every]
    join_far = each(reduce.join, *((k, layers - 2, 2) for k in every))
    join_near = each(reduce.join, *((k, 1, 1) for k in every))
    final = each(reduce.final, (0, 3), 1, (2, 1), (3, 2))
    feed_pair = each(feed.add_pair, 0, 1, 2)
    gain_send = [lambda n=n: gains_across(n).start() for n in range(3)]
    gain_add = each(gains_add, 0, 1, 2)
    d3_far = functools.partial(reduce.direct, 3, least=2)
    d3_near = functools.partial(reduce.direct, 3, most=1)
    blocks, parts = 2 * GROUPS, D // SLICE
    proj = Loop(GROUPS, project)
    mix = Loop(blocks, lambda n: branch.make(n, convolve))
    hid1 = Loop(blocks, from_spread(two, functools.partial(hidden, *chunks[0])))
    hid2, hid3 = (Loop(blocks, functools.partial(hidden, *chunk)) for chunk in chunks[1:])
    grad1, grad2 = (Loop(parts, functools.partial(grads, *chunk)) for chunk in chunks[:2])
    down3 = Loop(parts, functools.partial(down_grads, *chunks[2]))
    back2 = Loop(blocks, lambda n: down.make(n, second))
    gate3 = Loop(parts, functools.partial(gate_up_grads, *chunks[2]))
    ffn = Loop(blocks, forward)
    back_mix = Loop(blocks, from_spread(three, mix_back))
    back_conv = Loop(blocks, conv_back)
    grad0 = Loop(parts, conv_grads)
    back1 = Loop(blocks, lambda n: inputs.make(n, first))
    play(
        [
            start, exchange[0], send_own[0], first_norm, cuts[1], send_other[0], one.start, send_own[1], cuts[2],
            exchange[1], step[0][0], one.first, up_start, one.near, exchange[2], step[0][1], cuts[3], send_other[1],
            one.far, step[0][2], one.end, proj[0], proj[1], up.first, up.near, hold, proj[2], proj[3], halo,
            step[1][0], hold_end, halo_end, mix[0], mix[1], mix[2], mix[3], mix[4], up.far, mix[5], mix[6], mix[7],
            step[1][1], up.end, exchange[3], send_own[3], send_other[2], send_own[2], branch_end, second_norm,
            two.start, step[1][2], send_other[3], hid1[0], hid1[1], hid1[2], hid1[3], hid1[4], step[2][0], hid1[5],
            gather.crossed, hid1[6], hid1[7], two.sent, grad1[0], grad1[1], grad1[2], step[2][1], step[3][0],
            step[2][2], grad1[3], hid2[0], hid2[1], hid2[2], hid2[3], hid2[4], hid2[5], hid2[6], hid2[7], grad2[0],
            grad2[1], grad2[2], grad2[3], step[3][1], step[3][2], hid3[0], hid3[1], hid3[2], hid3[3], hid3[4],
            hid3[5], hid3[6], hid3[7], down3[0], down3[1], down3[2], down3[3], back2[0], back2[1], join_far[1],
            back2[2], back2[3], back2[4], back2[5], back2[6], back2[7], gate3[0], gate3[1], join_near[1], gate3[2],
            gate3[3], down_end, second_back, three.start, d3_far, ffn[0], ffn[1], ffn[2], ffn[3], ffn[4], ffn[5],
            ffn[6], ffn[7], back_mix[0], back_mix[1], feed.push, back_mix[2], join_far[2], feed_pair[0],
            back_mix[3], gather.finish, back_mix[4], feed_pair[1], back_mix[5], reload_end, back_mix[6],
            feed_pair[2], back_mix[7], three.sent, halo_back, back_conv[0], join_near[2], back_conv[1], d3_near,
            back_conv[2], back_conv[3], feed.pass_on, final[1], feed.add_own, halo_back_end, back_conv[4],
            join_far[3], back_conv[5], back_conv[6], back_conv[7], grad0[0], grad0[1], grad0[2], grad0[3], feed_end,
            join_near[3], feed_credit, back1[0], back1[1], back1[2], back1[3], back1[4], join_far[0], back1[5],
            back1[6], final[2], back1[7], join_near[0], inputs.end, first_back, gain_send[0], final[3], gain_add[0],
            gain_send[1], gain_add[1], gain_send[2], gain_add[2], gains_line, final[0], gains_end, end,
        ]
    )


class Loop:
    def __init__(self, count, body):
        self.count, self.body = count, body

    def __getitem__(self, n):
        return (self, n)


def play(order):
    order = list(order)
    while order:
        entry = order.pop(0)
        if not isinstance(entry, tuple):
            entry()
            continue
        loop, _ = entry
        between = {}
        for n in range(1, loop.count):
            between[n] = []
            while order[0] != (loop, n):
                between[n].append(order.pop(0))
            order.pop(0)

        def turn(n, _):
            for m, acts in between.items():
                if acts:

                    @pl.when(n == m)
                    def _():
                        play(acts)

            loop.body(n)
            return 0

        lax.fori_loop(0, loop.count, turn, 0)


def block_step(tok, cot, gains, weights, layers):
    rows, seg = weights.shape[0], tok.shape[0]
    count = len(WIDTHS)
    tokens = 2 * GROUPS * seg
    vmem, anywhere = pl.BlockSpec(memory_space=pltpu.VMEM), pl.BlockSpec(memory_space=pl.ANY)
    shape, scratch = jax.ShapeDtypeStruct, pltpu.VMEM
    dma, regular = pltpu.SemaphoreType.DMA, pltpu.SemaphoreType.REGULAR
    hops = layers - 1
    wide, biggest = sum(WIDTHS), max(WIDTHS)
    out_shape = [
        shape((seg, D), BF16),
        shape((seg, D), BF16),
        shape((8, 2 * GROUPS * WIDE), F32),
        shape((rows, wide), F32),
        shape((rows, wide), BF16),
        shape((tokens, D), BF16),
    ] + [shape((2, hops, 2 * rows, width), BF16) for width in WIDTHS]
    scratch_shapes = (
        [scratch((D, width), BF16) for width in WIDTHS]
        + [
            scratch((tokens, D), BF16),
            scratch((tokens, D), BF16),
            scratch((tokens, 2 * PAD_F), BF16),
            scratch((tokens, PAD_F), BF16),
            scratch((GROUPS, 8 + 2 * seg, WIDE), F32),
            scratch((GROUPS, 8 + 2 * seg, WIDE), F32),
            scratch((tokens, WIDE), BF16),
            scratch((seg, D), F32),
            scratch((seg, D), F32),
            scratch((seg, D), F32),
            scratch((4, seg, D), BF16),
            scratch((2, seg, D), BF16),
            scratch((seg, D), BF16),
        ]
        + [scratch((D, width), BF16) for width in WIDTHS[1:]]
        + [
            scratch((2 * rows, biggest), BF16),
            scratch((rows, biggest), F32),
            scratch((rows, GROUP_COLS - 4 * D), F32),
            scratch((rows, wide), BF16),
            scratch((8, WIDE), F32),
            scratch((3, 8, 2 * GROUPS * WIDE), F32),
            scratch((2, hops, 8, 2 * GROUPS * WIDE), F32),
            dma,
            dma((5,)),
            dma((count,)),
            dma((count,)),
            dma((count, 2, hops, 2)),
            dma((count, 2, hops, 2)),
            dma((4, 11)),
            dma((4, 11)),
            dma((4, 10)),
            dma((4, 10)),
            regular((3,)),
            dma((2,)),
            dma((2,)),
            dma((count, 2, hops)),
            dma((count, 2, hops)),
            dma,
            dma((4,)),
            dma((count,)),
            dma((count,)),
            dma((count,)),
            dma((3,)),
            dma((3,)),
            dma((2, hops)),
            dma((2, hops)),
        ]
    )
    return pl.pallas_call(
        functools.partial(block_kernel, layers, rows),
        out_shape=out_shape,
        in_specs=[vmem] * 3 + [anywhere],
        out_specs=[vmem] * 3 + [anywhere] * (3 + count),
        scratch_shapes=scratch_shapes,
        compiler_params=pltpu.CompilerParams(
            collective_id=0, has_side_effects=True, vmem_limit_bytes=VMEM_BYTES
        ),
        name="block_step",
    )(tok, cot, gains, weights)[:5]


def band(rows, most):
    return max(size for size in range(16, most + 1, 16) if rows % size == 0)


def adam_update(param, grad, first, second, rate, decay):
    first_new = MOMENT_DECAY * first + (1.0 - MOMENT_DECAY) * grad
    second_new = SQUARE_DECAY * second + (1.0 - SQUARE_DECAY) * grad * grad
    root = jnp.sqrt(second_new * (1.0 / (1.0 - SQUARE_DECAY**STEP))) + ADAM_EPSILON
    step = first_new * (rate / (1.0 - MOMENT_DECAY**STEP)) / root
    return (first_new, second_new, param * (1.0 - rate * decay) - step)


def update_kernel(
    inner_ref, mine_ref, theirs_ref, weights_ref, first_ref, second_ref, sums_ref, gains_ref, gains_first_ref,
    gains_second_ref, block_ref, input_ref, grad_out, first_out, second_out, weights_out, gains_grad_out,
    gains_first_out, gains_second_out, gains_out, block_out, input_out,
):
    is_low = inner_ref[0] == 0
    mine, theirs = mine_ref[...], theirs_ref[...].astype(F32)
    for half in (0, 1):
        chosen = jnp.where(is_low, mine, theirs) if half == 0 else jnp.where(is_low, theirs, mine)
        for first, own, width, _ in column_pieces(half):
            grad_out[:, first : first + width] = chosen[:, own : own + width]
    first_out[...], second_out[...], weights_out[...] = adam_update(
        weights_ref[...], grad_out[...], first_ref[...], second_ref[...], WEIGHT_RATE, WEIGHT_DECAY
    )

    @pl.when(pl.program_id(0) == 0)
    def _():
        gains_grad_out[0:2] = sums_ref[0:2, :D]
        for n in range(2 * GROUPS):
            gains_grad_out[2:5, n * HALF_Q : (n + 1) * HALF_Q] = sums_ref[2:5, n * WIDE : n * WIDE + HALF_Q]
        gains_first_out[...], gains_second_out[...], gains_out[...] = adam_update(
            gains_ref[...], gains_grad_out[...], gains_first_ref[...], gains_second_ref[...], GAIN_RATE, 0.0
        )
        block_out[...] = block_ref[...]
        input_out[...] = input_ref[...]


def update(inner, mine, theirs, weights, first, second, sums, gains, gains_first, gains_second, block, grad):
    rows, cols = weights.shape
    wide = mine.shape[1]
    size = band(rows, 64)
    by_row = lambda width: pl.BlockSpec((size, width), lambda n: (n, 0))
    whole = lambda values: pl.BlockSpec(values.shape, lambda n: (0, 0))
    shape = jax.ShapeDtypeStruct
    return pl.pallas_call(
        update_kernel,
        grid=(rows // size,),
        out_shape=[shape((rows, cols), F32)] * 4 + [shape(gains.shape, F32)] * 4 + [shape(block.shape, BF16)] * 2,
        in_specs=[pl.BlockSpec(memory_space=pltpu.SMEM)]
        + [by_row(wide)] * 2
        + [by_row(cols)] * 3
        + [whole(sums)]
        + [whole(gains)] * 3
        + [whole(block)] * 2,
        out_specs=[by_row(cols)] * 4 + [whole(gains)] * 4 + [whole(block)] * 2,
        compiler_params=pltpu.CompilerParams(vmem_limit_bytes=VMEM_BYTES),
        name="update",
    )(inner, mine, theirs, weights, first, second, sums, gains, gains_first, gains_second, block, grad)


def on_device(
    tokens, gains_taps, weights, cotangent, weight_first, weight_second, gains_first, gains_second
):
    layers = lax.axis_size("seq") // 2
    inner_word = (lax.axis_index("seq") % 2).astype(jnp.int32).reshape(1)
    block_out, input_grad, gain_sums, mine, theirs = block_step(
        tokens[0], cotangent[0], gains_taps, weights, layers
    )
    (
        weight_grad, weight_first_new, weight_second_new, weight_new,
        gains_grad, gains_first_new, gains_second_new, gains_new, block_out, input_grad,
    ) = update(
        inner_word, mine, theirs, weights, weight_first, weight_second,
        gain_sums, gains_taps, gains_first, gains_second, block_out, input_grad,
    )
    return (
        block_out[None],
        input_grad[None],
        weight_grad,
        weight_first_new,
        weight_second_new,
        weight_new,
        gains_grad,
        gains_first_new,
        gains_second_new,
        gains_new,
    )


def solution(mesh):
    tokens, rows, whole = P("shard", "seq", None), P("seq", "shard"), P()
    return jax.shard_map(
        on_device,
        mesh=mesh,
        in_specs=(tokens, whole, rows, tokens, rows, rows, whole, whole),
        out_specs=(tokens, tokens, rows, rows, rows, rows, whole, whole, whole, whole),
        check_vma=False,
    )
```
